32 devices in a mesh: dp: 4 (over x, core), chan: 8 (over z, y).
Axes of the slice: x: 2, y: 2, z: 4, core: 2. Of those that a mesh axis runs over, the one named last changes fastest.
Arguments:
- tokens: bfloat16 [4096, 512], P('dp', 'chan'), may hold values from -6 to 6
- cotangent: float32 [4096, 512], P('dp', 'chan'), may hold values from -6 to 6
- group_bucket: int32 [4], P('dp'), may hold values from 0 to 2, as said below
- group_items: int32 [4], P('dp'), may hold values from 1 to 4, as said below
- first_norm_gain: float32 [512], P('chan'), may hold values from 0.5 to 1.5
- first_norm_bias: float32 [512], P('chan'), may hold values from -1 to 1
- modes: float32 [8, 512, 32], P(None, 'chan'), may hold values from -3 to 3
- log_dt: float32 [512], P('chan'), may hold values from -6.9 to -2.3
- d_skip: float32 [512], P('chan'), may hold values from -4 to 4
- w_a: float32 [512, 512], P('dp', 'chan'), may hold values from -0.25 to 0.25
- b_a: float32 [512], P('chan'), may hold values from -1 to 1
- w_b: float32 [512, 512], P('dp', 'chan'), may hold values from -0.25 to 0.25
- b_b: float32 [512], P('chan'), may hold values from -1 to 1
- second_norm_gain: float32 [512], P('chan'), may hold values from 0.5 to 1.5
- second_norm_bias: float32 [512], P('chan'), may hold values from -1 to 1
- w_up: float32 [512, 2048], P('dp', 'chan'), may hold values from -0.25 to 0.25
- b_up: float32 [2048], P('chan'), may hold values from -1 to 1
- w_down: float32 [2048, 512], P('chan', 'dp'), may hold values from -0.125 to 0.125
- b_down: float32 [512], P('chan'), may hold values from -1 to 1
Outputs:
- output: bfloat16 [4096, 512], P('dp', 'chan')
- grad_tokens: float32 [4096, 512], P('dp', 'chan')
- first_norm_gain_gradient: float32 [512], P('chan')
- grad_ln1_bias: float32 [512], P('chan')
- grad_modes: float32 [8, 512, 32], P(None, 'chan')
- grad_log_dt: float32 [512], P('chan')
- grad_d_skip: float32 [512], P('chan')
- grad_w_a: float32 [512, 512], P('dp', 'chan')
- grad_b_a: float32 [512], P('chan')
- grad_w_b: float32 [512, 512], P('dp', 'chan')
- grad_b_b: float32 [512], P('chan')
- second_norm_gain_gradient: float32 [512], P('chan')
- grad_ln2_bias: float32 [512], P('chan')
- grad_w_up: float32 [512, 2048], P('dp', 'chan')
- grad_b_up: float32 [2048], P('chan')
- grad_w_down: float32 [2048, 512], P('chan', 'dp')
- grad_b_down: float32 [512], P('chan')
The draws below stay inside these ranges and needn't reach their ends.
Inputs may be any that keep to these rules, and one draw needn't show every extreme that they name: Data group g holds items of 256 * 2^group_bucket[g] tokens; some group is at level 2 and some at level 0 in every draw. `group_items`: A group at level b holds at least half of 4 // 2^b items and at most 4 // 2^b; some group holds one item of 1024 tokens and some other group four items in every draw.
All inputs are finite; a program needn't handle non-finite values.
Results may differ from the reference program's by a relative error of at most 0.0078.
Values may be sent and summed in bfloat16 or wider, within the bound.
A program may use at most 128 MiB of HBM per device.

```python
import math
from functools import partial
import jax
import jax.numpy as jnp
from jax import lax

MODEL_WIDTH = 512
FF = 2048
NM = 32
TOK_DEV = 1024
TOKENS = 4096
N_DP = 4


def bucket_plan(key):
    levels = jax.random.randint(jax.random.fold_in(key, 11), (N_DP,), 0, 3)
    room = jnp.where(levels == 0, 4, jnp.where(levels == 1, 2, 1))
    spare = jax.random.randint(jax.random.fold_in(key, 12), (N_DP,), 0, 12)
    items = room - spare % (room // 2 + 1)
    order = jax.random.permutation(jax.random.fold_in(key, 13), N_DP)
    levels = levels.at[order[0]].set(2).at[order[1]].set(0)
    items = items.at[order[0]].set(1).at[order[1]].set(4)
    return (levels.astype(jnp.int32), items.astype(jnp.int32))


def draw_group_bucket(key, part):
    levels, items = bucket_plan(key)
    return levels


def draw_group_items(key, part):
    levels, items = bucket_plan(key)
    return items


def level_of(key, shape, cuts, low, largest):
    level = 1.0
    for position, parts in cuts:
        draws = jax.random.uniform(jax.random.fold_in(jax.random.fold_in(key, 6), position), (parts,), jnp.float32, low / len(cuts), largest / len(cuts))
        level = level * jnp.repeat(jnp.exp(draws), shape[position] // parts).reshape((-1,) + (1,) * (len(shape) - 1 - position))
    return level


def gaussian(rng, dims, scale, limit, split=(), kind=jnp.bfloat16):
    array = jax.random.normal(rng, dims, jnp.float32) * scale
    if len(split) > 0:
        array = level_of(rng, dims, split, -0.22, 0.18) * array
    return jnp.clip(array, min=-limit, max=limit).astype(kind)


def setup_inputs(seed: int = 0) -> dict:
    splits = jax.random.split(jax.random.key(seed), 20)
    tokens = gaussian(splits[0], (TOKENS, MODEL_WIDTH), 1.0, 6.0, ((0, 4), (1, 8)))
    cotangent = gaussian(splits[1], (TOKENS, MODEL_WIDTH), 1.0, 6.0, ((0, 4), (1, 8)), jnp.float32)
    group_bucket = draw_group_bucket(jax.random.fold_in(splits[19], 71), 0)
    group_items = draw_group_items(jax.random.fold_in(splits[19], 71), 0)
    first_norm_gain = jnp.clip(1.0 + 0.1 * jax.random.normal(splits[4], (MODEL_WIDTH,), jnp.float32), 0.5, 1.5)
    first_norm_bias = gaussian(splits[5], (MODEL_WIDTH,), 0.2, 1.0, ((0, 8),), jnp.float32)
    modes = gaussian(splits[6], (8, MODEL_WIDTH, NM), 0.5, 3.0, ((1, 8),), jnp.float32)
    log_dt = jnp.clip(-6.9 + 4.6000001430511475 * jax.random.uniform(splits[7], (MODEL_WIDTH,), jnp.float32) ** level_of(splits[7], (MODEL_WIDTH,), ((0, 8),), -0.2, 0.2), -6.9, -2.3)
    d_skip = gaussian(splits[8], (MODEL_WIDTH,), 1.0, 4.0, ((0, 8),), jnp.float32)
    w_a = gaussian(splits[9], (MODEL_WIDTH, MODEL_WIDTH), MODEL_WIDTH ** -0.5, 0.25, ((0, 4), (1, 8)), jnp.float32)
    b_a = gaussian(splits[10], (MODEL_WIDTH,), 0.2, 1.0, ((0, 8),), jnp.float32)
    w_b = gaussian(splits[11], (MODEL_WIDTH, MODEL_WIDTH), MODEL_WIDTH ** -0.5, 0.25, ((0, 4), (1, 8)), jnp.float32)
    b_b = gaussian(splits[12], (MODEL_WIDTH,), 0.2, 1.0, ((0, 8),), jnp.float32)
    second_norm_gain = jnp.clip(1.0 + 0.1 * jax.random.normal(splits[13], (MODEL_WIDTH,), jnp.float32), 0.5, 1.5)
    second_norm_bias = gaussian(splits[14], (MODEL_WIDTH,), 0.2, 1.0, ((0, 8),), jnp.float32)
    w_up = gaussian(splits[15], (MODEL_WIDTH, FF), MODEL_WIDTH ** -0.5, 0.25, ((0, 4), (1, 8)), jnp.float32)
    b_up = gaussian(splits[16], (FF,), 0.2, 1.0, ((0, 8),), jnp.float32)
    w_down = gaussian(splits[17], (FF, MODEL_WIDTH), FF ** -0.5, 0.125, ((0, 8), (1, 4)), jnp.float32)
    b_down = gaussian(splits[18], (MODEL_WIDTH,), 0.2, 1.0, ((0, 8),), jnp.float32)
    return {"tokens": tokens, "cotangent": cotangent, "group_bucket": group_bucket, "group_items": group_items, "first_norm_gain": first_norm_gain, "first_norm_bias": first_norm_bias, "modes": modes, "log_dt": log_dt, "d_skip": d_skip, "w_a": w_a, "b_a": b_a, "w_b": w_b, "b_b": b_b, "second_norm_gain": second_norm_gain, "second_norm_bias": second_norm_bias, "w_up": w_up, "b_up": b_up, "w_down": w_down, "b_down": b_down}


@jax.custom_vjp
def low(v):
    return lax.optimization_barrier(v.astype(jnp.bfloat16)).astype(jnp.float32)

@jax.custom_vjp
def low_back(v):
    return v

def low_keep(v):
    return (low(v), None)

def low_pass(kept, grad):
    return (grad,)

def back_keep(v):
    return (v, None)

def back_low(kept, grad):
    return (low(grad),)
low.defvjp(low_keep, low_pass)
low_back.defvjp(back_keep, back_low)
HIGHEST = lax.Precision.HIGHEST
EPSILON = 1e-05

def matmul_high(left, right):
    return jnp.dot(left, right, preferred_element_type=jnp.float32, precision=HIGHEST)

def layer_norm(values, gain, offset):
    centre = lax.optimization_barrier(jnp.mean(values, axis=1, keepdims=True))
    centred = values - centre
    spread = lax.optimization_barrier(jnp.mean(centred * centred, axis=1, keepdims=True))
    return centred * lax.rsqrt(spread + EPSILON) * gain + offset

def phase_table(row_count, col_count, length, direction):
    product = jnp.arange(row_count, dtype=jnp.int32)[:, None] * jnp.arange(col_count, dtype=jnp.int32)[None, :] % length
    angle = product.astype(jnp.float32) * (direction * 2.0 * math.pi / length)
    return (jnp.cos(angle), jnp.sin(angle))

def kernel_spectrum(modes, log_dt, length):
    mode_count = modes.shape[2]
    mode_index = jnp.arange(mode_count, dtype=jnp.int32).astype(jnp.float32)[None, :, None]
    lam_re = -0.5 * jnp.exp(modes[0])[:, :, None]
    lam_im = math.pi * (mode_index + modes[1][:, :, None])
    rank_re = modes[2][:, :, None]
    rank_im = modes[3][:, :, None]
    in_re = modes[4][:, :, None]
    in_im = modes[5][:, :, None]
    out_re = modes[6][:, :, None]
    out_im = modes[7][:, :, None]
    phase = jnp.arange(length, dtype=jnp.int32).astype(jnp.float32) * (2.0 * math.pi / length)
    root_re = jnp.cos(phase)
    root_im = -jnp.sin(phase)
    two_over = (2.0 * jnp.exp(-log_dt))[:, None, None]
    rank_sq = rank_re * rank_re + rank_im * rank_im
    totals = None
    for mirror in (1.0, -1.0):
        lam_mirror = mirror * lam_im
        den_re = two_over * (1.0 - root_re) - ((1.0 + root_re) * lam_re - root_im * lam_mirror)
        den_im = -two_over * root_im - ((1.0 + root_re) * lam_mirror + root_im * lam_re)
        den_sq = den_re * den_re + den_im * den_im
        inv_re = 2.0 * den_re / den_sq
        inv_im = -2.0 * den_im / den_sq
        pairs = ((out_re * in_re + out_im * in_im, mirror * (out_re * in_im - out_im * in_re)), (out_re * rank_re + out_im * rank_im, mirror * (out_re * rank_im - out_im * rank_re)), (rank_re * in_re + rank_im * in_im, mirror * (rank_re * in_im - rank_im * in_re)), (rank_sq, 0.0 * rank_sq))
        term_list = []
        for coeff_re, coeff_im in pairs:
            term_list.append(lax.optimization_barrier(jnp.sum(coeff_re * inv_re - coeff_im * inv_im, axis=1)))
            term_list.append(lax.optimization_barrier(jnp.sum(coeff_re * inv_im + coeff_im * inv_re, axis=1)))
        totals = term_list if totals is None else [earlier + latest for earlier, latest in zip(totals, term_list)]
    cross_re, cross_im, left_re, left_im, right_re, right_im, self_re, self_im = totals
    half_re = 0.5 * (1.0 + root_re)
    half_im = 0.5 * root_im
    loop_re = 1.0 + half_re * self_re - half_im * self_im
    loop_im = half_re * self_im + half_im * self_re
    back_re = half_re * right_re - half_im * right_im
    back_im = half_re * right_im + half_im * right_re
    loop_sq = loop_re * loop_re + loop_im * loop_im
    ratio_re = (back_re * loop_re + back_im * loop_im) / loop_sq
    ratio_im = (back_im * loop_re - back_re * loop_im) / loop_sq
    return (cross_re - (left_re * ratio_re - left_im * ratio_im), cross_im - (left_re * ratio_im + left_im * ratio_re))

def full_kernel(modes, log_dt):
    block_count = MODEL_WIDTH // 16
    blocked = jnp.moveaxis(modes.reshape(8, block_count, 16, NM), 1, 0)
    cos_tab, sin_tab = phase_table(TOK_DEV, TOK_DEV, TOK_DEV, 1.0)

    def one_block(operands):
        spec_re, spec_im = kernel_spectrum(operands[0], operands[1], TOK_DEV)
        return (matmul_high(spec_re, cos_tab) - matmul_high(spec_im, sin_tab)) / TOK_DEV
    return lax.map(jax.checkpoint(one_block), (blocked, log_dt.reshape(block_count, 16))).reshape(MODEL_WIDTH, TOK_DEV)

def group_mix(normed, kernel_taps, skip_gain, bucket, filled):
    shortest = TOK_DEV // 4

    def branch_at(level):
        width = shortest * 2 ** level

        def run_branch(values):
            blocks = values.T.reshape(MODEL_WIDTH, TOK_DEV // width, width)
            signal = jnp.fft.rfft(blocks, n=2 * width, axis=-1)
            answer = jnp.fft.rfft(kernel_taps[:, :width], n=2 * width, axis=-1)[:, None, :]
            joined = jnp.fft.irfft(signal * answer, n=2 * width, axis=-1)[..., :width]
            return joined.reshape(MODEL_WIDTH, TOK_DEV).T
        return run_branch
    convolved = lax.switch(bucket, [branch_at(0), branch_at(1), branch_at(2)], normed)
    width = jnp.where(bucket == 0, shortest, jnp.where(bucket == 1, 2 * shortest, 4 * shortest))
    live = jnp.arange(TOK_DEV, dtype=jnp.int32)[:, None] < filled * width
    return jnp.where(live, convolved, 0.0) + skip_gain * normed

def forward(group_bucket, group_items, tokens, first_norm_gain, first_norm_bias, modes, log_dt, d_skip, w_a, b_a, w_b, b_b, second_norm_gain, second_norm_bias, w_up, b_up, w_down, b_down):
    normed_one = layer_norm(tokens, first_norm_gain, first_norm_bias)
    kernel_taps = full_kernel(modes, log_dt)
    per_group = normed_one.reshape(N_DP, TOK_DEV, MODEL_WIDTH)

    def mix_group(operands):
        return group_mix(operands[0], kernel_taps, d_skip, operands[1], operands[2])
    mixed = lax.map(jax.checkpoint(mix_group), (per_group, group_bucket, group_items)).reshape(TOKENS, MODEL_WIDTH)
    acts = low(jax.nn.gelu(mixed, approximate=False))
    gate_a = low_back(matmul_high(acts, low(w_a)) + b_a)
    gate_b = low_back(matmul_high(acts, low(w_b)) + b_b)
    residual_stream = tokens + gate_a * jax.nn.sigmoid(gate_b)
    normed_two = low(layer_norm(residual_stream, second_norm_gain, second_norm_bias))
    pre_act = low_back(matmul_high(normed_two, low(w_up)) + b_up)
    hidden = low(jax.nn.gelu(pre_act, approximate=False))
    branch = low_back(matmul_high(hidden, low(w_down)) + b_down)
    return residual_stream + branch

def reference(tokens, cotangent, group_bucket, group_items, first_norm_gain, first_norm_bias, modes, log_dt, d_skip, w_a, b_a, w_b, b_b, second_norm_gain, second_norm_bias, w_up, b_up, w_down, b_down):
    floats = (tokens.astype(jnp.float32), first_norm_gain, first_norm_bias, modes, log_dt, d_skip, w_a, b_a, w_b, b_b, second_norm_gain, second_norm_bias, w_up, b_up, w_down, b_down)
    result, pullback = jax.vjp(partial(forward, group_bucket, group_items), *floats)
    grads = pullback(cotangent)
    return (result.astype(jnp.bfloat16), grads[0], grads[1], grads[2], grads[3], grads[4], grads[5], grads[6], grads[7], grads[8], grads[9], grads[10], grads[11], grads[12], grads[13], grads[14], grads[15])
```

```python
import math

import jax
import jax.numpy as jnp
import numpy as np
from jax import lax
from jax.sharding import PartitionSpec as P

MODEL_WIDTH = 512
TOK_DEV = 1024


HIGHEST = lax.Precision.HIGHEST
EPSILON = 1e-05


def product(left, right):
    return jnp.dot(left, right, preferred_element_type=jnp.float32)


def product_nt(left, right):
    return lax.dot_general(
        left, right, (((1,), (1,)), ((), ())), preferred_element_type=jnp.float32
    )


def product_tn(left, right):
    return lax.dot_general(
        left, right, (((0,), (0,)), ((), ())), preferred_element_type=jnp.float32
    )


def gelu_slope(values):
    return (
        0.5 * (1.0 + lax.erf(values * 0.7071067811865476))
        + values * jnp.exp(-0.5 * values * values) * 0.3989422804014327
    )


def half_angles(length):
    angle = np.arange(length // 2 + 1, dtype=np.float64) * (math.pi / length)
    cosine, sine = np.cos(angle), np.sin(angle)
    cosine[-1] = 0.0
    return cosine.astype(np.float32), sine.astype(np.float32)


def inverse_tables(length):
    freq = np.arange(length // 2 + 1)
    turn = (freq[:, None] * np.arange(length)[None, :]) % length * (2.0 * math.pi / length)
    weight = np.where((freq == 0) | (freq == length // 2), 1.0, 2.0)[:, None] / length
    return (weight * np.cos(turn)).astype(np.float32), (weight * np.sin(turn)).astype(np.float32)


def high_einsum(form, left, right):
    return jnp.einsum(form, left, right, precision=HIGHEST)


def ssm_kernel(modes, log_dt):
    cos_h, sin_h = half_angles(TOK_DEV)
    index = jnp.arange(modes.shape[2], dtype=jnp.int32).astype(jnp.float32)
    lam_re = -0.5 * jnp.exp(modes[0])
    lam_im = math.pi * (index + modes[1])
    rank_re, rank_im, in_re, in_im, out_re, out_im = (modes[i] for i in range(2, 8))
    sigma = (2.0 * jnp.exp(-log_dt))[:, None]

    def points(values):
        return values.T[:, None, :]

    den_re = points(lam_re * lam_re + lam_im * lam_im) * (cos_h * cos_h)[:, None] - (
        sigma * sigma
    ).T * (sin_h * sin_h)[:, None]
    den_im = points(-2.0 * sigma * lam_re) * (sin_h * cos_h)[:, None]
    den_sq = den_re * den_re + den_im * den_im
    inv_re = den_re / den_sq
    inv_im = -den_im / den_sq
    sums = []
    for real, imag in (
        (out_re * in_re + out_im * in_im, out_re * in_im - out_im * in_re),
        (out_re * rank_re + out_im * rank_im, out_re * rank_im - out_im * rank_re),
        (rank_re * in_re + rank_im * in_im, rank_re * in_im - rank_im * in_re),
        (rank_re * rank_re + rank_im * rank_im, jnp.zeros_like(rank_re)),
    ):
        turned = points(real * lam_re + imag * lam_im)
        real = points(real)
        p_re, p_im = jnp.sum(real * inv_re, axis=0), jnp.sum(real * inv_im, axis=0)
        q_re, q_im = jnp.sum(turned * inv_re, axis=0), jnp.sum(turned * inv_im, axis=0)
        sine = sin_h[:, None] * sigma.T
        sums.append((-sine * p_im - cos_h[:, None] * q_re, sine * p_re - cos_h[:, None] * q_im))
    (cross_re, cross_im), (left_re, left_im), (right_re, right_im), (self_re, self_im) = sums
    twice = 2.0 * cos_h[:, None]
    loop_re, loop_im = 1.0 + twice * self_re, twice * self_im
    back_re, back_im = twice * right_re, twice * right_im
    loop_sq = loop_re * loop_re + loop_im * loop_im
    ratio_re = (back_re * loop_re + back_im * loop_im) / loop_sq
    ratio_im = (back_im * loop_re - back_re * loop_im) / loop_sq
    part_re = cross_re - (left_re * ratio_re - left_im * ratio_im)
    part_im = cross_im - (left_re * ratio_im + left_im * ratio_re)
    spec_re = 2.0 * (cos_h[:, None] * part_re - sin_h[:, None] * part_im)
    spec_im = 2.0 * (cos_h[:, None] * part_im + sin_h[:, None] * part_re)
    cos_tab, sin_tab = inverse_tables(TOK_DEV)
    return high_einsum("kl,kc->lc", cos_tab, spec_re) - high_einsum("kl,kc->lc", sin_tab, spec_im)


BLOCK = 128
BLOCKS = TOK_DEV // BLOCK
FIRST = 2 * BLOCKS
KEPT = FIRST // 2 + 1


def transform_tables():
    length = 2 * TOK_DEV
    turn = np.arange(KEPT)[:, None] * np.arange(BLOCK)[None, :] * (2.0 * math.pi / length)
    small = np.arange(BLOCK)[:, None] * np.arange(BLOCK)[None, :] % BLOCK * (2.0 * math.pi / BLOCK)
    spots = np.stack([np.arange(BLOCKS) + np.arange(BLOCKS) // (2 << b) * (2 << b) for b in range(3)])
    angle = spots[:, None, :] * np.arange(KEPT)[None, :, None] % FIRST * (2.0 * math.pi / FIRST)
    parts = (np.cos(turn), np.sin(turn), np.cos(small), np.sin(small), np.cos(angle), np.sin(angle))
    return [part.astype(np.float32) for part in parts]


def forward_transform(blocks, cos_a, sin_a):
    cos_t, sin_t, cos_s, sin_s, _, _ = transform_tables()
    step_re = high_einsum("ka,abc->kbc", cos_a, blocks)
    step_im = -high_einsum("ka,abc->kbc", sin_a, blocks)
    turned_re = step_re * cos_t[..., None] + step_im * sin_t[..., None]
    turned_im = step_im * cos_t[..., None] - step_re * sin_t[..., None]
    both = jnp.concatenate([turned_re, turned_im], axis=1)
    matrix = np.block([[cos_s, sin_s], [-sin_s, cos_s]])
    return high_einsum("pb,kbc->kpc", matrix, both)


def inverse_transform(spectrum, cos_a, sin_a):
    cos_t, sin_t, cos_s, sin_s, _, _ = transform_tables()
    matrix = np.block([[cos_s, -sin_s], [sin_s, cos_s]])
    both = high_einsum("bp,kpc->kbc", matrix, spectrum)
    step_re, step_im = both[:, :BLOCK], both[:, BLOCK:]
    turned_re = step_re * cos_t[..., None] - step_im * sin_t[..., None]
    turned_im = step_im * cos_t[..., None] + step_re * sin_t[..., None]
    weight = np.where(np.arange(KEPT) % (KEPT - 1) == 0, 1.0, 2.0).astype(np.float32) / (2 * TOK_DEV)
    return high_einsum("ka,kbc->abc", cos_a * weight[:, None], turned_re) - high_einsum(
        "ka,kbc->abc", sin_a * weight[:, None], turned_im
    )


def multiply(left, right):
    left_re, left_im = left[:, :BLOCK], left[:, BLOCK:]
    right_re, right_im = right[:, :BLOCK], right[:, BLOCK:]
    return jnp.concatenate(
        [left_re * right_re - left_im * right_im, left_re * right_im + left_im * right_re], axis=1
    )


def mixer(normed, kernel_taps, skip_gain, bucket, filled):
    _, _, _, _, cos_a, sin_a = transform_tables()
    cos_x, sin_x = jnp.asarray(cos_a)[bucket], jnp.asarray(sin_a)[bucket]
    item_blocks = 2 << bucket
    block_id = jnp.arange(BLOCKS, dtype=jnp.int32)[:, None, None]
    taps = jnp.where(block_id < item_blocks, kernel_taps.reshape(BLOCKS, BLOCK, -1), 0.0)
    signal = forward_transform(normed.reshape(BLOCKS, BLOCK, -1), cos_x, sin_x)
    answer = forward_transform(taps, cos_a[2], sin_a[2])
    result = inverse_transform(multiply(signal, answer), cos_x, sin_x)
    result = jnp.where(block_id < filled * item_blocks, result, 0.0)
    return result.reshape(normed.shape) + skip_gain * normed


def shards(
    tokens,
    cotangent,
    group_bucket,
    group_items,
    first_norm_gain,
    first_norm_bias,
    modes,
    log_dt,
    d_skip,
    w_a,
    b_a,
    w_b,
    b_b,
    second_norm_gain,
    second_norm_bias,
    w_up,
    b_up,
    w_down,
    b_down,
):
    input_tokens = tokens.astype(jnp.float32)
    sums_in = lax.psum(
        (jnp.sum(input_tokens, axis=1), jnp.sum(input_tokens * input_tokens, axis=1)), "chan"
    )
    input_average = sums_in[0][:, None] / MODEL_WIDTH
    input_inverse_deviation = lax.rsqrt(
        sums_in[1][:, None] / MODEL_WIDTH - input_average * input_average + EPSILON
    )
    input_standardized = (input_tokens - input_average) * input_inverse_deviation
    input_normalized = input_standardized * first_norm_gain + first_norm_bias
    level = group_bucket[0]
    filled = group_items[0]
    kernel_taps, kernel_back = jax.vjp(ssm_kernel, modes, log_dt)

    def local_mix(values, taps_now, skip_gain):
        return mixer(values, taps_now, skip_gain, level, filled)

    mixed, mix_back = jax.vjp(local_mix, input_normalized, kernel_taps, d_skip)
    acts_low = jax.nn.gelu(mixed, approximate=False).astype(jnp.bfloat16)
    wa_full, wb_full, up_full, down_full = (
        lax.all_gather(w_a.astype(jnp.bfloat16), "dp", axis=0, tiled=True),
        lax.all_gather(w_b.astype(jnp.bfloat16), "dp", axis=0, tiled=True),
        lax.all_gather(w_up.astype(jnp.bfloat16), "dp", axis=0, tiled=True),
        lax.all_gather(w_down.astype(jnp.bfloat16), "dp", axis=1, tiled=True),
    )
    acts_full = lax.all_gather(acts_low, "chan", axis=1, tiled=True)
    gate_a = product(acts_full, wa_full) + b_a
    gate_b = product(acts_full, wb_full) + b_b
    gate_sig = jax.nn.sigmoid(gate_b)
    residual_stream = input_tokens + gate_a * gate_sig
    sums_mid = lax.psum(
        (jnp.sum(residual_stream, axis=1), jnp.sum(residual_stream * residual_stream, axis=1)),
        "chan",
    )
    middle_average = sums_mid[0][:, None] / MODEL_WIDTH
    middle_inverse_deviation = lax.rsqrt(
        sums_mid[1][:, None] / MODEL_WIDTH - middle_average * middle_average + EPSILON
    )
    middle_standardized = (residual_stream - middle_average) * middle_inverse_deviation
    middle_reduced = (middle_standardized * second_norm_gain + second_norm_bias).astype(
        jnp.bfloat16
    )
    mid_full = lax.all_gather(middle_reduced, "chan", axis=1, tiled=True)
    pre_act = product(mid_full, up_full) + b_up
    hidden_low = jax.nn.gelu(pre_act, approximate=False).astype(jnp.bfloat16)
    branch = (
        lax.psum_scatter(product(hidden_low, down_full), "chan", scatter_dimension=1, tiled=True)
        + b_down
    )
    output = (residual_stream + branch).astype(jnp.bfloat16)
    grad_f = cotangent.astype(jnp.bfloat16)
    grad_b_down = jnp.sum(grad_f.astype(jnp.float32), axis=0)
    grad_f_full = lax.all_gather(grad_f, "chan", axis=1, tiled=True)
    grad_w_down = product_tn(hidden_low, grad_f_full)
    grad_pre = (product_nt(grad_f_full, down_full) * gelu_slope(pre_act)).astype(jnp.bfloat16)
    grad_b_up = jnp.sum(grad_pre.astype(jnp.float32), axis=0)
    grad_w_up = product_tn(mid_full, grad_pre)
    middle_gradient = lax.psum_scatter(
        product_nt(grad_pre, up_full), "chan", scatter_dimension=1, tiled=True
    )
    second_norm_gain_gradient = jnp.sum(middle_gradient * middle_standardized, axis=0)
    grad_ln2_bias = jnp.sum(middle_gradient, axis=0)
    middle_rescaled = middle_gradient * second_norm_gain
    middle_backward = lax.psum(
        (jnp.sum(middle_rescaled, axis=1), jnp.sum(middle_rescaled * middle_standardized, axis=1)),
        "chan",
    )
    grad_resid = cotangent + middle_inverse_deviation * (
        middle_rescaled
        - middle_backward[0][:, None] / MODEL_WIDTH
        - middle_standardized * middle_backward[1][:, None] / MODEL_WIDTH
    )
    grad_a = (grad_resid * gate_sig).astype(jnp.bfloat16)
    grad_b = (grad_resid * gate_a * gate_sig * (1.0 - gate_sig)).astype(jnp.bfloat16)
    grad_b_a = jnp.sum(grad_a.astype(jnp.float32), axis=0)
    grad_b_b = jnp.sum(grad_b.astype(jnp.float32), axis=0)
    grad_w_a = product_tn(acts_full, grad_a)
    grad_w_b = product_tn(acts_full, grad_b)
    grad_acts = lax.psum_scatter(
        product_nt(grad_a, wa_full) + product_nt(grad_b, wb_full),
        "chan",
        scatter_dimension=1,
        tiled=True,
    )
    grad_mixed = grad_acts * gelu_slope(mixed)
    normalized_gradient, grad_kernel, grad_skip = mix_back(grad_mixed)
    grad_modes, grad_log_dt = kernel_back(grad_kernel)
    first_norm_gain_gradient = jnp.sum(normalized_gradient * input_standardized, axis=0)
    grad_ln1_bias = jnp.sum(normalized_gradient, axis=0)
    input_rescaled = normalized_gradient * first_norm_gain
    input_backward = lax.psum(
        (jnp.sum(input_rescaled, axis=1), jnp.sum(input_rescaled * input_standardized, axis=1)),
        "chan",
    )
    grad_tokens = grad_resid + input_inverse_deviation * (
        input_rescaled
        - input_backward[0][:, None] / MODEL_WIDTH
        - input_standardized * input_backward[1][:, None] / MODEL_WIDTH
    )
    grad_w_a, grad_w_b, grad_w_up, grad_w_down = (
        lax.psum_scatter(grad_w_a, "dp", scatter_dimension=0, tiled=True),
        lax.psum_scatter(grad_w_b, "dp", scatter_dimension=0, tiled=True),
        lax.psum_scatter(grad_w_up, "dp", scatter_dimension=0, tiled=True),
        lax.psum_scatter(grad_w_down, "dp", scatter_dimension=1, tiled=True),
    )
    (
        first_norm_gain_gradient,
        grad_ln1_bias,
        grad_modes,
        grad_log_dt,
        grad_skip,
        grad_b_a,
        grad_b_b,
        second_norm_gain_gradient,
        grad_ln2_bias,
        grad_b_up,
        grad_b_down,
    ) = lax.psum(
        (
            first_norm_gain_gradient,
            grad_ln1_bias,
            grad_modes,
            grad_log_dt,
            grad_skip,
            grad_b_a,
            grad_b_b,
            second_norm_gain_gradient,
            grad_ln2_bias,
            grad_b_up,
            grad_b_down,
        ),
        "dp",
    )
    return (
        output,
        grad_tokens,
        first_norm_gain_gradient,
        grad_ln1_bias,
        grad_modes,
        grad_log_dt,
        grad_skip,
        grad_w_a,
        grad_b_a,
        grad_w_b,
        grad_b_b,
        second_norm_gain_gradient,
        grad_ln2_bias,
        grad_w_up,
        grad_b_up,
        grad_w_down,
        grad_b_down,
    )


def solution(mesh):
    return jax.shard_map(
        shards,
        mesh=mesh,
        in_specs=(
            P("dp", "chan"),
            P("dp", "chan"),
            P("dp"),
            P("dp"),
            P("chan"),
            P("chan"),
            P(None, "chan", None),
            P("chan"),
            P("chan"),
            P("dp", "chan"),
            P("chan"),
            P("dp", "chan"),
            P("chan"),
            P("chan"),
            P("chan"),
            P("dp", "chan"),
            P("chan"),
            P("chan", "dp"),
            P("chan"),
        ),
        out_specs=(
            P("dp", "chan"),
            P("dp", "chan"),
            P("chan"),
            P("chan"),
            P(None, "chan", None),
            P("chan"),
            P("chan"),
            P("dp", "chan"),
            P("chan"),
            P("dp", "chan"),
            P("chan"),
            P("chan"),
            P("chan"),
            P("dp", "chan"),
            P("chan"),
            P("chan", "dp"),
            P("chan"),
        ),
        check_vma=False,
    )
```

```python
import math

import jax
import jax.numpy as jnp
import ml_dtypes
import numpy as np
from jax import lax
from jax.experimental import pallas as pl
from jax.experimental.pallas import tpu as pltpu
from jax.sharding import PartitionSpec as P

MODEL_WIDTH = 512
TOK_DEV = 1024


HIGHEST = lax.Precision.HIGHEST
EPSILON = 1e-05


def product(left, right):
    return jnp.dot(left, right, preferred_element_type=jnp.float32)


def product_nt(left, right):
    return lax.dot_general(
        left, right, (((1,), (1,)), ((), ())), preferred_element_type=jnp.float32
    )


def product_tn(left, right):
    return lax.dot_general(
        left, right, (((0,), (0,)), ((), ())), preferred_element_type=jnp.float32
    )


def gelu_slope(values):
    return (
        0.5 * (1.0 + lax.erf(values * 0.7071067811865476))
        + values * jnp.exp(-0.5 * values * values) * 0.3989422804014327
    )


def half_angles(length):
    angle = np.arange(length // 2 + 1, dtype=np.float64) * (math.pi / length)
    cosine, sine = np.cos(angle), np.sin(angle)
    cosine[-1] = 0.0
    return cosine.astype(np.float32), sine.astype(np.float32)


def inverse_tables(length):
    freq = np.arange(length // 2 + 1)
    turn = (freq[:, None] * np.arange(length)[None, :]) % length * (2.0 * math.pi / length)
    weight = np.where((freq == 0) | (freq == length // 2), 1.0, 2.0)[:, None] / length
    return (weight * np.cos(turn)).astype(np.float32), (weight * np.sin(turn)).astype(np.float32)


def high_einsum(form, left, right):
    return jnp.einsum(form, left, right, precision=HIGHEST)


def ssm_kernel(modes, log_dt):
    cos_h, sin_h = half_angles(TOK_DEV)
    index = jnp.arange(modes.shape[2], dtype=jnp.int32).astype(jnp.float32)
    lam_re = -0.5 * jnp.exp(modes[0])
    lam_im = math.pi * (index + modes[1])
    rank_re, rank_im, in_re, in_im, out_re, out_im = (modes[i] for i in range(2, 8))
    sigma = (2.0 * jnp.exp(-log_dt))[:, None]

    def points(values):
        return values.T[:, None, :]

    den_re = points(lam_re * lam_re + lam_im * lam_im) * (cos_h * cos_h)[:, None] - (
        sigma * sigma
    ).T * (sin_h * sin_h)[:, None]
    den_im = points(-2.0 * sigma * lam_re) * (sin_h * cos_h)[:, None]
    den_sq = den_re * den_re + den_im * den_im
    inv_re = den_re / den_sq
    inv_im = -den_im / den_sq
    sums = []
    for real, imag in (
        (out_re * in_re + out_im * in_im, out_re * in_im - out_im * in_re),
        (out_re * rank_re + out_im * rank_im, out_re * rank_im - out_im * rank_re),
        (rank_re * in_re + rank_im * in_im, rank_re * in_im - rank_im * in_re),
        (rank_re * rank_re + rank_im * rank_im, jnp.zeros_like(rank_re)),
    ):
        turned = points(real * lam_re + imag * lam_im)
        real = points(real)
        p_re, p_im = jnp.sum(real * inv_re, axis=0), jnp.sum(real * inv_im, axis=0)
        q_re, q_im = jnp.sum(turned * inv_re, axis=0), jnp.sum(turned * inv_im, axis=0)
        sine = sin_h[:, None] * sigma.T
        sums.append((-sine * p_im - cos_h[:, None] * q_re, sine * p_re - cos_h[:, None] * q_im))
    (cross_re, cross_im), (left_re, left_im), (right_re, right_im), (self_re, self_im) = sums
    twice = 2.0 * cos_h[:, None]
    loop_re, loop_im = 1.0 + twice * self_re, twice * self_im
    back_re, back_im = twice * right_re, twice * right_im
    loop_sq = loop_re * loop_re + loop_im * loop_im
    ratio_re = (back_re * loop_re + back_im * loop_im) / loop_sq
    ratio_im = (back_im * loop_re - back_re * loop_im) / loop_sq
    part_re = cross_re - (left_re * ratio_re - left_im * ratio_im)
    part_im = cross_im - (left_re * ratio_im + left_im * ratio_re)
    spec_re = 2.0 * (cos_h[:, None] * part_re - sin_h[:, None] * part_im)
    spec_im = 2.0 * (cos_h[:, None] * part_im + sin_h[:, None] * part_re)
    cos_tab, sin_tab = inverse_tables(TOK_DEV)
    return high_einsum("kl,kc->lc", cos_tab, spec_re) - high_einsum("kl,kc->lc", sin_tab, spec_im)


BLOCK = 128
BLOCKS = TOK_DEV // BLOCK
FIRST = 2 * BLOCKS
KEPT = FIRST // 2 + 1


def transform_tables():
    length = 2 * TOK_DEV
    turn = np.arange(KEPT)[:, None] * np.arange(BLOCK)[None, :] * (2.0 * math.pi / length)
    small = np.arange(BLOCK)[:, None] * np.arange(BLOCK)[None, :] % BLOCK * (2.0 * math.pi / BLOCK)
    spots = np.stack([np.arange(BLOCKS) + np.arange(BLOCKS) // (2 << b) * (2 << b) for b in range(3)])
    angle = spots[:, None, :] * np.arange(KEPT)[None, :, None] % FIRST * (2.0 * math.pi / FIRST)
    parts = (np.cos(turn), np.sin(turn), np.cos(small), np.sin(small), np.cos(angle), np.sin(angle))
    return [part.astype(np.float32) for part in parts]


def forward_transform(blocks, cos_a, sin_a):
    cos_t, sin_t, cos_s, sin_s, _, _ = transform_tables()
    step_re = high_einsum("ka,abc->kbc", cos_a, blocks)
    step_im = -high_einsum("ka,abc->kbc", sin_a, blocks)
    turned_re = step_re * cos_t[..., None] + step_im * sin_t[..., None]
    turned_im = step_im * cos_t[..., None] - step_re * sin_t[..., None]
    both = jnp.concatenate([turned_re, turned_im], axis=1)
    matrix = np.block([[cos_s, sin_s], [-sin_s, cos_s]])
    return high_einsum("pb,kbc->kpc", matrix, both)


def inverse_transform(spectrum, cos_a, sin_a):
    cos_t, sin_t, cos_s, sin_s, _, _ = transform_tables()
    matrix = np.block([[cos_s, -sin_s], [sin_s, cos_s]])
    both = high_einsum("bp,kpc->kbc", matrix, spectrum)
    step_re, step_im = both[:, :BLOCK], both[:, BLOCK:]
    turned_re = step_re * cos_t[..., None] - step_im * sin_t[..., None]
    turned_im = step_im * cos_t[..., None] + step_re * sin_t[..., None]
    weight = np.where(np.arange(KEPT) % (KEPT - 1) == 0, 1.0, 2.0).astype(np.float32) / (2 * TOK_DEV)
    return high_einsum("ka,kbc->abc", cos_a * weight[:, None], turned_re) - high_einsum(
        "ka,kbc->abc", sin_a * weight[:, None], turned_im
    )


def multiply(left, right):
    left_re, left_im = left[:, :BLOCK], left[:, BLOCK:]
    right_re, right_im = right[:, :BLOCK], right[:, BLOCK:]
    return jnp.concatenate(
        [left_re * right_re - left_im * right_im, left_re * right_im + left_im * right_re], axis=1
    )


def mixer(normed, kernel_taps, skip_gain, bucket, filled):
    _, _, _, _, cos_a, sin_a = transform_tables()
    cos_x, sin_x = jnp.asarray(cos_a)[bucket], jnp.asarray(sin_a)[bucket]
    item_blocks = 2 << bucket
    block_id = jnp.arange(BLOCKS, dtype=jnp.int32)[:, None, None]
    taps = jnp.where(block_id < item_blocks, kernel_taps.reshape(BLOCKS, BLOCK, -1), 0.0)
    signal = forward_transform(normed.reshape(BLOCKS, BLOCK, -1), cos_x, sin_x)
    answer = forward_transform(taps, cos_a[2], sin_a[2])
    result = inverse_transform(multiply(signal, answer), cos_x, sin_x)
    result = jnp.where(block_id < filled * item_blocks, result, 0.0)
    return result.reshape(normed.shape) + skip_gain * normed


def shards(
    tokens,
    cotangent,
    group_bucket,
    group_items,
    first_norm_gain,
    first_norm_bias,
    modes,
    log_dt,
    d_skip,
    w_a,
    b_a,
    w_b,
    b_b,
    second_norm_gain,
    second_norm_bias,
    w_up,
    b_up,
    w_down,
    b_down,
):
    input_tokens = tokens.astype(jnp.float32)
    sums_in = lax.psum(
        (jnp.sum(input_tokens, axis=1), jnp.sum(input_tokens * input_tokens, axis=1)), "chan"
    )
    input_average = sums_in[0][:, None] / MODEL_WIDTH
    input_inverse_deviation = lax.rsqrt(
        sums_in[1][:, None] / MODEL_WIDTH - input_average * input_average + EPSILON
    )
    input_standardized = (input_tokens - input_average) * input_inverse_deviation
    input_normalized = input_standardized * first_norm_gain + first_norm_bias
    level = group_bucket[0]
    filled = group_items[0]
    kernel_taps, kernel_back = jax.vjp(ssm_kernel, modes, log_dt)

    def local_mix(values, taps_now, skip_gain):
        return mixer(values, taps_now, skip_gain, level, filled)

    mixed, mix_back = jax.vjp(local_mix, input_normalized, kernel_taps, d_skip)
    acts_low = jax.nn.gelu(mixed, approximate=False).astype(jnp.bfloat16)
    wa_full, wb_full, up_full, down_full = (
        lax.all_gather(w_a.astype(jnp.bfloat16), "dp", axis=0, tiled=True),
        lax.all_gather(w_b.astype(jnp.bfloat16), "dp", axis=0, tiled=True),
        lax.all_gather(w_up.astype(jnp.bfloat16), "dp", axis=0, tiled=True),
        lax.all_gather(w_down.astype(jnp.bfloat16), "dp", axis=1, tiled=True),
    )
    acts_full = lax.all_gather(acts_low, "chan", axis=1, tiled=True)
    gate_a = product(acts_full, wa_full) + b_a
    gate_b = product(acts_full, wb_full) + b_b
    gate_sig = jax.nn.sigmoid(gate_b)
    residual_stream = input_tokens + gate_a * gate_sig
    sums_mid = lax.psum(
        (jnp.sum(residual_stream, axis=1), jnp.sum(residual_stream * residual_stream, axis=1)),
        "chan",
    )
    middle_average = sums_mid[0][:, None] / MODEL_WIDTH
    middle_inverse_deviation = lax.rsqrt(
        sums_mid[1][:, None] / MODEL_WIDTH - middle_average * middle_average + EPSILON
    )
    middle_standardized = (residual_stream - middle_average) * middle_inverse_deviation
    middle_reduced = (middle_standardized * second_norm_gain + second_norm_bias).astype(
        jnp.bfloat16
    )
    mid_full = lax.all_gather(middle_reduced, "chan", axis=1, tiled=True)
    pre_act = product(mid_full, up_full) + b_up
    hidden_low = jax.nn.gelu(pre_act, approximate=False).astype(jnp.bfloat16)
    branch = (
        lax.psum_scatter(product(hidden_low, down_full), "chan", scatter_dimension=1, tiled=True)
        + b_down
    )
    output = (residual_stream + branch).astype(jnp.bfloat16)
    grad_f = cotangent.astype(jnp.bfloat16)
    grad_b_down = jnp.sum(grad_f.astype(jnp.float32), axis=0)
    grad_f_full = lax.all_gather(grad_f, "chan", axis=1, tiled=True)
    grad_w_down = product_tn(hidden_low, grad_f_full)
    grad_pre = (product_nt(grad_f_full, down_full) * gelu_slope(pre_act)).astype(jnp.bfloat16)
    grad_b_up = jnp.sum(grad_pre.astype(jnp.float32), axis=0)
    grad_w_up = product_tn(mid_full, grad_pre)
    middle_gradient = lax.psum_scatter(
        product_nt(grad_pre, up_full), "chan", scatter_dimension=1, tiled=True
    )
    second_norm_gain_gradient = jnp.sum(middle_gradient * middle_standardized, axis=0)
    grad_ln2_bias = jnp.sum(middle_gradient, axis=0)
    middle_rescaled = middle_gradient * second_norm_gain
    middle_backward = lax.psum(
        (jnp.sum(middle_rescaled, axis=1), jnp.sum(middle_rescaled * middle_standardized, axis=1)),
        "chan",
    )
    grad_resid = cotangent + middle_inverse_deviation * (
        middle_rescaled
        - middle_backward[0][:, None] / MODEL_WIDTH
        - middle_standardized * middle_backward[1][:, None] / MODEL_WIDTH
    )
    grad_a = (grad_resid * gate_sig).astype(jnp.bfloat16)
    grad_b = (grad_resid * gate_a * gate_sig * (1.0 - gate_sig)).astype(jnp.bfloat16)
    grad_b_a = jnp.sum(grad_a.astype(jnp.float32), axis=0)
    grad_b_b = jnp.sum(grad_b.astype(jnp.float32), axis=0)
    grad_w_a = product_tn(acts_full, grad_a)
    grad_w_b = product_tn(acts_full, grad_b)
    grad_acts = lax.psum_scatter(
        product_nt(grad_a, wa_full) + product_nt(grad_b, wb_full),
        "chan",
        scatter_dimension=1,
        tiled=True,
    )
    grad_mixed = grad_acts * gelu_slope(mixed)
    normalized_gradient, grad_kernel, grad_skip = mix_back(grad_mixed)
    grad_modes, grad_log_dt = kernel_back(grad_kernel)
    first_norm_gain_gradient = jnp.sum(normalized_gradient * input_standardized, axis=0)
    grad_ln1_bias = jnp.sum(normalized_gradient, axis=0)
    input_rescaled = normalized_gradient * first_norm_gain
    input_backward = lax.psum(
        (jnp.sum(input_rescaled, axis=1), jnp.sum(input_rescaled * input_standardized, axis=1)),
        "chan",
    )
    grad_tokens = grad_resid + input_inverse_deviation * (
        input_rescaled
        - input_backward[0][:, None] / MODEL_WIDTH
        - input_standardized * input_backward[1][:, None] / MODEL_WIDTH
    )
    grad_w_a, grad_w_b, grad_w_up, grad_w_down = (
        lax.psum_scatter(grad_w_a, "dp", scatter_dimension=0, tiled=True),
        lax.psum_scatter(grad_w_b, "dp", scatter_dimension=0, tiled=True),
        lax.psum_scatter(grad_w_up, "dp", scatter_dimension=0, tiled=True),
        lax.psum_scatter(grad_w_down, "dp", scatter_dimension=1, tiled=True),
    )
    (
        first_norm_gain_gradient,
        grad_ln1_bias,
        grad_modes,
        grad_log_dt,
        grad_skip,
        grad_b_a,
        grad_b_b,
        second_norm_gain_gradient,
        grad_ln2_bias,
        grad_b_up,
        grad_b_down,
    ) = lax.psum(
        (
            first_norm_gain_gradient,
            grad_ln1_bias,
            grad_modes,
            grad_log_dt,
            grad_skip,
            grad_b_a,
            grad_b_b,
            second_norm_gain_gradient,
            grad_ln2_bias,
            grad_b_up,
            grad_b_down,
        ),
        "dp",
    )
    return (
        output,
        grad_tokens,
        first_norm_gain_gradient,
        grad_ln1_bias,
        grad_modes,
        grad_log_dt,
        grad_skip,
        grad_w_a,
        grad_b_a,
        grad_w_b,
        grad_b_b,
        second_norm_gain_gradient,
        grad_ln2_bias,
        grad_w_up,
        grad_b_up,
        grad_w_down,
        grad_b_down,
    )


LANES = 128
HALF = 64
PAIRS = 4
ROWS = 128
N_CHAN = 8
WIDE = 640
MESH = pl.DeviceIdType.MESH
F32 = jnp.float32
BF16 = jnp.bfloat16


def split_two(matrix):
    high = matrix.astype(ml_dtypes.bfloat16)
    low = (matrix - high.astype(np.float64)).astype(ml_dtypes.bfloat16)
    return np.concatenate([high, low], axis=1)


def lane_rows(values_low, values_high):
    return np.repeat(np.stack([values_low, values_high], -1), HALF, axis=-1)


def mixer_tables():
    line = np.arange(ROWS)
    small = np.outer(line, line) % ROWS * (2.0 * math.pi / ROWS)
    cos_s, sin_s = np.cos(small), np.sin(small)
    forward = np.block([[cos_s, sin_s], [-sin_s, cos_s]])
    real = np.zeros((2 * ROWS, 2 * ROWS))
    for row in range(HALF):
        weight = 1.0 if row == 0 else 2.0
        turn = 2.0 * math.pi / ROWS * row * line
        real[:ROWS, row] = weight * np.cos(turn)
        real[:ROWS, ROWS + row] = -weight * np.sin(turn)
        turn = 2.0 * math.pi / TOK_DEV * (4 + 8 * row) * line
        real[ROWS:, HALF + row] = 2.0 * np.cos(turn)
        real[ROWS:, ROWS + HALF + row] = -2.0 * np.sin(turn)
    mats = np.stack([split_two(m) for m in (forward, forward.T, real, real.T)])

    twiddle = []
    for pair in range(5):
        turn = np.stack([line * k * (math.pi / TOK_DEV) for k in (2 * pair, 2 * pair + 1)])
        twiddle += [lane_rows(np.cos(turn[0]), np.cos(turn[1])), lane_rows(np.sin(turn[0]), np.sin(turn[1]))]
    for first, second in ((1, 2), (3, 0)):
        turn = np.stack([line * k * (2.0 * math.pi / TOK_DEV) for k in (first, second)])
        twiddle += [lane_rows(np.cos(turn[0]), np.cos(turn[1])), lane_rows(np.sin(turn[0]), np.sin(turn[1]))]

    def forward_rows(coef, pairs):
        out = []
        for low, high in pairs:
            for part in range(2):
                for j in range(PAIRS):
                    out.append(lane_rows(coef(2 * j, low, part), coef(2 * j + 1, high, part)))
                for j in range(PAIRS):
                    out.append(lane_rows(coef(2 * j, high, part), coef(2 * j + 1, low, part)))
        return np.stack(out)

    def inverse_rows(coef, pairs):
        out = []
        for low, high in pairs:
            for part in range(2):
                for j in range(PAIRS):
                    out.append(lane_rows(coef(2 * j, low, part), coef(2 * j + 1, high, part)))
                for j in range(PAIRS):
                    out.append(lane_rows(coef(2 * j + 1, low, part), coef(2 * j, high, part)))
        return np.stack(out)

    levels = []
    pairs = [(2 * p, 2 * p + 1) for p in range(5)]
    for level in range(3):
        item = 2 << level

        def angle(block, k):
            return 2.0 * math.pi / 16 * ((block + block // item * item) * k % 16)

        def fwd(block, k, part):
            if k > 8:
                return np.zeros(())
            return np.cos(angle(block, k)) if part == 0 else -np.sin(angle(block, k))

        def inv(block, k, part):
            weight = (1.0 if k in (0, 8) else 2.0) / (2 * TOK_DEV)
            return weight * fwd(block, k, part)

        levels.append(np.concatenate([forward_rows(fwd, pairs), inverse_rows(inv, pairs)]))

    def taps(block, k, part):
        if k == 0:
            return np.asarray((1.0 if part == 0 else (-1.0) ** block) / TOK_DEV)
        turn = 2.0 * math.pi / 8 * (block * k % 8)
        return np.asarray((np.cos(turn) if part == 0 else -np.sin(turn)) * 2.0 / TOK_DEV)

    tap_pairs = [(1, 2), (3, 0)]
    taps_back = forward_rows(taps, tap_pairs)
    taps_rows = inverse_rows(taps, tap_pairs)
    freq_even = np.where(line < HALF, 8 * line, 4 + 8 * (line - HALF))
    half_angle = np.stack(
        [lane_rows(1 + 8 * line, 2 + 8 * line), lane_rows(3 + 8 * line, freq_even)]
    ) * (math.pi / TOK_DEV)
    wave = np.stack([np.cos(half_angle), np.sin(half_angle)])
    return (
        mats,
        np.stack(twiddle).astype(np.float32),
        np.stack(levels).astype(np.float32),
        np.concatenate([levels[2], taps_rows, taps_back]).astype(np.float32),
        wave.astype(np.float32),
    )


def low_lanes(rows):
    return lax.broadcasted_iota(jnp.int32, (rows, LANES), 1) < HALF


def turn_half(values):
    return pltpu.roll(values, HALF, 1)


def split_pair(values):
    upper, lower = values[:HALF], values[HALF:]
    mask = low_lanes(HALF)
    return jnp.where(mask, upper, turn_half(lower)), jnp.where(mask, turn_half(upper), lower)


def join_pair(first, second):
    mask = low_lanes(HALF)
    return jnp.concatenate(
        [jnp.where(mask, first, turn_half(second)), jnp.where(mask, turn_half(first), second)], axis=0
    )


def interleave(first, second):
    mask = low_lanes(first.shape[0])
    return jnp.where(mask, first, turn_half(second)), jnp.where(mask, turn_half(first), second)


def fold(values):
    return values + turn_half(values)


def normal_parts(values):
    cumulative = 0.5 * (1.0 + lax.erf(values * 0.7071067811865476))
    density = jnp.exp(-0.5 * values * values) * 0.3989422804014327
    return cumulative, density


def column_sum(values):
    return jnp.sum(values, axis=0, keepdims=True)


def dot_nt(left, right):
    return lax.dot_general(left, right, (((1,), (1,)), ((), ())), preferred_element_type=F32)


def dot_nn(left, right):
    return jnp.dot(left, right, preferred_element_type=F32)


def store_split(ref, row, lane, values):
    high = values.astype(BF16)
    place = (pl.ds(row, values.shape[0]), pl.ds(lane, values.shape[1]))
    ref[(0,) + place] = high
    ref[(1,) + place] = (values - high.astype(F32)).astype(BF16)


def split_product(mat_ref, which, rhs_ref, lane, width):
    high = mat_ref[which, :, 0:256]
    low = mat_ref[which, :, 256:512]
    rhs_high = rhs_ref[0, :, lane : lane + width]
    return dot_nn(high, rhs_high) + dot_nn(high, rhs_ref[1, :, lane : lane + width]) + dot_nn(low, rhs_high)


CHUNK = 32


def over_chunks(body, size=CHUNK):
    def step(index, carry):
        body(pl.multiple_of(index * size, size))
        return carry

    lax.fori_loop(0, ROWS // size, step, 0)


def spread_pairs(src, coef_ref, base, twiddle_ref, twiddle_base, pairs, rhs_ref):
    def body(row):
        rows = pl.ds(row, CHUNK)
        blocks = [src(j, rows) for j in range(PAIRS)]
        for pair in range(pairs):
            parts = []
            for part in range(2):
                at = base + (pair * 2 + part) * 8
                straight = sum(blocks[j] * coef_ref[at + j : at + j + 1, :] for j in range(PAIRS))
                crossed = sum(blocks[j] * coef_ref[at + 4 + j : at + 5 + j, :] for j in range(PAIRS))
                parts.append(straight + turn_half(crossed))
            cosine = twiddle_ref[twiddle_base + 2 * pair, rows, :]
            sine = twiddle_ref[twiddle_base + 2 * pair + 1, rows, :]
            store_split(rhs_ref, row, pair * LANES, parts[0] * cosine + parts[1] * sine)
            store_split(rhs_ref, row + ROWS, pair * LANES, parts[1] * cosine - parts[0] * sine)

    over_chunks(body)


def gather_pairs(values_ref, coef_ref, base, twiddle_ref, twiddle_base, pairs, store):
    def body(row):
        rows = pl.ds(row, CHUNK)
        straight, crossed = [0.0] * PAIRS, [0.0] * PAIRS
        for pair in range(pairs):
            lanes = slice(pair * LANES, (pair + 1) * LANES)
            real, imag = values_ref[rows, lanes], values_ref[pl.ds(row + ROWS, CHUNK), lanes]
            cosine = twiddle_ref[twiddle_base + 2 * pair, rows, :]
            sine = twiddle_ref[twiddle_base + 2 * pair + 1, rows, :]
            for part, value in enumerate((real * cosine - imag * sine, imag * cosine + real * sine)):
                at = base + (pair * 2 + part) * 8
                for j in range(PAIRS):
                    straight[j] = straight[j] + value * coef_ref[at + j : at + j + 1, :]
                    crossed[j] = crossed[j] + value * coef_ref[at + 4 + j : at + 5 + j, :]
        for j in range(PAIRS):
            store(j, rows, straight[j] + turn_half(crossed[j]))

    over_chunks(body)


GROUPS = ((0, 256), (256, 256), (512, 128))


def transform_into(dst_ref, mat_ref, which, rhs_ref, groups=GROUPS):
    for lane, width in groups:
        dst_ref[:, lane : lane + width] = split_product(mat_ref, which, rhs_ref, lane, width)


def multiply_spectra(left_ref, right_ref, rhs_ref, conjugate):
    def body(row):
        top, bottom = pl.ds(row, CHUNK), pl.ds(row + ROWS, CHUNK)
        for pair in range(5):
            lanes = slice(pair * LANES, (pair + 1) * LANES)
            a_re, a_im = left_ref[top, lanes], left_ref[bottom, lanes]
            b_re, b_im = right_ref[top, lanes], right_ref[bottom, lanes]
            if conjugate:
                out_re, out_im = a_re * b_re + a_im * b_im, a_re * b_im - a_im * b_re
            else:
                out_re, out_im = a_re * b_re - a_im * b_im, a_re * b_im + a_im * b_re
            store_split(rhs_ref, row, pair * LANES, out_re)
            store_split(rhs_ref, row + ROWS, pair * LANES, out_im)

    over_chunks(body)


def pair_terms(modes_ref):
    rank_re, rank_im, in_re, in_im, out_re, out_im = (modes_ref[i] for i in range(2, 8))
    return (
        (out_re * in_re + out_im * in_im, out_re * in_im - out_im * in_re),
        (out_re * rank_re + out_im * rank_im, out_re * rank_im - out_im * rank_re),
        (rank_re * in_re + rank_im * in_im, rank_re * in_im - rank_im * in_re),
        (rank_re * rank_re + rank_im * rank_im, None),
    )


def mode_values(modes_ref):
    index = lax.broadcasted_iota(jnp.int32, modes_ref.shape[1:], 0).astype(F32)
    return -0.5 * jnp.exp(modes_ref[0]), math.pi * (index + modes_ref[1])


POINT_ROWS = 16


def resolvent(coef_ref, n, square_cos, cos_sin, scaled):
    den_re = coef_ref[8, pl.ds(n, 1), :] * square_cos - scaled
    den_im = coef_ref[9, pl.ds(n, 1), :] * cos_sin
    inverse = 1.0 / (den_re * den_re + den_im * den_im)
    return den_re * inverse, -(den_im * inverse)


def complex_multiply(a_re, a_im, b_re, b_im):
    return a_re * b_re - a_im * b_im, a_re * b_im + a_im * b_re


def conj_multiply(a_re, a_im, b_re, b_im):
    return a_re * b_re + a_im * b_im, a_re * b_im - a_im * b_re


def combine(sums, sigma, cosine, sine):
    terms = []
    for p_re, p_im, q_re, q_im in (sums[4 * q : 4 * q + 4] for q in range(4)):
        swing = sigma * sine
        terms.append((-swing * p_im - cosine * q_re, swing * p_re - cosine * q_im))
    twice = 2.0 * cosine
    loop_re, loop_im = 1.0 + twice * terms[3][0], twice * terms[3][1]
    scale = 1.0 / (loop_re * loop_re + loop_im * loop_im)
    inv = (loop_re * scale, -(loop_im * scale))
    ratio = complex_multiply(twice * terms[2][0], twice * terms[2][1], *inv)
    return terms, inv, ratio


def cauchy_forward(modes_ref, sigma, coef_ref, wave_ref, sums_ref, rhs_ref, middle):
    lam_re, lam_im = mode_values(modes_ref)
    for q, (real, imag) in enumerate(pair_terms(modes_ref)):
        coef_ref[q] = real
        coef_ref[4 + q] = real * lam_re if imag is None else real * lam_re + imag * lam_im
    coef_ref[8] = lam_re * lam_re + lam_im * lam_im
    coef_ref[9] = -2.0 * sigma * lam_re
    sigma_sq = sigma * sigma
    for pair in range(2):

        def body(row, pair=pair):
            rows = pl.ds(row, POINT_ROWS)
            cosine, sine = wave_ref[0, pair, rows, :], wave_ref[1, pair, rows, :]
            square_cos, cos_sin, scaled = cosine * cosine, cosine * sine, sigma_sq * (sine * sine)

            def add_mode(n, sums):
                sums = list(sums)
                for k in range(4):
                    at = n * 4 + k
                    inv_re, inv_im = resolvent(coef_ref, at, square_cos, cos_sin, scaled)
                    for q in range(4):
                        plain = coef_ref[q, pl.ds(at, 1), :]
                        turned = coef_ref[4 + q, pl.ds(at, 1), :]
                        sums[4 * q] = sums[4 * q] + plain * inv_re
                        sums[4 * q + 1] = sums[4 * q + 1] + plain * inv_im
                        sums[4 * q + 2] = sums[4 * q + 2] + turned * inv_re
                        sums[4 * q + 3] = sums[4 * q + 3] + turned * inv_im
                return tuple(sums)

            zero = jnp.zeros((POINT_ROWS, LANES), F32)
            sums = lax.fori_loop(0, 8, add_mode, (zero,) * 16)
            for i in range(16):
                sums_ref[pair, i, rows, :] = sums[i]
            terms, _, ratio = combine(sums, sigma, cosine, sine)
            cut_re, cut_im = complex_multiply(*terms[1], *ratio)
            part_re, part_im = terms[0][0] - cut_re, terms[0][1] - cut_im
            spec_re, spec_im = complex_multiply(2.0 * cosine, 2.0 * sine, part_re, part_im)
            store_split(rhs_ref, row, pair * LANES, spec_re)
            store_split(rhs_ref, row + ROWS, pair * LANES, spec_im)

        over_chunks(body, POINT_ROWS)
        middle(pair)


def cauchy_backward(modes_ref, sigma, nyquist_grad, step, coef_ref, wave_ref, sums_ref, spec_ref, grad_ref, back_ref, middle):
    zero = jnp.zeros((8, LANES), F32)
    sigma_sum = zero
    for pair in range(2):
        lanes = slice(pair * LANES, (pair + 1) * LANES)

        def start(index, total, pair=pair, lanes=lanes):
            row = pl.multiple_of(index * POINT_ROWS, POINT_ROWS)
            rows = pl.ds(row, POINT_ROWS)
            cosine, sine = wave_ref[0, pair, rows, :], wave_ref[1, pair, rows, :]
            sums = [sums_ref[pair, i, rows, :] for i in range(16)]
            terms, inv, ratio = combine(sums, sigma, cosine, sine)
            spec_re, spec_im = spec_ref[rows, lanes], spec_ref[pl.ds(row + ROWS, POINT_ROWS), lanes]
            part = conj_multiply(2.0 * cosine, 2.0 * sine, spec_re, spec_im)
            left = conj_multiply(*ratio, *part)
            ratio_grad = conj_multiply(*terms[1], *part)
            back = conj_multiply(*inv, -ratio_grad[0], -ratio_grad[1])
            twice = 2.0 * cosine
            loop = conj_multiply(*ratio, *back)
            grads = (
                part,
                (-left[0], -left[1]),
                (twice * back[0], twice * back[1]),
                (-twice * loop[0], -twice * loop[1]),
            )
            swing = sigma * sine
            for q, (g_re, g_im) in enumerate(grads):
                grad_ref[pair, 4 * q, rows, :] = swing * g_im
                grad_ref[pair, 4 * q + 1, rows, :] = -swing * g_re
                grad_ref[pair, 4 * q + 2, rows, :] = -cosine * g_re
                grad_ref[pair, 4 * q + 3, rows, :] = -cosine * g_im
                piece = sine * (g_im * sums[4 * q] - g_re * sums[4 * q + 1])
                total = total + piece[:8] + piece[8:]
            return total

        sigma_sum = lax.fori_loop(0, ROWS // POINT_ROWS, start, sigma_sum)
    sigma_sq = sigma * sigma

    def mode(n, square_sum):
        def point(index, sums):
            row = pl.multiple_of(index * 8, 8)
            rows = pl.ds(row, 8)
            sums = list(sums)
            for pair in range(2):
                cosine, sine = wave_ref[0, pair, rows, :], wave_ref[1, pair, rows, :]
                square_cos, cos_sin, square_sin = cosine * cosine, cosine * sine, sine * sine
                inv_re, inv_im = resolvent(coef_ref, n, square_cos, cos_sin, sigma_sq * square_sin)
                grad_re, grad_im = 0.0, 0.0
                for q in range(4):
                    plain = coef_ref[q, pl.ds(n, 1), :]
                    turned = coef_ref[4 + q, pl.ds(n, 1), :]
                    p_re, p_im = grad_ref[pair, 4 * q, rows, :], grad_ref[pair, 4 * q + 1, rows, :]
                    q_re, q_im = grad_ref[pair, 4 * q + 2, rows, :], grad_ref[pair, 4 * q + 3, rows, :]
                    grad_re = grad_re + plain * p_re + turned * q_re
                    grad_im = grad_im + plain * p_im + turned * q_im
                    sums[q] = sums[q] + (p_re * inv_re + p_im * inv_im)
                    sums[4 + q] = sums[4 + q] + (q_re * inv_re + q_im * inv_im)
                square_re = inv_re * inv_re - inv_im * inv_im
                square_im = 2.0 * inv_re * inv_im
                den_re, den_im = conj_multiply(square_re, square_im, grad_re, grad_im)
                sums[8] = sums[8] - den_re * square_cos
                sums[9] = sums[9] - den_im * cos_sin
                sums[10] = sums[10] + den_re * square_sin
            return tuple(sums)

        sums = lax.fori_loop(0, ROWS // 8, point, (zero,) * 10 + (square_sum,))
        for i in range(10):
            back_ref[i, pl.ds(n, 1), :] = column_sum(sums[i])
        return sums[10]

    square_sum = lax.fori_loop(0, 32, mode, zero)
    middle()
    plain_grad = [fold(back_ref[q]) for q in range(4)]
    turned_grad = [fold(back_ref[4 + q]) for q in range(4)]
    abs_grad, skew_grad = fold(back_ref[8]), fold(back_ref[9])
    lam_re, lam_im = mode_values(modes_ref)
    plain_grad[0] = plain_grad[0] + step * nyquist_grad
    rank_re, rank_im, in_re, in_im, out_re, out_im = (modes_ref[i] for i in range(2, 8))
    lam_re_grad = 2.0 * lam_re * abs_grad - 2.0 * sigma * skew_grad
    lam_im_grad = 2.0 * lam_im * abs_grad
    real_grad, imag_grad = [], []
    terms = pair_terms(modes_ref)
    for q, (real, imag) in enumerate(terms):
        lam_re_grad = lam_re_grad + turned_grad[q] * real
        if imag is not None:
            lam_im_grad = lam_im_grad + turned_grad[q] * imag
        real_grad.append(plain_grad[q] + turned_grad[q] * lam_re)
        imag_grad.append(turned_grad[q] * lam_im)
    r0, r1, r2, r3 = real_grad
    i0, i1, i2, _ = imag_grad
    grads = (
        lam_re_grad * lam_re,
        math.pi * lam_im_grad,
        r1 * out_re - i1 * out_im + r2 * in_re + i2 * in_im + 2.0 * r3 * rank_re,
        r1 * out_im + i1 * out_re + r2 * in_im - i2 * in_re + 2.0 * r3 * rank_im,
        r0 * out_re - i0 * out_im + r2 * rank_re - i2 * rank_im,
        r0 * out_im + i0 * out_re + r2 * rank_im + i2 * rank_re,
        r0 * in_re + i0 * in_im + r1 * rank_re + i1 * rank_im,
        r0 * in_im - i0 * in_re + r1 * rank_im - i1 * rank_re,
    )
    sigma_grad = (
        fold(column_sum(sigma_sum) + 2.0 * sigma * column_sum(square_sum))
        - 2.0 * column_sum(skew_grad * lam_re)
    )
    nyquist = step * column_sum(terms[0][0])
    return grads, nyquist * nyquist_grad - sigma * sigma_grad


def ring_place(chan):
    z, y = chan // 2, chan % 2
    return z + y * (7 - 2 * z)


def ring_chan(place):
    back = place // 4
    z = place * (1 - back) + (7 - place) * back
    return 2 * z + back


TURNS = (1, -1)


def ring_items():
    out = []
    for step in range(1, 5):
        for turn in range(2):
            for block in range(2):
                if step < 4 or block == turn:
                    out.append((turn, step, block))
    return out


def item_slot(turn, step, block):
    return (turn * 4 + step - 1) * 2 + block


def block_kernel(
    tok_ref, cot_ref, shard_ref, vec_ref, aux_ref, coefl_ref, coefc_ref, modes_ref, mat_ref, tw_ref, wave_ref,
    out_ref, dtok_ref, gw_ref, gm_ref, gv_ref,
    w_ref, grad_ref, sib_ref, ring_ref, part_ref,
    in_send, in_recv, head_send, head_recv, acts_send, acts_recv, back_send, back_recv, late_send, late_recv,
    sum_send, sum_recv, tail_send, tail_recv, dp_send, dp_recv,
    hat_ref, norm_ref, slope_ref, conv_ref, rhs_ref, freq_ref, sig_ref, ans_ref, taps_ref,
    mcoef_ref, sums_ref, pgrad_ref, mback_ref,
    gate_ref, swish_ref, res_ref, hat2_ref, low_ref, branch_ref, back2_ref, gab_ref, hid_ref, gpre_ref,
    ring_ss, ring_rs, sib_ss, sib_rs, x_ss, x_rs, rring_ss, rring_rs, rsib_ss, rsib_rs, rx_ss, rx_rs, a2a_ss, a2a_rs, dp_ss, dp_rs,
):
    dp, chan = lax.axis_index("dp"), lax.axis_index("chan")
    core = dp % 2
    sibling = dp + 1 - 2 * core
    across = (dp + 2) % 4
    place = ring_place(chan)
    nexts = [ring_chan((place + 1) % 8), ring_chan((place + 7) % 8)]

    def chan_at(offset):
        return ring_chan((place + offset + 8) % 8)

    barrier = pltpu.get_barrier_semaphore()
    for r in range(1, N_CHAN):
        pl.semaphore_signal(barrier, inc=1, device_id={"chan": (chan + r) % N_CHAN}, device_id_type=MESH)
    for r in range(1, 4):
        pl.semaphore_signal(barrier, inc=1, device_id={"dp": (dp + r) % 4}, device_id_type=MESH)
    pl.semaphore_wait(barrier, N_CHAN - 1 + 3)

    pending = []

    def remote(src, dst, send_sem, recv_sem, **device):
        return pltpu.make_async_remote_copy(
            src_ref=src, dst_ref=dst, send_sem=send_sem, recv_sem=recv_sem, device_id=device, device_id_type=MESH
        )

    def send(*args, **device):
        copy = remote(*args, **device)
        copy.start()
        pending.append(copy)

    def exchange(which, source, recv_ref):
        def copy(r):
            peer = (chan + r) % N_CHAN
            return remote(
                source(peer), recv_ref.at[chan], a2a_ss.at[which, r - 1], a2a_rs.at[which, r - 1], chan=peer
            )

        def start():
            for r in range(1, N_CHAN):
                copy(r).start()

        def wait():
            for r in range(1, N_CHAN):
                copy(r).wait_recv()

        def finish():
            for r in range(1, N_CHAN):
                copy(r).wait_send()

        return start, wait, finish

    def row_of(group):
        return pl.multiple_of(group * ROWS, ROWS)

    def weight(chan_id, group):
        return w_ref.at[chan_id, pl.ds(row_of(group), ROWS), :]

    mine = (dp, across)
    theirs = (sibling, (sibling + 2) % 4)

    def origin(turn, step):
        return chan_at(-TURNS[turn] * step)

    def ring_copy(turn, step, block):
        slot = item_slot(turn, step, block)
        ref = weight(origin(turn, step - 1), mine[block])
        return remote(ref, ref, ring_ss.at[slot], ring_rs.at[slot], chan=nexts[turn])

    def sib_copy(chan_id, block, slot):
        ref = weight(chan_id, mine[block])
        return remote(ref, ref, sib_ss.at[slot], sib_rs.at[slot], dp=sibling)

    def ring_got(turn, step, block):
        slot = item_slot(turn, step, block)
        ref = weight(origin(turn, step), mine[block])
        remote(ref, ref, ring_ss.at[slot], ring_rs.at[slot], chan=nexts[turn]).wait_recv()

    def gather_start():
        w_ref[chan, pl.ds(row_of(dp), ROWS), :] = shard_ref[...]
        x_ref = weight(chan, dp)
        send(x_ref, x_ref, x_ss, x_rs, dp=across)
        for turn in range(2):
            copy = ring_copy(turn, 1, 0)
            copy.start()
            pending.append(copy)
        copy = sib_copy(chan, 0, 16)
        copy.start()
        pending.append(copy)

    def gather_across():
        x_ref = weight(chan, across)
        remote(x_ref, x_ref, x_ss, x_rs, dp=across).wait_recv()
        for turn in range(2):
            copy = ring_copy(turn, 1, 1)
            copy.start()
            pending.append(copy)
        copy = sib_copy(chan, 1, 17)
        copy.start()
        pending.append(copy)

    items = ring_items()

    def gather_step(step):
        for turn, at, block in items:
            if at != step:
                continue
            ring_got(turn, step, block)
            if (turn, step + 1, block) in items:
                copy = ring_copy(turn, step + 1, block)
                copy.start()
                pending.append(copy)
            copy = sib_copy(origin(turn, step), block, item_slot(turn, step, block))
            copy.start()
            pending.append(copy)

    def gather_finish():
        def got(chan_id, block, slot):
            ref = weight(chan_id, theirs[block])
            remote(ref, ref, sib_ss.at[slot], sib_rs.at[slot], dp=sibling).wait_recv()

        got(chan, 0, 16)
        got(chan, 1, 17)
        for turn, step, block in items:
            got(origin(turn, step), block, item_slot(turn, step, block))

    for j in range(PAIRS):
        for first, ref in ((0, tok_ref), (HALF, cot_ref)):
            low, high = split_pair(ref[j * ROWS : (j + 1) * ROWS, :].astype(F32))
            in_send[2 * j, first : first + HALF, :] = low.astype(BF16)
            in_send[2 * j + 1, first : first + HALF, :] = high.astype(BF16)
    in_recv[chan] = in_send[chan]

    lane_id = lax.broadcasted_iota(jnp.int32, (8, LANES), 1)
    row_id = lax.broadcasted_iota(jnp.int32, (8, LANES), 0)
    halves = jnp.where((lane_id >= HALF) == (row_id == 1), 1.0, 0.0) * jnp.where(row_id < 2, 1.0, 0.0)
    halves = halves.astype(BF16)

    def token_sums(parts):
        total = 0.0
        for part in parts:
            total = total + dot_nt(halves, part)
        return [total[h : h + 1, j * ROWS : (j + 1) * ROWS] for h in range(2) for j in range(PAIRS)]

    def split(values):
        high = values.astype(BF16)
        return high, (values - high.astype(F32)).astype(BF16)

    tokens = tok_ref[...]
    wide_tokens = tokens.astype(F32)
    for i, row in enumerate(token_sums([tokens]) + token_sums(split(wide_tokens * wide_tokens))):
        head_send[i : i + 1, :] = row
    head_send[16:24, :] = vec_ref[...]
    head_recv[chan] = head_send[...]
    head = exchange(0, lambda peer: head_send, head_recv)
    inputs = exchange(1, lambda peer: in_send.at[peer], in_recv)
    head[0]()
    gather_start()
    inputs[0]()

    log_dt = aux_ref[8:9, :]
    sigma, step_size = 2.0 * jnp.exp(-log_dt), jnp.exp(log_dt)

    def after_pair(pair):
        if pair == 0:
            gather_across()
        else:
            gather_step(1)

    cauchy_forward(modes_ref, sigma, mcoef_ref, wave_ref, sums_ref, rhs_ref, after_pair)
    freq_ref[:, 0:256] = split_product(mat_ref, 1, rhs_ref, 0, 256)
    even = split_product(mat_ref, 2, rhs_ref, LANES, LANES)
    freq_ref[:, LANES:256] = jnp.where(low_lanes(256), freq_ref[:, LANES:256], even)
    sign = 1.0 - 2.0 * (lax.broadcasted_iota(jnp.int32, (CHUNK, LANES), 0) % 2).astype(F32)
    nyquist = step_size * column_sum(mcoef_ref[0]) * (1.0 / TOK_DEV)

    def store_taps(j, rows, values):
        taps_ref[j, rows, :] = (values + sign * nyquist) * aux_ref[4 + j : 5 + j, :]

    gather_pairs(freq_ref, coefc_ref, 160, tw_ref, 10, 2, store_taps)
    spread_pairs(lambda j, rows: taps_ref[j, rows, :], coefc_ref, 0, tw_ref, 0, 5, rhs_ref)
    transform_into(ans_ref, mat_ref, 0, rhs_ref)

    head[1]()
    sums = head_recv[0, 0:16, :]
    for c in range(1, N_CHAN):
        sums = sums + head_recv[c, 0:16, :]
    mean = sums[0:8] * (1.0 / MODEL_WIDTH)
    rstd = lax.rsqrt(sums[8:16] * (1.0 / MODEL_WIDTH) - mean * mean + EPSILON)

    def columns(rows):
        tall = rows.T
        return [jnp.where(low_lanes(ROWS), tall[:, j : j + 1], tall[:, 4 + j : 5 + j]) for j in range(PAIRS)]

    gain1, bias1, skip = (vec_ref[5 + i : 6 + i, :] for i in range(3))
    mean_cols, rstd_cols = columns(mean), columns(rstd)
    for j in range(PAIRS):
        hat = (tok_ref[j * ROWS : (j + 1) * ROWS, :].astype(F32) - mean_cols[j]) * rstd_cols[j]
        hat_ref[j] = hat
        norm_ref[j] = hat * gain1 + bias1

    spread_pairs(lambda j, rows: norm_ref[j, rows, :], coefl_ref, 0, tw_ref, 0, 5, rhs_ref)
    transform_into(sig_ref, mat_ref, 0, rhs_ref)
    gather_step(2)
    multiply_spectra(sig_ref, ans_ref, rhs_ref, False)
    transform_into(freq_ref, mat_ref, 1, rhs_ref)

    def store_conv(j, rows, values):
        conv_ref[j, rows, :] = values

    gather_pairs(freq_ref, coefl_ref, 80, tw_ref, 0, 5, store_conv)
    for j in range(PAIRS):
        mixed = conv_ref[j] * aux_ref[j : j + 1, :] + skip * norm_ref[j]
        cumulative, density = normal_parts(mixed)
        slope_ref[j] = cumulative + mixed * density
        low, high = split_pair(mixed * cumulative)
        acts_send[2 * j] = low.astype(BF16)
        acts_send[2 * j + 1] = high.astype(BF16)
    acts_recv[chan] = acts_send[chan]
    acts = exchange(2, lambda peer: acts_send.at[peer], acts_recv)
    acts[0]()
    gather_step(3)
    gather_step(4)
    inputs[1]()
    acts[1]()

    def joined(ref, pair, first):
        return join_pair(
            ref[2 * pair, first : first + HALF, :].astype(F32), ref[2 * pair + 1, first : first + HALF, :].astype(F32)
        )

    def lanes_of(pair):
        return slice(pair * LANES, (pair + 1) * LANES)

    ACTS, NORM2, GRADF = range(3)
    for p in range(PAIRS):
        low_ref[ACTS, :, lanes_of(p)] = joined(acts_recv, p, 0).astype(BF16)
        low_ref[GRADF, :, lanes_of(p)] = joined(in_recv, p, HALF).astype(BF16)
    gather_finish()

    def vector(row, first, second):
        return interleave(head_recv[first, 16 + row : 17 + row, :], head_recv[second, 16 + row : 17 + row, :])

    total = 0.0
    for p in range(PAIRS):
        first = dot_nn(low_ref[ACTS], w_ref[2 * p, :, 0:LANES]) + head_recv[2 * p, 16:17, :]
        second = dot_nn(low_ref[ACTS], w_ref[2 * p + 1, :, 0:LANES]) + head_recv[2 * p + 1, 16:17, :]
        gate, raw = interleave(first, second)
        swish = lax.logistic(raw)
        gate_ref[p], swish_ref[p] = gate, swish
        resid = joined(in_recv, p, 0) + gate * swish
        res_ref[p] = resid
        total = total + resid
    mean2 = jnp.sum(total, axis=1, keepdims=True) * (1.0 / MODEL_WIDTH)
    total = 0.0
    for p in range(PAIRS):
        centred = res_ref[p] - mean2
        total = total + centred * centred
    rstd2 = lax.rsqrt(jnp.sum(total, axis=1, keepdims=True) * (1.0 / MODEL_WIDTH) + EPSILON)
    gain2 = []
    for p in range(PAIRS):
        gain, bias = vector(1, 2 * p, 2 * p + 1)
        gain2.append(gain)
        hat = (res_ref[p] - mean2) * rstd2
        hat2_ref[p] = hat
        low_ref[NORM2, :, lanes_of(p)] = (hat * gain + bias).astype(BF16)
    branch_ref[...] = jnp.zeros_like(branch_ref)
    back2_ref[...] = jnp.zeros_like(back2_ref)

    def hidden_block(c, carry):
        bias = jnp.concatenate([head_recv[c, 19:20, :], head_recv[c, 20:21, :]], axis=1)
        pre = dot_nn(low_ref[NORM2], w_ref[c, :, 128:384]) + bias
        cumulative, density = normal_parts(pre)
        hidden = (pre * cumulative).astype(BF16)
        hid_ref[c] = hidden
        grad = dot_nn(low_ref[GRADF], w_ref[c, :, 384:640]) * (cumulative + pre * density)
        grad = grad.astype(BF16)
        gpre_ref[c] = grad
        sums = column_sum(grad.astype(F32))
        tail_send[c, 3:4, :] = sums[:, 0:LANES]
        tail_send[c, 4:5, :] = sums[:, LANES : 2 * LANES]
        branch_ref[...] += dot_nt(hidden, w_ref[c, :, 384:640])
        back2_ref[...] += dot_nt(grad, w_ref[c, :, 128:384])
        return carry

    lax.fori_loop(0, N_CHAN, hidden_block, 0)

    mean_q, mean_qx = 0.0, 0.0
    for p in range(PAIRS):
        grad, hat = back2_ref[:, lanes_of(p)], hat2_ref[p]
        q = grad * gain2[p]
        mean_q = mean_q + q
        mean_qx = mean_qx + q * hat
        gain_grad, bias_grad = interleave(column_sum(grad * hat), column_sum(grad))
        tail_send[2 * p, 1:2, :] = gain_grad
        first, second = interleave(turn_half(column_sum(grad * hat)), turn_half(column_sum(grad)))
        tail_send[2 * p + 1, 1:2, :] = first
    mean_q = jnp.sum(mean_q, axis=1, keepdims=True) * (1.0 / MODEL_WIDTH)
    mean_qx = jnp.sum(mean_qx, axis=1, keepdims=True) * (1.0 / MODEL_WIDTH)
    for p in range(PAIRS):
        hat = hat2_ref[p]
        extra = rstd2 * (back2_ref[:, lanes_of(p)] * gain2[p] - mean_q - hat * mean_qx)
        grad_f = joined(in_recv, p, HALF)
        grad_resid = grad_f + extra
        gate, swish = gate_ref[p], swish_ref[p]
        grad_a = (grad_resid * swish).astype(BF16).astype(F32)
        grad_b = (grad_resid * gate * swish * (1.0 - swish)).astype(BF16).astype(F32)
        first, second = interleave(grad_a, grad_b)
        gab_ref[2 * p] = first.astype(BF16)
        gab_ref[2 * p + 1] = second.astype(BF16)
        tail_send[2 * p, 0:1, :] = column_sum(first)
        tail_send[2 * p + 1, 0:1, :] = column_sum(second)
        low, high = interleave(column_sum(grad_f), column_sum(grad_f))
        tail_send[2 * p, 2:3, :] = low
        tail_send[2 * p + 1, 2:3, :] = high
        low, high = split_pair(extra)
        late_send[2 * p, HALF:, :] = low.astype(BF16)
        late_send[2 * p + 1, HALF:, :] = high.astype(BF16)
    grad_acts = 0.0
    for c in range(N_CHAN):
        grad_acts = grad_acts + dot_nt(gab_ref[c], w_ref[c, :, 0:LANES])
    for p in range(PAIRS):
        low, high = split_pair(grad_acts[:, lanes_of(p)])
        back_send[2 * p] = low.astype(BF16)
        back_send[2 * p + 1] = high.astype(BF16)
    back_recv[chan] = back_send[chan]
    back = exchange(3, lambda peer: back_send.at[peer], back_recv)
    back[0]()

    def rsib_copy(offset, block):
        slot = (offset + 3) * 2 + block
        src = grad_ref.at[chan_at(offset), pl.ds(row_of(theirs[block]), ROWS), :]
        return remote(src, sib_ref.at[slot], rsib_ss.at[slot], rsib_rs.at[slot], dp=sibling)

    tall = [low_ref[i].astype(F32).T.astype(BF16) for i in range(3)]
    order = (4, 3, -3, 2, -2, 1, -1, 0)
    for offset in order:
        c = chan_at(offset)
        grad_ref[c, :, 0:128] = dot_nn(tall[ACTS], gab_ref[c]).astype(BF16)
        grad_ref[c, :, 128:384] = dot_nn(tall[NORM2], gpre_ref[c]).astype(BF16)
        grad_ref[c, :, 384:640] = dot_nn(tall[GRADF], hid_ref[c]).astype(BF16)
        for block in range(2):
            copy = rsib_copy(offset, block)
            copy.start()
            pending.append(copy)
    for p in range(PAIRS):
        out = res_ref[p] + branch_ref[:, lanes_of(p)] + interleave(head_recv[2 * p, 18:19, :], head_recv[2 * p + 1, 18:19, :])[0]
        low, high = split_pair(out)
        late_send[2 * p, :HALF, :] = low.astype(BF16)
        late_send[2 * p + 1, :HALF, :] = high.astype(BF16)
    for c in range(N_CHAN):
        tail_send[c, 5:8, :] = jnp.zeros((3, LANES), F32)
    late_recv[chan] = late_send[chan]
    tail_recv[chan] = tail_send[chan]
    late = exchange(4, lambda peer: late_send.at[peer], late_recv)
    tail = exchange(5, lambda peer: tail_send.at[peer], tail_recv)
    late[0]()
    tail[0]()

    def offset_of(turn, step):
        return TURNS[turn] * (5 - step)

    def rring_copy(turn, step, block):
        slot = item_slot(turn, step, block)
        src = grad_ref.at[chan_at(offset_of(turn, step)), pl.ds(row_of(mine[block]), ROWS), :]
        return remote(src, ring_ref.at[slot], rring_ss.at[slot], rring_rs.at[slot], chan=nexts[turn])

    ritems = [(turn, 5 - step, block) for turn, step, block in items]

    def own_and_sibling(offset, block):
        slot = ((offset if offset != -4 else 4) + 3) * 2 + block
        rsib_copy(offset if offset != -4 else 4, block).wait_recv()
        own = grad_ref[chan_at(offset), pl.ds(row_of(mine[block]), ROWS), :].astype(F32)
        return own + sib_ref[slot].astype(F32)

    def reduce_step(step):
        for turn, at, block in ritems:
            if at != step:
                continue
            total = own_and_sibling(offset_of(turn, step), block)
            if (turn, step - 1, block) in ritems:
                rring_copy(turn, step - 1, block).wait_recv()
                total = total + ring_ref[item_slot(turn, step - 1, block)].astype(F32)
            grad_ref[chan_at(offset_of(turn, step)), pl.ds(row_of(mine[block]), ROWS), :] = total.astype(BF16)
            copy = rring_copy(turn, step, block)
            copy.start()
            pending.append(copy)

    def reduce_last():
        for block in (1, 0):
            total = own_and_sibling(0, block)
            for turn in range(2):
                rring_copy(turn, 4, block).wait_recv()
                total = total + ring_ref[item_slot(turn, 4, block)].astype(F32)
            if block == 1:
                part_ref[0] = total.astype(BF16)
                send(part_ref.at[0], part_ref.at[1], rx_ss, rx_rs, dp=across)
            else:
                gw_ref[...] = total

    def reduce_finish():
        remote(part_ref.at[0], part_ref.at[1], rx_ss, rx_rs, dp=across).wait_recv()
        gw_ref[...] += part_ref[1].astype(F32)

    reduce_step(1)

    back[1]()
    skip_grad = 0.0
    for j in range(PAIRS):
        grad = joined(back_recv, j, 0) * slope_ref[j]
        slope_ref[j] = grad
        conv_ref[j] = grad * aux_ref[j : j + 1, :]
        skip_grad = skip_grad + column_sum(grad * norm_ref[j])
    spread_pairs(lambda j, rows: conv_ref[j, rows, :], coefl_ref, 0, tw_ref, 0, 5, rhs_ref)
    transform_into(freq_ref, mat_ref, 0, rhs_ref)
    multiply_spectra(sig_ref, freq_ref, rhs_ref, True)
    transform_into(sig_ref, mat_ref, 1, rhs_ref)

    def store_kernel_grad(j, rows, values):
        taps_ref[j, rows, :] = values * aux_ref[4 + j : 5 + j, :]

    gather_pairs(sig_ref, coefc_ref, 80, tw_ref, 0, 5, store_kernel_grad)
    multiply_spectra(ans_ref, freq_ref, rhs_ref, True)
    transform_into(freq_ref, mat_ref, 1, rhs_ref)
    gather_pairs(freq_ref, coefl_ref, 80, tw_ref, 0, 5, store_conv)
    gain_grad, bias_grad = 0.0, 0.0
    scaled, crossed = [], []
    for j in range(PAIRS):
        grad = conv_ref[j] + skip * slope_ref[j]
        conv_ref[j] = grad
        gain_grad = gain_grad + column_sum(grad * hat_ref[j])
        bias_grad = bias_grad + column_sum(grad)
    conv = conv_ref[...].reshape(PAIRS * ROWS, LANES) * gain1
    for i, row in enumerate(
        token_sums(split(conv)) + token_sums(split(conv * hat_ref[...].reshape(PAIRS * ROWS, LANES)))
    ):
        sum_send[i : i + 1, :] = row
    sum_recv[chan] = sum_send[...]
    sums_back = exchange(6, lambda peer: sum_send, sum_recv)
    sums_back[0]()
    reduce_step(2)

    nyquist_grad = 0.0
    for j in range(PAIRS):
        whole_sign = 1.0 - 2.0 * (lax.broadcasted_iota(jnp.int32, (ROWS, LANES), 0) % 2).astype(F32)
        nyquist_grad = nyquist_grad + column_sum(taps_ref[j] * whole_sign)
    nyquist_grad = fold(nyquist_grad) * (1.0 / TOK_DEV)
    spread_pairs(lambda j, rows: taps_ref[j, rows, :], coefc_ref, 192, tw_ref, 10, 2, rhs_ref)
    freq_ref[:, 0:256] = split_product(mat_ref, 0, rhs_ref, 0, 256)
    even = split_product(mat_ref, 3, rhs_ref, LANES, LANES)
    freq_ref[:, LANES:256] = jnp.where(low_lanes(256), freq_ref[:, LANES:256], even)
    mode_grads, dt_grad = cauchy_backward(
        modes_ref, sigma, nyquist_grad, step_size, mcoef_ref, wave_ref, sums_ref, freq_ref, pgrad_ref, mback_ref,
        lambda: reduce_step(3),
    )
    mask = low_lanes(32)
    for i in range(4):
        dp_send[i * 32 : (i + 1) * 32, :] = jnp.where(mask, mode_grads[i], mode_grads[i + 4])
    first = low_lanes(1)
    dp_send[128:129, :] = jnp.where(first, dt_grad, fold(skip_grad))
    dp_send[129:130, :] = jnp.where(first, fold(gain_grad), fold(bias_grad))
    dp_send[130:136, :] = jnp.zeros((6, LANES), F32)
    tail[1]()
    tail_sum = tail_recv[0]
    for c in range(1, N_CHAN):
        tail_sum = tail_sum + tail_recv[c]
    dp_send[136:144, :] = tail_sum
    dp_recv[0] = dp_send[...]

    def dp_copy(r):
        return remote(dp_send, dp_recv.at[r], dp_ss.at[r - 1], dp_rs.at[r - 1], dp=(dp + r) % 4)

    for r in range(1, 4):
        dp_copy(r).start()

    sums_back[1]()
    sums = sum_recv[0]
    for c in range(1, N_CHAN):
        sums = sums + sum_recv[c]
    sums = sums * (1.0 / MODEL_WIDTH)
    rstd_cols, q_cols, qx_cols = columns(rstd), columns(sums[0:8]), columns(sums[8:16])
    late[1]()
    for j in range(PAIRS):
        rows = slice(j * ROWS, (j + 1) * ROWS)
        out_ref[rows, :] = joined(late_recv, j, 0).astype(BF16)
        dtok_ref[rows, :] = joined(late_recv, j, HALF) + rstd_cols[j] * (
            conv_ref[j] * gain1 - q_cols[j] - hat_ref[j] * qx_cols[j]
        )
    reduce_step(4)
    reduce_last()
    for r in range(1, 4):
        dp_copy(r).wait_recv()
    total = dp_recv[0] + dp_recv[1] + dp_recv[2] + dp_recv[3]
    gm_ref[...] = total[0:128]
    gv_ref[...] = total[128:144]
    reduce_finish()
    for copy in pending:
        copy.wait_send()
    for group in (head, inputs, acts, back, late, tail, sums_back):
        group[2]()
    for r in range(1, 4):
        dp_copy(r).wait_send()


def block_program(level_tables, tables):
    mats, twiddle, levels, constant, wave = tables

    def run(tokens, cotangent, bucket, items, gain1, bias1, modes, log_dt, skip, w_a, b_a, w_b, b_b, gain2, bias2, w_up, b_up, w_down, b_down):
        def pack(values):
            return values.reshape(PAIRS, 2, ROWS, HALF).transpose(0, 2, 1, 3).reshape(PAIRS * ROWS, LANES)

        def unpack(values):
            return values.reshape(PAIRS, ROWS, 2, HALF).transpose(0, 2, 1, 3).reshape(TOK_DEV, HALF)

        def twice(values):
            return jnp.concatenate([values, values])

        level, filled = bucket[0], items[0]
        shard = jnp.concatenate([w_a, w_b, w_up, w_down.T], axis=1).astype(BF16)
        vec = jnp.stack(
            [
                jnp.concatenate([b_a, b_b]), jnp.concatenate([gain2, bias2]), twice(b_down), b_up[:LANES], b_up[LANES:],
                twice(gain1), twice(bias1), twice(skip),
            ]
        )
        block = np.repeat(np.arange(8).reshape(PAIRS, 2), HALF, axis=1)
        item_blocks = 2 << level
        aux = jnp.concatenate(
            [
                (block < filled * item_blocks).astype(F32), (block < item_blocks).astype(F32),
                jnp.broadcast_to(twice(log_dt)[None], (8, LANES)),
            ]
        )
        swapped = jnp.swapaxes(modes, 1, 2)
        modes_two = jnp.concatenate([swapped, swapped], axis=2)
        vmem = pl.BlockSpec(memory_space=pltpu.VMEM)
        dma = pltpu.SemaphoreType.DMA

        def buf(*shape):
            return pltpu.VMEM(shape, F32)

        def low(*shape):
            return pltpu.VMEM(shape, BF16)

        big, wide = (PAIRS, ROWS, LANES), (256, WIDE)
        out, dtok, gw, gm, gv = pl.pallas_call(
            block_kernel,
            out_shape=(
                jax.ShapeDtypeStruct((512, LANES), BF16), jax.ShapeDtypeStruct((512, LANES), F32),
                jax.ShapeDtypeStruct((ROWS, WIDE), F32), jax.ShapeDtypeStruct((ROWS, LANES), F32),
                jax.ShapeDtypeStruct((16, LANES), F32),
            ),
            in_specs=[vmem] * 11,
            out_specs=(vmem,) * 5,
            scratch_shapes=[
                low(N_CHAN, 512, WIDE), low(N_CHAN, 512, WIDE), low(16, ROWS, WIDE), low(16, ROWS, WIDE), low(2, ROWS, WIDE),
                low(N_CHAN, ROWS, LANES), low(N_CHAN, ROWS, LANES), buf(24, LANES), buf(N_CHAN, 24, LANES),
                low(N_CHAN, HALF, LANES), low(N_CHAN, HALF, LANES), low(N_CHAN, HALF, LANES), low(N_CHAN, HALF, LANES),
                low(N_CHAN, ROWS, LANES), low(N_CHAN, ROWS, LANES),
                buf(16, LANES), buf(N_CHAN, 16, LANES), buf(N_CHAN, 8, LANES), buf(N_CHAN, 8, LANES),
                buf(144, LANES), buf(4, 144, LANES),
                buf(*big), buf(*big), buf(*big), buf(*big), low(2, *wide), buf(*wide), buf(*wide), buf(*wide), buf(*big),
                buf(10, 32, LANES), buf(2, 16, ROWS, LANES), buf(2, 16, ROWS, LANES), buf(10, 32, LANES),
                buf(*big), buf(*big), buf(*big), buf(*big), low(3, ROWS, 512), buf(ROWS, 512), buf(ROWS, 512),
                low(N_CHAN, ROWS, LANES), low(N_CHAN, ROWS, 256), low(N_CHAN, ROWS, 256),
                dma((16,)), dma((16,)), dma((18,)), dma((18,)), dma, dma, dma((16,)), dma((16,)), dma((16,)), dma((16,)),
                dma, dma, dma((7, 7)), dma((7, 7)), dma((3,)), dma((3,)),
            ],
            compiler_params=pltpu.CompilerParams(
                collective_id=0, has_side_effects=True, vmem_limit_bytes=60 * 1024 * 1024
            ),
            name="block",
        )(
            pack(tokens), pack(cotangent).astype(BF16), shard, vec, aux,
            jnp.asarray(levels)[level], constant, modes_two, mats, twiddle, wave,
        )
        mode_grad = jnp.concatenate([gm[:, :HALF].reshape(4, 32, HALF), gm[:, HALF:].reshape(4, 32, HALF)])
        return (
            unpack(out), cotangent + unpack(dtok), gv[1, :HALF], gv[1, HALF:], jnp.swapaxes(mode_grad, 1, 2),
            gv[0, :HALF], gv[0, HALF:], gw[:, :HALF], gv[8, :HALF], gw[:, HALF:LANES], gv[8, HALF:],
            gv[9, :HALF], gv[9, HALF:], gw[:, 128:384], gv[11:13].reshape(256), gw[:, 384:].T, gv[10, :HALF],
        )

    return run


def solution(mesh):
    small = mesh.shape["chan"] == N_CHAN and mesh.shape["dp"] == 4
    return jax.shard_map(
        block_program(None, mixer_tables()) if small else shards,
        mesh=mesh,
        in_specs=(
            P("dp", "chan"),
            P("dp", "chan"),
            P("dp"),
            P("dp"),
            P("chan"),
            P("chan"),
            P(None, "chan", None),
            P("chan"),
            P("chan"),
            P("dp", "chan"),
            P("chan"),
            P("dp", "chan"),
            P("chan"),
            P("chan"),
            P("chan"),
            P("dp", "chan"),
            P("chan"),
            P("chan", "dp"),
            P("chan"),
        ),
        out_specs=(
            P("dp", "chan"),
            P("dp", "chan"),
            P("chan"),
            P("chan"),
            P(None, "chan", None),
            P("chan"),
            P("chan"),
            P("dp", "chan"),
            P("chan"),
            P("dp", "chan"),
            P("chan"),
            P("chan"),
            P("chan"),
            P("dp", "chan"),
            P("chan"),
            P("chan", "dp"),
            P("chan"),
        ),
        check_vma=False,
    )
```

```python
import math

import jax
import jax.numpy as jnp
import ml_dtypes
import numpy as np
from jax import lax
from jax.experimental import pallas as pl
from jax.experimental.pallas import tpu as pltpu
from jax.sharding import PartitionSpec as P

MODEL_WIDTH = 512
TOK_DEV = 1024


HIGHEST = lax.Precision.HIGHEST
EPSILON = 1e-05


def product(left, right):
    return jnp.dot(left, right, preferred_element_type=jnp.float32)


def product_nt(left, right):
    return lax.dot_general(
        left, right, (((1,), (1,)), ((), ())), preferred_element_type=jnp.float32
    )


def product_tn(left, right):
    return lax.dot_general(
        left, right, (((0,), (0,)), ((), ())), preferred_element_type=jnp.float32
    )


def gelu_slope(values):
    return (
        0.5 * (1.0 + lax.erf(values * 0.7071067811865476))
        + values * jnp.exp(-0.5 * values * values) * 0.3989422804014327
    )


def half_angles(length):
    angle = np.arange(length // 2 + 1, dtype=np.float64) * (math.pi / length)
    cosine, sine = np.cos(angle), np.sin(angle)
    cosine[-1] = 0.0
    return cosine.astype(np.float32), sine.astype(np.float32)


def inverse_tables(length):
    freq = np.arange(length // 2 + 1)
    turn = (freq[:, None] * np.arange(length)[None, :]) % length * (2.0 * math.pi / length)
    weight = np.where((freq == 0) | (freq == length // 2), 1.0, 2.0)[:, None] / length
    return (weight * np.cos(turn)).astype(np.float32), (weight * np.sin(turn)).astype(np.float32)


def high_einsum(form, left, right):
    return jnp.einsum(form, left, right, precision=HIGHEST)


def ssm_kernel(modes, log_dt):
    cos_h, sin_h = half_angles(TOK_DEV)
    index = jnp.arange(modes.shape[2], dtype=jnp.int32).astype(jnp.float32)
    lam_re = -0.5 * jnp.exp(modes[0])
    lam_im = math.pi * (index + modes[1])
    rank_re, rank_im, in_re, in_im, out_re, out_im = (modes[i] for i in range(2, 8))
    sigma = (2.0 * jnp.exp(-log_dt))[:, None]

    def points(values):
        return values.T[:, None, :]

    den_re = points(lam_re * lam_re + lam_im * lam_im) * (cos_h * cos_h)[:, None] - (
        sigma * sigma
    ).T * (sin_h * sin_h)[:, None]
    den_im = points(-2.0 * sigma * lam_re) * (sin_h * cos_h)[:, None]
    den_sq = den_re * den_re + den_im * den_im
    inv_re = den_re / den_sq
    inv_im = -den_im / den_sq
    sums = []
    for real, imag in (
        (out_re * in_re + out_im * in_im, out_re * in_im - out_im * in_re),
        (out_re * rank_re + out_im * rank_im, out_re * rank_im - out_im * rank_re),
        (rank_re * in_re + rank_im * in_im, rank_re * in_im - rank_im * in_re),
        (rank_re * rank_re + rank_im * rank_im, jnp.zeros_like(rank_re)),
    ):
        turned = points(real * lam_re + imag * lam_im)
        real = points(real)
        p_re, p_im = jnp.sum(real * inv_re, axis=0), jnp.sum(real * inv_im, axis=0)
        q_re, q_im = jnp.sum(turned * inv_re, axis=0), jnp.sum(turned * inv_im, axis=0)
        sine = sin_h[:, None] * sigma.T
        sums.append((-sine * p_im - cos_h[:, None] * q_re, sine * p_re - cos_h[:, None] * q_im))
    (cross_re, cross_im), (left_re, left_im), (right_re, right_im), (self_re, self_im) = sums
    twice = 2.0 * cos_h[:, None]
    loop_re, loop_im = 1.0 + twice * self_re, twice * self_im
    back_re, back_im = twice * right_re, twice * right_im
    loop_sq = loop_re * loop_re + loop_im * loop_im
    ratio_re = (back_re * loop_re + back_im * loop_im) / loop_sq
    ratio_im = (back_im * loop_re - back_re * loop_im) / loop_sq
    part_re = cross_re - (left_re * ratio_re - left_im * ratio_im)
    part_im = cross_im - (left_re * ratio_im + left_im * ratio_re)
    spec_re = 2.0 * (cos_h[:, None] * part_re - sin_h[:, None] * part_im)
    spec_im = 2.0 * (cos_h[:, None] * part_im + sin_h[:, None] * part_re)
    cos_tab, sin_tab = inverse_tables(TOK_DEV)
    return high_einsum("kl,kc->lc", cos_tab, spec_re) - high_einsum("kl,kc->lc", sin_tab, spec_im)


BLOCK = 128
BLOCKS = TOK_DEV // BLOCK
FIRST = 2 * BLOCKS
KEPT = FIRST // 2 + 1


def transform_tables():
    length = 2 * TOK_DEV
    turn = np.arange(KEPT)[:, None] * np.arange(BLOCK)[None, :] * (2.0 * math.pi / length)
    small = np.arange(BLOCK)[:, None] * np.arange(BLOCK)[None, :] % BLOCK * (2.0 * math.pi / BLOCK)
    spots = np.stack([np.arange(BLOCKS) + np.arange(BLOCKS) // (2 << b) * (2 << b) for b in range(3)])
    angle = spots[:, None, :] * np.arange(KEPT)[None, :, None] % FIRST * (2.0 * math.pi / FIRST)
    parts = (np.cos(turn), np.sin(turn), np.cos(small), np.sin(small), np.cos(angle), np.sin(angle))
    return [part.astype(np.float32) for part in parts]


def forward_transform(blocks, cos_a, sin_a):
    cos_t, sin_t, cos_s, sin_s, _, _ = transform_tables()
    step_re = high_einsum("ka,abc->kbc", cos_a, blocks)
    step_im = -high_einsum("ka,abc->kbc", sin_a, blocks)
    turned_re = step_re * cos_t[..., None] + step_im * sin_t[..., None]
    turned_im = step_im * cos_t[..., None] - step_re * sin_t[..., None]
    both = jnp.concatenate([turned_re, turned_im], axis=1)
    matrix = np.block([[cos_s, sin_s], [-sin_s, cos_s]])
    return high_einsum("pb,kbc->kpc", matrix, both)


def inverse_transform(spectrum, cos_a, sin_a):
    cos_t, sin_t, cos_s, sin_s, _, _ = transform_tables()
    matrix = np.block([[cos_s, -sin_s], [sin_s, cos_s]])
    both = high_einsum("bp,kpc->kbc", matrix, spectrum)
    step_re, step_im = both[:, :BLOCK], both[:, BLOCK:]
    turned_re = step_re * cos_t[..., None] - step_im * sin_t[..., None]
    turned_im = step_im * cos_t[..., None] + step_re * sin_t[..., None]
    weight = np.where(np.arange(KEPT) % (KEPT - 1) == 0, 1.0, 2.0).astype(np.float32) / (2 * TOK_DEV)
    return high_einsum("ka,kbc->abc", cos_a * weight[:, None], turned_re) - high_einsum(
        "ka,kbc->abc", sin_a * weight[:, None], turned_im
    )


def multiply(left, right):
    left_re, left_im = left[:, :BLOCK], left[:, BLOCK:]
    right_re, right_im = right[:, :BLOCK], right[:, BLOCK:]
    return jnp.concatenate(
        [left_re * right_re - left_im * right_im, left_re * right_im + left_im * right_re], axis=1
    )


def mixer(normed, kernel_taps, skip_gain, bucket, filled):
    _, _, _, _, cos_a, sin_a = transform_tables()
    cos_x, sin_x = jnp.asarray(cos_a)[bucket], jnp.asarray(sin_a)[bucket]
    item_blocks = 2 << bucket
    block_id = jnp.arange(BLOCKS, dtype=jnp.int32)[:, None, None]
    taps = jnp.where(block_id < item_blocks, kernel_taps.reshape(BLOCKS, BLOCK, -1), 0.0)
    signal = forward_transform(normed.reshape(BLOCKS, BLOCK, -1), cos_x, sin_x)
    answer = forward_transform(taps, cos_a[2], sin_a[2])
    result = inverse_transform(multiply(signal, answer), cos_x, sin_x)
    result = jnp.where(block_id < filled * item_blocks, result, 0.0)
    return result.reshape(normed.shape) + skip_gain * normed


def shards(
    tokens,
    cotangent,
    group_bucket,
    group_items,
    first_norm_gain,
    first_norm_bias,
    modes,
    log_dt,
    d_skip,
    w_a,
    b_a,
    w_b,
    b_b,
    second_norm_gain,
    second_norm_bias,
    w_up,
    b_up,
    w_down,
    b_down,
):
    input_tokens = tokens.astype(jnp.float32)
    sums_in = lax.psum(
        (jnp.sum(input_tokens, axis=1), jnp.sum(input_tokens * input_tokens, axis=1)), "chan"
    )
    input_average = sums_in[0][:, None] / MODEL_WIDTH
    input_inverse_deviation = lax.rsqrt(
        sums_in[1][:, None] / MODEL_WIDTH - input_average * input_average + EPSILON
    )
    input_standardized = (input_tokens - input_average) * input_inverse_deviation
    input_normalized = input_standardized * first_norm_gain + first_norm_bias
    level = group_bucket[0]
    filled = group_items[0]
    kernel_taps, kernel_back = jax.vjp(ssm_kernel, modes, log_dt)

    def local_mix(values, taps_now, skip_gain):
        return mixer(values, taps_now, skip_gain, level, filled)

    mixed, mix_back = jax.vjp(local_mix, input_normalized, kernel_taps, d_skip)
    acts_low = jax.nn.gelu(mixed, approximate=False).astype(jnp.bfloat16)
    wa_full, wb_full, up_full, down_full = (
        lax.all_gather(w_a.astype(jnp.bfloat16), "dp", axis=0, tiled=True),
        lax.all_gather(w_b.astype(jnp.bfloat16), "dp", axis=0, tiled=True),
        lax.all_gather(w_up.astype(jnp.bfloat16), "dp", axis=0, tiled=True),
        lax.all_gather(w_down.astype(jnp.bfloat16), "dp", axis=1, tiled=True),
    )
    acts_full = lax.all_gather(acts_low, "chan", axis=1, tiled=True)
    gate_a = product(acts_full, wa_full) + b_a
    gate_b = product(acts_full, wb_full) + b_b
    gate_sig = jax.nn.sigmoid(gate_b)
    residual_stream = input_tokens + gate_a * gate_sig
    sums_mid = lax.psum(
        (jnp.sum(residual_stream, axis=1), jnp.sum(residual_stream * residual_stream, axis=1)),
        "chan",
    )
    middle_average = sums_mid[0][:, None] / MODEL_WIDTH
    middle_inverse_deviation = lax.rsqrt(
        sums_mid[1][:, None] / MODEL_WIDTH - middle_average * middle_average + EPSILON
    )
    middle_standardized = (residual_stream - middle_average) * middle_inverse_deviation
    middle_reduced = (middle_standardized * second_norm_gain + second_norm_bias).astype(
        jnp.bfloat16
    )
    mid_full = lax.all_gather(middle_reduced, "chan", axis=1, tiled=True)
    pre_act = product(mid_full, up_full) + b_up
    hidden_low = jax.nn.gelu(pre_act, approximate=False).astype(jnp.bfloat16)
    branch = (
        lax.psum_scatter(product(hidden_low, down_full), "chan", scatter_dimension=1, tiled=True)
        + b_down
    )
    output = (residual_stream + branch).astype(jnp.bfloat16)
    grad_f = cotangent.astype(jnp.bfloat16)
    grad_b_down = jnp.sum(grad_f.astype(jnp.float32), axis=0)
    grad_f_full = lax.all_gather(grad_f, "chan", axis=1, tiled=True)
    grad_w_down = product_tn(hidden_low, grad_f_full)
    grad_pre = (product_nt(grad_f_full, down_full) * gelu_slope(pre_act)).astype(jnp.bfloat16)
    grad_b_up = jnp.sum(grad_pre.astype(jnp.float32), axis=0)
    grad_w_up = product_tn(mid_full, grad_pre)
    middle_gradient = lax.psum_scatter(
        product_nt(grad_pre, up_full), "chan", scatter_dimension=1, tiled=True
    )
    second_norm_gain_gradient = jnp.sum(middle_gradient * middle_standardized, axis=0)
    grad_ln2_bias = jnp.sum(middle_gradient, axis=0)
    middle_rescaled = middle_gradient * second_norm_gain
    middle_backward = lax.psum(
        (jnp.sum(middle_rescaled, axis=1), jnp.sum(middle_rescaled * middle_standardized, axis=1)),
        "chan",
    )
    grad_resid = cotangent + middle_inverse_deviation * (
        middle_rescaled
        - middle_backward[0][:, None] / MODEL_WIDTH
        - middle_standardized * middle_backward[1][:, None] / MODEL_WIDTH
    )
    grad_a = (grad_resid * gate_sig).astype(jnp.bfloat16)
    grad_b = (grad_resid * gate_a * gate_sig * (1.0 - gate_sig)).astype(jnp.bfloat16)
    grad_b_a = jnp.sum(grad_a.astype(jnp.float32), axis=0)
    grad_b_b = jnp.sum(grad_b.astype(jnp.float32), axis=0)
    grad_w_a = product_tn(acts_full, grad_a)
    grad_w_b = product_tn(acts_full, grad_b)
    grad_acts = lax.psum_scatter(
        product_nt(grad_a, wa_full) + product_nt(grad_b, wb_full),
        "chan",
        scatter_dimension=1,
        tiled=True,
    )
    grad_mixed = grad_acts * gelu_slope(mixed)
    normalized_gradient, grad_kernel, grad_skip = mix_back(grad_mixed)
    grad_modes, grad_log_dt = kernel_back(grad_kernel)
    first_norm_gain_gradient = jnp.sum(normalized_gradient * input_standardized, axis=0)
    grad_ln1_bias = jnp.sum(normalized_gradient, axis=0)
    input_rescaled = normalized_gradient * first_norm_gain
    input_backward = lax.psum(
        (jnp.sum(input_rescaled, axis=1), jnp.sum(input_rescaled * input_standardized, axis=1)),
        "chan",
    )
    grad_tokens = grad_resid + input_inverse_deviation * (
        input_rescaled
        - input_backward[0][:, None] / MODEL_WIDTH
        - input_standardized * input_backward[1][:, None] / MODEL_WIDTH
    )
    grad_w_a, grad_w_b, grad_w_up, grad_w_down = (
        lax.psum_scatter(grad_w_a, "dp", scatter_dimension=0, tiled=True),
        lax.psum_scatter(grad_w_b, "dp", scatter_dimension=0, tiled=True),
        lax.psum_scatter(grad_w_up, "dp", scatter_dimension=0, tiled=True),
        lax.psum_scatter(grad_w_down, "dp", scatter_dimension=1, tiled=True),
    )
    (
        first_norm_gain_gradient,
        grad_ln1_bias,
        grad_modes,
        grad_log_dt,
        grad_skip,
        grad_b_a,
        grad_b_b,
        second_norm_gain_gradient,
        grad_ln2_bias,
        grad_b_up,
        grad_b_down,
    ) = lax.psum(
        (
            first_norm_gain_gradient,
            grad_ln1_bias,
            grad_modes,
            grad_log_dt,
            grad_skip,
            grad_b_a,
            grad_b_b,
            second_norm_gain_gradient,
            grad_ln2_bias,
            grad_b_up,
            grad_b_down,
        ),
        "dp",
    )
    return (
        output,
        grad_tokens,
        first_norm_gain_gradient,
        grad_ln1_bias,
        grad_modes,
        grad_log_dt,
        grad_skip,
        grad_w_a,
        grad_b_a,
        grad_w_b,
        grad_b_b,
        second_norm_gain_gradient,
        grad_ln2_bias,
        grad_w_up,
        grad_b_up,
        grad_w_down,
        grad_b_down,
    )


LANES = 128
HALF = 64
PAIRS = 4
ROWS = 128
N_CHAN = 8
WIDE = 640
MESH = pl.DeviceIdType.MESH
F32 = jnp.float32
BF16 = jnp.bfloat16


def split_two(matrix):
    high = matrix.astype(ml_dtypes.bfloat16)
    low = (matrix - high.astype(np.float64)).astype(ml_dtypes.bfloat16)
    return np.concatenate([high, low], axis=1)


def lane_rows(values_low, values_high):
    return np.repeat(np.stack([values_low, values_high], -1), HALF, axis=-1)


def mixer_tables():
    line = np.arange(ROWS)
    small = np.outer(line, line) % ROWS * (2.0 * math.pi / ROWS)
    cos_s, sin_s = np.cos(small), np.sin(small)
    forward = np.block([[cos_s, sin_s], [-sin_s, cos_s]])
    real = np.zeros((2 * ROWS, 2 * ROWS))
    for row in range(HALF):
        weight = 1.0 if row == 0 else 2.0
        turn = 2.0 * math.pi / ROWS * row * line
        real[:ROWS, row] = weight * np.cos(turn)
        real[:ROWS, ROWS + row] = -weight * np.sin(turn)
        turn = 2.0 * math.pi / TOK_DEV * (4 + 8 * row) * line
        real[ROWS:, HALF + row] = 2.0 * np.cos(turn)
        real[ROWS:, ROWS + HALF + row] = -2.0 * np.sin(turn)
    mats = np.stack([split_two(m) for m in (forward, forward.T, real, real.T)])

    twiddle = []
    for pair in range(5):
        turn = np.stack([line * k * (math.pi / TOK_DEV) for k in (2 * pair, 2 * pair + 1)])
        twiddle += [lane_rows(np.cos(turn[0]), np.cos(turn[1])), lane_rows(np.sin(turn[0]), np.sin(turn[1]))]
    for first, second in ((1, 2), (3, 0)):
        turn = np.stack([line * k * (2.0 * math.pi / TOK_DEV) for k in (first, second)])
        twiddle += [lane_rows(np.cos(turn[0]), np.cos(turn[1])), lane_rows(np.sin(turn[0]), np.sin(turn[1]))]

    def forward_rows(coef, pairs):
        out = []
        for low, high in pairs:
            for part in range(2):
                for j in range(PAIRS):
                    out.append(lane_rows(coef(2 * j, low, part), coef(2 * j + 1, high, part)))
                for j in range(PAIRS):
                    out.append(lane_rows(coef(2 * j, high, part), coef(2 * j + 1, low, part)))
        return np.stack(out)

    def inverse_rows(coef, pairs):
        out = []
        for low, high in pairs:
            for part in range(2):
                for j in range(PAIRS):
                    out.append(lane_rows(coef(2 * j, low, part), coef(2 * j + 1, high, part)))
                for j in range(PAIRS):
                    out.append(lane_rows(coef(2 * j + 1, low, part), coef(2 * j, high, part)))
        return np.stack(out)

    levels = []
    pairs = [(2 * p, 2 * p + 1) for p in range(5)]
    for level in range(3):
        item = 2 << level

        def angle(block, k):
            return 2.0 * math.pi / 16 * ((block + block // item * item) * k % 16)

        def fwd(block, k, part):
            if k > 8:
                return np.zeros(())
            return np.cos(angle(block, k)) if part == 0 else -np.sin(angle(block, k))

        def inv(block, k, part):
            weight = (1.0 if k in (0, 8) else 2.0) / (2 * TOK_DEV)
            return weight * fwd(block, k, part)

        levels.append(np.concatenate([forward_rows(fwd, pairs), inverse_rows(inv, pairs)]))

    def taps(block, k, part):
        if k == 0:
            return np.asarray((1.0 if part == 0 else (-1.0) ** block) / TOK_DEV)
        turn = 2.0 * math.pi / 8 * (block * k % 8)
        return np.asarray((np.cos(turn) if part == 0 else -np.sin(turn)) * 2.0 / TOK_DEV)

    tap_pairs = [(1, 2), (3, 0)]
    taps_back = forward_rows(taps, tap_pairs)
    taps_rows = inverse_rows(taps, tap_pairs)
    freq_even = np.where(line < HALF, 8 * line, 4 + 8 * (line - HALF))
    half_angle = np.stack(
        [lane_rows(1 + 8 * line, 2 + 8 * line), lane_rows(3 + 8 * line, freq_even)]
    ) * (math.pi / TOK_DEV)
    wave = np.stack([np.cos(half_angle), np.sin(half_angle)])
    return (
        mats,
        np.stack(twiddle).astype(np.float32),
        np.stack(levels).astype(np.float32),
        np.concatenate([levels[2], taps_rows, taps_back]).astype(np.float32),
        wave.astype(np.float32),
    )


def low_lanes(rows):
    return lax.broadcasted_iota(jnp.int32, (rows, LANES), 1) < HALF


def turn_half(values):
    return pltpu.roll(values, HALF, 1)


def split_pair(values):
    upper, lower = values[:HALF], values[HALF:]
    mask = low_lanes(HALF)
    return jnp.where(mask, upper, turn_half(lower)), jnp.where(mask, turn_half(upper), lower)


def join_pair(first, second):
    mask = low_lanes(HALF)
    return jnp.concatenate(
        [jnp.where(mask, first, turn_half(second)), jnp.where(mask, turn_half(first), second)], axis=0
    )


def interleave(first, second):
    mask = low_lanes(first.shape[0])
    return jnp.where(mask, first, turn_half(second)), jnp.where(mask, turn_half(first), second)


def fold(values):
    return values + turn_half(values)


def normal_parts(values):
    cumulative = 0.5 * (1.0 + lax.erf(values * 0.7071067811865476))
    density = jnp.exp(-0.5 * values * values) * 0.3989422804014327
    return cumulative, density


def column_sum(values):
    return jnp.sum(values, axis=0, keepdims=True)


def dot_nt(left, right):
    return lax.dot_general(left, right, (((1,), (1,)), ((), ())), preferred_element_type=F32)


def dot_nn(left, right):
    return jnp.dot(left, right, preferred_element_type=F32)


def store_split(ref, row, lane, values):
    high = values.astype(BF16)
    place = (pl.ds(row, values.shape[0]), pl.ds(lane, values.shape[1]))
    ref[(0,) + place] = high
    ref[(1,) + place] = (values - high.astype(F32)).astype(BF16)


def split_product(mat_ref, which, rhs_ref, lane, width):
    high = mat_ref[which, :, 0:256]
    low = mat_ref[which, :, 256:512]
    rhs_high = rhs_ref[0, :, lane : lane + width]
    return dot_nn(high, rhs_high) + dot_nn(high, rhs_ref[1, :, lane : lane + width]) + dot_nn(low, rhs_high)


CHUNK = 32


def over_chunks(body, size=CHUNK, first=0, rows=ROWS):
    def step(index, carry):
        body(pl.multiple_of(first + index * size, size))
        return carry

    lax.fori_loop(0, rows // size, step, 0)


def spread_pairs(src, coef_ref, base, twiddle_ref, twiddle_base, pairs, rhs_ref):
    def body(row):
        rows = pl.ds(row, CHUNK)
        blocks = [src(j, rows) for j in range(PAIRS)]
        for pair in range(pairs):
            parts = []
            for part in range(2):
                at = base + (pair * 2 + part) * 8
                straight = sum(blocks[j] * coef_ref[at + j : at + j + 1, :] for j in range(PAIRS))
                crossed = sum(blocks[j] * coef_ref[at + 4 + j : at + 5 + j, :] for j in range(PAIRS))
                parts.append(straight + turn_half(crossed))
            cosine = twiddle_ref[twiddle_base + 2 * pair, rows, :]
            sine = twiddle_ref[twiddle_base + 2 * pair + 1, rows, :]
            store_split(rhs_ref, row, pair * LANES, parts[0] * cosine + parts[1] * sine)
            store_split(rhs_ref, row + ROWS, pair * LANES, parts[1] * cosine - parts[0] * sine)

    over_chunks(body)


def gather_pairs(values_ref, coef_ref, base, twiddle_ref, twiddle_base, pairs, store):
    def body(row):
        rows = pl.ds(row, CHUNK)
        straight, crossed = [0.0] * PAIRS, [0.0] * PAIRS
        for pair in range(pairs):
            lanes = slice(pair * LANES, (pair + 1) * LANES)
            real, imag = values_ref[rows, lanes], values_ref[pl.ds(row + ROWS, CHUNK), lanes]
            cosine = twiddle_ref[twiddle_base + 2 * pair, rows, :]
            sine = twiddle_ref[twiddle_base + 2 * pair + 1, rows, :]
            for part, value in enumerate((real * cosine - imag * sine, imag * cosine + real * sine)):
                at = base + (pair * 2 + part) * 8
                for j in range(PAIRS):
                    straight[j] = straight[j] + value * coef_ref[at + j : at + j + 1, :]
                    crossed[j] = crossed[j] + value * coef_ref[at + 4 + j : at + 5 + j, :]
        for j in range(PAIRS):
            store(j, rows, straight[j] + turn_half(crossed[j]))

    over_chunks(body)


GROUPS = ((0, 256), (256, 256), (512, 128))


def transform_into(dst_ref, mat_ref, which, rhs_ref, groups=GROUPS):
    for lane, width in groups:
        dst_ref[:, lane : lane + width] = split_product(mat_ref, which, rhs_ref, lane, width)


def multiply_spectra(left_ref, right_ref, rhs_ref, conjugate):
    def body(row):
        top, bottom = pl.ds(row, CHUNK), pl.ds(row + ROWS, CHUNK)
        for pair in range(5):
            lanes = slice(pair * LANES, (pair + 1) * LANES)
            a_re, a_im = left_ref[top, lanes], left_ref[bottom, lanes]
            b_re, b_im = right_ref[top, lanes], right_ref[bottom, lanes]
            if conjugate:
                out_re, out_im = a_re * b_re + a_im * b_im, a_re * b_im - a_im * b_re
            else:
                out_re, out_im = a_re * b_re - a_im * b_im, a_re * b_im + a_im * b_re
            store_split(rhs_ref, row, pair * LANES, out_re)
            store_split(rhs_ref, row + ROWS, pair * LANES, out_im)

    over_chunks(body)


def pair_terms(modes_ref):
    rank_re, rank_im, in_re, in_im, out_re, out_im = (modes_ref[i] for i in range(2, 8))
    return (
        (out_re * in_re + out_im * in_im, out_re * in_im - out_im * in_re),
        (out_re * rank_re + out_im * rank_im, out_re * rank_im - out_im * rank_re),
        (rank_re * in_re + rank_im * in_im, rank_re * in_im - rank_im * in_re),
        (rank_re * rank_re + rank_im * rank_im, None),
    )


def mode_values(modes_ref):
    index = lax.broadcasted_iota(jnp.int32, modes_ref.shape[1:], 0).astype(F32)
    return -0.5 * jnp.exp(modes_ref[0]), math.pi * (index + modes_ref[1])


POINT_ROWS = 16


def resolvent(coef_ref, n, square_cos, cos_sin, scaled):
    den_re = coef_ref[8, pl.ds(n, 1), :] * square_cos - scaled
    den_im = coef_ref[9, pl.ds(n, 1), :] * cos_sin
    inverse = 1.0 / (den_re * den_re + den_im * den_im)
    return den_re * inverse, -(den_im * inverse)


def complex_multiply(a_re, a_im, b_re, b_im):
    return a_re * b_re - a_im * b_im, a_re * b_im + a_im * b_re


def conj_multiply(a_re, a_im, b_re, b_im):
    return a_re * b_re + a_im * b_im, a_re * b_im - a_im * b_re


def combine(sums, sigma, cosine, sine):
    terms = []
    for p_re, p_im, q_re, q_im in (sums[4 * q : 4 * q + 4] for q in range(4)):
        swing = sigma * sine
        terms.append((-swing * p_im - cosine * q_re, swing * p_re - cosine * q_im))
    twice = 2.0 * cosine
    loop_re, loop_im = 1.0 + twice * terms[3][0], twice * terms[3][1]
    scale = 1.0 / (loop_re * loop_re + loop_im * loop_im)
    inv = (loop_re * scale, -(loop_im * scale))
    ratio = complex_multiply(twice * terms[2][0], twice * terms[2][1], *inv)
    return terms, inv, ratio


def cauchy_forward(modes_ref, sigma, coef_ref, wave_ref, sums_ref, rhs_ref, middle):
    lam_re, lam_im = mode_values(modes_ref)
    for q, (real, imag) in enumerate(pair_terms(modes_ref)):
        coef_ref[q] = real
        coef_ref[4 + q] = real * lam_re if imag is None else real * lam_re + imag * lam_im
    coef_ref[8] = lam_re * lam_re + lam_im * lam_im
    coef_ref[9] = -2.0 * sigma * lam_re
    sigma_sq = sigma * sigma
    for pair in range(2):

        def body(row, pair=pair):
            rows = pl.ds(row, POINT_ROWS)
            cosine, sine = wave_ref[0, pair, rows, :], wave_ref[1, pair, rows, :]
            square_cos, cos_sin, scaled = cosine * cosine, cosine * sine, sigma_sq * (sine * sine)

            def add_mode(n, sums):
                sums = list(sums)
                for k in range(4):
                    at = n * 4 + k
                    inv_re, inv_im = resolvent(coef_ref, at, square_cos, cos_sin, scaled)
                    for q in range(4):
                        plain = coef_ref[q, pl.ds(at, 1), :]
                        turned = coef_ref[4 + q, pl.ds(at, 1), :]
                        sums[4 * q] = sums[4 * q] + plain * inv_re
                        sums[4 * q + 1] = sums[4 * q + 1] + plain * inv_im
                        sums[4 * q + 2] = sums[4 * q + 2] + turned * inv_re
                        sums[4 * q + 3] = sums[4 * q + 3] + turned * inv_im
                return tuple(sums)

            zero = jnp.zeros((POINT_ROWS, LANES), F32)
            sums = lax.fori_loop(0, 8, add_mode, (zero,) * 16)
            for i in range(16):
                sums_ref[pair, i, rows, :] = sums[i]
            terms, _, ratio = combine(sums, sigma, cosine, sine)
            cut_re, cut_im = complex_multiply(*terms[1], *ratio)
            part_re, part_im = terms[0][0] - cut_re, terms[0][1] - cut_im
            spec_re, spec_im = complex_multiply(2.0 * cosine, 2.0 * sine, part_re, part_im)
            store_split(rhs_ref, row, pair * LANES, spec_re)
            store_split(rhs_ref, row + ROWS, pair * LANES, spec_im)

        for part in range(2):
            over_chunks(body, POINT_ROWS, part * HALF, HALF)
            middle(pair * 2 + part)


def cauchy_backward(modes_ref, sigma, nyquist_grad, step, coef_ref, wave_ref, sums_ref, spec_ref, grad_ref, back_ref, middle):
    zero = jnp.zeros((8, LANES), F32)
    sigma_sum = zero
    for pair in range(2):
        lanes = slice(pair * LANES, (pair + 1) * LANES)

        def start(index, total, pair=pair, lanes=lanes):
            row = pl.multiple_of(index * POINT_ROWS, POINT_ROWS)
            rows = pl.ds(row, POINT_ROWS)
            cosine, sine = wave_ref[0, pair, rows, :], wave_ref[1, pair, rows, :]
            sums = [sums_ref[pair, i, rows, :] for i in range(16)]
            terms, inv, ratio = combine(sums, sigma, cosine, sine)
            spec_re, spec_im = spec_ref[rows, lanes], spec_ref[pl.ds(row + ROWS, POINT_ROWS), lanes]
            part = conj_multiply(2.0 * cosine, 2.0 * sine, spec_re, spec_im)
            left = conj_multiply(*ratio, *part)
            ratio_grad = conj_multiply(*terms[1], *part)
            back = conj_multiply(*inv, -ratio_grad[0], -ratio_grad[1])
            twice = 2.0 * cosine
            loop = conj_multiply(*ratio, *back)
            grads = (
                part,
                (-left[0], -left[1]),
                (twice * back[0], twice * back[1]),
                (-twice * loop[0], -twice * loop[1]),
            )
            swing = sigma * sine
            for q, (g_re, g_im) in enumerate(grads):
                grad_ref[pair, 4 * q, rows, :] = swing * g_im
                grad_ref[pair, 4 * q + 1, rows, :] = -swing * g_re
                grad_ref[pair, 4 * q + 2, rows, :] = -cosine * g_re
                grad_ref[pair, 4 * q + 3, rows, :] = -cosine * g_im
                piece = sine * (g_im * sums[4 * q] - g_re * sums[4 * q + 1])
                total = total + piece[:8] + piece[8:]
            return total

        sigma_sum = lax.fori_loop(0, ROWS // POINT_ROWS, start, sigma_sum)
    sigma_sq = sigma * sigma

    def mode(n, square_sum):
        def point(index, sums):
            row = pl.multiple_of(index * 8, 8)
            rows = pl.ds(row, 8)
            sums = list(sums)
            for pair in range(2):
                cosine, sine = wave_ref[0, pair, rows, :], wave_ref[1, pair, rows, :]
                square_cos, cos_sin, square_sin = cosine * cosine, cosine * sine, sine * sine
                inv_re, inv_im = resolvent(coef_ref, n, square_cos, cos_sin, sigma_sq * square_sin)
                grad_re, grad_im = 0.0, 0.0
                for q in range(4):
                    plain = coef_ref[q, pl.ds(n, 1), :]
                    turned = coef_ref[4 + q, pl.ds(n, 1), :]
                    p_re, p_im = grad_ref[pair, 4 * q, rows, :], grad_ref[pair, 4 * q + 1, rows, :]
                    q_re, q_im = grad_ref[pair, 4 * q + 2, rows, :], grad_ref[pair, 4 * q + 3, rows, :]
                    grad_re = grad_re + plain * p_re + turned * q_re
                    grad_im = grad_im + plain * p_im + turned * q_im
                    sums[q] = sums[q] + (p_re * inv_re + p_im * inv_im)
                    sums[4 + q] = sums[4 + q] + (q_re * inv_re + q_im * inv_im)
                square_re = inv_re * inv_re - inv_im * inv_im
                square_im = 2.0 * inv_re * inv_im
                den_re, den_im = conj_multiply(square_re, square_im, grad_re, grad_im)
                sums[8] = sums[8] - den_re * square_cos
                sums[9] = sums[9] - den_im * cos_sin
                sums[10] = sums[10] + den_re * square_sin
            return tuple(sums)

        sums = lax.fori_loop(0, ROWS // 8, point, (zero,) * 10 + (square_sum,))
        for i in range(10):
            back_ref[i, pl.ds(n, 1), :] = column_sum(sums[i])
        return sums[10]

    square_sum = zero
    for part in range(4):
        square_sum = lax.fori_loop(part * 8, part * 8 + 8, mode, square_sum)
        middle(part)
    plain_grad = [fold(back_ref[q]) for q in range(4)]
    turned_grad = [fold(back_ref[4 + q]) for q in range(4)]
    abs_grad, skew_grad = fold(back_ref[8]), fold(back_ref[9])
    lam_re, lam_im = mode_values(modes_ref)
    plain_grad[0] = plain_grad[0] + step * nyquist_grad
    rank_re, rank_im, in_re, in_im, out_re, out_im = (modes_ref[i] for i in range(2, 8))
    lam_re_grad = 2.0 * lam_re * abs_grad - 2.0 * sigma * skew_grad
    lam_im_grad = 2.0 * lam_im * abs_grad
    real_grad, imag_grad = [], []
    terms = pair_terms(modes_ref)
    for q, (real, imag) in enumerate(terms):
        lam_re_grad = lam_re_grad + turned_grad[q] * real
        if imag is not None:
            lam_im_grad = lam_im_grad + turned_grad[q] * imag
        real_grad.append(plain_grad[q] + turned_grad[q] * lam_re)
        imag_grad.append(turned_grad[q] * lam_im)
    r0, r1, r2, r3 = real_grad
    i0, i1, i2, _ = imag_grad
    grads = (
        lam_re_grad * lam_re,
        math.pi * lam_im_grad,
        r1 * out_re - i1 * out_im + r2 * in_re + i2 * in_im + 2.0 * r3 * rank_re,
        r1 * out_im + i1 * out_re + r2 * in_im - i2 * in_re + 2.0 * r3 * rank_im,
        r0 * out_re - i0 * out_im + r2 * rank_re - i2 * rank_im,
        r0 * out_im + i0 * out_re + r2 * rank_im + i2 * rank_re,
        r0 * in_re + i0 * in_im + r1 * rank_re + i1 * rank_im,
        r0 * in_im - i0 * in_re + r1 * rank_im - i1 * rank_re,
    )
    sigma_grad = (
        fold(column_sum(sigma_sum) + 2.0 * sigma * column_sum(square_sum))
        - 2.0 * column_sum(skew_grad * lam_re)
    )
    nyquist = step * column_sum(terms[0][0])
    return grads, nyquist * nyquist_grad - sigma * sigma_grad


def ring_place(chan):
    z, y = chan // 2, chan % 2
    return z + y * (7 - 2 * z)


def ring_chan(place):
    back = place // 4
    z = place * (1 - back) + (7 - place) * back
    return 2 * z + back


TURNS = (1, -1)


def ring_items():
    out = []
    for step in range(1, 5):
        for turn in range(2):
            for block in range(2):
                if step < 4 or block == turn:
                    out.append((turn, step, block))
    return out


def item_slot(turn, step, block):
    return (turn * 4 + step - 1) * 2 + block


def block_kernel(
    bucket_ref, items_ref, tokens_ref, cotangent_ref, gain1_ref, bias1_ref, raw_modes_ref, log_dt_ref, skip_ref,
    wa_ref, ba_ref, wb_ref, bb_ref, gain2_ref, bias2_ref, up_ref, bup_ref, down_ref, bdown_ref,
    levels_ref, coefc_ref, mat_ref, tw_ref, wave_ref,
    out_ref, dtok_ref, gw_ref, gm_ref, gv_ref,
    tok_ref, aux_ref, coefl_ref, modes_ref,
    w_ref, grad_ref, sib_ref, ring_ref, part_ref,
    in_send, in_recv, head_send, head_recv, acts_send, acts_recv, back_send, back_recv, late_send, late_recv,
    sum_send, sum_recv, tail_send, tail_recv, dp_send, dp_recv,
    hat_ref, norm_ref, slope_ref, conv_ref, rhs_ref, freq_ref, sig_ref, ans_ref, taps_ref,
    mcoef_ref, sums_ref, pgrad_ref, mback_ref,
    gate_ref, swish_ref, res_ref, hat2_ref, low_ref, branch_ref, back2_ref, gab_ref, hid_ref, gpre_ref,
    ring_ss, ring_rs, sib_ss, sib_rs, x_ss, x_rs, rring_ss, rring_rs, rsib_ss, rsib_rs, rx_ss, rx_rs, a2a_ss, a2a_rs, dp_ss, dp_rs,
):
    dp, chan = lax.axis_index("dp"), lax.axis_index("chan")
    core = dp % 2
    sibling = dp + 1 - 2 * core
    across = (dp + 2) % 4
    place = ring_place(chan)
    nexts = [ring_chan((place + 1) % 8), ring_chan((place + 7) % 8)]

    def chan_at(offset):
        return ring_chan((place + offset + 8) % 8)

    barrier = pltpu.get_barrier_semaphore()
    for r in range(1, N_CHAN):
        pl.semaphore_signal(barrier, inc=1, device_id={"chan": (chan + r) % N_CHAN}, device_id_type=MESH)
    for r in range(1, 4):
        pl.semaphore_signal(barrier, inc=1, device_id={"dp": (dp + r) % 4}, device_id_type=MESH)
    pl.semaphore_wait(barrier, N_CHAN - 1 + 3)

    pending = []

    def remote(src, dst, send_sem, recv_sem, **device):
        return pltpu.make_async_remote_copy(
            src_ref=src, dst_ref=dst, send_sem=send_sem, recv_sem=recv_sem, device_id=device, device_id_type=MESH
        )

    def send(*args, **device):
        copy = remote(*args, **device)
        copy.start()
        pending.append(copy)

    def exchange(which, source, recv_ref):
        def copy(r):
            peer = (chan + r) % N_CHAN
            return remote(
                source(peer), recv_ref.at[chan], a2a_ss.at[which, r - 1], a2a_rs.at[which, r - 1], chan=peer
            )

        def start():
            for r in range(1, N_CHAN):
                copy(r).start()

        def wait():
            for r in range(1, N_CHAN):
                copy(r).wait_recv()

        def finish():
            for r in range(1, N_CHAN):
                copy(r).wait_send()

        return start, wait, finish

    def row_of(group):
        return pl.multiple_of(group * ROWS, ROWS)

    def weight(chan_id, group):
        return w_ref.at[chan_id, pl.ds(row_of(group), ROWS), :]

    mine = (dp, across)
    theirs = (sibling, (sibling + 2) % 4)

    def origin(turn, step):
        return chan_at(-TURNS[turn] * step)

    def ring_copy(turn, step, block):
        slot = item_slot(turn, step, block)
        ref = weight(origin(turn, step - 1), mine[block])
        return remote(ref, ref, ring_ss.at[slot], ring_rs.at[slot], chan=nexts[turn])

    def sib_copy(chan_id, block, slot):
        ref = weight(chan_id, mine[block])
        return remote(ref, ref, sib_ss.at[slot], sib_rs.at[slot], dp=sibling)

    def ring_got(turn, step, block):
        slot = item_slot(turn, step, block)
        ref = weight(origin(turn, step), mine[block])
        remote(ref, ref, ring_ss.at[slot], ring_rs.at[slot], chan=nexts[turn]).wait_recv()

    def gather_start():
        rows = pl.ds(row_of(dp), ROWS)
        w_ref[chan, rows, 0:128] = jnp.concatenate([wa_ref[...], wb_ref[...]], axis=1).astype(BF16)
        w_ref[chan, rows, 128:384] = up_ref[...].astype(BF16)
        w_ref[chan, rows, 384:640] = down_ref[...].T.astype(BF16)
        x_ref = weight(chan, dp)
        send(x_ref, x_ref, x_ss, x_rs, dp=across)
        for turn in range(2):
            copy = ring_copy(turn, 1, 0)
            copy.start()
            pending.append(copy)
        copy = sib_copy(chan, 0, 16)
        copy.start()
        pending.append(copy)

    def gather_across():
        x_ref = weight(chan, across)
        remote(x_ref, x_ref, x_ss, x_rs, dp=across).wait_recv()
        for turn in range(2):
            copy = ring_copy(turn, 1, 1)
            copy.start()
            pending.append(copy)
        copy = sib_copy(chan, 1, 17)
        copy.start()
        pending.append(copy)

    items = ring_items()

    def gather_step(step, which):
        for turn, at, block in items:
            if at != step or block != which:
                continue
            ring_got(turn, step, block)
            if (turn, step + 1, block) in items:
                copy = ring_copy(turn, step + 1, block)
                copy.start()
                pending.append(copy)
            copy = sib_copy(origin(turn, step), block, item_slot(turn, step, block))
            copy.start()
            pending.append(copy)

    def gather_finish():
        def got(chan_id, block, slot):
            ref = weight(chan_id, theirs[block])
            remote(ref, ref, sib_ss.at[slot], sib_rs.at[slot], dp=sibling).wait_recv()

        got(chan, 0, 16)
        got(chan, 1, 17)
        for turn, step, block in items:
            got(origin(turn, step), block, item_slot(turn, step, block))

    def beside(ref, j):
        start = 2 * j * ROWS
        return jnp.concatenate(
            [ref[start : start + ROWS, :].astype(F32), ref[start + ROWS : start + 2 * ROWS, :].astype(F32)], axis=1
        )

    for j in range(PAIRS):
        packed = beside(tokens_ref, j)
        tok_ref[j * ROWS : (j + 1) * ROWS, :] = packed.astype(BF16)
        for first, values in ((0, packed), (HALF, beside(cotangent_ref, j))):
            low, high = split_pair(values)
            in_send[2 * j, first : first + HALF, :] = low.astype(BF16)
            in_send[2 * j + 1, first : first + HALF, :] = high.astype(BF16)
    in_recv[chan] = in_send[chan]

    lane_id = lax.broadcasted_iota(jnp.int32, (8, LANES), 1)
    row_id = lax.broadcasted_iota(jnp.int32, (8, LANES), 0)
    halves = jnp.where((lane_id >= HALF) == (row_id == 1), 1.0, 0.0) * jnp.where(row_id < 2, 1.0, 0.0)
    halves = halves.astype(BF16)

    def token_sums(parts):
        total = 0.0
        for part in parts:
            total = total + dot_nt(halves, part)
        return [total[h : h + 1, j * ROWS : (j + 1) * ROWS] for h in range(2) for j in range(PAIRS)]

    def split(values):
        high = values.astype(BF16)
        return high, (values - high.astype(F32)).astype(BF16)

    tokens = tok_ref[...]
    wide_tokens = tokens.astype(F32)
    for i, sums in enumerate(token_sums([tokens]) + token_sums(split(wide_tokens * wide_tokens))):
        head_send[i : i + 1, :] = sums

    def row(*refs):
        return jnp.concatenate([ref[...].reshape(1, HALF) for ref in refs], axis=1)

    bup = bup_ref[...].reshape(1, 2 * LANES)
    head_send[16:17, :] = row(ba_ref, bb_ref)
    head_send[17:18, :] = row(gain2_ref, bias2_ref)
    head_send[18:19, :] = row(bdown_ref, bdown_ref)
    head_send[19:20, :] = bup[:, :LANES]
    head_send[20:21, :] = bup[:, LANES:]
    head_send[21:24, :] = jnp.zeros((3, LANES), F32)
    head_recv[chan] = head_send[...]
    head = exchange(0, lambda peer: head_send, head_recv)
    inputs = exchange(1, lambda peer: in_send.at[peer], in_recv)
    head[0]()
    gather_start()
    inputs[0]()

    level, filled = bucket_ref[0], items_ref[0]
    coefl_ref[...] = levels_ref[level]
    item_blocks = jnp.where(level == 0, 2, jnp.where(level == 1, 4, 8))
    block_id = 2 * (row_id % PAIRS) + jnp.where(lane_id >= HALF, 1, 0)
    bound = jnp.where(row_id < PAIRS, filled * item_blocks, item_blocks)
    aux_ref[...] = jnp.where(block_id < bound, 1.0, 0.0)
    for i in range(8):
        turned = raw_modes_ref[i].T
        modes_ref[i] = jnp.concatenate([turned, turned], axis=1)
    log_dt = row(log_dt_ref, log_dt_ref)
    sigma, step_size = 2.0 * jnp.exp(-log_dt), jnp.exp(log_dt)

    def after_quarter(quarter):
        if quarter == 0:
            gather_across()
        elif quarter == 1:
            gather_step(1, 0)
        elif quarter == 3:
            gather_step(1, 1)

    cauchy_forward(modes_ref, sigma, mcoef_ref, wave_ref, sums_ref, rhs_ref, after_quarter)
    freq_ref[:, 0:256] = split_product(mat_ref, 1, rhs_ref, 0, 256)
    even = split_product(mat_ref, 2, rhs_ref, LANES, LANES)
    freq_ref[:, LANES:256] = jnp.where(low_lanes(256), freq_ref[:, LANES:256], even)
    sign = 1.0 - 2.0 * (lax.broadcasted_iota(jnp.int32, (CHUNK, LANES), 0) % 2).astype(F32)
    nyquist = step_size * column_sum(mcoef_ref[0]) * (1.0 / TOK_DEV)

    def store_taps(j, rows, values):
        taps_ref[j, rows, :] = (values + sign * nyquist) * aux_ref[4 + j : 5 + j, :]

    gather_pairs(freq_ref, coefc_ref, 160, tw_ref, 10, 2, store_taps)
    gather_step(2, 0)
    spread_pairs(lambda j, rows: taps_ref[j, rows, :], coefc_ref, 0, tw_ref, 0, 5, rhs_ref)
    transform_into(ans_ref, mat_ref, 0, rhs_ref)

    head[1]()
    sums = head_recv[0, 0:16, :]
    for c in range(1, N_CHAN):
        sums = sums + head_recv[c, 0:16, :]
    mean = sums[0:8] * (1.0 / MODEL_WIDTH)
    rstd = lax.rsqrt(sums[8:16] * (1.0 / MODEL_WIDTH) - mean * mean + EPSILON)

    def columns(rows):
        tall = rows.T
        return [jnp.where(low_lanes(ROWS), tall[:, j : j + 1], tall[:, 4 + j : 5 + j]) for j in range(PAIRS)]

    gain1, bias1, skip = row(gain1_ref, gain1_ref), row(bias1_ref, bias1_ref), row(skip_ref, skip_ref)
    mean_cols, rstd_cols = columns(mean), columns(rstd)
    for j in range(PAIRS):
        hat = (tok_ref[j * ROWS : (j + 1) * ROWS, :].astype(F32) - mean_cols[j]) * rstd_cols[j]
        hat_ref[j] = hat
        norm_ref[j] = hat * gain1 + bias1

    spread_pairs(lambda j, rows: norm_ref[j, rows, :], coefl_ref, 0, tw_ref, 0, 5, rhs_ref)
    transform_into(sig_ref, mat_ref, 0, rhs_ref)
    gather_step(2, 1)
    multiply_spectra(sig_ref, ans_ref, rhs_ref, False)
    transform_into(freq_ref, mat_ref, 1, rhs_ref)

    def store_conv(j, rows, values):
        conv_ref[j, rows, :] = values

    gather_pairs(freq_ref, coefl_ref, 80, tw_ref, 0, 5, store_conv)
    gather_step(3, 0)
    for j in range(PAIRS):
        mixed = conv_ref[j] * aux_ref[j : j + 1, :] + skip * norm_ref[j]
        cumulative, density = normal_parts(mixed)
        slope_ref[j] = cumulative + mixed * density
        low, high = split_pair(mixed * cumulative)
        acts_send[2 * j] = low.astype(BF16)
        acts_send[2 * j + 1] = high.astype(BF16)
    acts_recv[chan] = acts_send[chan]
    acts = exchange(2, lambda peer: acts_send.at[peer], acts_recv)
    acts[0]()
    gather_step(3, 1)
    gather_step(4, 0)
    gather_step(4, 1)
    inputs[1]()
    acts[1]()

    def joined(ref, pair, first):
        return join_pair(
            ref[2 * pair, first : first + HALF, :].astype(F32), ref[2 * pair + 1, first : first + HALF, :].astype(F32)
        )

    def lanes_of(pair):
        return slice(pair * LANES, (pair + 1) * LANES)

    ACTS, NORM2, GRADF = range(3)
    for p in range(PAIRS):
        low_ref[ACTS, :, lanes_of(p)] = joined(acts_recv, p, 0).astype(BF16)
        low_ref[GRADF, :, lanes_of(p)] = joined(in_recv, p, HALF).astype(BF16)
    gather_finish()

    def vector(row, first, second):
        return interleave(head_recv[first, 16 + row : 17 + row, :], head_recv[second, 16 + row : 17 + row, :])

    total = 0.0
    for p in range(PAIRS):
        first = dot_nn(low_ref[ACTS], w_ref[2 * p, :, 0:LANES]) + head_recv[2 * p, 16:17, :]
        second = dot_nn(low_ref[ACTS], w_ref[2 * p + 1, :, 0:LANES]) + head_recv[2 * p + 1, 16:17, :]
        gate, raw = interleave(first, second)
        swish = lax.logistic(raw)
        gate_ref[p], swish_ref[p] = gate, swish
        resid = joined(in_recv, p, 0) + gate * swish
        res_ref[p] = resid
        total = total + resid
    mean2 = jnp.sum(total, axis=1, keepdims=True) * (1.0 / MODEL_WIDTH)
    total = 0.0
    for p in range(PAIRS):
        centred = res_ref[p] - mean2
        total = total + centred * centred
    rstd2 = lax.rsqrt(jnp.sum(total, axis=1, keepdims=True) * (1.0 / MODEL_WIDTH) + EPSILON)
    gain2 = []
    for p in range(PAIRS):
        gain, bias = vector(1, 2 * p, 2 * p + 1)
        gain2.append(gain)
        hat = (res_ref[p] - mean2) * rstd2
        hat2_ref[p] = hat
        low_ref[NORM2, :, lanes_of(p)] = (hat * gain + bias).astype(BF16)
    branch_ref[...] = jnp.zeros_like(branch_ref)
    back2_ref[...] = jnp.zeros_like(back2_ref)

    def hidden_block(c, carry):
        bias = jnp.concatenate([head_recv[c, 19:20, :], head_recv[c, 20:21, :]], axis=1)
        pre = dot_nn(low_ref[NORM2], w_ref[c, :, 128:384]) + bias
        cumulative, density = normal_parts(pre)
        hidden = (pre * cumulative).astype(BF16)
        hid_ref[c] = hidden
        grad = dot_nn(low_ref[GRADF], w_ref[c, :, 384:640]) * (cumulative + pre * density)
        grad = grad.astype(BF16)
        gpre_ref[c] = grad
        sums = column_sum(grad.astype(F32))
        tail_send[c, 3:4, :] = sums[:, 0:LANES]
        tail_send[c, 4:5, :] = sums[:, LANES : 2 * LANES]
        branch_ref[...] += dot_nt(hidden, w_ref[c, :, 384:640])
        back2_ref[...] += dot_nt(grad, w_ref[c, :, 128:384])
        return carry

    lax.fori_loop(0, N_CHAN, hidden_block, 0)

    mean_q, mean_qx = 0.0, 0.0
    for p in range(PAIRS):
        grad, hat = back2_ref[:, lanes_of(p)], hat2_ref[p]
        q = grad * gain2[p]
        mean_q = mean_q + q
        mean_qx = mean_qx + q * hat
        gain_grad, bias_grad = interleave(column_sum(grad * hat), column_sum(grad))
        tail_send[2 * p, 1:2, :] = gain_grad
        first, second = interleave(turn_half(column_sum(grad * hat)), turn_half(column_sum(grad)))
        tail_send[2 * p + 1, 1:2, :] = first
    mean_q = jnp.sum(mean_q, axis=1, keepdims=True) * (1.0 / MODEL_WIDTH)
    mean_qx = jnp.sum(mean_qx, axis=1, keepdims=True) * (1.0 / MODEL_WIDTH)
    for p in range(PAIRS):
        hat = hat2_ref[p]
        extra = rstd2 * (back2_ref[:, lanes_of(p)] * gain2[p] - mean_q - hat * mean_qx)
        grad_f = joined(in_recv, p, HALF)
        grad_resid = grad_f + extra
        gate, swish = gate_ref[p], swish_ref[p]
        grad_a = (grad_resid * swish).astype(BF16).astype(F32)
        grad_b = (grad_resid * gate * swish * (1.0 - swish)).astype(BF16).astype(F32)
        first, second = interleave(grad_a, grad_b)
        gab_ref[2 * p] = first.astype(BF16)
        gab_ref[2 * p + 1] = second.astype(BF16)
        tail_send[2 * p, 0:1, :] = column_sum(first)
        tail_send[2 * p + 1, 0:1, :] = column_sum(second)
        low, high = interleave(column_sum(grad_f), column_sum(grad_f))
        tail_send[2 * p, 2:3, :] = low
        tail_send[2 * p + 1, 2:3, :] = high
        low, high = split_pair(extra)
        late_send[2 * p, HALF:, :] = low.astype(BF16)
        late_send[2 * p + 1, HALF:, :] = high.astype(BF16)
    grad_acts = 0.0
    for c in range(N_CHAN):
        grad_acts = grad_acts + dot_nt(gab_ref[c], w_ref[c, :, 0:LANES])
    for p in range(PAIRS):
        low, high = split_pair(grad_acts[:, lanes_of(p)])
        back_send[2 * p] = low.astype(BF16)
        back_send[2 * p + 1] = high.astype(BF16)
    back_recv[chan] = back_send[chan]
    back = exchange(3, lambda peer: back_send.at[peer], back_recv)
    back[0]()

    def rsib_copy(offset, block):
        slot = (offset + 3) * 2 + block
        src = grad_ref.at[chan_at(offset), pl.ds(row_of(theirs[block]), ROWS), :]
        return remote(src, sib_ref.at[slot], rsib_ss.at[slot], rsib_rs.at[slot], dp=sibling)

    def offset_of(turn, step):
        return TURNS[turn] * (5 - step)

    def rring_copy(turn, step, block):
        slot = item_slot(turn, step, block)
        src = grad_ref.at[chan_at(offset_of(turn, step)), pl.ds(row_of(mine[block]), ROWS), :]
        return remote(src, ring_ref.at[slot], rring_ss.at[slot], rring_rs.at[slot], chan=nexts[turn])

    ritems = [(turn, 5 - step, block) for turn, step, block in items]

    def own_and_sibling(offset, block):
        slot = ((offset if offset != -4 else 4) + 3) * 2 + block
        rsib_copy(offset if offset != -4 else 4, block).wait_recv()
        own = grad_ref[chan_at(offset), pl.ds(row_of(mine[block]), ROWS), :].astype(F32)
        return own + sib_ref[slot].astype(F32)

    def reduce_step(step):
        for turn, at, block in ritems:
            if at != step:
                continue
            total = own_and_sibling(offset_of(turn, step), block)
            if (turn, step - 1, block) in ritems:
                rring_copy(turn, step - 1, block).wait_recv()
                total = total + ring_ref[item_slot(turn, step - 1, block)].astype(F32)
            grad_ref[chan_at(offset_of(turn, step)), pl.ds(row_of(mine[block]), ROWS), :] = total.astype(BF16)
            copy = rring_copy(turn, step, block)
            copy.start()
            pending.append(copy)

    def reduce_last():
        for block in (1, 0):
            total = own_and_sibling(0, block)
            for turn in range(2):
                rring_copy(turn, 4, block).wait_recv()
                total = total + ring_ref[item_slot(turn, 4, block)].astype(F32)
            if block == 1:
                part_ref[0] = total.astype(BF16)
                send(part_ref.at[0], part_ref.at[1], rx_ss, rx_rs, dp=across)
            else:
                gw_ref[...] = total

    def reduce_finish():
        remote(part_ref.at[0], part_ref.at[1], rx_ss, rx_rs, dp=across).wait_recv()
        gw_ref[...] += part_ref[1].astype(F32)

    tall = [low_ref[i].astype(F32).T.astype(BF16) for i in range(3)]
    order = (4, 3, -3, 2, -2, 1, -1, 0)
    for offset in order:
        c = chan_at(offset)
        grad_ref[c, :, 0:128] = dot_nn(tall[ACTS], gab_ref[c]).astype(BF16)
        grad_ref[c, :, 128:384] = dot_nn(tall[NORM2], gpre_ref[c]).astype(BF16)
        grad_ref[c, :, 384:640] = dot_nn(tall[GRADF], hid_ref[c]).astype(BF16)
        for block in range(2):
            copy = rsib_copy(offset, block)
            copy.start()
            pending.append(copy)
        if offset == -3:
            reduce_step(1)
        elif offset == -1:
            reduce_step(2)
    for p in range(PAIRS):
        out = res_ref[p] + branch_ref[:, lanes_of(p)] + interleave(head_recv[2 * p, 18:19, :], head_recv[2 * p + 1, 18:19, :])[0]
        low, high = split_pair(out)
        late_send[2 * p, :HALF, :] = low.astype(BF16)
        late_send[2 * p + 1, :HALF, :] = high.astype(BF16)
    for c in range(N_CHAN):
        tail_send[c, 5:8, :] = jnp.zeros((3, LANES), F32)
    late_recv[chan] = late_send[chan]
    tail_recv[chan] = tail_send[chan]
    late = exchange(4, lambda peer: late_send.at[peer], late_recv)
    tail = exchange(5, lambda peer: tail_send.at[peer], tail_recv)
    late[0]()
    tail[0]()

    back[1]()
    skip_grad = 0.0
    for j in range(PAIRS):
        grad = joined(back_recv, j, 0) * slope_ref[j]
        slope_ref[j] = grad
        conv_ref[j] = grad * aux_ref[j : j + 1, :]
        skip_grad = skip_grad + column_sum(grad * norm_ref[j])
    spread_pairs(lambda j, rows: conv_ref[j, rows, :], coefl_ref, 0, tw_ref, 0, 5, rhs_ref)
    transform_into(freq_ref, mat_ref, 0, rhs_ref)
    multiply_spectra(sig_ref, freq_ref, rhs_ref, True)
    transform_into(sig_ref, mat_ref, 1, rhs_ref)

    def store_kernel_grad(j, rows, values):
        taps_ref[j, rows, :] = values * aux_ref[4 + j : 5 + j, :]

    gather_pairs(sig_ref, coefc_ref, 80, tw_ref, 0, 5, store_kernel_grad)
    multiply_spectra(ans_ref, freq_ref, rhs_ref, True)
    transform_into(freq_ref, mat_ref, 1, rhs_ref)
    gather_pairs(freq_ref, coefl_ref, 80, tw_ref, 0, 5, store_conv)
    gain_grad, bias_grad = 0.0, 0.0
    scaled, crossed = [], []
    for j in range(PAIRS):
        grad = conv_ref[j] + skip * slope_ref[j]
        conv_ref[j] = grad
        gain_grad = gain_grad + column_sum(grad * hat_ref[j])
        bias_grad = bias_grad + column_sum(grad)
    conv = conv_ref[...].reshape(PAIRS * ROWS, LANES) * gain1
    for i, sums in enumerate(
        token_sums(split(conv)) + token_sums(split(conv * hat_ref[...].reshape(PAIRS * ROWS, LANES)))
    ):
        sum_send[i : i + 1, :] = sums
    sum_recv[chan] = sum_send[...]
    sums_back = exchange(6, lambda peer: sum_send, sum_recv)
    sums_back[0]()
    reduce_step(3)

    nyquist_grad = 0.0
    for j in range(PAIRS):
        whole_sign = 1.0 - 2.0 * (lax.broadcasted_iota(jnp.int32, (ROWS, LANES), 0) % 2).astype(F32)
        nyquist_grad = nyquist_grad + column_sum(taps_ref[j] * whole_sign)
    nyquist_grad = fold(nyquist_grad) * (1.0 / TOK_DEV)
    spread_pairs(lambda j, rows: taps_ref[j, rows, :], coefc_ref, 192, tw_ref, 10, 2, rhs_ref)
    freq_ref[:, 0:256] = split_product(mat_ref, 0, rhs_ref, 0, 256)
    even = split_product(mat_ref, 3, rhs_ref, LANES, LANES)
    freq_ref[:, LANES:256] = jnp.where(low_lanes(256), freq_ref[:, LANES:256], even)

    def after_part(part):
        if part == 1:
            reduce_step(4)
        elif part == 3:
            reduce_last()

    mode_grads, dt_grad = cauchy_backward(
        modes_ref, sigma, nyquist_grad, step_size, mcoef_ref, wave_ref, sums_ref, freq_ref, pgrad_ref, mback_ref,
        after_part,
    )
    mask = low_lanes(32)
    for i in range(4):
        dp_send[i * 32 : (i + 1) * 32, :] = jnp.where(mask, mode_grads[i], mode_grads[i + 4])
    first = low_lanes(1)
    dp_send[128:129, :] = jnp.where(first, dt_grad, fold(skip_grad))
    dp_send[129:130, :] = jnp.where(first, fold(gain_grad), fold(bias_grad))
    dp_send[130:136, :] = jnp.zeros((6, LANES), F32)
    tail[1]()
    tail_sum = tail_recv[0]
    for c in range(1, N_CHAN):
        tail_sum = tail_sum + tail_recv[c]
    dp_send[136:144, :] = tail_sum
    dp_recv[0] = dp_send[...]

    def dp_copy(r):
        return remote(dp_send, dp_recv.at[r], dp_ss.at[r - 1], dp_rs.at[r - 1], dp=(dp + r) % 4)

    for r in range(1, 4):
        dp_copy(r).start()

    sums_back[1]()
    sums = sum_recv[0]
    for c in range(1, N_CHAN):
        sums = sums + sum_recv[c]
    sums = sums * (1.0 / MODEL_WIDTH)
    rstd_cols, q_cols, qx_cols = columns(rstd), columns(sums[0:8]), columns(sums[8:16])
    late[1]()
    for j in range(PAIRS):
        rows = slice(j * ROWS, (j + 1) * ROWS)
        out_ref[rows, :] = joined(late_recv, j, 0).astype(BF16)
        dtok_ref[rows, :] = joined(late_recv, j, HALF) + rstd_cols[j] * (
            conv_ref[j] * gain1 - q_cols[j] - hat_ref[j] * qx_cols[j]
        )
    for r in range(1, 4):
        dp_copy(r).wait_recv()
    total = dp_recv[0] + dp_recv[1] + dp_recv[2] + dp_recv[3]
    gm_ref[...] = total[0:128]
    gv_ref[...] = total[128:144]
    reduce_finish()
    for copy in pending:
        copy.wait_send()
    for group in (head, inputs, acts, back, late, tail, sums_back):
        group[2]()
    for r in range(1, 4):
        dp_copy(r).wait_send()


def unpack_kernel(
    out_ref, dtok_ref, gw_ref, gm_ref, gv_ref, cotangent_ref,
    output_ref, tokens_ref, gain1_ref, bias1_ref, modes_ref, dt_ref, skip_ref, wa_ref, ba_ref, wb_ref, bb_ref,
    gain2_ref, bias2_ref, up_ref, bup_ref, down_ref, bdown_ref,
):
    for j in range(PAIRS):
        out = out_ref[j * ROWS : (j + 1) * ROWS, :].astype(F32)
        grad = dtok_ref[j * ROWS : (j + 1) * ROWS, :]
        for h in range(2):
            rows, lanes = slice((2 * j + h) * ROWS, (2 * j + h + 1) * ROWS), slice(h * HALF, (h + 1) * HALF)
            output_ref[rows, :] = out[:, lanes].astype(BF16)
            tokens_ref[rows, :] = cotangent_ref[rows, :] + grad[:, lanes]
    for i in range(8):
        modes_ref[i] = gm_ref[i % 4 * 32 : i % 4 * 32 + 32, i // 4 * HALF : (i // 4 + 1) * HALF].T
    wa_ref[...] = gw_ref[:, :HALF]
    wb_ref[...] = gw_ref[:, HALF:LANES]
    up_ref[...] = gw_ref[:, 128:384]
    down_ref[...] = gw_ref[:, 384:640].T
    for at, low, high in (
        (0, dt_ref, skip_ref), (1, gain1_ref, bias1_ref), (8, ba_ref, bb_ref), (9, gain2_ref, bias2_ref),
    ):
        low[...] = gv_ref[at, :HALF]
        high[...] = gv_ref[at, HALF:]
    bdown_ref[...] = gv_ref[10, :HALF]
    bup_ref[:LANES] = gv_ref[11, :]
    bup_ref[LANES:] = gv_ref[12, :]


def block_program():
    mats, twiddle, levels, constant, wave = mixer_tables()

    def run(tokens, cotangent, bucket, items, gain1, bias1, modes, log_dt, skip, w_a, b_a, w_b, b_b, gain2, bias2, w_up, b_up, w_down, b_down):
        vmem = pl.BlockSpec(memory_space=pltpu.VMEM)
        smem = pl.BlockSpec(memory_space=pltpu.SMEM)
        dma = pltpu.SemaphoreType.DMA

        def buf(*shape):
            return pltpu.VMEM(shape, F32)

        def low(*shape):
            return pltpu.VMEM(shape, BF16)

        def full(*shape):
            return jax.ShapeDtypeStruct(shape, F32)

        big, wide = (PAIRS, ROWS, LANES), (256, WIDE)
        packed = pl.pallas_call(
            block_kernel,
            out_shape=(
                jax.ShapeDtypeStruct((512, LANES), BF16), full(512, LANES), full(ROWS, WIDE), full(ROWS, LANES),
                full(16, LANES),
            ),
            in_specs=[smem] * 2 + [vmem] * 22,
            out_specs=(vmem,) * 5,
            scratch_shapes=[
                low(512, LANES), buf(8, LANES), buf(160, LANES), buf(8, 32, LANES),
                low(N_CHAN, 512, WIDE), low(N_CHAN, 512, WIDE), low(16, ROWS, WIDE), low(16, ROWS, WIDE), low(2, ROWS, WIDE),
                low(N_CHAN, ROWS, LANES), low(N_CHAN, ROWS, LANES), buf(24, LANES), buf(N_CHAN, 24, LANES),
                low(N_CHAN, HALF, LANES), low(N_CHAN, HALF, LANES), low(N_CHAN, HALF, LANES), low(N_CHAN, HALF, LANES),
                low(N_CHAN, ROWS, LANES), low(N_CHAN, ROWS, LANES),
                buf(16, LANES), buf(N_CHAN, 16, LANES), buf(N_CHAN, 8, LANES), buf(N_CHAN, 8, LANES),
                buf(144, LANES), buf(4, 144, LANES),
                buf(*big), buf(*big), buf(*big), buf(*big), low(2, *wide), buf(*wide), buf(*wide), buf(*wide), buf(*big),
                buf(10, 32, LANES), buf(2, 16, ROWS, LANES), buf(2, 16, ROWS, LANES), buf(10, 32, LANES),
                buf(*big), buf(*big), buf(*big), buf(*big), low(3, ROWS, 512), buf(ROWS, 512), buf(ROWS, 512),
                low(N_CHAN, ROWS, LANES), low(N_CHAN, ROWS, 256), low(N_CHAN, ROWS, 256),
                dma((16,)), dma((16,)), dma((18,)), dma((18,)), dma, dma, dma((16,)), dma((16,)), dma((16,)), dma((16,)),
                dma, dma, dma((7, 7)), dma((7, 7)), dma((3,)), dma((3,)),
            ],
            compiler_params=pltpu.CompilerParams(
                collective_id=0, has_side_effects=True, vmem_limit_bytes=60 * 1024 * 1024
            ),
            name="block",
        )(
            bucket, items, tokens, cotangent, gain1, bias1, modes, log_dt, skip, w_a, b_a, w_b, b_b, gain2, bias2,
            w_up, b_up, w_down, b_down, levels, constant, mats, twiddle, wave,
        )
        small = full(HALF)
        return pl.pallas_call(
            unpack_kernel,
            out_shape=(
                jax.ShapeDtypeStruct((TOK_DEV, HALF), BF16), full(TOK_DEV, HALF), small, small, full(8, HALF, 32),
                small, small, full(ROWS, HALF), small, full(ROWS, HALF), small, small, small, full(ROWS, 256),
                full(256), full(256, ROWS), small,
            ),
            in_specs=[vmem] * 6,
            out_specs=(vmem,) * 17,
            name="unpack",
        )(*packed, cotangent)

    return run


def solution(mesh):
    small = mesh.shape["chan"] == N_CHAN and mesh.shape["dp"] == 4
    return jax.shard_map(
        block_program() if small else shards,
        mesh=mesh,
        in_specs=(
            P("dp", "chan"),
            P("dp", "chan"),
            P("dp"),
            P("dp"),
            P("chan"),
            P("chan"),
            P(None, "chan", None),
            P("chan"),
            P("chan"),
            P("dp", "chan"),
            P("chan"),
            P("dp", "chan"),
            P("chan"),
            P("chan"),
            P("chan"),
            P("dp", "chan"),
            P("chan"),
            P("chan", "dp"),
            P("chan"),
        ),
        out_specs=(
            P("dp", "chan"),
            P("dp", "chan"),
            P("chan"),
            P("chan"),
            P(None, "chan", None),
            P("chan"),
            P("chan"),
            P("dp", "chan"),
            P("chan"),
            P("dp", "chan"),
            P("chan"),
            P("chan"),
            P("chan"),
            P("dp", "chan"),
            P("chan"),
            P("chan", "dp"),
            P("chan"),
        ),
        check_vma=False,
    )
```

```python
import math

import jax
import jax.numpy as jnp
import ml_dtypes
import numpy as np
from jax import lax
from jax.experimental import pallas as pl
from jax.experimental.pallas import tpu as pltpu
from jax.sharding import PartitionSpec as P

MODEL_WIDTH = 512
TOK_DEV = 1024


HIGHEST = lax.Precision.HIGHEST
EPSILON = 1e-05


def product(left, right):
    return jnp.dot(left, right, preferred_element_type=jnp.float32)


def product_nt(left, right):
    return lax.dot_general(
        left, right, (((1,), (1,)), ((), ())), preferred_element_type=jnp.float32
    )


def product_tn(left, right):
    return lax.dot_general(
        left, right, (((0,), (0,)), ((), ())), preferred_element_type=jnp.float32
    )


def gelu_slope(values):
    return (
        0.5 * (1.0 + lax.erf(values * 0.7071067811865476))
        + values * jnp.exp(-0.5 * values * values) * 0.3989422804014327
    )


def half_angles(length):
    angle = np.arange(length // 2 + 1, dtype=np.float64) * (math.pi / length)
    cosine, sine = np.cos(angle), np.sin(angle)
    cosine[-1] = 0.0
    return cosine.astype(np.float32), sine.astype(np.float32)


def inverse_tables(length):
    freq = np.arange(length // 2 + 1)
    turn = (freq[:, None] * np.arange(length)[None, :]) % length * (2.0 * math.pi / length)
    weight = np.where((freq == 0) | (freq == length // 2), 1.0, 2.0)[:, None] / length
    return (weight * np.cos(turn)).astype(np.float32), (weight * np.sin(turn)).astype(np.float32)


def high_einsum(form, left, right):
    return jnp.einsum(form, left, right, precision=HIGHEST)


def ssm_kernel(modes, log_dt):
    cos_h, sin_h = half_angles(TOK_DEV)
    index = jnp.arange(modes.shape[2], dtype=jnp.int32).astype(jnp.float32)
    lam_re = -0.5 * jnp.exp(modes[0])
    lam_im = math.pi * (index + modes[1])
    rank_re, rank_im, in_re, in_im, out_re, out_im = (modes[i] for i in range(2, 8))
    sigma = (2.0 * jnp.exp(-log_dt))[:, None]

    def points(values):
        return values.T[:, None, :]

    den_re = points(lam_re * lam_re + lam_im * lam_im) * (cos_h * cos_h)[:, None] - (
        sigma * sigma
    ).T * (sin_h * sin_h)[:, None]
    den_im = points(-2.0 * sigma * lam_re) * (sin_h * cos_h)[:, None]
    den_sq = den_re * den_re + den_im * den_im
    inv_re = den_re / den_sq
    inv_im = -den_im / den_sq
    sums = []
    for real, imag in (
        (out_re * in_re + out_im * in_im, out_re * in_im - out_im * in_re),
        (out_re * rank_re + out_im * rank_im, out_re * rank_im - out_im * rank_re),
        (rank_re * in_re + rank_im * in_im, rank_re * in_im - rank_im * in_re),
        (rank_re * rank_re + rank_im * rank_im, jnp.zeros_like(rank_re)),
    ):
        turned = points(real * lam_re + imag * lam_im)
        real = points(real)
        p_re, p_im = jnp.sum(real * inv_re, axis=0), jnp.sum(real * inv_im, axis=0)
        q_re, q_im = jnp.sum(turned * inv_re, axis=0), jnp.sum(turned * inv_im, axis=0)
        sine = sin_h[:, None] * sigma.T
        sums.append((-sine * p_im - cos_h[:, None] * q_re, sine * p_re - cos_h[:, None] * q_im))
    (cross_re, cross_im), (left_re, left_im), (right_re, right_im), (self_re, self_im) = sums
    twice = 2.0 * cos_h[:, None]
    loop_re, loop_im = 1.0 + twice * self_re, twice * self_im
    back_re, back_im = twice * right_re, twice * right_im
    loop_sq = loop_re * loop_re + loop_im * loop_im
    ratio_re = (back_re * loop_re + back_im * loop_im) / loop_sq
    ratio_im = (back_im * loop_re - back_re * loop_im) / loop_sq
    part_re = cross_re - (left_re * ratio_re - left_im * ratio_im)
    part_im = cross_im - (left_re * ratio_im + left_im * ratio_re)
    spec_re = 2.0 * (cos_h[:, None] * part_re - sin_h[:, None] * part_im)
    spec_im = 2.0 * (cos_h[:, None] * part_im + sin_h[:, None] * part_re)
    cos_tab, sin_tab = inverse_tables(TOK_DEV)
    return high_einsum("kl,kc->lc", cos_tab, spec_re) - high_einsum("kl,kc->lc", sin_tab, spec_im)


BLOCK = 128
BLOCKS = TOK_DEV // BLOCK
FIRST = 2 * BLOCKS
KEPT = FIRST // 2 + 1


def transform_tables():
    length = 2 * TOK_DEV
    turn = np.arange(KEPT)[:, None] * np.arange(BLOCK)[None, :] * (2.0 * math.pi / length)
    small = np.arange(BLOCK)[:, None] * np.arange(BLOCK)[None, :] % BLOCK * (2.0 * math.pi / BLOCK)
    spots = np.stack([np.arange(BLOCKS) + np.arange(BLOCKS) // (2 << b) * (2 << b) for b in range(3)])
    angle = spots[:, None, :] * np.arange(KEPT)[None, :, None] % FIRST * (2.0 * math.pi / FIRST)
    parts = (np.cos(turn), np.sin(turn), np.cos(small), np.sin(small), np.cos(angle), np.sin(angle))
    return [part.astype(np.float32) for part in parts]


def forward_transform(blocks, cos_a, sin_a):
    cos_t, sin_t, cos_s, sin_s, _, _ = transform_tables()
    step_re = high_einsum("ka,abc->kbc", cos_a, blocks)
    step_im = -high_einsum("ka,abc->kbc", sin_a, blocks)
    turned_re = step_re * cos_t[..., None] + step_im * sin_t[..., None]
    turned_im = step_im * cos_t[..., None] - step_re * sin_t[..., None]
    both = jnp.concatenate([turned_re, turned_im], axis=1)
    matrix = np.block([[cos_s, sin_s], [-sin_s, cos_s]])
    return high_einsum("pb,kbc->kpc", matrix, both)


def inverse_transform(spectrum, cos_a, sin_a):
    cos_t, sin_t, cos_s, sin_s, _, _ = transform_tables()
    matrix = np.block([[cos_s, -sin_s], [sin_s, cos_s]])
    both = high_einsum("bp,kpc->kbc", matrix, spectrum)
    step_re, step_im = both[:, :BLOCK], both[:, BLOCK:]
    turned_re = step_re * cos_t[..., None] - step_im * sin_t[..., None]
    turned_im = step_im * cos_t[..., None] + step_re * sin_t[..., None]
    weight = np.where(np.arange(KEPT) % (KEPT - 1) == 0, 1.0, 2.0).astype(np.float32) / (2 * TOK_DEV)
    return high_einsum("ka,kbc->abc", cos_a * weight[:, None], turned_re) - high_einsum(
        "ka,kbc->abc", sin_a * weight[:, None], turned_im
    )


def multiply(left, right):
    left_re, left_im = left[:, :BLOCK], left[:, BLOCK:]
    right_re, right_im = right[:, :BLOCK], right[:, BLOCK:]
    return jnp.concatenate(
        [left_re * right_re - left_im * right_im, left_re * right_im + left_im * right_re], axis=1
    )


def mixer(normed, kernel_taps, skip_gain, bucket, filled):
    _, _, _, _, cos_a, sin_a = transform_tables()
    cos_x, sin_x = jnp.asarray(cos_a)[bucket], jnp.asarray(sin_a)[bucket]
    item_blocks = 2 << bucket
    block_id = jnp.arange(BLOCKS, dtype=jnp.int32)[:, None, None]
    taps = jnp.where(block_id < item_blocks, kernel_taps.reshape(BLOCKS, BLOCK, -1), 0.0)
    signal = forward_transform(normed.reshape(BLOCKS, BLOCK, -1), cos_x, sin_x)
    answer = forward_transform(taps, cos_a[2], sin_a[2])
    result = inverse_transform(multiply(signal, answer), cos_x, sin_x)
    result = jnp.where(block_id < filled * item_blocks, result, 0.0)
    return result.reshape(normed.shape) + skip_gain * normed


def shards(
    tokens,
    cotangent,
    group_bucket,
    group_items,
    first_norm_gain,
    first_norm_bias,
    modes,
    log_dt,
    d_skip,
    w_a,
    b_a,
    w_b,
    b_b,
    second_norm_gain,
    second_norm_bias,
    w_up,
    b_up,
    w_down,
    b_down,
):
    input_tokens = tokens.astype(jnp.float32)
    sums_in = lax.psum(
        (jnp.sum(input_tokens, axis=1), jnp.sum(input_tokens * input_tokens, axis=1)), "chan"
    )
    input_average = sums_in[0][:, None] / MODEL_WIDTH
    input_inverse_deviation = lax.rsqrt(
        sums_in[1][:, None] / MODEL_WIDTH - input_average * input_average + EPSILON
    )
    input_standardized = (input_tokens - input_average) * input_inverse_deviation
    input_normalized = input_standardized * first_norm_gain + first_norm_bias
    level = group_bucket[0]
    filled = group_items[0]
    kernel_taps, kernel_back = jax.vjp(ssm_kernel, modes, log_dt)

    def local_mix(values, taps_now, skip_gain):
        return mixer(values, taps_now, skip_gain, level, filled)

    mixed, mix_back = jax.vjp(local_mix, input_normalized, kernel_taps, d_skip)
    acts_low = jax.nn.gelu(mixed, approximate=False).astype(jnp.bfloat16)
    wa_full, wb_full, up_full, down_full = (
        lax.all_gather(w_a.astype(jnp.bfloat16), "dp", axis=0, tiled=True),
        lax.all_gather(w_b.astype(jnp.bfloat16), "dp", axis=0, tiled=True),
        lax.all_gather(w_up.astype(jnp.bfloat16), "dp", axis=0, tiled=True),
        lax.all_gather(w_down.astype(jnp.bfloat16), "dp", axis=1, tiled=True),
    )
    acts_full = lax.all_gather(acts_low, "chan", axis=1, tiled=True)
    gate_a = product(acts_full, wa_full) + b_a
    gate_b = product(acts_full, wb_full) + b_b
    gate_sig = jax.nn.sigmoid(gate_b)
    residual_stream = input_tokens + gate_a * gate_sig
    sums_mid = lax.psum(
        (jnp.sum(residual_stream, axis=1), jnp.sum(residual_stream * residual_stream, axis=1)),
        "chan",
    )
    middle_average = sums_mid[0][:, None] / MODEL_WIDTH
    middle_inverse_deviation = lax.rsqrt(
        sums_mid[1][:, None] / MODEL_WIDTH - middle_average * middle_average + EPSILON
    )
    middle_standardized = (residual_stream - middle_average) * middle_inverse_deviation
    middle_reduced = (middle_standardized * second_norm_gain + second_norm_bias).astype(
        jnp.bfloat16
    )
    mid_full = lax.all_gather(middle_reduced, "chan", axis=1, tiled=True)
    pre_act = product(mid_full, up_full) + b_up
    hidden_low = jax.nn.gelu(pre_act, approximate=False).astype(jnp.bfloat16)
    branch = (
        lax.psum_scatter(product(hidden_low, down_full), "chan", scatter_dimension=1, tiled=True)
        + b_down
    )
    output = (residual_stream + branch).astype(jnp.bfloat16)
    grad_f = cotangent.astype(jnp.bfloat16)
    grad_b_down = jnp.sum(grad_f.astype(jnp.float32), axis=0)
    grad_f_full = lax.all_gather(grad_f, "chan", axis=1, tiled=True)
    grad_w_down = product_tn(hidden_low, grad_f_full)
    grad_pre = (product_nt(grad_f_full, down_full) * gelu_slope(pre_act)).astype(jnp.bfloat16)
    grad_b_up = jnp.sum(grad_pre.astype(jnp.float32), axis=0)
    grad_w_up = product_tn(mid_full, grad_pre)
    middle_gradient = lax.psum_scatter(
        product_nt(grad_pre, up_full), "chan", scatter_dimension=1, tiled=True
    )
    second_norm_gain_gradient = jnp.sum(middle_gradient * middle_standardized, axis=0)
    grad_ln2_bias = jnp.sum(middle_gradient, axis=0)
    middle_rescaled = middle_gradient * second_norm_gain
    middle_backward = lax.psum(
        (jnp.sum(middle_rescaled, axis=1), jnp.sum(middle_rescaled * middle_standardized, axis=1)),
        "chan",
    )
    grad_resid = cotangent + middle_inverse_deviation * (
        middle_rescaled
        - middle_backward[0][:, None] / MODEL_WIDTH
        - middle_standardized * middle_backward[1][:, None] / MODEL_WIDTH
    )
    grad_a = (grad_resid * gate_sig).astype(jnp.bfloat16)
    grad_b = (grad_resid * gate_a * gate_sig * (1.0 - gate_sig)).astype(jnp.bfloat16)
    grad_b_a = jnp.sum(grad_a.astype(jnp.float32), axis=0)
    grad_b_b = jnp.sum(grad_b.astype(jnp.float32), axis=0)
    grad_w_a = product_tn(acts_full, grad_a)
    grad_w_b = product_tn(acts_full, grad_b)
    grad_acts = lax.psum_scatter(
        product_nt(grad_a, wa_full) + product_nt(grad_b, wb_full),
        "chan",
        scatter_dimension=1,
        tiled=True,
    )
    grad_mixed = grad_acts * gelu_slope(mixed)
    normalized_gradient, grad_kernel, grad_skip = mix_back(grad_mixed)
    grad_modes, grad_log_dt = kernel_back(grad_kernel)
    first_norm_gain_gradient = jnp.sum(normalized_gradient * input_standardized, axis=0)
    grad_ln1_bias = jnp.sum(normalized_gradient, axis=0)
    input_rescaled = normalized_gradient * first_norm_gain
    input_backward = lax.psum(
        (jnp.sum(input_rescaled, axis=1), jnp.sum(input_rescaled * input_standardized, axis=1)),
        "chan",
    )
    grad_tokens = grad_resid + input_inverse_deviation * (
        input_rescaled
        - input_backward[0][:, None] / MODEL_WIDTH
        - input_standardized * input_backward[1][:, None] / MODEL_WIDTH
    )
    grad_w_a, grad_w_b, grad_w_up, grad_w_down = (
        lax.psum_scatter(grad_w_a, "dp", scatter_dimension=0, tiled=True),
        lax.psum_scatter(grad_w_b, "dp", scatter_dimension=0, tiled=True),
        lax.psum_scatter(grad_w_up, "dp", scatter_dimension=0, tiled=True),
        lax.psum_scatter(grad_w_down, "dp", scatter_dimension=1, tiled=True),
    )
    (
        first_norm_gain_gradient,
        grad_ln1_bias,
        grad_modes,
        grad_log_dt,
        grad_skip,
        grad_b_a,
        grad_b_b,
        second_norm_gain_gradient,
        grad_ln2_bias,
        grad_b_up,
        grad_b_down,
    ) = lax.psum(
        (
            first_norm_gain_gradient,
            grad_ln1_bias,
            grad_modes,
            grad_log_dt,
            grad_skip,
            grad_b_a,
            grad_b_b,
            second_norm_gain_gradient,
            grad_ln2_bias,
            grad_b_up,
            grad_b_down,
        ),
        "dp",
    )
    return (
        output,
        grad_tokens,
        first_norm_gain_gradient,
        grad_ln1_bias,
        grad_modes,
        grad_log_dt,
        grad_skip,
        grad_w_a,
        grad_b_a,
        grad_w_b,
        grad_b_b,
        second_norm_gain_gradient,
        grad_ln2_bias,
        grad_w_up,
        grad_b_up,
        grad_w_down,
        grad_b_down,
    )


LANES = 128
HALF = 64
PAIRS = 4
ROWS = 128
N_CHAN = 8
WIDE = 640
MESH = pl.DeviceIdType.MESH
F32 = jnp.float32
BF16 = jnp.bfloat16


def split_two(matrix):
    high = matrix.astype(ml_dtypes.bfloat16)
    low = (matrix - high.astype(np.float64)).astype(ml_dtypes.bfloat16)
    return np.concatenate([high, low], axis=1)


def lane_rows(values_low, values_high):
    return np.repeat(np.stack([values_low, values_high], -1), HALF, axis=-1)


def mixer_tables():
    line = np.arange(ROWS)
    small = np.outer(line, line) % ROWS * (2.0 * math.pi / ROWS)
    cos_s, sin_s = np.cos(small), np.sin(small)
    forward = np.block([[cos_s, sin_s], [-sin_s, cos_s]])
    real = np.zeros((2 * ROWS, 2 * ROWS))
    for row in range(HALF):
        weight = 1.0 if row == 0 else 2.0
        turn = 2.0 * math.pi / ROWS * row * line
        real[:ROWS, row] = weight * np.cos(turn)
        real[:ROWS, ROWS + row] = -weight * np.sin(turn)
        turn = 2.0 * math.pi / TOK_DEV * (4 + 8 * row) * line
        real[ROWS:, HALF + row] = 2.0 * np.cos(turn)
        real[ROWS:, ROWS + HALF + row] = -2.0 * np.sin(turn)
    mats = np.stack([split_two(m) for m in (forward, forward.T, real, real.T)])

    twiddle = []
    for pair in range(5):
        turn = np.stack([line * k * (math.pi / TOK_DEV) for k in (2 * pair, 2 * pair + 1)])
        twiddle += [lane_rows(np.cos(turn[0]), np.cos(turn[1])), lane_rows(np.sin(turn[0]), np.sin(turn[1]))]
    for first, second in ((1, 2), (3, 0)):
        turn = np.stack([line * k * (2.0 * math.pi / TOK_DEV) for k in (first, second)])
        twiddle += [lane_rows(np.cos(turn[0]), np.cos(turn[1])), lane_rows(np.sin(turn[0]), np.sin(turn[1]))]

    def forward_rows(coef, pairs):
        out = []
        for low, high in pairs:
            for part in range(2):
                for j in range(PAIRS):
                    out.append(lane_rows(coef(2 * j, low, part), coef(2 * j + 1, high, part)))
                for j in range(PAIRS):
                    out.append(lane_rows(coef(2 * j, high, part), coef(2 * j + 1, low, part)))
        return np.stack(out)

    def inverse_rows(coef, pairs):
        out = []
        for low, high in pairs:
            for part in range(2):
                for j in range(PAIRS):
                    out.append(lane_rows(coef(2 * j, low, part), coef(2 * j + 1, high, part)))
                for j in range(PAIRS):
                    out.append(lane_rows(coef(2 * j + 1, low, part), coef(2 * j, high, part)))
        return np.stack(out)

    levels = []
    pairs = [(2 * p, 2 * p + 1) for p in range(5)]
    for level in range(3):
        item = 2 << level

        def angle(block, k):
            return 2.0 * math.pi / 16 * ((block + block // item * item) * k % 16)

        def fwd(block, k, part):
            if k > 8:
                return np.zeros(())
            return np.cos(angle(block, k)) if part == 0 else -np.sin(angle(block, k))

        def inv(block, k, part):
            weight = (1.0 if k in (0, 8) else 2.0) / (2 * TOK_DEV)
            return weight * fwd(block, k, part)

        levels.append(np.concatenate([forward_rows(fwd, pairs), inverse_rows(inv, pairs)]))

    def taps(block, k, part):
        if k == 0:
            return np.asarray((1.0 if part == 0 else (-1.0) ** block) / TOK_DEV)
        turn = 2.0 * math.pi / 8 * (block * k % 8)
        return np.asarray((np.cos(turn) if part == 0 else -np.sin(turn)) * 2.0 / TOK_DEV)

    tap_pairs = [(1, 2), (3, 0)]
    taps_back = forward_rows(taps, tap_pairs)
    taps_rows = inverse_rows(taps, tap_pairs)
    freq_even = np.where(line < HALF, 8 * line, 4 + 8 * (line - HALF))
    half_angle = np.stack(
        [lane_rows(1 + 8 * line, 2 + 8 * line), lane_rows(3 + 8 * line, freq_even)]
    ) * (math.pi / TOK_DEV)
    wave = np.stack([np.cos(half_angle), np.sin(half_angle)])
    return (
        mats,
        np.stack(twiddle).astype(np.float32),
        np.stack(levels).astype(np.float32),
        np.concatenate([levels[2], taps_rows, taps_back]).astype(np.float32),
        wave.astype(np.float32),
    )


def low_lanes(rows):
    return lax.broadcasted_iota(jnp.int32, (rows, LANES), 1) < HALF


def turn_half(values):
    return pltpu.roll(values, HALF, 1)


def split_pair(values):
    upper, lower = values[:HALF], values[HALF:]
    mask = low_lanes(HALF)
    return jnp.where(mask, upper, turn_half(lower)), jnp.where(mask, turn_half(upper), lower)


def join_pair(first, second):
    mask = low_lanes(HALF)
    return jnp.concatenate(
        [jnp.where(mask, first, turn_half(second)), jnp.where(mask, turn_half(first), second)], axis=0
    )


def interleave(first, second):
    mask = low_lanes(first.shape[0])
    return jnp.where(mask, first, turn_half(second)), jnp.where(mask, turn_half(first), second)


def fold(values):
    return values + turn_half(values)


def normal_parts(values):
    cumulative = 0.5 * (1.0 + lax.erf(values * 0.7071067811865476))
    density = jnp.exp(-0.5 * values * values) * 0.3989422804014327
    return cumulative, density


def column_sum(values):
    return jnp.sum(values, axis=0, keepdims=True)


def dot_nt(left, right):
    return lax.dot_general(left, right, (((1,), (1,)), ((), ())), preferred_element_type=F32)


def dot_nn(left, right):
    return jnp.dot(left, right, preferred_element_type=F32)


def store_split(ref, row, lane, values):
    high = values.astype(BF16)
    place = (pl.ds(row, values.shape[0]), pl.ds(lane, values.shape[1]))
    ref[(0,) + place] = high
    ref[(1,) + place] = (values - high.astype(F32)).astype(BF16)


def split_product(mat_ref, which, rhs_ref, lane, width):
    high = mat_ref[which, :, 0:256]
    low = mat_ref[which, :, 256:512]
    rhs_high = rhs_ref[0, :, lane : lane + width]
    return dot_nn(high, rhs_high) + dot_nn(high, rhs_ref[1, :, lane : lane + width]) + dot_nn(low, rhs_high)


CHUNK = 32


def over_chunks(body, size=CHUNK, first=0, rows=ROWS):
    def step(index, carry):
        body(pl.multiple_of(first + index * size, size))
        return carry

    lax.fori_loop(0, rows // size, step, 0)


def spread_pairs(src, coef_ref, base, twiddle_ref, twiddle_base, pairs, rhs_ref):
    def body(row):
        rows = pl.ds(row, CHUNK)
        blocks = [src(j, rows) for j in range(PAIRS)]
        for pair in range(pairs):
            parts = []
            for part in range(2):
                at = base + (pair * 2 + part) * 8
                straight = sum(blocks[j] * coef_ref[at + j : at + j + 1, :] for j in range(PAIRS))
                crossed = sum(blocks[j] * coef_ref[at + 4 + j : at + 5 + j, :] for j in range(PAIRS))
                parts.append(straight + turn_half(crossed))
            cosine = twiddle_ref[twiddle_base + 2 * pair, rows, :]
            sine = twiddle_ref[twiddle_base + 2 * pair + 1, rows, :]
            store_split(rhs_ref, row, pair * LANES, parts[0] * cosine + parts[1] * sine)
            store_split(rhs_ref, row + ROWS, pair * LANES, parts[1] * cosine - parts[0] * sine)

    over_chunks(body)


def gather_pairs(values_ref, coef_ref, base, twiddle_ref, twiddle_base, pairs, store):
    def body(row):
        rows = pl.ds(row, CHUNK)
        straight, crossed = [0.0] * PAIRS, [0.0] * PAIRS
        for pair in range(pairs):
            lanes = slice(pair * LANES, (pair + 1) * LANES)
            real, imag = values_ref[rows, lanes], values_ref[pl.ds(row + ROWS, CHUNK), lanes]
            cosine = twiddle_ref[twiddle_base + 2 * pair, rows, :]
            sine = twiddle_ref[twiddle_base + 2 * pair + 1, rows, :]
            for part, value in enumerate((real * cosine - imag * sine, imag * cosine + real * sine)):
                at = base + (pair * 2 + part) * 8
                for j in range(PAIRS):
                    straight[j] = straight[j] + value * coef_ref[at + j : at + j + 1, :]
                    crossed[j] = crossed[j] + value * coef_ref[at + 4 + j : at + 5 + j, :]
        for j in range(PAIRS):
            store(j, rows, straight[j] + turn_half(crossed[j]))

    over_chunks(body)


GROUPS = ((0, 256), (256, 256), (512, 128))


def transform_into(dst_ref, mat_ref, which, rhs_ref, groups=GROUPS):
    for lane, width in groups:
        dst_ref[:, lane : lane + width] = split_product(mat_ref, which, rhs_ref, lane, width)


def multiply_spectra(left_ref, right_ref, rhs_ref, conjugate):
    def body(row):
        top, bottom = pl.ds(row, CHUNK), pl.ds(row + ROWS, CHUNK)
        for pair in range(5):
            lanes = slice(pair * LANES, (pair + 1) * LANES)
            a_re, a_im = left_ref[top, lanes], left_ref[bottom, lanes]
            b_re, b_im = right_ref[top, lanes], right_ref[bottom, lanes]
            if conjugate:
                out_re, out_im = a_re * b_re + a_im * b_im, a_re * b_im - a_im * b_re
            else:
                out_re, out_im = a_re * b_re - a_im * b_im, a_re * b_im + a_im * b_re
            store_split(rhs_ref, row, pair * LANES, out_re)
            store_split(rhs_ref, row + ROWS, pair * LANES, out_im)

    over_chunks(body)


def pair_terms(modes_ref):
    rank_re, rank_im, in_re, in_im, out_re, out_im = (modes_ref[i] for i in range(2, 8))
    return (
        (out_re * in_re + out_im * in_im, out_re * in_im - out_im * in_re),
        (out_re * rank_re + out_im * rank_im, out_re * rank_im - out_im * rank_re),
        (rank_re * in_re + rank_im * in_im, rank_re * in_im - rank_im * in_re),
        (rank_re * rank_re + rank_im * rank_im, None),
    )


def mode_values(modes_ref):
    index = lax.broadcasted_iota(jnp.int32, modes_ref.shape[1:], 0).astype(F32)
    return -0.5 * jnp.exp(modes_ref[0]), math.pi * (index + modes_ref[1])


POINT_ROWS = 16


def resolvent(coef_ref, n, square_cos, cos_sin, scaled):
    den_re = coef_ref[8, pl.ds(n, 1), :] * square_cos - scaled
    den_im = coef_ref[9, pl.ds(n, 1), :] * cos_sin
    inverse = 1.0 / (den_re * den_re + den_im * den_im)
    return den_re * inverse, -(den_im * inverse)


def complex_multiply(a_re, a_im, b_re, b_im):
    return a_re * b_re - a_im * b_im, a_re * b_im + a_im * b_re


def conj_multiply(a_re, a_im, b_re, b_im):
    return a_re * b_re + a_im * b_im, a_re * b_im - a_im * b_re


def combine(sums, sigma, cosine, sine):
    terms = []
    for p_re, p_im, q_re, q_im in (sums[4 * q : 4 * q + 4] for q in range(4)):
        swing = sigma * sine
        terms.append((-swing * p_im - cosine * q_re, swing * p_re - cosine * q_im))
    twice = 2.0 * cosine
    loop_re, loop_im = 1.0 + twice * terms[3][0], twice * terms[3][1]
    scale = 1.0 / (loop_re * loop_re + loop_im * loop_im)
    inv = (loop_re * scale, -(loop_im * scale))
    ratio = complex_multiply(twice * terms[2][0], twice * terms[2][1], *inv)
    return terms, inv, ratio


def cauchy_forward(modes_ref, sigma, coef_ref, wave_ref, sums_ref, rhs_ref, middle):
    lam_re, lam_im = mode_values(modes_ref)
    for q, (real, imag) in enumerate(pair_terms(modes_ref)):
        coef_ref[q] = real
        coef_ref[4 + q] = real * lam_re if imag is None else real * lam_re + imag * lam_im
    coef_ref[8] = lam_re * lam_re + lam_im * lam_im
    coef_ref[9] = -2.0 * sigma * lam_re
    sigma_sq = sigma * sigma
    for pair in range(2):

        def body(row, pair=pair):
            rows = pl.ds(row, POINT_ROWS)
            cosine, sine = wave_ref[0, pair, rows, :], wave_ref[1, pair, rows, :]
            square_cos, cos_sin, scaled = cosine * cosine, cosine * sine, sigma_sq * (sine * sine)

            def add_mode(n, sums):
                sums = list(sums)
                for k in range(4):
                    at = n * 4 + k
                    inv_re, inv_im = resolvent(coef_ref, at, square_cos, cos_sin, scaled)
                    for q in range(4):
                        plain = coef_ref[q, pl.ds(at, 1), :]
                        turned = coef_ref[4 + q, pl.ds(at, 1), :]
                        sums[4 * q] = sums[4 * q] + plain * inv_re
                        sums[4 * q + 1] = sums[4 * q + 1] + plain * inv_im
                        sums[4 * q + 2] = sums[4 * q + 2] + turned * inv_re
                        sums[4 * q + 3] = sums[4 * q + 3] + turned * inv_im
                return tuple(sums)

            zero = jnp.zeros((POINT_ROWS, LANES), F32)
            sums = lax.fori_loop(0, 8, add_mode, (zero,) * 16)
            for i in range(16):
                sums_ref[pair, i, rows, :] = sums[i]
            terms, _, ratio = combine(sums, sigma, cosine, sine)
            cut_re, cut_im = complex_multiply(*terms[1], *ratio)
            part_re, part_im = terms[0][0] - cut_re, terms[0][1] - cut_im
            spec_re, spec_im = complex_multiply(2.0 * cosine, 2.0 * sine, part_re, part_im)
            store_split(rhs_ref, row, pair * LANES, spec_re)
            store_split(rhs_ref, row + ROWS, pair * LANES, spec_im)

        for part in range(2):
            over_chunks(body, POINT_ROWS, part * HALF, HALF)
            middle(pair * 2 + part)


def cauchy_backward(modes_ref, sigma, nyquist_grad, step, coef_ref, wave_ref, sums_ref, spec_ref, grad_ref, back_ref, middle):
    zero = jnp.zeros((8, LANES), F32)
    sigma_sum = zero
    for pair in range(2):
        lanes = slice(pair * LANES, (pair + 1) * LANES)

        def start(index, total, pair=pair, lanes=lanes):
            row = pl.multiple_of(index * POINT_ROWS, POINT_ROWS)
            rows = pl.ds(row, POINT_ROWS)
            cosine, sine = wave_ref[0, pair, rows, :], wave_ref[1, pair, rows, :]
            sums = [sums_ref[pair, i, rows, :] for i in range(16)]
            terms, inv, ratio = combine(sums, sigma, cosine, sine)
            spec_re, spec_im = spec_ref[rows, lanes], spec_ref[pl.ds(row + ROWS, POINT_ROWS), lanes]
            part = conj_multiply(2.0 * cosine, 2.0 * sine, spec_re, spec_im)
            left = conj_multiply(*ratio, *part)
            ratio_grad = conj_multiply(*terms[1], *part)
            back = conj_multiply(*inv, -ratio_grad[0], -ratio_grad[1])
            twice = 2.0 * cosine
            loop = conj_multiply(*ratio, *back)
            grads = (
                part,
                (-left[0], -left[1]),
                (twice * back[0], twice * back[1]),
                (-twice * loop[0], -twice * loop[1]),
            )
            swing = sigma * sine
            for q, (g_re, g_im) in enumerate(grads):
                grad_ref[pair, 4 * q, rows, :] = swing * g_im
                grad_ref[pair, 4 * q + 1, rows, :] = -swing * g_re
                grad_ref[pair, 4 * q + 2, rows, :] = -cosine * g_re
                grad_ref[pair, 4 * q + 3, rows, :] = -cosine * g_im
                piece = sine * (g_im * sums[4 * q] - g_re * sums[4 * q + 1])
                total = total + piece[:8] + piece[8:]
            return total

        sigma_sum = lax.fori_loop(0, ROWS // POINT_ROWS, start, sigma_sum)
    sigma_sq = sigma * sigma

    def mode(n, square_sum):
        def point(index, sums):
            row = pl.multiple_of(index * 8, 8)
            rows = pl.ds(row, 8)
            sums = list(sums)
            for pair in range(2):
                cosine, sine = wave_ref[0, pair, rows, :], wave_ref[1, pair, rows, :]
                square_cos, cos_sin, square_sin = cosine * cosine, cosine * sine, sine * sine
                inv_re, inv_im = resolvent(coef_ref, n, square_cos, cos_sin, sigma_sq * square_sin)
                grad_re, grad_im = 0.0, 0.0
                for q in range(4):
                    plain = coef_ref[q, pl.ds(n, 1), :]
                    turned = coef_ref[4 + q, pl.ds(n, 1), :]
                    p_re, p_im = grad_ref[pair, 4 * q, rows, :], grad_ref[pair, 4 * q + 1, rows, :]
                    q_re, q_im = grad_ref[pair, 4 * q + 2, rows, :], grad_ref[pair, 4 * q + 3, rows, :]
                    grad_re = grad_re + plain * p_re + turned * q_re
                    grad_im = grad_im + plain * p_im + turned * q_im
                    sums[q] = sums[q] + (p_re * inv_re + p_im * inv_im)
                    sums[4 + q] = sums[4 + q] + (q_re * inv_re + q_im * inv_im)
                square_re = inv_re * inv_re - inv_im * inv_im
                square_im = 2.0 * inv_re * inv_im
                den_re, den_im = conj_multiply(square_re, square_im, grad_re, grad_im)
                sums[8] = sums[8] - den_re * square_cos
                sums[9] = sums[9] - den_im * cos_sin
                sums[10] = sums[10] + den_re * square_sin
            return tuple(sums)

        sums = lax.fori_loop(0, ROWS // 8, point, (zero,) * 10 + (square_sum,))
        for i in range(10):
            back_ref[i, pl.ds(n, 1), :] = column_sum(sums[i])
        return sums[10]

    square_sum = zero
    for part in range(4):
        square_sum = lax.fori_loop(part * 8, part * 8 + 8, mode, square_sum)
        middle(part)
    plain_grad = [fold(back_ref[q]) for q in range(4)]
    turned_grad = [fold(back_ref[4 + q]) for q in range(4)]
    abs_grad, skew_grad = fold(back_ref[8]), fold(back_ref[9])
    lam_re, lam_im = mode_values(modes_ref)
    plain_grad[0] = plain_grad[0] + step * nyquist_grad
    rank_re, rank_im, in_re, in_im, out_re, out_im = (modes_ref[i] for i in range(2, 8))
    lam_re_grad = 2.0 * lam_re * abs_grad - 2.0 * sigma * skew_grad
    lam_im_grad = 2.0 * lam_im * abs_grad
    real_grad, imag_grad = [], []
    terms = pair_terms(modes_ref)
    for q, (real, imag) in enumerate(terms):
        lam_re_grad = lam_re_grad + turned_grad[q] * real
        if imag is not None:
            lam_im_grad = lam_im_grad + turned_grad[q] * imag
        real_grad.append(plain_grad[q] + turned_grad[q] * lam_re)
        imag_grad.append(turned_grad[q] * lam_im)
    r0, r1, r2, r3 = real_grad
    i0, i1, i2, _ = imag_grad
    grads = (
        lam_re_grad * lam_re,
        math.pi * lam_im_grad,
        r1 * out_re - i1 * out_im + r2 * in_re + i2 * in_im + 2.0 * r3 * rank_re,
        r1 * out_im + i1 * out_re + r2 * in_im - i2 * in_re + 2.0 * r3 * rank_im,
        r0 * out_re - i0 * out_im + r2 * rank_re - i2 * rank_im,
        r0 * out_im + i0 * out_re + r2 * rank_im + i2 * rank_re,
        r0 * in_re + i0 * in_im + r1 * rank_re + i1 * rank_im,
        r0 * in_im - i0 * in_re + r1 * rank_im - i1 * rank_re,
    )
    sigma_grad = (
        fold(column_sum(sigma_sum) + 2.0 * sigma * column_sum(square_sum))
        - 2.0 * column_sum(skew_grad * lam_re)
    )
    nyquist = step * column_sum(terms[0][0])
    return grads, nyquist * nyquist_grad - sigma * sigma_grad


def ring_place(chan):
    z, y = chan // 2, chan % 2
    return z + y * (7 - 2 * z)


def ring_chan(place):
    back = place // 4
    z = place * (1 - back) + (7 - place) * back
    return 2 * z + back


TURNS = (1, -1)


def ring_items():
    out = []
    for step in range(1, 5):
        for turn in range(2):
            for block in range(2):
                if step < 4 or block == turn:
                    out.append((turn, step, block))
    return out


def item_slot(turn, step, block):
    return (turn * 4 + step - 1) * 2 + block


def block_kernel(
    bucket_ref, items_ref, tokens_ref, cotangent_ref, gain1_ref, bias1_ref, raw_modes_ref, log_dt_ref, skip_ref,
    wa_ref, ba_ref, wb_ref, bb_ref, gain2_ref, bias2_ref, up_ref, bup_ref, down_ref, bdown_ref,
    levels_ref, coefc_ref, mat_ref, tw_ref, wave_ref,
    out_ref, dtok_ref, gw_ref, gm_ref, gv_ref,
    tok_ref, aux_ref, coefl_ref, modes_ref,
    w_ref, grad_ref, sib_ref, ring_ref, part_ref,
    in_send, in_recv, head_send, head_recv, acts_send, acts_recv, back_send, back_recv, late_send, late_recv,
    sum_send, sum_recv, tail_send, tail_recv, dp_send, dp_recv,
    hat_ref, norm_ref, slope_ref, conv_ref, rhs_ref, freq_ref, sig_ref, ans_ref, taps_ref,
    mcoef_ref, sums_ref, pgrad_ref, mback_ref,
    gate_ref, swish_ref, res_ref, hat2_ref, low_ref, branch_ref, back2_ref, gab_ref, hid_ref, gpre_ref,
    ring_ss, ring_rs, sib_ss, sib_rs, x_ss, x_rs, rring_ss, rring_rs, rsib_ss, rsib_rs, rx_ss, rx_rs, a2a_ss, a2a_rs, dp_ss, dp_rs,
):
    dp, chan = lax.axis_index("dp"), lax.axis_index("chan")
    core = dp % 2
    sibling = dp + 1 - 2 * core
    across = (dp + 2) % 4
    place = ring_place(chan)
    nexts = [ring_chan((place + 1) % 8), ring_chan((place + 7) % 8)]

    def chan_at(offset):
        return ring_chan((place + offset + 8) % 8)

    barrier = pltpu.get_barrier_semaphore()
    for r in range(1, N_CHAN):
        pl.semaphore_signal(barrier, inc=1, device_id={"chan": (chan + r) % N_CHAN}, device_id_type=MESH)
    for r in range(1, 4):
        pl.semaphore_signal(barrier, inc=1, device_id={"dp": (dp + r) % 4}, device_id_type=MESH)
    pl.semaphore_wait(barrier, N_CHAN - 1 + 3)

    pending = []

    def remote(src, dst, send_sem, recv_sem, **device):
        return pltpu.make_async_remote_copy(
            src_ref=src, dst_ref=dst, send_sem=send_sem, recv_sem=recv_sem, device_id=device, device_id_type=MESH
        )

    def send(*args, **device):
        copy = remote(*args, **device)
        copy.start()
        pending.append(copy)

    def exchange(which, source, recv_ref):
        def copy(r):
            peer = (chan + r) % N_CHAN
            return remote(
                source(peer), recv_ref.at[chan], a2a_ss.at[which, r - 1], a2a_rs.at[which, r - 1], chan=peer
            )

        def start():
            for r in range(1, N_CHAN):
                copy(r).start()

        def wait():
            for r in range(1, N_CHAN):
                copy(r).wait_recv()

        def finish():
            for r in range(1, N_CHAN):
                copy(r).wait_send()

        return start, wait, finish

    def row_of(group):
        return pl.multiple_of(group * ROWS, ROWS)

    def weight(chan_id, group):
        return w_ref.at[chan_id, pl.ds(row_of(group), ROWS), :]

    mine = (dp, across)
    theirs = (sibling, (sibling + 2) % 4)

    def origin(turn, step):
        return chan_at(-TURNS[turn] * step)

    def ring_copy(turn, step, block):
        slot = item_slot(turn, step, block)
        ref = weight(origin(turn, step - 1), mine[block])
        return remote(ref, ref, ring_ss.at[slot], ring_rs.at[slot], chan=nexts[turn])

    def sib_copy(chan_id, block, slot):
        ref = weight(chan_id, mine[block])
        return remote(ref, ref, sib_ss.at[slot], sib_rs.at[slot], dp=sibling)

    def ring_got(turn, step, block):
        slot = item_slot(turn, step, block)
        ref = weight(origin(turn, step), mine[block])
        remote(ref, ref, ring_ss.at[slot], ring_rs.at[slot], chan=nexts[turn]).wait_recv()

    def gather_start():
        rows = pl.ds(row_of(dp), ROWS)
        w_ref[chan, rows, 0:128] = jnp.concatenate([wa_ref[...], wb_ref[...]], axis=0).T.astype(BF16)
        w_ref[chan, rows, 128:384] = up_ref[...].astype(BF16)
        w_ref[chan, rows, 384:640] = down_ref[...].T.astype(BF16)
        x_ref = weight(chan, dp)
        send(x_ref, x_ref, x_ss, x_rs, dp=across)
        for turn in range(2):
            copy = ring_copy(turn, 1, 0)
            copy.start()
            pending.append(copy)
        copy = sib_copy(chan, 0, 16)
        copy.start()
        pending.append(copy)

    def gather_across():
        x_ref = weight(chan, across)
        remote(x_ref, x_ref, x_ss, x_rs, dp=across).wait_recv()
        for turn in range(2):
            copy = ring_copy(turn, 1, 1)
            copy.start()
            pending.append(copy)
        copy = sib_copy(chan, 1, 17)
        copy.start()
        pending.append(copy)

    items = ring_items()

    def gather_step(step, which):
        for turn, at, block in items:
            if at != step or block != which:
                continue
            ring_got(turn, step, block)
            if (turn, step + 1, block) in items:
                copy = ring_copy(turn, step + 1, block)
                copy.start()
                pending.append(copy)
            copy = sib_copy(origin(turn, step), block, item_slot(turn, step, block))
            copy.start()
            pending.append(copy)

    def gather_finish():
        def got(chan_id, block, slot):
            ref = weight(chan_id, theirs[block])
            remote(ref, ref, sib_ss.at[slot], sib_rs.at[slot], dp=sibling).wait_recv()

        got(chan, 0, 16)
        got(chan, 1, 17)
        for turn, step, block in items:
            got(origin(turn, step), block, item_slot(turn, step, block))

    def beside(ref, j):
        start = 2 * j * ROWS
        return jnp.concatenate(
            [ref[:, start : start + ROWS].astype(F32), ref[:, start + ROWS : start + 2 * ROWS].astype(F32)], axis=0
        ).T

    for j in range(PAIRS):
        packed = beside(tokens_ref, j)
        tok_ref[j * ROWS : (j + 1) * ROWS, :] = packed.astype(BF16)
        for first, values in ((0, packed), (HALF, beside(cotangent_ref, j))):
            low, high = split_pair(values)
            in_send[2 * j, first : first + HALF, :] = low.astype(BF16)
            in_send[2 * j + 1, first : first + HALF, :] = high.astype(BF16)
    in_recv[chan] = in_send[chan]

    lane_id = lax.broadcasted_iota(jnp.int32, (8, LANES), 1)
    row_id = lax.broadcasted_iota(jnp.int32, (8, LANES), 0)
    halves = jnp.where((lane_id >= HALF) == (row_id == 1), 1.0, 0.0) * jnp.where(row_id < 2, 1.0, 0.0)
    halves = halves.astype(BF16)

    def token_sums(parts):
        total = 0.0
        for part in parts:
            total = total + dot_nt(halves, part)
        return [total[h : h + 1, j * ROWS : (j + 1) * ROWS] for h in range(2) for j in range(PAIRS)]

    def split(values):
        high = values.astype(BF16)
        return high, (values - high.astype(F32)).astype(BF16)

    tokens = tok_ref[...]
    wide_tokens = tokens.astype(F32)
    for i, sums in enumerate(token_sums([tokens]) + token_sums(split(wide_tokens * wide_tokens))):
        head_send[i : i + 1, :] = sums

    def row(*refs):
        return jnp.concatenate([ref[...].reshape(1, HALF) for ref in refs], axis=1)

    bup = bup_ref[...].reshape(1, 2 * LANES)
    head_send[16:17, :] = row(ba_ref, bb_ref)
    head_send[17:18, :] = row(gain2_ref, bias2_ref)
    head_send[18:19, :] = row(bdown_ref, bdown_ref)
    head_send[19:20, :] = bup[:, :LANES]
    head_send[20:21, :] = bup[:, LANES:]
    head_send[21:24, :] = jnp.zeros((3, LANES), F32)
    head_recv[chan] = head_send[...]
    head = exchange(0, lambda peer: head_send, head_recv)
    inputs = exchange(1, lambda peer: in_send.at[peer], in_recv)
    head[0]()
    gather_start()
    inputs[0]()

    level, filled = bucket_ref[0], items_ref[0]
    coefl_ref[...] = levels_ref[level]
    item_blocks = jnp.where(level == 0, 2, jnp.where(level == 1, 4, 8))
    block_id = 2 * (row_id % PAIRS) + jnp.where(lane_id >= HALF, 1, 0)
    bound = jnp.where(row_id < PAIRS, filled * item_blocks, item_blocks)
    aux_ref[...] = jnp.where(block_id < bound, 1.0, 0.0)
    for i in range(8):
        modes_ref[i] = jnp.concatenate([raw_modes_ref[i], raw_modes_ref[i]], axis=1)
    log_dt = row(log_dt_ref, log_dt_ref)
    sigma, step_size = 2.0 * jnp.exp(-log_dt), jnp.exp(log_dt)

    def after_quarter(quarter):
        if quarter == 0:
            gather_across()
        elif quarter == 1:
            gather_step(1, 0)
        elif quarter == 3:
            gather_step(1, 1)

    cauchy_forward(modes_ref, sigma, mcoef_ref, wave_ref, sums_ref, rhs_ref, after_quarter)
    freq_ref[:, 0:256] = split_product(mat_ref, 1, rhs_ref, 0, 256)
    even = split_product(mat_ref, 2, rhs_ref, LANES, LANES)
    freq_ref[:, LANES:256] = jnp.where(low_lanes(256), freq_ref[:, LANES:256], even)
    sign = 1.0 - 2.0 * (lax.broadcasted_iota(jnp.int32, (CHUNK, LANES), 0) % 2).astype(F32)
    nyquist = step_size * column_sum(mcoef_ref[0]) * (1.0 / TOK_DEV)

    def store_taps(j, rows, values):
        taps_ref[j, rows, :] = (values + sign * nyquist) * aux_ref[4 + j : 5 + j, :]

    gather_pairs(freq_ref, coefc_ref, 160, tw_ref, 10, 2, store_taps)
    gather_step(2, 0)
    spread_pairs(lambda j, rows: taps_ref[j, rows, :], coefc_ref, 0, tw_ref, 0, 5, rhs_ref)
    transform_into(ans_ref, mat_ref, 0, rhs_ref)

    head[1]()
    sums = head_recv[0, 0:16, :]
    for c in range(1, N_CHAN):
        sums = sums + head_recv[c, 0:16, :]
    mean = sums[0:8] * (1.0 / MODEL_WIDTH)
    rstd = lax.rsqrt(sums[8:16] * (1.0 / MODEL_WIDTH) - mean * mean + EPSILON)

    def columns(rows):
        tall = rows.T
        return [jnp.where(low_lanes(ROWS), tall[:, j : j + 1], tall[:, 4 + j : 5 + j]) for j in range(PAIRS)]

    gain1, bias1, skip = row(gain1_ref, gain1_ref), row(bias1_ref, bias1_ref), row(skip_ref, skip_ref)
    mean_cols, rstd_cols = columns(mean), columns(rstd)
    for j in range(PAIRS):
        hat = (tok_ref[j * ROWS : (j + 1) * ROWS, :].astype(F32) - mean_cols[j]) * rstd_cols[j]
        hat_ref[j] = hat
        norm_ref[j] = hat * gain1 + bias1

    spread_pairs(lambda j, rows: norm_ref[j, rows, :], coefl_ref, 0, tw_ref, 0, 5, rhs_ref)
    transform_into(sig_ref, mat_ref, 0, rhs_ref)
    gather_step(2, 1)
    multiply_spectra(sig_ref, ans_ref, rhs_ref, False)
    transform_into(freq_ref, mat_ref, 1, rhs_ref)

    def store_conv(j, rows, values):
        conv_ref[j, rows, :] = values

    gather_pairs(freq_ref, coefl_ref, 80, tw_ref, 0, 5, store_conv)
    gather_step(3, 0)
    for j in range(PAIRS):
        mixed = conv_ref[j] * aux_ref[j : j + 1, :] + skip * norm_ref[j]
        cumulative, density = normal_parts(mixed)
        slope_ref[j] = cumulative + mixed * density
        low, high = split_pair(mixed * cumulative)
        acts_send[2 * j] = low.astype(BF16)
        acts_send[2 * j + 1] = high.astype(BF16)
    acts_recv[chan] = acts_send[chan]
    acts = exchange(2, lambda peer: acts_send.at[peer], acts_recv)
    acts[0]()
    gather_step(3, 1)
    gather_step(4, 0)
    gather_step(4, 1)
    inputs[1]()
    acts[1]()

    def joined(ref, pair, first):
        return join_pair(
            ref[2 * pair, first : first + HALF, :].astype(F32), ref[2 * pair + 1, first : first + HALF, :].astype(F32)
        )

    def lanes_of(pair):
        return slice(pair * LANES, (pair + 1) * LANES)

    ACTS, NORM2, GRADF = range(3)
    for p in range(PAIRS):
        low_ref[ACTS, :, lanes_of(p)] = joined(acts_recv, p, 0).astype(BF16)
        low_ref[GRADF, :, lanes_of(p)] = joined(in_recv, p, HALF).astype(BF16)
    gather_finish()

    def vector(row, first, second):
        return interleave(head_recv[first, 16 + row : 17 + row, :], head_recv[second, 16 + row : 17 + row, :])

    total = 0.0
    for p in range(PAIRS):
        first = dot_nn(low_ref[ACTS], w_ref[2 * p, :, 0:LANES]) + head_recv[2 * p, 16:17, :]
        second = dot_nn(low_ref[ACTS], w_ref[2 * p + 1, :, 0:LANES]) + head_recv[2 * p + 1, 16:17, :]
        gate, raw = interleave(first, second)
        swish = lax.logistic(raw)
        gate_ref[p], swish_ref[p] = gate, swish
        resid = joined(in_recv, p, 0) + gate * swish
        res_ref[p] = resid
        total = total + resid
    mean2 = jnp.sum(total, axis=1, keepdims=True) * (1.0 / MODEL_WIDTH)
    total = 0.0
    for p in range(PAIRS):
        centred = res_ref[p] - mean2
        total = total + centred * centred
    rstd2 = lax.rsqrt(jnp.sum(total, axis=1, keepdims=True) * (1.0 / MODEL_WIDTH) + EPSILON)
    gain2 = []
    for p in range(PAIRS):
        gain, bias = vector(1, 2 * p, 2 * p + 1)
        gain2.append(gain)
        hat = (res_ref[p] - mean2) * rstd2
        hat2_ref[p] = hat
        low_ref[NORM2, :, lanes_of(p)] = (hat * gain + bias).astype(BF16)
    branch_ref[...] = jnp.zeros_like(branch_ref)
    back2_ref[...] = jnp.zeros_like(back2_ref)

    def hidden_block(c, carry):
        bias = jnp.concatenate([head_recv[c, 19:20, :], head_recv[c, 20:21, :]], axis=1)
        pre = dot_nn(low_ref[NORM2], w_ref[c, :, 128:384]) + bias
        cumulative, density = normal_parts(pre)
        hidden = (pre * cumulative).astype(BF16)
        hid_ref[c] = hidden
        grad = dot_nn(low_ref[GRADF], w_ref[c, :, 384:640]) * (cumulative + pre * density)
        grad = grad.astype(BF16)
        gpre_ref[c] = grad
        sums = column_sum(grad.astype(F32))
        tail_send[c, 3:4, :] = sums[:, 0:LANES]
        tail_send[c, 4:5, :] = sums[:, LANES : 2 * LANES]
        branch_ref[...] += dot_nt(hidden, w_ref[c, :, 384:640])
        back2_ref[...] += dot_nt(grad, w_ref[c, :, 128:384])
        return carry

    lax.fori_loop(0, N_CHAN, hidden_block, 0)

    mean_q, mean_qx = 0.0, 0.0
    for p in range(PAIRS):
        grad, hat = back2_ref[:, lanes_of(p)], hat2_ref[p]
        q = grad * gain2[p]
        mean_q = mean_q + q
        mean_qx = mean_qx + q * hat
        gain_grad, bias_grad = interleave(column_sum(grad * hat), column_sum(grad))
        tail_send[2 * p, 1:2, :] = gain_grad
        first, second = interleave(turn_half(column_sum(grad * hat)), turn_half(column_sum(grad)))
        tail_send[2 * p + 1, 1:2, :] = first
    mean_q = jnp.sum(mean_q, axis=1, keepdims=True) * (1.0 / MODEL_WIDTH)
    mean_qx = jnp.sum(mean_qx, axis=1, keepdims=True) * (1.0 / MODEL_WIDTH)
    for p in range(PAIRS):
        hat = hat2_ref[p]
        extra = rstd2 * (back2_ref[:, lanes_of(p)] * gain2[p] - mean_q - hat * mean_qx)
        grad_f = joined(in_recv, p, HALF)
        grad_resid = grad_f + extra
        gate, swish = gate_ref[p], swish_ref[p]
        grad_a = (grad_resid * swish).astype(BF16).astype(F32)
        grad_b = (grad_resid * gate * swish * (1.0 - swish)).astype(BF16).astype(F32)
        first, second = interleave(grad_a, grad_b)
        gab_ref[2 * p] = first.astype(BF16)
        gab_ref[2 * p + 1] = second.astype(BF16)
        tail_send[2 * p, 0:1, :] = column_sum(first)
        tail_send[2 * p + 1, 0:1, :] = column_sum(second)
        low, high = interleave(column_sum(grad_f), column_sum(grad_f))
        tail_send[2 * p, 2:3, :] = low
        tail_send[2 * p + 1, 2:3, :] = high
        low, high = split_pair(extra)
        late_send[2 * p, HALF:, :] = low.astype(BF16)
        late_send[2 * p + 1, HALF:, :] = high.astype(BF16)
    grad_acts = 0.0
    for c in range(N_CHAN):
        grad_acts = grad_acts + dot_nt(gab_ref[c], w_ref[c, :, 0:LANES])
    for p in range(PAIRS):
        low, high = split_pair(grad_acts[:, lanes_of(p)])
        back_send[2 * p] = low.astype(BF16)
        back_send[2 * p + 1] = high.astype(BF16)
    back_recv[chan] = back_send[chan]
    back = exchange(3, lambda peer: back_send.at[peer], back_recv)
    back[0]()

    def rsib_copy(offset, block):
        slot = (offset + 3) * 2 + block
        src = grad_ref.at[chan_at(offset), pl.ds(row_of(theirs[block]), ROWS), :]
        return remote(src, sib_ref.at[slot], rsib_ss.at[slot], rsib_rs.at[slot], dp=sibling)

    def offset_of(turn, step):
        return TURNS[turn] * (5 - step)

    def rring_copy(turn, step, block):
        slot = item_slot(turn, step, block)
        src = grad_ref.at[chan_at(offset_of(turn, step)), pl.ds(row_of(mine[block]), ROWS), :]
        return remote(src, ring_ref.at[slot], rring_ss.at[slot], rring_rs.at[slot], chan=nexts[turn])

    ritems = [(turn, 5 - step, block) for turn, step, block in items]

    def own_and_sibling(offset, block):
        slot = ((offset if offset != -4 else 4) + 3) * 2 + block
        rsib_copy(offset if offset != -4 else 4, block).wait_recv()
        own = grad_ref[chan_at(offset), pl.ds(row_of(mine[block]), ROWS), :].astype(F32)
        return own + sib_ref[slot].astype(F32)

    def reduce_step(step):
        for turn, at, block in ritems:
            if at != step:
                continue
            total = own_and_sibling(offset_of(turn, step), block)
            if (turn, step - 1, block) in ritems:
                rring_copy(turn, step - 1, block).wait_recv()
                total = total + ring_ref[item_slot(turn, step - 1, block)].astype(F32)
            grad_ref[chan_at(offset_of(turn, step)), pl.ds(row_of(mine[block]), ROWS), :] = total.astype(BF16)
            copy = rring_copy(turn, step, block)
            copy.start()
            pending.append(copy)

    def reduce_last():
        for block in (1, 0):
            total = own_and_sibling(0, block)
            for turn in range(2):
                rring_copy(turn, 4, block).wait_recv()
                total = total + ring_ref[item_slot(turn, 4, block)].astype(F32)
            if block == 1:
                part_ref[0] = total.astype(BF16)
                send(part_ref.at[0], part_ref.at[1], rx_ss, rx_rs, dp=across)
            else:
                gw_ref[...] = total

    def reduce_finish():
        remote(part_ref.at[0], part_ref.at[1], rx_ss, rx_rs, dp=across).wait_recv()
        gw_ref[...] += part_ref[1].astype(F32)

    tall = [low_ref[i].astype(F32).T.astype(BF16) for i in range(3)]
    order = (4, 3, -3, 2, -2, 1, -1, 0)
    for offset in order:
        c = chan_at(offset)
        grad_ref[c, :, 0:128] = dot_nn(tall[ACTS], gab_ref[c]).astype(BF16)
        grad_ref[c, :, 128:384] = dot_nn(tall[NORM2], gpre_ref[c]).astype(BF16)
        grad_ref[c, :, 384:640] = dot_nn(tall[GRADF], hid_ref[c]).astype(BF16)
        for block in range(2):
            copy = rsib_copy(offset, block)
            copy.start()
            pending.append(copy)
        if offset == -3:
            reduce_step(1)
        elif offset == -1:
            reduce_step(2)
    for p in range(PAIRS):
        out = res_ref[p] + branch_ref[:, lanes_of(p)] + interleave(head_recv[2 * p, 18:19, :], head_recv[2 * p + 1, 18:19, :])[0]
        low, high = split_pair(out)
        late_send[2 * p, :HALF, :] = low.astype(BF16)
        late_send[2 * p + 1, :HALF, :] = high.astype(BF16)
    for c in range(N_CHAN):
        tail_send[c, 5:8, :] = jnp.zeros((3, LANES), F32)
    late_recv[chan] = late_send[chan]
    tail_recv[chan] = tail_send[chan]
    late = exchange(4, lambda peer: late_send.at[peer], late_recv)
    tail = exchange(5, lambda peer: tail_send.at[peer], tail_recv)
    late[0]()
    tail[0]()

    back[1]()
    skip_grad = 0.0
    for j in range(PAIRS):
        grad = joined(back_recv, j, 0) * slope_ref[j]
        slope_ref[j] = grad
        conv_ref[j] = grad * aux_ref[j : j + 1, :]
        skip_grad = skip_grad + column_sum(grad * norm_ref[j])
    spread_pairs(lambda j, rows: conv_ref[j, rows, :], coefl_ref, 0, tw_ref, 0, 5, rhs_ref)
    transform_into(freq_ref, mat_ref, 0, rhs_ref)
    multiply_spectra(sig_ref, freq_ref, rhs_ref, True)
    transform_into(sig_ref, mat_ref, 1, rhs_ref)

    def store_kernel_grad(j, rows, values):
        taps_ref[j, rows, :] = values * aux_ref[4 + j : 5 + j, :]

    gather_pairs(sig_ref, coefc_ref, 80, tw_ref, 0, 5, store_kernel_grad)
    multiply_spectra(ans_ref, freq_ref, rhs_ref, True)
    transform_into(freq_ref, mat_ref, 1, rhs_ref)
    gather_pairs(freq_ref, coefl_ref, 80, tw_ref, 0, 5, store_conv)
    gain_grad, bias_grad = 0.0, 0.0
    scaled, crossed = [], []
    for j in range(PAIRS):
        grad = conv_ref[j] + skip * slope_ref[j]
        conv_ref[j] = grad
        gain_grad = gain_grad + column_sum(grad * hat_ref[j])
        bias_grad = bias_grad + column_sum(grad)
    conv = conv_ref[...].reshape(PAIRS * ROWS, LANES) * gain1
    for i, sums in enumerate(
        token_sums(split(conv)) + token_sums(split(conv * hat_ref[...].reshape(PAIRS * ROWS, LANES)))
    ):
        sum_send[i : i + 1, :] = sums
    sum_recv[chan] = sum_send[...]
    sums_back = exchange(6, lambda peer: sum_send, sum_recv)
    sums_back[0]()
    reduce_step(3)

    nyquist_grad = 0.0
    for j in range(PAIRS):
        whole_sign = 1.0 - 2.0 * (lax.broadcasted_iota(jnp.int32, (ROWS, LANES), 0) % 2).astype(F32)
        nyquist_grad = nyquist_grad + column_sum(taps_ref[j] * whole_sign)
    nyquist_grad = fold(nyquist_grad) * (1.0 / TOK_DEV)
    spread_pairs(lambda j, rows: taps_ref[j, rows, :], coefc_ref, 192, tw_ref, 10, 2, rhs_ref)
    freq_ref[:, 0:256] = split_product(mat_ref, 0, rhs_ref, 0, 256)
    even = split_product(mat_ref, 3, rhs_ref, LANES, LANES)
    freq_ref[:, LANES:256] = jnp.where(low_lanes(256), freq_ref[:, LANES:256], even)

    def after_part(part):
        if part == 1:
            reduce_step(4)
        elif part == 3:
            reduce_last()

    mode_grads, dt_grad = cauchy_backward(
        modes_ref, sigma, nyquist_grad, step_size, mcoef_ref, wave_ref, sums_ref, freq_ref, pgrad_ref, mback_ref,
        after_part,
    )
    mask = low_lanes(32)
    for i in range(4):
        dp_send[i * 32 : (i + 1) * 32, :] = jnp.where(mask, mode_grads[i], mode_grads[i + 4])
    first = low_lanes(1)
    dp_send[128:129, :] = jnp.where(first, dt_grad, fold(skip_grad))
    dp_send[129:130, :] = jnp.where(first, fold(gain_grad), fold(bias_grad))
    dp_send[130:136, :] = jnp.zeros((6, LANES), F32)
    tail[1]()
    tail_sum = tail_recv[0]
    for c in range(1, N_CHAN):
        tail_sum = tail_sum + tail_recv[c]
    dp_send[136:144, :] = tail_sum
    dp_recv[0] = dp_send[...]

    def dp_copy(r):
        return remote(dp_send, dp_recv.at[r], dp_ss.at[r - 1], dp_rs.at[r - 1], dp=(dp + r) % 4)

    for r in range(1, 4):
        dp_copy(r).start()

    sums_back[1]()
    sums = sum_recv[0]
    for c in range(1, N_CHAN):
        sums = sums + sum_recv[c]
    sums = sums * (1.0 / MODEL_WIDTH)
    rstd_cols, q_cols, qx_cols = columns(rstd), columns(sums[0:8]), columns(sums[8:16])
    late[1]()
    for j in range(PAIRS):
        rows = slice(j * ROWS, (j + 1) * ROWS)
        out_ref[rows, :] = joined(late_recv, j, 0).astype(BF16)
        dtok_ref[rows, :] = joined(late_recv, j, HALF) + rstd_cols[j] * (
            conv_ref[j] * gain1 - q_cols[j] - hat_ref[j] * qx_cols[j]
        )
    for r in range(1, 4):
        dp_copy(r).wait_recv()
    total = dp_recv[0] + dp_recv[1] + dp_recv[2] + dp_recv[3]
    gm_ref[...] = total[0:128]
    gv_ref[...] = total[128:144]
    reduce_finish()
    for copy in pending:
        copy.wait_send()
    for group in (head, inputs, acts, back, late, tail, sums_back):
        group[2]()
    for r in range(1, 4):
        dp_copy(r).wait_send()


def unpack_kernel(
    out_ref, dtok_ref, gw_ref, gm_ref, gv_ref, cotangent_ref,
    output_ref, tokens_ref, gain1_ref, bias1_ref, modes_ref, dt_ref, skip_ref, wa_ref, ba_ref, wb_ref, bb_ref,
    gain2_ref, bias2_ref, up_ref, bup_ref, down_ref, bdown_ref,
):
    for j in range(PAIRS):
        out = out_ref[j * ROWS : (j + 1) * ROWS, :].astype(F32).T.astype(BF16)
        grad = dtok_ref[j * ROWS : (j + 1) * ROWS, :].T
        for h in range(2):
            lanes, rows = slice((2 * j + h) * ROWS, (2 * j + h + 1) * ROWS), slice(h * HALF, (h + 1) * HALF)
            output_ref[:, lanes] = out[rows]
            tokens_ref[:, lanes] = cotangent_ref[:, lanes] + grad[rows]
    for i in range(8):
        modes_ref[i] = gm_ref[i % 4 * 32 : i % 4 * 32 + 32, i // 4 * HALF : (i // 4 + 1) * HALF]
    gates = gw_ref[:, :LANES].T
    wa_ref[...] = gates[:HALF]
    wb_ref[...] = gates[HALF:]
    up_ref[...] = gw_ref[:, 128:384]
    down_ref[...] = gw_ref[:, 384:640].T
    for at, low, high in (
        (0, dt_ref, skip_ref), (1, gain1_ref, bias1_ref), (8, ba_ref, bb_ref), (9, gain2_ref, bias2_ref),
    ):
        low[...] = gv_ref[at, :HALF]
        high[...] = gv_ref[at, HALF:]
    bdown_ref[...] = gv_ref[10, :HALF]
    bup_ref[:LANES] = gv_ref[11, :]
    bup_ref[LANES:] = gv_ref[12, :]


def block_program():
    mats, twiddle, levels, constant, wave = mixer_tables()

    def run(tokens, cotangent, bucket, items, gain1, bias1, modes, log_dt, skip, w_a, b_a, w_b, b_b, gain2, bias2, w_up, b_up, w_down, b_down):
        vmem = pl.BlockSpec(memory_space=pltpu.VMEM)
        smem = pl.BlockSpec(memory_space=pltpu.SMEM)
        dma = pltpu.SemaphoreType.DMA

        def buf(*shape):
            return pltpu.VMEM(shape, F32)

        def low(*shape):
            return pltpu.VMEM(shape, BF16)

        def full(*shape):
            return jax.ShapeDtypeStruct(shape, F32)

        big, wide = (PAIRS, ROWS, LANES), (256, WIDE)
        packed = pl.pallas_call(
            block_kernel,
            out_shape=(
                jax.ShapeDtypeStruct((512, LANES), BF16), full(512, LANES), full(ROWS, WIDE), full(ROWS, LANES),
                full(16, LANES),
            ),
            in_specs=[smem] * 2 + [vmem] * 22,
            out_specs=(vmem,) * 5,
            scratch_shapes=[
                low(512, LANES), buf(8, LANES), buf(160, LANES), buf(8, 32, LANES),
                low(N_CHAN, 512, WIDE), low(N_CHAN, 512, WIDE), low(16, ROWS, WIDE), low(16, ROWS, WIDE), low(2, ROWS, WIDE),
                low(N_CHAN, ROWS, LANES), low(N_CHAN, ROWS, LANES), buf(24, LANES), buf(N_CHAN, 24, LANES),
                low(N_CHAN, HALF, LANES), low(N_CHAN, HALF, LANES), low(N_CHAN, HALF, LANES), low(N_CHAN, HALF, LANES),
                low(N_CHAN, ROWS, LANES), low(N_CHAN, ROWS, LANES),
                buf(16, LANES), buf(N_CHAN, 16, LANES), buf(N_CHAN, 8, LANES), buf(N_CHAN, 8, LANES),
                buf(144, LANES), buf(4, 144, LANES),
                buf(*big), buf(*big), buf(*big), buf(*big), low(2, *wide), buf(*wide), buf(*wide), buf(*wide), buf(*big),
                buf(10, 32, LANES), buf(2, 16, ROWS, LANES), buf(2, 16, ROWS, LANES), buf(10, 32, LANES),
                buf(*big), buf(*big), buf(*big), buf(*big), low(3, ROWS, 512), buf(ROWS, 512), buf(ROWS, 512),
                low(N_CHAN, ROWS, LANES), low(N_CHAN, ROWS, 256), low(N_CHAN, ROWS, 256),
                dma((16,)), dma((16,)), dma((18,)), dma((18,)), dma, dma, dma((16,)), dma((16,)), dma((16,)), dma((16,)),
                dma, dma, dma((7, 7)), dma((7, 7)), dma((3,)), dma((3,)),
            ],
            compiler_params=pltpu.CompilerParams(
                collective_id=0, has_side_effects=True, vmem_limit_bytes=60 * 1024 * 1024
            ),
            name="block",
        )(
            bucket, items, tokens.T, cotangent.T, gain1, bias1, jnp.swapaxes(modes, 1, 2), log_dt, skip,
            w_a.T, b_a, w_b.T, b_b, gain2, bias2,
            w_up, b_up, w_down, b_down, levels, constant, mats, twiddle, wave,
        )
        small = full(HALF)
        results = pl.pallas_call(
            unpack_kernel,
            out_shape=(
                jax.ShapeDtypeStruct((HALF, TOK_DEV), BF16), full(HALF, TOK_DEV), small, small, full(8, 32, HALF),
                small, small, full(HALF, ROWS), small, full(HALF, ROWS), small, small, small, full(ROWS, 256),
                full(256), full(256, ROWS), small,
            ),
            in_specs=[vmem] * 6,
            out_specs=(vmem,) * 17,
            name="unpack",
        )(*packed, cotangent.T)
        turned = {0, 1, 4, 7, 9}
        return tuple(jnp.swapaxes(r, -1, -2) if i in turned else r for i, r in enumerate(results))

    return run


def solution(mesh):
    small = mesh.shape["chan"] == N_CHAN and mesh.shape["dp"] == 4
    return jax.shard_map(
        block_program() if small else shards,
        mesh=mesh,
        in_specs=(
            P("dp", "chan"),
            P("dp", "chan"),
            P("dp"),
            P("dp"),
            P("chan"),
            P("chan"),
            P(None, "chan", None),
            P("chan"),
            P("chan"),
            P("dp", "chan"),
            P("chan"),
            P("dp", "chan"),
            P("chan"),
            P("chan"),
            P("chan"),
            P("dp", "chan"),
            P("chan"),
            P("chan", "dp"),
            P("chan"),
        ),
        out_specs=(
            P("dp", "chan"),
            P("dp", "chan"),
            P("chan"),
            P("chan"),
            P(None, "chan", None),
            P("chan"),
            P("chan"),
            P("dp", "chan"),
            P("chan"),
            P("dp", "chan"),
            P("chan"),
            P("chan"),
            P("chan"),
            P("dp", "chan"),
            P("chan"),
            P("chan", "dp"),
            P("chan"),
        ),
        check_vma=False,
    )
```

```python
import math

import jax
import jax.numpy as jnp
import ml_dtypes
import numpy as np
from jax import lax
from jax.experimental import pallas as pl
from jax.experimental.pallas import tpu as pltpu
from jax.sharding import PartitionSpec as P

MODEL_WIDTH = 512
TOK_DEV = 1024


HIGHEST = lax.Precision.HIGHEST
EPSILON = 1e-05


def product(left, right):
    return jnp.dot(left, right, preferred_element_type=jnp.float32)


def product_nt(left, right):
    return lax.dot_general(
        left, right, (((1,), (1,)), ((), ())), preferred_element_type=jnp.float32
    )


def product_tn(left, right):
    return lax.dot_general(
        left, right, (((0,), (0,)), ((), ())), preferred_element_type=jnp.float32
    )


def gelu_slope(values):
    return (
        0.5 * (1.0 + lax.erf(values * 0.7071067811865476))
        + values * jnp.exp(-0.5 * values * values) * 0.3989422804014327
    )


def half_angles(length):
    angle = np.arange(length // 2 + 1, dtype=np.float64) * (math.pi / length)
    cosine, sine = np.cos(angle), np.sin(angle)
    cosine[-1] = 0.0
    return cosine.astype(np.float32), sine.astype(np.float32)


def inverse_tables(length):
    freq = np.arange(length // 2 + 1)
    turn = (freq[:, None] * np.arange(length)[None, :]) % length * (2.0 * math.pi / length)
    weight = np.where((freq == 0) | (freq == length // 2), 1.0, 2.0)[:, None] / length
    return (weight * np.cos(turn)).astype(np.float32), (weight * np.sin(turn)).astype(np.float32)


def high_einsum(form, left, right):
    return jnp.einsum(form, left, right, precision=HIGHEST)


def ssm_kernel(modes, log_dt):
    cos_h, sin_h = half_angles(TOK_DEV)
    index = jnp.arange(modes.shape[2], dtype=jnp.int32).astype(jnp.float32)
    lam_re = -0.5 * jnp.exp(modes[0])
    lam_im = math.pi * (index + modes[1])
    rank_re, rank_im, in_re, in_im, out_re, out_im = (modes[i] for i in range(2, 8))
    sigma = (2.0 * jnp.exp(-log_dt))[:, None]

    def points(values):
        return values.T[:, None, :]

    den_re = points(lam_re * lam_re + lam_im * lam_im) * (cos_h * cos_h)[:, None] - (
        sigma * sigma
    ).T * (sin_h * sin_h)[:, None]
    den_im = points(-2.0 * sigma * lam_re) * (sin_h * cos_h)[:, None]
    den_sq = den_re * den_re + den_im * den_im
    inv_re = den_re / den_sq
    inv_im = -den_im / den_sq
    sums = []
    for real, imag in (
        (out_re * in_re + out_im * in_im, out_re * in_im - out_im * in_re),
        (out_re * rank_re + out_im * rank_im, out_re * rank_im - out_im * rank_re),
        (rank_re * in_re + rank_im * in_im, rank_re * in_im - rank_im * in_re),
        (rank_re * rank_re + rank_im * rank_im, jnp.zeros_like(rank_re)),
    ):
        turned = points(real * lam_re + imag * lam_im)
        real = points(real)
        p_re, p_im = jnp.sum(real * inv_re, axis=0), jnp.sum(real * inv_im, axis=0)
        q_re, q_im = jnp.sum(turned * inv_re, axis=0), jnp.sum(turned * inv_im, axis=0)
        sine = sin_h[:, None] * sigma.T
        sums.append((-sine * p_im - cos_h[:, None] * q_re, sine * p_re - cos_h[:, None] * q_im))
    (cross_re, cross_im), (left_re, left_im), (right_re, right_im), (self_re, self_im) = sums
    twice = 2.0 * cos_h[:, None]
    loop_re, loop_im = 1.0 + twice * self_re, twice * self_im
    back_re, back_im = twice * right_re, twice * right_im
    loop_sq = loop_re * loop_re + loop_im * loop_im
    ratio_re = (back_re * loop_re + back_im * loop_im) / loop_sq
    ratio_im = (back_im * loop_re - back_re * loop_im) / loop_sq
    part_re = cross_re - (left_re * ratio_re - left_im * ratio_im)
    part_im = cross_im - (left_re * ratio_im + left_im * ratio_re)
    spec_re = 2.0 * (cos_h[:, None] * part_re - sin_h[:, None] * part_im)
    spec_im = 2.0 * (cos_h[:, None] * part_im + sin_h[:, None] * part_re)
    cos_tab, sin_tab = inverse_tables(TOK_DEV)
    return high_einsum("kl,kc->lc", cos_tab, spec_re) - high_einsum("kl,kc->lc", sin_tab, spec_im)


BLOCK = 128
BLOCKS = TOK_DEV // BLOCK
FIRST = 2 * BLOCKS
KEPT = FIRST // 2 + 1


def transform_tables():
    length = 2 * TOK_DEV
    turn = np.arange(KEPT)[:, None] * np.arange(BLOCK)[None, :] * (2.0 * math.pi / length)
    small = np.arange(BLOCK)[:, None] * np.arange(BLOCK)[None, :] % BLOCK * (2.0 * math.pi / BLOCK)
    spots = np.stack([np.arange(BLOCKS) + np.arange(BLOCKS) // (2 << b) * (2 << b) for b in range(3)])
    angle = spots[:, None, :] * np.arange(KEPT)[None, :, None] % FIRST * (2.0 * math.pi / FIRST)
    parts = (np.cos(turn), np.sin(turn), np.cos(small), np.sin(small), np.cos(angle), np.sin(angle))
    return [part.astype(np.float32) for part in parts]


def forward_transform(blocks, cos_a, sin_a):
    cos_t, sin_t, cos_s, sin_s, _, _ = transform_tables()
    step_re = high_einsum("ka,abc->kbc", cos_a, blocks)
    step_im = -high_einsum("ka,abc->kbc", sin_a, blocks)
    turned_re = step_re * cos_t[..., None] + step_im * sin_t[..., None]
    turned_im = step_im * cos_t[..., None] - step_re * sin_t[..., None]
    both = jnp.concatenate([turned_re, turned_im], axis=1)
    matrix = np.block([[cos_s, sin_s], [-sin_s, cos_s]])
    return high_einsum("pb,kbc->kpc", matrix, both)


def inverse_transform(spectrum, cos_a, sin_a):
    cos_t, sin_t, cos_s, sin_s, _, _ = transform_tables()
    matrix = np.block([[cos_s, -sin_s], [sin_s, cos_s]])
    both = high_einsum("bp,kpc->kbc", matrix, spectrum)
    step_re, step_im = both[:, :BLOCK], both[:, BLOCK:]
    turned_re = step_re * cos_t[..., None] - step_im * sin_t[..., None]
    turned_im = step_im * cos_t[..., None] + step_re * sin_t[..., None]
    weight = np.where(np.arange(KEPT) % (KEPT - 1) == 0, 1.0, 2.0).astype(np.float32) / (2 * TOK_DEV)
    return high_einsum("ka,kbc->abc", cos_a * weight[:, None], turned_re) - high_einsum(
        "ka,kbc->abc", sin_a * weight[:, None], turned_im
    )


def multiply(left, right):
    left_re, left_im = left[:, :BLOCK], left[:, BLOCK:]
    right_re, right_im = right[:, :BLOCK], right[:, BLOCK:]
    return jnp.concatenate(
        [left_re * right_re - left_im * right_im, left_re * right_im + left_im * right_re], axis=1
    )


def mixer(normed, kernel_taps, skip_gain, bucket, filled):
    _, _, _, _, cos_a, sin_a = transform_tables()
    cos_x, sin_x = jnp.asarray(cos_a)[bucket], jnp.asarray(sin_a)[bucket]
    item_blocks = 2 << bucket
    block_id = jnp.arange(BLOCKS, dtype=jnp.int32)[:, None, None]
    taps = jnp.where(block_id < item_blocks, kernel_taps.reshape(BLOCKS, BLOCK, -1), 0.0)
    signal = forward_transform(normed.reshape(BLOCKS, BLOCK, -1), cos_x, sin_x)
    answer = forward_transform(taps, cos_a[2], sin_a[2])
    result = inverse_transform(multiply(signal, answer), cos_x, sin_x)
    result = jnp.where(block_id < filled * item_blocks, result, 0.0)
    return result.reshape(normed.shape) + skip_gain * normed


def shards(
    tokens,
    cotangent,
    group_bucket,
    group_items,
    first_norm_gain,
    first_norm_bias,
    modes,
    log_dt,
    d_skip,
    w_a,
    b_a,
    w_b,
    b_b,
    second_norm_gain,
    second_norm_bias,
    w_up,
    b_up,
    w_down,
    b_down,
):
    input_tokens = tokens.astype(jnp.float32)
    sums_in = lax.psum(
        (jnp.sum(input_tokens, axis=1), jnp.sum(input_tokens * input_tokens, axis=1)), "chan"
    )
    input_average = sums_in[0][:, None] / MODEL_WIDTH
    input_inverse_deviation = lax.rsqrt(
        sums_in[1][:, None] / MODEL_WIDTH - input_average * input_average + EPSILON
    )
    input_standardized = (input_tokens - input_average) * input_inverse_deviation
    input_normalized = input_standardized * first_norm_gain + first_norm_bias
    level = group_bucket[0]
    filled = group_items[0]
    kernel_taps, kernel_back = jax.vjp(ssm_kernel, modes, log_dt)

    def local_mix(values, taps_now, skip_gain):
        return mixer(values, taps_now, skip_gain, level, filled)

    mixed, mix_back = jax.vjp(local_mix, input_normalized, kernel_taps, d_skip)
    acts_low = jax.nn.gelu(mixed, approximate=False).astype(jnp.bfloat16)
    wa_full, wb_full, up_full, down_full = (
        lax.all_gather(w_a.astype(jnp.bfloat16), "dp", axis=0, tiled=True),
        lax.all_gather(w_b.astype(jnp.bfloat16), "dp", axis=0, tiled=True),
        lax.all_gather(w_up.astype(jnp.bfloat16), "dp", axis=0, tiled=True),
        lax.all_gather(w_down.astype(jnp.bfloat16), "dp", axis=1, tiled=True),
    )
    acts_full = lax.all_gather(acts_low, "chan", axis=1, tiled=True)
    gate_a = product(acts_full, wa_full) + b_a
    gate_b = product(acts_full, wb_full) + b_b
    gate_sig = jax.nn.sigmoid(gate_b)
    residual_stream = input_tokens + gate_a * gate_sig
    sums_mid = lax.psum(
        (jnp.sum(residual_stream, axis=1), jnp.sum(residual_stream * residual_stream, axis=1)),
        "chan",
    )
    middle_average = sums_mid[0][:, None] / MODEL_WIDTH
    middle_inverse_deviation = lax.rsqrt(
        sums_mid[1][:, None] / MODEL_WIDTH - middle_average * middle_average + EPSILON
    )
    middle_standardized = (residual_stream - middle_average) * middle_inverse_deviation
    middle_reduced = (middle_standardized * second_norm_gain + second_norm_bias).astype(
        jnp.bfloat16
    )
    mid_full = lax.all_gather(middle_reduced, "chan", axis=1, tiled=True)
    pre_act = product(mid_full, up_full) + b_up
    hidden_low = jax.nn.gelu(pre_act, approximate=False).astype(jnp.bfloat16)
    branch = (
        lax.psum_scatter(product(hidden_low, down_full), "chan", scatter_dimension=1, tiled=True)
        + b_down
    )
    output = (residual_stream + branch).astype(jnp.bfloat16)
    grad_f = cotangent.astype(jnp.bfloat16)
    grad_b_down = jnp.sum(grad_f.astype(jnp.float32), axis=0)
    grad_f_full = lax.all_gather(grad_f, "chan", axis=1, tiled=True)
    grad_w_down = product_tn(hidden_low, grad_f_full)
    grad_pre = (product_nt(grad_f_full, down_full) * gelu_slope(pre_act)).astype(jnp.bfloat16)
    grad_b_up = jnp.sum(grad_pre.astype(jnp.float32), axis=0)
    grad_w_up = product_tn(mid_full, grad_pre)
    middle_gradient = lax.psum_scatter(
        product_nt(grad_pre, up_full), "chan", scatter_dimension=1, tiled=True
    )
    second_norm_gain_gradient = jnp.sum(middle_gradient * middle_standardized, axis=0)
    grad_ln2_bias = jnp.sum(middle_gradient, axis=0)
    middle_rescaled = middle_gradient * second_norm_gain
    middle_backward = lax.psum(
        (jnp.sum(middle_rescaled, axis=1), jnp.sum(middle_rescaled * middle_standardized, axis=1)),
        "chan",
    )
    grad_resid = cotangent + middle_inverse_deviation * (
        middle_rescaled
        - middle_backward[0][:, None] / MODEL_WIDTH
        - middle_standardized * middle_backward[1][:, None] / MODEL_WIDTH
    )
    grad_a = (grad_resid * gate_sig).astype(jnp.bfloat16)
    grad_b = (grad_resid * gate_a * gate_sig * (1.0 - gate_sig)).astype(jnp.bfloat16)
    grad_b_a = jnp.sum(grad_a.astype(jnp.float32), axis=0)
    grad_b_b = jnp.sum(grad_b.astype(jnp.float32), axis=0)
    grad_w_a = product_tn(acts_full, grad_a)
    grad_w_b = product_tn(acts_full, grad_b)
    grad_acts = lax.psum_scatter(
        product_nt(grad_a, wa_full) + product_nt(grad_b, wb_full),
        "chan",
        scatter_dimension=1,
        tiled=True,
    )
    grad_mixed = grad_acts * gelu_slope(mixed)
    normalized_gradient, grad_kernel, grad_skip = mix_back(grad_mixed)
    grad_modes, grad_log_dt = kernel_back(grad_kernel)
    first_norm_gain_gradient = jnp.sum(normalized_gradient * input_standardized, axis=0)
    grad_ln1_bias = jnp.sum(normalized_gradient, axis=0)
    input_rescaled = normalized_gradient * first_norm_gain
    input_backward = lax.psum(
        (jnp.sum(input_rescaled, axis=1), jnp.sum(input_rescaled * input_standardized, axis=1)),
        "chan",
    )
    grad_tokens = grad_resid + input_inverse_deviation * (
        input_rescaled
        - input_backward[0][:, None] / MODEL_WIDTH
        - input_standardized * input_backward[1][:, None] / MODEL_WIDTH
    )
    grad_w_a, grad_w_b, grad_w_up, grad_w_down = (
        lax.psum_scatter(grad_w_a, "dp", scatter_dimension=0, tiled=True),
        lax.psum_scatter(grad_w_b, "dp", scatter_dimension=0, tiled=True),
        lax.psum_scatter(grad_w_up, "dp", scatter_dimension=0, tiled=True),
        lax.psum_scatter(grad_w_down, "dp", scatter_dimension=1, tiled=True),
    )
    (
        first_norm_gain_gradient,
        grad_ln1_bias,
        grad_modes,
        grad_log_dt,
        grad_skip,
        grad_b_a,
        grad_b_b,
        second_norm_gain_gradient,
        grad_ln2_bias,
        grad_b_up,
        grad_b_down,
    ) = lax.psum(
        (
            first_norm_gain_gradient,
            grad_ln1_bias,
            grad_modes,
            grad_log_dt,
            grad_skip,
            grad_b_a,
            grad_b_b,
            second_norm_gain_gradient,
            grad_ln2_bias,
            grad_b_up,
            grad_b_down,
        ),
        "dp",
    )
    return (
        output,
        grad_tokens,
        first_norm_gain_gradient,
        grad_ln1_bias,
        grad_modes,
        grad_log_dt,
        grad_skip,
        grad_w_a,
        grad_b_a,
        grad_w_b,
        grad_b_b,
        second_norm_gain_gradient,
        grad_ln2_bias,
        grad_w_up,
        grad_b_up,
        grad_w_down,
        grad_b_down,
    )


LANES = 128
HALF = 64
PAIRS = 4
ROWS = 128
N_CHAN = 8
WIDE = 640
MESH = pl.DeviceIdType.MESH
F32 = jnp.float32
BF16 = jnp.bfloat16


def split_two(matrix):
    high = matrix.astype(ml_dtypes.bfloat16)
    low = (matrix - high.astype(np.float64)).astype(ml_dtypes.bfloat16)
    return np.concatenate([high, low], axis=1)


def lane_rows(values_low, values_high):
    return np.repeat(np.stack([values_low, values_high], -1), HALF, axis=-1)


def mixer_tables():
    line = np.arange(ROWS)
    small = np.outer(line, line) % ROWS * (2.0 * math.pi / ROWS)
    cos_s, sin_s = np.cos(small), np.sin(small)
    forward = np.block([[cos_s, sin_s], [-sin_s, cos_s]])
    real = np.zeros((2 * ROWS, 2 * ROWS))
    for row in range(HALF):
        weight = 1.0 if row == 0 else 2.0
        turn = 2.0 * math.pi / ROWS * row * line
        real[:ROWS, row] = weight * np.cos(turn)
        real[:ROWS, ROWS + row] = -weight * np.sin(turn)
        turn = 2.0 * math.pi / TOK_DEV * (4 + 8 * row) * line
        real[ROWS:, HALF + row] = 2.0 * np.cos(turn)
        real[ROWS:, ROWS + HALF + row] = -2.0 * np.sin(turn)
    mats = np.stack([split_two(m) for m in (forward, forward.T, real, real.T)])

    twiddle = []
    for pair in range(5):
        turn = np.stack([line * k * (math.pi / TOK_DEV) for k in (2 * pair, 2 * pair + 1)])
        twiddle += [lane_rows(np.cos(turn[0]), np.cos(turn[1])), lane_rows(np.sin(turn[0]), np.sin(turn[1]))]
    for first, second in ((1, 2), (3, 0)):
        turn = np.stack([line * k * (2.0 * math.pi / TOK_DEV) for k in (first, second)])
        twiddle += [lane_rows(np.cos(turn[0]), np.cos(turn[1])), lane_rows(np.sin(turn[0]), np.sin(turn[1]))]

    def forward_rows(coef, pairs):
        out = []
        for low, high in pairs:
            for part in range(2):
                for j in range(PAIRS):
                    out.append(lane_rows(coef(2 * j, low, part), coef(2 * j + 1, high, part)))
                for j in range(PAIRS):
                    out.append(lane_rows(coef(2 * j, high, part), coef(2 * j + 1, low, part)))
        return np.stack(out)

    def inverse_rows(coef, pairs):
        out = []
        for low, high in pairs:
            for part in range(2):
                for j in range(PAIRS):
                    out.append(lane_rows(coef(2 * j, low, part), coef(2 * j + 1, high, part)))
                for j in range(PAIRS):
                    out.append(lane_rows(coef(2 * j + 1, low, part), coef(2 * j, high, part)))
        return np.stack(out)

    levels = []
    pairs = [(2 * p, 2 * p + 1) for p in range(5)]
    for level in range(3):
        item = 2 << level

        def angle(block, k):
            return 2.0 * math.pi / 16 * ((block + block // item * item) * k % 16)

        def fwd(block, k, part):
            if k > 8:
                return np.zeros(())
            return np.cos(angle(block, k)) if part == 0 else -np.sin(angle(block, k))

        def inv(block, k, part):
            weight = (1.0 if k in (0, 8) else 2.0) / (2 * TOK_DEV)
            return weight * fwd(block, k, part)

        levels.append(np.concatenate([forward_rows(fwd, pairs), inverse_rows(inv, pairs)]))

    def taps(block, k, part):
        if k == 0:
            return np.asarray((1.0 if part == 0 else (-1.0) ** block) / TOK_DEV)
        turn = 2.0 * math.pi / 8 * (block * k % 8)
        return np.asarray((np.cos(turn) if part == 0 else -np.sin(turn)) * 2.0 / TOK_DEV)

    tap_pairs = [(1, 2), (3, 0)]
    taps_back = forward_rows(taps, tap_pairs)
    taps_rows = inverse_rows(taps, tap_pairs)
    freq_even = np.where(line < HALF, 8 * line, 4 + 8 * (line - HALF))
    half_angle = np.stack(
        [lane_rows(1 + 8 * line, 2 + 8 * line), lane_rows(3 + 8 * line, freq_even)]
    ) * (math.pi / TOK_DEV)
    wave = np.stack([np.cos(half_angle), np.sin(half_angle)])
    return (
        mats,
        np.stack(twiddle).astype(np.float32),
        np.stack(levels).astype(np.float32),
        np.concatenate([levels[2], taps_rows, taps_back]).astype(np.float32),
        wave.astype(np.float32),
    )


def low_lanes(rows):
    return lax.broadcasted_iota(jnp.int32, (rows, LANES), 1) < HALF


def turn_half(values):
    return pltpu.roll(values, HALF, 1)


def split_pair(values):
    upper, lower = values[:HALF], values[HALF:]
    mask = low_lanes(HALF)
    return jnp.where(mask, upper, turn_half(lower)), jnp.where(mask, turn_half(upper), lower)


def join_pair(first, second):
    mask = low_lanes(HALF)
    return jnp.concatenate(
        [jnp.where(mask, first, turn_half(second)), jnp.where(mask, turn_half(first), second)], axis=0
    )


def interleave(first, second):
    mask = low_lanes(first.shape[0])
    return jnp.where(mask, first, turn_half(second)), jnp.where(mask, turn_half(first), second)


def fold(values):
    return values + turn_half(values)


def normal_parts(values):
    cumulative = 0.5 * (1.0 + lax.erf(values * 0.7071067811865476))
    density = jnp.exp(-0.5 * values * values) * 0.3989422804014327
    return cumulative, density


def column_sum(values):
    return jnp.sum(values, axis=0, keepdims=True)


def dot_nt(left, right):
    return lax.dot_general(left, right, (((1,), (1,)), ((), ())), preferred_element_type=F32)


def dot_nn(left, right):
    return jnp.dot(left, right, preferred_element_type=F32)


def store_split(ref, row, lane, values):
    high = values.astype(BF16)
    place = (pl.ds(row, values.shape[0]), pl.ds(lane, values.shape[1]))
    ref[(0,) + place] = high
    ref[(1,) + place] = (values - high.astype(F32)).astype(BF16)


def split_product(mat_ref, which, rhs_ref, lane, width):
    high = mat_ref[which, :, 0:256]
    low = mat_ref[which, :, 256:512]
    rhs_high = rhs_ref[0, :, lane : lane + width]
    return dot_nn(high, rhs_high) + dot_nn(high, rhs_ref[1, :, lane : lane + width]) + dot_nn(low, rhs_high)


CHUNK = 32


def over_chunks(body, size=CHUNK, first=0, rows=ROWS):
    def step(index, carry):
        body(pl.multiple_of(first + index * size, size))
        return carry

    lax.fori_loop(0, rows // size, step, 0)


def spread_pairs(src, coef_ref, base, twiddle_ref, twiddle_base, pairs, rhs_ref):
    def body(row):
        rows = pl.ds(row, CHUNK)
        blocks = [src(j, rows) for j in range(PAIRS)]
        for pair in range(pairs):
            parts = []
            for part in range(2):
                at = base + (pair * 2 + part) * 8
                straight = sum(blocks[j] * coef_ref[at + j : at + j + 1, :] for j in range(PAIRS))
                crossed = sum(blocks[j] * coef_ref[at + 4 + j : at + 5 + j, :] for j in range(PAIRS))
                parts.append(straight + turn_half(crossed))
            cosine = twiddle_ref[twiddle_base + 2 * pair, rows, :]
            sine = twiddle_ref[twiddle_base + 2 * pair + 1, rows, :]
            store_split(rhs_ref, row, pair * LANES, parts[0] * cosine + parts[1] * sine)
            store_split(rhs_ref, row + ROWS, pair * LANES, parts[1] * cosine - parts[0] * sine)

    over_chunks(body)


def gather_pairs(values_ref, coef_ref, base, twiddle_ref, twiddle_base, pairs, store):
    def body(row):
        rows = pl.ds(row, CHUNK)
        straight, crossed = [0.0] * PAIRS, [0.0] * PAIRS
        for pair in range(pairs):
            lanes = slice(pair * LANES, (pair + 1) * LANES)
            real, imag = values_ref[rows, lanes], values_ref[pl.ds(row + ROWS, CHUNK), lanes]
            cosine = twiddle_ref[twiddle_base + 2 * pair, rows, :]
            sine = twiddle_ref[twiddle_base + 2 * pair + 1, rows, :]
            for part, value in enumerate((real * cosine - imag * sine, imag * cosine + real * sine)):
                at = base + (pair * 2 + part) * 8
                for j in range(PAIRS):
                    straight[j] = straight[j] + value * coef_ref[at + j : at + j + 1, :]
                    crossed[j] = crossed[j] + value * coef_ref[at + 4 + j : at + 5 + j, :]
        for j in range(PAIRS):
            store(j, rows, straight[j] + turn_half(crossed[j]))

    over_chunks(body)


GROUPS = ((0, 256), (256, 256), (512, 128))


def transform_into(dst_ref, mat_ref, which, rhs_ref, groups=GROUPS):
    for lane, width in groups:
        dst_ref[:, lane : lane + width] = split_product(mat_ref, which, rhs_ref, lane, width)


def multiply_spectra(left_ref, right_ref, rhs_ref, conjugate):
    def body(row):
        top, bottom = pl.ds(row, CHUNK), pl.ds(row + ROWS, CHUNK)
        for pair in range(5):
            lanes = slice(pair * LANES, (pair + 1) * LANES)
            a_re, a_im = left_ref[top, lanes], left_ref[bottom, lanes]
            b_re, b_im = right_ref[top, lanes], right_ref[bottom, lanes]
            if conjugate:
                out_re, out_im = a_re * b_re + a_im * b_im, a_re * b_im - a_im * b_re
            else:
                out_re, out_im = a_re * b_re - a_im * b_im, a_re * b_im + a_im * b_re
            store_split(rhs_ref, row, pair * LANES, out_re)
            store_split(rhs_ref, row + ROWS, pair * LANES, out_im)

    over_chunks(body)


def pair_terms(modes_ref):
    rank_re, rank_im, in_re, in_im, out_re, out_im = (modes_ref[i] for i in range(2, 8))
    return (
        (out_re * in_re + out_im * in_im, out_re * in_im - out_im * in_re),
        (out_re * rank_re + out_im * rank_im, out_re * rank_im - out_im * rank_re),
        (rank_re * in_re + rank_im * in_im, rank_re * in_im - rank_im * in_re),
        (rank_re * rank_re + rank_im * rank_im, None),
    )


def mode_values(modes_ref):
    index = lax.broadcasted_iota(jnp.int32, modes_ref.shape[1:], 0).astype(F32)
    return -0.5 * jnp.exp(modes_ref[0]), math.pi * (index + modes_ref[1])


POINT_ROWS = 16


def resolvent(coef_ref, n, square_cos, cos_sin, scaled):
    den_re = coef_ref[8, pl.ds(n, 1), :] * square_cos - scaled
    den_im = coef_ref[9, pl.ds(n, 1), :] * cos_sin
    inverse = 1.0 / (den_re * den_re + den_im * den_im)
    return den_re * inverse, -(den_im * inverse)


def complex_multiply(a_re, a_im, b_re, b_im):
    return a_re * b_re - a_im * b_im, a_re * b_im + a_im * b_re


def conj_multiply(a_re, a_im, b_re, b_im):
    return a_re * b_re + a_im * b_im, a_re * b_im - a_im * b_re


def combine(sums, sigma, cosine, sine):
    terms = []
    for p_re, p_im, q_re, q_im in (sums[4 * q : 4 * q + 4] for q in range(4)):
        swing = sigma * sine
        terms.append((-swing * p_im - cosine * q_re, swing * p_re - cosine * q_im))
    twice = 2.0 * cosine
    loop_re, loop_im = 1.0 + twice * terms[3][0], twice * terms[3][1]
    scale = 1.0 / (loop_re * loop_re + loop_im * loop_im)
    inv = (loop_re * scale, -(loop_im * scale))
    ratio = complex_multiply(twice * terms[2][0], twice * terms[2][1], *inv)
    return terms, inv, ratio


QUARTER = 32


def cauchy_coefficients(modes_ref, sigma, coef_ref):
    lam_re, lam_im = mode_values(modes_ref)
    for q, (real, imag) in enumerate(pair_terms(modes_ref)):
        coef_ref[q] = real
        coef_ref[4 + q] = real * lam_re if imag is None else real * lam_re + imag * lam_im
    coef_ref[8] = lam_re * lam_re + lam_im * lam_im
    coef_ref[9] = -2.0 * sigma * lam_re


def wave_rows(wave_ref, pair, base, row):
    rows = pl.ds(pl.multiple_of(base + row, POINT_ROWS), POINT_ROWS)
    return wave_ref[0, pair, rows, :], wave_ref[1, pair, rows, :]


def cauchy_forward(sigma, coef_ref, wave_ref, base, sums_ref, spec_ref, middle):
    sigma_sq = sigma * sigma
    for index in range(4):
        pair, row = index // 2, index % 2 * POINT_ROWS
        rows = slice(row, row + POINT_ROWS)
        lanes = slice(pair * LANES, (pair + 1) * LANES)
        cosine, sine = wave_rows(wave_ref, pair, base, row)
        square_cos, cos_sin, scaled = cosine * cosine, cosine * sine, sigma_sq * (sine * sine)

        def add_mode(n, sums):
            sums = list(sums)
            for k in range(4):
                at = n * 4 + k
                inv_re, inv_im = resolvent(coef_ref, at, square_cos, cos_sin, scaled)
                for q in range(4):
                    plain = coef_ref[q, pl.ds(at, 1), :]
                    turned = coef_ref[4 + q, pl.ds(at, 1), :]
                    sums[4 * q] = sums[4 * q] + plain * inv_re
                    sums[4 * q + 1] = sums[4 * q + 1] + plain * inv_im
                    sums[4 * q + 2] = sums[4 * q + 2] + turned * inv_re
                    sums[4 * q + 3] = sums[4 * q + 3] + turned * inv_im
            return tuple(sums)

        zero = jnp.zeros((POINT_ROWS, LANES), F32)
        sums = lax.fori_loop(0, 8, add_mode, (zero,) * 16)
        for i in range(16):
            sums_ref[pair, i, rows, :] = sums[i]
        terms, _, ratio = combine(sums, sigma, cosine, sine)
        cut_re, cut_im = complex_multiply(*terms[1], *ratio)
        part_re, part_im = terms[0][0] - cut_re, terms[0][1] - cut_im
        spec_re, spec_im = complex_multiply(2.0 * cosine, 2.0 * sine, part_re, part_im)
        spec_ref[rows, lanes] = spec_re
        spec_ref[row + QUARTER : row + QUARTER + POINT_ROWS, lanes] = spec_im
        middle(index)


def cauchy_backward(modes_ref, sigma, nyquist_grad, step, coef_ref, wave_ref, base, sums_ref, spec_ref, grad_ref, back_ref, middle):
    zero = jnp.zeros((POINT_ROWS, LANES), F32)
    sigma_sum = zero
    places = [(pair, row) for pair in range(2) for row in range(0, QUARTER, POINT_ROWS)]
    for pair, row in places:
        rows = slice(row, row + POINT_ROWS)
        lanes = slice(pair * LANES, (pair + 1) * LANES)
        cosine, sine = wave_rows(wave_ref, pair, base, row)
        sums = [sums_ref[pair, i, rows, :] for i in range(16)]
        terms, inv, ratio = combine(sums, sigma, cosine, sine)
        spec_re, spec_im = spec_ref[rows, lanes], spec_ref[row + QUARTER : row + QUARTER + POINT_ROWS, lanes]
        part = conj_multiply(2.0 * cosine, 2.0 * sine, spec_re, spec_im)
        left = conj_multiply(*ratio, *part)
        ratio_grad = conj_multiply(*terms[1], *part)
        back = conj_multiply(*inv, -ratio_grad[0], -ratio_grad[1])
        twice = 2.0 * cosine
        loop = conj_multiply(*ratio, *back)
        grads = (
            part,
            (-left[0], -left[1]),
            (twice * back[0], twice * back[1]),
            (-twice * loop[0], -twice * loop[1]),
        )
        swing = sigma * sine
        for q, (g_re, g_im) in enumerate(grads):
            grad_ref[pair, 4 * q, rows, :] = swing * g_im
            grad_ref[pair, 4 * q + 1, rows, :] = -swing * g_re
            grad_ref[pair, 4 * q + 2, rows, :] = -cosine * g_re
            grad_ref[pair, 4 * q + 3, rows, :] = -cosine * g_im
            sigma_sum = sigma_sum + sine * (g_im * sums[4 * q] - g_re * sums[4 * q + 1])
    sigma_sq = sigma * sigma

    def mode(n, square_sum):
        plain = [coef_ref[q, pl.ds(n, 1), :] for q in range(4)]
        turned = [coef_ref[4 + q, pl.ds(n, 1), :] for q in range(4)]
        sums = [0.0] * 10
        for pair, row in places:
            rows = slice(row, row + POINT_ROWS)
            cosine, sine = wave_rows(wave_ref, pair, base, row)
            square_cos, cos_sin, square_sin = cosine * cosine, cosine * sine, sine * sine
            inv_re, inv_im = resolvent(coef_ref, n, square_cos, cos_sin, sigma_sq * square_sin)
            grad_re, grad_im = 0.0, 0.0
            for q in range(4):
                p_re, p_im = grad_ref[pair, 4 * q, rows, :], grad_ref[pair, 4 * q + 1, rows, :]
                q_re, q_im = grad_ref[pair, 4 * q + 2, rows, :], grad_ref[pair, 4 * q + 3, rows, :]
                grad_re = grad_re + (plain[q] * p_re + turned[q] * q_re)
                grad_im = grad_im + (plain[q] * p_im + turned[q] * q_im)
                sums[q] = sums[q] + (p_re * inv_re + p_im * inv_im)
                sums[4 + q] = sums[4 + q] + (q_re * inv_re + q_im * inv_im)
            square_re = inv_re * inv_re - inv_im * inv_im
            square_im = 2.0 * inv_re * inv_im
            den_re, den_im = conj_multiply(square_re, square_im, grad_re, grad_im)
            sums[8] = sums[8] - den_re * square_cos
            sums[9] = sums[9] - den_im * cos_sin
            square_sum = square_sum + den_re * square_sin
        for i in range(10):
            back_ref[i, pl.ds(n, 1), :] = column_sum(sums[i])
        return square_sum

    square_sum = zero
    for part in range(4):
        square_sum = lax.fori_loop(part * 8, part * 8 + 8, mode, square_sum)
        middle(part)
    plain_grad = [fold(back_ref[q]) for q in range(4)]
    turned_grad = [fold(back_ref[4 + q]) for q in range(4)]
    abs_grad, skew_grad = fold(back_ref[8]), fold(back_ref[9])
    lam_re, lam_im = mode_values(modes_ref)
    plain_grad[0] = plain_grad[0] + step * nyquist_grad
    rank_re, rank_im, in_re, in_im, out_re, out_im = (modes_ref[i] for i in range(2, 8))
    lam_re_grad = 2.0 * lam_re * abs_grad - 2.0 * sigma * skew_grad
    lam_im_grad = 2.0 * lam_im * abs_grad
    real_grad, imag_grad = [], []
    terms = pair_terms(modes_ref)
    for q, (real, imag) in enumerate(terms):
        lam_re_grad = lam_re_grad + turned_grad[q] * real
        if imag is not None:
            lam_im_grad = lam_im_grad + turned_grad[q] * imag
        real_grad.append(plain_grad[q] + turned_grad[q] * lam_re)
        imag_grad.append(turned_grad[q] * lam_im)
    r0, r1, r2, r3 = real_grad
    i0, i1, i2, _ = imag_grad
    grads = (
        lam_re_grad * lam_re,
        math.pi * lam_im_grad,
        r1 * out_re - i1 * out_im + r2 * in_re + i2 * in_im + 2.0 * r3 * rank_re,
        r1 * out_im + i1 * out_re + r2 * in_im - i2 * in_re + 2.0 * r3 * rank_im,
        r0 * out_re - i0 * out_im + r2 * rank_re - i2 * rank_im,
        r0 * out_im + i0 * out_re + r2 * rank_im + i2 * rank_re,
        r0 * in_re + i0 * in_im + r1 * rank_re + i1 * rank_im,
        r0 * in_im - i0 * in_re + r1 * rank_im - i1 * rank_re,
    )
    sigma_grad = (
        fold(column_sum(sigma_sum) + 2.0 * sigma * column_sum(square_sum))
        - 2.0 * column_sum(skew_grad * lam_re)
    )
    nyquist = step * column_sum(terms[0][0])
    return grads, nyquist * nyquist_grad - sigma * sigma_grad


def ring_place(chan):
    z, y = chan // 2, chan % 2
    return z + y * (7 - 2 * z)


def ring_chan(place):
    back = place // 4
    z = place * (1 - back) + (7 - place) * back
    return 2 * z + back


TURNS = (1, -1)


def ring_items():
    out = []
    for step in range(1, 5):
        for turn in range(2):
            for block in range(2):
                if step < 4 or block == turn:
                    out.append((turn, step, block))
    return out


def item_slot(turn, step, block):
    return (turn * 4 + step - 1) * 2 + block


def block_kernel(
    bucket_ref, items_ref, tokens_ref, cotangent_ref, gain1_ref, bias1_ref, raw_modes_ref, log_dt_ref, skip_ref,
    wa_ref, ba_ref, wb_ref, bb_ref, gain2_ref, bias2_ref, up_ref, bup_ref, down_ref, bdown_ref,
    levels_ref, coefc_ref, mat_ref, tw_ref, wave_ref,
    out_ref, dtok_ref, gw_ref, gm_ref, gv_ref,
    tok_ref, aux_ref, coefl_ref, modes_ref,
    w_ref, grad_ref, sib_ref, ring_ref, part_ref,
    in_send, in_recv, head_send, head_recv, acts_send, acts_recv, back_send, back_recv, late_send, late_recv,
    sum_send, sum_recv, tail_send, tail_recv, dp_send, dp_recv, spec_send, spec_recv, sgrad_send, sgrad_recv,
    hat_ref, norm_ref, slope_ref, conv_ref, rhs_ref, freq_ref, sig_ref, ans_ref, taps_ref,
    mcoef_ref, sums_ref, pgrad_ref, mback_ref, sgrad_ref, taps_freq_ref,
    gate_ref, swish_ref, res_ref, hat2_ref, low_ref, branch_ref, back2_ref, gab_ref, hid_ref, gpre_ref,
    ring_ss, ring_rs, sib_ss, sib_rs, x_ss, x_rs, rring_ss, rring_rs, rsib_ss, rsib_rs, rx_ss, rx_rs, a2a_ss, a2a_rs, dp_ss, dp_rs, spec_ss, spec_rs,
):
    dp, chan = lax.axis_index("dp"), lax.axis_index("chan")
    core = dp % 2
    sibling = dp + 1 - 2 * core
    across = (dp + 2) % 4
    place = ring_place(chan)
    nexts = [ring_chan((place + 1) % 8), ring_chan((place + 7) % 8)]

    def chan_at(offset):
        return ring_chan((place + offset + 8) % 8)

    barrier = pltpu.get_barrier_semaphore()
    for r in range(1, N_CHAN):
        pl.semaphore_signal(barrier, inc=1, device_id={"chan": (chan + r) % N_CHAN}, device_id_type=MESH)
    for r in range(1, 4):
        pl.semaphore_signal(barrier, inc=1, device_id={"dp": (dp + r) % 4}, device_id_type=MESH)
    pl.semaphore_wait(barrier, N_CHAN - 1 + 3)

    pending = []

    def remote(src, dst, send_sem, recv_sem, **device):
        return pltpu.make_async_remote_copy(
            src_ref=src, dst_ref=dst, send_sem=send_sem, recv_sem=recv_sem, device_id=device, device_id_type=MESH
        )

    def send(*args, **device):
        copy = remote(*args, **device)
        copy.start()
        pending.append(copy)

    def exchange(which, source, recv_ref):
        def copy(r):
            peer = (chan + r) % N_CHAN
            return remote(
                source(peer), recv_ref.at[chan], a2a_ss.at[which, r - 1], a2a_rs.at[which, r - 1], chan=peer
            )

        def start():
            for r in range(1, N_CHAN):
                copy(r).start()

        def wait():
            for r in range(1, N_CHAN):
                copy(r).wait_recv()

        def finish():
            for r in range(1, N_CHAN):
                copy(r).wait_send()

        return start, wait, finish

    def row_of(group):
        return pl.multiple_of(group * ROWS, ROWS)

    def weight(chan_id, group):
        return w_ref.at[chan_id, pl.ds(row_of(group), ROWS), :]

    mine = (dp, across)
    theirs = (sibling, (sibling + 2) % 4)

    def origin(turn, step):
        return chan_at(-TURNS[turn] * step)

    def ring_copy(turn, step, block):
        slot = item_slot(turn, step, block)
        ref = weight(origin(turn, step - 1), mine[block])
        return remote(ref, ref, ring_ss.at[slot], ring_rs.at[slot], chan=nexts[turn])

    def sib_copy(chan_id, block, slot):
        ref = weight(chan_id, mine[block])
        return remote(ref, ref, sib_ss.at[slot], sib_rs.at[slot], dp=sibling)

    def ring_got(turn, step, block):
        slot = item_slot(turn, step, block)
        ref = weight(origin(turn, step), mine[block])
        remote(ref, ref, ring_ss.at[slot], ring_rs.at[slot], chan=nexts[turn]).wait_recv()

    def gather_start():
        rows = pl.ds(row_of(dp), ROWS)
        w_ref[chan, rows, 0:128] = jnp.concatenate([wa_ref[...], wb_ref[...]], axis=0).T.astype(BF16)
        w_ref[chan, rows, 128:384] = up_ref[...].astype(BF16)
        w_ref[chan, rows, 384:640] = down_ref[...].T.astype(BF16)
        x_ref = weight(chan, dp)
        send(x_ref, x_ref, x_ss, x_rs, dp=across)
        for turn in range(2):
            copy = ring_copy(turn, 1, 0)
            copy.start()
            pending.append(copy)
        copy = sib_copy(chan, 0, 16)
        copy.start()
        pending.append(copy)

    def gather_across():
        x_ref = weight(chan, across)
        remote(x_ref, x_ref, x_ss, x_rs, dp=across).wait_recv()
        for turn in range(2):
            copy = ring_copy(turn, 1, 1)
            copy.start()
            pending.append(copy)
        copy = sib_copy(chan, 1, 17)
        copy.start()
        pending.append(copy)

    items = ring_items()

    def gather_step(step, which):
        for turn, at, block in items:
            if at != step or block != which:
                continue
            ring_got(turn, step, block)
            if (turn, step + 1, block) in items:
                copy = ring_copy(turn, step + 1, block)
                copy.start()
                pending.append(copy)
            copy = sib_copy(origin(turn, step), block, item_slot(turn, step, block))
            copy.start()
            pending.append(copy)

    def gather_finish():
        def got(chan_id, block, slot):
            ref = weight(chan_id, theirs[block])
            remote(ref, ref, sib_ss.at[slot], sib_rs.at[slot], dp=sibling).wait_recv()

        got(chan, 0, 16)
        got(chan, 1, 17)
        for turn, step, block in items:
            got(origin(turn, step), block, item_slot(turn, step, block))

    def beside(ref, j):
        start = 2 * j * ROWS
        return jnp.concatenate(
            [ref[:, start : start + ROWS].astype(F32), ref[:, start + ROWS : start + 2 * ROWS].astype(F32)], axis=0
        ).T

    for j in range(PAIRS):
        packed = beside(tokens_ref, j)
        tok_ref[j * ROWS : (j + 1) * ROWS, :] = packed.astype(BF16)
        for first, values in ((0, packed), (HALF, beside(cotangent_ref, j))):
            low, high = split_pair(values)
            in_send[2 * j, first : first + HALF, :] = low.astype(BF16)
            in_send[2 * j + 1, first : first + HALF, :] = high.astype(BF16)
    in_recv[chan] = in_send[chan]

    lane_id = lax.broadcasted_iota(jnp.int32, (8, LANES), 1)
    row_id = lax.broadcasted_iota(jnp.int32, (8, LANES), 0)
    halves = jnp.where((lane_id >= HALF) == (row_id == 1), 1.0, 0.0) * jnp.where(row_id < 2, 1.0, 0.0)
    halves = halves.astype(BF16)

    def token_sums(parts):
        total = 0.0
        for part in parts:
            total = total + dot_nt(halves, part)
        return [total[h : h + 1, j * ROWS : (j + 1) * ROWS] for h in range(2) for j in range(PAIRS)]

    def split(values):
        high = values.astype(BF16)
        return high, (values - high.astype(F32)).astype(BF16)

    tokens = tok_ref[...]
    wide_tokens = tokens.astype(F32)
    for i, sums in enumerate(token_sums([tokens]) + token_sums(split(wide_tokens * wide_tokens))):
        head_send[i : i + 1, :] = sums

    def row(*refs):
        return jnp.concatenate([ref[...].reshape(1, HALF) for ref in refs], axis=1)

    bup = bup_ref[...].reshape(1, 2 * LANES)
    head_send[16:17, :] = row(ba_ref, bb_ref)
    head_send[17:18, :] = row(gain2_ref, bias2_ref)
    head_send[18:19, :] = row(bdown_ref, bdown_ref)
    head_send[19:20, :] = bup[:, :LANES]
    head_send[20:21, :] = bup[:, LANES:]
    head_send[21:24, :] = jnp.zeros((3, LANES), F32)
    head_recv[chan] = head_send[...]
    head = exchange(0, lambda peer: head_send, head_recv)
    inputs = exchange(1, lambda peer: in_send.at[peer], in_recv)
    head[0]()
    gather_start()
    inputs[0]()

    level, filled = bucket_ref[0], items_ref[0]
    coefl_ref[...] = levels_ref[level]
    item_blocks = jnp.where(level == 0, 2, jnp.where(level == 1, 4, 8))
    block_id = 2 * (row_id % PAIRS) + jnp.where(lane_id >= HALF, 1, 0)
    bound = jnp.where(row_id < PAIRS, filled * item_blocks, item_blocks)
    aux_ref[...] = jnp.where(block_id < bound, 1.0, 0.0)
    for i in range(8):
        modes_ref[i] = jnp.concatenate([raw_modes_ref[i], raw_modes_ref[i]], axis=1)
    log_dt = row(log_dt_ref, log_dt_ref)
    sigma, step_size = 2.0 * jnp.exp(-log_dt), jnp.exp(log_dt)

    def after_quarter(quarter):
        if quarter == 1:
            gather_across()

    base = pl.multiple_of(dp * QUARTER, QUARTER)

    def spec_copy(which, r):
        peer = (dp + r) % 4
        src, dst = ((spec_send, spec_recv), (sgrad_send.at[peer], sgrad_recv))[which]
        return remote(src, dst.at[dp], spec_ss.at[which, r - 1], spec_rs.at[which, r - 1], dp=peer)

    cauchy_coefficients(modes_ref, sigma, mcoef_ref)
    cauchy_forward(sigma, mcoef_ref, wave_ref, base, sums_ref, spec_send, after_quarter)
    spec_recv[dp] = spec_send[...]
    for r in range(1, 4):
        spec_copy(0, r).start()
    gather_step(1, 0)

    head[1]()
    sums = head_recv[0, 0:16, :]
    for c in range(1, N_CHAN):
        sums = sums + head_recv[c, 0:16, :]
    mean = sums[0:8] * (1.0 / MODEL_WIDTH)
    rstd = lax.rsqrt(sums[8:16] * (1.0 / MODEL_WIDTH) - mean * mean + EPSILON)

    def columns(rows):
        tall = rows.T
        return [jnp.where(low_lanes(ROWS), tall[:, j : j + 1], tall[:, 4 + j : 5 + j]) for j in range(PAIRS)]

    gain1, bias1, skip = row(gain1_ref, gain1_ref), row(bias1_ref, bias1_ref), row(skip_ref, skip_ref)
    mean_cols, rstd_cols = columns(mean), columns(rstd)
    for j in range(PAIRS):
        hat = (tok_ref[j * ROWS : (j + 1) * ROWS, :].astype(F32) - mean_cols[j]) * rstd_cols[j]
        hat_ref[j] = hat
        norm_ref[j] = hat * gain1 + bias1

    spread_pairs(lambda j, rows: norm_ref[j, rows, :], coefl_ref, 0, tw_ref, 0, 5, rhs_ref)
    transform_into(sig_ref, mat_ref, 0, rhs_ref)
    gather_step(1, 1)

    for r in range(1, 4):
        spec_copy(0, r).wait_recv()
    for source in range(4):
        store_split(rhs_ref, source * QUARTER, 0, spec_recv[source, :QUARTER, :])
        store_split(rhs_ref, ROWS + source * QUARTER, 0, spec_recv[source, QUARTER:, :])
    freq_ref[:, 0:256] = split_product(mat_ref, 1, rhs_ref, 0, 256)
    even = split_product(mat_ref, 2, rhs_ref, LANES, LANES)
    freq_ref[:, LANES:256] = jnp.where(low_lanes(256), freq_ref[:, LANES:256], even)
    sign = 1.0 - 2.0 * (lax.broadcasted_iota(jnp.int32, (CHUNK, LANES), 0) % 2).astype(F32)
    nyquist = step_size * column_sum(mcoef_ref[0]) * (1.0 / TOK_DEV)

    def store_taps(j, rows, values):
        taps_ref[j, rows, :] = (values + sign * nyquist) * aux_ref[4 + j : 5 + j, :]

    gather_pairs(freq_ref, coefc_ref, 160, tw_ref, 10, 2, store_taps)
    gather_step(2, 0)
    spread_pairs(lambda j, rows: taps_ref[j, rows, :], coefc_ref, 0, tw_ref, 0, 5, rhs_ref)
    transform_into(ans_ref, mat_ref, 0, rhs_ref)

    gather_step(2, 1)
    multiply_spectra(sig_ref, ans_ref, rhs_ref, False)
    transform_into(freq_ref, mat_ref, 1, rhs_ref)

    def store_conv(j, rows, values):
        conv_ref[j, rows, :] = values

    gather_pairs(freq_ref, coefl_ref, 80, tw_ref, 0, 5, store_conv)
    gather_step(3, 0)
    for j in range(PAIRS):
        mixed = conv_ref[j] * aux_ref[j : j + 1, :] + skip * norm_ref[j]
        cumulative, density = normal_parts(mixed)
        slope_ref[j] = cumulative + mixed * density
        low, high = split_pair(mixed * cumulative)
        acts_send[2 * j] = low.astype(BF16)
        acts_send[2 * j + 1] = high.astype(BF16)
    acts_recv[chan] = acts_send[chan]
    acts = exchange(2, lambda peer: acts_send.at[peer], acts_recv)
    acts[0]()
    gather_step(3, 1)
    gather_step(4, 0)
    gather_step(4, 1)
    inputs[1]()
    acts[1]()

    def joined(ref, pair, first):
        return join_pair(
            ref[2 * pair, first : first + HALF, :].astype(F32), ref[2 * pair + 1, first : first + HALF, :].astype(F32)
        )

    def lanes_of(pair):
        return slice(pair * LANES, (pair + 1) * LANES)

    ACTS, NORM2, GRADF = range(3)
    for p in range(PAIRS):
        low_ref[ACTS, :, lanes_of(p)] = joined(acts_recv, p, 0).astype(BF16)
        low_ref[GRADF, :, lanes_of(p)] = joined(in_recv, p, HALF).astype(BF16)
    gather_finish()

    def vector(row, first, second):
        return interleave(head_recv[first, 16 + row : 17 + row, :], head_recv[second, 16 + row : 17 + row, :])

    total = 0.0
    for p in range(PAIRS):
        first = dot_nn(low_ref[ACTS], w_ref[2 * p, :, 0:LANES]) + head_recv[2 * p, 16:17, :]
        second = dot_nn(low_ref[ACTS], w_ref[2 * p + 1, :, 0:LANES]) + head_recv[2 * p + 1, 16:17, :]
        gate, raw = interleave(first, second)
        swish = lax.logistic(raw)
        gate_ref[p], swish_ref[p] = gate, swish
        resid = joined(in_recv, p, 0) + gate * swish
        res_ref[p] = resid
        total = total + resid
    mean2 = jnp.sum(total, axis=1, keepdims=True) * (1.0 / MODEL_WIDTH)
    total = 0.0
    for p in range(PAIRS):
        centred = res_ref[p] - mean2
        total = total + centred * centred
    rstd2 = lax.rsqrt(jnp.sum(total, axis=1, keepdims=True) * (1.0 / MODEL_WIDTH) + EPSILON)
    gain2 = []
    for p in range(PAIRS):
        gain, bias = vector(1, 2 * p, 2 * p + 1)
        gain2.append(gain)
        hat = (res_ref[p] - mean2) * rstd2
        hat2_ref[p] = hat
        low_ref[NORM2, :, lanes_of(p)] = (hat * gain + bias).astype(BF16)
    branch_ref[...] = jnp.zeros_like(branch_ref)
    back2_ref[...] = jnp.zeros_like(back2_ref)

    def hidden_block(c, carry):
        bias = jnp.concatenate([head_recv[c, 19:20, :], head_recv[c, 20:21, :]], axis=1)
        pre = dot_nn(low_ref[NORM2], w_ref[c, :, 128:384]) + bias
        cumulative, density = normal_parts(pre)
        hidden = (pre * cumulative).astype(BF16)
        hid_ref[c] = hidden
        grad = dot_nn(low_ref[GRADF], w_ref[c, :, 384:640]) * (cumulative + pre * density)
        grad = grad.astype(BF16)
        gpre_ref[c] = grad
        sums = column_sum(grad.astype(F32))
        tail_send[c, 3:4, :] = sums[:, 0:LANES]
        tail_send[c, 4:5, :] = sums[:, LANES : 2 * LANES]
        branch_ref[...] += dot_nt(hidden, w_ref[c, :, 384:640])
        back2_ref[...] += dot_nt(grad, w_ref[c, :, 128:384])
        return carry

    lax.fori_loop(0, N_CHAN, hidden_block, 0)

    mean_q, mean_qx = 0.0, 0.0
    for p in range(PAIRS):
        grad, hat = back2_ref[:, lanes_of(p)], hat2_ref[p]
        q = grad * gain2[p]
        mean_q = mean_q + q
        mean_qx = mean_qx + q * hat
        gain_grad, bias_grad = interleave(column_sum(grad * hat), column_sum(grad))
        tail_send[2 * p, 1:2, :] = gain_grad
        first, second = interleave(turn_half(column_sum(grad * hat)), turn_half(column_sum(grad)))
        tail_send[2 * p + 1, 1:2, :] = first
    mean_q = jnp.sum(mean_q, axis=1, keepdims=True) * (1.0 / MODEL_WIDTH)
    mean_qx = jnp.sum(mean_qx, axis=1, keepdims=True) * (1.0 / MODEL_WIDTH)
    for p in range(PAIRS):
        hat = hat2_ref[p]
        extra = rstd2 * (back2_ref[:, lanes_of(p)] * gain2[p] - mean_q - hat * mean_qx)
        grad_f = joined(in_recv, p, HALF)
        grad_resid = grad_f + extra
        gate, swish = gate_ref[p], swish_ref[p]
        grad_a = (grad_resid * swish).astype(BF16).astype(F32)
        grad_b = (grad_resid * gate * swish * (1.0 - swish)).astype(BF16).astype(F32)
        first, second = interleave(grad_a, grad_b)
        gab_ref[2 * p] = first.astype(BF16)
        gab_ref[2 * p + 1] = second.astype(BF16)
        tail_send[2 * p, 0:1, :] = column_sum(first)
        tail_send[2 * p + 1, 0:1, :] = column_sum(second)
        low, high = interleave(column_sum(grad_f), column_sum(grad_f))
        tail_send[2 * p, 2:3, :] = low
        tail_send[2 * p + 1, 2:3, :] = high
        low, high = split_pair(extra)
        late_send[2 * p, HALF:, :] = low.astype(BF16)
        late_send[2 * p + 1, HALF:, :] = high.astype(BF16)
    grad_acts = 0.0
    for c in range(N_CHAN):
        grad_acts = grad_acts + dot_nt(gab_ref[c], w_ref[c, :, 0:LANES])
    for p in range(PAIRS):
        low, high = split_pair(grad_acts[:, lanes_of(p)])
        back_send[2 * p] = low.astype(BF16)
        back_send[2 * p + 1] = high.astype(BF16)
    back_recv[chan] = back_send[chan]
    back = exchange(3, lambda peer: back_send.at[peer], back_recv)
    back[0]()

    def rsib_copy(offset, block):
        slot = (offset + 3) * 2 + block
        src = grad_ref.at[chan_at(offset), pl.ds(row_of(theirs[block]), ROWS), :]
        return remote(src, sib_ref.at[slot], rsib_ss.at[slot], rsib_rs.at[slot], dp=sibling)

    def offset_of(turn, step):
        return TURNS[turn] * (5 - step)

    def rring_copy(turn, step, block):
        slot = item_slot(turn, step, block)
        src = grad_ref.at[chan_at(offset_of(turn, step)), pl.ds(row_of(mine[block]), ROWS), :]
        return remote(src, ring_ref.at[slot], rring_ss.at[slot], rring_rs.at[slot], chan=nexts[turn])

    ritems = [(turn, 5 - step, block) for turn, step, block in items]

    def own_and_sibling(offset, block):
        slot = ((offset if offset != -4 else 4) + 3) * 2 + block
        rsib_copy(offset if offset != -4 else 4, block).wait_recv()
        own = grad_ref[chan_at(offset), pl.ds(row_of(mine[block]), ROWS), :].astype(F32)
        return own + sib_ref[slot].astype(F32)

    def reduce_step(step):
        for turn, at, block in ritems:
            if at != step:
                continue
            total = own_and_sibling(offset_of(turn, step), block)
            if (turn, step - 1, block) in ritems:
                rring_copy(turn, step - 1, block).wait_recv()
                total = total + ring_ref[item_slot(turn, step - 1, block)].astype(F32)
            grad_ref[chan_at(offset_of(turn, step)), pl.ds(row_of(mine[block]), ROWS), :] = total.astype(BF16)
            copy = rring_copy(turn, step, block)
            copy.start()
            pending.append(copy)

    def reduce_last():
        for block in (1, 0):
            total = own_and_sibling(0, block)
            for turn in range(2):
                rring_copy(turn, 4, block).wait_recv()
                total = total + ring_ref[item_slot(turn, 4, block)].astype(F32)
            if block == 1:
                part_ref[0] = total.astype(BF16)
                send(part_ref.at[0], part_ref.at[1], rx_ss, rx_rs, dp=across)
            else:
                gw_ref[...] = total

    def reduce_finish():
        remote(part_ref.at[0], part_ref.at[1], rx_ss, rx_rs, dp=across).wait_recv()
        gw_ref[...] += part_ref[1].astype(F32)

    tall = [low_ref[i].astype(F32).T.astype(BF16) for i in range(3)]
    order = (4, 3, -3, 2, -2, 1, -1, 0)
    for offset in order:
        c = chan_at(offset)
        grad_ref[c, :, 0:128] = dot_nn(tall[ACTS], gab_ref[c]).astype(BF16)
        grad_ref[c, :, 128:384] = dot_nn(tall[NORM2], gpre_ref[c]).astype(BF16)
        grad_ref[c, :, 384:640] = dot_nn(tall[GRADF], hid_ref[c]).astype(BF16)
        for block in range(2):
            copy = rsib_copy(offset, block)
            copy.start()
            pending.append(copy)
        if offset == -3:
            reduce_step(1)
        elif offset == -1:
            reduce_step(2)
    for p in range(PAIRS):
        out = res_ref[p] + branch_ref[:, lanes_of(p)] + interleave(head_recv[2 * p, 18:19, :], head_recv[2 * p + 1, 18:19, :])[0]
        low, high = split_pair(out)
        late_send[2 * p, :HALF, :] = low.astype(BF16)
        late_send[2 * p + 1, :HALF, :] = high.astype(BF16)
    for c in range(N_CHAN):
        tail_send[c, 5:8, :] = jnp.zeros((3, LANES), F32)
    late_recv[chan] = late_send[chan]
    tail_recv[chan] = tail_send[chan]
    late = exchange(4, lambda peer: late_send.at[peer], late_recv)
    tail = exchange(5, lambda peer: tail_send.at[peer], tail_recv)
    late[0]()
    tail[0]()

    back[1]()
    skip_grad = 0.0
    for j in range(PAIRS):
        grad = joined(back_recv, j, 0) * slope_ref[j]
        slope_ref[j] = grad
        conv_ref[j] = grad * aux_ref[j : j + 1, :]
        skip_grad = skip_grad + column_sum(grad * norm_ref[j])
    spread_pairs(lambda j, rows: conv_ref[j, rows, :], coefl_ref, 0, tw_ref, 0, 5, rhs_ref)
    transform_into(freq_ref, mat_ref, 0, rhs_ref)
    multiply_spectra(sig_ref, freq_ref, rhs_ref, True)
    transform_into(sig_ref, mat_ref, 1, rhs_ref)

    def store_kernel_grad(j, rows, values):
        taps_ref[j, rows, :] = values * aux_ref[4 + j : 5 + j, :]

    gather_pairs(sig_ref, coefc_ref, 80, tw_ref, 0, 5, store_kernel_grad)
    nyquist_grad = 0.0
    for j in range(PAIRS):
        whole_sign = 1.0 - 2.0 * (lax.broadcasted_iota(jnp.int32, (ROWS, LANES), 0) % 2).astype(F32)
        nyquist_grad = nyquist_grad + column_sum(taps_ref[j] * whole_sign)
    nyquist_grad = fold(nyquist_grad) * (1.0 / TOK_DEV)
    spread_pairs(lambda j, rows: taps_ref[j, rows, :], coefc_ref, 192, tw_ref, 10, 2, rhs_ref)
    taps_freq_ref[...] = split_product(mat_ref, 0, rhs_ref, 0, 256)
    even = split_product(mat_ref, 3, rhs_ref, LANES, LANES)
    taps_freq_ref[:, LANES:256] = jnp.where(low_lanes(256), taps_freq_ref[:, LANES:256], even)
    for source in range(4):
        rows = slice(source * QUARTER, (source + 1) * QUARTER)
        sgrad_send[source, :QUARTER, :] = taps_freq_ref[rows, :]
        sgrad_send[source, QUARTER:, :] = taps_freq_ref[ROWS + source * QUARTER : ROWS + (source + 1) * QUARTER, :]
    sgrad_recv[dp] = sgrad_send[dp]
    for r in range(1, 4):
        spec_copy(1, r).start()

    multiply_spectra(ans_ref, freq_ref, rhs_ref, True)
    transform_into(freq_ref, mat_ref, 1, rhs_ref)
    gather_pairs(freq_ref, coefl_ref, 80, tw_ref, 0, 5, store_conv)
    gain_grad, bias_grad = 0.0, 0.0
    scaled, crossed = [], []
    for j in range(PAIRS):
        grad = conv_ref[j] + skip * slope_ref[j]
        conv_ref[j] = grad
        gain_grad = gain_grad + column_sum(grad * hat_ref[j])
        bias_grad = bias_grad + column_sum(grad)
    conv = conv_ref[...].reshape(PAIRS * ROWS, LANES) * gain1
    for i, sums in enumerate(
        token_sums(split(conv)) + token_sums(split(conv * hat_ref[...].reshape(PAIRS * ROWS, LANES)))
    ):
        sum_send[i : i + 1, :] = sums
    sum_recv[chan] = sum_send[...]
    sums_back = exchange(6, lambda peer: sum_send, sum_recv)
    sums_back[0]()
    reduce_step(3)

    for r in range(1, 4):
        spec_copy(1, r).wait_recv()
    sgrad_ref[...] = sgrad_recv[0] + sgrad_recv[1] + sgrad_recv[2] + sgrad_recv[3]

    def after_part(part):
        if part == 3:
            reduce_step(4)

    mode_grads, dt_grad = cauchy_backward(
        modes_ref, sigma, nyquist_grad, step_size, mcoef_ref, wave_ref, base, sums_ref, sgrad_ref, pgrad_ref, mback_ref,
        after_part,
    )
    mask = low_lanes(32)
    for i in range(4):
        dp_send[i * 32 : (i + 1) * 32, :] = jnp.where(mask, mode_grads[i], mode_grads[i + 4])
    first = low_lanes(1)
    dp_send[128:129, :] = jnp.where(first, dt_grad, fold(skip_grad))
    dp_send[129:130, :] = jnp.where(first, fold(gain_grad), fold(bias_grad))
    dp_send[130:136, :] = jnp.zeros((6, LANES), F32)
    tail[1]()
    tail_sum = tail_recv[0]
    for c in range(1, N_CHAN):
        tail_sum = tail_sum + tail_recv[c]
    dp_send[136:144, :] = tail_sum
    dp_recv[0] = dp_send[...]

    def dp_copy(r):
        return remote(dp_send, dp_recv.at[r], dp_ss.at[r - 1], dp_rs.at[r - 1], dp=(dp + r) % 4)

    for r in range(1, 4):
        dp_copy(r).start()

    sums_back[1]()
    sums = sum_recv[0]
    for c in range(1, N_CHAN):
        sums = sums + sum_recv[c]
    sums = sums * (1.0 / MODEL_WIDTH)
    rstd_cols, q_cols, qx_cols = columns(rstd), columns(sums[0:8]), columns(sums[8:16])
    late[1]()
    for j in range(PAIRS):
        rows = slice(j * ROWS, (j + 1) * ROWS)
        out_ref[rows, :] = joined(late_recv, j, 0).astype(BF16)
        dtok_ref[rows, :] = joined(late_recv, j, HALF) + rstd_cols[j] * (
            conv_ref[j] * gain1 - q_cols[j] - hat_ref[j] * qx_cols[j]
        )
    reduce_last()
    for r in range(1, 4):
        dp_copy(r).wait_recv()
    total = dp_recv[0] + dp_recv[1] + dp_recv[2] + dp_recv[3]
    gm_ref[...] = total[0:128]
    gv_ref[...] = total[128:144]
    reduce_finish()
    for copy in pending:
        copy.wait_send()
    for group in (head, inputs, acts, back, late, tail, sums_back):
        group[2]()
    for r in range(1, 4):
        dp_copy(r).wait_send()
        spec_copy(0, r).wait_send()
        spec_copy(1, r).wait_send()


def unpack_kernel(
    out_ref, dtok_ref, gw_ref, gm_ref, gv_ref, cotangent_ref,
    output_ref, tokens_ref, gain1_ref, bias1_ref, modes_ref, dt_ref, skip_ref, wa_ref, ba_ref, wb_ref, bb_ref,
    gain2_ref, bias2_ref, up_ref, bup_ref, down_ref, bdown_ref,
):
    for j in range(PAIRS):
        out = out_ref[j * ROWS : (j + 1) * ROWS, :].astype(F32).T.astype(BF16)
        grad = dtok_ref[j * ROWS : (j + 1) * ROWS, :].T
        for h in range(2):
            lanes, rows = slice((2 * j + h) * ROWS, (2 * j + h + 1) * ROWS), slice(h * HALF, (h + 1) * HALF)
            output_ref[:, lanes] = out[rows]
            tokens_ref[:, lanes] = cotangent_ref[:, lanes] + grad[rows]
    for i in range(8):
        modes_ref[i] = gm_ref[i % 4 * 32 : i % 4 * 32 + 32, i // 4 * HALF : (i // 4 + 1) * HALF]
    gates = gw_ref[:, :LANES].T
    wa_ref[...] = gates[:HALF]
    wb_ref[...] = gates[HALF:]
    up_ref[...] = gw_ref[:, 128:384]
    down_ref[...] = gw_ref[:, 384:640].T
    for at, low, high in (
        (0, dt_ref, skip_ref), (1, gain1_ref, bias1_ref), (8, ba_ref, bb_ref), (9, gain2_ref, bias2_ref),
    ):
        low[...] = gv_ref[at, :HALF]
        high[...] = gv_ref[at, HALF:]
    bdown_ref[...] = gv_ref[10, :HALF]
    bup_ref[:LANES] = gv_ref[11, :]
    bup_ref[LANES:] = gv_ref[12, :]


def block_program():
    mats, twiddle, levels, constant, wave = mixer_tables()

    def run(tokens, cotangent, bucket, items, gain1, bias1, modes, log_dt, skip, w_a, b_a, w_b, b_b, gain2, bias2, w_up, b_up, w_down, b_down):
        vmem = pl.BlockSpec(memory_space=pltpu.VMEM)
        smem = pl.BlockSpec(memory_space=pltpu.SMEM)
        dma = pltpu.SemaphoreType.DMA

        def buf(*shape):
            return pltpu.VMEM(shape, F32)

        def low(*shape):
            return pltpu.VMEM(shape, BF16)

        def full(*shape):
            return jax.ShapeDtypeStruct(shape, F32)

        big, wide = (PAIRS, ROWS, LANES), (256, WIDE)
        packed = pl.pallas_call(
            block_kernel,
            out_shape=(
                jax.ShapeDtypeStruct((512, LANES), BF16), full(512, LANES), full(ROWS, WIDE), full(ROWS, LANES),
                full(16, LANES),
            ),
            in_specs=[smem] * 2 + [vmem] * 22,
            out_specs=(vmem,) * 5,
            scratch_shapes=[
                low(512, LANES), buf(8, LANES), buf(160, LANES), buf(8, 32, LANES),
                low(N_CHAN, 512, WIDE), low(N_CHAN, 512, WIDE), low(16, ROWS, WIDE), low(16, ROWS, WIDE), low(2, ROWS, WIDE),
                low(N_CHAN, ROWS, LANES), low(N_CHAN, ROWS, LANES), buf(24, LANES), buf(N_CHAN, 24, LANES),
                low(N_CHAN, HALF, LANES), low(N_CHAN, HALF, LANES), low(N_CHAN, HALF, LANES), low(N_CHAN, HALF, LANES),
                low(N_CHAN, ROWS, LANES), low(N_CHAN, ROWS, LANES),
                buf(16, LANES), buf(N_CHAN, 16, LANES), buf(N_CHAN, 8, LANES), buf(N_CHAN, 8, LANES),
                buf(144, LANES), buf(4, 144, LANES), buf(64, 256), buf(4, 64, 256), buf(4, 64, 256), buf(4, 64, 256),
                buf(*big), buf(*big), buf(*big), buf(*big), low(2, *wide), buf(*wide), buf(*wide), buf(*wide), buf(*big),
                buf(10, 32, LANES), buf(2, 16, QUARTER, LANES), buf(2, 16, QUARTER, LANES), buf(10, 32, LANES),
                buf(64, 256), buf(256, 256),
                buf(*big), buf(*big), buf(*big), buf(*big), low(3, ROWS, 512), buf(ROWS, 512), buf(ROWS, 512),
                low(N_CHAN, ROWS, LANES), low(N_CHAN, ROWS, 256), low(N_CHAN, ROWS, 256),
                dma((16,)), dma((16,)), dma((18,)), dma((18,)), dma, dma, dma((16,)), dma((16,)), dma((16,)), dma((16,)),
                dma, dma, dma((7, 7)), dma((7, 7)), dma((3,)), dma((3,)), dma((2, 3)), dma((2, 3)),
            ],
            compiler_params=pltpu.CompilerParams(
                collective_id=0, has_side_effects=True, vmem_limit_bytes=60 * 1024 * 1024
            ),
            name="block",
        )(
            bucket, items, tokens.T, cotangent.T, gain1, bias1, jnp.swapaxes(modes, 1, 2), log_dt, skip,
            w_a.T, b_a, w_b.T, b_b, gain2, bias2,
            w_up, b_up, w_down, b_down, levels, constant, mats, twiddle, wave,
        )
        small = full(HALF)
        results = pl.pallas_call(
            unpack_kernel,
            out_shape=(
                jax.ShapeDtypeStruct((HALF, TOK_DEV), BF16), full(HALF, TOK_DEV), small, small, full(8, 32, HALF),
                small, small, full(HALF, ROWS), small, full(HALF, ROWS), small, small, small, full(ROWS, 256),
                full(256), full(256, ROWS), small,
            ),
            in_specs=[vmem] * 6,
            out_specs=(vmem,) * 17,
            name="unpack",
        )(*packed, cotangent.T)
        turned = {0, 1, 4, 7, 9}
        return tuple(jnp.swapaxes(r, -1, -2) if i in turned else r for i, r in enumerate(results))

    return run


def solution(mesh):
    small = mesh.shape["chan"] == N_CHAN and mesh.shape["dp"] == 4
    return jax.shard_map(
        block_program() if small else shards,
        mesh=mesh,
        in_specs=(
            P("dp", "chan"),
            P("dp", "chan"),
            P("dp"),
            P("dp"),
            P("chan"),
            P("chan"),
            P(None, "chan", None),
            P("chan"),
            P("chan"),
            P("dp", "chan"),
            P("chan"),
            P("dp", "chan"),
            P("chan"),
            P("chan"),
            P("chan"),
            P("dp", "chan"),
            P("chan"),
            P("chan", "dp"),
            P("chan"),
        ),
        out_specs=(
            P("dp", "chan"),
            P("dp", "chan"),
            P("chan"),
            P("chan"),
            P(None, "chan", None),
            P("chan"),
            P("chan"),
            P("dp", "chan"),
            P("chan"),
            P("dp", "chan"),
            P("chan"),
            P("chan"),
            P("chan"),
            P("dp", "chan"),
            P("chan"),
            P("chan", "dp"),
            P("chan"),
        ),
        check_vma=False,
    )
```

```python
import math

import jax
import jax.numpy as jnp
import ml_dtypes
import numpy as np
from jax import lax
from jax.experimental import pallas as pl
from jax.experimental.pallas import tpu as pltpu
from jax.sharding import PartitionSpec as P

MODEL_WIDTH = 512
TOK_DEV = 1024


HIGHEST = lax.Precision.HIGHEST
EPSILON = 1e-05


def product(left, right):
    return jnp.dot(left, right, preferred_element_type=jnp.float32)


def product_nt(left, right):
    return lax.dot_general(
        left, right, (((1,), (1,)), ((), ())), preferred_element_type=jnp.float32
    )


def product_tn(left, right):
    return lax.dot_general(
        left, right, (((0,), (0,)), ((), ())), preferred_element_type=jnp.float32
    )


def gelu_slope(values):
    return (
        0.5 * (1.0 + lax.erf(values * 0.7071067811865476))
        + values * jnp.exp(-0.5 * values * values) * 0.3989422804014327
    )


def half_angles(length):
    angle = np.arange(length // 2 + 1, dtype=np.float64) * (math.pi / length)
    cosine, sine = np.cos(angle), np.sin(angle)
    cosine[-1] = 0.0
    return cosine.astype(np.float32), sine.astype(np.float32)


def inverse_tables(length):
    freq = np.arange(length // 2 + 1)
    turn = (freq[:, None] * np.arange(length)[None, :]) % length * (2.0 * math.pi / length)
    weight = np.where((freq == 0) | (freq == length // 2), 1.0, 2.0)[:, None] / length
    return (weight * np.cos(turn)).astype(np.float32), (weight * np.sin(turn)).astype(np.float32)


def high_einsum(form, left, right):
    return jnp.einsum(form, left, right, precision=HIGHEST)


def ssm_kernel(modes, log_dt):
    cos_h, sin_h = half_angles(TOK_DEV)
    index = jnp.arange(modes.shape[2], dtype=jnp.int32).astype(jnp.float32)
    lam_re = -0.5 * jnp.exp(modes[0])
    lam_im = math.pi * (index + modes[1])
    rank_re, rank_im, in_re, in_im, out_re, out_im = (modes[i] for i in range(2, 8))
    sigma = (2.0 * jnp.exp(-log_dt))[:, None]

    def points(values):
        return values.T[:, None, :]

    den_re = points(lam_re * lam_re + lam_im * lam_im) * (cos_h * cos_h)[:, None] - (
        sigma * sigma
    ).T * (sin_h * sin_h)[:, None]
    den_im = points(-2.0 * sigma * lam_re) * (sin_h * cos_h)[:, None]
    den_sq = den_re * den_re + den_im * den_im
    inv_re = den_re / den_sq
    inv_im = -den_im / den_sq
    sums = []
    for real, imag in (
        (out_re * in_re + out_im * in_im, out_re * in_im - out_im * in_re),
        (out_re * rank_re + out_im * rank_im, out_re * rank_im - out_im * rank_re),
        (rank_re * in_re + rank_im * in_im, rank_re * in_im - rank_im * in_re),
        (rank_re * rank_re + rank_im * rank_im, jnp.zeros_like(rank_re)),
    ):
        turned = points(real * lam_re + imag * lam_im)
        real = points(real)
        p_re, p_im = jnp.sum(real * inv_re, axis=0), jnp.sum(real * inv_im, axis=0)
        q_re, q_im = jnp.sum(turned * inv_re, axis=0), jnp.sum(turned * inv_im, axis=0)
        sine = sin_h[:, None] * sigma.T
        sums.append((-sine * p_im - cos_h[:, None] * q_re, sine * p_re - cos_h[:, None] * q_im))
    (cross_re, cross_im), (left_re, left_im), (right_re, right_im), (self_re, self_im) = sums
    twice = 2.0 * cos_h[:, None]
    loop_re, loop_im = 1.0 + twice * self_re, twice * self_im
    back_re, back_im = twice * right_re, twice * right_im
    loop_sq = loop_re * loop_re + loop_im * loop_im
    ratio_re = (back_re * loop_re + back_im * loop_im) / loop_sq
    ratio_im = (back_im * loop_re - back_re * loop_im) / loop_sq
    part_re = cross_re - (left_re * ratio_re - left_im * ratio_im)
    part_im = cross_im - (left_re * ratio_im + left_im * ratio_re)
    spec_re = 2.0 * (cos_h[:, None] * part_re - sin_h[:, None] * part_im)
    spec_im = 2.0 * (cos_h[:, None] * part_im + sin_h[:, None] * part_re)
    cos_tab, sin_tab = inverse_tables(TOK_DEV)
    return high_einsum("kl,kc->lc", cos_tab, spec_re) - high_einsum("kl,kc->lc", sin_tab, spec_im)


BLOCK = 128
BLOCKS = TOK_DEV // BLOCK
FIRST = 2 * BLOCKS
KEPT = FIRST // 2 + 1


def transform_tables():
    length = 2 * TOK_DEV
    turn = np.arange(KEPT)[:, None] * np.arange(BLOCK)[None, :] * (2.0 * math.pi / length)
    small = np.arange(BLOCK)[:, None] * np.arange(BLOCK)[None, :] % BLOCK * (2.0 * math.pi / BLOCK)
    spots = np.stack([np.arange(BLOCKS) + np.arange(BLOCKS) // (2 << b) * (2 << b) for b in range(3)])
    angle = spots[:, None, :] * np.arange(KEPT)[None, :, None] % FIRST * (2.0 * math.pi / FIRST)
    parts = (np.cos(turn), np.sin(turn), np.cos(small), np.sin(small), np.cos(angle), np.sin(angle))
    return [part.astype(np.float32) for part in parts]


def forward_transform(blocks, cos_a, sin_a):
    cos_t, sin_t, cos_s, sin_s, _, _ = transform_tables()
    step_re = high_einsum("ka,abc->kbc", cos_a, blocks)
    step_im = -high_einsum("ka,abc->kbc", sin_a, blocks)
    turned_re = step_re * cos_t[..., None] + step_im * sin_t[..., None]
    turned_im = step_im * cos_t[..., None] - step_re * sin_t[..., None]
    both = jnp.concatenate([turned_re, turned_im], axis=1)
    matrix = np.block([[cos_s, sin_s], [-sin_s, cos_s]])
    return high_einsum("pb,kbc->kpc", matrix, both)


def inverse_transform(spectrum, cos_a, sin_a):
    cos_t, sin_t, cos_s, sin_s, _, _ = transform_tables()
    matrix = np.block([[cos_s, -sin_s], [sin_s, cos_s]])
    both = high_einsum("bp,kpc->kbc", matrix, spectrum)
    step_re, step_im = both[:, :BLOCK], both[:, BLOCK:]
    turned_re = step_re * cos_t[..., None] - step_im * sin_t[..., None]
    turned_im = step_im * cos_t[..., None] + step_re * sin_t[..., None]
    weight = np.where(np.arange(KEPT) % (KEPT - 1) == 0, 1.0, 2.0).astype(np.float32) / (2 * TOK_DEV)
    return high_einsum("ka,kbc->abc", cos_a * weight[:, None], turned_re) - high_einsum(
        "ka,kbc->abc", sin_a * weight[:, None], turned_im
    )


def multiply(left, right):
    left_re, left_im = left[:, :BLOCK], left[:, BLOCK:]
    right_re, right_im = right[:, :BLOCK], right[:, BLOCK:]
    return jnp.concatenate(
        [left_re * right_re - left_im * right_im, left_re * right_im + left_im * right_re], axis=1
    )


def mixer(normed, kernel_taps, skip_gain, bucket, filled):
    _, _, _, _, cos_a, sin_a = transform_tables()
    cos_x, sin_x = jnp.asarray(cos_a)[bucket], jnp.asarray(sin_a)[bucket]
    item_blocks = 2 << bucket
    block_id = jnp.arange(BLOCKS, dtype=jnp.int32)[:, None, None]
    taps = jnp.where(block_id < item_blocks, kernel_taps.reshape(BLOCKS, BLOCK, -1), 0.0)
    signal = forward_transform(normed.reshape(BLOCKS, BLOCK, -1), cos_x, sin_x)
    answer = forward_transform(taps, cos_a[2], sin_a[2])
    result = inverse_transform(multiply(signal, answer), cos_x, sin_x)
    result = jnp.where(block_id < filled * item_blocks, result, 0.0)
    return result.reshape(normed.shape) + skip_gain * normed


def shards(
    tokens,
    cotangent,
    group_bucket,
    group_items,
    first_norm_gain,
    first_norm_bias,
    modes,
    log_dt,
    d_skip,
    w_a,
    b_a,
    w_b,
    b_b,
    second_norm_gain,
    second_norm_bias,
    w_up,
    b_up,
    w_down,
    b_down,
):
    input_tokens = tokens.astype(jnp.float32)
    sums_in = lax.psum(
        (jnp.sum(input_tokens, axis=1), jnp.sum(input_tokens * input_tokens, axis=1)), "chan"
    )
    input_average = sums_in[0][:, None] / MODEL_WIDTH
    input_inverse_deviation = lax.rsqrt(
        sums_in[1][:, None] / MODEL_WIDTH - input_average * input_average + EPSILON
    )
    input_standardized = (input_tokens - input_average) * input_inverse_deviation
    input_normalized = input_standardized * first_norm_gain + first_norm_bias
    level = group_bucket[0]
    filled = group_items[0]
    kernel_taps, kernel_back = jax.vjp(ssm_kernel, modes, log_dt)

    def local_mix(values, taps_now, skip_gain):
        return mixer(values, taps_now, skip_gain, level, filled)

    mixed, mix_back = jax.vjp(local_mix, input_normalized, kernel_taps, d_skip)
    acts_low = jax.nn.gelu(mixed, approximate=False).astype(jnp.bfloat16)
    wa_full, wb_full, up_full, down_full = (
        lax.all_gather(w_a.astype(jnp.bfloat16), "dp", axis=0, tiled=True),
        lax.all_gather(w_b.astype(jnp.bfloat16), "dp", axis=0, tiled=True),
        lax.all_gather(w_up.astype(jnp.bfloat16), "dp", axis=0, tiled=True),
        lax.all_gather(w_down.astype(jnp.bfloat16), "dp", axis=1, tiled=True),
    )
    acts_full = lax.all_gather(acts_low, "chan", axis=1, tiled=True)
    gate_a = product(acts_full, wa_full) + b_a
    gate_b = product(acts_full, wb_full) + b_b
    gate_sig = jax.nn.sigmoid(gate_b)
    residual_stream = input_tokens + gate_a * gate_sig
    sums_mid = lax.psum(
        (jnp.sum(residual_stream, axis=1), jnp.sum(residual_stream * residual_stream, axis=1)),
        "chan",
    )
    middle_average = sums_mid[0][:, None] / MODEL_WIDTH
    middle_inverse_deviation = lax.rsqrt(
        sums_mid[1][:, None] / MODEL_WIDTH - middle_average * middle_average + EPSILON
    )
    middle_standardized = (residual_stream - middle_average) * middle_inverse_deviation
    middle_reduced = (middle_standardized * second_norm_gain + second_norm_bias).astype(
        jnp.bfloat16
    )
    mid_full = lax.all_gather(middle_reduced, "chan", axis=1, tiled=True)
    pre_act = product(mid_full, up_full) + b_up
    hidden_low = jax.nn.gelu(pre_act, approximate=False).astype(jnp.bfloat16)
    branch = (
        lax.psum_scatter(product(hidden_low, down_full), "chan", scatter_dimension=1, tiled=True)
        + b_down
    )
    output = (residual_stream + branch).astype(jnp.bfloat16)
    grad_f = cotangent.astype(jnp.bfloat16)
    grad_b_down = jnp.sum(grad_f.astype(jnp.float32), axis=0)
    grad_f_full = lax.all_gather(grad_f, "chan", axis=1, tiled=True)
    grad_w_down = product_tn(hidden_low, grad_f_full)
    grad_pre = (product_nt(grad_f_full, down_full) * gelu_slope(pre_act)).astype(jnp.bfloat16)
    grad_b_up = jnp.sum(grad_pre.astype(jnp.float32), axis=0)
    grad_w_up = product_tn(mid_full, grad_pre)
    middle_gradient = lax.psum_scatter(
        product_nt(grad_pre, up_full), "chan", scatter_dimension=1, tiled=True
    )
    second_norm_gain_gradient = jnp.sum(middle_gradient * middle_standardized, axis=0)
    grad_ln2_bias = jnp.sum(middle_gradient, axis=0)
    middle_rescaled = middle_gradient * second_norm_gain
    middle_backward = lax.psum(
        (jnp.sum(middle_rescaled, axis=1), jnp.sum(middle_rescaled * middle_standardized, axis=1)),
        "chan",
    )
    grad_resid = cotangent + middle_inverse_deviation * (
        middle_rescaled
        - middle_backward[0][:, None] / MODEL_WIDTH
        - middle_standardized * middle_backward[1][:, None] / MODEL_WIDTH
    )
    grad_a = (grad_resid * gate_sig).astype(jnp.bfloat16)
    grad_b = (grad_resid * gate_a * gate_sig * (1.0 - gate_sig)).astype(jnp.bfloat16)
    grad_b_a = jnp.sum(grad_a.astype(jnp.float32), axis=0)
    grad_b_b = jnp.sum(grad_b.astype(jnp.float32), axis=0)
    grad_w_a = product_tn(acts_full, grad_a)
    grad_w_b = product_tn(acts_full, grad_b)
    grad_acts = lax.psum_scatter(
        product_nt(grad_a, wa_full) + product_nt(grad_b, wb_full),
        "chan",
        scatter_dimension=1,
        tiled=True,
    )
    grad_mixed = grad_acts * gelu_slope(mixed)
    normalized_gradient, grad_kernel, grad_skip = mix_back(grad_mixed)
    grad_modes, grad_log_dt = kernel_back(grad_kernel)
    first_norm_gain_gradient = jnp.sum(normalized_gradient * input_standardized, axis=0)
    grad_ln1_bias = jnp.sum(normalized_gradient, axis=0)
    input_rescaled = normalized_gradient * first_norm_gain
    input_backward = lax.psum(
        (jnp.sum(input_rescaled, axis=1), jnp.sum(input_rescaled * input_standardized, axis=1)),
        "chan",
    )
    grad_tokens = grad_resid + input_inverse_deviation * (
        input_rescaled
        - input_backward[0][:, None] / MODEL_WIDTH
        - input_standardized * input_backward[1][:, None] / MODEL_WIDTH
    )
    grad_w_a, grad_w_b, grad_w_up, grad_w_down = (
        lax.psum_scatter(grad_w_a, "dp", scatter_dimension=0, tiled=True),
        lax.psum_scatter(grad_w_b, "dp", scatter_dimension=0, tiled=True),
        lax.psum_scatter(grad_w_up, "dp", scatter_dimension=0, tiled=True),
        lax.psum_scatter(grad_w_down, "dp", scatter_dimension=1, tiled=True),
    )
    (
        first_norm_gain_gradient,
        grad_ln1_bias,
        grad_modes,
        grad_log_dt,
        grad_skip,
        grad_b_a,
        grad_b_b,
        second_norm_gain_gradient,
        grad_ln2_bias,
        grad_b_up,
        grad_b_down,
    ) = lax.psum(
        (
            first_norm_gain_gradient,
            grad_ln1_bias,
            grad_modes,
            grad_log_dt,
            grad_skip,
            grad_b_a,
            grad_b_b,
            second_norm_gain_gradient,
            grad_ln2_bias,
            grad_b_up,
            grad_b_down,
        ),
        "dp",
    )
    return (
        output,
        grad_tokens,
        first_norm_gain_gradient,
        grad_ln1_bias,
        grad_modes,
        grad_log_dt,
        grad_skip,
        grad_w_a,
        grad_b_a,
        grad_w_b,
        grad_b_b,
        second_norm_gain_gradient,
        grad_ln2_bias,
        grad_w_up,
        grad_b_up,
        grad_w_down,
        grad_b_down,
    )


LANES = 128
HALF = 64
PAIRS = 4
ROWS = 128
N_CHAN = 8
WIDE = 640
MESH = pl.DeviceIdType.MESH
F32 = jnp.float32
BF16 = jnp.bfloat16


def split_two(matrix):
    high = matrix.astype(ml_dtypes.bfloat16)
    low = (matrix - high.astype(np.float64)).astype(ml_dtypes.bfloat16)
    return np.concatenate([high, low], axis=1)


def lane_rows(values_low, values_high):
    return np.repeat(np.stack([values_low, values_high], -1), HALF, axis=-1)


def mixer_tables():
    line = np.arange(ROWS)
    small = np.outer(line, line) % ROWS * (2.0 * math.pi / ROWS)
    cos_s, sin_s = np.cos(small), np.sin(small)
    forward = np.block([[cos_s, sin_s], [-sin_s, cos_s]])
    real = np.zeros((2 * ROWS, 2 * ROWS))
    for row in range(HALF):
        weight = 1.0 if row == 0 else 2.0
        turn = 2.0 * math.pi / ROWS * row * line
        real[:ROWS, row] = weight * np.cos(turn)
        real[:ROWS, ROWS + row] = -weight * np.sin(turn)
        turn = 2.0 * math.pi / TOK_DEV * (4 + 8 * row) * line
        real[ROWS:, HALF + row] = 2.0 * np.cos(turn)
        real[ROWS:, ROWS + HALF + row] = -2.0 * np.sin(turn)
    mats = np.stack([split_two(m) for m in (forward, forward.T, real, real.T)])

    twiddle = []
    for pair in range(5):
        turn = np.stack([line * k * (math.pi / TOK_DEV) for k in (2 * pair, 2 * pair + 1)])
        twiddle += [lane_rows(np.cos(turn[0]), np.cos(turn[1])), lane_rows(np.sin(turn[0]), np.sin(turn[1]))]
    for first, second in ((1, 2), (3, 0)):
        turn = np.stack([line * k * (2.0 * math.pi / TOK_DEV) for k in (first, second)])
        twiddle += [lane_rows(np.cos(turn[0]), np.cos(turn[1])), lane_rows(np.sin(turn[0]), np.sin(turn[1]))]

    def forward_rows(coef, pairs):
        out = []
        for low, high in pairs:
            for part in range(2):
                for j in range(PAIRS):
                    out.append(lane_rows(coef(2 * j, low, part), coef(2 * j + 1, high, part)))
                for j in range(PAIRS):
                    out.append(lane_rows(coef(2 * j, high, part), coef(2 * j + 1, low, part)))
        return np.stack(out)

    def inverse_rows(coef, pairs):
        out = []
        for low, high in pairs:
            for part in range(2):
                for j in range(PAIRS):
                    out.append(lane_rows(coef(2 * j, low, part), coef(2 * j + 1, high, part)))
                for j in range(PAIRS):
                    out.append(lane_rows(coef(2 * j + 1, low, part), coef(2 * j, high, part)))
        return np.stack(out)

    levels = []
    pairs = [(2 * p, 2 * p + 1) for p in range(5)]
    for level in range(3):
        item = 2 << level

        def angle(block, k):
            return 2.0 * math.pi / 16 * ((block + block // item * item) * k % 16)

        def fwd(block, k, part):
            if k > 8:
                return np.zeros(())
            return np.cos(angle(block, k)) if part == 0 else -np.sin(angle(block, k))

        def inv(block, k, part):
            weight = (1.0 if k in (0, 8) else 2.0) / (2 * TOK_DEV)
            return weight * fwd(block, k, part)

        levels.append(np.concatenate([forward_rows(fwd, pairs), inverse_rows(inv, pairs)]))

    def taps(block, k, part):
        if k == 0:
            return np.asarray((1.0 if part == 0 else (-1.0) ** block) / TOK_DEV)
        turn = 2.0 * math.pi / 8 * (block * k % 8)
        return np.asarray((np.cos(turn) if part == 0 else -np.sin(turn)) * 2.0 / TOK_DEV)

    tap_pairs = [(1, 2), (3, 0)]
    taps_back = forward_rows(taps, tap_pairs)
    taps_rows = inverse_rows(taps, tap_pairs)
    freq_even = np.where(line < HALF, 8 * line, 4 + 8 * (line - HALF))
    half_angle = np.stack(
        [lane_rows(1 + 8 * line, 2 + 8 * line), lane_rows(3 + 8 * line, freq_even)]
    ) * (math.pi / TOK_DEV)
    wave = np.stack([np.cos(half_angle), np.sin(half_angle)])
    return (
        mats,
        np.stack(twiddle).astype(np.float32),
        np.stack(levels).astype(np.float32),
        np.concatenate([levels[2], taps_rows, taps_back]).astype(np.float32),
        wave.astype(np.float32),
    )


def low_lanes(rows):
    return lax.broadcasted_iota(jnp.int32, (rows, LANES), 1) < HALF


def turn_half(values):
    return pltpu.roll(values, HALF, 1)


def split_pair(values):
    upper, lower = values[:HALF], values[HALF:]
    mask = low_lanes(HALF)
    return jnp.where(mask, upper, turn_half(lower)), jnp.where(mask, turn_half(upper), lower)


def join_pair(first, second):
    mask = low_lanes(HALF)
    return jnp.concatenate(
        [jnp.where(mask, first, turn_half(second)), jnp.where(mask, turn_half(first), second)], axis=0
    )


def interleave(first, second):
    mask = low_lanes(first.shape[0])
    return jnp.where(mask, first, turn_half(second)), jnp.where(mask, turn_half(first), second)


def fold(values):
    return values + turn_half(values)


def normal_parts(values):
    cumulative = 0.5 * (1.0 + lax.erf(values * 0.7071067811865476))
    density = jnp.exp(-0.5 * values * values) * 0.3989422804014327
    return cumulative, density


def column_sum(values):
    return jnp.sum(values, axis=0, keepdims=True)


def dot_nt(left, right):
    return lax.dot_general(left, right, (((1,), (1,)), ((), ())), preferred_element_type=F32)


def dot_nn(left, right):
    return jnp.dot(left, right, preferred_element_type=F32)


def store_split(ref, row, lane, values):
    high = values.astype(BF16)
    place = (pl.ds(row, values.shape[0]), pl.ds(lane, values.shape[1]))
    ref[(0,) + place] = high
    ref[(1,) + place] = (values - high.astype(F32)).astype(BF16)


def split_product(mat_ref, which, rhs_ref, lane, width):
    high = mat_ref[which, :, 0:256]
    low = mat_ref[which, :, 256:512]
    rhs_high = rhs_ref[0, :, lane : lane + width]
    return dot_nn(high, rhs_high) + dot_nn(high, rhs_ref[1, :, lane : lane + width]) + dot_nn(low, rhs_high)


CHUNK = 32


def over_chunks(body, size=CHUNK, first=0, rows=ROWS):
    def step(index, carry):
        body(pl.multiple_of(first + index * size, size))
        return carry

    lax.fori_loop(0, rows // size, step, 0)


def spread_pairs(src, coef_ref, base, twiddle_ref, twiddle_base, pairs, rhs_ref):
    def body(row):
        rows = pl.ds(row, CHUNK)
        blocks = [src(j, rows) for j in range(PAIRS)]
        for pair in range(pairs):
            parts = []
            for part in range(2):
                at = base + (pair * 2 + part) * 8
                straight = sum(blocks[j] * coef_ref[at + j : at + j + 1, :] for j in range(PAIRS))
                crossed = sum(blocks[j] * coef_ref[at + 4 + j : at + 5 + j, :] for j in range(PAIRS))
                parts.append(straight + turn_half(crossed))
            cosine = twiddle_ref[twiddle_base + 2 * pair, rows, :]
            sine = twiddle_ref[twiddle_base + 2 * pair + 1, rows, :]
            store_split(rhs_ref, row, pair * LANES, parts[0] * cosine + parts[1] * sine)
            store_split(rhs_ref, row + ROWS, pair * LANES, parts[1] * cosine - parts[0] * sine)

    over_chunks(body)


def gather_pairs(values_ref, coef_ref, base, twiddle_ref, twiddle_base, pairs, store):
    def body(row):
        rows = pl.ds(row, CHUNK)
        straight, crossed = [0.0] * PAIRS, [0.0] * PAIRS
        for pair in range(pairs):
            lanes = slice(pair * LANES, (pair + 1) * LANES)
            real, imag = values_ref[rows, lanes], values_ref[pl.ds(row + ROWS, CHUNK), lanes]
            cosine = twiddle_ref[twiddle_base + 2 * pair, rows, :]
            sine = twiddle_ref[twiddle_base + 2 * pair + 1, rows, :]
            for part, value in enumerate((real * cosine - imag * sine, imag * cosine + real * sine)):
                at = base + (pair * 2 + part) * 8
                for j in range(PAIRS):
                    straight[j] = straight[j] + value * coef_ref[at + j : at + j + 1, :]
                    crossed[j] = crossed[j] + value * coef_ref[at + 4 + j : at + 5 + j, :]
        for j in range(PAIRS):
            store(j, rows, straight[j] + turn_half(crossed[j]))

    over_chunks(body)


GROUPS = ((0, 256), (256, 256), (512, 128))


def transform_into(dst_ref, mat_ref, which, rhs_ref, groups=GROUPS):
    for lane, width in groups:
        dst_ref[:, lane : lane + width] = split_product(mat_ref, which, rhs_ref, lane, width)


def multiply_spectra(left_ref, right_ref, rhs_ref, conjugate):
    def body(row):
        top, bottom = pl.ds(row, CHUNK), pl.ds(row + ROWS, CHUNK)
        for pair in range(5):
            lanes = slice(pair * LANES, (pair + 1) * LANES)
            a_re, a_im = left_ref[top, lanes], left_ref[bottom, lanes]
            b_re, b_im = right_ref[top, lanes], right_ref[bottom, lanes]
            if conjugate:
                out_re, out_im = a_re * b_re + a_im * b_im, a_re * b_im - a_im * b_re
            else:
                out_re, out_im = a_re * b_re - a_im * b_im, a_re * b_im + a_im * b_re
            store_split(rhs_ref, row, pair * LANES, out_re)
            store_split(rhs_ref, row + ROWS, pair * LANES, out_im)

    over_chunks(body)


def pair_terms(modes_ref):
    rank_re, rank_im, in_re, in_im, out_re, out_im = (modes_ref[i] for i in range(2, 8))
    return (
        (out_re * in_re + out_im * in_im, out_re * in_im - out_im * in_re),
        (out_re * rank_re + out_im * rank_im, out_re * rank_im - out_im * rank_re),
        (rank_re * in_re + rank_im * in_im, rank_re * in_im - rank_im * in_re),
        (rank_re * rank_re + rank_im * rank_im, None),
    )


def mode_values(modes_ref):
    index = lax.broadcasted_iota(jnp.int32, modes_ref.shape[1:], 0).astype(F32)
    return -0.5 * jnp.exp(modes_ref[0]), math.pi * (index + modes_ref[1])


POINT_ROWS = 16


def resolvent(coef_ref, n, square_cos, cos_sin, scaled):
    den_re = coef_ref[8, pl.ds(n, 1), :] * square_cos - scaled
    den_im = coef_ref[9, pl.ds(n, 1), :] * cos_sin
    inverse = 1.0 / (den_re * den_re + den_im * den_im)
    return den_re * inverse, -(den_im * inverse)


def complex_multiply(a_re, a_im, b_re, b_im):
    return a_re * b_re - a_im * b_im, a_re * b_im + a_im * b_re


def conj_multiply(a_re, a_im, b_re, b_im):
    return a_re * b_re + a_im * b_im, a_re * b_im - a_im * b_re


def combine(sums, sigma, cosine, sine):
    terms = []
    for p_re, p_im, q_re, q_im in (sums[4 * q : 4 * q + 4] for q in range(4)):
        swing = sigma * sine
        terms.append((-swing * p_im - cosine * q_re, swing * p_re - cosine * q_im))
    twice = 2.0 * cosine
    loop_re, loop_im = 1.0 + twice * terms[3][0], twice * terms[3][1]
    scale = 1.0 / (loop_re * loop_re + loop_im * loop_im)
    inv = (loop_re * scale, -(loop_im * scale))
    ratio = complex_multiply(twice * terms[2][0], twice * terms[2][1], *inv)
    return terms, inv, ratio


QUARTER = 32


def cauchy_coefficients(modes_ref, sigma, coef_ref):
    lam_re, lam_im = mode_values(modes_ref)
    for q, (real, imag) in enumerate(pair_terms(modes_ref)):
        coef_ref[q] = real
        coef_ref[4 + q] = real * lam_re if imag is None else real * lam_re + imag * lam_im
    coef_ref[8] = lam_re * lam_re + lam_im * lam_im
    coef_ref[9] = -2.0 * sigma * lam_re


def wave_rows(wave_ref, pair, base, row):
    rows = pl.ds(pl.multiple_of(base + row, POINT_ROWS), POINT_ROWS)
    return wave_ref[0, pair, rows, :], wave_ref[1, pair, rows, :]


def cauchy_forward(sigma, coef_ref, wave_ref, base, sums_ref, spec_ref, middle):
    sigma_sq = sigma * sigma
    for index in range(4):
        pair, row = index // 2, index % 2 * POINT_ROWS
        rows = slice(row, row + POINT_ROWS)
        lanes = slice(pair * LANES, (pair + 1) * LANES)
        cosine, sine = wave_rows(wave_ref, pair, base, row)
        square_cos, cos_sin, scaled = cosine * cosine, cosine * sine, sigma_sq * (sine * sine)

        def add_mode(n, sums):
            sums = list(sums)
            for k in range(4):
                at = n * 4 + k
                inv_re, inv_im = resolvent(coef_ref, at, square_cos, cos_sin, scaled)
                for q in range(4):
                    plain = coef_ref[q, pl.ds(at, 1), :]
                    turned = coef_ref[4 + q, pl.ds(at, 1), :]
                    sums[4 * q] = sums[4 * q] + plain * inv_re
                    sums[4 * q + 1] = sums[4 * q + 1] + plain * inv_im
                    sums[4 * q + 2] = sums[4 * q + 2] + turned * inv_re
                    sums[4 * q + 3] = sums[4 * q + 3] + turned * inv_im
            return tuple(sums)

        zero = jnp.zeros((POINT_ROWS, LANES), F32)
        sums = lax.fori_loop(0, 8, add_mode, (zero,) * 16)
        for i in range(16):
            sums_ref[pair, i, rows, :] = sums[i]
        terms, _, ratio = combine(sums, sigma, cosine, sine)
        cut_re, cut_im = complex_multiply(*terms[1], *ratio)
        part_re, part_im = terms[0][0] - cut_re, terms[0][1] - cut_im
        spec_re, spec_im = complex_multiply(2.0 * cosine, 2.0 * sine, part_re, part_im)
        spec_ref[rows, lanes] = spec_re
        spec_ref[row + QUARTER : row + QUARTER + POINT_ROWS, lanes] = spec_im
        middle(index)


def cauchy_backward(modes_ref, sigma, nyquist_grad, step, coef_ref, wave_ref, base, sums_ref, spec_ref, grad_ref, back_ref, middle):
    zero = jnp.zeros((POINT_ROWS, LANES), F32)
    sigma_sum = zero
    places = [(pair, row) for pair in range(2) for row in range(0, QUARTER, POINT_ROWS)]
    for pair, row in places:
        rows = slice(row, row + POINT_ROWS)
        lanes = slice(pair * LANES, (pair + 1) * LANES)
        cosine, sine = wave_rows(wave_ref, pair, base, row)
        sums = [sums_ref[pair, i, rows, :] for i in range(16)]
        terms, inv, ratio = combine(sums, sigma, cosine, sine)
        spec_re, spec_im = spec_ref[rows, lanes], spec_ref[row + QUARTER : row + QUARTER + POINT_ROWS, lanes]
        part = conj_multiply(2.0 * cosine, 2.0 * sine, spec_re, spec_im)
        left = conj_multiply(*ratio, *part)
        ratio_grad = conj_multiply(*terms[1], *part)
        back = conj_multiply(*inv, -ratio_grad[0], -ratio_grad[1])
        twice = 2.0 * cosine
        loop = conj_multiply(*ratio, *back)
        grads = (
            part,
            (-left[0], -left[1]),
            (twice * back[0], twice * back[1]),
            (-twice * loop[0], -twice * loop[1]),
        )
        swing = sigma * sine
        for q, (g_re, g_im) in enumerate(grads):
            grad_ref[pair, 4 * q, rows, :] = swing * g_im
            grad_ref[pair, 4 * q + 1, rows, :] = -swing * g_re
            grad_ref[pair, 4 * q + 2, rows, :] = -cosine * g_re
            grad_ref[pair, 4 * q + 3, rows, :] = -cosine * g_im
            sigma_sum = sigma_sum + sine * (g_im * sums[4 * q] - g_re * sums[4 * q + 1])
    sigma_sq = sigma * sigma

    def mode(n, square_sum):
        plain = [coef_ref[q, pl.ds(n, 1), :] for q in range(4)]
        turned = [coef_ref[4 + q, pl.ds(n, 1), :] for q in range(4)]
        sums = [0.0] * 10
        for pair, row in places:
            rows = slice(row, row + POINT_ROWS)
            cosine, sine = wave_rows(wave_ref, pair, base, row)
            square_cos, cos_sin, square_sin = cosine * cosine, cosine * sine, sine * sine
            inv_re, inv_im = resolvent(coef_ref, n, square_cos, cos_sin, sigma_sq * square_sin)
            grad_re, grad_im = 0.0, 0.0
            for q in range(4):
                p_re, p_im = grad_ref[pair, 4 * q, rows, :], grad_ref[pair, 4 * q + 1, rows, :]
                q_re, q_im = grad_ref[pair, 4 * q + 2, rows, :], grad_ref[pair, 4 * q + 3, rows, :]
                grad_re = grad_re + (plain[q] * p_re + turned[q] * q_re)
                grad_im = grad_im + (plain[q] * p_im + turned[q] * q_im)
                sums[q] = sums[q] + (p_re * inv_re + p_im * inv_im)
                sums[4 + q] = sums[4 + q] + (q_re * inv_re + q_im * inv_im)
            square_re = inv_re * inv_re - inv_im * inv_im
            square_im = 2.0 * inv_re * inv_im
            den_re, den_im = conj_multiply(square_re, square_im, grad_re, grad_im)
            sums[8] = sums[8] - den_re * square_cos
            sums[9] = sums[9] - den_im * cos_sin
            square_sum = square_sum + den_re * square_sin
        for i in range(10):
            back_ref[i, pl.ds(n, 1), :] = column_sum(sums[i])
        return square_sum

    square_sum = zero
    for part in range(4):
        square_sum = lax.fori_loop(part * 8, part * 8 + 8, mode, square_sum)
        middle(part)
    plain_grad = [fold(back_ref[q]) for q in range(4)]
    turned_grad = [fold(back_ref[4 + q]) for q in range(4)]
    abs_grad, skew_grad = fold(back_ref[8]), fold(back_ref[9])
    lam_re, lam_im = mode_values(modes_ref)
    plain_grad[0] = plain_grad[0] + step * nyquist_grad
    rank_re, rank_im, in_re, in_im, out_re, out_im = (modes_ref[i] for i in range(2, 8))
    lam_re_grad = 2.0 * lam_re * abs_grad - 2.0 * sigma * skew_grad
    lam_im_grad = 2.0 * lam_im * abs_grad
    real_grad, imag_grad = [], []
    terms = pair_terms(modes_ref)
    for q, (real, imag) in enumerate(terms):
        lam_re_grad = lam_re_grad + turned_grad[q] * real
        if imag is not None:
            lam_im_grad = lam_im_grad + turned_grad[q] * imag
        real_grad.append(plain_grad[q] + turned_grad[q] * lam_re)
        imag_grad.append(turned_grad[q] * lam_im)
    r0, r1, r2, r3 = real_grad
    i0, i1, i2, _ = imag_grad
    grads = (
        lam_re_grad * lam_re,
        math.pi * lam_im_grad,
        r1 * out_re - i1 * out_im + r2 * in_re + i2 * in_im + 2.0 * r3 * rank_re,
        r1 * out_im + i1 * out_re + r2 * in_im - i2 * in_re + 2.0 * r3 * rank_im,
        r0 * out_re - i0 * out_im + r2 * rank_re - i2 * rank_im,
        r0 * out_im + i0 * out_re + r2 * rank_im + i2 * rank_re,
        r0 * in_re + i0 * in_im + r1 * rank_re + i1 * rank_im,
        r0 * in_im - i0 * in_re + r1 * rank_im - i1 * rank_re,
    )
    sigma_grad = (
        fold(column_sum(sigma_sum) + 2.0 * sigma * column_sum(square_sum))
        - 2.0 * column_sum(skew_grad * lam_re)
    )
    nyquist = step * column_sum(terms[0][0])
    return grads, nyquist * nyquist_grad - sigma * sigma_grad


def ring_place(chan):
    z, y = chan // 2, chan % 2
    return z + y * (7 - 2 * z)


def ring_chan(place):
    back = place // 4
    z = place * (1 - back) + (7 - place) * back
    return 2 * z + back


TURNS = (1, -1)
OFFSETS = (0, 1, -1, 2, -2, 3, -3, 4)


def ring_items():
    out = []
    for step in range(1, 5):
        for turn in range(2):
            for block in range(2):
                if step < 4 or block == turn:
                    out.append((turn, step, block))
    return out


def item_slot(turn, step, block):
    return (turn * 4 + step - 1) * 2 + block


def block_kernel(
    bucket_ref, items_ref, tokens_ref, cotangent_ref, gain1_ref, bias1_ref, raw_modes_ref, log_dt_ref, skip_ref,
    wa_ref, ba_ref, wb_ref, bb_ref, gain2_ref, bias2_ref, up_ref, bup_ref, down_ref, bdown_ref,
    levels_ref, coefc_ref, mat_ref, tw_ref, wave_ref,
    out_ref, dtok_ref, gw_ref, gm_ref, gv_ref,
    tok_ref, aux_ref, coefl_ref, modes_ref,
    wab_ref, wup_ref, wdn_ref, gab_w_ref, gup_w_ref, gdn_w_ref,
    sib_ab_ref, sib_up_ref, sib_dn_ref, ring_ab_ref, ring_up_ref, ring_dn_ref, part_ab_ref, part_up_ref, cross_ref,
    in_send, in_recv, head_send, head_recv, acts_send, acts_recv, back_send, back_recv, late_send, late_recv,
    sum_send, sum_recv, tail_send, tail_recv, dp_send, dp_recv, spec_send, spec_recv, sgrad_send, sgrad_recv,
    hat_ref, norm_ref, slope_ref, conv_ref, rhs_ref, freq_ref, sig_ref, ans_ref, taps_ref,
    mcoef_ref, sums_ref, pgrad_ref, mback_ref, sgrad_ref, taps_freq_ref,
    gate_ref, swish_ref, res_ref, hat2_ref, low_ref, branch_ref, back2_ref, gab_ref, hid_ref, gpre_ref, tall_ref,
    gring_ss, gring_rs, gsib_ss, gsib_rs, gx_ss, gx_rs, bring_ss, bring_rs, bsib_ss, bsib_rs, bx_ss, bx_rs,
    rring_ss, rring_rs, rsib_ss, rsib_rs, rx_ss, rx_rs, dring_ss, dring_rs, dx_ss, dx_rs,
    a2a_ss, a2a_rs, dp_ss, dp_rs, spec_ss, spec_rs,
):
    dp, chan = lax.axis_index("dp"), lax.axis_index("chan")
    core = dp % 2
    sibling = dp + 1 - 2 * core
    across = (dp + 2) % 4
    place = ring_place(chan)
    nexts = [ring_chan((place + 1) % 8), ring_chan((place + 7) % 8)]

    def chan_at(offset):
        return ring_chan((place + offset + 8) % 8)

    barrier = pltpu.get_barrier_semaphore()
    for r in range(1, N_CHAN):
        pl.semaphore_signal(barrier, inc=1, device_id={"chan": (chan + r) % N_CHAN}, device_id_type=MESH)
    for r in range(1, 4):
        pl.semaphore_signal(barrier, inc=1, device_id={"dp": (dp + r) % 4}, device_id_type=MESH)
    pl.semaphore_wait(barrier, N_CHAN - 1 + 3)

    pending = []

    def remote(src, dst, send_sem, recv_sem, **device):
        return pltpu.make_async_remote_copy(
            src_ref=src, dst_ref=dst, send_sem=send_sem, recv_sem=recv_sem, device_id=device, device_id_type=MESH
        )

    def send(*args, **device):
        copy = remote(*args, **device)
        copy.start()
        pending.append(copy)

    def exchange(which, source, recv_ref):
        def copy(r):
            peer = (chan + r) % N_CHAN
            return remote(
                source(peer), recv_ref.at[chan], a2a_ss.at[which, r - 1], a2a_rs.at[which, r - 1], chan=peer
            )

        def start():
            for r in range(1, N_CHAN):
                copy(r).start()

        def wait():
            for r in range(1, N_CHAN):
                copy(r).wait_recv()

        def finish():
            for r in range(1, N_CHAN):
                copy(r).wait_send()

        return start, wait, finish

    def row_of(group):
        return pl.multiple_of(group * ROWS, ROWS)

    def block(ref, chan_id, group):
        return ref.at[chan_id, pl.ds(row_of(group), ROWS), :]

    def launch(copy):
        copy.start()
        pending.append(copy)

    mine = (dp, across)
    theirs = (sibling, (sibling + 2) % 4)
    items = ring_items()

    def origin(turn, step):
        return chan_at(-TURNS[turn] * step)

    class Across:
        def __init__(self, which, ref):
            self.which, self.ref = which, ref

        def x_copy(self, group):
            ref = block(self.ref, chan, group)
            return remote(ref, ref, gx_ss.at[self.which], gx_rs.at[self.which], dp=across)

        def ring(self, turn, step, number):
            slot = item_slot(turn, step, number)
            ref = block(self.ref, origin(turn, step - 1), mine[number])
            return remote(ref, ref, gring_ss.at[self.which, slot], gring_rs.at[self.which, slot], chan=nexts[turn])

        def sib(self, chan_id, group, slot):
            ref = block(self.ref, chan_id, group)
            return remote(ref, ref, gsib_ss.at[self.which, slot], gsib_rs.at[self.which, slot], dp=sibling)

        def start(self):
            launch(self.x_copy(dp))
            for turn in range(2):
                launch(self.ring(turn, 1, 0))
            launch(self.sib(chan, mine[0], 16))

        def cross(self):
            self.x_copy(across).wait_recv()
            for turn in range(2):
                launch(self.ring(turn, 1, 1))
            launch(self.sib(chan, mine[1], 17))

        def step(self, step, numbers=(0, 1)):
            for turn, at, number in items:
                if at == step and number in numbers:
                    self.ring(turn, step, number).wait_recv()
                    if (turn, step + 1, number) in items:
                        launch(self.ring(turn, step + 1, number))
                    launch(self.sib(origin(turn, step), mine[number], item_slot(turn, step, number)))

        def arrived(self, offset):
            if offset == 0:
                self.sib(chan, theirs[0], 16).wait_recv()
                self.sib(chan, theirs[1], 17).wait_recv()
            for turn, step, number in items:
                if offset == -TURNS[turn] * step or (step == 4 and offset == 4):
                    self.sib(origin(turn, step), theirs[number], item_slot(turn, step, number)).wait_recv()

    class Along:
        def __init__(self, ref):
            self.ref = ref

        def part(self, turn, step, group):
            ref = self.ref
            if step == 4:
                return ref.at[origin(turn, 4), pl.ds(row_of(group) + turn * HALF, HALF), :]
            return block(ref, origin(turn, step), group)

        def ring(self, turn, step):
            slot = turn * 4 + step - 1
            if step == 4:
                ref = self.ref.at[origin(turn, 3), pl.ds(row_of(dp) + turn * HALF, HALF), :]
            else:
                ref = block(self.ref, origin(turn, step - 1), dp)
            return remote(ref, ref, bring_ss.at[slot], bring_rs.at[slot], chan=nexts[turn])

        def x_copy(self, turn, step, group):
            slot = turn * 4 + step - 1 if step else 8
            ref = self.part(turn, step, group)
            return remote(ref, ref, bx_ss.at[slot], bx_rs.at[slot], dp=across)

        def sib(self, turn, step, groups, number):
            slot = (turn * 4 + step - 1 if step else 8) + 9 * number
            ref = self.part(turn, step, groups[number])
            return remote(ref, ref, bsib_ss.at[slot], bsib_rs.at[slot], dp=sibling)

        def start(self):
            for turn in range(2):
                launch(self.ring(turn, 1))
            launch(self.x_copy(0, 0, dp))
            launch(self.sib(0, 0, mine, 0))

        def step(self, step):
            for turn in range(2):
                self.wait_ring(turn, step)
                if step < 4:
                    launch(self.ring(turn, step + 1))
                launch(self.x_copy(turn, step, dp))
                launch(self.sib(turn, step, mine, 0))

        def wait_ring(self, turn, step):
            slot = turn * 4 + step - 1
            ref = self.part(turn, step, dp)
            remote(ref, ref, bring_ss.at[slot], bring_rs.at[slot], chan=nexts[turn]).wait_recv()

        def cross(self, step):
            for turn in range(2 if step else 1):
                self.x_copy(turn, step, across).wait_recv()
                launch(self.sib(turn, step, mine, 1))

        def arrived(self, offset):
            for turn in range(2 if offset else 1):
                step = -TURNS[turn] * offset if offset != 4 else 4
                if 0 <= step <= 4:
                    for number in range(2):
                        self.sib(turn, step, theirs, number).wait_recv()

    gate_w, up_w, down_w = Across(0, wab_ref), Across(1, wup_ref), Along(wdn_ref)

    def gather_start():
        rows = pl.ds(row_of(dp), ROWS)
        wab_ref[chan, rows, :] = jnp.concatenate([wa_ref[...], wb_ref[...]], axis=0).T.astype(BF16)
        gate_w.start()
        wup_ref[chan, rows, :] = up_ref[...].astype(BF16)
        up_w.start()
        wdn_ref[chan, rows, :] = down_ref[...].T.astype(BF16)
        down_w.start()

    def beside(ref, j):
        start = 2 * j * ROWS
        return jnp.concatenate(
            [ref[:, start : start + ROWS].astype(F32), ref[:, start + ROWS : start + 2 * ROWS].astype(F32)], axis=0
        ).T

    for j in range(PAIRS):
        packed = beside(tokens_ref, j)
        tok_ref[j * ROWS : (j + 1) * ROWS, :] = packed.astype(BF16)
        for first, values in ((0, packed), (HALF, beside(cotangent_ref, j))):
            low, high = split_pair(values)
            in_send[2 * j, first : first + HALF, :] = low.astype(BF16)
            in_send[2 * j + 1, first : first + HALF, :] = high.astype(BF16)
    in_recv[chan] = in_send[chan]

    lane_id = lax.broadcasted_iota(jnp.int32, (8, LANES), 1)
    row_id = lax.broadcasted_iota(jnp.int32, (8, LANES), 0)
    halves = jnp.where((lane_id >= HALF) == (row_id == 1), 1.0, 0.0) * jnp.where(row_id < 2, 1.0, 0.0)
    halves = halves.astype(BF16)

    def token_sums(parts):
        total = 0.0
        for part in parts:
            total = total + dot_nt(halves, part)
        return [total[h : h + 1, j * ROWS : (j + 1) * ROWS] for h in range(2) for j in range(PAIRS)]

    def split(values):
        high = values.astype(BF16)
        return high, (values - high.astype(F32)).astype(BF16)

    tokens = tok_ref[...]
    wide_tokens = tokens.astype(F32)
    for i, sums in enumerate(token_sums([tokens]) + token_sums(split(wide_tokens * wide_tokens))):
        head_send[i : i + 1, :] = sums

    def row(*refs):
        return jnp.concatenate([ref[...].reshape(1, HALF) for ref in refs], axis=1)

    bup = bup_ref[...].reshape(1, 2 * LANES)
    head_send[16:17, :] = row(ba_ref, bb_ref)
    head_send[17:18, :] = row(gain2_ref, bias2_ref)
    head_send[18:19, :] = row(bdown_ref, bdown_ref)
    head_send[19:20, :] = bup[:, :LANES]
    head_send[20:21, :] = bup[:, LANES:]
    head_send[21:24, :] = jnp.zeros((3, LANES), F32)
    head_recv[chan] = head_send[...]
    head = exchange(0, lambda peer: head_send, head_recv)
    inputs = exchange(1, lambda peer: in_send.at[peer], in_recv)
    head[0]()
    gather_start()
    inputs[0]()

    level, filled = bucket_ref[0], items_ref[0]
    coefl_ref[...] = levels_ref[level]
    item_blocks = jnp.where(level == 0, 2, jnp.where(level == 1, 4, 8))
    block_id = 2 * (row_id % PAIRS) + jnp.where(lane_id >= HALF, 1, 0)
    bound = jnp.where(row_id < PAIRS, filled * item_blocks, item_blocks)
    aux_ref[...] = jnp.where(block_id < bound, 1.0, 0.0)
    for i in range(8):
        modes_ref[i] = jnp.concatenate([raw_modes_ref[i], raw_modes_ref[i]], axis=1)
    log_dt = row(log_dt_ref, log_dt_ref)
    sigma, step_size = 2.0 * jnp.exp(-log_dt), jnp.exp(log_dt)

    def after_quarter(quarter):
        if quarter == 1:
            gate_w.cross()
            up_w.cross()
        elif quarter == 3:
            gate_w.step(1)

    base = pl.multiple_of(dp * QUARTER, QUARTER)

    def spec_copy(which, r):
        peer = (dp + r) % 4
        src, dst = ((spec_send, spec_recv), (sgrad_send.at[peer], sgrad_recv))[which]
        return remote(src, dst.at[dp], spec_ss.at[which, r - 1], spec_rs.at[which, r - 1], dp=peer)

    cauchy_coefficients(modes_ref, sigma, mcoef_ref)
    cauchy_forward(sigma, mcoef_ref, wave_ref, base, sums_ref, spec_send, after_quarter)
    spec_recv[dp] = spec_send[...]
    for r in range(1, 4):
        spec_copy(0, r).start()
    down_w.cross(0)
    up_w.step(1, (0,))

    head[1]()
    sums = head_recv[0, 0:16, :]
    for c in range(1, N_CHAN):
        sums = sums + head_recv[c, 0:16, :]
    mean = sums[0:8] * (1.0 / MODEL_WIDTH)
    rstd = lax.rsqrt(sums[8:16] * (1.0 / MODEL_WIDTH) - mean * mean + EPSILON)

    def columns(rows):
        tall = rows.T
        return [jnp.where(low_lanes(ROWS), tall[:, j : j + 1], tall[:, 4 + j : 5 + j]) for j in range(PAIRS)]

    gain1, bias1, skip = row(gain1_ref, gain1_ref), row(bias1_ref, bias1_ref), row(skip_ref, skip_ref)
    mean_cols, rstd_cols = columns(mean), columns(rstd)
    for j in range(PAIRS):
        hat = (tok_ref[j * ROWS : (j + 1) * ROWS, :].astype(F32) - mean_cols[j]) * rstd_cols[j]
        hat_ref[j] = hat
        norm_ref[j] = hat * gain1 + bias1

    down_w.step(1)
    gate_w.step(2)
    spread_pairs(lambda j, rows: norm_ref[j, rows, :], coefl_ref, 0, tw_ref, 0, 5, rhs_ref)
    transform_into(sig_ref, mat_ref, 0, rhs_ref)
    up_w.step(1, (1,))

    for r in range(1, 4):
        spec_copy(0, r).wait_recv()
    for source in range(4):
        store_split(rhs_ref, source * QUARTER, 0, spec_recv[source, :QUARTER, :])
        store_split(rhs_ref, ROWS + source * QUARTER, 0, spec_recv[source, QUARTER:, :])
    freq_ref[:, 0:256] = split_product(mat_ref, 1, rhs_ref, 0, 256)
    even = split_product(mat_ref, 2, rhs_ref, LANES, LANES)
    freq_ref[:, LANES:256] = jnp.where(low_lanes(256), freq_ref[:, LANES:256], even)
    sign = 1.0 - 2.0 * (lax.broadcasted_iota(jnp.int32, (CHUNK, LANES), 0) % 2).astype(F32)
    nyquist = step_size * column_sum(mcoef_ref[0]) * (1.0 / TOK_DEV)

    def store_taps(j, rows, values):
        taps_ref[j, rows, :] = (values + sign * nyquist) * aux_ref[4 + j : 5 + j, :]

    gather_pairs(freq_ref, coefc_ref, 160, tw_ref, 10, 2, store_taps)
    gate_w.step(3)
    down_w.cross(1)
    up_w.step(2, (0,))
    spread_pairs(lambda j, rows: taps_ref[j, rows, :], coefc_ref, 0, tw_ref, 0, 5, rhs_ref)
    transform_into(ans_ref, mat_ref, 0, rhs_ref)

    down_w.step(2)
    gate_w.step(4)
    multiply_spectra(sig_ref, ans_ref, rhs_ref, False)
    transform_into(freq_ref, mat_ref, 1, rhs_ref)

    def store_conv(j, rows, values):
        conv_ref[j, rows, :] = values

    up_w.step(2, (1,))
    gather_pairs(freq_ref, coefl_ref, 80, tw_ref, 0, 5, store_conv)
    down_w.cross(2)
    for j in range(PAIRS):
        mixed = conv_ref[j] * aux_ref[j : j + 1, :] + skip * norm_ref[j]
        cumulative, density = normal_parts(mixed)
        slope_ref[j] = cumulative + mixed * density
        low, high = split_pair(mixed * cumulative)
        acts_send[2 * j] = low.astype(BF16)
        acts_send[2 * j + 1] = high.astype(BF16)
    acts_recv[chan] = acts_send[chan]
    acts = exchange(2, lambda peer: acts_send.at[peer], acts_recv)
    acts[0]()
    down_w.step(3)
    up_w.step(3, (0,))
    inputs[1]()
    acts[1]()

    def joined(ref, pair, first):
        return join_pair(
            ref[2 * pair, first : first + HALF, :].astype(F32), ref[2 * pair + 1, first : first + HALF, :].astype(F32)
        )

    def lanes_of(pair):
        return slice(pair * LANES, (pair + 1) * LANES)

    ACTS, NORM2, GRADF = range(3)
    for p in range(PAIRS):
        low_ref[ACTS, :, lanes_of(p)] = joined(acts_recv, p, 0).astype(BF16)
        low_ref[GRADF, :, lanes_of(p)] = joined(in_recv, p, HALF).astype(BF16)
    for offset in OFFSETS:
        gate_w.arrived(offset)

    def vector(row, first, second):
        return interleave(head_recv[first, 16 + row : 17 + row, :], head_recv[second, 16 + row : 17 + row, :])

    total = 0.0
    for p in range(PAIRS):
        first = dot_nn(low_ref[ACTS], wab_ref[2 * p]) + head_recv[2 * p, 16:17, :]
        second = dot_nn(low_ref[ACTS], wab_ref[2 * p + 1]) + head_recv[2 * p + 1, 16:17, :]
        gate, raw = interleave(first, second)
        swish = lax.logistic(raw)
        gate_ref[p], swish_ref[p] = gate, swish
        resid = joined(in_recv, p, 0) + gate * swish
        res_ref[p] = resid
        total = total + resid
    mean2 = jnp.sum(total, axis=1, keepdims=True) * (1.0 / MODEL_WIDTH)
    total = 0.0
    for p in range(PAIRS):
        centred = res_ref[p] - mean2
        total = total + centred * centred
    rstd2 = lax.rsqrt(jnp.sum(total, axis=1, keepdims=True) * (1.0 / MODEL_WIDTH) + EPSILON)
    gain2 = []
    for p in range(PAIRS):
        gain, bias = vector(1, 2 * p, 2 * p + 1)
        gain2.append(gain)
        hat = (res_ref[p] - mean2) * rstd2
        hat2_ref[p] = hat
        low_ref[NORM2, :, lanes_of(p)] = (hat * gain + bias).astype(BF16)
    branch_ref[...] = jnp.zeros_like(branch_ref)
    back2_ref[...] = jnp.zeros_like(back2_ref)

    def hidden_block(offset):
        c = chan_at(offset)
        bias = jnp.concatenate([head_recv[c, 19:20, :], head_recv[c, 20:21, :]], axis=1)
        pre = dot_nn(low_ref[NORM2], wup_ref[c]) + bias
        cumulative, density = normal_parts(pre)
        hidden = (pre * cumulative).astype(BF16)
        hid_ref[c] = hidden
        grad = dot_nn(low_ref[GRADF], wdn_ref[c]) * (cumulative + pre * density)
        grad = grad.astype(BF16)
        gpre_ref[c] = grad
        sums = column_sum(grad.astype(F32))
        tail_send[c, 3:4, :] = sums[:, 0:LANES]
        tail_send[c, 4:5, :] = sums[:, LANES : 2 * LANES]
        branch_ref[...] += dot_nt(hidden, wdn_ref[c])
        back2_ref[...] += dot_nt(grad, wup_ref[c])

    def hidden_ready(offset):
        up_w.arrived(offset)
        down_w.arrived(offset)
        hidden_block(offset)

    up_w.step(3, (1,))
    hidden_ready(0)
    down_w.cross(3)
    up_w.step(4)
    down_w.step(4)
    for offset in (1, -1, 2, -2):
        hidden_ready(offset)
    down_w.cross(4)
    for offset in (3, -3, 4):
        hidden_ready(offset)

    def offset_of(turn, step):
        return TURNS[turn] * (5 - step)

    def far(offset):
        return 4 if offset == -4 else offset

    class Summed:
        def __init__(self, which, ref, sib_ref):
            self.which, self.ref, self.sib_ref = which, ref, sib_ref

        def sib(self, offset, number):
            slot = (far(offset) + 3) * 2 + number
            return remote(
                block(self.ref, chan_at(offset), theirs[number]), self.sib_ref.at[slot],
                rsib_ss.at[self.which, slot], rsib_rs.at[self.which, slot], dp=sibling,
            )

        def share(self, offset):
            for number in range(2):
                launch(self.sib(offset, number))

        def both(self, offset, number):
            self.sib(offset, number).wait_recv()
            slot = (far(offset) + 3) * 2 + number
            own = self.ref[chan_at(offset), pl.ds(row_of(mine[number]), ROWS), :]
            return own.astype(F32) + self.sib_ref[slot].astype(F32)

    reverse_items = [(turn, 5 - step, number) for turn, step, number in items]

    class AcrossBack(Summed):
        def __init__(self, which, ref, sib_ref, ring_ref, part_ref, lanes):
            super().__init__(which, ref, sib_ref)
            self.ring_ref, self.part_ref, self.lanes = ring_ref, part_ref, lanes

        def ring(self, turn, step, number):
            slot = item_slot(turn, step, number)
            return remote(
                block(self.ref, chan_at(offset_of(turn, step)), mine[number]), self.ring_ref.at[slot],
                rring_ss.at[self.which, slot], rring_rs.at[self.which, slot], chan=nexts[turn],
            )

        def got(self, turn, step, number):
            self.ring(turn, step, number).wait_recv()
            return self.ring_ref[item_slot(turn, step, number)].astype(F32)

        def step(self, step):
            for turn, at, number in reverse_items:
                if at != step:
                    continue
                total = self.both(offset_of(turn, step), number)
                if (turn, step - 1, number) in reverse_items:
                    total = total + self.got(turn, step - 1, number)
                place = pl.ds(row_of(mine[number]), ROWS)
                self.ref[chan_at(offset_of(turn, step)), place, :] = total.astype(BF16)
                launch(self.ring(turn, step, number))

        def x_copy(self):
            return remote(self.part_ref.at[0], self.part_ref.at[1], rx_ss.at[self.which], rx_rs.at[self.which], dp=across)

        def last(self):
            for number in (1, 0):
                total = self.both(0, number)
                for turn in range(2):
                    total = total + self.got(turn, 4, number)
                if number == 1:
                    self.part_ref[0] = total.astype(BF16)
                    launch(self.x_copy())
                else:
                    gw_ref[:, self.lanes] = total

        def finish(self):
            self.x_copy().wait_recv()
            gw_ref[:, self.lanes] += self.part_ref[1].astype(F32)

    class AlongBack(Summed):
        def x_copy(self, offset):
            slot = far(offset) + 3
            return remote(
                block(self.ref, chan_at(offset), across), cross_ref.at[slot], dx_ss.at[slot], dx_rs.at[slot], dp=across
            )

        def cross(self, offset):
            total = self.both(offset, 1)
            self.ref[chan_at(offset), pl.ds(row_of(across), ROWS), :] = total.astype(BF16)
            launch(self.x_copy(offset))

        def ring(self, turn, step):
            slot = turn * 4 + step - 1
            c, row = chan_at(offset_of(turn, step)), row_of(dp)
            if step == 1:
                src = self.ref.at[c, pl.ds(row + turn * HALF, HALF), :]
                dst = ring_dn_ref.at[slot, pl.ds(0, HALF), :]
            else:
                src, dst = self.ref.at[c, pl.ds(row, ROWS), :], ring_dn_ref.at[slot]
            return remote(src, dst, dring_ss.at[slot], dring_rs.at[slot], chan=nexts[turn])

        def whole(self, offset):
            total = self.both(offset, 0)
            self.x_copy(offset).wait_recv()
            return total + cross_ref[far(offset) + 3].astype(F32)

        def store(self, offset, total):
            self.ref[chan_at(offset), pl.ds(row_of(dp), ROWS), :] = total.astype(BF16)

        def step(self, step):
            if step == 1:
                self.store(4, self.whole(4))
                for turn in range(2):
                    launch(self.ring(turn, 1))
                return
            for turn in range(2):
                offset = offset_of(turn, step)
                total = self.whole(offset)
                slot = turn * 4 + step - 2
                self.ring(turn, step - 1).wait_recv()
                if step == 2:
                    got = ring_dn_ref[slot, 0:HALF, :].astype(F32)
                    parts = [total[:HALF], total[HALF:]]
                    parts[turn] = parts[turn] + got
                    total = jnp.concatenate(parts, axis=0)
                else:
                    total = total + ring_dn_ref[slot].astype(F32)
                self.store(offset, total)
                launch(self.ring(turn, step))

        def last(self):
            total = self.whole(0)
            for turn in range(2):
                self.ring(turn, 4).wait_recv()
                total = total + ring_dn_ref[turn * 4 + 3].astype(F32)
            gw_ref[:, 384:640] = total

    gate_g = AcrossBack(0, gab_w_ref, sib_ab_ref, ring_ab_ref, part_ab_ref, slice(0, 128))
    up_g = AcrossBack(1, gup_w_ref, sib_up_ref, ring_up_ref, part_up_ref, slice(128, 384))
    down_g = AlongBack(2, gdn_w_ref, sib_dn_ref)

    def hidden_grads(offset):
        c = chan_at(offset)
        gdn_w_ref[c] = dot_nn(tall_ref[GRADF], hid_ref[c]).astype(BF16)
        down_g.share(offset)
        gup_w_ref[c] = dot_nn(tall_ref[NORM2], gpre_ref[c]).astype(BF16)
        up_g.share(offset)

    def gate_grads(offset):
        c = chan_at(offset)
        gab_w_ref[c] = dot_nn(tall_ref[ACTS], gab_ref[c]).astype(BF16)
        gate_g.share(offset)

    def turn_tall(which):
        tall_ref[which] = low_ref[which].astype(F32).T.astype(BF16)

    turn_tall(GRADF)
    turn_tall(NORM2)
    for offset in (4, 3, -3):
        hidden_grads(offset)
    down_g.cross(4)

    mean_q, mean_qx = 0.0, 0.0
    for p in range(PAIRS):
        grad, hat = back2_ref[:, lanes_of(p)], hat2_ref[p]
        q = grad * gain2[p]
        mean_q = mean_q + q
        mean_qx = mean_qx + q * hat
        gain_grad, bias_grad = interleave(column_sum(grad * hat), column_sum(grad))
        tail_send[2 * p, 1:2, :] = gain_grad
        first, second = interleave(turn_half(column_sum(grad * hat)), turn_half(column_sum(grad)))
        tail_send[2 * p + 1, 1:2, :] = first
    mean_q = jnp.sum(mean_q, axis=1, keepdims=True) * (1.0 / MODEL_WIDTH)
    mean_qx = jnp.sum(mean_qx, axis=1, keepdims=True) * (1.0 / MODEL_WIDTH)
    for p in range(PAIRS):
        hat = hat2_ref[p]
        extra = rstd2 * (back2_ref[:, lanes_of(p)] * gain2[p] - mean_q - hat * mean_qx)
        grad_f = joined(in_recv, p, HALF)
        grad_resid = grad_f + extra
        gate, swish = gate_ref[p], swish_ref[p]
        grad_a = (grad_resid * swish).astype(BF16).astype(F32)
        grad_b = (grad_resid * gate * swish * (1.0 - swish)).astype(BF16).astype(F32)
        first, second = interleave(grad_a, grad_b)
        gab_ref[2 * p] = first.astype(BF16)
        gab_ref[2 * p + 1] = second.astype(BF16)
        tail_send[2 * p, 0:1, :] = column_sum(first)
        tail_send[2 * p + 1, 0:1, :] = column_sum(second)
        low, high = interleave(column_sum(grad_f), column_sum(grad_f))
        tail_send[2 * p, 2:3, :] = low
        tail_send[2 * p + 1, 2:3, :] = high
        low, high = split_pair(extra)
        late_send[2 * p, HALF:, :] = low.astype(BF16)
        late_send[2 * p + 1, HALF:, :] = high.astype(BF16)
    grad_acts = 0.0
    for c in range(N_CHAN):
        grad_acts = grad_acts + dot_nt(gab_ref[c], wab_ref[c])
    for p in range(PAIRS):
        low, high = split_pair(grad_acts[:, lanes_of(p)])
        back_send[2 * p] = low.astype(BF16)
        back_send[2 * p + 1] = high.astype(BF16)
    back_recv[chan] = back_send[chan]
    back = exchange(3, lambda peer: back_send.at[peer], back_recv)
    back[0]()

    up_g.step(1)
    down_g.step(1)
    down_g.cross(3)
    down_g.cross(-3)
    for offset in (2, -2):
        hidden_grads(offset)
    up_g.step(2)
    turn_tall(ACTS)
    for offset in (4, 3, -3):
        gate_grads(offset)
    down_g.cross(2)
    down_g.cross(-2)
    down_g.step(2)
    gate_g.step(1)
    for offset in (1, -1, 0):
        hidden_grads(offset)
    for offset in (2, -2, 1, -1, 0):
        gate_grads(offset)
    gate_g.step(2)
    for offset in (1, -1, 0):
        down_g.cross(offset)
    for p in range(PAIRS):
        out = res_ref[p] + branch_ref[:, lanes_of(p)] + interleave(head_recv[2 * p, 18:19, :], head_recv[2 * p + 1, 18:19, :])[0]
        low, high = split_pair(out)
        late_send[2 * p, :HALF, :] = low.astype(BF16)
        late_send[2 * p + 1, :HALF, :] = high.astype(BF16)
    for c in range(N_CHAN):
        tail_send[c, 5:8, :] = jnp.zeros((3, LANES), F32)
    late_recv[chan] = late_send[chan]
    tail_recv[chan] = tail_send[chan]
    late = exchange(4, lambda peer: late_send.at[peer], late_recv)
    tail = exchange(5, lambda peer: tail_send.at[peer], tail_recv)
    late[0]()
    tail[0]()

    back[1]()
    skip_grad = 0.0
    for j in range(PAIRS):
        grad = joined(back_recv, j, 0) * slope_ref[j]
        slope_ref[j] = grad
        conv_ref[j] = grad * aux_ref[j : j + 1, :]
        skip_grad = skip_grad + column_sum(grad * norm_ref[j])
    spread_pairs(lambda j, rows: conv_ref[j, rows, :], coefl_ref, 0, tw_ref, 0, 5, rhs_ref)
    transform_into(freq_ref, mat_ref, 0, rhs_ref)
    multiply_spectra(sig_ref, freq_ref, rhs_ref, True)
    transform_into(sig_ref, mat_ref, 1, rhs_ref)

    def store_kernel_grad(j, rows, values):
        taps_ref[j, rows, :] = values * aux_ref[4 + j : 5 + j, :]

    gather_pairs(sig_ref, coefc_ref, 80, tw_ref, 0, 5, store_kernel_grad)
    down_g.step(3)
    gate_g.step(3)
    nyquist_grad = 0.0
    for j in range(PAIRS):
        whole_sign = 1.0 - 2.0 * (lax.broadcasted_iota(jnp.int32, (ROWS, LANES), 0) % 2).astype(F32)
        nyquist_grad = nyquist_grad + column_sum(taps_ref[j] * whole_sign)
    nyquist_grad = fold(nyquist_grad) * (1.0 / TOK_DEV)
    spread_pairs(lambda j, rows: taps_ref[j, rows, :], coefc_ref, 192, tw_ref, 10, 2, rhs_ref)
    taps_freq_ref[...] = split_product(mat_ref, 0, rhs_ref, 0, 256)
    even = split_product(mat_ref, 3, rhs_ref, LANES, LANES)
    taps_freq_ref[:, LANES:256] = jnp.where(low_lanes(256), taps_freq_ref[:, LANES:256], even)
    for source in range(4):
        rows = slice(source * QUARTER, (source + 1) * QUARTER)
        sgrad_send[source, :QUARTER, :] = taps_freq_ref[rows, :]
        sgrad_send[source, QUARTER:, :] = taps_freq_ref[ROWS + source * QUARTER : ROWS + (source + 1) * QUARTER, :]
    sgrad_recv[dp] = sgrad_send[dp]
    for r in range(1, 4):
        spec_copy(1, r).start()

    up_g.step(3)
    multiply_spectra(ans_ref, freq_ref, rhs_ref, True)
    transform_into(freq_ref, mat_ref, 1, rhs_ref)
    gather_pairs(freq_ref, coefl_ref, 80, tw_ref, 0, 5, store_conv)
    gain_grad, bias_grad = 0.0, 0.0
    scaled, crossed = [], []
    for j in range(PAIRS):
        grad = conv_ref[j] + skip * slope_ref[j]
        conv_ref[j] = grad
        gain_grad = gain_grad + column_sum(grad * hat_ref[j])
        bias_grad = bias_grad + column_sum(grad)
    conv = conv_ref[...].reshape(PAIRS * ROWS, LANES) * gain1
    for i, sums in enumerate(
        token_sums(split(conv)) + token_sums(split(conv * hat_ref[...].reshape(PAIRS * ROWS, LANES)))
    ):
        sum_send[i : i + 1, :] = sums
    sum_recv[chan] = sum_send[...]
    sums_back = exchange(6, lambda peer: sum_send, sum_recv)
    sums_back[0]()
    down_g.step(4)
    gate_g.step(4)

    for r in range(1, 4):
        spec_copy(1, r).wait_recv()
    sgrad_ref[...] = sgrad_recv[0] + sgrad_recv[1] + sgrad_recv[2] + sgrad_recv[3]

    def after_part(part):
        if part == 1:
            up_g.step(4)
        elif part == 3:
            gate_g.last()
            down_g.last()

    mode_grads, dt_grad = cauchy_backward(
        modes_ref, sigma, nyquist_grad, step_size, mcoef_ref, wave_ref, base, sums_ref, sgrad_ref, pgrad_ref, mback_ref,
        after_part,
    )
    mask = low_lanes(32)
    for i in range(4):
        dp_send[i * 32 : (i + 1) * 32, :] = jnp.where(mask, mode_grads[i], mode_grads[i + 4])
    first = low_lanes(1)
    dp_send[128:129, :] = jnp.where(first, dt_grad, fold(skip_grad))
    dp_send[129:130, :] = jnp.where(first, fold(gain_grad), fold(bias_grad))
    dp_send[130:136, :] = jnp.zeros((6, LANES), F32)
    tail[1]()
    tail_sum = tail_recv[0]
    for c in range(1, N_CHAN):
        tail_sum = tail_sum + tail_recv[c]
    dp_send[136:144, :] = tail_sum
    dp_recv[0] = dp_send[...]

    def dp_copy(r):
        return remote(dp_send, dp_recv.at[r], dp_ss.at[r - 1], dp_rs.at[r - 1], dp=(dp + r) % 4)

    for r in range(1, 4):
        dp_copy(r).start()

    sums_back[1]()
    sums = sum_recv[0]
    for c in range(1, N_CHAN):
        sums = sums + sum_recv[c]
    sums = sums * (1.0 / MODEL_WIDTH)
    rstd_cols, q_cols, qx_cols = columns(rstd), columns(sums[0:8]), columns(sums[8:16])
    late[1]()
    for j in range(PAIRS):
        rows = slice(j * ROWS, (j + 1) * ROWS)
        out_ref[rows, :] = joined(late_recv, j, 0).astype(BF16)
        dtok_ref[rows, :] = joined(late_recv, j, HALF) + rstd_cols[j] * (
            conv_ref[j] * gain1 - q_cols[j] - hat_ref[j] * qx_cols[j]
        )
    up_g.last()
    for r in range(1, 4):
        dp_copy(r).wait_recv()
    total = dp_recv[0] + dp_recv[1] + dp_recv[2] + dp_recv[3]
    gm_ref[...] = total[0:128]
    gv_ref[...] = total[128:144]
    gate_g.finish()
    up_g.finish()
    for copy in pending:
        copy.wait_send()
    for group in (head, inputs, acts, back, late, tail, sums_back):
        group[2]()
    for r in range(1, 4):
        dp_copy(r).wait_send()
        spec_copy(0, r).wait_send()
        spec_copy(1, r).wait_send()


def unpack_kernel(
    out_ref, dtok_ref, gw_ref, gm_ref, gv_ref, cotangent_ref,
    output_ref, tokens_ref, gain1_ref, bias1_ref, modes_ref, dt_ref, skip_ref, wa_ref, ba_ref, wb_ref, bb_ref,
    gain2_ref, bias2_ref, up_ref, bup_ref, down_ref, bdown_ref,
):
    for j in range(PAIRS):
        out = out_ref[j * ROWS : (j + 1) * ROWS, :].astype(F32).T.astype(BF16)
        grad = dtok_ref[j * ROWS : (j + 1) * ROWS, :].T
        for h in range(2):
            lanes, rows = slice((2 * j + h) * ROWS, (2 * j + h + 1) * ROWS), slice(h * HALF, (h + 1) * HALF)
            output_ref[:, lanes] = out[rows]
            tokens_ref[:, lanes] = cotangent_ref[:, lanes] + grad[rows]
    for i in range(8):
        modes_ref[i] = gm_ref[i % 4 * 32 : i % 4 * 32 + 32, i // 4 * HALF : (i // 4 + 1) * HALF]
    gates = gw_ref[:, :LANES].T
    wa_ref[...] = gates[:HALF]
    wb_ref[...] = gates[HALF:]
    up_ref[...] = gw_ref[:, 128:384]
    down_ref[...] = gw_ref[:, 384:640].T
    for at, low, high in (
        (0, dt_ref, skip_ref), (1, gain1_ref, bias1_ref), (8, ba_ref, bb_ref), (9, gain2_ref, bias2_ref),
    ):
        low[...] = gv_ref[at, :HALF]
        high[...] = gv_ref[at, HALF:]
    bdown_ref[...] = gv_ref[10, :HALF]
    bup_ref[:LANES] = gv_ref[11, :]
    bup_ref[LANES:] = gv_ref[12, :]


def block_program():
    mats, twiddle, levels, constant, wave = mixer_tables()

    def run(tokens, cotangent, bucket, items, gain1, bias1, modes, log_dt, skip, w_a, b_a, w_b, b_b, gain2, bias2, w_up, b_up, w_down, b_down):
        vmem = pl.BlockSpec(memory_space=pltpu.VMEM)
        smem = pl.BlockSpec(memory_space=pltpu.SMEM)
        dma = pltpu.SemaphoreType.DMA

        def buf(*shape):
            return pltpu.VMEM(shape, F32)

        def low(*shape):
            return pltpu.VMEM(shape, BF16)

        def full(*shape):
            return jax.ShapeDtypeStruct(shape, F32)

        big, wide = (PAIRS, ROWS, LANES), (256, WIDE)
        packed = pl.pallas_call(
            block_kernel,
            out_shape=(
                jax.ShapeDtypeStruct((512, LANES), BF16), full(512, LANES), full(ROWS, WIDE), full(ROWS, LANES),
                full(16, LANES),
            ),
            in_specs=[smem] * 2 + [vmem] * 22,
            out_specs=(vmem,) * 5,
            scratch_shapes=[
                low(512, LANES), buf(8, LANES), buf(160, LANES), buf(8, 32, LANES),
                low(N_CHAN, 512, 128), low(N_CHAN, 512, 256), low(N_CHAN, 512, 256),
                low(N_CHAN, 512, 128), low(N_CHAN, 512, 256), low(N_CHAN, 512, 256),
                low(16, ROWS, 128), low(16, ROWS, 256), low(16, ROWS, 256),
                low(16, ROWS, 128), low(16, ROWS, 256), low(8, ROWS, 256),
                low(2, ROWS, 128), low(2, ROWS, 256), low(8, ROWS, 256),
                low(N_CHAN, ROWS, LANES), low(N_CHAN, ROWS, LANES), buf(24, LANES), buf(N_CHAN, 24, LANES),
                low(N_CHAN, HALF, LANES), low(N_CHAN, HALF, LANES), low(N_CHAN, HALF, LANES), low(N_CHAN, HALF, LANES),
                low(N_CHAN, ROWS, LANES), low(N_CHAN, ROWS, LANES),
                buf(16, LANES), buf(N_CHAN, 16, LANES), buf(N_CHAN, 8, LANES), buf(N_CHAN, 8, LANES),
                buf(144, LANES), buf(4, 144, LANES), buf(64, 256), buf(4, 64, 256), buf(4, 64, 256), buf(4, 64, 256),
                buf(*big), buf(*big), buf(*big), buf(*big), low(2, *wide), buf(*wide), buf(*wide), buf(*wide), buf(*big),
                buf(10, 32, LANES), buf(2, 16, QUARTER, LANES), buf(2, 16, QUARTER, LANES), buf(10, 32, LANES),
                buf(64, 256), buf(256, 256),
                buf(*big), buf(*big), buf(*big), buf(*big), low(3, ROWS, 512), buf(ROWS, 512), buf(ROWS, 512),
                low(N_CHAN, ROWS, LANES), low(N_CHAN, ROWS, 256), low(N_CHAN, ROWS, 256), low(3, 512, ROWS),
                dma((2, 16)), dma((2, 16)), dma((2, 18)), dma((2, 18)), dma((2,)), dma((2,)),
                dma((8,)), dma((8,)), dma((18,)), dma((18,)), dma((9,)), dma((9,)),
                dma((2, 16)), dma((2, 16)), dma((3, 16)), dma((3, 16)), dma((2,)), dma((2,)),
                dma((8,)), dma((8,)), dma((8,)), dma((8,)),
                dma((7, 7)), dma((7, 7)), dma((3,)), dma((3,)), dma((2, 3)), dma((2, 3)),
            ],
            compiler_params=pltpu.CompilerParams(
                collective_id=0, has_side_effects=True, vmem_limit_bytes=60 * 1024 * 1024
            ),
            name="block",
        )(
            bucket, items, tokens.T, cotangent.T, gain1, bias1, jnp.swapaxes(modes, 1, 2), log_dt, skip,
            w_a.T, b_a, w_b.T, b_b, gain2, bias2,
            w_up, b_up, w_down, b_down, levels, constant, mats, twiddle, wave,
        )
        small = full(HALF)
        results = pl.pallas_call(
            unpack_kernel,
            out_shape=(
                jax.ShapeDtypeStruct((HALF, TOK_DEV), BF16), full(HALF, TOK_DEV), small, small, full(8, 32, HALF),
                small, small, full(HALF, ROWS), small, full(HALF, ROWS), small, small, small, full(ROWS, 256),
                full(256), full(256, ROWS), small,
            ),
            in_specs=[vmem] * 6,
            out_specs=(vmem,) * 17,
            name="unpack",
        )(*packed, cotangent.T)
        turned = {0, 1, 4, 7, 9}
        return tuple(jnp.swapaxes(r, -1, -2) if i in turned else r for i, r in enumerate(results))

    return run


def solution(mesh):
    small = mesh.shape["chan"] == N_CHAN and mesh.shape["dp"] == 4
    return jax.shard_map(
        block_program() if small else shards,
        mesh=mesh,
        in_specs=(
            P("dp", "chan"),
            P("dp", "chan"),
            P("dp"),
            P("dp"),
            P("chan"),
            P("chan"),
            P(None, "chan", None),
            P("chan"),
            P("chan"),
            P("dp", "chan"),
            P("chan"),
            P("dp", "chan"),
            P("chan"),
            P("chan"),
            P("chan"),
            P("dp", "chan"),
            P("chan"),
            P("chan", "dp"),
            P("chan"),
        ),
        out_specs=(
            P("dp", "chan"),
            P("dp", "chan"),
            P("chan"),
            P("chan"),
            P(None, "chan", None),
            P("chan"),
            P("chan"),
            P("dp", "chan"),
            P("chan"),
            P("dp", "chan"),
            P("chan"),
            P("chan"),
            P("chan"),
            P("dp", "chan"),
            P("chan"),
            P("chan", "dp"),
            P("chan"),
        ),
        check_vma=False,
    )
```

```python
import math

import jax
import jax.numpy as jnp
import ml_dtypes
import numpy as np
from jax import lax
from jax.experimental import pallas as pl
from jax.experimental.pallas import tpu as pltpu
from jax.sharding import PartitionSpec as P

MODEL_WIDTH = 512
TOK_DEV = 1024


HIGHEST = lax.Precision.HIGHEST
EPSILON = 1e-05


def product(left, right):
    return jnp.dot(left, right, preferred_element_type=jnp.float32)


def product_nt(left, right):
    return lax.dot_general(
        left, right, (((1,), (1,)), ((), ())), preferred_element_type=jnp.float32
    )


def product_tn(left, right):
    return lax.dot_general(
        left, right, (((0,), (0,)), ((), ())), preferred_element_type=jnp.float32
    )


def gelu_slope(values):
    return (
        0.5 * (1.0 + lax.erf(values * 0.7071067811865476))
        + values * jnp.exp(-0.5 * values * values) * 0.3989422804014327
    )


def half_angles(length):
    angle = np.arange(length // 2 + 1, dtype=np.float64) * (math.pi / length)
    cosine, sine = np.cos(angle), np.sin(angle)
    cosine[-1] = 0.0
    return cosine.astype(np.float32), sine.astype(np.float32)


def inverse_tables(length):
    freq = np.arange(length // 2 + 1)
    turn = (freq[:, None] * np.arange(length)[None, :]) % length * (2.0 * math.pi / length)
    weight = np.where((freq == 0) | (freq == length // 2), 1.0, 2.0)[:, None] / length
    return (weight * np.cos(turn)).astype(np.float32), (weight * np.sin(turn)).astype(np.float32)


def high_einsum(form, left, right):
    return jnp.einsum(form, left, right, precision=HIGHEST)


def ssm_kernel(modes, log_dt):
    cos_h, sin_h = half_angles(TOK_DEV)
    index = jnp.arange(modes.shape[2], dtype=jnp.int32).astype(jnp.float32)
    lam_re = -0.5 * jnp.exp(modes[0])
    lam_im = math.pi * (index + modes[1])
    rank_re, rank_im, in_re, in_im, out_re, out_im = (modes[i] for i in range(2, 8))
    sigma = (2.0 * jnp.exp(-log_dt))[:, None]

    def points(values):
        return values.T[:, None, :]

    den_re = points(lam_re * lam_re + lam_im * lam_im) * (cos_h * cos_h)[:, None] - (
        sigma * sigma
    ).T * (sin_h * sin_h)[:, None]
    den_im = points(-2.0 * sigma * lam_re) * (sin_h * cos_h)[:, None]
    den_sq = den_re * den_re + den_im * den_im
    inv_re = den_re / den_sq
    inv_im = -den_im / den_sq
    sums = []
    for real, imag in (
        (out_re * in_re + out_im * in_im, out_re * in_im - out_im * in_re),
        (out_re * rank_re + out_im * rank_im, out_re * rank_im - out_im * rank_re),
        (rank_re * in_re + rank_im * in_im, rank_re * in_im - rank_im * in_re),
        (rank_re * rank_re + rank_im * rank_im, jnp.zeros_like(rank_re)),
    ):
        turned = points(real * lam_re + imag * lam_im)
        real = points(real)
        p_re, p_im = jnp.sum(real * inv_re, axis=0), jnp.sum(real * inv_im, axis=0)
        q_re, q_im = jnp.sum(turned * inv_re, axis=0), jnp.sum(turned * inv_im, axis=0)
        sine = sin_h[:, None] * sigma.T
        sums.append((-sine * p_im - cos_h[:, None] * q_re, sine * p_re - cos_h[:, None] * q_im))
    (cross_re, cross_im), (left_re, left_im), (right_re, right_im), (self_re, self_im) = sums
    twice = 2.0 * cos_h[:, None]
    loop_re, loop_im = 1.0 + twice * self_re, twice * self_im
    back_re, back_im = twice * right_re, twice * right_im
    loop_sq = loop_re * loop_re + loop_im * loop_im
    ratio_re = (back_re * loop_re + back_im * loop_im) / loop_sq
    ratio_im = (back_im * loop_re - back_re * loop_im) / loop_sq
    part_re = cross_re - (left_re * ratio_re - left_im * ratio_im)
    part_im = cross_im - (left_re * ratio_im + left_im * ratio_re)
    spec_re = 2.0 * (cos_h[:, None] * part_re - sin_h[:, None] * part_im)
    spec_im = 2.0 * (cos_h[:, None] * part_im + sin_h[:, None] * part_re)
    cos_tab, sin_tab = inverse_tables(TOK_DEV)
    return high_einsum("kl,kc->lc", cos_tab, spec_re) - high_einsum("kl,kc->lc", sin_tab, spec_im)


BLOCK = 128
BLOCKS = TOK_DEV // BLOCK
FIRST = 2 * BLOCKS
KEPT = FIRST // 2 + 1


def transform_tables():
    length = 2 * TOK_DEV
    turn = np.arange(KEPT)[:, None] * np.arange(BLOCK)[None, :] * (2.0 * math.pi / length)
    small = np.arange(BLOCK)[:, None] * np.arange(BLOCK)[None, :] % BLOCK * (2.0 * math.pi / BLOCK)
    spots = np.stack([np.arange(BLOCKS) + np.arange(BLOCKS) // (2 << b) * (2 << b) for b in range(3)])
    angle = spots[:, None, :] * np.arange(KEPT)[None, :, None] % FIRST * (2.0 * math.pi / FIRST)
    parts = (np.cos(turn), np.sin(turn), np.cos(small), np.sin(small), np.cos(angle), np.sin(angle))
    return [part.astype(np.float32) for part in parts]


def forward_transform(blocks, cos_a, sin_a):
    cos_t, sin_t, cos_s, sin_s, _, _ = transform_tables()
    step_re = high_einsum("ka,abc->kbc", cos_a, blocks)
    step_im = -high_einsum("ka,abc->kbc", sin_a, blocks)
    turned_re = step_re * cos_t[..., None] + step_im * sin_t[..., None]
    turned_im = step_im * cos_t[..., None] - step_re * sin_t[..., None]
    both = jnp.concatenate([turned_re, turned_im], axis=1)
    matrix = np.block([[cos_s, sin_s], [-sin_s, cos_s]])
    return high_einsum("pb,kbc->kpc", matrix, both)


def inverse_transform(spectrum, cos_a, sin_a):
    cos_t, sin_t, cos_s, sin_s, _, _ = transform_tables()
    matrix = np.block([[cos_s, -sin_s], [sin_s, cos_s]])
    both = high_einsum("bp,kpc->kbc", matrix, spectrum)
    step_re, step_im = both[:, :BLOCK], both[:, BLOCK:]
    turned_re = step_re * cos_t[..., None] - step_im * sin_t[..., None]
    turned_im = step_im * cos_t[..., None] + step_re * sin_t[..., None]
    weight = np.where(np.arange(KEPT) % (KEPT - 1) == 0, 1.0, 2.0).astype(np.float32) / (2 * TOK_DEV)
    return high_einsum("ka,kbc->abc", cos_a * weight[:, None], turned_re) - high_einsum(
        "ka,kbc->abc", sin_a * weight[:, None], turned_im
    )


def multiply(left, right):
    left_re, left_im = left[:, :BLOCK], left[:, BLOCK:]
    right_re, right_im = right[:, :BLOCK], right[:, BLOCK:]
    return jnp.concatenate(
        [left_re * right_re - left_im * right_im, left_re * right_im + left_im * right_re], axis=1
    )


def mixer(normed, kernel_taps, skip_gain, bucket, filled):
    _, _, _, _, cos_a, sin_a = transform_tables()
    cos_x, sin_x = jnp.asarray(cos_a)[bucket], jnp.asarray(sin_a)[bucket]
    item_blocks = 2 << bucket
    block_id = jnp.arange(BLOCKS, dtype=jnp.int32)[:, None, None]
    taps = jnp.where(block_id < item_blocks, kernel_taps.reshape(BLOCKS, BLOCK, -1), 0.0)
    signal = forward_transform(normed.reshape(BLOCKS, BLOCK, -1), cos_x, sin_x)
    answer = forward_transform(taps, cos_a[2], sin_a[2])
    result = inverse_transform(multiply(signal, answer), cos_x, sin_x)
    result = jnp.where(block_id < filled * item_blocks, result, 0.0)
    return result.reshape(normed.shape) + skip_gain * normed


def shards(
    tokens,
    cotangent,
    group_bucket,
    group_items,
    first_norm_gain,
    first_norm_bias,
    modes,
    log_dt,
    d_skip,
    w_a,
    b_a,
    w_b,
    b_b,
    second_norm_gain,
    second_norm_bias,
    w_up,
    b_up,
    w_down,
    b_down,
):
    input_tokens = tokens.astype(jnp.float32)
    sums_in = lax.psum(
        (jnp.sum(input_tokens, axis=1), jnp.sum(input_tokens * input_tokens, axis=1)), "chan"
    )
    input_average = sums_in[0][:, None] / MODEL_WIDTH
    input_inverse_deviation = lax.rsqrt(
        sums_in[1][:, None] / MODEL_WIDTH - input_average * input_average + EPSILON
    )
    input_standardized = (input_tokens - input_average) * input_inverse_deviation
    input_normalized = input_standardized * first_norm_gain + first_norm_bias
    level = group_bucket[0]
    filled = group_items[0]
    kernel_taps, kernel_back = jax.vjp(ssm_kernel, modes, log_dt)

    def local_mix(values, taps_now, skip_gain):
        return mixer(values, taps_now, skip_gain, level, filled)

    mixed, mix_back = jax.vjp(local_mix, input_normalized, kernel_taps, d_skip)
    acts_low = jax.nn.gelu(mixed, approximate=False).astype(jnp.bfloat16)
    wa_full, wb_full, up_full, down_full = (
        lax.all_gather(w_a.astype(jnp.bfloat16), "dp", axis=0, tiled=True),
        lax.all_gather(w_b.astype(jnp.bfloat16), "dp", axis=0, tiled=True),
        lax.all_gather(w_up.astype(jnp.bfloat16), "dp", axis=0, tiled=True),
        lax.all_gather(w_down.astype(jnp.bfloat16), "dp", axis=1, tiled=True),
    )
    acts_full = lax.all_gather(acts_low, "chan", axis=1, tiled=True)
    gate_a = product(acts_full, wa_full) + b_a
    gate_b = product(acts_full, wb_full) + b_b
    gate_sig = jax.nn.sigmoid(gate_b)
    residual_stream = input_tokens + gate_a * gate_sig
    sums_mid = lax.psum(
        (jnp.sum(residual_stream, axis=1), jnp.sum(residual_stream * residual_stream, axis=1)),
        "chan",
    )
    middle_average = sums_mid[0][:, None] / MODEL_WIDTH
    middle_inverse_deviation = lax.rsqrt(
        sums_mid[1][:, None] / MODEL_WIDTH - middle_average * middle_average + EPSILON
    )
    middle_standardized = (residual_stream - middle_average) * middle_inverse_deviation
    middle_reduced = (middle_standardized * second_norm_gain + second_norm_bias).astype(
        jnp.bfloat16
    )
    mid_full = lax.all_gather(middle_reduced, "chan", axis=1, tiled=True)
    pre_act = product(mid_full, up_full) + b_up
    hidden_low = jax.nn.gelu(pre_act, approximate=False).astype(jnp.bfloat16)
    branch = (
        lax.psum_scatter(product(hidden_low, down_full), "chan", scatter_dimension=1, tiled=True)
        + b_down
    )
    output = (residual_stream + branch).astype(jnp.bfloat16)
    grad_f = cotangent.astype(jnp.bfloat16)
    grad_b_down = jnp.sum(grad_f.astype(jnp.float32), axis=0)
    grad_f_full = lax.all_gather(grad_f, "chan", axis=1, tiled=True)
    grad_w_down = product_tn(hidden_low, grad_f_full)
    grad_pre = (product_nt(grad_f_full, down_full) * gelu_slope(pre_act)).astype(jnp.bfloat16)
    grad_b_up = jnp.sum(grad_pre.astype(jnp.float32), axis=0)
    grad_w_up = product_tn(mid_full, grad_pre)
    middle_gradient = lax.psum_scatter(
        product_nt(grad_pre, up_full), "chan", scatter_dimension=1, tiled=True
    )
    second_norm_gain_gradient = jnp.sum(middle_gradient * middle_standardized, axis=0)
    grad_ln2_bias = jnp.sum(middle_gradient, axis=0)
    middle_rescaled = middle_gradient * second_norm_gain
    middle_backward = lax.psum(
        (jnp.sum(middle_rescaled, axis=1), jnp.sum(middle_rescaled * middle_standardized, axis=1)),
        "chan",
    )
    grad_resid = cotangent + middle_inverse_deviation * (
        middle_rescaled
        - middle_backward[0][:, None] / MODEL_WIDTH
        - middle_standardized * middle_backward[1][:, None] / MODEL_WIDTH
    )
    grad_a = (grad_resid * gate_sig).astype(jnp.bfloat16)
    grad_b = (grad_resid * gate_a * gate_sig * (1.0 - gate_sig)).astype(jnp.bfloat16)
    grad_b_a = jnp.sum(grad_a.astype(jnp.float32), axis=0)
    grad_b_b = jnp.sum(grad_b.astype(jnp.float32), axis=0)
    grad_w_a = product_tn(acts_full, grad_a)
    grad_w_b = product_tn(acts_full, grad_b)
    grad_acts = lax.psum_scatter(
        product_nt(grad_a, wa_full) + product_nt(grad_b, wb_full),
        "chan",
        scatter_dimension=1,
        tiled=True,
    )
    grad_mixed = grad_acts * gelu_slope(mixed)
    normalized_gradient, grad_kernel, grad_skip = mix_back(grad_mixed)
    grad_modes, grad_log_dt = kernel_back(grad_kernel)
    first_norm_gain_gradient = jnp.sum(normalized_gradient * input_standardized, axis=0)
    grad_ln1_bias = jnp.sum(normalized_gradient, axis=0)
    input_rescaled = normalized_gradient * first_norm_gain
    input_backward = lax.psum(
        (jnp.sum(input_rescaled, axis=1), jnp.sum(input_rescaled * input_standardized, axis=1)),
        "chan",
    )
    grad_tokens = grad_resid + input_inverse_deviation * (
        input_rescaled
        - input_backward[0][:, None] / MODEL_WIDTH
        - input_standardized * input_backward[1][:, None] / MODEL_WIDTH
    )
    grad_w_a, grad_w_b, grad_w_up, grad_w_down = (
        lax.psum_scatter(grad_w_a, "dp", scatter_dimension=0, tiled=True),
        lax.psum_scatter(grad_w_b, "dp", scatter_dimension=0, tiled=True),
        lax.psum_scatter(grad_w_up, "dp", scatter_dimension=0, tiled=True),
        lax.psum_scatter(grad_w_down, "dp", scatter_dimension=1, tiled=True),
    )
    (
        first_norm_gain_gradient,
        grad_ln1_bias,
        grad_modes,
        grad_log_dt,
        grad_skip,
        grad_b_a,
        grad_b_b,
        second_norm_gain_gradient,
        grad_ln2_bias,
        grad_b_up,
        grad_b_down,
    ) = lax.psum(
        (
            first_norm_gain_gradient,
            grad_ln1_bias,
            grad_modes,
            grad_log_dt,
            grad_skip,
            grad_b_a,
            grad_b_b,
            second_norm_gain_gradient,
            grad_ln2_bias,
            grad_b_up,
            grad_b_down,
        ),
        "dp",
    )
    return (
        output,
        grad_tokens,
        first_norm_gain_gradient,
        grad_ln1_bias,
        grad_modes,
        grad_log_dt,
        grad_skip,
        grad_w_a,
        grad_b_a,
        grad_w_b,
        grad_b_b,
        second_norm_gain_gradient,
        grad_ln2_bias,
        grad_w_up,
        grad_b_up,
        grad_w_down,
        grad_b_down,
    )


LANES = 128
HALF = 64
PAIRS = 4
ROWS = 128
N_CHAN = 8
WIDE = 640
MESH = pl.DeviceIdType.MESH
F32 = jnp.float32
BF16 = jnp.bfloat16


def split_two(matrix):
    high = matrix.astype(ml_dtypes.bfloat16)
    low = (matrix - high.astype(np.float64)).astype(ml_dtypes.bfloat16)
    return np.concatenate([high, low], axis=1)


def lane_rows(values_low, values_high):
    return np.repeat(np.stack([values_low, values_high], -1), HALF, axis=-1)


def mixer_tables():
    line = np.arange(ROWS)
    small = np.outer(line, line) % ROWS * (2.0 * math.pi / ROWS)
    cos_s, sin_s = np.cos(small), np.sin(small)
    forward = np.block([[cos_s, sin_s], [-sin_s, cos_s]])
    real = np.zeros((2 * ROWS, 2 * ROWS))
    for row in range(HALF):
        weight = 1.0 if row == 0 else 2.0
        turn = 2.0 * math.pi / ROWS * row * line
        real[:ROWS, row] = weight * np.cos(turn)
        real[:ROWS, ROWS + row] = -weight * np.sin(turn)
        turn = 2.0 * math.pi / TOK_DEV * (4 + 8 * row) * line
        real[ROWS:, HALF + row] = 2.0 * np.cos(turn)
        real[ROWS:, ROWS + HALF + row] = -2.0 * np.sin(turn)
    mats = np.stack([split_two(m) for m in (forward, forward.T, real, real.T)])

    twiddle = []
    for pair in range(5):
        turn = np.stack([line * k * (math.pi / TOK_DEV) for k in (2 * pair, 2 * pair + 1)])
        twiddle += [lane_rows(np.cos(turn[0]), np.cos(turn[1])), lane_rows(np.sin(turn[0]), np.sin(turn[1]))]
    for first, second in ((1, 2), (3, 0)):
        turn = np.stack([line * k * (2.0 * math.pi / TOK_DEV) for k in (first, second)])
        twiddle += [lane_rows(np.cos(turn[0]), np.cos(turn[1])), lane_rows(np.sin(turn[0]), np.sin(turn[1]))]

    def forward_rows(coef, pairs):
        out = []
        for low, high in pairs:
            for part in range(2):
                for j in range(PAIRS):
                    out.append(lane_rows(coef(2 * j, low, part), coef(2 * j + 1, high, part)))
                for j in range(PAIRS):
                    out.append(lane_rows(coef(2 * j, high, part), coef(2 * j + 1, low, part)))
        return np.stack(out)

    def inverse_rows(coef, pairs):
        out = []
        for low, high in pairs:
            for part in range(2):
                for j in range(PAIRS):
                    out.append(lane_rows(coef(2 * j, low, part), coef(2 * j + 1, high, part)))
                for j in range(PAIRS):
                    out.append(lane_rows(coef(2 * j + 1, low, part), coef(2 * j, high, part)))
        return np.stack(out)

    levels = []
    pairs = [(2 * p, 2 * p + 1) for p in range(5)]
    for level in range(3):
        item = 2 << level

        def angle(block, k):
            return 2.0 * math.pi / 16 * ((block + block // item * item) * k % 16)

        def fwd(block, k, part):
            if k > 8:
                return np.zeros(())
            return np.cos(angle(block, k)) if part == 0 else -np.sin(angle(block, k))

        def inv(block, k, part):
            weight = (1.0 if k in (0, 8) else 2.0) / (2 * TOK_DEV)
            return weight * fwd(block, k, part)

        levels.append(np.concatenate([forward_rows(fwd, pairs), inverse_rows(inv, pairs)]))

    def taps(block, k, part):
        if k == 0:
            return np.asarray((1.0 if part == 0 else (-1.0) ** block) / TOK_DEV)
        turn = 2.0 * math.pi / 8 * (block * k % 8)
        return np.asarray((np.cos(turn) if part == 0 else -np.sin(turn)) * 2.0 / TOK_DEV)

    tap_pairs = [(1, 2), (3, 0)]
    taps_back = forward_rows(taps, tap_pairs)
    taps_rows = inverse_rows(taps, tap_pairs)
    freq_even = np.where(line < HALF, 8 * line, 4 + 8 * (line - HALF))
    half_angle = np.stack(
        [lane_rows(1 + 8 * line, 2 + 8 * line), lane_rows(3 + 8 * line, freq_even)]
    ) * (math.pi / TOK_DEV)
    wave = np.stack([np.cos(half_angle), np.sin(half_angle)])
    return (
        mats,
        np.stack(twiddle).astype(np.float32),
        np.stack(levels).astype(np.float32),
        np.concatenate([levels[2], taps_rows, taps_back]).astype(np.float32),
        wave.astype(np.float32),
    )


def low_lanes(rows):
    return lax.broadcasted_iota(jnp.int32, (rows, LANES), 1) < HALF


def turn_half(values):
    return pltpu.roll(values, HALF, 1)


def split_pair(values):
    upper, lower = values[:HALF], values[HALF:]
    mask = low_lanes(HALF)
    return jnp.where(mask, upper, turn_half(lower)), jnp.where(mask, turn_half(upper), lower)


def join_pair(first, second):
    mask = low_lanes(HALF)
    return jnp.concatenate(
        [jnp.where(mask, first, turn_half(second)), jnp.where(mask, turn_half(first), second)], axis=0
    )


def interleave(first, second):
    mask = low_lanes(first.shape[0])
    return jnp.where(mask, first, turn_half(second)), jnp.where(mask, turn_half(first), second)


def fold(values):
    return values + turn_half(values)


def normal_parts(values):
    cumulative = 0.5 * (1.0 + lax.erf(values * 0.7071067811865476))
    density = jnp.exp(-0.5 * values * values) * 0.3989422804014327
    return cumulative, density


def column_sum(values):
    return jnp.sum(values, axis=0, keepdims=True)


def dot_nt(left, right):
    return lax.dot_general(left, right, (((1,), (1,)), ((), ())), preferred_element_type=F32)


def dot_nn(left, right):
    return jnp.dot(left, right, preferred_element_type=F32)


def store_split(ref, row, lane, values):
    high = values.astype(BF16)
    place = (pl.ds(row, values.shape[0]), pl.ds(lane, values.shape[1]))
    ref[(0,) + place] = high
    ref[(1,) + place] = (values - high.astype(F32)).astype(BF16)


def split_product(mat_ref, which, rhs_ref, lane, width):
    high = mat_ref[which, :, 0:256]
    low = mat_ref[which, :, 256:512]
    rhs_high = rhs_ref[0, :, lane : lane + width]
    return dot_nn(high, rhs_high) + dot_nn(high, rhs_ref[1, :, lane : lane + width]) + dot_nn(low, rhs_high)


CHUNK = 32


def over_chunks(body, size=CHUNK, first=0, rows=ROWS):
    def step(index, carry):
        body(pl.multiple_of(first + index * size, size))
        return carry

    lax.fori_loop(0, rows // size, step, 0)


def spread_pairs(src, coef_ref, base, twiddle_ref, twiddle_base, pairs, rhs_ref):
    def body(row):
        rows = pl.ds(row, CHUNK)
        blocks = [src(j, rows) for j in range(PAIRS)]
        for pair in range(pairs):
            parts = []
            for part in range(2):
                at = base + (pair * 2 + part) * 8
                straight = sum(blocks[j] * coef_ref[at + j : at + j + 1, :] for j in range(PAIRS))
                crossed = sum(blocks[j] * coef_ref[at + 4 + j : at + 5 + j, :] for j in range(PAIRS))
                parts.append(straight + turn_half(crossed))
            cosine = twiddle_ref[twiddle_base + 2 * pair, rows, :]
            sine = twiddle_ref[twiddle_base + 2 * pair + 1, rows, :]
            store_split(rhs_ref, row, pair * LANES, parts[0] * cosine + parts[1] * sine)
            store_split(rhs_ref, row + ROWS, pair * LANES, parts[1] * cosine - parts[0] * sine)

    over_chunks(body)


def gather_pairs(values_ref, coef_ref, base, twiddle_ref, twiddle_base, pairs, store):
    def body(row):
        rows = pl.ds(row, CHUNK)
        straight, crossed = [0.0] * PAIRS, [0.0] * PAIRS
        for pair in range(pairs):
            lanes = slice(pair * LANES, (pair + 1) * LANES)
            real, imag = values_ref[rows, lanes], values_ref[pl.ds(row + ROWS, CHUNK), lanes]
            cosine = twiddle_ref[twiddle_base + 2 * pair, rows, :]
            sine = twiddle_ref[twiddle_base + 2 * pair + 1, rows, :]
            for part, value in enumerate((real * cosine - imag * sine, imag * cosine + real * sine)):
                at = base + (pair * 2 + part) * 8
                for j in range(PAIRS):
                    straight[j] = straight[j] + value * coef_ref[at + j : at + j + 1, :]
                    crossed[j] = crossed[j] + value * coef_ref[at + 4 + j : at + 5 + j, :]
        for j in range(PAIRS):
            store(j, rows, straight[j] + turn_half(crossed[j]))

    over_chunks(body)


GROUPS = ((0, 256), (256, 256), (512, 128))


def transform_into(dst_ref, mat_ref, which, rhs_ref, groups=GROUPS):
    for lane, width in groups:
        dst_ref[:, lane : lane + width] = split_product(mat_ref, which, rhs_ref, lane, width)


def multiply_spectra(left_ref, right_ref, rhs_ref, conjugate):
    def body(row):
        top, bottom = pl.ds(row, CHUNK), pl.ds(row + ROWS, CHUNK)
        for pair in range(5):
            lanes = slice(pair * LANES, (pair + 1) * LANES)
            a_re, a_im = left_ref[top, lanes], left_ref[bottom, lanes]
            b_re, b_im = right_ref[top, lanes], right_ref[bottom, lanes]
            if conjugate:
                out_re, out_im = a_re * b_re + a_im * b_im, a_re * b_im - a_im * b_re
            else:
                out_re, out_im = a_re * b_re - a_im * b_im, a_re * b_im + a_im * b_re
            store_split(rhs_ref, row, pair * LANES, out_re)
            store_split(rhs_ref, row + ROWS, pair * LANES, out_im)

    over_chunks(body)


def pair_terms(modes_ref):
    rank_re, rank_im, in_re, in_im, out_re, out_im = (modes_ref[i] for i in range(2, 8))
    return (
        (out_re * in_re + out_im * in_im, out_re * in_im - out_im * in_re),
        (out_re * rank_re + out_im * rank_im, out_re * rank_im - out_im * rank_re),
        (rank_re * in_re + rank_im * in_im, rank_re * in_im - rank_im * in_re),
        (rank_re * rank_re + rank_im * rank_im, None),
    )


def mode_values(modes_ref):
    index = lax.broadcasted_iota(jnp.int32, modes_ref.shape[1:], 0).astype(F32)
    return -0.5 * jnp.exp(modes_ref[0]), math.pi * (index + modes_ref[1])


POINT_ROWS = 16


def resolvent(coef_ref, n, square_cos, cos_sin, scaled):
    den_re = coef_ref[8, pl.ds(n, 1), :] * square_cos - scaled
    den_im = coef_ref[9, pl.ds(n, 1), :] * cos_sin
    inverse = 1.0 / (den_re * den_re + den_im * den_im)
    return den_re * inverse, -(den_im * inverse)


def complex_multiply(a_re, a_im, b_re, b_im):
    return a_re * b_re - a_im * b_im, a_re * b_im + a_im * b_re


def conj_multiply(a_re, a_im, b_re, b_im):
    return a_re * b_re + a_im * b_im, a_re * b_im - a_im * b_re


def combine(sums, sigma, cosine, sine):
    terms = []
    for p_re, p_im, q_re, q_im in (sums[4 * q : 4 * q + 4] for q in range(4)):
        swing = sigma * sine
        terms.append((-swing * p_im - cosine * q_re, swing * p_re - cosine * q_im))
    twice = 2.0 * cosine
    loop_re, loop_im = 1.0 + twice * terms[3][0], twice * terms[3][1]
    scale = 1.0 / (loop_re * loop_re + loop_im * loop_im)
    inv = (loop_re * scale, -(loop_im * scale))
    ratio = complex_multiply(twice * terms[2][0], twice * terms[2][1], *inv)
    return terms, inv, ratio


QUARTER = 32


def cauchy_coefficients(modes_ref, sigma, coef_ref):
    lam_re, lam_im = mode_values(modes_ref)
    for q, (real, imag) in enumerate(pair_terms(modes_ref)):
        coef_ref[q] = real
        coef_ref[4 + q] = real * lam_re if imag is None else real * lam_re + imag * lam_im
    coef_ref[8] = lam_re * lam_re + lam_im * lam_im
    coef_ref[9] = -2.0 * sigma * lam_re


def wave_rows(wave_ref, pair, base, row):
    rows = pl.ds(pl.multiple_of(base + row, POINT_ROWS), POINT_ROWS)
    return wave_ref[0, pair, rows, :], wave_ref[1, pair, rows, :]


def cauchy_forward(sigma, coef_ref, wave_ref, base, sums_ref, spec_ref, middle):
    sigma_sq = sigma * sigma
    for index in range(4):
        pair, row = index // 2, index % 2 * POINT_ROWS
        rows = slice(row, row + POINT_ROWS)
        lanes = slice(pair * LANES, (pair + 1) * LANES)
        cosine, sine = wave_rows(wave_ref, pair, base, row)
        square_cos, cos_sin, scaled = cosine * cosine, cosine * sine, sigma_sq * (sine * sine)

        def add_mode(n, sums):
            sums = list(sums)
            for k in range(4):
                at = n * 4 + k
                inv_re, inv_im = resolvent(coef_ref, at, square_cos, cos_sin, scaled)
                for q in range(4):
                    plain = coef_ref[q, pl.ds(at, 1), :]
                    turned = coef_ref[4 + q, pl.ds(at, 1), :]
                    sums[4 * q] = sums[4 * q] + plain * inv_re
                    sums[4 * q + 1] = sums[4 * q + 1] + plain * inv_im
                    sums[4 * q + 2] = sums[4 * q + 2] + turned * inv_re
                    sums[4 * q + 3] = sums[4 * q + 3] + turned * inv_im
            return tuple(sums)

        zero = jnp.zeros((POINT_ROWS, LANES), F32)
        sums = lax.fori_loop(0, 8, add_mode, (zero,) * 16)
        for i in range(16):
            sums_ref[pair, i, rows, :] = sums[i]
        terms, _, ratio = combine(sums, sigma, cosine, sine)
        cut_re, cut_im = complex_multiply(*terms[1], *ratio)
        part_re, part_im = terms[0][0] - cut_re, terms[0][1] - cut_im
        spec_re, spec_im = complex_multiply(2.0 * cosine, 2.0 * sine, part_re, part_im)
        spec_ref[rows, lanes] = spec_re
        spec_ref[row + QUARTER : row + QUARTER + POINT_ROWS, lanes] = spec_im
        middle(index)


def cauchy_backward(modes_ref, sigma, nyquist_grad, step, coef_ref, wave_ref, base, sums_ref, spec_ref, grad_ref, back_ref, middle):
    zero = jnp.zeros((POINT_ROWS, LANES), F32)
    sigma_sum = zero
    places = [(pair, row) for pair in range(2) for row in range(0, QUARTER, POINT_ROWS)]
    for pair, row in places:
        rows = slice(row, row + POINT_ROWS)
        lanes = slice(pair * LANES, (pair + 1) * LANES)
        cosine, sine = wave_rows(wave_ref, pair, base, row)
        sums = [sums_ref[pair, i, rows, :] for i in range(16)]
        terms, inv, ratio = combine(sums, sigma, cosine, sine)
        spec_re, spec_im = spec_ref[rows, lanes], spec_ref[row + QUARTER : row + QUARTER + POINT_ROWS, lanes]
        part = conj_multiply(2.0 * cosine, 2.0 * sine, spec_re, spec_im)
        left = conj_multiply(*ratio, *part)
        ratio_grad = conj_multiply(*terms[1], *part)
        back = conj_multiply(*inv, -ratio_grad[0], -ratio_grad[1])
        twice = 2.0 * cosine
        loop = conj_multiply(*ratio, *back)
        grads = (
            part,
            (-left[0], -left[1]),
            (twice * back[0], twice * back[1]),
            (-twice * loop[0], -twice * loop[1]),
        )
        swing = sigma * sine
        for q, (g_re, g_im) in enumerate(grads):
            grad_ref[pair, 4 * q, rows, :] = swing * g_im
            grad_ref[pair, 4 * q + 1, rows, :] = -swing * g_re
            grad_ref[pair, 4 * q + 2, rows, :] = -cosine * g_re
            grad_ref[pair, 4 * q + 3, rows, :] = -cosine * g_im
            sigma_sum = sigma_sum + sine * (g_im * sums[4 * q] - g_re * sums[4 * q + 1])
    sigma_sq = sigma * sigma

    def mode(n, square_sum):
        plain = [coef_ref[q, pl.ds(n, 1), :] for q in range(4)]
        turned = [coef_ref[4 + q, pl.ds(n, 1), :] for q in range(4)]
        sums = [0.0] * 10
        for pair, row in places:
            rows = slice(row, row + POINT_ROWS)
            cosine, sine = wave_rows(wave_ref, pair, base, row)
            square_cos, cos_sin, square_sin = cosine * cosine, cosine * sine, sine * sine
            inv_re, inv_im = resolvent(coef_ref, n, square_cos, cos_sin, sigma_sq * square_sin)
            grad_re, grad_im = 0.0, 0.0
            for q in range(4):
                p_re, p_im = grad_ref[pair, 4 * q, rows, :], grad_ref[pair, 4 * q + 1, rows, :]
                q_re, q_im = grad_ref[pair, 4 * q + 2, rows, :], grad_ref[pair, 4 * q + 3, rows, :]
                grad_re = grad_re + (plain[q] * p_re + turned[q] * q_re)
                grad_im = grad_im + (plain[q] * p_im + turned[q] * q_im)
                sums[q] = sums[q] + (p_re * inv_re + p_im * inv_im)
                sums[4 + q] = sums[4 + q] + (q_re * inv_re + q_im * inv_im)
            square_re = inv_re * inv_re - inv_im * inv_im
            square_im = 2.0 * inv_re * inv_im
            den_re, den_im = conj_multiply(square_re, square_im, grad_re, grad_im)
            sums[8] = sums[8] - den_re * square_cos
            sums[9] = sums[9] - den_im * cos_sin
            square_sum = square_sum + den_re * square_sin
        for i in range(10):
            back_ref[i, pl.ds(n, 1), :] = column_sum(sums[i])
        return square_sum

    square_sum = zero
    for part in range(4):
        square_sum = lax.fori_loop(part * 8, part * 8 + 8, mode, square_sum)
        middle(part)
    plain_grad = [fold(back_ref[q]) for q in range(4)]
    turned_grad = [fold(back_ref[4 + q]) for q in range(4)]
    abs_grad, skew_grad = fold(back_ref[8]), fold(back_ref[9])
    lam_re, lam_im = mode_values(modes_ref)
    plain_grad[0] = plain_grad[0] + step * nyquist_grad
    rank_re, rank_im, in_re, in_im, out_re, out_im = (modes_ref[i] for i in range(2, 8))
    lam_re_grad = 2.0 * lam_re * abs_grad - 2.0 * sigma * skew_grad
    lam_im_grad = 2.0 * lam_im * abs_grad
    real_grad, imag_grad = [], []
    terms = pair_terms(modes_ref)
    for q, (real, imag) in enumerate(terms):
        lam_re_grad = lam_re_grad + turned_grad[q] * real
        if imag is not None:
            lam_im_grad = lam_im_grad + turned_grad[q] * imag
        real_grad.append(plain_grad[q] + turned_grad[q] * lam_re)
        imag_grad.append(turned_grad[q] * lam_im)
    r0, r1, r2, r3 = real_grad
    i0, i1, i2, _ = imag_grad
    grads = (
        lam_re_grad * lam_re,
        math.pi * lam_im_grad,
        r1 * out_re - i1 * out_im + r2 * in_re + i2 * in_im + 2.0 * r3 * rank_re,
        r1 * out_im + i1 * out_re + r2 * in_im - i2 * in_re + 2.0 * r3 * rank_im,
        r0 * out_re - i0 * out_im + r2 * rank_re - i2 * rank_im,
        r0 * out_im + i0 * out_re + r2 * rank_im + i2 * rank_re,
        r0 * in_re + i0 * in_im + r1 * rank_re + i1 * rank_im,
        r0 * in_im - i0 * in_re + r1 * rank_im - i1 * rank_re,
    )
    sigma_grad = (
        fold(column_sum(sigma_sum) + 2.0 * sigma * column_sum(square_sum))
        - 2.0 * column_sum(skew_grad * lam_re)
    )
    nyquist = step * column_sum(terms[0][0])
    return grads, nyquist * nyquist_grad - sigma * sigma_grad


def ring_place(chan):
    z, y = lax.div(chan, 2), lax.rem(chan, 2)
    return z + y * (7 - 2 * z)


def ring_chan(place):
    back = lax.div(place, 4)
    z = place * (1 - back) + (7 - place) * back
    return 2 * z + back


TURNS = (1, -1)
OFFSETS = (0, 1, -1, 2, -2, 3, -3, 4)


def ring_items():
    out = []
    for step in range(1, 5):
        for turn in range(2):
            for block in range(2):
                if step < 4 or block == turn:
                    out.append((turn, step, block))
    return out


def item_slot(turn, step, block):
    return (turn * 4 + step - 1) * 2 + block


def block_kernel(
    bucket_ref, items_ref, tokens_ref, cotangent_ref, gain1_ref, bias1_ref, raw_modes_ref, log_dt_ref, skip_ref,
    wa_ref, ba_ref, wb_ref, bb_ref, gain2_ref, bias2_ref, up_ref, bup_ref, down_ref, bdown_ref,
    levels_ref, coefc_ref, mat_ref, tw_ref, wave_ref,
    out_ref, dtok_ref, gw_ref, gm_ref, gv_ref,
    tok_ref, aux_ref, coefl_ref, modes_ref,
    wab_ref, wup_ref, wdn_ref, gab_w_ref, gup_w_ref, gdn_w_ref,
    sib_ab_ref, sib_up_ref, sib_dn_ref, ring_ab_ref, ring_up_ref, ring_dn_ref, part_ab_ref, part_up_ref, cross_ref,
    in_send, in_recv, head_send, head_recv, acts_send, acts_recv, back_send, back_recv, late_send, late_recv,
    sum_send, sum_recv, tail_send, tail_recv, dp_send, dp_recv, spec_send, spec_recv, sgrad_send, sgrad_recv,
    hat_ref, norm_ref, slope_ref, conv_ref, rhs_ref, freq_ref, sig_ref, ans_ref, taps_ref,
    mcoef_ref, sums_ref, pgrad_ref, mback_ref, sgrad_ref, taps_freq_ref,
    gate_ref, swish_ref, res_ref, hat2_ref, low_ref, branch_ref, back2_ref, gab_ref, hid_ref, gpre_ref, tall_ref,
    gring_ss, gring_rs, gsib_ss, gsib_rs, gx_ss, gx_rs, bring_ss, bring_rs, bsib_ss, bsib_rs, bx_ss, bx_rs,
    rring_ss, rring_rs, rsib_ss, rsib_rs, rx_ss, rx_rs, dring_ss, dring_rs, dx_ss, dx_rs,
    a2a_ss, a2a_rs, dp_ss, dp_rs, spec_ss, spec_rs,
):
    dp, chan = lax.axis_index("dp"), lax.axis_index("chan")
    core = lax.rem(dp, 2)
    sibling = dp + 1 - 2 * core
    place = ring_place(chan)
    around = [ring_chan(lax.rem(place + offset, 8)) if offset else chan for offset in range(8)]
    nexts = [around[1], around[7]]
    chan_peers = [chan] + [lax.rem(chan + r, N_CHAN) for r in range(1, N_CHAN)]
    dp_peers = [dp] + [lax.rem(dp + r, 4) for r in range(1, 4)]
    across = dp_peers[2]

    def chan_at(offset):
        return around[offset % 8]

    barrier = pltpu.get_barrier_semaphore()
    for r in range(1, N_CHAN):
        pl.semaphore_signal(barrier, inc=1, device_id={"chan": chan_peers[r]}, device_id_type=MESH)
    for r in range(1, 4):
        pl.semaphore_signal(barrier, inc=1, device_id={"dp": dp_peers[r]}, device_id_type=MESH)
    pl.semaphore_wait(barrier, N_CHAN - 1 + 3)

    pending = []

    def remote(src, dst, send_sem, recv_sem, **device):
        return pltpu.make_async_remote_copy(
            src_ref=src, dst_ref=dst, send_sem=send_sem, recv_sem=recv_sem, device_id=device, device_id_type=MESH
        )

    def send(*args, **device):
        copy = remote(*args, **device)
        copy.start()
        pending.append(copy)

    def exchange(which, source, recv_ref):
        def copy(r):
            peer = chan_peers[r]
            return remote(
                source(peer), recv_ref.at[chan], a2a_ss.at[which, r - 1], a2a_rs.at[which, r - 1], chan=peer
            )

        def start():
            for r in range(1, N_CHAN):
                copy(r).start()

        def wait():
            for r in range(1, N_CHAN):
                copy(r).wait_recv()

        def finish():
            for r in range(1, N_CHAN):
                copy(r).wait_send()

        return start, wait, finish

    def row_of(group):
        return pl.multiple_of(group * ROWS, ROWS)

    def block(ref, chan_id, group):
        return ref.at[chan_id, pl.ds(row_of(group), ROWS), :]

    def launch(copy):
        copy.start()
        pending.append(copy)

    mine = (dp, across)
    theirs = (sibling, lax.rem(sibling + 2, 4))
    items = ring_items()

    def origin(turn, step):
        return chan_at(-TURNS[turn] * step)

    class Across:
        def __init__(self, which, ref):
            self.which, self.ref = which, ref

        def x_copy(self, group):
            ref = block(self.ref, chan, group)
            return remote(ref, ref, gx_ss.at[self.which], gx_rs.at[self.which], dp=across)

        def ring(self, turn, step, number):
            slot = item_slot(turn, step, number)
            ref = block(self.ref, origin(turn, step - 1), mine[number])
            return remote(ref, ref, gring_ss.at[self.which, slot], gring_rs.at[self.which, slot], chan=nexts[turn])

        def sib(self, chan_id, group, slot):
            ref = block(self.ref, chan_id, group)
            return remote(ref, ref, gsib_ss.at[self.which, slot], gsib_rs.at[self.which, slot], dp=sibling)

        def start(self):
            launch(self.x_copy(dp))
            for turn in range(2):
                launch(self.ring(turn, 1, 0))
            launch(self.sib(chan, mine[0], 16))

        def cross(self):
            self.x_copy(across).wait_recv()
            for turn in range(2):
                launch(self.ring(turn, 1, 1))
            launch(self.sib(chan, mine[1], 17))

        def step(self, step, numbers=(0, 1)):
            for turn, at, number in items:
                if at == step and number in numbers:
                    self.ring(turn, step, number).wait_recv()
                    if (turn, step + 1, number) in items:
                        launch(self.ring(turn, step + 1, number))
                    launch(self.sib(origin(turn, step), mine[number], item_slot(turn, step, number)))

        def arrived(self, offset):
            if offset == 0:
                self.sib(chan, theirs[0], 16).wait_recv()
                self.sib(chan, theirs[1], 17).wait_recv()
            for turn, step, number in items:
                if offset == -TURNS[turn] * step or (step == 4 and offset == 4):
                    self.sib(origin(turn, step), theirs[number], item_slot(turn, step, number)).wait_recv()

    class Along:
        def __init__(self, ref):
            self.ref = ref

        def part(self, turn, step, group):
            ref = self.ref
            if step == 4:
                return ref.at[origin(turn, 4), pl.ds(row_of(group) + turn * HALF, HALF), :]
            return block(ref, origin(turn, step), group)

        def ring(self, turn, step):
            slot = turn * 4 + step - 1
            if step == 4:
                ref = self.ref.at[origin(turn, 3), pl.ds(row_of(dp) + turn * HALF, HALF), :]
            else:
                ref = block(self.ref, origin(turn, step - 1), dp)
            return remote(ref, ref, bring_ss.at[slot], bring_rs.at[slot], chan=nexts[turn])

        def x_copy(self, turn, step, group):
            slot = turn * 4 + step - 1 if step else 8
            ref = self.part(turn, step, group)
            return remote(ref, ref, bx_ss.at[slot], bx_rs.at[slot], dp=across)

        def sib(self, turn, step, groups, number):
            slot = (turn * 4 + step - 1 if step else 8) + 9 * number
            ref = self.part(turn, step, groups[number])
            return remote(ref, ref, bsib_ss.at[slot], bsib_rs.at[slot], dp=sibling)

        def start(self):
            for turn in range(2):
                launch(self.ring(turn, 1))
            launch(self.x_copy(0, 0, dp))
            launch(self.sib(0, 0, mine, 0))

        def step(self, step):
            for turn in range(2):
                self.wait_ring(turn, step)
                if step < 4:
                    launch(self.ring(turn, step + 1))
                launch(self.x_copy(turn, step, dp))
                launch(self.sib(turn, step, mine, 0))

        def wait_ring(self, turn, step):
            slot = turn * 4 + step - 1
            ref = self.part(turn, step, dp)
            remote(ref, ref, bring_ss.at[slot], bring_rs.at[slot], chan=nexts[turn]).wait_recv()

        def cross(self, step):
            for turn in range(2 if step else 1):
                self.x_copy(turn, step, across).wait_recv()
                launch(self.sib(turn, step, mine, 1))

        def arrived(self, offset):
            for turn in range(2 if offset else 1):
                step = -TURNS[turn] * offset if offset != 4 else 4
                if 0 <= step <= 4:
                    for number in range(2):
                        self.sib(turn, step, theirs, number).wait_recv()

    gate_w, up_w, down_w = Across(0, wab_ref), Across(1, wup_ref), Along(wdn_ref)

    def gather_start():
        rows = pl.ds(row_of(dp), ROWS)
        wab_ref[chan, rows, :] = jnp.concatenate([wa_ref[...], wb_ref[...]], axis=0).T.astype(BF16)
        gate_w.start()
        wup_ref[chan, rows, :] = up_ref[...].astype(BF16)
        up_w.start()
        wdn_ref[chan, rows, :] = down_ref[...].T.astype(BF16)
        down_w.start()

    def beside(ref, j):
        start = 2 * j * ROWS
        return jnp.concatenate(
            [ref[:, start : start + ROWS].astype(F32), ref[:, start + ROWS : start + 2 * ROWS].astype(F32)], axis=0
        ).T

    for j in range(PAIRS):
        packed = beside(tokens_ref, j)
        tok_ref[j * ROWS : (j + 1) * ROWS, :] = packed.astype(BF16)
        for first, values in ((0, packed), (HALF, beside(cotangent_ref, j))):
            low, high = split_pair(values)
            in_send[2 * j, first : first + HALF, :] = low.astype(BF16)
            in_send[2 * j + 1, first : first + HALF, :] = high.astype(BF16)
    in_recv[chan] = in_send[chan]

    lane_id = lax.broadcasted_iota(jnp.int32, (8, LANES), 1)
    row_id = lax.broadcasted_iota(jnp.int32, (8, LANES), 0)
    halves = jnp.where((lane_id >= HALF) == (row_id == 1), 1.0, 0.0) * jnp.where(row_id < 2, 1.0, 0.0)
    halves = halves.astype(BF16)

    def token_sums(parts):
        total = 0.0
        for part in parts:
            total = total + dot_nt(halves, part)
        return [total[h : h + 1, j * ROWS : (j + 1) * ROWS] for h in range(2) for j in range(PAIRS)]

    def split(values):
        high = values.astype(BF16)
        return high, (values - high.astype(F32)).astype(BF16)

    tokens = tok_ref[...]
    wide_tokens = tokens.astype(F32)
    for i, sums in enumerate(token_sums([tokens]) + token_sums(split(wide_tokens * wide_tokens))):
        head_send[i : i + 1, :] = sums

    def row(*refs):
        return jnp.concatenate([ref[...].reshape(1, HALF) for ref in refs], axis=1)

    bup = bup_ref[...].reshape(1, 2 * LANES)
    head_send[16:17, :] = row(ba_ref, bb_ref)
    head_send[17:18, :] = row(gain2_ref, bias2_ref)
    head_send[18:19, :] = row(bdown_ref, bdown_ref)
    head_send[19:20, :] = bup[:, :LANES]
    head_send[20:21, :] = bup[:, LANES:]
    head_send[21:24, :] = jnp.zeros((3, LANES), F32)
    head_recv[chan] = head_send[...]
    head = exchange(0, lambda peer: head_send, head_recv)
    inputs = exchange(1, lambda peer: in_send.at[peer], in_recv)
    head[0]()
    gather_start()
    inputs[0]()

    level, filled = bucket_ref[0], items_ref[0]
    coefl_ref[...] = levels_ref[level]
    item_blocks = jnp.where(level == 0, 2, jnp.where(level == 1, 4, 8))
    block_id = 2 * (row_id % PAIRS) + jnp.where(lane_id >= HALF, 1, 0)
    bound = jnp.where(row_id < PAIRS, filled * item_blocks, item_blocks)
    aux_ref[...] = jnp.where(block_id < bound, 1.0, 0.0)
    for i in range(8):
        modes_ref[i] = jnp.concatenate([raw_modes_ref[i], raw_modes_ref[i]], axis=1)
    log_dt = row(log_dt_ref, log_dt_ref)
    sigma, step_size = 2.0 * jnp.exp(-log_dt), jnp.exp(log_dt)

    def after_quarter(quarter):
        if quarter == 1:
            gate_w.cross()
            up_w.cross()
        elif quarter == 3:
            gate_w.step(1)

    base = pl.multiple_of(dp * QUARTER, QUARTER)

    def spec_copy(which, r):
        peer = dp_peers[r]
        src, dst = ((spec_send, spec_recv), (sgrad_send.at[peer], sgrad_recv))[which]
        return remote(src, dst.at[dp], spec_ss.at[which, r - 1], spec_rs.at[which, r - 1], dp=peer)

    cauchy_coefficients(modes_ref, sigma, mcoef_ref)
    cauchy_forward(sigma, mcoef_ref, wave_ref, base, sums_ref, spec_send, after_quarter)
    spec_recv[dp] = spec_send[...]
    for r in range(1, 4):
        spec_copy(0, r).start()
    down_w.cross(0)
    up_w.step(1, (0,))

    head[1]()
    sums = head_recv[0, 0:16, :]
    for c in range(1, N_CHAN):
        sums = sums + head_recv[c, 0:16, :]
    mean = sums[0:8] * (1.0 / MODEL_WIDTH)
    rstd = lax.rsqrt(sums[8:16] * (1.0 / MODEL_WIDTH) - mean * mean + EPSILON)

    def columns(rows):
        tall = rows.T
        return [jnp.where(low_lanes(ROWS), tall[:, j : j + 1], tall[:, 4 + j : 5 + j]) for j in range(PAIRS)]

    gain1, bias1, skip = row(gain1_ref, gain1_ref), row(bias1_ref, bias1_ref), row(skip_ref, skip_ref)
    mean_cols, rstd_cols = columns(mean), columns(rstd)
    for j in range(PAIRS):
        hat = (tok_ref[j * ROWS : (j + 1) * ROWS, :].astype(F32) - mean_cols[j]) * rstd_cols[j]
        hat_ref[j] = hat
        norm_ref[j] = hat * gain1 + bias1

    down_w.step(1)
    gate_w.step(2)
    spread_pairs(lambda j, rows: norm_ref[j, rows, :], coefl_ref, 0, tw_ref, 0, 5, rhs_ref)
    transform_into(sig_ref, mat_ref, 0, rhs_ref)
    up_w.step(1, (1,))

    for r in range(1, 4):
        spec_copy(0, r).wait_recv()
    for source in range(4):
        store_split(rhs_ref, source * QUARTER, 0, spec_recv[source, :QUARTER, :])
        store_split(rhs_ref, ROWS + source * QUARTER, 0, spec_recv[source, QUARTER:, :])
    freq_ref[:, 0:256] = split_product(mat_ref, 1, rhs_ref, 0, 256)
    even = split_product(mat_ref, 2, rhs_ref, LANES, LANES)
    freq_ref[:, LANES:256] = jnp.where(low_lanes(256), freq_ref[:, LANES:256], even)
    sign = 1.0 - 2.0 * (lax.broadcasted_iota(jnp.int32, (CHUNK, LANES), 0) % 2).astype(F32)
    nyquist = step_size * column_sum(mcoef_ref[0]) * (1.0 / TOK_DEV)

    def store_taps(j, rows, values):
        taps_ref[j, rows, :] = (values + sign * nyquist) * aux_ref[4 + j : 5 + j, :]

    gather_pairs(freq_ref, coefc_ref, 160, tw_ref, 10, 2, store_taps)
    gate_w.step(3)
    down_w.cross(1)
    up_w.step(2, (0,))
    spread_pairs(lambda j, rows: taps_ref[j, rows, :], coefc_ref, 0, tw_ref, 0, 5, rhs_ref)
    transform_into(ans_ref, mat_ref, 0, rhs_ref)

    down_w.step(2)
    gate_w.step(4)
    multiply_spectra(sig_ref, ans_ref, rhs_ref, False)
    transform_into(freq_ref, mat_ref, 1, rhs_ref)

    def store_conv(j, rows, values):
        conv_ref[j, rows, :] = values

    up_w.step(2, (1,))
    gather_pairs(freq_ref, coefl_ref, 80, tw_ref, 0, 5, store_conv)
    down_w.cross(2)
    for j in range(PAIRS):
        mixed = conv_ref[j] * aux_ref[j : j + 1, :] + skip * norm_ref[j]
        cumulative, density = normal_parts(mixed)
        slope_ref[j] = cumulative + mixed * density
        low, high = split_pair(mixed * cumulative)
        acts_send[2 * j] = low.astype(BF16)
        acts_send[2 * j + 1] = high.astype(BF16)
    acts_recv[chan] = acts_send[chan]
    acts = exchange(2, lambda peer: acts_send.at[peer], acts_recv)
    acts[0]()
    down_w.step(3)
    up_w.step(3, (0,))
    inputs[1]()
    acts[1]()

    def joined(ref, pair, first):
        return join_pair(
            ref[2 * pair, first : first + HALF, :].astype(F32), ref[2 * pair + 1, first : first + HALF, :].astype(F32)
        )

    def lanes_of(pair):
        return slice(pair * LANES, (pair + 1) * LANES)

    ACTS, NORM2, GRADF = range(3)
    for p in range(PAIRS):
        low_ref[ACTS, :, lanes_of(p)] = joined(acts_recv, p, 0).astype(BF16)
        low_ref[GRADF, :, lanes_of(p)] = joined(in_recv, p, HALF).astype(BF16)
    for offset in OFFSETS:
        gate_w.arrived(offset)

    def vector(row, first, second):
        return interleave(head_recv[first, 16 + row : 17 + row, :], head_recv[second, 16 + row : 17 + row, :])

    total = 0.0
    for p in range(PAIRS):
        first = dot_nn(low_ref[ACTS], wab_ref[2 * p]) + head_recv[2 * p, 16:17, :]
        second = dot_nn(low_ref[ACTS], wab_ref[2 * p + 1]) + head_recv[2 * p + 1, 16:17, :]
        gate, raw = interleave(first, second)
        swish = lax.logistic(raw)
        gate_ref[p], swish_ref[p] = gate, swish
        resid = joined(in_recv, p, 0) + gate * swish
        res_ref[p] = resid
        total = total + resid
    mean2 = jnp.sum(total, axis=1, keepdims=True) * (1.0 / MODEL_WIDTH)
    total = 0.0
    for p in range(PAIRS):
        centred = res_ref[p] - mean2
        total = total + centred * centred
    rstd2 = lax.rsqrt(jnp.sum(total, axis=1, keepdims=True) * (1.0 / MODEL_WIDTH) + EPSILON)
    gain2 = []
    for p in range(PAIRS):
        gain, bias = vector(1, 2 * p, 2 * p + 1)
        gain2.append(gain)
        hat = (res_ref[p] - mean2) * rstd2
        hat2_ref[p] = hat
        low_ref[NORM2, :, lanes_of(p)] = (hat * gain + bias).astype(BF16)
    branch_ref[...] = jnp.zeros_like(branch_ref)
    back2_ref[...] = jnp.zeros_like(back2_ref)

    def hidden_block(offset):
        c = chan_at(offset)
        bias = jnp.concatenate([head_recv[c, 19:20, :], head_recv[c, 20:21, :]], axis=1)
        pre = dot_nn(low_ref[NORM2], wup_ref[c]) + bias
        cumulative, density = normal_parts(pre)
        hidden = (pre * cumulative).astype(BF16)
        hid_ref[c] = hidden
        grad = dot_nn(low_ref[GRADF], wdn_ref[c]) * (cumulative + pre * density)
        grad = grad.astype(BF16)
        gpre_ref[c] = grad
        sums = column_sum(grad.astype(F32))
        tail_send[c, 3:4, :] = sums[:, 0:LANES]
        tail_send[c, 4:5, :] = sums[:, LANES : 2 * LANES]
        branch_ref[...] += dot_nt(hidden, wdn_ref[c])
        back2_ref[...] += dot_nt(grad, wup_ref[c])

    def hidden_ready(offset):
        up_w.arrived(offset)
        down_w.arrived(offset)
        hidden_block(offset)

    up_w.step(3, (1,))
    hidden_ready(0)
    down_w.cross(3)
    up_w.step(4)
    down_w.step(4)
    for offset in (1, -1, 2, -2):
        hidden_ready(offset)
    down_w.cross(4)
    for offset in (3, -3, 4):
        hidden_ready(offset)

    def offset_of(turn, step):
        return TURNS[turn] * (5 - step)

    def far(offset):
        return 4 if offset == -4 else offset

    class Summed:
        def __init__(self, which, ref, sib_ref):
            self.which, self.ref, self.sib_ref = which, ref, sib_ref

        def sib(self, offset, number):
            slot = (far(offset) + 3) * 2 + number
            return remote(
                block(self.ref, chan_at(offset), theirs[number]), self.sib_ref.at[slot],
                rsib_ss.at[self.which, slot], rsib_rs.at[self.which, slot], dp=sibling,
            )

        def share(self, offset):
            for number in range(2):
                launch(self.sib(offset, number))

        def both(self, offset, number):
            self.sib(offset, number).wait_recv()
            slot = (far(offset) + 3) * 2 + number
            own = self.ref[chan_at(offset), pl.ds(row_of(mine[number]), ROWS), :]
            return own.astype(F32) + self.sib_ref[slot].astype(F32)

    reverse_items = [(turn, 5 - step, number) for turn, step, number in items]

    class AcrossBack(Summed):
        def __init__(self, which, ref, sib_ref, ring_ref, part_ref, lanes):
            super().__init__(which, ref, sib_ref)
            self.ring_ref, self.part_ref, self.lanes = ring_ref, part_ref, lanes

        def ring(self, turn, step, number):
            slot = item_slot(turn, step, number)
            return remote(
                block(self.ref, chan_at(offset_of(turn, step)), mine[number]), self.ring_ref.at[slot],
                rring_ss.at[self.which, slot], rring_rs.at[self.which, slot], chan=nexts[turn],
            )

        def got(self, turn, step, number):
            self.ring(turn, step, number).wait_recv()
            return self.ring_ref[item_slot(turn, step, number)].astype(F32)

        def step(self, step):
            for turn, at, number in reverse_items:
                if at != step:
                    continue
                total = self.both(offset_of(turn, step), number)
                if (turn, step - 1, number) in reverse_items:
                    total = total + self.got(turn, step - 1, number)
                place = pl.ds(row_of(mine[number]), ROWS)
                self.ref[chan_at(offset_of(turn, step)), place, :] = total.astype(BF16)
                launch(self.ring(turn, step, number))

        def x_copy(self):
            return remote(self.part_ref.at[0], self.part_ref.at[1], rx_ss.at[self.which], rx_rs.at[self.which], dp=across)

        def last(self):
            for number in (1, 0):
                total = self.both(0, number)
                for turn in range(2):
                    total = total + self.got(turn, 4, number)
                if number == 1:
                    self.part_ref[0] = total.astype(BF16)
                    launch(self.x_copy())
                else:
                    gw_ref[:, self.lanes] = total

        def finish(self):
            self.x_copy().wait_recv()
            gw_ref[:, self.lanes] += self.part_ref[1].astype(F32)

    class AlongBack(Summed):
        def x_copy(self, offset):
            slot = far(offset) + 3
            return remote(
                block(self.ref, chan_at(offset), across), cross_ref.at[slot], dx_ss.at[slot], dx_rs.at[slot], dp=across
            )

        def cross(self, offset):
            total = self.both(offset, 1)
            self.ref[chan_at(offset), pl.ds(row_of(across), ROWS), :] = total.astype(BF16)
            launch(self.x_copy(offset))

        def ring(self, turn, step):
            slot = turn * 4 + step - 1
            c, row = chan_at(offset_of(turn, step)), row_of(dp)
            if step == 1:
                src = self.ref.at[c, pl.ds(row + turn * HALF, HALF), :]
                dst = ring_dn_ref.at[slot, pl.ds(0, HALF), :]
            else:
                src, dst = self.ref.at[c, pl.ds(row, ROWS), :], ring_dn_ref.at[slot]
            return remote(src, dst, dring_ss.at[slot], dring_rs.at[slot], chan=nexts[turn])

        def whole(self, offset):
            total = self.both(offset, 0)
            self.x_copy(offset).wait_recv()
            return total + cross_ref[far(offset) + 3].astype(F32)

        def store(self, offset, total):
            self.ref[chan_at(offset), pl.ds(row_of(dp), ROWS), :] = total.astype(BF16)

        def step(self, step):
            if step == 1:
                self.store(4, self.whole(4))
                for turn in range(2):
                    launch(self.ring(turn, 1))
                return
            for turn in range(2):
                offset = offset_of(turn, step)
                total = self.whole(offset)
                slot = turn * 4 + step - 2
                self.ring(turn, step - 1).wait_recv()
                if step == 2:
                    got = ring_dn_ref[slot, 0:HALF, :].astype(F32)
                    parts = [total[:HALF], total[HALF:]]
                    parts[turn] = parts[turn] + got
                    total = jnp.concatenate(parts, axis=0)
                else:
                    total = total + ring_dn_ref[slot].astype(F32)
                self.store(offset, total)
                launch(self.ring(turn, step))

        def last(self):
            total = self.whole(0)
            for turn in range(2):
                self.ring(turn, 4).wait_recv()
                total = total + ring_dn_ref[turn * 4 + 3].astype(F32)
            gw_ref[:, 384:640] = total

    gate_g = AcrossBack(0, gab_w_ref, sib_ab_ref, ring_ab_ref, part_ab_ref, slice(0, 128))
    up_g = AcrossBack(1, gup_w_ref, sib_up_ref, ring_up_ref, part_up_ref, slice(128, 384))
    down_g = AlongBack(2, gdn_w_ref, sib_dn_ref)

    def hidden_grads(offset):
        c = chan_at(offset)
        gdn_w_ref[c] = dot_nn(tall_ref[GRADF], hid_ref[c]).astype(BF16)
        down_g.share(offset)
        gup_w_ref[c] = dot_nn(tall_ref[NORM2], gpre_ref[c]).astype(BF16)
        up_g.share(offset)

    def gate_grads(offset):
        c = chan_at(offset)
        gab_w_ref[c] = dot_nn(tall_ref[ACTS], gab_ref[c]).astype(BF16)
        gate_g.share(offset)

    def turn_tall(which):
        tall_ref[which] = low_ref[which].astype(F32).T.astype(BF16)

    turn_tall(GRADF)
    turn_tall(NORM2)
    for offset in (4, 3, -3):
        hidden_grads(offset)
    down_g.cross(4)

    mean_q, mean_qx = 0.0, 0.0
    for p in range(PAIRS):
        grad, hat = back2_ref[:, lanes_of(p)], hat2_ref[p]
        q = grad * gain2[p]
        mean_q = mean_q + q
        mean_qx = mean_qx + q * hat
        gain_grad, bias_grad = interleave(column_sum(grad * hat), column_sum(grad))
        tail_send[2 * p, 1:2, :] = gain_grad
        first, second = interleave(turn_half(column_sum(grad * hat)), turn_half(column_sum(grad)))
        tail_send[2 * p + 1, 1:2, :] = first
    mean_q = jnp.sum(mean_q, axis=1, keepdims=True) * (1.0 / MODEL_WIDTH)
    mean_qx = jnp.sum(mean_qx, axis=1, keepdims=True) * (1.0 / MODEL_WIDTH)
    for p in range(PAIRS):
        hat = hat2_ref[p]
        extra = rstd2 * (back2_ref[:, lanes_of(p)] * gain2[p] - mean_q - hat * mean_qx)
        grad_f = joined(in_recv, p, HALF)
        grad_resid = grad_f + extra
        gate, swish = gate_ref[p], swish_ref[p]
        grad_a = (grad_resid * swish).astype(BF16).astype(F32)
        grad_b = (grad_resid * gate * swish * (1.0 - swish)).astype(BF16).astype(F32)
        first, second = interleave(grad_a, grad_b)
        gab_ref[2 * p] = first.astype(BF16)
        gab_ref[2 * p + 1] = second.astype(BF16)
        tail_send[2 * p, 0:1, :] = column_sum(first)
        tail_send[2 * p + 1, 0:1, :] = column_sum(second)
        low, high = interleave(column_sum(grad_f), column_sum(grad_f))
        tail_send[2 * p, 2:3, :] = low
        tail_send[2 * p + 1, 2:3, :] = high
        low, high = split_pair(extra)
        late_send[2 * p, HALF:, :] = low.astype(BF16)
        late_send[2 * p + 1, HALF:, :] = high.astype(BF16)
    grad_acts = 0.0
    for c in range(N_CHAN):
        grad_acts = grad_acts + dot_nt(gab_ref[c], wab_ref[c])
    for p in range(PAIRS):
        low, high = split_pair(grad_acts[:, lanes_of(p)])
        back_send[2 * p] = low.astype(BF16)
        back_send[2 * p + 1] = high.astype(BF16)
    back_recv[chan] = back_send[chan]
    back = exchange(3, lambda peer: back_send.at[peer], back_recv)
    back[0]()

    up_g.step(1)
    down_g.step(1)
    down_g.cross(3)
    down_g.cross(-3)
    for offset in (2, -2):
        hidden_grads(offset)
    up_g.step(2)
    turn_tall(ACTS)
    for offset in (4, 3, -3):
        gate_grads(offset)
    down_g.cross(2)
    down_g.cross(-2)
    down_g.step(2)
    gate_g.step(1)
    for offset in (1, -1, 0):
        hidden_grads(offset)
    for offset in (2, -2, 1, -1, 0):
        gate_grads(offset)
    gate_g.step(2)
    for offset in (1, -1, 0):
        down_g.cross(offset)
    for p in range(PAIRS):
        out = res_ref[p] + branch_ref[:, lanes_of(p)] + interleave(head_recv[2 * p, 18:19, :], head_recv[2 * p + 1, 18:19, :])[0]
        low, high = split_pair(out)
        late_send[2 * p, :HALF, :] = low.astype(BF16)
        late_send[2 * p + 1, :HALF, :] = high.astype(BF16)
    for c in range(N_CHAN):
        tail_send[c, 5:8, :] = jnp.zeros((3, LANES), F32)
    late_recv[chan] = late_send[chan]
    tail_recv[chan] = tail_send[chan]
    late = exchange(4, lambda peer: late_send.at[peer], late_recv)
    tail = exchange(5, lambda peer: tail_send.at[peer], tail_recv)
    late[0]()
    tail[0]()

    back[1]()
    skip_grad = 0.0
    for j in range(PAIRS):
        grad = joined(back_recv, j, 0) * slope_ref[j]
        slope_ref[j] = grad
        conv_ref[j] = grad * aux_ref[j : j + 1, :]
        skip_grad = skip_grad + column_sum(grad * norm_ref[j])
    spread_pairs(lambda j, rows: conv_ref[j, rows, :], coefl_ref, 0, tw_ref, 0, 5, rhs_ref)
    transform_into(freq_ref, mat_ref, 0, rhs_ref)
    multiply_spectra(sig_ref, freq_ref, rhs_ref, True)
    transform_into(sig_ref, mat_ref, 1, rhs_ref)

    def store_kernel_grad(j, rows, values):
        taps_ref[j, rows, :] = values * aux_ref[4 + j : 5 + j, :]

    gather_pairs(sig_ref, coefc_ref, 80, tw_ref, 0, 5, store_kernel_grad)
    down_g.step(3)
    gate_g.step(3)
    nyquist_grad = 0.0
    for j in range(PAIRS):
        whole_sign = 1.0 - 2.0 * (lax.broadcasted_iota(jnp.int32, (ROWS, LANES), 0) % 2).astype(F32)
        nyquist_grad = nyquist_grad + column_sum(taps_ref[j] * whole_sign)
    nyquist_grad = fold(nyquist_grad) * (1.0 / TOK_DEV)
    spread_pairs(lambda j, rows: taps_ref[j, rows, :], coefc_ref, 192, tw_ref, 10, 2, rhs_ref)
    taps_freq_ref[...] = split_product(mat_ref, 0, rhs_ref, 0, 256)
    even = split_product(mat_ref, 3, rhs_ref, LANES, LANES)
    taps_freq_ref[:, LANES:256] = jnp.where(low_lanes(256), taps_freq_ref[:, LANES:256], even)
    for source in range(4):
        rows = slice(source * QUARTER, (source + 1) * QUARTER)
        sgrad_send[source, :QUARTER, :] = taps_freq_ref[rows, :]
        sgrad_send[source, QUARTER:, :] = taps_freq_ref[ROWS + source * QUARTER : ROWS + (source + 1) * QUARTER, :]
    sgrad_recv[dp] = sgrad_send[dp]
    for r in range(1, 4):
        spec_copy(1, r).start()

    up_g.step(3)
    multiply_spectra(ans_ref, freq_ref, rhs_ref, True)
    transform_into(freq_ref, mat_ref, 1, rhs_ref)
    gather_pairs(freq_ref, coefl_ref, 80, tw_ref, 0, 5, store_conv)
    gain_grad, bias_grad = 0.0, 0.0
    scaled, crossed = [], []
    for j in range(PAIRS):
        grad = conv_ref[j] + skip * slope_ref[j]
        conv_ref[j] = grad
        gain_grad = gain_grad + column_sum(grad * hat_ref[j])
        bias_grad = bias_grad + column_sum(grad)
    conv = conv_ref[...].reshape(PAIRS * ROWS, LANES) * gain1
    for i, sums in enumerate(
        token_sums(split(conv)) + token_sums(split(conv * hat_ref[...].reshape(PAIRS * ROWS, LANES)))
    ):
        sum_send[i : i + 1, :] = sums
    sum_recv[chan] = sum_send[...]
    sums_back = exchange(6, lambda peer: sum_send, sum_recv)
    sums_back[0]()
    down_g.step(4)
    gate_g.step(4)

    for r in range(1, 4):
        spec_copy(1, r).wait_recv()
    sgrad_ref[...] = sgrad_recv[0] + sgrad_recv[1] + sgrad_recv[2] + sgrad_recv[3]

    def after_part(part):
        if part == 1:
            up_g.step(4)
        elif part == 3:
            gate_g.last()
            down_g.last()

    mode_grads, dt_grad = cauchy_backward(
        modes_ref, sigma, nyquist_grad, step_size, mcoef_ref, wave_ref, base, sums_ref, sgrad_ref, pgrad_ref, mback_ref,
        after_part,
    )
    mask = low_lanes(32)
    for i in range(4):
        dp_send[i * 32 : (i + 1) * 32, :] = jnp.where(mask, mode_grads[i], mode_grads[i + 4])
    first = low_lanes(1)
    dp_send[128:129, :] = jnp.where(first, dt_grad, fold(skip_grad))
    dp_send[129:130, :] = jnp.where(first, fold(gain_grad), fold(bias_grad))
    dp_send[130:136, :] = jnp.zeros((6, LANES), F32)
    tail[1]()
    tail_sum = tail_recv[0]
    for c in range(1, N_CHAN):
        tail_sum = tail_sum + tail_recv[c]
    dp_send[136:144, :] = tail_sum
    dp_recv[0] = dp_send[...]

    def dp_copy(r):
        return remote(dp_send, dp_recv.at[r], dp_ss.at[r - 1], dp_rs.at[r - 1], dp=dp_peers[r])

    for r in range(1, 4):
        dp_copy(r).start()

    sums_back[1]()
    sums = sum_recv[0]
    for c in range(1, N_CHAN):
        sums = sums + sum_recv[c]
    sums = sums * (1.0 / MODEL_WIDTH)
    rstd_cols, q_cols, qx_cols = columns(rstd), columns(sums[0:8]), columns(sums[8:16])
    late[1]()
    for j in range(PAIRS):
        rows = slice(j * ROWS, (j + 1) * ROWS)
        out_ref[rows, :] = joined(late_recv, j, 0).astype(BF16)
        dtok_ref[rows, :] = joined(late_recv, j, HALF) + rstd_cols[j] * (
            conv_ref[j] * gain1 - q_cols[j] - hat_ref[j] * qx_cols[j]
        )
    up_g.last()
    for r in range(1, 4):
        dp_copy(r).wait_recv()
    total = dp_recv[0] + dp_recv[1] + dp_recv[2] + dp_recv[3]
    gm_ref[...] = total[0:128]
    gv_ref[...] = total[128:144]
    gate_g.finish()
    up_g.finish()
    for copy in pending:
        copy.wait_send()
    for group in (head, inputs, acts, back, late, tail, sums_back):
        group[2]()
    for r in range(1, 4):
        dp_copy(r).wait_send()
        spec_copy(0, r).wait_send()
        spec_copy(1, r).wait_send()


def unpack_kernel(
    out_ref, dtok_ref, gw_ref, gm_ref, gv_ref, cotangent_ref,
    output_ref, tokens_ref, gain1_ref, bias1_ref, modes_ref, dt_ref, skip_ref, wa_ref, ba_ref, wb_ref, bb_ref,
    gain2_ref, bias2_ref, up_ref, bup_ref, down_ref, bdown_ref,
):
    for j in range(PAIRS):
        out = out_ref[j * ROWS : (j + 1) * ROWS, :].astype(F32).T.astype(BF16)
        grad = dtok_ref[j * ROWS : (j + 1) * ROWS, :].T
        for h in range(2):
            lanes, rows = slice((2 * j + h) * ROWS, (2 * j + h + 1) * ROWS), slice(h * HALF, (h + 1) * HALF)
            output_ref[:, lanes] = out[rows]
            tokens_ref[:, lanes] = cotangent_ref[:, lanes] + grad[rows]
    for i in range(8):
        modes_ref[i] = gm_ref[i % 4 * 32 : i % 4 * 32 + 32, i // 4 * HALF : (i // 4 + 1) * HALF]
    gates = gw_ref[:, :LANES].T
    wa_ref[...] = gates[:HALF]
    wb_ref[...] = gates[HALF:]
    up_ref[...] = gw_ref[:, 128:384]
    down_ref[...] = gw_ref[:, 384:640].T
    for at, low, high in (
        (0, dt_ref, skip_ref), (1, gain1_ref, bias1_ref), (8, ba_ref, bb_ref), (9, gain2_ref, bias2_ref),
    ):
        low[...] = gv_ref[at, :HALF]
        high[...] = gv_ref[at, HALF:]
    bdown_ref[...] = gv_ref[10, :HALF]
    bup_ref[:LANES] = gv_ref[11, :]
    bup_ref[LANES:] = gv_ref[12, :]


def block_program():
    mats, twiddle, levels, constant, wave = mixer_tables()

    def run(tokens, cotangent, bucket, items, gain1, bias1, modes, log_dt, skip, w_a, b_a, w_b, b_b, gain2, bias2, w_up, b_up, w_down, b_down):
        vmem = pl.BlockSpec(memory_space=pltpu.VMEM)
        smem = pl.BlockSpec(memory_space=pltpu.SMEM)
        dma = pltpu.SemaphoreType.DMA

        def buf(*shape):
            return pltpu.VMEM(shape, F32)

        def low(*shape):
            return pltpu.VMEM(shape, BF16)

        def full(*shape):
            return jax.ShapeDtypeStruct(shape, F32)

        big, wide = (PAIRS, ROWS, LANES), (256, WIDE)
        packed = pl.pallas_call(
            block_kernel,
            out_shape=(
                jax.ShapeDtypeStruct((512, LANES), BF16), full(512, LANES), full(ROWS, WIDE), full(ROWS, LANES),
                full(16, LANES),
            ),
            in_specs=[smem] * 2 + [vmem] * 22,
            out_specs=(vmem,) * 5,
            scratch_shapes=[
                low(512, LANES), buf(8, LANES), buf(160, LANES), buf(8, 32, LANES),
                low(N_CHAN, 512, 128), low(N_CHAN, 512, 256), low(N_CHAN, 512, 256),
                low(N_CHAN, 512, 128), low(N_CHAN, 512, 256), low(N_CHAN, 512, 256),
                low(16, ROWS, 128), low(16, ROWS, 256), low(16, ROWS, 256),
                low(16, ROWS, 128), low(16, ROWS, 256), low(8, ROWS, 256),
                low(2, ROWS, 128), low(2, ROWS, 256), low(8, ROWS, 256),
                low(N_CHAN, ROWS, LANES), low(N_CHAN, ROWS, LANES), buf(24, LANES), buf(N_CHAN, 24, LANES),
                low(N_CHAN, HALF, LANES), low(N_CHAN, HALF, LANES), low(N_CHAN, HALF, LANES), low(N_CHAN, HALF, LANES),
                low(N_CHAN, ROWS, LANES), low(N_CHAN, ROWS, LANES),
                buf(16, LANES), buf(N_CHAN, 16, LANES), buf(N_CHAN, 8, LANES), buf(N_CHAN, 8, LANES),
                buf(144, LANES), buf(4, 144, LANES), buf(64, 256), buf(4, 64, 256), buf(4, 64, 256), buf(4, 64, 256),
                buf(*big), buf(*big), buf(*big), buf(*big), low(2, *wide), buf(*wide), buf(*wide), buf(*wide), buf(*big),
                buf(10, 32, LANES), buf(2, 16, QUARTER, LANES), buf(2, 16, QUARTER, LANES), buf(10, 32, LANES),
                buf(64, 256), buf(256, 256),
                buf(*big), buf(*big), buf(*big), buf(*big), low(3, ROWS, 512), buf(ROWS, 512), buf(ROWS, 512),
                low(N_CHAN, ROWS, LANES), low(N_CHAN, ROWS, 256), low(N_CHAN, ROWS, 256), low(3, 512, ROWS),
                dma((2, 16)), dma((2, 16)), dma((2, 18)), dma((2, 18)), dma((2,)), dma((2,)),
                dma((8,)), dma((8,)), dma((18,)), dma((18,)), dma((9,)), dma((9,)),
                dma((2, 16)), dma((2, 16)), dma((3, 16)), dma((3, 16)), dma((2,)), dma((2,)),
                dma((8,)), dma((8,)), dma((8,)), dma((8,)),
                dma((7, 7)), dma((7, 7)), dma((3,)), dma((3,)), dma((2, 3)), dma((2, 3)),
            ],
            compiler_params=pltpu.CompilerParams(
                collective_id=0, has_side_effects=True, vmem_limit_bytes=60 * 1024 * 1024
            ),
            name="block",
        )(
            bucket, items, tokens.T, cotangent.T, gain1, bias1, jnp.swapaxes(modes, 1, 2), log_dt, skip,
            w_a.T, b_a, w_b.T, b_b, gain2, bias2,
            w_up, b_up, w_down, b_down, levels, constant, mats, twiddle, wave,
        )
        small = full(HALF)
        results = pl.pallas_call(
            unpack_kernel,
            out_shape=(
                jax.ShapeDtypeStruct((HALF, TOK_DEV), BF16), full(HALF, TOK_DEV), small, small, full(8, 32, HALF),
                small, small, full(HALF, ROWS), small, full(HALF, ROWS), small, small, small, full(ROWS, 256),
                full(256), full(256, ROWS), small,
            ),
            in_specs=[vmem] * 6,
            out_specs=(vmem,) * 17,
            name="unpack",
        )(*packed, cotangent.T)
        turned = {0, 1, 4, 7, 9}
        return tuple(jnp.swapaxes(r, -1, -2) if i in turned else r for i, r in enumerate(results))

    return run


def solution(mesh):
    small = mesh.shape["chan"] == N_CHAN and mesh.shape["dp"] == 4
    return jax.shard_map(
        block_program() if small else shards,
        mesh=mesh,
        in_specs=(
            P("dp", "chan"),
            P("dp", "chan"),
            P("dp"),
            P("dp"),
            P("chan"),
            P("chan"),
            P(None, "chan", None),
            P("chan"),
            P("chan"),
            P("dp", "chan"),
            P("chan"),
            P("dp", "chan"),
            P("chan"),
            P("chan"),
            P("chan"),
            P("dp", "chan"),
            P("chan"),
            P("chan", "dp"),
            P("chan"),
        ),
        out_specs=(
            P("dp", "chan"),
            P("dp", "chan"),
            P("chan"),
            P("chan"),
            P(None, "chan", None),
            P("chan"),
            P("chan"),
            P("dp", "chan"),
            P("chan"),
            P("dp", "chan"),
            P("chan"),
            P("chan"),
            P("chan"),
            P("dp", "chan"),
            P("chan"),
            P("chan", "dp"),
            P("chan"),
        ),
        check_vma=False,
    )
```

```python
import math

import jax
import jax.numpy as jnp
import ml_dtypes
import numpy as np
from jax import lax
from jax.experimental import pallas as pl
from jax.experimental.pallas import tpu as pltpu
from jax.sharding import PartitionSpec as P

MODEL_WIDTH = 512
TOK_DEV = 1024


HIGHEST = lax.Precision.HIGHEST
EPSILON = 1e-05


def product(left, right):
    return jnp.dot(left, right, preferred_element_type=jnp.float32)


def product_nt(left, right):
    return lax.dot_general(
        left, right, (((1,), (1,)), ((), ())), preferred_element_type=jnp.float32
    )


def product_tn(left, right):
    return lax.dot_general(
        left, right, (((0,), (0,)), ((), ())), preferred_element_type=jnp.float32
    )


def gelu_slope(values):
    return (
        0.5 * (1.0 + lax.erf(values * 0.7071067811865476))
        + values * jnp.exp(-0.5 * values * values) * 0.3989422804014327
    )


def half_angles(length):
    angle = np.arange(length // 2 + 1, dtype=np.float64) * (math.pi / length)
    cosine, sine = np.cos(angle), np.sin(angle)
    cosine[-1] = 0.0
    return cosine.astype(np.float32), sine.astype(np.float32)


def inverse_tables(length):
    freq = np.arange(length // 2 + 1)
    turn = (freq[:, None] * np.arange(length)[None, :]) % length * (2.0 * math.pi / length)
    weight = np.where((freq == 0) | (freq == length // 2), 1.0, 2.0)[:, None] / length
    return (weight * np.cos(turn)).astype(np.float32), (weight * np.sin(turn)).astype(np.float32)


def high_einsum(form, left, right):
    return jnp.einsum(form, left, right, precision=HIGHEST)


def ssm_kernel(modes, log_dt):
    cos_h, sin_h = half_angles(TOK_DEV)
    index = jnp.arange(modes.shape[2], dtype=jnp.int32).astype(jnp.float32)
    lam_re = -0.5 * jnp.exp(modes[0])
    lam_im = math.pi * (index + modes[1])
    rank_re, rank_im, in_re, in_im, out_re, out_im = (modes[i] for i in range(2, 8))
    sigma = (2.0 * jnp.exp(-log_dt))[:, None]

    def points(values):
        return values.T[:, None, :]

    den_re = points(lam_re * lam_re + lam_im * lam_im) * (cos_h * cos_h)[:, None] - (
        sigma * sigma
    ).T * (sin_h * sin_h)[:, None]
    den_im = points(-2.0 * sigma * lam_re) * (sin_h * cos_h)[:, None]
    den_sq = den_re * den_re + den_im * den_im
    inv_re = den_re / den_sq
    inv_im = -den_im / den_sq
    sums = []
    for real, imag in (
        (out_re * in_re + out_im * in_im, out_re * in_im - out_im * in_re),
        (out_re * rank_re + out_im * rank_im, out_re * rank_im - out_im * rank_re),
        (rank_re * in_re + rank_im * in_im, rank_re * in_im - rank_im * in_re),
        (rank_re * rank_re + rank_im * rank_im, jnp.zeros_like(rank_re)),
    ):
        turned = points(real * lam_re + imag * lam_im)
        real = points(real)
        p_re, p_im = jnp.sum(real * inv_re, axis=0), jnp.sum(real * inv_im, axis=0)
        q_re, q_im = jnp.sum(turned * inv_re, axis=0), jnp.sum(turned * inv_im, axis=0)
        sine = sin_h[:, None] * sigma.T
        sums.append((-sine * p_im - cos_h[:, None] * q_re, sine * p_re - cos_h[:, None] * q_im))
    (cross_re, cross_im), (left_re, left_im), (right_re, right_im), (self_re, self_im) = sums
    twice = 2.0 * cos_h[:, None]
    loop_re, loop_im = 1.0 + twice * self_re, twice * self_im
    back_re, back_im = twice * right_re, twice * right_im
    loop_sq = loop_re * loop_re + loop_im * loop_im
    ratio_re = (back_re * loop_re + back_im * loop_im) / loop_sq
    ratio_im = (back_im * loop_re - back_re * loop_im) / loop_sq
    part_re = cross_re - (left_re * ratio_re - left_im * ratio_im)
    part_im = cross_im - (left_re * ratio_im + left_im * ratio_re)
    spec_re = 2.0 * (cos_h[:, None] * part_re - sin_h[:, None] * part_im)
    spec_im = 2.0 * (cos_h[:, None] * part_im + sin_h[:, None] * part_re)
    cos_tab, sin_tab = inverse_tables(TOK_DEV)
    return high_einsum("kl,kc->lc", cos_tab, spec_re) - high_einsum("kl,kc->lc", sin_tab, spec_im)


BLOCK = 128
BLOCKS = TOK_DEV // BLOCK
FIRST = 2 * BLOCKS
KEPT = FIRST // 2 + 1


def transform_tables():
    length = 2 * TOK_DEV
    turn = np.arange(KEPT)[:, None] * np.arange(BLOCK)[None, :] * (2.0 * math.pi / length)
    small = np.arange(BLOCK)[:, None] * np.arange(BLOCK)[None, :] % BLOCK * (2.0 * math.pi / BLOCK)
    spots = np.stack([np.arange(BLOCKS) + np.arange(BLOCKS) // (2 << b) * (2 << b) for b in range(3)])
    angle = spots[:, None, :] * np.arange(KEPT)[None, :, None] % FIRST * (2.0 * math.pi / FIRST)
    parts = (np.cos(turn), np.sin(turn), np.cos(small), np.sin(small), np.cos(angle), np.sin(angle))
    return [part.astype(np.float32) for part in parts]


def forward_transform(blocks, cos_a, sin_a):
    cos_t, sin_t, cos_s, sin_s, _, _ = transform_tables()
    step_re = high_einsum("ka,abc->kbc", cos_a, blocks)
    step_im = -high_einsum("ka,abc->kbc", sin_a, blocks)
    turned_re = step_re * cos_t[..., None] + step_im * sin_t[..., None]
    turned_im = step_im * cos_t[..., None] - step_re * sin_t[..., None]
    both = jnp.concatenate([turned_re, turned_im], axis=1)
    matrix = np.block([[cos_s, sin_s], [-sin_s, cos_s]])
    return high_einsum("pb,kbc->kpc", matrix, both)


def inverse_transform(spectrum, cos_a, sin_a):
    cos_t, sin_t, cos_s, sin_s, _, _ = transform_tables()
    matrix = np.block([[cos_s, -sin_s], [sin_s, cos_s]])
    both = high_einsum("bp,kpc->kbc", matrix, spectrum)
    step_re, step_im = both[:, :BLOCK], both[:, BLOCK:]
    turned_re = step_re * cos_t[..., None] - step_im * sin_t[..., None]
    turned_im = step_im * cos_t[..., None] + step_re * sin_t[..., None]
    weight = np.where(np.arange(KEPT) % (KEPT - 1) == 0, 1.0, 2.0).astype(np.float32) / (2 * TOK_DEV)
    return high_einsum("ka,kbc->abc", cos_a * weight[:, None], turned_re) - high_einsum(
        "ka,kbc->abc", sin_a * weight[:, None], turned_im
    )


def multiply(left, right):
    left_re, left_im = left[:, :BLOCK], left[:, BLOCK:]
    right_re, right_im = right[:, :BLOCK], right[:, BLOCK:]
    return jnp.concatenate(
        [left_re * right_re - left_im * right_im, left_re * right_im + left_im * right_re], axis=1
    )


def mixer(normed, kernel_taps, skip_gain, bucket, filled):
    _, _, _, _, cos_a, sin_a = transform_tables()
    cos_x, sin_x = jnp.asarray(cos_a)[bucket], jnp.asarray(sin_a)[bucket]
    item_blocks = 2 << bucket
    block_id = jnp.arange(BLOCKS, dtype=jnp.int32)[:, None, None]
    taps = jnp.where(block_id < item_blocks, kernel_taps.reshape(BLOCKS, BLOCK, -1), 0.0)
    signal = forward_transform(normed.reshape(BLOCKS, BLOCK, -1), cos_x, sin_x)
    answer = forward_transform(taps, cos_a[2], sin_a[2])
    result = inverse_transform(multiply(signal, answer), cos_x, sin_x)
    result = jnp.where(block_id < filled * item_blocks, result, 0.0)
    return result.reshape(normed.shape) + skip_gain * normed


def shards(
    tokens,
    cotangent,
    group_bucket,
    group_items,
    first_norm_gain,
    first_norm_bias,
    modes,
    log_dt,
    d_skip,
    w_a,
    b_a,
    w_b,
    b_b,
    second_norm_gain,
    second_norm_bias,
    w_up,
    b_up,
    w_down,
    b_down,
):
    input_tokens = tokens.astype(jnp.float32)
    sums_in = lax.psum(
        (jnp.sum(input_tokens, axis=1), jnp.sum(input_tokens * input_tokens, axis=1)), "chan"
    )
    input_average = sums_in[0][:, None] / MODEL_WIDTH
    input_inverse_deviation = lax.rsqrt(
        sums_in[1][:, None] / MODEL_WIDTH - input_average * input_average + EPSILON
    )
    input_standardized = (input_tokens - input_average) * input_inverse_deviation
    input_normalized = input_standardized * first_norm_gain + first_norm_bias
    level = group_bucket[0]
    filled = group_items[0]
    kernel_taps, kernel_back = jax.vjp(ssm_kernel, modes, log_dt)

    def local_mix(values, taps_now, skip_gain):
        return mixer(values, taps_now, skip_gain, level, filled)

    mixed, mix_back = jax.vjp(local_mix, input_normalized, kernel_taps, d_skip)
    acts_low = jax.nn.gelu(mixed, approximate=False).astype(jnp.bfloat16)
    wa_full, wb_full, up_full, down_full = (
        lax.all_gather(w_a.astype(jnp.bfloat16), "dp", axis=0, tiled=True),
        lax.all_gather(w_b.astype(jnp.bfloat16), "dp", axis=0, tiled=True),
        lax.all_gather(w_up.astype(jnp.bfloat16), "dp", axis=0, tiled=True),
        lax.all_gather(w_down.astype(jnp.bfloat16), "dp", axis=1, tiled=True),
    )
    acts_full = lax.all_gather(acts_low, "chan", axis=1, tiled=True)
    gate_a = product(acts_full, wa_full) + b_a
    gate_b = product(acts_full, wb_full) + b_b
    gate_sig = jax.nn.sigmoid(gate_b)
    residual_stream = input_tokens + gate_a * gate_sig
    sums_mid = lax.psum(
        (jnp.sum(residual_stream, axis=1), jnp.sum(residual_stream * residual_stream, axis=1)),
        "chan",
    )
    middle_average = sums_mid[0][:, None] / MODEL_WIDTH
    middle_inverse_deviation = lax.rsqrt(
        sums_mid[1][:, None] / MODEL_WIDTH - middle_average * middle_average + EPSILON
    )
    middle_standardized = (residual_stream - middle_average) * middle_inverse_deviation
    middle_reduced = (middle_standardized * second_norm_gain + second_norm_bias).astype(
        jnp.bfloat16
    )
    mid_full = lax.all_gather(middle_reduced, "chan", axis=1, tiled=True)
    pre_act = product(mid_full, up_full) + b_up
    hidden_low = jax.nn.gelu(pre_act, approximate=False).astype(jnp.bfloat16)
    branch = (
        lax.psum_scatter(product(hidden_low, down_full), "chan", scatter_dimension=1, tiled=True)
        + b_down
    )
    output = (residual_stream + branch).astype(jnp.bfloat16)
    grad_f = cotangent.astype(jnp.bfloat16)
    grad_b_down = jnp.sum(grad_f.astype(jnp.float32), axis=0)
    grad_f_full = lax.all_gather(grad_f, "chan", axis=1, tiled=True)
    grad_w_down = product_tn(hidden_low, grad_f_full)
    grad_pre = (product_nt(grad_f_full, down_full) * gelu_slope(pre_act)).astype(jnp.bfloat16)
    grad_b_up = jnp.sum(grad_pre.astype(jnp.float32), axis=0)
    grad_w_up = product_tn(mid_full, grad_pre)
    middle_gradient = lax.psum_scatter(
        product_nt(grad_pre, up_full), "chan", scatter_dimension=1, tiled=True
    )
    second_norm_gain_gradient = jnp.sum(middle_gradient * middle_standardized, axis=0)
    grad_ln2_bias = jnp.sum(middle_gradient, axis=0)
    middle_rescaled = middle_gradient * second_norm_gain
    middle_backward = lax.psum(
        (jnp.sum(middle_rescaled, axis=1), jnp.sum(middle_rescaled * middle_standardized, axis=1)),
        "chan",
    )
    grad_resid = cotangent + middle_inverse_deviation * (
        middle_rescaled
        - middle_backward[0][:, None] / MODEL_WIDTH
        - middle_standardized * middle_backward[1][:, None] / MODEL_WIDTH
    )
    grad_a = (grad_resid * gate_sig).astype(jnp.bfloat16)
    grad_b = (grad_resid * gate_a * gate_sig * (1.0 - gate_sig)).astype(jnp.bfloat16)
    grad_b_a = jnp.sum(grad_a.astype(jnp.float32), axis=0)
    grad_b_b = jnp.sum(grad_b.astype(jnp.float32), axis=0)
    grad_w_a = product_tn(acts_full, grad_a)
    grad_w_b = product_tn(acts_full, grad_b)
    grad_acts = lax.psum_scatter(
        product_nt(grad_a, wa_full) + product_nt(grad_b, wb_full),
        "chan",
        scatter_dimension=1,
        tiled=True,
    )
    grad_mixed = grad_acts * gelu_slope(mixed)
    normalized_gradient, grad_kernel, grad_skip = mix_back(grad_mixed)
    grad_modes, grad_log_dt = kernel_back(grad_kernel)
    first_norm_gain_gradient = jnp.sum(normalized_gradient * input_standardized, axis=0)
    grad_ln1_bias = jnp.sum(normalized_gradient, axis=0)
    input_rescaled = normalized_gradient * first_norm_gain
    input_backward = lax.psum(
        (jnp.sum(input_rescaled, axis=1), jnp.sum(input_rescaled * input_standardized, axis=1)),
        "chan",
    )
    grad_tokens = grad_resid + input_inverse_deviation * (
        input_rescaled
        - input_backward[0][:, None] / MODEL_WIDTH
        - input_standardized * input_backward[1][:, None] / MODEL_WIDTH
    )
    grad_w_a, grad_w_b, grad_w_up, grad_w_down = (
        lax.psum_scatter(grad_w_a, "dp", scatter_dimension=0, tiled=True),
        lax.psum_scatter(grad_w_b, "dp", scatter_dimension=0, tiled=True),
        lax.psum_scatter(grad_w_up, "dp", scatter_dimension=0, tiled=True),
        lax.psum_scatter(grad_w_down, "dp", scatter_dimension=1, tiled=True),
    )
    (
        first_norm_gain_gradient,
        grad_ln1_bias,
        grad_modes,
        grad_log_dt,
        grad_skip,
        grad_b_a,
        grad_b_b,
        second_norm_gain_gradient,
        grad_ln2_bias,
        grad_b_up,
        grad_b_down,
    ) = lax.psum(
        (
            first_norm_gain_gradient,
            grad_ln1_bias,
            grad_modes,
            grad_log_dt,
            grad_skip,
            grad_b_a,
            grad_b_b,
            second_norm_gain_gradient,
            grad_ln2_bias,
            grad_b_up,
            grad_b_down,
        ),
        "dp",
    )
    return (
        output,
        grad_tokens,
        first_norm_gain_gradient,
        grad_ln1_bias,
        grad_modes,
        grad_log_dt,
        grad_skip,
        grad_w_a,
        grad_b_a,
        grad_w_b,
        grad_b_b,
        second_norm_gain_gradient,
        grad_ln2_bias,
        grad_w_up,
        grad_b_up,
        grad_w_down,
        grad_b_down,
    )


LANES = 128
HALF = 64
PAIRS = 4
ROWS = 128
N_CHAN = 8
WIDE = 640
MESH = pl.DeviceIdType.MESH
F32 = jnp.float32
BF16 = jnp.bfloat16


def split_two(matrix):
    high = matrix.astype(ml_dtypes.bfloat16)
    low = (matrix - high.astype(np.float64)).astype(ml_dtypes.bfloat16)
    return np.concatenate([high, low], axis=1)


def lane_rows(values_low, values_high):
    return np.repeat(np.stack([values_low, values_high], -1), HALF, axis=-1)


def mixer_tables():
    line = np.arange(ROWS)
    small = np.outer(line, line) % ROWS * (2.0 * math.pi / ROWS)
    cos_s, sin_s = np.cos(small), np.sin(small)
    forward = np.block([[cos_s, sin_s], [-sin_s, cos_s]])
    real = np.zeros((2 * ROWS, 2 * ROWS))
    for row in range(HALF):
        weight = 1.0 if row == 0 else 2.0
        turn = 2.0 * math.pi / ROWS * row * line
        real[:ROWS, row] = weight * np.cos(turn)
        real[:ROWS, ROWS + row] = -weight * np.sin(turn)
        turn = 2.0 * math.pi / TOK_DEV * (4 + 8 * row) * line
        real[ROWS:, HALF + row] = 2.0 * np.cos(turn)
        real[ROWS:, ROWS + HALF + row] = -2.0 * np.sin(turn)
    mats = np.stack([split_two(m) for m in (forward, forward.T, real, real.T)])

    twiddle = []
    for pair in range(5):
        turn = np.stack([line * k * (math.pi / TOK_DEV) for k in (2 * pair, 2 * pair + 1)])
        twiddle += [lane_rows(np.cos(turn[0]), np.cos(turn[1])), lane_rows(np.sin(turn[0]), np.sin(turn[1]))]
    for first, second in ((1, 2), (3, 0)):
        turn = np.stack([line * k * (2.0 * math.pi / TOK_DEV) for k in (first, second)])
        twiddle += [lane_rows(np.cos(turn[0]), np.cos(turn[1])), lane_rows(np.sin(turn[0]), np.sin(turn[1]))]

    def forward_rows(coef, pairs):
        out = []
        for low, high in pairs:
            for part in range(2):
                for j in range(PAIRS):
                    out.append(lane_rows(coef(2 * j, low, part), coef(2 * j + 1, high, part)))
                for j in range(PAIRS):
                    out.append(lane_rows(coef(2 * j, high, part), coef(2 * j + 1, low, part)))
        return np.stack(out)

    def inverse_rows(coef, pairs):
        out = []
        for low, high in pairs:
            for part in range(2):
                for j in range(PAIRS):
                    out.append(lane_rows(coef(2 * j, low, part), coef(2 * j + 1, high, part)))
                for j in range(PAIRS):
                    out.append(lane_rows(coef(2 * j + 1, low, part), coef(2 * j, high, part)))
        return np.stack(out)

    levels = []
    pairs = [(2 * p, 2 * p + 1) for p in range(5)]
    for level in range(3):
        item = 2 << level

        def angle(block, k):
            return 2.0 * math.pi / 16 * ((block + block // item * item) * k % 16)

        def fwd(block, k, part):
            if k > 8:
                return np.zeros(())
            return np.cos(angle(block, k)) if part == 0 else -np.sin(angle(block, k))

        def inv(block, k, part):
            weight = (1.0 if k in (0, 8) else 2.0) / (2 * TOK_DEV)
            return weight * fwd(block, k, part)

        levels.append(np.concatenate([forward_rows(fwd, pairs), inverse_rows(inv, pairs)]))

    def taps(block, k, part):
        if k == 0:
            return np.asarray((1.0 if part == 0 else (-1.0) ** block) / TOK_DEV)
        turn = 2.0 * math.pi / 8 * (block * k % 8)
        return np.asarray((np.cos(turn) if part == 0 else -np.sin(turn)) * 2.0 / TOK_DEV)

    tap_pairs = [(1, 2), (3, 0)]
    taps_back = forward_rows(taps, tap_pairs)
    taps_rows = inverse_rows(taps, tap_pairs)
    freq_even = np.where(line < HALF, 8 * line, 4 + 8 * (line - HALF))
    half_angle = np.stack(
        [lane_rows(1 + 8 * line, 2 + 8 * line), lane_rows(3 + 8 * line, freq_even)]
    ) * (math.pi / TOK_DEV)
    wave = np.stack([np.cos(half_angle), np.sin(half_angle)])
    return (
        mats,
        np.stack(twiddle).astype(np.float32),
        np.stack(levels).astype(np.float32),
        np.concatenate([levels[2], taps_rows, taps_back]).astype(np.float32),
        wave.astype(np.float32),
    )


def low_lanes(rows):
    return lax.broadcasted_iota(jnp.int32, (rows, LANES), 1) < HALF


def turn_half(values):
    return pltpu.roll(values, HALF, 1)


def split_pair(values):
    upper, lower = values[:HALF], values[HALF:]
    mask = low_lanes(HALF)
    return jnp.where(mask, upper, turn_half(lower)), jnp.where(mask, turn_half(upper), lower)


def join_pair(first, second):
    mask = low_lanes(HALF)
    return jnp.concatenate(
        [jnp.where(mask, first, turn_half(second)), jnp.where(mask, turn_half(first), second)], axis=0
    )


def interleave(first, second):
    mask = low_lanes(first.shape[0])
    return jnp.where(mask, first, turn_half(second)), jnp.where(mask, turn_half(first), second)


def fold(values):
    return values + turn_half(values)


def normal_parts(values):
    cumulative = 0.5 * (1.0 + lax.erf(values * 0.7071067811865476))
    density = jnp.exp(-0.5 * values * values) * 0.3989422804014327
    return cumulative, density


def column_sum(values):
    return jnp.sum(values, axis=0, keepdims=True)


def dot_nt(left, right):
    return lax.dot_general(left, right, (((1,), (1,)), ((), ())), preferred_element_type=F32)


def dot_nn(left, right):
    return jnp.dot(left, right, preferred_element_type=F32)


def store_split(ref, row, lane, values):
    high = values.astype(BF16)
    place = (pl.ds(row, values.shape[0]), pl.ds(lane, values.shape[1]))
    ref[(0,) + place] = high
    ref[(1,) + place] = (values - high.astype(F32)).astype(BF16)


def split_product(mat_ref, which, rhs_ref, lane, width):
    high = mat_ref[which, :, 0:256]
    low = mat_ref[which, :, 256:512]
    rhs_high = rhs_ref[0, :, lane : lane + width]
    return dot_nn(high, rhs_high) + dot_nn(high, rhs_ref[1, :, lane : lane + width]) + dot_nn(low, rhs_high)


CHUNK = 32


def over_chunks(body, size=CHUNK, first=0, rows=ROWS):
    def step(index, carry):
        body(pl.multiple_of(first + index * size, size))
        return carry

    lax.fori_loop(0, rows // size, step, 0)


def spread_pairs(src, coef_ref, base, twiddle_ref, twiddle_base, pairs, rhs_ref):
    def body(row):
        rows = pl.ds(row, CHUNK)
        blocks = [src(j, rows) for j in range(PAIRS)]
        for pair in range(pairs):
            parts = []
            for part in range(2):
                at = base + (pair * 2 + part) * 8
                straight = sum(blocks[j] * coef_ref[at + j : at + j + 1, :] for j in range(PAIRS))
                crossed = sum(blocks[j] * coef_ref[at + 4 + j : at + 5 + j, :] for j in range(PAIRS))
                parts.append(straight + turn_half(crossed))
            cosine = twiddle_ref[twiddle_base + 2 * pair, rows, :]
            sine = twiddle_ref[twiddle_base + 2 * pair + 1, rows, :]
            store_split(rhs_ref, row, pair * LANES, parts[0] * cosine + parts[1] * sine)
            store_split(rhs_ref, row + ROWS, pair * LANES, parts[1] * cosine - parts[0] * sine)

    over_chunks(body)


def gather_pairs(values_ref, coef_ref, base, twiddle_ref, twiddle_base, pairs, store):
    def body(row):
        rows = pl.ds(row, CHUNK)
        straight, crossed = [0.0] * PAIRS, [0.0] * PAIRS
        for pair in range(pairs):
            lanes = slice(pair * LANES, (pair + 1) * LANES)
            real, imag = values_ref[rows, lanes], values_ref[pl.ds(row + ROWS, CHUNK), lanes]
            cosine = twiddle_ref[twiddle_base + 2 * pair, rows, :]
            sine = twiddle_ref[twiddle_base + 2 * pair + 1, rows, :]
            for part, value in enumerate((real * cosine - imag * sine, imag * cosine + real * sine)):
                at = base + (pair * 2 + part) * 8
                for j in range(PAIRS):
                    straight[j] = straight[j] + value * coef_ref[at + j : at + j + 1, :]
                    crossed[j] = crossed[j] + value * coef_ref[at + 4 + j : at + 5 + j, :]
        for j in range(PAIRS):
            store(j, rows, straight[j] + turn_half(crossed[j]))

    over_chunks(body)


GROUPS = ((0, 256), (256, 256), (512, 128))


def transform_into(dst_ref, mat_ref, which, rhs_ref, groups=GROUPS):
    for lane, width in groups:
        dst_ref[:, lane : lane + width] = split_product(mat_ref, which, rhs_ref, lane, width)


def multiply_spectra(left_ref, right_ref, rhs_ref, conjugate):
    def body(row):
        top, bottom = pl.ds(row, CHUNK), pl.ds(row + ROWS, CHUNK)
        for pair in range(5):
            lanes = slice(pair * LANES, (pair + 1) * LANES)
            a_re, a_im = left_ref[top, lanes], left_ref[bottom, lanes]
            b_re, b_im = right_ref[top, lanes], right_ref[bottom, lanes]
            if conjugate:
                out_re, out_im = a_re * b_re + a_im * b_im, a_re * b_im - a_im * b_re
            else:
                out_re, out_im = a_re * b_re - a_im * b_im, a_re * b_im + a_im * b_re
            store_split(rhs_ref, row, pair * LANES, out_re)
            store_split(rhs_ref, row + ROWS, pair * LANES, out_im)

    over_chunks(body)


def pair_terms(modes_ref):
    rank_re, rank_im, in_re, in_im, out_re, out_im = (modes_ref[i] for i in range(2, 8))
    return (
        (out_re * in_re + out_im * in_im, out_re * in_im - out_im * in_re),
        (out_re * rank_re + out_im * rank_im, out_re * rank_im - out_im * rank_re),
        (rank_re * in_re + rank_im * in_im, rank_re * in_im - rank_im * in_re),
        (rank_re * rank_re + rank_im * rank_im, None),
    )


def mode_values(modes_ref):
    index = lax.broadcasted_iota(jnp.int32, modes_ref.shape[1:], 0).astype(F32)
    return -0.5 * jnp.exp(modes_ref[0]), math.pi * (index + modes_ref[1])


POINT_ROWS = 16


def resolvent(coef_ref, n, square_cos, cos_sin, scaled):
    den_re = coef_ref[8, pl.ds(n, 1), :] * square_cos - scaled
    den_im = coef_ref[9, pl.ds(n, 1), :] * cos_sin
    inverse = 1.0 / (den_re * den_re + den_im * den_im)
    return den_re * inverse, -(den_im * inverse)


def complex_multiply(a_re, a_im, b_re, b_im):
    return a_re * b_re - a_im * b_im, a_re * b_im + a_im * b_re


def conj_multiply(a_re, a_im, b_re, b_im):
    return a_re * b_re + a_im * b_im, a_re * b_im - a_im * b_re


def combine(sums, sigma, cosine, sine):
    terms = []
    for p_re, p_im, q_re, q_im in (sums[4 * q : 4 * q + 4] for q in range(4)):
        swing = sigma * sine
        terms.append((-swing * p_im - cosine * q_re, swing * p_re - cosine * q_im))
    twice = 2.0 * cosine
    loop_re, loop_im = 1.0 + twice * terms[3][0], twice * terms[3][1]
    scale = 1.0 / (loop_re * loop_re + loop_im * loop_im)
    inv = (loop_re * scale, -(loop_im * scale))
    ratio = complex_multiply(twice * terms[2][0], twice * terms[2][1], *inv)
    return terms, inv, ratio


QUARTER = 32


def cauchy_coefficients(modes_ref, sigma, coef_ref):
    lam_re, lam_im = mode_values(modes_ref)
    for q, (real, imag) in enumerate(pair_terms(modes_ref)):
        coef_ref[q] = real
        coef_ref[4 + q] = real * lam_re if imag is None else real * lam_re + imag * lam_im
    coef_ref[8] = lam_re * lam_re + lam_im * lam_im
    coef_ref[9] = -2.0 * sigma * lam_re


def wave_rows(wave_ref, pair, base, row):
    rows = pl.ds(pl.multiple_of(base + row, POINT_ROWS), POINT_ROWS)
    return wave_ref[0, pair, rows, :], wave_ref[1, pair, rows, :]


def cauchy_forward(sigma, coef_ref, wave_ref, base, sums_ref, spec_ref, middle):
    sigma_sq = sigma * sigma
    for index in range(4):
        pair, row = index // 2, index % 2 * POINT_ROWS
        rows = slice(row, row + POINT_ROWS)
        lanes = slice(pair * LANES, (pair + 1) * LANES)
        cosine, sine = wave_rows(wave_ref, pair, base, row)
        square_cos, cos_sin, scaled = cosine * cosine, cosine * sine, sigma_sq * (sine * sine)

        def add_mode(n, sums):
            sums = list(sums)
            for k in range(4):
                at = n * 4 + k
                inv_re, inv_im = resolvent(coef_ref, at, square_cos, cos_sin, scaled)
                for q in range(4):
                    plain = coef_ref[q, pl.ds(at, 1), :]
                    turned = coef_ref[4 + q, pl.ds(at, 1), :]
                    sums[4 * q] = sums[4 * q] + plain * inv_re
                    sums[4 * q + 1] = sums[4 * q + 1] + plain * inv_im
                    sums[4 * q + 2] = sums[4 * q + 2] + turned * inv_re
                    sums[4 * q + 3] = sums[4 * q + 3] + turned * inv_im
            return tuple(sums)

        zero = jnp.zeros((POINT_ROWS, LANES), F32)
        sums = lax.fori_loop(0, 8, add_mode, (zero,) * 16)
        for i in range(16):
            sums_ref[pair, i, rows, :] = sums[i]
        terms, _, ratio = combine(sums, sigma, cosine, sine)
        cut_re, cut_im = complex_multiply(*terms[1], *ratio)
        part_re, part_im = terms[0][0] - cut_re, terms[0][1] - cut_im
        spec_re, spec_im = complex_multiply(2.0 * cosine, 2.0 * sine, part_re, part_im)
        spec_ref[rows, lanes] = spec_re
        spec_ref[row + QUARTER : row + QUARTER + POINT_ROWS, lanes] = spec_im
        middle(index)


def cauchy_backward(modes_ref, sigma, nyquist_grad, step, coef_ref, wave_ref, base, sums_ref, spec_ref, grad_ref, back_ref, middle):
    zero = jnp.zeros((POINT_ROWS, LANES), F32)
    sigma_sum = zero
    places = [(pair, row) for pair in range(2) for row in range(0, QUARTER, POINT_ROWS)]
    for pair, row in places:
        rows = slice(row, row + POINT_ROWS)
        lanes = slice(pair * LANES, (pair + 1) * LANES)
        cosine, sine = wave_rows(wave_ref, pair, base, row)
        sums = [sums_ref[pair, i, rows, :] for i in range(16)]
        terms, inv, ratio = combine(sums, sigma, cosine, sine)
        spec_re, spec_im = spec_ref[rows, lanes], spec_ref[row + QUARTER : row + QUARTER + POINT_ROWS, lanes]
        part = conj_multiply(2.0 * cosine, 2.0 * sine, spec_re, spec_im)
        left = conj_multiply(*ratio, *part)
        ratio_grad = conj_multiply(*terms[1], *part)
        back = conj_multiply(*inv, -ratio_grad[0], -ratio_grad[1])
        twice = 2.0 * cosine
        loop = conj_multiply(*ratio, *back)
        grads = (
            part,
            (-left[0], -left[1]),
            (twice * back[0], twice * back[1]),
            (-twice * loop[0], -twice * loop[1]),
        )
        swing = sigma * sine
        for q, (g_re, g_im) in enumerate(grads):
            grad_ref[pair, 4 * q, rows, :] = swing * g_im
            grad_ref[pair, 4 * q + 1, rows, :] = -swing * g_re
            grad_ref[pair, 4 * q + 2, rows, :] = -cosine * g_re
            grad_ref[pair, 4 * q + 3, rows, :] = -cosine * g_im
            sigma_sum = sigma_sum + sine * (g_im * sums[4 * q] - g_re * sums[4 * q + 1])
    sigma_sq = sigma * sigma

    def mode(n, square_sum):
        plain = [coef_ref[q, pl.ds(n, 1), :] for q in range(4)]
        turned = [coef_ref[4 + q, pl.ds(n, 1), :] for q in range(4)]
        sums = [0.0] * 10
        for pair, row in places:
            rows = slice(row, row + POINT_ROWS)
            cosine, sine = wave_rows(wave_ref, pair, base, row)
            square_cos, cos_sin, square_sin = cosine * cosine, cosine * sine, sine * sine
            inv_re, inv_im = resolvent(coef_ref, n, square_cos, cos_sin, sigma_sq * square_sin)
            grad_re, grad_im = 0.0, 0.0
            for q in range(4):
                p_re, p_im = grad_ref[pair, 4 * q, rows, :], grad_ref[pair, 4 * q + 1, rows, :]
                q_re, q_im = grad_ref[pair, 4 * q + 2, rows, :], grad_ref[pair, 4 * q + 3, rows, :]
                grad_re = grad_re + (plain[q] * p_re + turned[q] * q_re)
                grad_im = grad_im + (plain[q] * p_im + turned[q] * q_im)
                sums[q] = sums[q] + (p_re * inv_re + p_im * inv_im)
                sums[4 + q] = sums[4 + q] + (q_re * inv_re + q_im * inv_im)
            square_re = inv_re * inv_re - inv_im * inv_im
            square_im = 2.0 * inv_re * inv_im
            den_re, den_im = conj_multiply(square_re, square_im, grad_re, grad_im)
            sums[8] = sums[8] - den_re * square_cos
            sums[9] = sums[9] - den_im * cos_sin
            square_sum = square_sum + den_re * square_sin
        for i in range(10):
            back_ref[i, pl.ds(n, 1), :] = column_sum(sums[i])
        return square_sum

    square_sum = zero
    for part in range(4):
        square_sum = lax.fori_loop(part * 8, part * 8 + 8, mode, square_sum)
        middle(part)
    plain_grad = [fold(back_ref[q]) for q in range(4)]
    turned_grad = [fold(back_ref[4 + q]) for q in range(4)]
    abs_grad, skew_grad = fold(back_ref[8]), fold(back_ref[9])
    lam_re, lam_im = mode_values(modes_ref)
    plain_grad[0] = plain_grad[0] + step * nyquist_grad
    rank_re, rank_im, in_re, in_im, out_re, out_im = (modes_ref[i] for i in range(2, 8))
    lam_re_grad = 2.0 * lam_re * abs_grad - 2.0 * sigma * skew_grad
    lam_im_grad = 2.0 * lam_im * abs_grad
    real_grad, imag_grad = [], []
    terms = pair_terms(modes_ref)
    for q, (real, imag) in enumerate(terms):
        lam_re_grad = lam_re_grad + turned_grad[q] * real
        if imag is not None:
            lam_im_grad = lam_im_grad + turned_grad[q] * imag
        real_grad.append(plain_grad[q] + turned_grad[q] * lam_re)
        imag_grad.append(turned_grad[q] * lam_im)
    r0, r1, r2, r3 = real_grad
    i0, i1, i2, _ = imag_grad
    grads = (
        lam_re_grad * lam_re,
        math.pi * lam_im_grad,
        r1 * out_re - i1 * out_im + r2 * in_re + i2 * in_im + 2.0 * r3 * rank_re,
        r1 * out_im + i1 * out_re + r2 * in_im - i2 * in_re + 2.0 * r3 * rank_im,
        r0 * out_re - i0 * out_im + r2 * rank_re - i2 * rank_im,
        r0 * out_im + i0 * out_re + r2 * rank_im + i2 * rank_re,
        r0 * in_re + i0 * in_im + r1 * rank_re + i1 * rank_im,
        r0 * in_im - i0 * in_re + r1 * rank_im - i1 * rank_re,
    )
    sigma_grad = (
        fold(column_sum(sigma_sum) + 2.0 * sigma * column_sum(square_sum))
        - 2.0 * column_sum(skew_grad * lam_re)
    )
    nyquist = step * column_sum(terms[0][0])
    return grads, nyquist * nyquist_grad - sigma * sigma_grad


def block_kernel(
    bucket_ref, items_ref, tokens_ref, cotangent_ref, gain1_ref, bias1_ref, raw_modes_ref, log_dt_ref, skip_ref,
    wa_ref, ba_ref, wb_ref, bb_ref, gain2_ref, bias2_ref, up_ref, bup_ref, down_ref, bdown_ref,
    levels_ref, coefc_ref, mat_ref, tw_ref, wave_ref,
    out_ref, dtok_ref, gw_ref, gm_ref, gv_ref,
    tok_ref, aux_ref, coefl_ref, modes_ref,
    wab_ref, wup_ref, wdn_ref, gab_w_ref, gup_w_ref, gdn_w_ref,
    up_stage, down_flow, sib_ab_ref, y_ab_ref, y_up_ref, y_dn_ref, z_ab_ref, z_up_ref, z_dn_ref, dp_up_ref, dp_dn_ref,
    up_send, down_send, part_ab_ref, total_ab_ref, total_up_ref, total_dn_ref,
    in_send, in_recv, head_send, head_recv, acts_send, acts_recv, back_send, back_recv, late_send, late_recv,
    sum_send, sum_recv, tail_send, tail_recv, dp_send, dp_recv, spec_send, spec_recv, sgrad_send, sgrad_recv,
    hat_ref, norm_ref, slope_ref, conv_ref, rhs_ref, freq_ref, sig_ref, ans_ref, taps_ref,
    mcoef_ref, sums_ref, pgrad_ref, mback_ref, sgrad_ref, taps_freq_ref,
    gate_ref, swish_ref, res_ref, hat2_ref, acts_ref, norm2_ref, gradf_ref, branch_ref, back2_ref, half_send, half_recv,
    gab_ref, hid_ref, gpre_ref, acts_t_ref, norm2_t_ref, gradf_t_ref,
    gz_ss, gz_rs, gy_ss, gy_rs, gx_ss, gx_rs, gup_ss, gup_rs, gdn_ss, gdn_rs, gsib_ss, gsib_rs, core_ss, core_rs,
    rz_ss, rz_rs, ry_ss, ry_rs, rx_ss, rx_rs, rup_ss, rup_rs, rdn_ss, rdn_rs, rsib_ss, rsib_rs,
    a2a_ss, a2a_rs, dp_ss, dp_rs, spec_ss, spec_rs,
):
    dp, chan = lax.axis_index("dp"), lax.axis_index("chan")
    core = lax.rem(dp, 2)
    sibling = dp + 1 - 2 * core
    z, y = lax.div(chan, 2), lax.rem(chan, 2)
    z_on = [z] + [lax.rem(z + r, 4) for r in range(1, 4)]
    z_back = [z] + [z_on[4 - r] for r in range(1, 4)]
    chan_peers = [chan] + [lax.rem(chan + r, N_CHAN) for r in range(1, N_CHAN)]
    dp_peers = [dp] + [lax.rem(dp + r, 4) for r in range(1, 4)]
    across = dp_peers[2]
    diagonal = lax.rem(sibling + 2, 4)
    dp_others = (across, sibling, diagonal)

    barrier = pltpu.get_barrier_semaphore()
    for r in range(1, N_CHAN):
        pl.semaphore_signal(barrier, inc=1, device_id={"chan": chan_peers[r]}, device_id_type=MESH)
    for r in range(1, 4):
        pl.semaphore_signal(barrier, inc=1, device_id={"dp": dp_peers[r]}, device_id_type=MESH)

    pending = []

    def remote(src, dst, send_sem, recv_sem, **device):
        return pltpu.make_async_remote_copy(
            src_ref=src, dst_ref=dst, send_sem=send_sem, recv_sem=recv_sem, device_id=device, device_id_type=MESH
        )

    def send(*args, **device):
        copy = remote(*args, **device)
        copy.start()
        pending.append(copy)

    def exchange(which, source, recv_ref):
        def copy(r):
            peer = chan_peers[r]
            return remote(
                source(peer), recv_ref.at[chan], a2a_ss.at[which, r - 1], a2a_rs.at[which, r - 1], chan=peer
            )

        def start():
            for r in range(1, N_CHAN):
                copy(r).start()

        def wait():
            for r in range(1, N_CHAN):
                copy(r).wait_recv()

        def finish():
            for r in range(1, N_CHAN):
                copy(r).wait_send()

        return start, wait, finish

    def rows_at(number, count):
        return pl.ds(pl.multiple_of(number, ROWS), count)

    def lanes_at(number):
        return pl.ds(pl.multiple_of(number * LANES, LANES), LANES)

    def launch(copy):
        copy.start()
        pending.append(copy)

    x = lax.div(dp, 2)
    own_row = dp * ROWS
    gate_row, gate_away = (core * 2 + x) * ROWS, (core * 2 + 1 - x) * ROWS
    gate_pair, gate_other = core * 2 * ROWS, (1 - core) * 2 * ROWS

    class Plane:
        def __init__(self, which, view, hook):
            self.which, self.view, self.hook = which, view, hook

        def z_copy(self, r, source):
            ref, which = self.view(source, y), self.which
            return remote(ref, ref, gz_ss.at[which, r - 1], gz_rs.at[which, r - 1], chan=z_on[r] * 2 + y)

        def y_copy(self, r, line):
            ref, which = self.view(z_back[r], line), self.which
            return remote(ref, ref, gy_ss.at[which, r], gy_rs.at[which, r], chan=z * 2 + 1 - y)

        def start(self):
            for r in (2, 1, 3):
                launch(self.z_copy(r, z))
            launch(self.y_copy(0, y))
            self.hook(0, y)

        def z_step(self, *steps):
            for r in steps:
                self.z_copy(r, z_back[r]).wait_recv()
                launch(self.y_copy(r, y))
                self.hook(r, y)

        def y_step(self, *steps):
            for r in steps:
                self.y_copy(r, 1 - y).wait_recv()
                self.hook(r, 1 - y)

    def gate_sib(r, line, base):
        ref = wab_ref.at[z_back[r] * 2 + line, rows_at(base, 256), :]
        slot = r * 2 + jnp.where(line == y, 0, 1)
        return remote(ref, ref, gsib_ss.at[slot], gsib_rs.at[slot], dp=sibling)

    def down_copy(number, r, line, row):
        half = core if number == 0 else 1 - core
        slot = (r * 2 + jnp.where(line == y, 0, 1)) * 3 + number
        return remote(
            down_flow.at[z_back[r] * 2 + line, :, lanes_at(half)],
            wdn_ref.at[z_back[r], rows_at(row, ROWS), lanes_at(line)],
            gdn_ss.at[slot], gdn_rs.at[slot], dp=dp_others[number],
        )

    def down_hook(r, line):
        for number in range(3):
            launch(down_copy(number, r, line, own_row))
        wdn_ref[z_back[r], rows_at(own_row, ROWS), lanes_at(line)] = down_flow[z_back[r] * 2 + line, :, lanes_at(core)]

    gates = Plane(
        0, lambda at, line: wab_ref.at[at * 2 + line, rows_at(gate_pair, 256), :],
        lambda r, line: launch(gate_sib(r, line, gate_pair)),
    )
    ups = Plane(1, lambda at, line: wup_ref.at[at, :, lanes_at(line)], lambda r, line: None)
    downs = Plane(2, lambda at, line: down_flow.at[at * 2 + line], down_hook)

    def gate_first(row):
        ref = wab_ref.at[chan, rows_at(row, ROWS), :]
        return remote(ref, ref, gx_ss, gx_rs, dp=across)

    def up_first(number, row):
        half = core if number == 0 else 1 - core
        return remote(
            up_stage.at[:, lanes_at(half)], wup_ref.at[z, rows_at(row, ROWS), lanes_at(y)],
            gup_ss.at[number], gup_rs.at[number], dp=dp_others[number],
        )

    def gather_prepare():
        wab_ref[chan, rows_at(gate_row, ROWS), :] = jnp.concatenate([wa_ref[...], wb_ref[...]], axis=0).T.astype(BF16)
        up_stage[...] = up_ref[...].astype(BF16)
        wup_ref[z, rows_at(own_row, ROWS), lanes_at(y)] = up_stage[:, lanes_at(core)]
        down_flow[chan] = down_ref[...].T.astype(BF16)

    def gather_start():
        launch(gate_first(gate_row))
        for number in range(3):
            launch(up_first(number, own_row))
        downs.start()

    def gather_cross():
        gate_first(gate_away).wait_recv()
        gates.start()
        for number in range(3):
            up_first(number, dp_others[number] * ROWS).wait_recv()
        ups.start()

    def gates_arrived():
        for r in range(4):
            for line in (y, 1 - y):
                gate_sib(r, line, gate_other).wait_recv()

    def down_arrived(r):
        for line in (y, 1 - y):
            for number in range(3):
                down_copy(number, r, line, dp_others[number] * ROWS).wait_recv()

    gather_prepare()

    def beside(ref, j):
        start = 2 * j * ROWS
        return jnp.concatenate(
            [ref[:, start : start + ROWS].astype(F32), ref[:, start + ROWS : start + 2 * ROWS].astype(F32)], axis=0
        ).T

    for j in range(PAIRS):
        packed = beside(tokens_ref, j)
        tok_ref[j * ROWS : (j + 1) * ROWS, :] = packed.astype(BF16)
        for first, values in ((0, packed), (HALF, beside(cotangent_ref, j))):
            low, high = split_pair(values)
            in_send[2 * j, first : first + HALF, :] = low.astype(BF16)
            in_send[2 * j + 1, first : first + HALF, :] = high.astype(BF16)
    in_recv[chan] = in_send[chan]

    lane_id = lax.broadcasted_iota(jnp.int32, (8, LANES), 1)
    row_id = lax.broadcasted_iota(jnp.int32, (8, LANES), 0)
    halves = jnp.where((lane_id >= HALF) == (row_id == 1), 1.0, 0.0) * jnp.where(row_id < 2, 1.0, 0.0)
    halves = halves.astype(BF16)

    def token_sums(parts):
        total = 0.0
        for part in parts:
            total = total + dot_nt(halves, part)
        return [total[h : h + 1, j * ROWS : (j + 1) * ROWS] for h in range(2) for j in range(PAIRS)]

    def split(values):
        high = values.astype(BF16)
        return high, (values - high.astype(F32)).astype(BF16)

    tokens = tok_ref[...]
    wide_tokens = tokens.astype(F32)
    for i, sums in enumerate(token_sums([tokens]) + token_sums(split(wide_tokens * wide_tokens))):
        head_send[i : i + 1, :] = sums

    def row(*refs):
        return jnp.concatenate([ref[...].reshape(1, HALF) for ref in refs], axis=1)

    bup = bup_ref[...].reshape(1, 2 * LANES)
    head_send[16:17, :] = row(ba_ref, bb_ref)
    head_send[17:18, :] = row(gain2_ref, bias2_ref)
    head_send[18:19, :] = row(bdown_ref, bdown_ref)
    head_send[19:20, :] = bup[:, :LANES]
    head_send[20:21, :] = bup[:, LANES:]
    head_send[21:24, :] = jnp.zeros((3, LANES), F32)
    head_recv[chan] = head_send[...]
    head = exchange(0, lambda peer: head_send, head_recv)
    inputs = exchange(1, lambda peer: in_send.at[peer], in_recv)
    pl.semaphore_wait(barrier, N_CHAN - 1 + 3)
    gather_start()
    head[0]()
    inputs[0]()

    level, filled = bucket_ref[0], items_ref[0]
    coefl_ref[...] = levels_ref[level]
    item_blocks = jnp.where(level == 0, 2, jnp.where(level == 1, 4, 8))
    block_id = 2 * (row_id % PAIRS) + jnp.where(lane_id >= HALF, 1, 0)
    bound = jnp.where(row_id < PAIRS, filled * item_blocks, item_blocks)
    aux_ref[...] = jnp.where(block_id < bound, 1.0, 0.0)
    for i in range(8):
        modes_ref[i] = jnp.concatenate([raw_modes_ref[i], raw_modes_ref[i]], axis=1)
    log_dt = row(log_dt_ref, log_dt_ref)
    sigma, step_size = 2.0 * jnp.exp(-log_dt), jnp.exp(log_dt)

    def after_quarter(quarter):
        if quarter == 1:
            gather_cross()

    base = pl.multiple_of(dp * QUARTER, QUARTER)

    def spec_copy(which, r):
        peer = dp_peers[r]
        src, dst = ((spec_send, spec_recv), (sgrad_send.at[peer], sgrad_recv))[which]
        return remote(src, dst.at[dp], spec_ss.at[which, r - 1], spec_rs.at[which, r - 1], dp=peer)

    cauchy_coefficients(modes_ref, sigma, mcoef_ref)
    cauchy_forward(sigma, mcoef_ref, wave_ref, base, sums_ref, spec_send, after_quarter)
    spec_recv[dp] = spec_send[...]
    for r in range(1, 4):
        spec_copy(0, r).start()

    head[1]()
    sums = head_recv[0, 0:16, :]
    for c in range(1, N_CHAN):
        sums = sums + head_recv[c, 0:16, :]
    mean = sums[0:8] * (1.0 / MODEL_WIDTH)
    rstd = lax.rsqrt(sums[8:16] * (1.0 / MODEL_WIDTH) - mean * mean + EPSILON)

    def columns(rows):
        tall = rows.T
        return [jnp.where(low_lanes(ROWS), tall[:, j : j + 1], tall[:, 4 + j : 5 + j]) for j in range(PAIRS)]

    gain1, bias1, skip = row(gain1_ref, gain1_ref), row(bias1_ref, bias1_ref), row(skip_ref, skip_ref)
    mean_cols, rstd_cols = columns(mean), columns(rstd)
    for j in range(PAIRS):
        hat = (tok_ref[j * ROWS : (j + 1) * ROWS, :].astype(F32) - mean_cols[j]) * rstd_cols[j]
        hat_ref[j] = hat
        norm_ref[j] = hat * gain1 + bias1

    downs.y_step(0)
    downs.z_step(1)
    spread_pairs(lambda j, rows: norm_ref[j, rows, :], coefl_ref, 0, tw_ref, 0, 5, rhs_ref)
    transform_into(sig_ref, mat_ref, 0, rhs_ref)
    downs.z_step(3, 2)
    gates.y_step(0)

    for r in range(1, 4):
        spec_copy(0, r).wait_recv()
    for source in range(4):
        store_split(rhs_ref, source * QUARTER, 0, spec_recv[source, :QUARTER, :])
        store_split(rhs_ref, ROWS + source * QUARTER, 0, spec_recv[source, QUARTER:, :])
    freq_ref[:, 0:256] = split_product(mat_ref, 1, rhs_ref, 0, 256)
    even = split_product(mat_ref, 2, rhs_ref, LANES, LANES)
    freq_ref[:, LANES:256] = jnp.where(low_lanes(256), freq_ref[:, LANES:256], even)
    sign = 1.0 - 2.0 * (lax.broadcasted_iota(jnp.int32, (CHUNK, LANES), 0) % 2).astype(F32)
    nyquist = step_size * column_sum(mcoef_ref[0]) * (1.0 / TOK_DEV)

    def store_taps(j, rows, values):
        taps_ref[j, rows, :] = (values + sign * nyquist) * aux_ref[4 + j : 5 + j, :]

    gather_pairs(freq_ref, coefc_ref, 160, tw_ref, 10, 2, store_taps)
    gates.z_step(1, 3)
    downs.y_step(1, 3)
    spread_pairs(lambda j, rows: taps_ref[j, rows, :], coefc_ref, 0, tw_ref, 0, 5, rhs_ref)
    transform_into(ans_ref, mat_ref, 0, rhs_ref)

    gates.z_step(2)
    downs.y_step(2)
    multiply_spectra(sig_ref, ans_ref, rhs_ref, False)
    transform_into(freq_ref, mat_ref, 1, rhs_ref)

    def store_conv(j, rows, values):
        conv_ref[j, rows, :] = values

    gates.y_step(1, 3)
    gather_pairs(freq_ref, coefl_ref, 80, tw_ref, 0, 5, store_conv)
    for j in range(PAIRS):
        mixed = conv_ref[j] * aux_ref[j : j + 1, :] + skip * norm_ref[j]
        cumulative, density = normal_parts(mixed)
        slope_ref[j] = cumulative + mixed * density
        low, high = split_pair(mixed * cumulative)
        acts_send[2 * j] = low.astype(BF16)
        acts_send[2 * j + 1] = high.astype(BF16)
    acts_recv[chan] = acts_send[chan]
    acts = exchange(2, lambda peer: acts_send.at[peer], acts_recv)
    acts[0]()

    def joined(ref, pair, first):
        return join_pair(
            ref[2 * pair, first : first + HALF, :].astype(F32), ref[2 * pair + 1, first : first + HALF, :].astype(F32)
        )

    def lanes_of(pair):
        return slice(pair * LANES, (pair + 1) * LANES)

    def gate_lanes(pair):
        return lanes_of(pair % 2 * 2 + pair // 2)

    def core_copy(which, src, dst):
        return remote(src, dst, core_ss.at[which], core_rs.at[which], dp=sibling)

    def other_core(which, ref):
        return core_copy(which, ref.at[core], ref.at[core])

    inputs[1]()
    for p in range(PAIRS):
        gradf_ref[core, :, lanes_of(p)] = joined(in_recv, p, HALF).astype(BF16)
    launch(other_core(0, gradf_ref))
    gates.y_step(2)
    ups.z_step(1, 3)
    gates_arrived()
    acts[1]()
    for p in range(PAIRS):
        acts_ref[:, gate_lanes(p)] = joined(acts_recv, p, 0).astype(BF16)

    def vector(row, first, second):
        return interleave(head_recv[first, 16 + row : 17 + row, :], head_recv[second, 16 + row : 17 + row, :])

    total = 0.0
    for p in range(PAIRS):
        first = dot_nn(acts_ref[...], wab_ref[2 * p]) + head_recv[2 * p, 16:17, :]
        second = dot_nn(acts_ref[...], wab_ref[2 * p + 1]) + head_recv[2 * p + 1, 16:17, :]
        gate, raw = interleave(first, second)
        swish = lax.logistic(raw)
        gate_ref[p], swish_ref[p] = gate, swish
        resid = joined(in_recv, p, 0) + gate * swish
        res_ref[p] = resid
        total = total + resid
    mean2 = jnp.sum(total, axis=1, keepdims=True) * (1.0 / MODEL_WIDTH)
    total = 0.0
    for p in range(PAIRS):
        centred = res_ref[p] - mean2
        total = total + centred * centred
    rstd2 = lax.rsqrt(jnp.sum(total, axis=1, keepdims=True) * (1.0 / MODEL_WIDTH) + EPSILON)
    gain2 = []
    for p in range(PAIRS):
        gain, bias = vector(1, 2 * p, 2 * p + 1)
        gain2.append(gain)
        hat = (res_ref[p] - mean2) * rstd2
        hat2_ref[p] = hat
        norm2_ref[core, :, lanes_of(p)] = (hat * gain + bias).astype(BF16)
    launch(other_core(1, norm2_ref))
    branch_ref[...] = jnp.zeros_like(branch_ref)
    back2_ref[...] = jnp.zeros_like(back2_ref)
    for c in range(N_CHAN):
        tail_send[c, 3:8, :] = jnp.zeros((5, LANES), F32)
    other_core(0, gradf_ref).wait_recv()
    other_core(1, norm2_ref).wait_recv()

    def both_cores(ref):
        return ref[...].reshape(2 * ROWS, MODEL_WIDTH)

    def hidden_group(r):
        group = z_back[r]
        low, high = 2 * group, 2 * group + 1
        bias = jnp.concatenate(
            [jnp.where(core == 0, head_recv[c, 19:20, :], head_recv[c, 20:21, :]) for c in (low, high)], axis=1
        )
        pre = dot_nn(both_cores(norm2_ref), wup_ref[group]) + bias
        cumulative, density = normal_parts(pre)
        hidden = (pre * cumulative).astype(BF16)
        hid_ref[group] = hidden
        grad = dot_nn(both_cores(gradf_ref), wdn_ref[group]) * (cumulative + pre * density)
        grad = grad.astype(BF16)
        gpre_ref[group] = grad
        sums = column_sum(grad.astype(F32))
        tail_send[low, pl.ds(3 + core, 1), :] = sums[:, 0:LANES]
        tail_send[high, pl.ds(3 + core, 1), :] = sums[:, LANES : 2 * LANES]
        branch_ref[...] += dot_nt(hidden, wdn_ref[group]).reshape(2, ROWS, MODEL_WIDTH)
        back2_ref[...] += dot_nt(grad, wup_ref[group]).reshape(2, ROWS, MODEL_WIDTH)

    ups.y_step(0)
    down_arrived(0)
    hidden_group(0)
    ups.z_step(2)
    for r in (1, 3, 2):
        ups.y_step(r)
        down_arrived(r)
        hidden_group(r)
    half_send[0] = back2_ref[1 - core].astype(BF16)
    launch(core_copy(2, half_send.at[0], half_recv.at[0]))
    half_send[1] = branch_ref[1 - core].astype(BF16)
    launch(core_copy(3, half_send.at[1], half_recv.at[1]))

    def wide(values):
        return values.astype(F32)

    class PlaneBack:
        def __init__(self, which, part, send_view, y_ref, z_ref, total_ref):
            self.which, self.part, self.send_view = which, part, send_view
            self.y_ref, self.z_ref, self.total_ref = y_ref, z_ref, total_ref

        def y_copy(self, r):
            at, which = z_on[r], self.which
            return remote(
                self.send_view(at, 1 - y), self.y_ref.at[r], ry_ss.at[which, r], ry_rs.at[which, r], chan=z * 2 + 1 - y
            )

        def z_copy(self, r):
            which = self.which
            return remote(
                self.send_view(z_on[r], y), self.z_ref.at[r - 1], rz_ss.at[which, r - 1], rz_rs.at[which, r - 1],
                chan=z_on[r] * 2 + y,
            )

        def y_send(self, r, ready=False):
            if not ready:
                self.send_view(z_on[r], 1 - y)[...] = self.part(z_on[r], 1 - y).astype(BF16)
            launch(self.y_copy(r))

        def z_send(self, *steps):
            for r in steps:
                self.y_copy(r).wait_recv()
                total = self.part(z_on[r], y) + wide(self.y_ref[r])
                if r:
                    self.send_view(z_on[r], y)[...] = total.astype(BF16)
                    launch(self.z_copy(r))
                else:
                    self.total_ref[...] = total

        def z_add(self, *steps):
            for r in steps:
                self.z_copy(r).wait_recv()
                self.total_ref[...] += wide(self.z_ref[r - 1])

    def gate_share():
        ref = gab_w_ref.at[:, rows_at(gate_other, 256), :]
        return remote(ref, sib_ab_ref, rsib_ss, rsib_rs, dp=sibling)

    def gate_part(at, line):
        return wide(gab_w_ref[at * 2 + line, rows_at(gate_pair, 256), :]) + wide(sib_ab_ref[at * 2 + line])

    def up_part(at, line):
        return wide(gup_w_ref[at, :, lanes_at(line)])

    def down_share(number, r):
        at = z_on[r]
        return remote(
            gdn_w_ref.at[at, rows_at(dp_others[number] * ROWS, ROWS), :], dp_dn_ref.at[number, r],
            rdn_ss.at[number, r], rdn_rs.at[number, r], dp=dp_others[number],
        )

    def down_sums(r):
        for number in range(3):
            down_share(number, r).wait_recv()
        own = wide(gdn_w_ref[z_on[r], rows_at(own_row, ROWS), :]) + wide(dp_dn_ref[0, r])
        other = wide(dp_dn_ref[1, r]) + wide(dp_dn_ref[2, r])
        for line in range(2):
            lanes = slice(line * LANES, (line + 1) * LANES)
            down_send[z_on[r] * 2 + line] = jnp.concatenate([own[:, lanes], other[:, lanes]], axis=1).astype(BF16)

    gate_g = PlaneBack(
        0, gate_part, lambda at, line: gab_w_ref.at[at * 2 + line, rows_at(gate_pair, 256), :], y_ab_ref, z_ab_ref,
        total_ab_ref,
    )
    up_g = PlaneBack(
        1, up_part, lambda at, line: gup_w_ref.at[at, :, lanes_at(line)], y_up_ref, z_up_ref, total_up_ref
    )
    down_g = PlaneBack(
        2, lambda at, line: wide(down_send[at * 2 + line]), lambda at, line: down_send.at[at * 2 + line], y_dn_ref,
        z_dn_ref, total_dn_ref,
    )

    def hidden_grads(r):
        group = z_on[r]
        gdn_w_ref[group] = dot_nn(gradf_t_ref[...], hid_ref[group]).astype(BF16)
        for number in range(3):
            launch(down_share(number, r))
        gup_w_ref[group] = dot_nn(norm2_t_ref[...], gpre_ref[group]).astype(BF16)
        up_g.y_send(r, ready=True)

    def down_y(*steps):
        for r in steps:
            down_sums(r)
            down_g.y_send(r, ready=True)

    def gate_x():
        return remote(part_ab_ref.at[0], part_ab_ref.at[1], rx_ss, rx_rs, dp=across)

    def gate_last():
        gate_g.z_add(1, 2, 3)
        part_ab_ref[0] = total_ab_ref[rows_at((1 - x) * ROWS, ROWS), :].astype(BF16)
        launch(gate_x())

    def gate_finish():
        gate_x().wait_recv()
        gw_ref[:, 0:128] = total_ab_ref[rows_at(x * ROWS, ROWS), :] + wide(part_ab_ref[1])

    def up_share(number):
        return remote(
            up_send.at[number], dp_up_ref.at[number], rup_ss.at[number], rup_rs.at[number], dp=dp_others[number]
        )

    def up_last():
        up_g.z_add(1, 2, 3)
        for number in range(3):
            up_send[number] = total_up_ref[rows_at(dp_others[number] * ROWS, ROWS), :].astype(BF16)
            launch(up_share(number))

    def up_finish():
        for number in range(3):
            up_share(number).wait_recv()
        gw_ref[:, lanes_at(1 + core)] = total_up_ref[rows_at(own_row, ROWS), :] + wide(dp_up_ref[0])
        gw_ref[:, lanes_at(2 - core)] = wide(dp_up_ref[1]) + wide(dp_up_ref[2])

    def down_last():
        down_g.z_add(1, 2, 3)
        gw_ref[:, lanes_at(3 + core)] = total_dn_ref[:, :LANES]
        gw_ref[:, lanes_at(4 - core)] = total_dn_ref[:, LANES:]

    gradf_t_ref[...] = both_cores(gradf_ref).astype(F32).T.astype(BF16)
    norm2_t_ref[...] = both_cores(norm2_ref).astype(F32).T.astype(BF16)
    for r in (2, 1, 3):
        hidden_grads(r)
    core_copy(2, half_send.at[0], half_recv.at[0]).wait_recv()
    back2 = back2_ref[core] + half_recv[0].astype(F32)
    back2_ref[core] = back2

    mean_q, mean_qx = 0.0, 0.0
    for p in range(PAIRS):
        grad, hat = back2_ref[core, :, lanes_of(p)], hat2_ref[p]
        q = grad * gain2[p]
        mean_q = mean_q + q
        mean_qx = mean_qx + q * hat
        gain_grad, bias_grad = interleave(column_sum(grad * hat), column_sum(grad))
        tail_send[2 * p, 1:2, :] = gain_grad
        first, second = interleave(turn_half(column_sum(grad * hat)), turn_half(column_sum(grad)))
        tail_send[2 * p + 1, 1:2, :] = first
    mean_q = jnp.sum(mean_q, axis=1, keepdims=True) * (1.0 / MODEL_WIDTH)
    mean_qx = jnp.sum(mean_qx, axis=1, keepdims=True) * (1.0 / MODEL_WIDTH)
    for p in range(PAIRS):
        hat = hat2_ref[p]
        extra = rstd2 * (back2_ref[core, :, lanes_of(p)] * gain2[p] - mean_q - hat * mean_qx)
        grad_f = joined(in_recv, p, HALF)
        grad_resid = grad_f + extra
        gate, swish = gate_ref[p], swish_ref[p]
        grad_a = (grad_resid * swish).astype(BF16).astype(F32)
        grad_b = (grad_resid * gate * swish * (1.0 - swish)).astype(BF16).astype(F32)
        first, second = interleave(grad_a, grad_b)
        gab_ref[2 * p] = first.astype(BF16)
        gab_ref[2 * p + 1] = second.astype(BF16)
        tail_send[2 * p, 0:1, :] = column_sum(first)
        tail_send[2 * p + 1, 0:1, :] = column_sum(second)
        low, high = interleave(column_sum(grad_f), column_sum(grad_f))
        tail_send[2 * p, 2:3, :] = low
        tail_send[2 * p + 1, 2:3, :] = high
        low, high = split_pair(extra)
        late_send[2 * p, HALF:, :] = low.astype(BF16)
        late_send[2 * p + 1, HALF:, :] = high.astype(BF16)
    grad_acts = 0.0
    for c in range(N_CHAN):
        grad_acts = grad_acts + dot_nt(gab_ref[c], wab_ref[c])
    for p in range(PAIRS):
        low, high = split_pair(grad_acts[:, gate_lanes(p)])
        back_send[2 * p] = low.astype(BF16)
        back_send[2 * p + 1] = high.astype(BF16)
    back_recv[chan] = back_send[chan]
    back = exchange(3, lambda peer: back_send.at[peer], back_recv)
    back[0]()

    hidden_grads(0)
    acts_t_ref[...] = acts_ref[...].astype(F32).T.astype(BF16)
    for c in range(N_CHAN):
        gab_w_ref[c] = dot_nn(acts_t_ref[...], gab_ref[c]).astype(BF16)
    launch(gate_share())
    down_y(2, 1, 3, 0)
    up_g.z_send(2, 1, 3, 0)
    core_copy(3, half_send.at[1], half_recv.at[1]).wait_recv()
    for p in range(PAIRS):
        out = res_ref[p] + (branch_ref[core, :, lanes_of(p)] + half_recv[1, :, lanes_of(p)].astype(F32)) + interleave(head_recv[2 * p, 18:19, :], head_recv[2 * p + 1, 18:19, :])[0]
        low, high = split_pair(out)
        late_send[2 * p, :HALF, :] = low.astype(BF16)
        late_send[2 * p + 1, :HALF, :] = high.astype(BF16)
    late_recv[chan] = late_send[chan]
    tail_recv[chan] = tail_send[chan]
    late = exchange(4, lambda peer: late_send.at[peer], late_recv)
    tail = exchange(5, lambda peer: tail_send.at[peer], tail_recv)
    late[0]()
    tail[0]()
    gate_share().wait_recv()
    for r in (2, 1, 3, 0):
        gate_g.y_send(r)
    down_g.z_send(2, 1, 3, 0)

    back[1]()
    skip_grad = 0.0
    for j in range(PAIRS):
        grad = joined(back_recv, j, 0) * slope_ref[j]
        slope_ref[j] = grad
        conv_ref[j] = grad * aux_ref[j : j + 1, :]
        skip_grad = skip_grad + column_sum(grad * norm_ref[j])
    spread_pairs(lambda j, rows: conv_ref[j, rows, :], coefl_ref, 0, tw_ref, 0, 5, rhs_ref)
    transform_into(freq_ref, mat_ref, 0, rhs_ref)
    multiply_spectra(sig_ref, freq_ref, rhs_ref, True)
    transform_into(sig_ref, mat_ref, 1, rhs_ref)

    def store_kernel_grad(j, rows, values):
        taps_ref[j, rows, :] = values * aux_ref[4 + j : 5 + j, :]

    gather_pairs(sig_ref, coefc_ref, 80, tw_ref, 0, 5, store_kernel_grad)
    nyquist_grad = 0.0
    for j in range(PAIRS):
        whole_sign = 1.0 - 2.0 * (lax.broadcasted_iota(jnp.int32, (ROWS, LANES), 0) % 2).astype(F32)
        nyquist_grad = nyquist_grad + column_sum(taps_ref[j] * whole_sign)
    nyquist_grad = fold(nyquist_grad) * (1.0 / TOK_DEV)
    spread_pairs(lambda j, rows: taps_ref[j, rows, :], coefc_ref, 192, tw_ref, 10, 2, rhs_ref)
    taps_freq_ref[...] = split_product(mat_ref, 0, rhs_ref, 0, 256)
    even = split_product(mat_ref, 3, rhs_ref, LANES, LANES)
    taps_freq_ref[:, LANES:256] = jnp.where(low_lanes(256), taps_freq_ref[:, LANES:256], even)
    for source in range(4):
        rows = slice(source * QUARTER, (source + 1) * QUARTER)
        sgrad_send[source, :QUARTER, :] = taps_freq_ref[rows, :]
        sgrad_send[source, QUARTER:, :] = taps_freq_ref[ROWS + source * QUARTER : ROWS + (source + 1) * QUARTER, :]
    sgrad_recv[dp] = sgrad_send[dp]
    for r in range(1, 4):
        spec_copy(1, r).start()

    gate_g.z_send(2, 1, 3, 0)
    multiply_spectra(ans_ref, freq_ref, rhs_ref, True)
    transform_into(freq_ref, mat_ref, 1, rhs_ref)
    gather_pairs(freq_ref, coefl_ref, 80, tw_ref, 0, 5, store_conv)
    gain_grad, bias_grad = 0.0, 0.0
    scaled, crossed = [], []
    for j in range(PAIRS):
        grad = conv_ref[j] + skip * slope_ref[j]
        conv_ref[j] = grad
        gain_grad = gain_grad + column_sum(grad * hat_ref[j])
        bias_grad = bias_grad + column_sum(grad)
    conv = conv_ref[...].reshape(PAIRS * ROWS, LANES) * gain1
    for i, sums in enumerate(
        token_sums(split(conv)) + token_sums(split(conv * hat_ref[...].reshape(PAIRS * ROWS, LANES)))
    ):
        sum_send[i : i + 1, :] = sums
    sum_recv[chan] = sum_send[...]
    sums_back = exchange(6, lambda peer: sum_send, sum_recv)
    sums_back[0]()

    for r in range(1, 4):
        spec_copy(1, r).wait_recv()
    sgrad_ref[...] = sgrad_recv[0] + sgrad_recv[1] + sgrad_recv[2] + sgrad_recv[3]

    def after_part(part):
        if part == 1:
            up_last()
        elif part == 3:
            down_last()
            gate_last()

    mode_grads, dt_grad = cauchy_backward(
        modes_ref, sigma, nyquist_grad, step_size, mcoef_ref, wave_ref, base, sums_ref, sgrad_ref, pgrad_ref, mback_ref,
        after_part,
    )
    mask = low_lanes(32)
    for i in range(4):
        dp_send[i * 32 : (i + 1) * 32, :] = jnp.where(mask, mode_grads[i], mode_grads[i + 4])
    first = low_lanes(1)
    dp_send[128:129, :] = jnp.where(first, dt_grad, fold(skip_grad))
    dp_send[129:130, :] = jnp.where(first, fold(gain_grad), fold(bias_grad))
    dp_send[130:136, :] = jnp.zeros((6, LANES), F32)
    tail[1]()
    tail_sum = tail_recv[0]
    for c in range(1, N_CHAN):
        tail_sum = tail_sum + tail_recv[c]
    dp_send[136:144, :] = tail_sum
    dp_recv[0] = dp_send[...]

    def dp_copy(r):
        return remote(dp_send, dp_recv.at[r], dp_ss.at[r - 1], dp_rs.at[r - 1], dp=dp_peers[r])

    for r in range(1, 4):
        dp_copy(r).start()

    sums_back[1]()
    sums = sum_recv[0]
    for c in range(1, N_CHAN):
        sums = sums + sum_recv[c]
    sums = sums * (1.0 / MODEL_WIDTH)
    rstd_cols, q_cols, qx_cols = columns(rstd), columns(sums[0:8]), columns(sums[8:16])
    late[1]()
    for j in range(PAIRS):
        rows = slice(j * ROWS, (j + 1) * ROWS)
        out_ref[rows, :] = joined(late_recv, j, 0).astype(BF16)
        dtok_ref[rows, :] = joined(late_recv, j, HALF) + rstd_cols[j] * (
            conv_ref[j] * gain1 - q_cols[j] - hat_ref[j] * qx_cols[j]
        )
    for r in range(1, 4):
        dp_copy(r).wait_recv()
    total = dp_recv[0] + dp_recv[1] + dp_recv[2] + dp_recv[3]
    gm_ref[...] = total[0:128]
    gv_ref[...] = total[128:144]
    gate_finish()
    up_finish()
    for copy in pending:
        copy.wait_send()
    for group in (head, inputs, acts, back, late, tail, sums_back):
        group[2]()
    for r in range(1, 4):
        dp_copy(r).wait_send()
        spec_copy(0, r).wait_send()
        spec_copy(1, r).wait_send()


def unpack_kernel(
    out_ref, dtok_ref, gw_ref, gm_ref, gv_ref, cotangent_ref,
    output_ref, tokens_ref, gain1_ref, bias1_ref, modes_ref, dt_ref, skip_ref, wa_ref, ba_ref, wb_ref, bb_ref,
    gain2_ref, bias2_ref, up_ref, bup_ref, down_ref, bdown_ref,
):
    for j in range(PAIRS):
        out = out_ref[j * ROWS : (j + 1) * ROWS, :].astype(F32).T.astype(BF16)
        grad = dtok_ref[j * ROWS : (j + 1) * ROWS, :].T
        for h in range(2):
            lanes, rows = slice((2 * j + h) * ROWS, (2 * j + h + 1) * ROWS), slice(h * HALF, (h + 1) * HALF)
            output_ref[:, lanes] = out[rows]
            tokens_ref[:, lanes] = cotangent_ref[:, lanes] + grad[rows]
    for i in range(8):
        modes_ref[i] = gm_ref[i % 4 * 32 : i % 4 * 32 + 32, i // 4 * HALF : (i // 4 + 1) * HALF]
    gates = gw_ref[:, :LANES].T
    wa_ref[...] = gates[:HALF]
    wb_ref[...] = gates[HALF:]
    up_ref[...] = gw_ref[:, 128:384]
    down_ref[...] = gw_ref[:, 384:640].T
    for at, low, high in (
        (0, dt_ref, skip_ref), (1, gain1_ref, bias1_ref), (8, ba_ref, bb_ref), (9, gain2_ref, bias2_ref),
    ):
        low[...] = gv_ref[at, :HALF]
        high[...] = gv_ref[at, HALF:]
    bdown_ref[...] = gv_ref[10, :HALF]
    bup_ref[:LANES] = gv_ref[11, :]
    bup_ref[LANES:] = gv_ref[12, :]


def block_program():
    mats, twiddle, levels, constant, wave = mixer_tables()

    def run(tokens, cotangent, bucket, items, gain1, bias1, modes, log_dt, skip, w_a, b_a, w_b, b_b, gain2, bias2, w_up, b_up, w_down, b_down):
        vmem = pl.BlockSpec(memory_space=pltpu.VMEM)
        smem = pl.BlockSpec(memory_space=pltpu.SMEM)
        dma = pltpu.SemaphoreType.DMA

        def buf(*shape):
            return pltpu.VMEM(shape, F32)

        def low(*shape):
            return pltpu.VMEM(shape, BF16)

        def full(*shape):
            return jax.ShapeDtypeStruct(shape, F32)

        big, wide = (PAIRS, ROWS, LANES), (256, WIDE)
        packed = pl.pallas_call(
            block_kernel,
            out_shape=(
                jax.ShapeDtypeStruct((512, LANES), BF16), full(512, LANES), full(ROWS, WIDE), full(ROWS, LANES),
                full(16, LANES),
            ),
            in_specs=[smem] * 2 + [vmem] * 22,
            out_specs=(vmem,) * 5,
            scratch_shapes=[
                low(512, LANES), buf(8, LANES), buf(160, LANES), buf(8, 32, LANES),
                low(N_CHAN, 512, 128), low(4, 512, 256), low(4, 512, 256),
                low(N_CHAN, 512, 128), low(4, 512, 256), low(4, 512, 256),
                low(ROWS, 256), low(N_CHAN, ROWS, 256), low(N_CHAN, 256, LANES),
                low(4, 256, LANES), low(4, 512, LANES), low(4, ROWS, 256), low(3, 256, LANES), low(3, 512, LANES), low(3, ROWS, 256),
                low(3, ROWS, LANES), low(3, 4, ROWS, 256), low(3, ROWS, LANES), low(N_CHAN, ROWS, 256), low(2, ROWS, LANES),
                buf(256, LANES), buf(512, LANES), buf(ROWS, 256),
                low(N_CHAN, ROWS, LANES), low(N_CHAN, ROWS, LANES), buf(24, LANES), buf(N_CHAN, 24, LANES),
                low(N_CHAN, HALF, LANES), low(N_CHAN, HALF, LANES), low(N_CHAN, HALF, LANES), low(N_CHAN, HALF, LANES),
                low(N_CHAN, ROWS, LANES), low(N_CHAN, ROWS, LANES),
                buf(16, LANES), buf(N_CHAN, 16, LANES), buf(N_CHAN, 8, LANES), buf(N_CHAN, 8, LANES),
                buf(144, LANES), buf(4, 144, LANES), buf(64, 256), buf(4, 64, 256), buf(4, 64, 256), buf(4, 64, 256),
                buf(*big), buf(*big), buf(*big), buf(*big), low(2, *wide), buf(*wide), buf(*wide), buf(*wide), buf(*big),
                buf(10, 32, LANES), buf(2, 16, QUARTER, LANES), buf(2, 16, QUARTER, LANES), buf(10, 32, LANES),
                buf(64, 256), buf(256, 256),
                buf(*big), buf(*big), buf(*big), buf(*big), low(ROWS, 512), low(2, ROWS, 512), low(2, ROWS, 512),
                buf(2, ROWS, 512), buf(2, ROWS, 512), low(2, ROWS, 512), low(2, ROWS, 512),
                low(N_CHAN, ROWS, LANES), low(4, 256, 256), low(4, 256, 256), low(512, ROWS), low(512, 256), low(512, 256),
                dma((3, 3)), dma((3, 3)), dma((3, 4)), dma((3, 4)), dma, dma, dma((3,)), dma((3,)), dma((24,)), dma((24,)),
                dma((8,)), dma((8,)), dma((4,)), dma((4,)),
                dma((3, 3)), dma((3, 3)), dma((3, 4)), dma((3, 4)), dma, dma, dma((3,)), dma((3,)), dma((3, 4)), dma((3, 4)),
                dma, dma,
                dma((7, 7)), dma((7, 7)), dma((3,)), dma((3,)), dma((2, 3)), dma((2, 3)),
            ],
            compiler_params=pltpu.CompilerParams(
                collective_id=0, has_side_effects=True, vmem_limit_bytes=60 * 1024 * 1024
            ),
            name="block",
        )(
            bucket, items, tokens.T, cotangent.T, gain1, bias1, jnp.swapaxes(modes, 1, 2), log_dt, skip,
            w_a.T, b_a, w_b.T, b_b, gain2, bias2,
            w_up, b_up, w_down, b_down, levels, constant, mats, twiddle, wave,
        )
        small = full(HALF)
        results = pl.pallas_call(
            unpack_kernel,
            out_shape=(
                jax.ShapeDtypeStruct((HALF, TOK_DEV), BF16), full(HALF, TOK_DEV), small, small, full(8, 32, HALF),
                small, small, full(HALF, ROWS), small, full(HALF, ROWS), small, small, small, full(ROWS, 256),
                full(256), full(256, ROWS), small,
            ),
            in_specs=[vmem] * 6,
            out_specs=(vmem,) * 17,
            name="unpack",
        )(*packed, cotangent.T)
        turned = {0, 1, 4, 7, 9}
        return tuple(jnp.swapaxes(r, -1, -2) if i in turned else r for i, r in enumerate(results))

    return run


def solution(mesh):
    small = mesh.shape["chan"] == N_CHAN and mesh.shape["dp"] == 4
    return jax.shard_map(
        block_program() if small else shards,
        mesh=mesh,
        in_specs=(
            P("dp", "chan"),
            P("dp", "chan"),
            P("dp"),
            P("dp"),
            P("chan"),
            P("chan"),
            P(None, "chan", None),
            P("chan"),
            P("chan"),
            P("dp", "chan"),
            P("chan"),
            P("dp", "chan"),
            P("chan"),
            P("chan"),
            P("chan"),
            P("dp", "chan"),
            P("chan"),
            P("chan", "dp"),
            P("chan"),
        ),
        out_specs=(
            P("dp", "chan"),
            P("dp", "chan"),
            P("chan"),
            P("chan"),
            P(None, "chan", None),
            P("chan"),
            P("chan"),
            P("dp", "chan"),
            P("chan"),
            P("dp", "chan"),
            P("chan"),
            P("chan"),
            P("chan"),
            P("dp", "chan"),
            P("chan"),
            P("chan", "dp"),
            P("chan"),
        ),
        check_vma=False,
    )
```

```python
import math

import jax
import jax.numpy as jnp
import ml_dtypes
import numpy as np
from jax import lax
from jax.experimental import pallas as pl
from jax.experimental.pallas import tpu as pltpu
from jax.sharding import PartitionSpec as P

MODEL_WIDTH = 512
TOK_DEV = 1024


HIGHEST = lax.Precision.HIGHEST
EPSILON = 1e-05


def product(left, right):
    return jnp.dot(left, right, preferred_element_type=jnp.float32)


def product_nt(left, right):
    return lax.dot_general(
        left, right, (((1,), (1,)), ((), ())), preferred_element_type=jnp.float32
    )


def product_tn(left, right):
    return lax.dot_general(
        left, right, (((0,), (0,)), ((), ())), preferred_element_type=jnp.float32
    )


def gelu_slope(values):
    return (
        0.5 * (1.0 + lax.erf(values * 0.7071067811865476))
        + values * jnp.exp(-0.5 * values * values) * 0.3989422804014327
    )


def half_angles(length):
    angle = np.arange(length // 2 + 1, dtype=np.float64) * (math.pi / length)
    cosine, sine = np.cos(angle), np.sin(angle)
    cosine[-1] = 0.0
    return cosine.astype(np.float32), sine.astype(np.float32)


def inverse_tables(length):
    freq = np.arange(length // 2 + 1)
    turn = (freq[:, None] * np.arange(length)[None, :]) % length * (2.0 * math.pi / length)
    weight = np.where((freq == 0) | (freq == length // 2), 1.0, 2.0)[:, None] / length
    return (weight * np.cos(turn)).astype(np.float32), (weight * np.sin(turn)).astype(np.float32)


def high_einsum(form, left, right):
    return jnp.einsum(form, left, right, precision=HIGHEST)


def ssm_kernel(modes, log_dt):
    cos_h, sin_h = half_angles(TOK_DEV)
    index = jnp.arange(modes.shape[2], dtype=jnp.int32).astype(jnp.float32)
    lam_re = -0.5 * jnp.exp(modes[0])
    lam_im = math.pi * (index + modes[1])
    rank_re, rank_im, in_re, in_im, out_re, out_im = (modes[i] for i in range(2, 8))
    sigma = (2.0 * jnp.exp(-log_dt))[:, None]

    def points(values):
        return values.T[:, None, :]

    den_re = points(lam_re * lam_re + lam_im * lam_im) * (cos_h * cos_h)[:, None] - (
        sigma * sigma
    ).T * (sin_h * sin_h)[:, None]
    den_im = points(-2.0 * sigma * lam_re) * (sin_h * cos_h)[:, None]
    den_sq = den_re * den_re + den_im * den_im
    inv_re = den_re / den_sq
    inv_im = -den_im / den_sq
    sums = []
    for real, imag in (
        (out_re * in_re + out_im * in_im, out_re * in_im - out_im * in_re),
        (out_re * rank_re + out_im * rank_im, out_re * rank_im - out_im * rank_re),
        (rank_re * in_re + rank_im * in_im, rank_re * in_im - rank_im * in_re),
        (rank_re * rank_re + rank_im * rank_im, jnp.zeros_like(rank_re)),
    ):
        turned = points(real * lam_re + imag * lam_im)
        real = points(real)
        p_re, p_im = jnp.sum(real * inv_re, axis=0), jnp.sum(real * inv_im, axis=0)
        q_re, q_im = jnp.sum(turned * inv_re, axis=0), jnp.sum(turned * inv_im, axis=0)
        sine = sin_h[:, None] * sigma.T
        sums.append((-sine * p_im - cos_h[:, None] * q_re, sine * p_re - cos_h[:, None] * q_im))
    (cross_re, cross_im), (left_re, left_im), (right_re, right_im), (self_re, self_im) = sums
    twice = 2.0 * cos_h[:, None]
    loop_re, loop_im = 1.0 + twice * self_re, twice * self_im
    back_re, back_im = twice * right_re, twice * right_im
    loop_sq = loop_re * loop_re + loop_im * loop_im
    ratio_re = (back_re * loop_re + back_im * loop_im) / loop_sq
    ratio_im = (back_im * loop_re - back_re * loop_im) / loop_sq
    part_re = cross_re - (left_re * ratio_re - left_im * ratio_im)
    part_im = cross_im - (left_re * ratio_im + left_im * ratio_re)
    spec_re = 2.0 * (cos_h[:, None] * part_re - sin_h[:, None] * part_im)
    spec_im = 2.0 * (cos_h[:, None] * part_im + sin_h[:, None] * part_re)
    cos_tab, sin_tab = inverse_tables(TOK_DEV)
    return high_einsum("kl,kc->lc", cos_tab, spec_re) - high_einsum("kl,kc->lc", sin_tab, spec_im)


BLOCK = 128
BLOCKS = TOK_DEV // BLOCK
FIRST = 2 * BLOCKS
KEPT = FIRST // 2 + 1


def transform_tables():
    length = 2 * TOK_DEV
    turn = np.arange(KEPT)[:, None] * np.arange(BLOCK)[None, :] * (2.0 * math.pi / length)
    small = np.arange(BLOCK)[:, None] * np.arange(BLOCK)[None, :] % BLOCK * (2.0 * math.pi / BLOCK)
    spots = np.stack([np.arange(BLOCKS) + np.arange(BLOCKS) // (2 << b) * (2 << b) for b in range(3)])
    angle = spots[:, None, :] * np.arange(KEPT)[None, :, None] % FIRST * (2.0 * math.pi / FIRST)
    parts = (np.cos(turn), np.sin(turn), np.cos(small), np.sin(small), np.cos(angle), np.sin(angle))
    return [part.astype(np.float32) for part in parts]


def forward_transform(blocks, cos_a, sin_a):
    cos_t, sin_t, cos_s, sin_s, _, _ = transform_tables()
    step_re = high_einsum("ka,abc->kbc", cos_a, blocks)
    step_im = -high_einsum("ka,abc->kbc", sin_a, blocks)
    turned_re = step_re * cos_t[..., None] + step_im * sin_t[..., None]
    turned_im = step_im * cos_t[..., None] - step_re * sin_t[..., None]
    both = jnp.concatenate([turned_re, turned_im], axis=1)
    matrix = np.block([[cos_s, sin_s], [-sin_s, cos_s]])
    return high_einsum("pb,kbc->kpc", matrix, both)


def inverse_transform(spectrum, cos_a, sin_a):
    cos_t, sin_t, cos_s, sin_s, _, _ = transform_tables()
    matrix = np.block([[cos_s, -sin_s], [sin_s, cos_s]])
    both = high_einsum("bp,kpc->kbc", matrix, spectrum)
    step_re, step_im = both[:, :BLOCK], both[:, BLOCK:]
    turned_re = step_re * cos_t[..., None] - step_im * sin_t[..., None]
    turned_im = step_im * cos_t[..., None] + step_re * sin_t[..., None]
    weight = np.where(np.arange(KEPT) % (KEPT - 1) == 0, 1.0, 2.0).astype(np.float32) / (2 * TOK_DEV)
    return high_einsum("ka,kbc->abc", cos_a * weight[:, None], turned_re) - high_einsum(
        "ka,kbc->abc", sin_a * weight[:, None], turned_im
    )


def multiply(left, right):
    left_re, left_im = left[:, :BLOCK], left[:, BLOCK:]
    right_re, right_im = right[:, :BLOCK], right[:, BLOCK:]
    return jnp.concatenate(
        [left_re * right_re - left_im * right_im, left_re * right_im + left_im * right_re], axis=1
    )


def mixer(normed, kernel_taps, skip_gain, bucket, filled):
    _, _, _, _, cos_a, sin_a = transform_tables()
    cos_x, sin_x = jnp.asarray(cos_a)[bucket], jnp.asarray(sin_a)[bucket]
    item_blocks = 2 << bucket
    block_id = jnp.arange(BLOCKS, dtype=jnp.int32)[:, None, None]
    taps = jnp.where(block_id < item_blocks, kernel_taps.reshape(BLOCKS, BLOCK, -1), 0.0)
    signal = forward_transform(normed.reshape(BLOCKS, BLOCK, -1), cos_x, sin_x)
    answer = forward_transform(taps, cos_a[2], sin_a[2])
    result = inverse_transform(multiply(signal, answer), cos_x, sin_x)
    result = jnp.where(block_id < filled * item_blocks, result, 0.0)
    return result.reshape(normed.shape) + skip_gain * normed


def shards(
    tokens,
    cotangent,
    group_bucket,
    group_items,
    first_norm_gain,
    first_norm_bias,
    modes,
    log_dt,
    d_skip,
    w_a,
    b_a,
    w_b,
    b_b,
    second_norm_gain,
    second_norm_bias,
    w_up,
    b_up,
    w_down,
    b_down,
):
    input_tokens = tokens.astype(jnp.float32)
    sums_in = lax.psum(
        (jnp.sum(input_tokens, axis=1), jnp.sum(input_tokens * input_tokens, axis=1)), "chan"
    )
    input_average = sums_in[0][:, None] / MODEL_WIDTH
    input_inverse_deviation = lax.rsqrt(
        sums_in[1][:, None] / MODEL_WIDTH - input_average * input_average + EPSILON
    )
    input_standardized = (input_tokens - input_average) * input_inverse_deviation
    input_normalized = input_standardized * first_norm_gain + first_norm_bias
    level = group_bucket[0]
    filled = group_items[0]
    kernel_taps, kernel_back = jax.vjp(ssm_kernel, modes, log_dt)

    def local_mix(values, taps_now, skip_gain):
        return mixer(values, taps_now, skip_gain, level, filled)

    mixed, mix_back = jax.vjp(local_mix, input_normalized, kernel_taps, d_skip)
    acts_low = jax.nn.gelu(mixed, approximate=False).astype(jnp.bfloat16)
    wa_full, wb_full, up_full, down_full = (
        lax.all_gather(w_a.astype(jnp.bfloat16), "dp", axis=0, tiled=True),
        lax.all_gather(w_b.astype(jnp.bfloat16), "dp", axis=0, tiled=True),
        lax.all_gather(w_up.astype(jnp.bfloat16), "dp", axis=0, tiled=True),
        lax.all_gather(w_down.astype(jnp.bfloat16), "dp", axis=1, tiled=True),
    )
    acts_full = lax.all_gather(acts_low, "chan", axis=1, tiled=True)
    gate_a = product(acts_full, wa_full) + b_a
    gate_b = product(acts_full, wb_full) + b_b
    gate_sig = jax.nn.sigmoid(gate_b)
    residual_stream = input_tokens + gate_a * gate_sig
    sums_mid = lax.psum(
        (jnp.sum(residual_stream, axis=1), jnp.sum(residual_stream * residual_stream, axis=1)),
        "chan",
    )
    middle_average = sums_mid[0][:, None] / MODEL_WIDTH
    middle_inverse_deviation = lax.rsqrt(
        sums_mid[1][:, None] / MODEL_WIDTH - middle_average * middle_average + EPSILON
    )
    middle_standardized = (residual_stream - middle_average) * middle_inverse_deviation
    middle_reduced = (middle_standardized * second_norm_gain + second_norm_bias).astype(
        jnp.bfloat16
    )
    mid_full = lax.all_gather(middle_reduced, "chan", axis=1, tiled=True)
    pre_act = product(mid_full, up_full) + b_up
    hidden_low = jax.nn.gelu(pre_act, approximate=False).astype(jnp.bfloat16)
    branch = (
        lax.psum_scatter(product(hidden_low, down_full), "chan", scatter_dimension=1, tiled=True)
        + b_down
    )
    output = (residual_stream + branch).astype(jnp.bfloat16)
    grad_f = cotangent.astype(jnp.bfloat16)
    grad_b_down = jnp.sum(grad_f.astype(jnp.float32), axis=0)
    grad_f_full = lax.all_gather(grad_f, "chan", axis=1, tiled=True)
    grad_w_down = product_tn(hidden_low, grad_f_full)
    grad_pre = (product_nt(grad_f_full, down_full) * gelu_slope(pre_act)).astype(jnp.bfloat16)
    grad_b_up = jnp.sum(grad_pre.astype(jnp.float32), axis=0)
    grad_w_up = product_tn(mid_full, grad_pre)
    middle_gradient = lax.psum_scatter(
        product_nt(grad_pre, up_full), "chan", scatter_dimension=1, tiled=True
    )
    second_norm_gain_gradient = jnp.sum(middle_gradient * middle_standardized, axis=0)
    grad_ln2_bias = jnp.sum(middle_gradient, axis=0)
    middle_rescaled = middle_gradient * second_norm_gain
    middle_backward = lax.psum(
        (jnp.sum(middle_rescaled, axis=1), jnp.sum(middle_rescaled * middle_standardized, axis=1)),
        "chan",
    )
    grad_resid = cotangent + middle_inverse_deviation * (
        middle_rescaled
        - middle_backward[0][:, None] / MODEL_WIDTH
        - middle_standardized * middle_backward[1][:, None] / MODEL_WIDTH
    )
    grad_a = (grad_resid * gate_sig).astype(jnp.bfloat16)
    grad_b = (grad_resid * gate_a * gate_sig * (1.0 - gate_sig)).astype(jnp.bfloat16)
    grad_b_a = jnp.sum(grad_a.astype(jnp.float32), axis=0)
    grad_b_b = jnp.sum(grad_b.astype(jnp.float32), axis=0)
    grad_w_a = product_tn(acts_full, grad_a)
    grad_w_b = product_tn(acts_full, grad_b)
    grad_acts = lax.psum_scatter(
        product_nt(grad_a, wa_full) + product_nt(grad_b, wb_full),
        "chan",
        scatter_dimension=1,
        tiled=True,
    )
    grad_mixed = grad_acts * gelu_slope(mixed)
    normalized_gradient, grad_kernel, grad_skip = mix_back(grad_mixed)
    grad_modes, grad_log_dt = kernel_back(grad_kernel)
    first_norm_gain_gradient = jnp.sum(normalized_gradient * input_standardized, axis=0)
    grad_ln1_bias = jnp.sum(normalized_gradient, axis=0)
    input_rescaled = normalized_gradient * first_norm_gain
    input_backward = lax.psum(
        (jnp.sum(input_rescaled, axis=1), jnp.sum(input_rescaled * input_standardized, axis=1)),
        "chan",
    )
    grad_tokens = grad_resid + input_inverse_deviation * (
        input_rescaled
        - input_backward[0][:, None] / MODEL_WIDTH
        - input_standardized * input_backward[1][:, None] / MODEL_WIDTH
    )
    grad_w_a, grad_w_b, grad_w_up, grad_w_down = (
        lax.psum_scatter(grad_w_a, "dp", scatter_dimension=0, tiled=True),
        lax.psum_scatter(grad_w_b, "dp", scatter_dimension=0, tiled=True),
        lax.psum_scatter(grad_w_up, "dp", scatter_dimension=0, tiled=True),
        lax.psum_scatter(grad_w_down, "dp", scatter_dimension=1, tiled=True),
    )
    (
        first_norm_gain_gradient,
        grad_ln1_bias,
        grad_modes,
        grad_log_dt,
        grad_skip,
        grad_b_a,
        grad_b_b,
        second_norm_gain_gradient,
        grad_ln2_bias,
        grad_b_up,
        grad_b_down,
    ) = lax.psum(
        (
            first_norm_gain_gradient,
            grad_ln1_bias,
            grad_modes,
            grad_log_dt,
            grad_skip,
            grad_b_a,
            grad_b_b,
            second_norm_gain_gradient,
            grad_ln2_bias,
            grad_b_up,
            grad_b_down,
        ),
        "dp",
    )
    return (
        output,
        grad_tokens,
        first_norm_gain_gradient,
        grad_ln1_bias,
        grad_modes,
        grad_log_dt,
        grad_skip,
        grad_w_a,
        grad_b_a,
        grad_w_b,
        grad_b_b,
        second_norm_gain_gradient,
        grad_ln2_bias,
        grad_w_up,
        grad_b_up,
        grad_w_down,
        grad_b_down,
    )


LANES = 128
HALF = 64
PAIRS = 4
ROWS = 128
N_CHAN = 8
WIDE = 640
MESH = pl.DeviceIdType.MESH
F32 = jnp.float32
BF16 = jnp.bfloat16


def split_two(matrix):
    high = matrix.astype(ml_dtypes.bfloat16)
    low = (matrix - high.astype(np.float64)).astype(ml_dtypes.bfloat16)
    return np.concatenate([high, low], axis=1)


def lane_rows(values_low, values_high):
    return np.repeat(np.stack([values_low, values_high], -1), HALF, axis=-1)


def mixer_tables():
    line = np.arange(ROWS)
    small = np.outer(line, line) % ROWS * (2.0 * math.pi / ROWS)
    cos_s, sin_s = np.cos(small), np.sin(small)
    forward = np.block([[cos_s, sin_s], [-sin_s, cos_s]])
    real = np.zeros((2 * ROWS, 2 * ROWS))
    for row in range(HALF):
        weight = 1.0 if row == 0 else 2.0
        turn = 2.0 * math.pi / ROWS * row * line
        real[:ROWS, row] = weight * np.cos(turn)
        real[:ROWS, ROWS + row] = -weight * np.sin(turn)
        turn = 2.0 * math.pi / TOK_DEV * (4 + 8 * row) * line
        real[ROWS:, HALF + row] = 2.0 * np.cos(turn)
        real[ROWS:, ROWS + HALF + row] = -2.0 * np.sin(turn)
    mats = np.stack([split_two(m) for m in (forward, forward.T, real, real.T)])

    twiddle = []
    for pair in range(5):
        turn = np.stack([line * k * (math.pi / TOK_DEV) for k in (2 * pair, 2 * pair + 1)])
        twiddle += [lane_rows(np.cos(turn[0]), np.cos(turn[1])), lane_rows(np.sin(turn[0]), np.sin(turn[1]))]
    for first, second in ((1, 2), (3, 0)):
        turn = np.stack([line * k * (2.0 * math.pi / TOK_DEV) for k in (first, second)])
        twiddle += [lane_rows(np.cos(turn[0]), np.cos(turn[1])), lane_rows(np.sin(turn[0]), np.sin(turn[1]))]

    def forward_rows(coef, pairs):
        out = []
        for low, high in pairs:
            for part in range(2):
                for j in range(PAIRS):
                    out.append(lane_rows(coef(2 * j, low, part), coef(2 * j + 1, high, part)))
                for j in range(PAIRS):
                    out.append(lane_rows(coef(2 * j, high, part), coef(2 * j + 1, low, part)))
        return np.stack(out)

    def inverse_rows(coef, pairs):
        out = []
        for low, high in pairs:
            for part in range(2):
                for j in range(PAIRS):
                    out.append(lane_rows(coef(2 * j, low, part), coef(2 * j + 1, high, part)))
                for j in range(PAIRS):
                    out.append(lane_rows(coef(2 * j + 1, low, part), coef(2 * j, high, part)))
        return np.stack(out)

    levels = []
    pairs = [(2 * p, 2 * p + 1) for p in range(5)]
    for level in range(3):
        item = 2 << level

        def angle(block, k):
            return 2.0 * math.pi / 16 * ((block + block // item * item) * k % 16)

        def fwd(block, k, part):
            if k > 8:
                return np.zeros(())
            return np.cos(angle(block, k)) if part == 0 else -np.sin(angle(block, k))

        def inv(block, k, part):
            weight = (1.0 if k in (0, 8) else 2.0) / (2 * TOK_DEV)
            return weight * fwd(block, k, part)

        levels.append(np.concatenate([forward_rows(fwd, pairs), inverse_rows(inv, pairs)]))

    def taps(block, k, part):
        if k == 0:
            return np.asarray((1.0 if part == 0 else (-1.0) ** block) / TOK_DEV)
        turn = 2.0 * math.pi / 8 * (block * k % 8)
        return np.asarray((np.cos(turn) if part == 0 else -np.sin(turn)) * 2.0 / TOK_DEV)

    tap_pairs = [(1, 2), (3, 0)]
    taps_back = forward_rows(taps, tap_pairs)
    taps_rows = inverse_rows(taps, tap_pairs)
    freq_even = np.where(line < HALF, 8 * line, 4 + 8 * (line - HALF))
    half_angle = np.stack(
        [lane_rows(1 + 8 * line, 2 + 8 * line), lane_rows(3 + 8 * line, freq_even)]
    ) * (math.pi / TOK_DEV)
    wave = np.stack([np.cos(half_angle), np.sin(half_angle)])
    return (
        mats,
        np.stack(twiddle).astype(np.float32),
        np.stack(levels).astype(np.float32),
        np.concatenate([levels[2], taps_rows, taps_back]).astype(np.float32),
        wave.astype(np.float32),
    )


def low_lanes(rows):
    return lax.broadcasted_iota(jnp.int32, (rows, LANES), 1) < HALF


def turn_half(values):
    return pltpu.roll(values, HALF, 1)


def split_pair(values):
    upper, lower = values[:HALF], values[HALF:]
    mask = low_lanes(HALF)
    return jnp.where(mask, upper, turn_half(lower)), jnp.where(mask, turn_half(upper), lower)


def join_pair(first, second):
    mask = low_lanes(HALF)
    return jnp.concatenate(
        [jnp.where(mask, first, turn_half(second)), jnp.where(mask, turn_half(first), second)], axis=0
    )


def interleave(first, second):
    mask = low_lanes(first.shape[0])
    return jnp.where(mask, first, turn_half(second)), jnp.where(mask, turn_half(first), second)


def fold(values):
    return values + turn_half(values)


def normal_parts(values):
    cumulative = 0.5 * (1.0 + lax.erf(values * 0.7071067811865476))
    density = jnp.exp(-0.5 * values * values) * 0.3989422804014327
    return cumulative, density


def column_sum(values):
    return jnp.sum(values, axis=0, keepdims=True)


def dot_nt(left, right):
    return lax.dot_general(left, right, (((1,), (1,)), ((), ())), preferred_element_type=F32)


def dot_nn(left, right):
    return jnp.dot(left, right, preferred_element_type=F32)


def store_split(ref, row, lane, values):
    high = values.astype(BF16)
    place = (pl.ds(row, values.shape[0]), pl.ds(lane, values.shape[1]))
    ref[(0,) + place] = high
    ref[(1,) + place] = (values - high.astype(F32)).astype(BF16)


def split_product(mat_ref, which, rhs_ref, lane, width):
    high = mat_ref[which, :, 0:256]
    low = mat_ref[which, :, 256:512]
    rhs_high = rhs_ref[0, :, lane : lane + width]
    return dot_nn(high, rhs_high) + dot_nn(high, rhs_ref[1, :, lane : lane + width]) + dot_nn(low, rhs_high)


CHUNK = 32


def over_chunks(body, size=CHUNK, first=0, rows=ROWS):
    def step(index, carry):
        body(pl.multiple_of(first + index * size, size))
        return carry

    lax.fori_loop(0, rows // size, step, 0)


def spread_pairs(src, coef_ref, base, twiddle_ref, twiddle_base, pairs, rhs_ref):
    def body(row):
        rows = pl.ds(row, CHUNK)
        blocks = [src(j, rows) for j in range(PAIRS)]
        for pair in range(pairs):
            parts = []
            for part in range(2):
                at = base + (pair * 2 + part) * 8
                straight = sum(blocks[j] * coef_ref[at + j : at + j + 1, :] for j in range(PAIRS))
                crossed = sum(blocks[j] * coef_ref[at + 4 + j : at + 5 + j, :] for j in range(PAIRS))
                parts.append(straight + turn_half(crossed))
            cosine = twiddle_ref[twiddle_base + 2 * pair, rows, :]
            sine = twiddle_ref[twiddle_base + 2 * pair + 1, rows, :]
            store_split(rhs_ref, row, pair * LANES, parts[0] * cosine + parts[1] * sine)
            store_split(rhs_ref, row + ROWS, pair * LANES, parts[1] * cosine - parts[0] * sine)

    over_chunks(body)


def gather_pairs(values_ref, coef_ref, base, twiddle_ref, twiddle_base, pairs, store):
    def body(row):
        rows = pl.ds(row, CHUNK)
        straight, crossed = [0.0] * PAIRS, [0.0] * PAIRS
        for pair in range(pairs):
            lanes = slice(pair * LANES, (pair + 1) * LANES)
            real, imag = values_ref[rows, lanes], values_ref[pl.ds(row + ROWS, CHUNK), lanes]
            cosine = twiddle_ref[twiddle_base + 2 * pair, rows, :]
            sine = twiddle_ref[twiddle_base + 2 * pair + 1, rows, :]
            for part, value in enumerate((real * cosine - imag * sine, imag * cosine + real * sine)):
                at = base + (pair * 2 + part) * 8
                for j in range(PAIRS):
                    straight[j] = straight[j] + value * coef_ref[at + j : at + j + 1, :]
                    crossed[j] = crossed[j] + value * coef_ref[at + 4 + j : at + 5 + j, :]
        for j in range(PAIRS):
            store(j, rows, straight[j] + turn_half(crossed[j]))

    over_chunks(body)


GROUPS = ((0, 256), (256, 256), (512, 128))


def transform_into(dst_ref, mat_ref, which, rhs_ref, groups=GROUPS):
    for lane, width in groups:
        dst_ref[:, lane : lane + width] = split_product(mat_ref, which, rhs_ref, lane, width)


def multiply_spectra(left_ref, right_ref, rhs_ref, conjugate):
    def body(row):
        top, bottom = pl.ds(row, CHUNK), pl.ds(row + ROWS, CHUNK)
        for pair in range(5):
            lanes = slice(pair * LANES, (pair + 1) * LANES)
            a_re, a_im = left_ref[top, lanes], left_ref[bottom, lanes]
            b_re, b_im = right_ref[top, lanes], right_ref[bottom, lanes]
            if conjugate:
                out_re, out_im = a_re * b_re + a_im * b_im, a_re * b_im - a_im * b_re
            else:
                out_re, out_im = a_re * b_re - a_im * b_im, a_re * b_im + a_im * b_re
            store_split(rhs_ref, row, pair * LANES, out_re)
            store_split(rhs_ref, row + ROWS, pair * LANES, out_im)

    over_chunks(body)


def pair_terms(modes_ref):
    rank_re, rank_im, in_re, in_im, out_re, out_im = (modes_ref[i] for i in range(2, 8))
    return (
        (out_re * in_re + out_im * in_im, out_re * in_im - out_im * in_re),
        (out_re * rank_re + out_im * rank_im, out_re * rank_im - out_im * rank_re),
        (rank_re * in_re + rank_im * in_im, rank_re * in_im - rank_im * in_re),
        (rank_re * rank_re + rank_im * rank_im, None),
    )


def mode_values(modes_ref):
    index = lax.broadcasted_iota(jnp.int32, modes_ref.shape[1:], 0).astype(F32)
    return -0.5 * jnp.exp(modes_ref[0]), math.pi * (index + modes_ref[1])


POINT_ROWS = 16


def resolvent(coef_ref, n, square_cos, cos_sin, scaled):
    den_re = coef_ref[8, pl.ds(n, 1), :] * square_cos - scaled
    den_im = coef_ref[9, pl.ds(n, 1), :] * cos_sin
    inverse = 1.0 / (den_re * den_re + den_im * den_im)
    return den_re * inverse, -(den_im * inverse)


def complex_multiply(a_re, a_im, b_re, b_im):
    return a_re * b_re - a_im * b_im, a_re * b_im + a_im * b_re


def conj_multiply(a_re, a_im, b_re, b_im):
    return a_re * b_re + a_im * b_im, a_re * b_im - a_im * b_re


def combine(sums, sigma, cosine, sine):
    terms = []
    for p_re, p_im, q_re, q_im in (sums[4 * q : 4 * q + 4] for q in range(4)):
        swing = sigma * sine
        terms.append((-swing * p_im - cosine * q_re, swing * p_re - cosine * q_im))
    twice = 2.0 * cosine
    loop_re, loop_im = 1.0 + twice * terms[3][0], twice * terms[3][1]
    scale = 1.0 / (loop_re * loop_re + loop_im * loop_im)
    inv = (loop_re * scale, -(loop_im * scale))
    ratio = complex_multiply(twice * terms[2][0], twice * terms[2][1], *inv)
    return terms, inv, ratio


QUARTER = 32


def cauchy_coefficients(modes_ref, sigma, coef_ref):
    lam_re, lam_im = mode_values(modes_ref)
    for q, (real, imag) in enumerate(pair_terms(modes_ref)):
        coef_ref[q] = real
        coef_ref[4 + q] = real * lam_re if imag is None else real * lam_re + imag * lam_im
    coef_ref[8] = lam_re * lam_re + lam_im * lam_im
    coef_ref[9] = -2.0 * sigma * lam_re


def wave_rows(wave_ref, pair, base, row):
    rows = pl.ds(pl.multiple_of(base + row, POINT_ROWS), POINT_ROWS)
    return wave_ref[0, pair, rows, :], wave_ref[1, pair, rows, :]


def cauchy_forward(index, sigma, coef_ref, wave_ref, base, sums_ref, spec_ref):
    sigma_sq = sigma * sigma
    pair, row = index // 2, index % 2 * POINT_ROWS
    rows = slice(row, row + POINT_ROWS)
    lanes = slice(pair * LANES, (pair + 1) * LANES)
    cosine, sine = wave_rows(wave_ref, pair, base, row)
    square_cos, cos_sin, scaled = cosine * cosine, cosine * sine, sigma_sq * (sine * sine)

    def add_mode(n, sums):
        sums = list(sums)
        for k in range(4):
            at = n * 4 + k
            inv_re, inv_im = resolvent(coef_ref, at, square_cos, cos_sin, scaled)
            for q in range(4):
                plain = coef_ref[q, pl.ds(at, 1), :]
                turned = coef_ref[4 + q, pl.ds(at, 1), :]
                sums[4 * q] = sums[4 * q] + plain * inv_re
                sums[4 * q + 1] = sums[4 * q + 1] + plain * inv_im
                sums[4 * q + 2] = sums[4 * q + 2] + turned * inv_re
                sums[4 * q + 3] = sums[4 * q + 3] + turned * inv_im
        return tuple(sums)

    zero = jnp.zeros((POINT_ROWS, LANES), F32)
    sums = lax.fori_loop(0, 8, add_mode, (zero,) * 16)
    for i in range(16):
        sums_ref[pair, i, rows, :] = sums[i]
    terms, _, ratio = combine(sums, sigma, cosine, sine)
    cut_re, cut_im = complex_multiply(*terms[1], *ratio)
    part_re, part_im = terms[0][0] - cut_re, terms[0][1] - cut_im
    spec_re, spec_im = complex_multiply(2.0 * cosine, 2.0 * sine, part_re, part_im)
    spec_ref[rows, lanes] = spec_re
    spec_ref[row + QUARTER : row + QUARTER + POINT_ROWS, lanes] = spec_im


PLACES = [(pair, row) for pair in range(2) for row in range(0, QUARTER, POINT_ROWS)]


def point_grads(sigma, wave_ref, base, sums_ref, spec_ref, grad_ref):
    zero = jnp.zeros((POINT_ROWS, LANES), F32)
    sigma_sum = zero
    for pair, row in PLACES:
        rows = slice(row, row + POINT_ROWS)
        lanes = slice(pair * LANES, (pair + 1) * LANES)
        cosine, sine = wave_rows(wave_ref, pair, base, row)
        sums = [sums_ref[pair, i, rows, :] for i in range(16)]
        terms, inv, ratio = combine(sums, sigma, cosine, sine)
        spec_re, spec_im = spec_ref[rows, lanes], spec_ref[row + QUARTER : row + QUARTER + POINT_ROWS, lanes]
        part = conj_multiply(2.0 * cosine, 2.0 * sine, spec_re, spec_im)
        left = conj_multiply(*ratio, *part)
        ratio_grad = conj_multiply(*terms[1], *part)
        back = conj_multiply(*inv, -ratio_grad[0], -ratio_grad[1])
        twice = 2.0 * cosine
        loop = conj_multiply(*ratio, *back)
        grads = (
            part,
            (-left[0], -left[1]),
            (twice * back[0], twice * back[1]),
            (-twice * loop[0], -twice * loop[1]),
        )
        swing = sigma * sine
        for q, (g_re, g_im) in enumerate(grads):
            grad_ref[pair, 4 * q, rows, :] = swing * g_im
            grad_ref[pair, 4 * q + 1, rows, :] = -swing * g_re
            grad_ref[pair, 4 * q + 2, rows, :] = -cosine * g_re
            grad_ref[pair, 4 * q + 3, rows, :] = -cosine * g_im
            sigma_sum = sigma_sum + sine * (g_im * sums[4 * q] - g_re * sums[4 * q + 1])
    return sigma_sum


def mode_sums(part, square_sum, sigma, coef_ref, wave_ref, base, grad_ref, back_ref):
    sigma_sq = sigma * sigma

    def mode(n, square_sum):
        plain = [coef_ref[q, pl.ds(n, 1), :] for q in range(4)]
        turned = [coef_ref[4 + q, pl.ds(n, 1), :] for q in range(4)]
        sums = [0.0] * 10
        for pair, row in PLACES:
            rows = slice(row, row + POINT_ROWS)
            cosine, sine = wave_rows(wave_ref, pair, base, row)
            square_cos, cos_sin, square_sin = cosine * cosine, cosine * sine, sine * sine
            inv_re, inv_im = resolvent(coef_ref, n, square_cos, cos_sin, sigma_sq * square_sin)
            grad_re, grad_im = 0.0, 0.0
            for q in range(4):
                p_re, p_im = grad_ref[pair, 4 * q, rows, :], grad_ref[pair, 4 * q + 1, rows, :]
                q_re, q_im = grad_ref[pair, 4 * q + 2, rows, :], grad_ref[pair, 4 * q + 3, rows, :]
                grad_re = grad_re + (plain[q] * p_re + turned[q] * q_re)
                grad_im = grad_im + (plain[q] * p_im + turned[q] * q_im)
                sums[q] = sums[q] + (p_re * inv_re + p_im * inv_im)
                sums[4 + q] = sums[4 + q] + (q_re * inv_re + q_im * inv_im)
            square_re = inv_re * inv_re - inv_im * inv_im
            square_im = 2.0 * inv_re * inv_im
            den_re, den_im = conj_multiply(square_re, square_im, grad_re, grad_im)
            sums[8] = sums[8] - den_re * square_cos
            sums[9] = sums[9] - den_im * cos_sin
            square_sum = square_sum + den_re * square_sin
        for i in range(10):
            back_ref[i, pl.ds(n, 1), :] = column_sum(sums[i])
        return square_sum

    return lax.fori_loop(part * 8, part * 8 + 8, mode, square_sum)


def mode_gradients(modes_ref, sigma, nyquist_grad, step, sigma_sum, square_sum, back_ref):
    plain_grad = [fold(back_ref[q]) for q in range(4)]
    turned_grad = [fold(back_ref[4 + q]) for q in range(4)]
    abs_grad, skew_grad = fold(back_ref[8]), fold(back_ref[9])
    lam_re, lam_im = mode_values(modes_ref)
    plain_grad[0] = plain_grad[0] + step * nyquist_grad
    rank_re, rank_im, in_re, in_im, out_re, out_im = (modes_ref[i] for i in range(2, 8))
    lam_re_grad = 2.0 * lam_re * abs_grad - 2.0 * sigma * skew_grad
    lam_im_grad = 2.0 * lam_im * abs_grad
    real_grad, imag_grad = [], []
    terms = pair_terms(modes_ref)
    for q, (real, imag) in enumerate(terms):
        lam_re_grad = lam_re_grad + turned_grad[q] * real
        if imag is not None:
            lam_im_grad = lam_im_grad + turned_grad[q] * imag
        real_grad.append(plain_grad[q] + turned_grad[q] * lam_re)
        imag_grad.append(turned_grad[q] * lam_im)
    r0, r1, r2, r3 = real_grad
    i0, i1, i2, _ = imag_grad
    grads = (
        lam_re_grad * lam_re,
        math.pi * lam_im_grad,
        r1 * out_re - i1 * out_im + r2 * in_re + i2 * in_im + 2.0 * r3 * rank_re,
        r1 * out_im + i1 * out_re + r2 * in_im - i2 * in_re + 2.0 * r3 * rank_im,
        r0 * out_re - i0 * out_im + r2 * rank_re - i2 * rank_im,
        r0 * out_im + i0 * out_re + r2 * rank_im + i2 * rank_re,
        r0 * in_re + i0 * in_im + r1 * rank_re + i1 * rank_im,
        r0 * in_im - i0 * in_re + r1 * rank_im - i1 * rank_re,
    )
    sigma_grad = (
        fold(column_sum(sigma_sum) + 2.0 * sigma * column_sum(square_sum))
        - 2.0 * column_sum(skew_grad * lam_re)
    )
    nyquist = step * column_sum(terms[0][0])
    return grads, nyquist * nyquist_grad - sigma * sigma_grad


def ring_place(chan):
    z, y = lax.div(chan, 2), lax.rem(chan, 2)
    return z + y * (7 - 2 * z)


def ring_chan(place):
    back = lax.div(place, 4)
    z = place * (1 - back) + (7 - place) * back
    return 2 * z + back


TURNS = (1, -1)


def block_kernel(
    bucket_ref, items_ref, tokens_ref, cotangent_ref, gain1_ref, bias1_ref, raw_modes_ref, log_dt_ref, skip_ref,
    wa_ref, ba_ref, wb_ref, bb_ref, gain2_ref, bias2_ref, up_ref, bup_ref, down_ref, bdown_ref,
    levels_ref, coefc_ref, mat_ref, tw_ref, wave_ref,
    out_ref, dtok_ref, gw_ref, gm_ref, gv_ref,
    tok_ref, aux_ref, coefl_ref, modes_ref,
    wab_ref, wh_ref, gab_w_ref, gh_ref,
    stage_ref, sib_ab_ref, ring_ab_ref, ring_h_ref, part_ab_ref, cross_ref, keep_ref, swap_ref, gate_total_ref,
    in_send, in_recv, head_send, head_recv, acts_send, acts_recv, back_send, back_recv, late_send, late_recv,
    sum_send, sum_recv, tail_send, tail_recv, dp_send, dp_low, dp_recv, spec_send, spec_recv, sgrad_send, sgrad_recv,
    hat_ref, norm_ref, slope_ref, conv_ref, rhs_ref, freq_ref, sig_ref, ans_ref, taps_ref,
    mcoef_ref, sums_ref, pgrad_ref, mback_ref, sgrad_ref, taps_freq_ref,
    gate_ref, swish_ref, res_ref, hat2_ref, acts_ref, norm2_ref, gradf_ref, branch_ref, back2_ref, half_send, half_recv,
    gab_ref, hid_ref, gpre_ref, acts_t_ref, norm2_t_ref, gradf_t_ref,
    gring_ss, gring_rs, gsib_ss, gsib_rs, gx_ss, gx_rs, gdx_ss, gdx_rs, gswap_ss, gswap_rs, core_ss, core_rs,
    rring_ss, rring_rs, rsib_ss, rsib_rs, rx_ss, rx_rs, rdx_ss, rdx_rs, rswap_ss, rswap_rs,
    a2a_ss, a2a_rs, dp_ss, dp_rs, spec_ss, spec_rs,
):
    dp, chan = lax.axis_index("dp"), lax.axis_index("chan")
    core = lax.rem(dp, 2)
    sibling = dp + 1 - 2 * core
    place = ring_place(chan)
    spots = [lax.rem(place + offset, 8) if offset else place for offset in range(8)]
    around = [ring_chan(spot) if offset else chan for offset, spot in enumerate(spots)]
    groups = [lax.rem(spot, 4) for spot in spots]
    group_lanes = [pl.multiple_of(lax.div(spot, 4) * LANES, LANES) for spot in spots]
    nexts = [around[1], around[7]]
    chan_peers = [chan] + [lax.rem(chan + r, N_CHAN) for r in range(1, N_CHAN)]
    dp_peers = [dp] + [lax.rem(dp + r, 4) for r in range(1, 4)]
    across = dp_peers[2]

    def chan_at(offset):
        return around[offset % 8]

    barrier = pltpu.get_barrier_semaphore()
    for r in range(1, N_CHAN):
        pl.semaphore_signal(barrier, inc=1, device_id={"chan": chan_peers[r]}, device_id_type=MESH)
    for r in range(1, 4):
        pl.semaphore_signal(barrier, inc=1, device_id={"dp": dp_peers[r]}, device_id_type=MESH)

    pending = []

    def remote(src, dst, send_sem, recv_sem, **device):
        return pltpu.make_async_remote_copy(
            src_ref=src, dst_ref=dst, send_sem=send_sem, recv_sem=recv_sem, device_id=device, device_id_type=MESH
        )

    def send(*args, **device):
        copy = remote(*args, **device)
        copy.start()
        pending.append(copy)

    def exchange(which, source, recv_ref):
        def copy(r):
            peer = chan_peers[r]
            return remote(
                source(peer), recv_ref.at[chan], a2a_ss.at[which, r - 1], a2a_rs.at[which, r - 1], chan=peer
            )

        def start():
            for r in range(1, N_CHAN):
                copy(r).start()

        def wait():
            for r in range(1, N_CHAN):
                copy(r).wait_recv()

        def finish():
            for r in range(1, N_CHAN):
                copy(r).wait_send()

        return start, wait, finish

    def rows_at(number, count):
        return pl.ds(pl.multiple_of(number, ROWS), count)

    def launch(copy):
        copy.start()
        pending.append(copy)

    own_row = dp * ROWS
    pair_row = (dp - core) * ROWS
    away_row = 2 * ROWS - pair_row
    gate_row, gate_away = (core * 2 + lax.div(dp, 2)) * ROWS, (core * 2 + 1 - lax.div(dp, 2)) * ROWS
    gate_pair, gate_other = core * 2 * ROWS, (1 - core) * 2 * ROWS
    half_lanes = pl.multiple_of(core * LANES, LANES)
    other_lanes = pl.multiple_of((1 - core) * LANES, LANES)

    def gate_view(ref):
        return lambda offset, row, count: ref.at[around[offset % 8], rows_at(row, count), :]

    def hidden_view(ref):
        return lambda offset, row, count: ref.at[
            :, groups[offset % 8], rows_at(row, count), pl.ds(group_lanes[offset % 8], LANES)
        ]

    class Ring:
        def __init__(self, which, view, base, count, hook=None):
            self.which, self.view, self.base, self.count, self.hook = which, view, base, count, hook

        def piece(self, turn, step, base):
            half = self.count // 2
            if step == 4:
                return self.view(4, base + turn * half, half)
            return self.view(-TURNS[turn] * step, base, self.count)

        def copy(self, turn, step, ref):
            slot = turn * 4 + step - 1
            return remote(ref, ref, gring_ss.at[self.which, slot], gring_rs.at[self.which, slot], chan=nexts[turn])

        def send(self, turn, step):
            half = self.count // 2
            if step == 4:
                ref = self.view(-TURNS[turn] * 3, self.base + turn * half, half)
            else:
                ref = self.piece(turn, step - 1, self.base)
            launch(self.copy(turn, step, ref))

        def start(self):
            for turn in range(2):
                self.send(turn, 1)

        def step(self, step):
            for turn in range(2):
                self.copy(turn, step, self.piece(turn, step, self.base)).wait_recv()
                if step < 4:
                    self.send(turn, step + 1)
                if self.hook:
                    self.hook(turn, step)

    def slot_of(turn, step):
        return turn * 4 + step - 1 if step else 8

    def gate_sib(turn, step, base):
        ref, slot = gate_ring.piece(turn, step, base), slot_of(turn, step)
        return remote(ref, ref, gsib_ss.at[slot], gsib_rs.at[slot], dp=sibling)

    def hidden_cross(turn, step, base):
        ref, slot = hidden_ring.piece(turn, step, base), slot_of(turn, step)
        return remote(ref, ref, gdx_ss.at[slot], gdx_rs.at[slot], dp=across)

    gate_ring = Ring(0, gate_view(wab_ref), gate_pair, 256, lambda turn, step: launch(gate_sib(turn, step, gate_pair)))
    hidden_ring = Ring(
        1, hidden_view(wh_ref), pair_row, 256, lambda turn, step: launch(hidden_cross(turn, step, pair_row))
    )

    def gate_over(row):
        ref = gate_ring.view(0, row, ROWS)
        return remote(ref, ref, gx_ss, gx_rs, dp=across)

    def swap_copy(row):
        return remote(stage_ref, hidden_ring.view(0, row, ROWS), gswap_ss, gswap_rs, dp=sibling)

    def gather_prepare():
        gates = jnp.concatenate([wa_ref[...], wb_ref[...]], axis=0).T.astype(BF16)
        wab_ref[chan, rows_at(gate_row, ROWS), :] = gates
        for which, values in enumerate((up_ref[...], down_ref[...].T)):
            first, second = values[:, :LANES], values[:, LANES:]
            kept = jnp.where(core == 0, first, second)
            wh_ref[which, groups[0], rows_at(own_row, ROWS), pl.ds(group_lanes[0], LANES)] = kept.astype(BF16)
            stage_ref[which] = jnp.where(core == 0, second, first).astype(BF16)

    def gather_start():
        launch(swap_copy(own_row))
        launch(gate_over(gate_row))

    def hidden_first():
        swap_copy(sibling * ROWS).wait_recv()
        hidden_ring.start()
        launch(hidden_cross(0, 0, pair_row))

    def gate_first():
        gate_over(gate_away).wait_recv()
        gate_ring.start()
        launch(gate_sib(0, 0, gate_pair))

    ring_steps = [(0, 0)] + [(turn, step) for step in range(1, 5) for turn in range(2)]

    def gates_arrived():
        for turn, step in ring_steps:
            gate_sib(turn, step, gate_other).wait_recv()

    def hidden_arrived(*steps):
        for turn, step in ring_steps:
            if step in steps:
                hidden_cross(turn, step, away_row).wait_recv()

    def beside(ref, j):
        start = 2 * j * ROWS
        return jnp.concatenate(
            [ref[:, start : start + ROWS].astype(F32), ref[:, start + ROWS : start + 2 * ROWS].astype(F32)], axis=0
        ).T

    for j in range(PAIRS):
        packed = beside(tokens_ref, j)
        tok_ref[j * ROWS : (j + 1) * ROWS, :] = packed.astype(BF16)
        for first, values in ((0, packed), (HALF, beside(cotangent_ref, j))):
            low, high = split_pair(values)
            in_send[2 * j, first : first + HALF, :] = low.astype(BF16)
            in_send[2 * j + 1, first : first + HALF, :] = high.astype(BF16)
    in_recv[chan] = in_send[chan]

    lane_id = lax.broadcasted_iota(jnp.int32, (8, LANES), 1)
    row_id = lax.broadcasted_iota(jnp.int32, (8, LANES), 0)
    halves = jnp.where((lane_id >= HALF) == (row_id == 1), 1.0, 0.0) * jnp.where(row_id < 2, 1.0, 0.0)
    halves = halves.astype(BF16)

    def token_sums(parts):
        total = 0.0
        for part in parts:
            total = total + dot_nt(halves, part)
        return [total[h : h + 1, j * ROWS : (j + 1) * ROWS] for h in range(2) for j in range(PAIRS)]

    def split(values):
        high = values.astype(BF16)
        return high, (values - high.astype(F32)).astype(BF16)

    tokens = tok_ref[...]
    wide_tokens = tokens.astype(F32)
    for i, sums in enumerate(token_sums([tokens]) + token_sums(split(wide_tokens * wide_tokens))):
        head_send[i : i + 1, :] = sums

    def row(*refs):
        return jnp.concatenate([ref[...].reshape(1, HALF) for ref in refs], axis=1)

    bup = bup_ref[...].reshape(1, 2 * LANES)
    head_send[16:17, :] = row(ba_ref, bb_ref)
    head_send[17:18, :] = row(gain2_ref, bias2_ref)
    head_send[18:19, :] = row(bdown_ref, bdown_ref)
    head_send[19:20, :] = bup[:, :LANES]
    head_send[20:21, :] = bup[:, LANES:]
    head_send[21:24, :] = jnp.zeros((3, LANES), F32)
    head_recv[chan] = head_send[...]
    head = exchange(0, lambda peer: head_send, head_recv)
    inputs = exchange(1, lambda peer: in_send.at[peer], in_recv)
    gather_prepare()
    pl.semaphore_wait(barrier, N_CHAN - 1 + 3)
    head[0]()
    gather_start()
    hidden_first()

    level, filled = bucket_ref[0], items_ref[0]
    coefl_ref[...] = levels_ref[level]
    item_blocks = jnp.where(level == 0, 2, jnp.where(level == 1, 4, 8))
    gate_first()
    block_id = 2 * (row_id % PAIRS) + jnp.where(lane_id >= HALF, 1, 0)
    bound = jnp.where(row_id < PAIRS, filled * item_blocks, item_blocks)
    aux_ref[...] = jnp.where(block_id < bound, 1.0, 0.0)
    for i in range(8):
        modes_ref[i] = jnp.concatenate([raw_modes_ref[i], raw_modes_ref[i]], axis=1)
    log_dt = row(log_dt_ref, log_dt_ref)
    sigma, step_size = 2.0 * jnp.exp(-log_dt), jnp.exp(log_dt)

    base = pl.multiple_of(dp * QUARTER, QUARTER)

    def spec_copy(which, r):
        peer = dp_peers[r]
        src, dst = ((spec_send, spec_recv), (sgrad_send.at[peer], sgrad_recv))[which]
        return remote(src, dst.at[dp], spec_ss.at[which, r - 1], spec_rs.at[which, r - 1], dp=peer)

    cauchy_coefficients(modes_ref, sigma, mcoef_ref)
    cauchy_forward(0, sigma, mcoef_ref, wave_ref, base, sums_ref, spec_send)
    gate_ring.step(1)
    inputs[0]()
    cauchy_forward(1, sigma, mcoef_ref, wave_ref, base, sums_ref, spec_send)
    cauchy_forward(2, sigma, mcoef_ref, wave_ref, base, sums_ref, spec_send)
    cauchy_forward(3, sigma, mcoef_ref, wave_ref, base, sums_ref, spec_send)
    spec_recv[dp] = spec_send[...]
    for r in range(1, 4):
        spec_copy(0, r).start()

    head[1]()
    sums = head_recv[0, 0:16, :]
    for c in range(1, N_CHAN):
        sums = sums + head_recv[c, 0:16, :]
    hidden_ring.step(1)
    mean = sums[0:8] * (1.0 / MODEL_WIDTH)
    rstd = lax.rsqrt(sums[8:16] * (1.0 / MODEL_WIDTH) - mean * mean + EPSILON)

    def columns(rows):
        tall = rows.T
        return [jnp.where(low_lanes(ROWS), tall[:, j : j + 1], tall[:, 4 + j : 5 + j]) for j in range(PAIRS)]

    gain1, bias1, skip = row(gain1_ref, gain1_ref), row(bias1_ref, bias1_ref), row(skip_ref, skip_ref)
    mean_cols, rstd_cols = columns(mean), columns(rstd)
    for j in range(PAIRS):
        hat = (tok_ref[j * ROWS : (j + 1) * ROWS, :].astype(F32) - mean_cols[j]) * rstd_cols[j]
        hat_ref[j] = hat
        norm_ref[j] = hat * gain1 + bias1

    spread_pairs(lambda j, rows: norm_ref[j, rows, :], coefl_ref, 0, tw_ref, 0, 5, rhs_ref)
    transform_into(sig_ref, mat_ref, 0, rhs_ref)

    for r in range(1, 4):
        spec_copy(0, r).wait_recv()
    for source in range(4):
        store_split(rhs_ref, source * QUARTER, 0, spec_recv[source, :QUARTER, :])
        store_split(rhs_ref, ROWS + source * QUARTER, 0, spec_recv[source, QUARTER:, :])
    gate_ring.step(2)
    freq_ref[:, 0:256] = split_product(mat_ref, 1, rhs_ref, 0, 256)
    even = split_product(mat_ref, 2, rhs_ref, LANES, LANES)
    freq_ref[:, LANES:256] = jnp.where(low_lanes(256), freq_ref[:, LANES:256], even)
    sign = 1.0 - 2.0 * (lax.broadcasted_iota(jnp.int32, (CHUNK, LANES), 0) % 2).astype(F32)
    nyquist = step_size * column_sum(mcoef_ref[0]) * (1.0 / TOK_DEV)

    def store_taps(j, rows, values):
        taps_ref[j, rows, :] = (values + sign * nyquist) * aux_ref[4 + j : 5 + j, :]

    gather_pairs(freq_ref, coefc_ref, 160, tw_ref, 10, 2, store_taps)
    hidden_ring.step(2)
    spread_pairs(lambda j, rows: taps_ref[j, rows, :], coefc_ref, 0, tw_ref, 0, 5, rhs_ref)
    transform_into(ans_ref, mat_ref, 0, rhs_ref)
    gate_ring.step(3)
    multiply_spectra(sig_ref, ans_ref, rhs_ref, False)
    transform_into(freq_ref, mat_ref, 1, rhs_ref)
    hidden_ring.step(3)

    def store_conv(j, rows, values):
        conv_ref[j, rows, :] = values
    gather_pairs(freq_ref, coefl_ref, 80, tw_ref, 0, 5, store_conv)
    for j in range(PAIRS):
        mixed = conv_ref[j] * aux_ref[j : j + 1, :] + skip * norm_ref[j]
        cumulative, density = normal_parts(mixed)
        slope_ref[j] = cumulative + mixed * density
        low, high = split_pair(mixed * cumulative)
        acts_send[2 * j] = low.astype(BF16)
        acts_send[2 * j + 1] = high.astype(BF16)
    acts_recv[chan] = acts_send[chan]
    acts = exchange(2, lambda peer: acts_send.at[peer], acts_recv)
    acts[0]()

    def joined(ref, pair, first):
        return join_pair(
            ref[2 * pair, first : first + HALF, :].astype(F32), ref[2 * pair + 1, first : first + HALF, :].astype(F32)
        )

    def lanes_of(pair):
        return slice(pair * LANES, (pair + 1) * LANES)

    def gate_lanes(pair):
        return lanes_of(pair % 2 * 2 + pair // 2)

    def core_copy(which, src, dst):
        return remote(src, dst, core_ss.at[which], core_rs.at[which], dp=sibling)

    def other_core(which, ref):
        return core_copy(which, ref.at[core], ref.at[core])

    def vector(row, first, second):
        return interleave(head_recv[first, 16 + row : 17 + row, :], head_recv[second, 16 + row : 17 + row, :])

    def both_cores(ref):
        return ref[...].reshape(2 * ROWS, MODEL_WIDTH)

    def hidden_group(offset):
        group = groups[offset]
        low, high = 2 * group, 7 - 2 * group
        bias = jnp.concatenate(
            [jnp.where(core == 0, head_recv[c, 19:20, :], head_recv[c, 20:21, :]) for c in (low, high)], axis=1
        )
        pre = dot_nn(both_cores(norm2_ref), wh_ref[0, group]) + bias
        cumulative, density = normal_parts(pre)
        hidden = (pre * cumulative).astype(BF16)
        hid_ref[group] = hidden
        grad = dot_nn(both_cores(gradf_ref), wh_ref[1, group]) * (cumulative + pre * density)
        grad = grad.astype(BF16)
        gpre_ref[group] = grad
        sums = column_sum(grad.astype(F32))
        tail_send[low, pl.ds(3 + core, 1), :] = sums[:, 0:LANES]
        tail_send[high, pl.ds(3 + core, 1), :] = sums[:, LANES : 2 * LANES]
        branch_ref[...] += dot_nt(hidden, wh_ref[1, group]).reshape(2, ROWS, MODEL_WIDTH)
        back2_ref[...] += dot_nt(grad, wh_ref[0, group]).reshape(2, ROWS, MODEL_WIDTH)

    def offset_of(turn, step):
        return TURNS[turn] * (5 - step)

    def far(offset):
        return 4 if offset == -4 else offset

    class RingBack:
        def __init__(self, which, view, base, count, ring_ref, extra):
            self.which, self.view, self.base, self.count = which, view, base, count
            self.ring_ref, self.extra = ring_ref, extra

        def copy(self, turn, step):
            slot = turn * 4 + step - 1
            half = self.count // 2
            if step == 1:
                dst = self.ring_ref.at[slot]
                lead = (slice(None),) * (len(dst.shape) - 2)
                src, dst = self.view(4, self.base + turn * half, half), dst.at[lead + (pl.ds(0, half), slice(None))]
            else:
                src, dst = self.view(offset_of(turn, step), self.base, self.count), self.ring_ref.at[slot]
            return remote(src, dst, rring_ss.at[self.which, slot], rring_rs.at[self.which, slot], chan=nexts[turn])

        def whole(self, offset):
            return self.view(offset, self.base, self.count)[...].astype(F32) + self.extra(offset)

        def step(self, step):
            half = self.count // 2
            if step == 1:
                self.view(4, self.base, self.count)[...] = self.whole(4).astype(BF16)
                for turn in range(2):
                    launch(self.copy(turn, 1))
                return
            for turn in range(2):
                offset, slot = offset_of(turn, step), turn * 4 + step - 2
                total = self.whole(offset)
                self.copy(turn, step - 1).wait_recv()
                if step == 2:
                    parts = [total[..., :half, :], total[..., half:, :]]
                    parts[turn] = parts[turn] + self.ring_ref[slot][..., :half, :].astype(F32)
                    total = jnp.concatenate(parts, axis=-2)
                else:
                    total = total + self.ring_ref[slot].astype(F32)
                self.view(offset, self.base, self.count)[...] = total.astype(BF16)
                launch(self.copy(turn, step))

        def total(self):
            total = self.whole(0)
            for turn in range(2):
                self.copy(turn, 4).wait_recv()
                total = total + self.ring_ref[turn * 4 + 3].astype(F32)
            return total

    def gate_share(offset):
        slot = far(offset) + 3
        src = gate_view(gab_w_ref)(offset, gate_other, 256)
        return remote(src, sib_ab_ref.at[slot], rsib_ss.at[slot], rsib_rs.at[slot], dp=sibling)

    def gate_extra(offset):
        gate_share(offset).wait_recv()
        return sib_ab_ref[far(offset) + 3].astype(F32)

    def cross_copy(offset):
        slot = far(offset) + 3
        src = hidden_view(gh_ref)(offset, away_row, 256)
        return remote(src, cross_ref.at[slot], rdx_ss.at[slot], rdx_rs.at[slot], dp=across)

    def hidden_extra(offset):
        cross_copy(offset).wait_recv()
        return cross_ref[far(offset) + 3].astype(F32)

    gate_g = RingBack(0, gate_view(gab_w_ref), gate_pair, 256, ring_ab_ref, gate_extra)

    hidden_g = RingBack(1, hidden_view(gh_ref), pair_row, 256, ring_h_ref, hidden_extra)

    def hidden_grads(offset):
        group = groups[offset]
        gh_ref[1, group] = dot_nn(gradf_t_ref[...], hid_ref[group]).astype(BF16)
        gh_ref[0, group] = dot_nn(norm2_t_ref[...], gpre_ref[group]).astype(BF16)
        launch(cross_copy(offset - 4 if offset else 4))
        launch(cross_copy(offset))

    def part_copy():
        return remote(part_ab_ref.at[0], part_ab_ref.at[1], rx_ss, rx_rs, dp=across)

    def last_swap():
        return remote(keep_ref.at[:, rows_at((1 - core) * ROWS, ROWS), :], swap_ref, rswap_ss, rswap_rs, dp=sibling)

    def gate_last():
        gate_total_ref[...] = gate_g.total()
        part_ab_ref[0] = gate_total_ref[rows_at((1 - lax.div(dp, 2)) * ROWS, ROWS), :].astype(BF16)
        launch(part_copy())

    def gate_finish():
        part_copy().wait_recv()
        gw_ref[:, 0:128] = gate_total_ref[rows_at(lax.div(dp, 2) * ROWS, ROWS), :] + part_ab_ref[1].astype(F32)

    def hidden_last():
        keep_ref[...] = hidden_g.total()
        launch(last_swap())
        for which in range(2):
            gw_ref[:, pl.ds(pl.multiple_of(128 + 256 * which + half_lanes, LANES), LANES)] = keep_ref[
                which, rows_at(core * ROWS, ROWS), :
            ]

    def hidden_finish():
        last_swap().wait_recv()
        for which in range(2):
            gw_ref[:, pl.ds(pl.multiple_of(128 + 256 * which + other_lanes, LANES), LANES)] = swap_ref[which]

    late = exchange(4, lambda peer: late_send.at[peer], late_recv)

    tail = exchange(5, lambda peer: tail_send.at[peer], tail_recv)

    def gate_grads(*offsets):
        for offset in offsets:
            c = chan_at(offset)
            gab_w_ref[c] = dot_nn(acts_t_ref[...], gab_ref[c]).astype(BF16)
            launch(gate_share(offset))

    def late_messages():
        core_copy(3, half_send.at[1], half_recv.at[1]).wait_recv()
        for p in range(PAIRS):
            out = res_ref[p] + (branch_ref[core, :, lanes_of(p)] + half_recv[1, :, lanes_of(p)].astype(F32)) + interleave(head_recv[2 * p, 18:19, :], head_recv[2 * p + 1, 18:19, :])[0]
            low, high = split_pair(out)
            late_send[2 * p, :HALF, :] = low.astype(BF16)
            late_send[2 * p + 1, :HALF, :] = high.astype(BF16)
        late_recv[chan] = late_send[chan]
        late[0]()

    back = exchange(3, lambda peer: back_send.at[peer], back_recv)

    inputs[1]()
    for p in range(PAIRS):
        gradf_ref[core, :, lanes_of(p)] = joined(in_recv, p, HALF).astype(BF16)
    gate_ring.step(4)
    gates_arrived()
    launch(other_core(0, gradf_ref))
    acts[1]()
    for p in range(PAIRS):
        acts_ref[:, gate_lanes(p)] = joined(acts_recv, p, 0).astype(BF16)

    total = 0.0
    for p in range(PAIRS):
        first = dot_nn(acts_ref[...], wab_ref[2 * p]) + head_recv[2 * p, 16:17, :]
        second = dot_nn(acts_ref[...], wab_ref[2 * p + 1]) + head_recv[2 * p + 1, 16:17, :]
        gate, raw = interleave(first, second)
        swish = lax.logistic(raw)
        gate_ref[p], swish_ref[p] = gate, swish
        resid = joined(in_recv, p, 0) + gate * swish
        res_ref[p] = resid
        total = total + resid
    mean2 = jnp.sum(total, axis=1, keepdims=True) * (1.0 / MODEL_WIDTH)
    total = 0.0
    for p in range(PAIRS):
        centred = res_ref[p] - mean2
        total = total + centred * centred
    rstd2 = lax.rsqrt(jnp.sum(total, axis=1, keepdims=True) * (1.0 / MODEL_WIDTH) + EPSILON)
    gain2 = []
    for p in range(PAIRS):
        gain, bias = vector(1, 2 * p, 2 * p + 1)
        gain2.append(gain)
        hat = (res_ref[p] - mean2) * rstd2
        hat2_ref[p] = hat
        norm2_ref[core, :, lanes_of(p)] = (hat * gain + bias).astype(BF16)
    launch(other_core(1, norm2_ref))
    hidden_ring.step(4)
    acts_t_ref[...] = acts_ref[...].astype(F32).T.astype(BF16)
    branch_ref[...] = jnp.zeros_like(branch_ref)
    back2_ref[...] = jnp.zeros_like(back2_ref)
    for c in range(N_CHAN):
        tail_send[c, 3:8, :] = jnp.zeros((5, LANES), F32)
    other_core(0, gradf_ref).wait_recv()
    gradf_t_ref[...] = both_cores(gradf_ref).astype(F32).T.astype(BF16)
    other_core(1, norm2_ref).wait_recv()

    hidden_arrived(2)
    norm2_t_ref[...] = both_cores(norm2_ref).astype(F32).T.astype(BF16)
    hidden_group(2)
    hidden_arrived(1, 3)
    hidden_group(1)
    hidden_group(3)
    hidden_arrived(0, 4)
    hidden_group(0)
    half_send[0] = back2_ref[1 - core].astype(BF16)
    launch(core_copy(2, half_send.at[0], half_recv.at[0]))
    hidden_grads(0)
    half_send[1] = branch_ref[1 - core].astype(BF16)
    launch(core_copy(3, half_send.at[1], half_recv.at[1]))
    core_copy(2, half_send.at[0], half_recv.at[0]).wait_recv()
    back2 = back2_ref[core] + half_recv[0].astype(F32)
    back2_ref[core] = back2

    mean_q, mean_qx = 0.0, 0.0
    for p in range(PAIRS):
        grad, hat = back2_ref[core, :, lanes_of(p)], hat2_ref[p]
        q = grad * gain2[p]
        mean_q = mean_q + q
        mean_qx = mean_qx + q * hat
        gain_grad, bias_grad = interleave(column_sum(grad * hat), column_sum(grad))
        tail_send[2 * p, 1:2, :] = gain_grad
        first, second = interleave(turn_half(column_sum(grad * hat)), turn_half(column_sum(grad)))
        tail_send[2 * p + 1, 1:2, :] = first
    mean_q = jnp.sum(mean_q, axis=1, keepdims=True) * (1.0 / MODEL_WIDTH)
    mean_qx = jnp.sum(mean_qx, axis=1, keepdims=True) * (1.0 / MODEL_WIDTH)
    for p in range(PAIRS):
        hat = hat2_ref[p]
        extra = rstd2 * (back2_ref[core, :, lanes_of(p)] * gain2[p] - mean_q - hat * mean_qx)
        grad_f = joined(in_recv, p, HALF)
        grad_resid = grad_f + extra
        gate, swish = gate_ref[p], swish_ref[p]
        grad_a = (grad_resid * swish).astype(BF16).astype(F32)
        grad_b = (grad_resid * gate * swish * (1.0 - swish)).astype(BF16).astype(F32)
        first, second = interleave(grad_a, grad_b)
        gab_ref[2 * p] = first.astype(BF16)
        gab_ref[2 * p + 1] = second.astype(BF16)
        tail_send[2 * p, 0:1, :] = column_sum(first)
        tail_send[2 * p + 1, 0:1, :] = column_sum(second)
        low, high = interleave(column_sum(grad_f), column_sum(grad_f))
        tail_send[2 * p, 2:3, :] = low
        tail_send[2 * p + 1, 2:3, :] = high
        low, high = split_pair(extra)
        late_send[2 * p, HALF:, :] = low.astype(BF16)
        late_send[2 * p + 1, HALF:, :] = high.astype(BF16)
    grad_acts = 0.0
    for c in range(N_CHAN):
        grad_acts = grad_acts + dot_nt(gab_ref[c], wab_ref[c])
    for p in range(PAIRS):
        low, high = split_pair(grad_acts[:, gate_lanes(p)])
        back_send[2 * p] = low.astype(BF16)
        back_send[2 * p + 1] = high.astype(BF16)
    hidden_grads(3)
    back_recv[chan] = back_send[chan]
    back[0]()
    late_messages()
    gate_grads(4, 3, -3)
    tail_recv[chan] = tail_send[chan]
    hidden_g.step(1)
    hidden_grads(1)

    back[1]()
    skip_grad = 0.0
    for j in range(PAIRS):
        grad = joined(back_recv, j, 0) * slope_ref[j]
        slope_ref[j] = grad
        conv_ref[j] = grad * aux_ref[j : j + 1, :]
        skip_grad = skip_grad + column_sum(grad * norm_ref[j])
    gate_grads(2, -2, 1, -1, 0)
    tail[0]()
    gate_g.step(1)
    spread_pairs(lambda j, rows: conv_ref[j, rows, :], coefl_ref, 0, tw_ref, 0, 5, rhs_ref)
    transform_into(freq_ref, mat_ref, 0, rhs_ref)
    gate_g.step(2)
    multiply_spectra(sig_ref, freq_ref, rhs_ref, True)
    hidden_grads(2)
    transform_into(sig_ref, mat_ref, 1, rhs_ref)
    gate_g.step(3)

    def store_kernel_grad(j, rows, values):
        taps_ref[j, rows, :] = values * aux_ref[4 + j : 5 + j, :]

    gather_pairs(sig_ref, coefc_ref, 80, tw_ref, 0, 5, store_kernel_grad)
    nyquist_grad = 0.0
    for j in range(PAIRS):
        whole_sign = 1.0 - 2.0 * (lax.broadcasted_iota(jnp.int32, (ROWS, LANES), 0) % 2).astype(F32)
        nyquist_grad = nyquist_grad + column_sum(taps_ref[j] * whole_sign)
    hidden_g.step(2)
    tail[1]()
    nyquist_grad = fold(nyquist_grad) * (1.0 / TOK_DEV)
    spread_pairs(lambda j, rows: taps_ref[j, rows, :], coefc_ref, 192, tw_ref, 10, 2, rhs_ref)
    taps_freq_ref[...] = split_product(mat_ref, 0, rhs_ref, 0, 256)
    even = split_product(mat_ref, 3, rhs_ref, LANES, LANES)
    taps_freq_ref[:, LANES:256] = jnp.where(low_lanes(256), taps_freq_ref[:, LANES:256], even)
    for source in range(4):
        rows = slice(source * QUARTER, (source + 1) * QUARTER)
        sgrad_send[source, :QUARTER, :] = taps_freq_ref[rows, :]
        sgrad_send[source, QUARTER:, :] = taps_freq_ref[ROWS + source * QUARTER : ROWS + (source + 1) * QUARTER, :]
    hidden_g.step(3)
    sgrad_recv[dp] = sgrad_send[dp]
    for r in range(1, 4):
        spec_copy(1, r).start()

    multiply_spectra(ans_ref, freq_ref, rhs_ref, True)
    transform_into(freq_ref, mat_ref, 1, rhs_ref)
    gather_pairs(freq_ref, coefl_ref, 80, tw_ref, 0, 5, store_conv)
    gain_grad, bias_grad = 0.0, 0.0
    scaled, crossed = [], []
    for j in range(PAIRS):
        grad = conv_ref[j] + skip * slope_ref[j]
        conv_ref[j] = grad
        gain_grad = gain_grad + column_sum(grad * hat_ref[j])
        bias_grad = bias_grad + column_sum(grad)
    late[1]()
    gate_g.step(4)
    conv = conv_ref[...].reshape(PAIRS * ROWS, LANES) * gain1
    for i, sums in enumerate(
        token_sums(split(conv)) + token_sums(split(conv * hat_ref[...].reshape(PAIRS * ROWS, LANES)))
    ):
        sum_send[i : i + 1, :] = sums
    hidden_g.step(4)
    sum_recv[chan] = sum_send[...]
    sums_back = exchange(6, lambda peer: sum_send, sum_recv)

    for r in range(1, 4):
        spec_copy(1, r).wait_recv()
    sgrad_ref[...] = sgrad_recv[0] + sgrad_recv[1] + sgrad_recv[2] + sgrad_recv[3]
    sums_back[0]()

    sigma_sum = point_grads(sigma, wave_ref, base, sums_ref, sgrad_ref, pgrad_ref)
    square_sum = mode_sums(0, jnp.zeros_like(sigma_sum), sigma, mcoef_ref, wave_ref, base, pgrad_ref, mback_ref)
    square_sum = mode_sums(1, square_sum, sigma, mcoef_ref, wave_ref, base, pgrad_ref, mback_ref)
    square_sum = mode_sums(2, square_sum, sigma, mcoef_ref, wave_ref, base, pgrad_ref, mback_ref)
    gate_last()
    square_sum = mode_sums(3, square_sum, sigma, mcoef_ref, wave_ref, base, pgrad_ref, mback_ref)
    mode_grads, dt_grad = mode_gradients(modes_ref, sigma, nyquist_grad, step_size, sigma_sum, square_sum, mback_ref)
    mask = low_lanes(32)
    for i in range(4):
        dp_send[i * 32 : (i + 1) * 32, :] = jnp.where(mask, mode_grads[i], mode_grads[i + 4])
    first = low_lanes(1)
    dp_send[128:129, :] = jnp.where(first, dt_grad, fold(skip_grad))
    dp_send[129:130, :] = jnp.where(first, fold(gain_grad), fold(bias_grad))
    dp_send[130:136, :] = jnp.zeros((6, LANES), F32)
    tail_sum = tail_recv[0]
    for c in range(1, N_CHAN):
        tail_sum = tail_sum + tail_recv[c]
    dp_send[136:144, :] = tail_sum
    dp_low[...] = dp_send[...].astype(BF16)

    def dp_copy(r):
        return remote(dp_low, dp_recv.at[r - 1], dp_ss.at[r - 1], dp_rs.at[r - 1], dp=dp_peers[r])

    for r in range(1, 4):
        dp_copy(r).start()
    hidden_last()

    sums_back[1]()
    sums = sum_recv[0]
    for c in range(1, N_CHAN):
        sums = sums + sum_recv[c]
    gate_finish()
    sums = sums * (1.0 / MODEL_WIDTH)
    rstd_cols, q_cols, qx_cols = columns(rstd), columns(sums[0:8]), columns(sums[8:16])
    for j in range(PAIRS):
        rows = slice(j * ROWS, (j + 1) * ROWS)
        out_ref[rows, :] = joined(late_recv, j, 0).astype(BF16)
        dtok_ref[rows, :] = joined(late_recv, j, HALF) + rstd_cols[j] * (
            conv_ref[j] * gain1 - q_cols[j] - hat_ref[j] * qx_cols[j]
        )
    for r in range(1, 4):
        dp_copy(r).wait_recv()
    hidden_finish()
    total = dp_send[...] + (dp_recv[0].astype(F32) + dp_recv[1].astype(F32) + dp_recv[2].astype(F32))
    gm_ref[...] = total[0:128]
    gv_ref[...] = total[128:144]
    for copy in pending:
        copy.wait_send()
    for group in (head, inputs, acts, back, late, tail, sums_back):
        group[2]()
    for r in range(1, 4):
        dp_copy(r).wait_send()
        spec_copy(0, r).wait_send()
        spec_copy(1, r).wait_send()

def unpack_kernel(
    out_ref, dtok_ref, gw_ref, gm_ref, gv_ref, cotangent_ref,
    output_ref, tokens_ref, gain1_ref, bias1_ref, modes_ref, dt_ref, skip_ref, wa_ref, ba_ref, wb_ref, bb_ref,
    gain2_ref, bias2_ref, up_ref, bup_ref, down_ref, bdown_ref,
):
    for j in range(PAIRS):
        out = out_ref[j * ROWS : (j + 1) * ROWS, :].astype(F32).T.astype(BF16)
        grad = dtok_ref[j * ROWS : (j + 1) * ROWS, :].T
        for h in range(2):
            lanes, rows = slice((2 * j + h) * ROWS, (2 * j + h + 1) * ROWS), slice(h * HALF, (h + 1) * HALF)
            output_ref[:, lanes] = out[rows]
            tokens_ref[:, lanes] = cotangent_ref[:, lanes] + grad[rows]
    for i in range(8):
        modes_ref[i] = gm_ref[i % 4 * 32 : i % 4 * 32 + 32, i // 4 * HALF : (i // 4 + 1) * HALF]
    gates = gw_ref[:, :LANES].T
    wa_ref[...] = gates[:HALF]
    wb_ref[...] = gates[HALF:]
    up_ref[...] = gw_ref[:, 128:384]
    down_ref[...] = gw_ref[:, 384:640].T
    for at, low, high in (
        (0, dt_ref, skip_ref), (1, gain1_ref, bias1_ref), (8, ba_ref, bb_ref), (9, gain2_ref, bias2_ref),
    ):
        low[...] = gv_ref[at, :HALF]
        high[...] = gv_ref[at, HALF:]
    bdown_ref[...] = gv_ref[10, :HALF]
    bup_ref[:LANES] = gv_ref[11, :]
    bup_ref[LANES:] = gv_ref[12, :]


def block_program():
    mats, twiddle, levels, constant, wave = mixer_tables()

    def run(tokens, cotangent, bucket, items, gain1, bias1, modes, log_dt, skip, w_a, b_a, w_b, b_b, gain2, bias2, w_up, b_up, w_down, b_down):
        vmem = pl.BlockSpec(memory_space=pltpu.VMEM)
        smem = pl.BlockSpec(memory_space=pltpu.SMEM)
        dma = pltpu.SemaphoreType.DMA

        def buf(*shape):
            return pltpu.VMEM(shape, F32)

        def low(*shape):
            return pltpu.VMEM(shape, BF16)

        def full(*shape):
            return jax.ShapeDtypeStruct(shape, F32)

        big, wide = (PAIRS, ROWS, LANES), (256, WIDE)
        packed = pl.pallas_call(
            block_kernel,
            out_shape=(
                jax.ShapeDtypeStruct((512, LANES), BF16), full(512, LANES), full(ROWS, WIDE), full(ROWS, LANES),
                full(16, LANES),
            ),
            in_specs=[smem] * 2 + [vmem] * 22,
            out_specs=(vmem,) * 5,
            scratch_shapes=[
                low(512, LANES), buf(8, LANES), buf(160, LANES), buf(8, 32, LANES),
                low(N_CHAN, 512, 128), low(2, 4, 512, 256), low(N_CHAN, 512, 128), low(2, 4, 512, 256),
                low(2, ROWS, LANES), low(N_CHAN, 256, LANES), low(8, 256, LANES), low(8, 2, 256, LANES), low(2, ROWS, LANES),
                low(8, 2, 256, LANES), buf(2, 256, LANES), buf(2, ROWS, LANES), buf(256, LANES),
                low(N_CHAN, ROWS, LANES), low(N_CHAN, ROWS, LANES), buf(24, LANES), buf(N_CHAN, 24, LANES),
                low(N_CHAN, HALF, LANES), low(N_CHAN, HALF, LANES), low(N_CHAN, HALF, LANES), low(N_CHAN, HALF, LANES),
                low(N_CHAN, ROWS, LANES), low(N_CHAN, ROWS, LANES),
                buf(16, LANES), buf(N_CHAN, 16, LANES), buf(N_CHAN, 8, LANES), buf(N_CHAN, 8, LANES),
                buf(144, LANES), low(144, LANES), low(3, 144, LANES), buf(64, 256), buf(4, 64, 256), buf(4, 64, 256), buf(4, 64, 256),
                buf(*big), buf(*big), buf(*big), buf(*big), low(2, *wide), buf(*wide), buf(*wide), buf(*wide), buf(*big),
                buf(10, 32, LANES), buf(2, 16, QUARTER, LANES), buf(2, 16, QUARTER, LANES), buf(10, 32, LANES),
                buf(64, 256), buf(256, 256),
                buf(*big), buf(*big), buf(*big), buf(*big), low(ROWS, 512), low(2, ROWS, 512), low(2, ROWS, 512),
                buf(2, ROWS, 512), buf(2, ROWS, 512), low(2, ROWS, 512), low(2, ROWS, 512),
                low(N_CHAN, ROWS, LANES), low(4, 256, 256), low(4, 256, 256), low(512, ROWS), low(512, 256), low(512, 256),
                dma((2, 8)), dma((2, 8)), dma((9,)), dma((9,)), dma, dma, dma((9,)), dma((9,)), dma, dma, dma((4,)), dma((4,)),
                dma((2, 8)), dma((2, 8)), dma((8,)), dma((8,)), dma, dma, dma((8,)), dma((8,)), dma, dma,
                dma((7, 7)), dma((7, 7)), dma((3,)), dma((3,)), dma((2, 3)), dma((2, 3)),
            ],
            compiler_params=pltpu.CompilerParams(
                collective_id=0, has_side_effects=True, vmem_limit_bytes=60 * 1024 * 1024
            ),
            name="block",
        )(
            bucket, items, tokens.T, cotangent.T, gain1, bias1, jnp.swapaxes(modes, 1, 2), log_dt, skip,
            w_a.T, b_a, w_b.T, b_b, gain2, bias2,
            w_up, b_up, w_down, b_down, levels, constant, mats, twiddle, wave,
        )
        small = full(HALF)
        results = pl.pallas_call(
            unpack_kernel,
            out_shape=(
                jax.ShapeDtypeStruct((HALF, TOK_DEV), BF16), full(HALF, TOK_DEV), small, small, full(8, 32, HALF),
                small, small, full(HALF, ROWS), small, full(HALF, ROWS), small, small, small, full(ROWS, 256),
                full(256), full(256, ROWS), small,
            ),
            in_specs=[vmem] * 6,
            out_specs=(vmem,) * 17,
            name="unpack",
        )(*packed, cotangent.T)
        turned = {0, 1, 4, 7, 9}
        return tuple(jnp.swapaxes(r, -1, -2) if i in turned else r for i, r in enumerate(results))

    return run


def solution(mesh):
    small = mesh.shape["chan"] == N_CHAN and mesh.shape["dp"] == 4
    return jax.shard_map(
        block_program() if small else shards,
        mesh=mesh,
        in_specs=(
            P("dp", "chan"),
            P("dp", "chan"),
            P("dp"),
            P("dp"),
            P("chan"),
            P("chan"),
            P(None, "chan", None),
            P("chan"),
            P("chan"),
            P("dp", "chan"),
            P("chan"),
            P("dp", "chan"),
            P("chan"),
            P("chan"),
            P("chan"),
            P("dp", "chan"),
            P("chan"),
            P("chan", "dp"),
            P("chan"),
        ),
        out_specs=(
            P("dp", "chan"),
            P("dp", "chan"),
            P("chan"),
            P("chan"),
            P(None, "chan", None),
            P("chan"),
            P("chan"),
            P("dp", "chan"),
            P("chan"),
            P("dp", "chan"),
            P("chan"),
            P("chan"),
            P("chan"),
            P("dp", "chan"),
            P("chan"),
            P("chan", "dp"),
            P("chan"),
        ),
        check_vma=False,
    )
```

```python
import math

import jax
import jax.numpy as jnp
import ml_dtypes
import numpy as np
from jax import lax
from jax.experimental import pallas as pl
from jax.experimental.pallas import tpu as pltpu
from jax.sharding import PartitionSpec as P

MODEL_WIDTH = 512
TOK_DEV = 1024


HIGHEST = lax.Precision.HIGHEST
EPSILON = 1e-05


def product(left, right):
    return jnp.dot(left, right, preferred_element_type=jnp.float32)


def product_nt(left, right):
    return lax.dot_general(
        left, right, (((1,), (1,)), ((), ())), preferred_element_type=jnp.float32
    )


def product_tn(left, right):
    return lax.dot_general(
        left, right, (((0,), (0,)), ((), ())), preferred_element_type=jnp.float32
    )


def gelu_slope(values):
    return (
        0.5 * (1.0 + lax.erf(values * 0.7071067811865476))
        + values * jnp.exp(-0.5 * values * values) * 0.3989422804014327
    )


def half_angles(length):
    angle = np.arange(length // 2 + 1, dtype=np.float64) * (math.pi / length)
    cosine, sine = np.cos(angle), np.sin(angle)
    cosine[-1] = 0.0
    return cosine.astype(np.float32), sine.astype(np.float32)


def inverse_tables(length):
    freq = np.arange(length // 2 + 1)
    turn = (freq[:, None] * np.arange(length)[None, :]) % length * (2.0 * math.pi / length)
    weight = np.where((freq == 0) | (freq == length // 2), 1.0, 2.0)[:, None] / length
    return (weight * np.cos(turn)).astype(np.float32), (weight * np.sin(turn)).astype(np.float32)


def high_einsum(form, left, right):
    return jnp.einsum(form, left, right, precision=HIGHEST)


def ssm_kernel(modes, log_dt):
    cos_h, sin_h = half_angles(TOK_DEV)
    index = jnp.arange(modes.shape[2], dtype=jnp.int32).astype(jnp.float32)
    lam_re = -0.5 * jnp.exp(modes[0])
    lam_im = math.pi * (index + modes[1])
    rank_re, rank_im, in_re, in_im, out_re, out_im = (modes[i] for i in range(2, 8))
    sigma = (2.0 * jnp.exp(-log_dt))[:, None]

    def points(values):
        return values.T[:, None, :]

    den_re = points(lam_re * lam_re + lam_im * lam_im) * (cos_h * cos_h)[:, None] - (
        sigma * sigma
    ).T * (sin_h * sin_h)[:, None]
    den_im = points(-2.0 * sigma * lam_re) * (sin_h * cos_h)[:, None]
    den_sq = den_re * den_re + den_im * den_im
    inv_re = den_re / den_sq
    inv_im = -den_im / den_sq
    sums = []
    for real, imag in (
        (out_re * in_re + out_im * in_im, out_re * in_im - out_im * in_re),
        (out_re * rank_re + out_im * rank_im, out_re * rank_im - out_im * rank_re),
        (rank_re * in_re + rank_im * in_im, rank_re * in_im - rank_im * in_re),
        (rank_re * rank_re + rank_im * rank_im, jnp.zeros_like(rank_re)),
    ):
        turned = points(real * lam_re + imag * lam_im)
        real = points(real)
        p_re, p_im = jnp.sum(real * inv_re, axis=0), jnp.sum(real * inv_im, axis=0)
        q_re, q_im = jnp.sum(turned * inv_re, axis=0), jnp.sum(turned * inv_im, axis=0)
        sine = sin_h[:, None] * sigma.T
        sums.append((-sine * p_im - cos_h[:, None] * q_re, sine * p_re - cos_h[:, None] * q_im))
    (cross_re, cross_im), (left_re, left_im), (right_re, right_im), (self_re, self_im) = sums
    twice = 2.0 * cos_h[:, None]
    loop_re, loop_im = 1.0 + twice * self_re, twice * self_im
    back_re, back_im = twice * right_re, twice * right_im
    loop_sq = loop_re * loop_re + loop_im * loop_im
    ratio_re = (back_re * loop_re + back_im * loop_im) / loop_sq
    ratio_im = (back_im * loop_re - back_re * loop_im) / loop_sq
    part_re = cross_re - (left_re * ratio_re - left_im * ratio_im)
    part_im = cross_im - (left_re * ratio_im + left_im * ratio_re)
    spec_re = 2.0 * (cos_h[:, None] * part_re - sin_h[:, None] * part_im)
    spec_im = 2.0 * (cos_h[:, None] * part_im + sin_h[:, None] * part_re)
    cos_tab, sin_tab = inverse_tables(TOK_DEV)
    return high_einsum("kl,kc->lc", cos_tab, spec_re) - high_einsum("kl,kc->lc", sin_tab, spec_im)


BLOCK = 128
BLOCKS = TOK_DEV // BLOCK
FIRST = 2 * BLOCKS
KEPT = FIRST // 2 + 1


def transform_tables():
    length = 2 * TOK_DEV
    turn = np.arange(KEPT)[:, None] * np.arange(BLOCK)[None, :] * (2.0 * math.pi / length)
    small = np.arange(BLOCK)[:, None] * np.arange(BLOCK)[None, :] % BLOCK * (2.0 * math.pi / BLOCK)
    spots = np.stack([np.arange(BLOCKS) + np.arange(BLOCKS) // (2 << b) * (2 << b) for b in range(3)])
    angle = spots[:, None, :] * np.arange(KEPT)[None, :, None] % FIRST * (2.0 * math.pi / FIRST)
    parts = (np.cos(turn), np.sin(turn), np.cos(small), np.sin(small), np.cos(angle), np.sin(angle))
    return [part.astype(np.float32) for part in parts]


def forward_transform(blocks, cos_a, sin_a):
    cos_t, sin_t, cos_s, sin_s, _, _ = transform_tables()
    step_re = high_einsum("ka,abc->kbc", cos_a, blocks)
    step_im = -high_einsum("ka,abc->kbc", sin_a, blocks)
    turned_re = step_re * cos_t[..., None] + step_im * sin_t[..., None]
    turned_im = step_im * cos_t[..., None] - step_re * sin_t[..., None]
    both = jnp.concatenate([turned_re, turned_im], axis=1)
    matrix = np.block([[cos_s, sin_s], [-sin_s, cos_s]])
    return high_einsum("pb,kbc->kpc", matrix, both)


def inverse_transform(spectrum, cos_a, sin_a):
    cos_t, sin_t, cos_s, sin_s, _, _ = transform_tables()
    matrix = np.block([[cos_s, -sin_s], [sin_s, cos_s]])
    both = high_einsum("bp,kpc->kbc", matrix, spectrum)
    step_re, step_im = both[:, :BLOCK], both[:, BLOCK:]
    turned_re = step_re * cos_t[..., None] - step_im * sin_t[..., None]
    turned_im = step_im * cos_t[..., None] + step_re * sin_t[..., None]
    weight = np.where(np.arange(KEPT) % (KEPT - 1) == 0, 1.0, 2.0).astype(np.float32) / (2 * TOK_DEV)
    return high_einsum("ka,kbc->abc", cos_a * weight[:, None], turned_re) - high_einsum(
        "ka,kbc->abc", sin_a * weight[:, None], turned_im
    )


def multiply(left, right):
    left_re, left_im = left[:, :BLOCK], left[:, BLOCK:]
    right_re, right_im = right[:, :BLOCK], right[:, BLOCK:]
    return jnp.concatenate(
        [left_re * right_re - left_im * right_im, left_re * right_im + left_im * right_re], axis=1
    )


def mixer(normed, kernel_taps, skip_gain, bucket, filled):
    _, _, _, _, cos_a, sin_a = transform_tables()
    cos_x, sin_x = jnp.asarray(cos_a)[bucket], jnp.asarray(sin_a)[bucket]
    item_blocks = 2 << bucket
    block_id = jnp.arange(BLOCKS, dtype=jnp.int32)[:, None, None]
    taps = jnp.where(block_id < item_blocks, kernel_taps.reshape(BLOCKS, BLOCK, -1), 0.0)
    signal = forward_transform(normed.reshape(BLOCKS, BLOCK, -1), cos_x, sin_x)
    answer = forward_transform(taps, cos_a[2], sin_a[2])
    result = inverse_transform(multiply(signal, answer), cos_x, sin_x)
    result = jnp.where(block_id < filled * item_blocks, result, 0.0)
    return result.reshape(normed.shape) + skip_gain * normed


def shards(
    tokens,
    cotangent,
    group_bucket,
    group_items,
    first_norm_gain,
    first_norm_bias,
    modes,
    log_dt,
    d_skip,
    w_a,
    b_a,
    w_b,
    b_b,
    second_norm_gain,
    second_norm_bias,
    w_up,
    b_up,
    w_down,
    b_down,
):
    input_tokens = tokens.astype(jnp.float32)
    sums_in = lax.psum(
        (jnp.sum(input_tokens, axis=1), jnp.sum(input_tokens * input_tokens, axis=1)), "chan"
    )
    input_average = sums_in[0][:, None] / MODEL_WIDTH
    input_inverse_deviation = lax.rsqrt(
        sums_in[1][:, None] / MODEL_WIDTH - input_average * input_average + EPSILON
    )
    input_standardized = (input_tokens - input_average) * input_inverse_deviation
    input_normalized = input_standardized * first_norm_gain + first_norm_bias
    level = group_bucket[0]
    filled = group_items[0]
    kernel_taps, kernel_back = jax.vjp(ssm_kernel, modes, log_dt)

    def local_mix(values, taps_now, skip_gain):
        return mixer(values, taps_now, skip_gain, level, filled)

    mixed, mix_back = jax.vjp(local_mix, input_normalized, kernel_taps, d_skip)
    acts_low = jax.nn.gelu(mixed, approximate=False).astype(jnp.bfloat16)
    wa_full, wb_full, up_full, down_full = (
        lax.all_gather(w_a.astype(jnp.bfloat16), "dp", axis=0, tiled=True),
        lax.all_gather(w_b.astype(jnp.bfloat16), "dp", axis=0, tiled=True),
        lax.all_gather(w_up.astype(jnp.bfloat16), "dp", axis=0, tiled=True),
        lax.all_gather(w_down.astype(jnp.bfloat16), "dp", axis=1, tiled=True),
    )
    acts_full = lax.all_gather(acts_low, "chan", axis=1, tiled=True)
    gate_a = product(acts_full, wa_full) + b_a
    gate_b = product(acts_full, wb_full) + b_b
    gate_sig = jax.nn.sigmoid(gate_b)
    residual_stream = input_tokens + gate_a * gate_sig
    sums_mid = lax.psum(
        (jnp.sum(residual_stream, axis=1), jnp.sum(residual_stream * residual_stream, axis=1)),
        "chan",
    )
    middle_average = sums_mid[0][:, None] / MODEL_WIDTH
    middle_inverse_deviation = lax.rsqrt(
        sums_mid[1][:, None] / MODEL_WIDTH - middle_average * middle_average + EPSILON
    )
    middle_standardized = (residual_stream - middle_average) * middle_inverse_deviation
    middle_reduced = (middle_standardized * second_norm_gain + second_norm_bias).astype(
        jnp.bfloat16
    )
    mid_full = lax.all_gather(middle_reduced, "chan", axis=1, tiled=True)
    pre_act = product(mid_full, up_full) + b_up
    hidden_low = jax.nn.gelu(pre_act, approximate=False).astype(jnp.bfloat16)
    branch = (
        lax.psum_scatter(product(hidden_low, down_full), "chan", scatter_dimension=1, tiled=True)
        + b_down
    )
    output = (residual_stream + branch).astype(jnp.bfloat16)
    grad_f = cotangent.astype(jnp.bfloat16)
    grad_b_down = jnp.sum(grad_f.astype(jnp.float32), axis=0)
    grad_f_full = lax.all_gather(grad_f, "chan", axis=1, tiled=True)
    grad_w_down = product_tn(hidden_low, grad_f_full)
    grad_pre = (product_nt(grad_f_full, down_full) * gelu_slope(pre_act)).astype(jnp.bfloat16)
    grad_b_up = jnp.sum(grad_pre.astype(jnp.float32), axis=0)
    grad_w_up = product_tn(mid_full, grad_pre)
    middle_gradient = lax.psum_scatter(
        product_nt(grad_pre, up_full), "chan", scatter_dimension=1, tiled=True
    )
    second_norm_gain_gradient = jnp.sum(middle_gradient * middle_standardized, axis=0)
    grad_ln2_bias = jnp.sum(middle_gradient, axis=0)
    middle_rescaled = middle_gradient * second_norm_gain
    middle_backward = lax.psum(
        (jnp.sum(middle_rescaled, axis=1), jnp.sum(middle_rescaled * middle_standardized, axis=1)),
        "chan",
    )
    grad_resid = cotangent + middle_inverse_deviation * (
        middle_rescaled
        - middle_backward[0][:, None] / MODEL_WIDTH
        - middle_standardized * middle_backward[1][:, None] / MODEL_WIDTH
    )
    grad_a = (grad_resid * gate_sig).astype(jnp.bfloat16)
    grad_b = (grad_resid * gate_a * gate_sig * (1.0 - gate_sig)).astype(jnp.bfloat16)
    grad_b_a = jnp.sum(grad_a.astype(jnp.float32), axis=0)
    grad_b_b = jnp.sum(grad_b.astype(jnp.float32), axis=0)
    grad_w_a = product_tn(acts_full, grad_a)
    grad_w_b = product_tn(acts_full, grad_b)
    grad_acts = lax.psum_scatter(
        product_nt(grad_a, wa_full) + product_nt(grad_b, wb_full),
        "chan",
        scatter_dimension=1,
        tiled=True,
    )
    grad_mixed = grad_acts * gelu_slope(mixed)
    normalized_gradient, grad_kernel, grad_skip = mix_back(grad_mixed)
    grad_modes, grad_log_dt = kernel_back(grad_kernel)
    first_norm_gain_gradient = jnp.sum(normalized_gradient * input_standardized, axis=0)
    grad_ln1_bias = jnp.sum(normalized_gradient, axis=0)
    input_rescaled = normalized_gradient * first_norm_gain
    input_backward = lax.psum(
        (jnp.sum(input_rescaled, axis=1), jnp.sum(input_rescaled * input_standardized, axis=1)),
        "chan",
    )
    grad_tokens = grad_resid + input_inverse_deviation * (
        input_rescaled
        - input_backward[0][:, None] / MODEL_WIDTH
        - input_standardized * input_backward[1][:, None] / MODEL_WIDTH
    )
    grad_w_a, grad_w_b, grad_w_up, grad_w_down = (
        lax.psum_scatter(grad_w_a, "dp", scatter_dimension=0, tiled=True),
        lax.psum_scatter(grad_w_b, "dp", scatter_dimension=0, tiled=True),
        lax.psum_scatter(grad_w_up, "dp", scatter_dimension=0, tiled=True),
        lax.psum_scatter(grad_w_down, "dp", scatter_dimension=1, tiled=True),
    )
    (
        first_norm_gain_gradient,
        grad_ln1_bias,
        grad_modes,
        grad_log_dt,
        grad_skip,
        grad_b_a,
        grad_b_b,
        second_norm_gain_gradient,
        grad_ln2_bias,
        grad_b_up,
        grad_b_down,
    ) = lax.psum(
        (
            first_norm_gain_gradient,
            grad_ln1_bias,
            grad_modes,
            grad_log_dt,
            grad_skip,
            grad_b_a,
            grad_b_b,
            second_norm_gain_gradient,
            grad_ln2_bias,
            grad_b_up,
            grad_b_down,
        ),
        "dp",
    )
    return (
        output,
        grad_tokens,
        first_norm_gain_gradient,
        grad_ln1_bias,
        grad_modes,
        grad_log_dt,
        grad_skip,
        grad_w_a,
        grad_b_a,
        grad_w_b,
        grad_b_b,
        second_norm_gain_gradient,
        grad_ln2_bias,
        grad_w_up,
        grad_b_up,
        grad_w_down,
        grad_b_down,
    )


LANES = 128
HALF = 64
PAIRS = 4
ROWS = 128
N_CHAN = 8
WIDE = 640
MESH = pl.DeviceIdType.MESH
F32 = jnp.float32
BF16 = jnp.bfloat16


def split_two(matrix):
    high = matrix.astype(ml_dtypes.bfloat16)
    low = (matrix - high.astype(np.float64)).astype(ml_dtypes.bfloat16)
    return np.concatenate([high, low], axis=1)


def lane_rows(values_low, values_high):
    return np.repeat(np.stack([values_low, values_high], -1), HALF, axis=-1)


def mixer_tables():
    line = np.arange(ROWS)
    small = np.outer(line, line) % ROWS * (2.0 * math.pi / ROWS)
    cos_s, sin_s = np.cos(small), np.sin(small)
    forward = np.block([[cos_s, sin_s], [-sin_s, cos_s]])
    real = np.zeros((2 * ROWS, 2 * ROWS))
    for row in range(HALF):
        weight = 1.0 if row == 0 else 2.0
        turn = 2.0 * math.pi / ROWS * row * line
        real[:ROWS, row] = weight * np.cos(turn)
        real[:ROWS, ROWS + row] = -weight * np.sin(turn)
        turn = 2.0 * math.pi / TOK_DEV * (4 + 8 * row) * line
        real[ROWS:, HALF + row] = 2.0 * np.cos(turn)
        real[ROWS:, ROWS + HALF + row] = -2.0 * np.sin(turn)
    mats = np.stack([split_two(m) for m in (forward, forward.T, real, real.T)])

    twiddle = []
    for pair in range(5):
        turn = np.stack([line * k * (math.pi / TOK_DEV) for k in (2 * pair, 2 * pair + 1)])
        twiddle += [lane_rows(np.cos(turn[0]), np.cos(turn[1])), lane_rows(np.sin(turn[0]), np.sin(turn[1]))]
    for first, second in ((1, 2), (3, 0)):
        turn = np.stack([line * k * (2.0 * math.pi / TOK_DEV) for k in (first, second)])
        twiddle += [lane_rows(np.cos(turn[0]), np.cos(turn[1])), lane_rows(np.sin(turn[0]), np.sin(turn[1]))]

    def forward_rows(coef, pairs):
        out = []
        for low, high in pairs:
            for part in range(2):
                for j in range(PAIRS):
                    out.append(lane_rows(coef(2 * j, low, part), coef(2 * j + 1, high, part)))
                for j in range(PAIRS):
                    out.append(lane_rows(coef(2 * j, high, part), coef(2 * j + 1, low, part)))
        return np.stack(out)

    def inverse_rows(coef, pairs):
        out = []
        for low, high in pairs:
            for part in range(2):
                for j in range(PAIRS):
                    out.append(lane_rows(coef(2 * j, low, part), coef(2 * j + 1, high, part)))
                for j in range(PAIRS):
                    out.append(lane_rows(coef(2 * j + 1, low, part), coef(2 * j, high, part)))
        return np.stack(out)

    levels = []
    pairs = [(2 * p, 2 * p + 1) for p in range(5)]
    for level in range(3):
        item = 2 << level

        def angle(block, k):
            return 2.0 * math.pi / 16 * ((block + block // item * item) * k % 16)

        def fwd(block, k, part):
            if k > 8:
                return np.zeros(())
            return np.cos(angle(block, k)) if part == 0 else -np.sin(angle(block, k))

        def inv(block, k, part):
            weight = (1.0 if k in (0, 8) else 2.0) / (2 * TOK_DEV)
            return weight * fwd(block, k, part)

        levels.append(np.concatenate([forward_rows(fwd, pairs), inverse_rows(inv, pairs)]))

    def taps(block, k, part):
        if k == 0:
            return np.asarray((1.0 if part == 0 else (-1.0) ** block) / TOK_DEV)
        turn = 2.0 * math.pi / 8 * (block * k % 8)
        return np.asarray((np.cos(turn) if part == 0 else -np.sin(turn)) * 2.0 / TOK_DEV)

    tap_pairs = [(1, 2), (3, 0)]
    taps_back = forward_rows(taps, tap_pairs)
    taps_rows = inverse_rows(taps, tap_pairs)
    freq_even = np.where(line < HALF, 8 * line, 4 + 8 * (line - HALF))
    half_angle = np.stack(
        [lane_rows(1 + 8 * line, 2 + 8 * line), lane_rows(3 + 8 * line, freq_even)]
    ) * (math.pi / TOK_DEV)
    wave = np.stack([np.cos(half_angle), np.sin(half_angle)])
    return (
        mats,
        np.stack(twiddle).astype(np.float32),
        np.stack(levels).astype(np.float32),
        np.concatenate([levels[2], taps_rows, taps_back]).astype(np.float32),
        wave.astype(np.float32),
    )


def low_lanes(rows):
    return lax.broadcasted_iota(jnp.int32, (rows, LANES), 1) < HALF


def turn_half(values):
    return pltpu.roll(values, HALF, 1)


def split_pair(values):
    upper, lower = values[:HALF], values[HALF:]
    mask = low_lanes(HALF)
    return jnp.where(mask, upper, turn_half(lower)), jnp.where(mask, turn_half(upper), lower)


def join_pair(first, second):
    mask = low_lanes(HALF)
    return jnp.concatenate(
        [jnp.where(mask, first, turn_half(second)), jnp.where(mask, turn_half(first), second)], axis=0
    )


def interleave(first, second):
    mask = low_lanes(first.shape[0])
    return jnp.where(mask, first, turn_half(second)), jnp.where(mask, turn_half(first), second)


def fold(values):
    return values + turn_half(values)


def reciprocal(values):
    guess = pl.reciprocal(values, approx=True)
    return guess * (2.0 - values * guess)


ERF_TERMS = (1.061405429, -1.453152027, 1.421413741, -0.284496736, 0.254829592)


def normal_parts(values):
    bell = jnp.exp(-0.5 * values * values)
    t = reciprocal(1.0 + (0.3275911 * 0.7071067811865476) * jnp.abs(values))
    tail = ERF_TERMS[0]
    for term in ERF_TERMS[1:]:
        tail = tail * t + term
    tail = 0.5 * (tail * t) * bell
    return jnp.where(values < 0.0, tail, 1.0 - tail), bell * 0.3989422804014327


def column_sum(values):
    return jnp.sum(values, axis=0, keepdims=True)


def dot_nt(left, right):
    return lax.dot_general(left, right, (((1,), (1,)), ((), ())), preferred_element_type=F32)


def dot_nn(left, right):
    return jnp.dot(left, right, preferred_element_type=F32)


def store_split(ref, row, lane, values, exact=True):
    high = values.astype(BF16)
    place = (pl.ds(row, values.shape[0]), pl.ds(lane, values.shape[1]))
    ref[(0,) + place] = high
    if exact:
        ref[(1,) + place] = (values - high.astype(F32)).astype(BF16)


def split_product(mat_ref, which, rhs_ref, lane, width, exact=True):
    high = mat_ref[which, :, 0:256]
    low = mat_ref[which, :, 256:512]
    rhs_high = rhs_ref[0, :, lane : lane + width]
    product = dot_nn(high, rhs_high) + dot_nn(low, rhs_high)
    if exact:
        product = product + dot_nn(high, rhs_ref[1, :, lane : lane + width])
    return product


CHUNK = 32


def over_chunks(body, size=CHUNK, first=0, rows=ROWS):
    def step(index, carry):
        body(pl.multiple_of(first + index * size, size))
        return carry

    lax.fori_loop(0, rows // size, step, 0)


def spread_pairs(src, coef_ref, base, twiddle_ref, twiddle_base, pairs, rhs_ref, exact=True):
    def body(row):
        rows = pl.ds(row, CHUNK)
        blocks = [src(j, rows) for j in range(PAIRS)]
        for pair in range(pairs):
            parts = []
            for part in range(2):
                at = base + (pair * 2 + part) * 8
                straight = sum(blocks[j] * coef_ref[at + j : at + j + 1, :] for j in range(PAIRS))
                crossed = sum(blocks[j] * coef_ref[at + 4 + j : at + 5 + j, :] for j in range(PAIRS))
                parts.append(straight + turn_half(crossed))
            cosine = twiddle_ref[twiddle_base + 2 * pair, rows, :]
            sine = twiddle_ref[twiddle_base + 2 * pair + 1, rows, :]
            store_split(rhs_ref, row, pair * LANES, parts[0] * cosine + parts[1] * sine, exact)
            store_split(rhs_ref, row + ROWS, pair * LANES, parts[1] * cosine - parts[0] * sine, exact)

    over_chunks(body)


def gather_pairs(values_ref, coef_ref, base, twiddle_ref, twiddle_base, pairs, store):
    def body(row):
        rows = pl.ds(row, CHUNK)
        straight, crossed = [0.0] * PAIRS, [0.0] * PAIRS
        for pair in range(pairs):
            lanes = slice(pair * LANES, (pair + 1) * LANES)
            real, imag = values_ref[rows, lanes], values_ref[pl.ds(row + ROWS, CHUNK), lanes]
            cosine = twiddle_ref[twiddle_base + 2 * pair, rows, :]
            sine = twiddle_ref[twiddle_base + 2 * pair + 1, rows, :]
            for part, value in enumerate((real * cosine - imag * sine, imag * cosine + real * sine)):
                at = base + (pair * 2 + part) * 8
                for j in range(PAIRS):
                    straight[j] = straight[j] + value * coef_ref[at + j : at + j + 1, :]
                    crossed[j] = crossed[j] + value * coef_ref[at + 4 + j : at + 5 + j, :]
        for j in range(PAIRS):
            store(j, rows, straight[j] + turn_half(crossed[j]))

    over_chunks(body)


GROUPS = ((0, 256), (256, 256), (512, 128))


def transform_into(dst_ref, mat_ref, which, rhs_ref, exact=True):
    for lane, width in GROUPS:
        dst_ref[:, lane : lane + width] = split_product(mat_ref, which, rhs_ref, lane, width, exact)


def multiply_spectra(left_ref, right_ref, rhs_ref, conjugate, exact=True):
    def body(row):
        top, bottom = pl.ds(row, CHUNK), pl.ds(row + ROWS, CHUNK)
        for pair in range(5):
            lanes = slice(pair * LANES, (pair + 1) * LANES)
            a_re, a_im = left_ref[top, lanes], left_ref[bottom, lanes]
            b_re, b_im = right_ref[top, lanes], right_ref[bottom, lanes]
            if conjugate:
                out_re, out_im = a_re * b_re + a_im * b_im, a_re * b_im - a_im * b_re
            else:
                out_re, out_im = a_re * b_re - a_im * b_im, a_re * b_im + a_im * b_re
            store_split(rhs_ref, row, pair * LANES, out_re, exact)
            store_split(rhs_ref, row + ROWS, pair * LANES, out_im, exact)

    over_chunks(body)


def pair_terms(modes_ref):
    rank_re, rank_im, in_re, in_im, out_re, out_im = (modes_ref[i] for i in range(2, 8))
    return (
        (out_re * in_re + out_im * in_im, out_re * in_im - out_im * in_re),
        (out_re * rank_re + out_im * rank_im, out_re * rank_im - out_im * rank_re),
        (rank_re * in_re + rank_im * in_im, rank_re * in_im - rank_im * in_re),
        (rank_re * rank_re + rank_im * rank_im, None),
    )


def mode_values(modes_ref):
    index = lax.broadcasted_iota(jnp.int32, modes_ref.shape[1:], 0).astype(F32)
    return -0.5 * jnp.exp(modes_ref[0]), math.pi * (index + modes_ref[1])


POINT_ROWS = 16


def resolvent(coef_ref, n, square_cos, cos_sin, scaled):
    den_re = coef_ref[8, pl.ds(n, 1), :] * square_cos - scaled
    den_im = coef_ref[9, pl.ds(n, 1), :] * cos_sin
    inverse = reciprocal(den_re * den_re + den_im * den_im)
    return den_re * inverse, -(den_im * inverse)


def complex_multiply(a_re, a_im, b_re, b_im):
    return a_re * b_re - a_im * b_im, a_re * b_im + a_im * b_re


def conj_multiply(a_re, a_im, b_re, b_im):
    return a_re * b_re + a_im * b_im, a_re * b_im - a_im * b_re


def combine(sums, sigma, cosine, sine):
    terms = []
    for p_re, p_im, q_re, q_im in (sums[4 * q : 4 * q + 4] for q in range(4)):
        swing = sigma * sine
        terms.append((-swing * p_im - cosine * q_re, swing * p_re - cosine * q_im))
    twice = 2.0 * cosine
    loop_re, loop_im = 1.0 + twice * terms[3][0], twice * terms[3][1]
    scale = reciprocal(loop_re * loop_re + loop_im * loop_im)
    inv = (loop_re * scale, -(loop_im * scale))
    ratio = complex_multiply(twice * terms[2][0], twice * terms[2][1], *inv)
    return terms, inv, ratio


QUARTER = 32


def cauchy_coefficients(modes_ref, sigma, coef_ref):
    lam_re, lam_im = mode_values(modes_ref)
    for q, (real, imag) in enumerate(pair_terms(modes_ref)):
        coef_ref[q] = real
        coef_ref[4 + q] = real * lam_re if imag is None else real * lam_re + imag * lam_im
    coef_ref[8] = lam_re * lam_re + lam_im * lam_im
    coef_ref[9] = -2.0 * sigma * lam_re


def wave_rows(wave_ref, pair, base, row):
    rows = pl.ds(pl.multiple_of(base + row, POINT_ROWS), POINT_ROWS)
    return wave_ref[0, pair, rows, :], wave_ref[1, pair, rows, :]


def cauchy_forward(index, sigma, coef_ref, wave_ref, base, sums_ref, spec_ref):
    sigma_sq = sigma * sigma
    pair, row = index // 2, index % 2 * POINT_ROWS
    rows = slice(row, row + POINT_ROWS)
    lanes = slice(pair * LANES, (pair + 1) * LANES)
    cosine, sine = wave_rows(wave_ref, pair, base, row)
    square_cos, cos_sin, scaled = cosine * cosine, cosine * sine, sigma_sq * (sine * sine)

    def add_mode(n, sums):
        sums = list(sums)
        for k in range(4):
            at = n * 4 + k
            inv_re, inv_im = resolvent(coef_ref, at, square_cos, cos_sin, scaled)
            for q in range(4):
                plain = coef_ref[q, pl.ds(at, 1), :]
                turned = coef_ref[4 + q, pl.ds(at, 1), :]
                sums[4 * q] = sums[4 * q] + plain * inv_re
                sums[4 * q + 1] = sums[4 * q + 1] + plain * inv_im
                sums[4 * q + 2] = sums[4 * q + 2] + turned * inv_re
                sums[4 * q + 3] = sums[4 * q + 3] + turned * inv_im
        return tuple(sums)

    zero = jnp.zeros((POINT_ROWS, LANES), F32)
    sums = lax.fori_loop(0, 8, add_mode, (zero,) * 16)
    for i in range(16):
        sums_ref[pair, i, rows, :] = sums[i]
    terms, _, ratio = combine(sums, sigma, cosine, sine)
    cut_re, cut_im = complex_multiply(*terms[1], *ratio)
    part_re, part_im = terms[0][0] - cut_re, terms[0][1] - cut_im
    spec_re, spec_im = complex_multiply(2.0 * cosine, 2.0 * sine, part_re, part_im)
    spec_ref[rows, lanes] = spec_re
    spec_ref[row + QUARTER : row + QUARTER + POINT_ROWS, lanes] = spec_im


PLACES = [(pair, row) for pair in range(2) for row in range(0, QUARTER, POINT_ROWS)]


def point_grads(sigma, wave_ref, base, sums_ref, spec_ref, grad_ref):
    zero = jnp.zeros((POINT_ROWS, LANES), F32)
    sigma_sum = zero
    for pair, row in PLACES:
        rows = slice(row, row + POINT_ROWS)
        lanes = slice(pair * LANES, (pair + 1) * LANES)
        cosine, sine = wave_rows(wave_ref, pair, base, row)
        sums = [sums_ref[pair, i, rows, :] for i in range(16)]
        terms, inv, ratio = combine(sums, sigma, cosine, sine)
        spec_re, spec_im = spec_ref[rows, lanes], spec_ref[row + QUARTER : row + QUARTER + POINT_ROWS, lanes]
        part = conj_multiply(2.0 * cosine, 2.0 * sine, spec_re, spec_im)
        left = conj_multiply(*ratio, *part)
        ratio_grad = conj_multiply(*terms[1], *part)
        back = conj_multiply(*inv, -ratio_grad[0], -ratio_grad[1])
        twice = 2.0 * cosine
        loop = conj_multiply(*ratio, *back)
        grads = (
            part,
            (-left[0], -left[1]),
            (twice * back[0], twice * back[1]),
            (-twice * loop[0], -twice * loop[1]),
        )
        swing = sigma * sine
        for q, (g_re, g_im) in enumerate(grads):
            grad_ref[pair, 4 * q, rows, :] = swing * g_im
            grad_ref[pair, 4 * q + 1, rows, :] = -swing * g_re
            grad_ref[pair, 4 * q + 2, rows, :] = -cosine * g_re
            grad_ref[pair, 4 * q + 3, rows, :] = -cosine * g_im
            sigma_sum = sigma_sum + sine * (g_im * sums[4 * q] - g_re * sums[4 * q + 1])
    return sigma_sum


def mode_sums(part, square_sum, sigma, coef_ref, wave_ref, base, grad_ref, back_ref):
    sigma_sq = sigma * sigma

    def mode(n, square_sum):
        plain = [coef_ref[q, pl.ds(n, 1), :] for q in range(4)]
        turned = [coef_ref[4 + q, pl.ds(n, 1), :] for q in range(4)]
        sums = [0.0] * 10
        for pair, row in PLACES:
            rows = slice(row, row + POINT_ROWS)
            cosine, sine = wave_rows(wave_ref, pair, base, row)
            square_cos, cos_sin, square_sin = cosine * cosine, cosine * sine, sine * sine
            inv_re, inv_im = resolvent(coef_ref, n, square_cos, cos_sin, sigma_sq * square_sin)
            grad_re, grad_im = 0.0, 0.0
            for q in range(4):
                p_re, p_im = grad_ref[pair, 4 * q, rows, :], grad_ref[pair, 4 * q + 1, rows, :]
                q_re, q_im = grad_ref[pair, 4 * q + 2, rows, :], grad_ref[pair, 4 * q + 3, rows, :]
                grad_re = grad_re + (plain[q] * p_re + turned[q] * q_re)
                grad_im = grad_im + (plain[q] * p_im + turned[q] * q_im)
                sums[q] = sums[q] + (p_re * inv_re + p_im * inv_im)
                sums[4 + q] = sums[4 + q] + (q_re * inv_re + q_im * inv_im)
            square_re = inv_re * inv_re - inv_im * inv_im
            square_im = 2.0 * inv_re * inv_im
            den_re, den_im = conj_multiply(square_re, square_im, grad_re, grad_im)
            sums[8] = sums[8] - den_re * square_cos
            sums[9] = sums[9] - den_im * cos_sin
            square_sum = square_sum + den_re * square_sin
        for i in range(10):
            back_ref[i, pl.ds(n, 1), :] = column_sum(sums[i])
        return square_sum

    return lax.fori_loop(part * 8, part * 8 + 8, mode, square_sum)


def mode_gradients(modes_ref, sigma, nyquist_grad, step, sigma_sum, square_sum, back_ref):
    plain_grad = [fold(back_ref[q]) for q in range(4)]
    turned_grad = [fold(back_ref[4 + q]) for q in range(4)]
    abs_grad, skew_grad = fold(back_ref[8]), fold(back_ref[9])
    lam_re, lam_im = mode_values(modes_ref)
    plain_grad[0] = plain_grad[0] + step * nyquist_grad
    rank_re, rank_im, in_re, in_im, out_re, out_im = (modes_ref[i] for i in range(2, 8))
    lam_re_grad = 2.0 * lam_re * abs_grad - 2.0 * sigma * skew_grad
    lam_im_grad = 2.0 * lam_im * abs_grad
    real_grad, imag_grad = [], []
    terms = pair_terms(modes_ref)
    for q, (real, imag) in enumerate(terms):
        lam_re_grad = lam_re_grad + turned_grad[q] * real
        if imag is not None:
            lam_im_grad = lam_im_grad + turned_grad[q] * imag
        real_grad.append(plain_grad[q] + turned_grad[q] * lam_re)
        imag_grad.append(turned_grad[q] * lam_im)
    r0, r1, r2, r3 = real_grad
    i0, i1, i2, _ = imag_grad
    grads = (
        lam_re_grad * lam_re,
        math.pi * lam_im_grad,
        r1 * out_re - i1 * out_im + r2 * in_re + i2 * in_im + 2.0 * r3 * rank_re,
        r1 * out_im + i1 * out_re + r2 * in_im - i2 * in_re + 2.0 * r3 * rank_im,
        r0 * out_re - i0 * out_im + r2 * rank_re - i2 * rank_im,
        r0 * out_im + i0 * out_re + r2 * rank_im + i2 * rank_re,
        r0 * in_re + i0 * in_im + r1 * rank_re + i1 * rank_im,
        r0 * in_im - i0 * in_re + r1 * rank_im - i1 * rank_re,
    )
    sigma_grad = (
        fold(column_sum(sigma_sum) + 2.0 * sigma * column_sum(square_sum))
        - 2.0 * column_sum(skew_grad * lam_re)
    )
    nyquist = step * column_sum(terms[0][0])
    return grads, nyquist * nyquist_grad - sigma * sigma_grad


def ring_place(chan):
    z, y = lax.div(chan, 2), lax.rem(chan, 2)
    return z + y * (7 - 2 * z)


def ring_chan(place):
    back = lax.div(place, 4)
    z = place * (1 - back) + (7 - place) * back
    return 2 * z + back


TURNS = (1, -1)


def block_kernel(
    bucket_ref, items_ref, tokens_ref, cotangent_ref, gain1_ref, bias1_ref, raw_modes_ref, log_dt_ref, skip_ref,
    wa_ref, ba_ref, wb_ref, bb_ref, gain2_ref, bias2_ref, up_ref, bup_ref, down_ref, bdown_ref,
    levels_ref, coefc_ref, mat_ref, tw_ref, wave_ref,
    out_ref, dtok_ref, gw_ref, gm_ref, gv_ref,
    tok_ref, aux_ref, coefl_ref, modes_ref,
    wab_ref, wh_ref, gab_w_ref, gh_ref,
    stage_ref, sib_ab_ref, ring_ab_ref, ring_h_ref, part_ab_ref, cross_ref, keep_ref, swap_ref, gate_total_ref,
    in_send, in_recv, head_send, head_recv, acts_send, acts_recv, back_send, back_recv, late_send, late_recv,
    sum_send, sum_recv, tail_send, dp_send, dp_low, dp_recv, spec_send, spec_recv, sgrad_send, sgrad_recv,
    hat_ref, norm_ref, slope_ref, conv_ref, rhs_ref, freq_ref, sig_ref, ans_ref, taps_ref,
    mcoef_ref, sums_ref, pgrad_ref, mback_ref, sgrad_ref, taps_freq_ref,
    gate_ref, swish_ref, res_ref, hat2_ref, acts_ref, norm2_ref, gradf_ref, branch_ref, back2_ref, half_send, half_recv,
    gab_ref, hid_ref, gpre_ref, acts_t_ref, norm2_t_ref, gradf_t_ref,
    gring_ss, gring_rs, gsib_ss, gsib_rs, gx_ss, gx_rs, gdx_ss, gdx_rs, gswap_ss, gswap_rs, core_ss, core_rs,
    rring_ss, rring_rs, rsib_ss, rsib_rs, rx_ss, rx_rs, rdx_ss, rdx_rs, rswap_ss, rswap_rs,
    a2a_ss, a2a_rs, dp_ss, dp_rs, spec_ss, spec_rs,
):
    dp, chan = lax.axis_index("dp"), lax.axis_index("chan")
    core = lax.rem(dp, 2)
    sibling = dp + 1 - 2 * core
    place = ring_place(chan)
    spots = [lax.rem(place + offset, 8) if offset else place for offset in range(8)]
    around = [ring_chan(spot) if offset else chan for offset, spot in enumerate(spots)]
    groups = [lax.rem(spot, 4) for spot in spots]
    group_lanes = [pl.multiple_of(lax.div(spot, 4) * LANES, LANES) for spot in spots]
    nexts = [around[1], around[7]]
    chan_peers = [chan] + [lax.rem(chan + r, N_CHAN) for r in range(1, N_CHAN)]
    dp_peers = [dp] + [lax.rem(dp + r, 4) for r in range(1, 4)]
    across = dp_peers[2]

    def chan_at(offset):
        return around[offset % 8]

    barrier = pltpu.get_barrier_semaphore()
    for r in range(1, N_CHAN):
        pl.semaphore_signal(barrier, inc=1, device_id={"chan": chan_peers[r]}, device_id_type=MESH)
    for r in range(1, 4):
        pl.semaphore_signal(barrier, inc=1, device_id={"dp": dp_peers[r]}, device_id_type=MESH)

    pending = []

    def remote(src, dst, send_sem, recv_sem, **device):
        return pltpu.make_async_remote_copy(
            src_ref=src, dst_ref=dst, send_sem=send_sem, recv_sem=recv_sem, device_id=device, device_id_type=MESH
        )

    def send(*args, **device):
        copy = remote(*args, **device)
        copy.start()
        pending.append(copy)

    def exchange(which, source, recv_ref):
        def copy(r):
            peer = chan_peers[r]
            return remote(
                source(peer), recv_ref.at[chan], a2a_ss.at[which, r - 1], a2a_rs.at[which, r - 1], chan=peer
            )

        def start():
            for r in range(1, N_CHAN):
                copy(r).start()

        def wait():
            for r in range(1, N_CHAN):
                copy(r).wait_recv()

        def finish():
            for r in range(1, N_CHAN):
                copy(r).wait_send()

        return start, wait, finish

    def rows_at(number, count):
        return pl.ds(pl.multiple_of(number, ROWS), count)

    def launch(copy):
        copy.start()
        pending.append(copy)

    own_row = dp * ROWS
    pair_row = (dp - core) * ROWS
    away_row = 2 * ROWS - pair_row
    gate_row, gate_away = (core * 2 + lax.div(dp, 2)) * ROWS, (core * 2 + 1 - lax.div(dp, 2)) * ROWS
    gate_pair, gate_other = core * 2 * ROWS, (1 - core) * 2 * ROWS
    half_lanes = pl.multiple_of(core * LANES, LANES)
    other_lanes = pl.multiple_of((1 - core) * LANES, LANES)

    def gate_view(ref):
        return lambda offset, row, count: ref.at[around[offset % 8], rows_at(row, count), :]

    def hidden_view(ref):
        return lambda offset, row, count: ref.at[
            :, groups[offset % 8], rows_at(row, count), pl.ds(group_lanes[offset % 8], LANES)
        ]

    class Ring:
        def __init__(self, which, view, base, count, hook=None):
            self.which, self.view, self.base, self.count, self.hook = which, view, base, count, hook

        def piece(self, turn, step, base):
            half = self.count // 2
            if step == 4:
                return self.view(4, base + turn * half, half)
            return self.view(-TURNS[turn] * step, base, self.count)

        def copy(self, turn, step, ref):
            slot = turn * 4 + step - 1
            return remote(ref, ref, gring_ss.at[self.which, slot], gring_rs.at[self.which, slot], chan=nexts[turn])

        def send(self, turn, step):
            half = self.count // 2
            if step == 4:
                ref = self.view(-TURNS[turn] * 3, self.base + turn * half, half)
            else:
                ref = self.piece(turn, step - 1, self.base)
            launch(self.copy(turn, step, ref))

        def start(self):
            for turn in range(2):
                self.send(turn, 1)

        def step(self, step):
            for turn in range(2):
                self.copy(turn, step, self.piece(turn, step, self.base)).wait_recv()
                if step < 4:
                    self.send(turn, step + 1)
                if self.hook:
                    self.hook(turn, step)

    def slot_of(turn, step):
        return turn * 4 + step - 1 if step else 8

    def gate_sib(base):
        ref = wab_ref.at[:, rows_at(base, 256), :]
        return remote(ref, ref, gsib_ss, gsib_rs, dp=sibling)

    def gate_spread():
        launch(gate_sib(gate_pair))

    def hidden_cross(turn, step, base):
        ref, slot = hidden_ring.piece(turn, step, base), slot_of(turn, step)
        return remote(ref, ref, gdx_ss.at[slot], gdx_rs.at[slot], dp=across)

    gate_ring = Ring(0, gate_view(wab_ref), gate_pair, 256)
    hidden_ring = Ring(
        1, hidden_view(wh_ref), pair_row, 256, lambda turn, step: launch(hidden_cross(turn, step, pair_row))
    )

    def gate_over(row):
        ref = gate_ring.view(0, row, ROWS)
        return remote(ref, ref, gx_ss, gx_rs, dp=across)

    def swap_copy(row):
        return remote(stage_ref, hidden_ring.view(0, row, ROWS), gswap_ss, gswap_rs, dp=sibling)

    def gather_prepare():
        gates = jnp.concatenate([wa_ref[...], wb_ref[...]], axis=0).T.astype(BF16)
        wab_ref[chan, rows_at(gate_row, ROWS), :] = gates
        for which, values in enumerate((up_ref[...], down_ref[...].T)):
            first, second = values[:, :LANES], values[:, LANES:]
            kept = jnp.where(core == 0, first, second)
            wh_ref[which, groups[0], rows_at(own_row, ROWS), pl.ds(group_lanes[0], LANES)] = kept.astype(BF16)
            stage_ref[which] = jnp.where(core == 0, second, first).astype(BF16)

    def gather_start():
        launch(swap_copy(own_row))
        launch(gate_over(gate_row))

    def hidden_first():
        swap_copy(sibling * ROWS).wait_recv()
        hidden_ring.start()
        launch(hidden_cross(0, 0, pair_row))

    def gate_first():
        gate_over(gate_away).wait_recv()
        gate_ring.start()

    ring_steps = [(0, 0)] + [(turn, step) for step in range(1, 5) for turn in range(2)]

    def gates_arrived():
        gate_sib(gate_other).wait_recv()

    def hidden_arrived(*steps):
        for turn, step in ring_steps:
            if step in steps:
                hidden_cross(turn, step, away_row).wait_recv()

    def beside(ref, j):
        start = 2 * j * ROWS
        return jnp.concatenate(
            [ref[:, start : start + ROWS].astype(F32), ref[:, start + ROWS : start + 2 * ROWS].astype(F32)], axis=0
        ).T

    for j in range(PAIRS):
        packed = beside(tokens_ref, j)
        tok_ref[j * ROWS : (j + 1) * ROWS, :] = packed.astype(BF16)
        for first, values in ((0, packed), (HALF, beside(cotangent_ref, j))):
            low, high = split_pair(values)
            in_send[2 * j, first : first + HALF, :] = low.astype(BF16)
            in_send[2 * j + 1, first : first + HALF, :] = high.astype(BF16)
    in_recv[chan] = in_send[chan]

    lane_id = lax.broadcasted_iota(jnp.int32, (8, LANES), 1)
    row_id = lax.broadcasted_iota(jnp.int32, (8, LANES), 0)
    halves = jnp.where((lane_id >= HALF) == (row_id == 1), 1.0, 0.0) * jnp.where(row_id < 2, 1.0, 0.0)
    halves = halves.astype(BF16)

    def token_sums(parts):
        total = 0.0
        for part in parts:
            total = total + dot_nt(halves, part)
        return [total[h : h + 1, j * ROWS : (j + 1) * ROWS] for h in range(2) for j in range(PAIRS)]

    def split(values):
        high = values.astype(BF16)
        return high, (values - high.astype(F32)).astype(BF16)

    tokens = tok_ref[...]
    wide_tokens = tokens.astype(F32)
    for i, sums in enumerate(token_sums([tokens]) + token_sums(split(wide_tokens * wide_tokens))):
        head_send[i : i + 1, :] = sums

    def row(*refs):
        return jnp.concatenate([ref[...].reshape(1, HALF) for ref in refs], axis=1)

    bup = bup_ref[...].reshape(1, 2 * LANES)
    head_send[16:17, :] = row(ba_ref, bb_ref)
    head_send[17:18, :] = row(gain2_ref, bias2_ref)
    head_send[18:19, :] = row(bdown_ref, bdown_ref)
    head_send[19:20, :] = bup[:, :LANES]
    head_send[20:21, :] = bup[:, LANES:]
    head_send[21:24, :] = jnp.zeros((3, LANES), F32)
    head_recv[chan] = head_send[...]
    head = exchange(0, lambda peer: head_send, head_recv)
    inputs = exchange(1, lambda peer: in_send.at[peer], in_recv)
    gather_prepare()
    pl.semaphore_wait(barrier, N_CHAN - 1 + 3)
    head[0]()
    gather_start()

    level, filled = bucket_ref[0], items_ref[0]
    hidden_first()
    coefl_ref[...] = levels_ref[level]
    item_blocks = jnp.where(level == 0, 2, jnp.where(level == 1, 4, 8))
    block_id = 2 * (row_id % PAIRS) + jnp.where(lane_id >= HALF, 1, 0)
    bound = jnp.where(row_id < PAIRS, filled * item_blocks, item_blocks)
    aux_ref[...] = jnp.where(block_id < bound, 1.0, 0.0)
    for i in range(8):
        modes_ref[i] = jnp.concatenate([raw_modes_ref[i], raw_modes_ref[i]], axis=1)
    gate_first()
    log_dt = row(log_dt_ref, log_dt_ref)
    sigma, step_size = 2.0 * jnp.exp(-log_dt), jnp.exp(log_dt)

    base = pl.multiple_of(dp * QUARTER, QUARTER)

    def spec_copy(which, r):
        peer = dp_peers[r]
        src, dst = ((spec_send, spec_recv), (sgrad_send.at[peer], sgrad_recv))[which]
        return remote(src, dst.at[dp], spec_ss.at[which, r - 1], spec_rs.at[which, r - 1], dp=peer)

    cauchy_coefficients(modes_ref, sigma, mcoef_ref)
    cauchy_forward(0, sigma, mcoef_ref, wave_ref, base, sums_ref, spec_send)
    inputs[0]()
    cauchy_forward(1, sigma, mcoef_ref, wave_ref, base, sums_ref, spec_send)
    cauchy_forward(2, sigma, mcoef_ref, wave_ref, base, sums_ref, spec_send)
    cauchy_forward(3, sigma, mcoef_ref, wave_ref, base, sums_ref, spec_send)
    spec_recv[dp] = spec_send[...]
    for r in range(1, 4):
        spec_copy(0, r).start()

    head[1]()
    sums = head_recv[0, 0:16, :]
    for c in range(1, N_CHAN):
        sums = sums + head_recv[c, 0:16, :]
    gate_ring.step(1)
    mean = sums[0:8] * (1.0 / MODEL_WIDTH)
    rstd = lax.rsqrt(sums[8:16] * (1.0 / MODEL_WIDTH) - mean * mean + EPSILON)

    def columns(rows):
        tall = rows.T
        return [jnp.where(low_lanes(ROWS), tall[:, j : j + 1], tall[:, 4 + j : 5 + j]) for j in range(PAIRS)]

    gain1, bias1, skip = row(gain1_ref, gain1_ref), row(bias1_ref, bias1_ref), row(skip_ref, skip_ref)
    hidden_ring.step(1)
    mean_cols, rstd_cols = columns(mean), columns(rstd)
    for j in range(PAIRS):
        hat = (tok_ref[j * ROWS : (j + 1) * ROWS, :].astype(F32) - mean_cols[j]) * rstd_cols[j]
        hat_ref[j] = hat
        norm_ref[j] = hat * gain1 + bias1

    spread_pairs(lambda j, rows: norm_ref[j, rows, :], coefl_ref, 0, tw_ref, 0, 5, rhs_ref, False)
    transform_into(sig_ref, mat_ref, 0, rhs_ref, False)

    for r in range(1, 4):
        spec_copy(0, r).wait_recv()
    for source in range(4):
        store_split(rhs_ref, source * QUARTER, 0, spec_recv[source, :QUARTER, :])
        store_split(rhs_ref, ROWS + source * QUARTER, 0, spec_recv[source, QUARTER:, :])
    gate_ring.step(2)
    hidden_ring.step(2)
    freq_ref[:, 0:256] = split_product(mat_ref, 1, rhs_ref, 0, 256)
    even = split_product(mat_ref, 2, rhs_ref, LANES, LANES)
    freq_ref[:, LANES:256] = jnp.where(low_lanes(256), freq_ref[:, LANES:256], even)
    sign = 1.0 - 2.0 * (lax.broadcasted_iota(jnp.int32, (CHUNK, LANES), 0) % 2).astype(F32)
    nyquist = step_size * column_sum(mcoef_ref[0]) * (1.0 / TOK_DEV)

    def store_taps(j, rows, values):
        taps_ref[j, rows, :] = (values + sign * nyquist) * aux_ref[4 + j : 5 + j, :]

    gather_pairs(freq_ref, coefc_ref, 160, tw_ref, 10, 2, store_taps)
    spread_pairs(lambda j, rows: taps_ref[j, rows, :], coefc_ref, 0, tw_ref, 0, 5, rhs_ref, False)
    transform_into(ans_ref, mat_ref, 0, rhs_ref, False)
    multiply_spectra(sig_ref, ans_ref, rhs_ref, False, False)
    gate_ring.step(3)
    transform_into(freq_ref, mat_ref, 1, rhs_ref, False)
    hidden_ring.step(3)

    def store_conv(j, rows, values):
        conv_ref[j, rows, :] = values
    gather_pairs(freq_ref, coefl_ref, 80, tw_ref, 0, 5, store_conv)
    for j in range(PAIRS):
        mixed = conv_ref[j] * aux_ref[j : j + 1, :] + skip * norm_ref[j]
        cumulative, density = normal_parts(mixed)
        slope_ref[j] = cumulative + mixed * density
        low, high = split_pair(mixed * cumulative)
        acts_send[2 * j] = low.astype(BF16)
        acts_send[2 * j + 1] = high.astype(BF16)
    acts_recv[chan] = acts_send[chan]
    acts = exchange(2, lambda peer: acts_send.at[peer], acts_recv)
    acts[0]()

    def joined(ref, pair, first):
        return join_pair(
            ref[2 * pair, first : first + HALF, :].astype(F32), ref[2 * pair + 1, first : first + HALF, :].astype(F32)
        )

    def lanes_of(pair):
        return slice(pair * LANES, (pair + 1) * LANES)

    def gate_lanes(pair):
        return lanes_of(pair % 2 * 2 + pair // 2)

    def core_copy(which, src, dst):
        return remote(src, dst, core_ss.at[which], core_rs.at[which], dp=sibling)

    def other_core(which, ref):
        return core_copy(which, ref.at[core], ref.at[core])

    def vector(row, first, second):
        return interleave(head_recv[first, 16 + row : 17 + row, :], head_recv[second, 16 + row : 17 + row, :])

    def both_cores(ref):
        return ref[...].reshape(2 * ROWS, MODEL_WIDTH)

    def hidden_group(offset):
        group = groups[offset]
        low, high = 2 * group, 7 - 2 * group
        bias = jnp.concatenate(
            [jnp.where(core == 0, head_recv[c, 19:20, :], head_recv[c, 20:21, :]) for c in (low, high)], axis=1
        )
        pre = dot_nn(both_cores(norm2_ref), wh_ref[0, group]) + bias
        cumulative, density = normal_parts(pre)
        hidden = (pre * cumulative).astype(BF16)
        hid_ref[group] = hidden
        grad = dot_nn(both_cores(gradf_ref), wh_ref[1, group]) * (cumulative + pre * density)
        grad = grad.astype(BF16)
        gpre_ref[group] = grad
        sums = column_sum(grad.astype(F32))
        tail_send[low, pl.ds(3 + core, 1), :] = sums[:, 0:LANES]
        tail_send[high, pl.ds(3 + core, 1), :] = sums[:, LANES : 2 * LANES]
        branch_ref[...] += dot_nt(hidden, wh_ref[1, group]).reshape(2, ROWS, MODEL_WIDTH)
        back2_ref[...] += dot_nt(grad, wh_ref[0, group]).reshape(2, ROWS, MODEL_WIDTH)

    def offset_of(turn, step):
        return TURNS[turn] * (5 - step)

    def far(offset):
        return 4 if offset == -4 else offset

    class RingBack:
        def __init__(self, which, view, base, count, ring_ref, extra):
            self.which, self.view, self.base, self.count = which, view, base, count
            self.ring_ref, self.extra = ring_ref, extra

        def copy(self, turn, step):
            slot = turn * 4 + step - 1
            half = self.count // 2
            if step == 1:
                dst = self.ring_ref.at[slot]
                lead = (slice(None),) * (len(dst.shape) - 2)
                src, dst = self.view(4, self.base + turn * half, half), dst.at[lead + (pl.ds(0, half), slice(None))]
            else:
                src, dst = self.view(offset_of(turn, step), self.base, self.count), self.ring_ref.at[slot]
            return remote(src, dst, rring_ss.at[self.which, slot], rring_rs.at[self.which, slot], chan=nexts[turn])

        def whole(self, offset):
            return self.view(offset, self.base, self.count)[...].astype(F32) + self.extra(offset)

        def step(self, step):
            half = self.count // 2
            if step == 1:
                self.view(4, self.base, self.count)[...] = self.whole(4).astype(BF16)
                for turn in range(2):
                    launch(self.copy(turn, 1))
                return
            for turn in range(2):
                offset, slot = offset_of(turn, step), turn * 4 + step - 2
                total = self.whole(offset)
                self.copy(turn, step - 1).wait_recv()
                if step == 2:
                    parts = [total[..., :half, :], total[..., half:, :]]
                    parts[turn] = parts[turn] + self.ring_ref[slot][..., :half, :].astype(F32)
                    total = jnp.concatenate(parts, axis=-2)
                else:
                    total = total + self.ring_ref[slot].astype(F32)
                self.view(offset, self.base, self.count)[...] = total.astype(BF16)
                launch(self.copy(turn, step))

        def total(self):
            total = self.whole(0)
            for turn in range(2):
                self.copy(turn, 4).wait_recv()
                total = total + self.ring_ref[turn * 4 + 3].astype(F32)
            return total

    waited = set()

    def wait_once(name, copy):
        if name not in waited:
            waited.add(name)
            copy().wait_recv()

    def gate_share():
        ref = gab_w_ref.at[:, rows_at(gate_other, 256), :]
        return remote(ref, sib_ab_ref, rsib_ss, rsib_rs, dp=sibling)

    def gate_extra(offset):
        wait_once("gates", gate_share)
        return sib_ab_ref[around[offset % 8]].astype(F32)

    def cross_copy(pair):
        src = gh_ref.at[:, groups[pair], rows_at(away_row, 256), :]
        return remote(src, cross_ref.at[pair], rdx_ss.at[pair], rdx_rs.at[pair], dp=across)

    def hidden_extra(offset):
        pair = offset % 4
        wait_once(pair, lambda: cross_copy(pair))
        return cross_ref[pair, :, :, pl.ds(group_lanes[offset % 8], LANES)].astype(F32)

    gate_g = RingBack(0, gate_view(gab_w_ref), gate_pair, 256, ring_ab_ref, gate_extra)

    hidden_g = RingBack(1, hidden_view(gh_ref), pair_row, 256, ring_h_ref, hidden_extra)

    def hidden_grads(offset):
        group = groups[offset]
        gh_ref[1, group] = dot_nn(gradf_t_ref[...], hid_ref[group]).astype(BF16)
        gh_ref[0, group] = dot_nn(norm2_t_ref[...], gpre_ref[group]).astype(BF16)
        launch(cross_copy(offset))

    def part_copy():
        return remote(part_ab_ref.at[0], part_ab_ref.at[1], rx_ss, rx_rs, dp=across)

    def last_swap():
        return remote(keep_ref.at[:, rows_at((1 - core) * ROWS, ROWS), :], swap_ref, rswap_ss, rswap_rs, dp=sibling)

    def gate_last():
        gate_total_ref[...] = gate_g.total()
        part_ab_ref[0] = gate_total_ref[rows_at((1 - lax.div(dp, 2)) * ROWS, ROWS), :].astype(BF16)
        launch(part_copy())

    def gate_finish():
        part_copy().wait_recv()
        gw_ref[:, 0:128] = gate_total_ref[rows_at(lax.div(dp, 2) * ROWS, ROWS), :] + part_ab_ref[1].astype(F32)

    def hidden_last():
        keep_ref[...] = hidden_g.total()
        launch(last_swap())
        for which in range(2):
            gw_ref[:, pl.ds(pl.multiple_of(128 + 256 * which + half_lanes, LANES), LANES)] = keep_ref[
                which, rows_at(core * ROWS, ROWS), :
            ]

    def hidden_finish():
        last_swap().wait_recv()
        for which in range(2):
            gw_ref[:, pl.ds(pl.multiple_of(128 + 256 * which + other_lanes, LANES), LANES)] = swap_ref[which]

    late = exchange(4, lambda peer: late_send.at[peer], late_recv)


    def gate_grads(*offsets):
        for offset in offsets:
            c = chan_at(offset)
            gab_w_ref[c] = dot_nn(acts_t_ref[...], gab_ref[c]).astype(BF16)
        if 0 in offsets:
            launch(gate_share())

    def late_messages():
        core_copy(3, half_send.at[1], half_recv.at[1]).wait_recv()
        for p in range(PAIRS):
            out = res_ref[p] + (branch_ref[core, :, lanes_of(p)] + half_recv[1, :, lanes_of(p)].astype(F32)) + interleave(head_recv[2 * p, 18:19, :], head_recv[2 * p + 1, 18:19, :])[0]
            low, high = split_pair(out)
            late_send[2 * p, :HALF, :] = low.astype(BF16)
            late_send[2 * p + 1, :HALF, :] = high.astype(BF16)
        for c in range(N_CHAN):
            late_send[c, ROWS:, :] = jnp.concatenate([tail_send[c], jnp.zeros((8, LANES), F32)], axis=0).astype(BF16)
        late_recv[chan] = late_send[chan]
        late[0]()

    back = exchange(3, lambda peer: back_send.at[peer], back_recv)

    inputs[1]()
    for p in range(PAIRS):
        gradf_ref[core, :, lanes_of(p)] = joined(in_recv, p, HALF).astype(BF16)
    launch(other_core(0, gradf_ref))
    gate_ring.step(4)
    gate_spread()
    gates_arrived()
    acts[1]()
    for p in range(PAIRS):
        acts_ref[:, gate_lanes(p)] = joined(acts_recv, p, 0).astype(BF16)

    total = 0.0
    for p in range(PAIRS):
        first = dot_nn(acts_ref[...], wab_ref[2 * p]) + head_recv[2 * p, 16:17, :]
        second = dot_nn(acts_ref[...], wab_ref[2 * p + 1]) + head_recv[2 * p + 1, 16:17, :]
        gate, raw = interleave(first, second)
        swish = lax.logistic(raw)
        gate_ref[p], swish_ref[p] = gate, swish
        resid = joined(in_recv, p, 0) + gate * swish
        res_ref[p] = resid
        total = total + resid
    mean2 = jnp.sum(total, axis=1, keepdims=True) * (1.0 / MODEL_WIDTH)
    total = 0.0
    for p in range(PAIRS):
        centred = res_ref[p] - mean2
        total = total + centred * centred
    rstd2 = lax.rsqrt(jnp.sum(total, axis=1, keepdims=True) * (1.0 / MODEL_WIDTH) + EPSILON)
    gain2 = []
    for p in range(PAIRS):
        gain, bias = vector(1, 2 * p, 2 * p + 1)
        gain2.append(gain)
        hat = (res_ref[p] - mean2) * rstd2
        hat2_ref[p] = hat
        norm2_ref[core, :, lanes_of(p)] = (hat * gain + bias).astype(BF16)
    launch(other_core(1, norm2_ref))
    hidden_ring.step(4)
    branch_ref[...] = jnp.zeros_like(branch_ref)
    back2_ref[...] = jnp.zeros_like(back2_ref)
    for c in range(N_CHAN):
        tail_send[c, 3:8, :] = jnp.zeros((5, LANES), F32)
    other_core(0, gradf_ref).wait_recv()
    gradf_t_ref[...] = both_cores(gradf_ref).astype(F32).T.astype(BF16)
    other_core(1, norm2_ref).wait_recv()

    hidden_arrived(2)
    hidden_group(2)
    hidden_arrived(1, 3)
    hidden_group(1)
    hidden_group(3)
    hidden_arrived(0, 4)
    hidden_group(0)
    half_send[0] = back2_ref[1 - core].astype(BF16)
    launch(core_copy(2, half_send.at[0], half_recv.at[0]))
    half_send[1] = branch_ref[1 - core].astype(BF16)
    norm2_t_ref[...] = both_cores(norm2_ref).astype(F32).T.astype(BF16)
    hidden_grads(0)
    launch(core_copy(3, half_send.at[1], half_recv.at[1]))
    core_copy(2, half_send.at[0], half_recv.at[0]).wait_recv()
    back2 = back2_ref[core] + half_recv[0].astype(F32)
    back2_ref[core] = back2

    mean_q, mean_qx = 0.0, 0.0
    for p in range(PAIRS):
        grad, hat = back2_ref[core, :, lanes_of(p)], hat2_ref[p]
        q = grad * gain2[p]
        mean_q = mean_q + q
        mean_qx = mean_qx + q * hat
        gain_grad, bias_grad = interleave(column_sum(grad * hat), column_sum(grad))
        tail_send[2 * p, 1:2, :] = gain_grad
        first, second = interleave(turn_half(column_sum(grad * hat)), turn_half(column_sum(grad)))
        tail_send[2 * p + 1, 1:2, :] = first
    acts_t_ref[...] = acts_ref[...].astype(F32).T.astype(BF16)
    mean_q = jnp.sum(mean_q, axis=1, keepdims=True) * (1.0 / MODEL_WIDTH)
    mean_qx = jnp.sum(mean_qx, axis=1, keepdims=True) * (1.0 / MODEL_WIDTH)
    for p in range(PAIRS):
        hat = hat2_ref[p]
        extra = rstd2 * (back2_ref[core, :, lanes_of(p)] * gain2[p] - mean_q - hat * mean_qx)
        grad_f = joined(in_recv, p, HALF)
        grad_resid = grad_f + extra
        gate, swish = gate_ref[p], swish_ref[p]
        grad_a = (grad_resid * swish).astype(BF16).astype(F32)
        grad_b = (grad_resid * gate * swish * (1.0 - swish)).astype(BF16).astype(F32)
        first, second = interleave(grad_a, grad_b)
        gab_ref[2 * p] = first.astype(BF16)
        gab_ref[2 * p + 1] = second.astype(BF16)
        tail_send[2 * p, 0:1, :] = column_sum(first)
        tail_send[2 * p + 1, 0:1, :] = column_sum(second)
        low, high = interleave(column_sum(grad_f), column_sum(grad_f))
        tail_send[2 * p, 2:3, :] = low
        tail_send[2 * p + 1, 2:3, :] = high
        low, high = split_pair(extra)
        late_send[2 * p, HALF:ROWS, :] = low.astype(BF16)
        late_send[2 * p + 1, HALF:ROWS, :] = high.astype(BF16)
    grad_acts = 0.0
    for c in range(N_CHAN):
        grad_acts = grad_acts + dot_nt(gab_ref[c], wab_ref[c])
    for p in range(PAIRS):
        low, high = split_pair(grad_acts[:, gate_lanes(p)])
        back_send[2 * p] = low.astype(BF16)
        back_send[2 * p + 1] = high.astype(BF16)
    hidden_grads(3)
    gate_grads(4, 3, -3)
    back_recv[chan] = back_send[chan]
    back[0]()
    hidden_grads(1)
    late_messages()

    back[1]()
    skip_grad = 0.0
    for j in range(PAIRS):
        grad = joined(back_recv, j, 0) * slope_ref[j]
        slope_ref[j] = grad
        conv_ref[j] = grad * aux_ref[j : j + 1, :]
        skip_grad = skip_grad + column_sum(grad * norm_ref[j])
    gate_grads(2, -2, 1, -1, 0)
    gate_g.step(1)
    spread_pairs(lambda j, rows: conv_ref[j, rows, :], coefl_ref, 0, tw_ref, 0, 5, rhs_ref, False)
    transform_into(freq_ref, mat_ref, 0, rhs_ref, False)
    hidden_g.step(1)
    hidden_grads(2)
    gate_g.step(2)
    multiply_spectra(sig_ref, freq_ref, rhs_ref, True)
    hidden_g.step(2)
    transform_into(sig_ref, mat_ref, 1, rhs_ref)

    def store_kernel_grad(j, rows, values):
        taps_ref[j, rows, :] = values * aux_ref[4 + j : 5 + j, :]

    gather_pairs(sig_ref, coefc_ref, 80, tw_ref, 0, 5, store_kernel_grad)
    nyquist_grad = 0.0
    for j in range(PAIRS):
        whole_sign = 1.0 - 2.0 * (lax.broadcasted_iota(jnp.int32, (ROWS, LANES), 0) % 2).astype(F32)
        nyquist_grad = nyquist_grad + column_sum(taps_ref[j] * whole_sign)
    nyquist_grad = fold(nyquist_grad) * (1.0 / TOK_DEV)
    gate_g.step(3)
    spread_pairs(lambda j, rows: taps_ref[j, rows, :], coefc_ref, 192, tw_ref, 10, 2, rhs_ref)
    taps_freq_ref[...] = split_product(mat_ref, 0, rhs_ref, 0, 256)
    even = split_product(mat_ref, 3, rhs_ref, LANES, LANES)
    taps_freq_ref[:, LANES:256] = jnp.where(low_lanes(256), taps_freq_ref[:, LANES:256], even)
    for source in range(4):
        rows = slice(source * QUARTER, (source + 1) * QUARTER)
        sgrad_send[source, :QUARTER, :] = taps_freq_ref[rows, :]
        sgrad_send[source, QUARTER:, :] = taps_freq_ref[ROWS + source * QUARTER : ROWS + (source + 1) * QUARTER, :]
    hidden_g.step(3)
    sgrad_recv[dp] = sgrad_send[dp]
    for r in range(1, 4):
        spec_copy(1, r).start()

    multiply_spectra(ans_ref, freq_ref, rhs_ref, True, False)
    transform_into(freq_ref, mat_ref, 1, rhs_ref, False)
    gather_pairs(freq_ref, coefl_ref, 80, tw_ref, 0, 5, store_conv)
    gain_grad, bias_grad = 0.0, 0.0
    scaled, crossed = [], []
    for j in range(PAIRS):
        grad = conv_ref[j] + skip * slope_ref[j]
        conv_ref[j] = grad
        gain_grad = gain_grad + column_sum(grad * hat_ref[j])
        bias_grad = bias_grad + column_sum(grad)
    conv = conv_ref[...].reshape(PAIRS * ROWS, LANES) * gain1
    for i, sums in enumerate(
        token_sums(split(conv)) + token_sums(split(conv * hat_ref[...].reshape(PAIRS * ROWS, LANES)))
    ):
        sum_send[i : i + 1, :] = sums
    late[1]()
    gate_g.step(4)
    hidden_g.step(4)
    sum_recv[chan] = sum_send[...]
    sums_back = exchange(6, lambda peer: sum_send, sum_recv)

    for r in range(1, 4):
        spec_copy(1, r).wait_recv()
    sgrad_ref[...] = sgrad_recv[0] + sgrad_recv[1] + sgrad_recv[2] + sgrad_recv[3]

    sigma_sum = point_grads(sigma, wave_ref, base, sums_ref, sgrad_ref, pgrad_ref)
    sums_back[0]()
    square_sum = mode_sums(0, jnp.zeros_like(sigma_sum), sigma, mcoef_ref, wave_ref, base, pgrad_ref, mback_ref)
    gate_last()
    square_sum = mode_sums(1, square_sum, sigma, mcoef_ref, wave_ref, base, pgrad_ref, mback_ref)
    square_sum = mode_sums(2, square_sum, sigma, mcoef_ref, wave_ref, base, pgrad_ref, mback_ref)
    square_sum = mode_sums(3, square_sum, sigma, mcoef_ref, wave_ref, base, pgrad_ref, mback_ref)
    mode_grads, dt_grad = mode_gradients(modes_ref, sigma, nyquist_grad, step_size, sigma_sum, square_sum, mback_ref)
    mask = low_lanes(32)
    for i in range(4):
        dp_send[i * 32 : (i + 1) * 32, :] = jnp.where(mask, mode_grads[i], mode_grads[i + 4])
    first = low_lanes(1)
    dp_send[128:129, :] = jnp.where(first, dt_grad, fold(skip_grad))
    dp_send[129:130, :] = jnp.where(first, fold(gain_grad), fold(bias_grad))
    dp_send[130:136, :] = jnp.zeros((6, LANES), F32)
    tail_sum = late_recv[0, ROWS:, :].astype(F32)
    for c in range(1, N_CHAN):
        tail_sum = tail_sum + late_recv[c, ROWS:, :].astype(F32)
    dp_send[136:144, :] = tail_sum[:8]
    dp_low[...] = dp_send[...].astype(BF16)

    def dp_copy(r):
        return remote(dp_low, dp_recv.at[r - 1], dp_ss.at[r - 1], dp_rs.at[r - 1], dp=dp_peers[r])

    for r in range(1, 4):
        dp_copy(r).start()
    gate_finish()
    hidden_last()

    sums_back[1]()
    sums = sum_recv[0]
    for c in range(1, N_CHAN):
        sums = sums + sum_recv[c]
    sums = sums * (1.0 / MODEL_WIDTH)
    rstd_cols, q_cols, qx_cols = columns(rstd), columns(sums[0:8]), columns(sums[8:16])
    for j in range(PAIRS):
        rows = slice(j * ROWS, (j + 1) * ROWS)
        out_ref[rows, :] = joined(late_recv, j, 0).astype(BF16)
        dtok_ref[rows, :] = joined(late_recv, j, HALF) + rstd_cols[j] * (
            conv_ref[j] * gain1 - q_cols[j] - hat_ref[j] * qx_cols[j]
        )
    for r in range(1, 4):
        dp_copy(r).wait_recv()
    hidden_finish()
    total = dp_send[...] + (dp_recv[0].astype(F32) + dp_recv[1].astype(F32) + dp_recv[2].astype(F32))
    gm_ref[...] = total[0:128]
    gv_ref[...] = total[128:144]
    for copy in pending:
        copy.wait_send()
    for group in (head, inputs, acts, back, late, sums_back):
        group[2]()
    for r in range(1, 4):
        dp_copy(r).wait_send()
        spec_copy(0, r).wait_send()
        spec_copy(1, r).wait_send()
def unpack_kernel(
    out_ref, dtok_ref, gw_ref, gm_ref, gv_ref, cotangent_ref,
    output_ref, tokens_ref, gain1_ref, bias1_ref, modes_ref, dt_ref, skip_ref, wa_ref, ba_ref, wb_ref, bb_ref,
    gain2_ref, bias2_ref, up_ref, bup_ref, down_ref, bdown_ref,
):
    for j in range(PAIRS):
        out = out_ref[j * ROWS : (j + 1) * ROWS, :].astype(F32).T.astype(BF16)
        grad = dtok_ref[j * ROWS : (j + 1) * ROWS, :].T
        for h in range(2):
            lanes, rows = slice((2 * j + h) * ROWS, (2 * j + h + 1) * ROWS), slice(h * HALF, (h + 1) * HALF)
            output_ref[:, lanes] = out[rows]
            tokens_ref[:, lanes] = cotangent_ref[:, lanes] + grad[rows]
    for i in range(8):
        modes_ref[i] = gm_ref[i % 4 * 32 : i % 4 * 32 + 32, i // 4 * HALF : (i // 4 + 1) * HALF]
    gates = gw_ref[:, :LANES].T
    wa_ref[...] = gates[:HALF]
    wb_ref[...] = gates[HALF:]
    up_ref[...] = gw_ref[:, 128:384]
    down_ref[...] = gw_ref[:, 384:640].T
    for at, low, high in (
        (0, dt_ref, skip_ref), (1, gain1_ref, bias1_ref), (8, ba_ref, bb_ref), (9, gain2_ref, bias2_ref),
    ):
        low[...] = gv_ref[at, :HALF]
        high[...] = gv_ref[at, HALF:]
    bdown_ref[...] = gv_ref[10, :HALF]
    bup_ref[:LANES] = gv_ref[11, :]
    bup_ref[LANES:] = gv_ref[12, :]


def block_program():
    mats, twiddle, levels, constant, wave = mixer_tables()

    def run(tokens, cotangent, bucket, items, gain1, bias1, modes, log_dt, skip, w_a, b_a, w_b, b_b, gain2, bias2, w_up, b_up, w_down, b_down):
        vmem = pl.BlockSpec(memory_space=pltpu.VMEM)
        smem = pl.BlockSpec(memory_space=pltpu.SMEM)
        dma = pltpu.SemaphoreType.DMA

        def buf(*shape):
            return pltpu.VMEM(shape, F32)

        def low(*shape):
            return pltpu.VMEM(shape, BF16)

        def full(*shape):
            return jax.ShapeDtypeStruct(shape, F32)

        big, wide = (PAIRS, ROWS, LANES), (256, WIDE)
        packed = pl.pallas_call(
            block_kernel,
            out_shape=(
                jax.ShapeDtypeStruct((512, LANES), BF16), full(512, LANES), full(ROWS, WIDE), full(ROWS, LANES),
                full(16, LANES),
            ),
            in_specs=[smem] * 2 + [vmem] * 22,
            out_specs=(vmem,) * 5,
            scratch_shapes=[
                low(512, LANES), buf(8, LANES), buf(160, LANES), buf(8, 32, LANES),
                low(N_CHAN, 512, 128), low(2, 4, 512, 256), low(N_CHAN, 512, 128), low(2, 4, 512, 256),
                low(2, ROWS, LANES), low(N_CHAN, 256, LANES), low(8, 256, LANES), low(8, 2, 256, LANES), low(2, ROWS, LANES),
                low(4, 2, 256, 256), buf(2, 256, LANES), buf(2, ROWS, LANES), buf(256, LANES),
                low(N_CHAN, ROWS, LANES), low(N_CHAN, ROWS, LANES), buf(24, LANES), buf(N_CHAN, 24, LANES),
                low(N_CHAN, HALF, LANES), low(N_CHAN, HALF, LANES), low(N_CHAN, HALF, LANES), low(N_CHAN, HALF, LANES),
                low(N_CHAN, 144, LANES), low(N_CHAN, 144, LANES),
                buf(16, LANES), buf(N_CHAN, 16, LANES), buf(N_CHAN, 8, LANES),
                buf(144, LANES), low(144, LANES), low(3, 144, LANES), buf(64, 256), buf(4, 64, 256), buf(4, 64, 256), buf(4, 64, 256),
                buf(*big), buf(*big), buf(*big), buf(*big), low(2, *wide), buf(*wide), buf(*wide), buf(*wide), buf(*big),
                buf(10, 32, LANES), buf(2, 16, QUARTER, LANES), buf(2, 16, QUARTER, LANES), buf(10, 32, LANES),
                buf(64, 256), buf(256, 256),
                buf(*big), buf(*big), buf(*big), buf(*big), low(ROWS, 512), low(2, ROWS, 512), low(2, ROWS, 512),
                buf(2, ROWS, 512), buf(2, ROWS, 512), low(2, ROWS, 512), low(2, ROWS, 512),
                low(N_CHAN, ROWS, LANES), low(4, 256, 256), low(4, 256, 256), low(512, ROWS), low(512, 256), low(512, 256),
                dma((2, 8)), dma((2, 8)), dma, dma, dma, dma, dma((9,)), dma((9,)), dma, dma, dma((4,)), dma((4,)),
                dma((2, 8)), dma((2, 8)), dma, dma, dma, dma, dma((4,)), dma((4,)), dma, dma,
                dma((7, 7)), dma((7, 7)), dma((3,)), dma((3,)), dma((2, 3)), dma((2, 3)),
            ],
            compiler_params=pltpu.CompilerParams(
                collective_id=0, has_side_effects=True, vmem_limit_bytes=60 * 1024 * 1024
            ),
            name="block",
        )(
            bucket, items, tokens.T, cotangent.T, gain1, bias1, jnp.swapaxes(modes, 1, 2), log_dt, skip,
            w_a.T, b_a, w_b.T, b_b, gain2, bias2,
            w_up, b_up, w_down, b_down, levels, constant, mats, twiddle, wave,
        )
        small = full(HALF)
        results = pl.pallas_call(
            unpack_kernel,
            out_shape=(
                jax.ShapeDtypeStruct((HALF, TOK_DEV), BF16), full(HALF, TOK_DEV), small, small, full(8, 32, HALF),
                small, small, full(HALF, ROWS), small, full(HALF, ROWS), small, small, small, full(ROWS, 256),
                full(256), full(256, ROWS), small,
            ),
            in_specs=[vmem] * 6,
            out_specs=(vmem,) * 17,
            name="unpack",
        )(*packed, cotangent.T)
        turned = {0, 1, 4, 7, 9}
        return tuple(jnp.swapaxes(r, -1, -2) if i in turned else r for i, r in enumerate(results))

    return run


def solution(mesh):
    small = mesh.shape["chan"] == N_CHAN and mesh.shape["dp"] == 4
    return jax.shard_map(
        block_program() if small else shards,
        mesh=mesh,
        in_specs=(
            P("dp", "chan"),
            P("dp", "chan"),
            P("dp"),
            P("dp"),
            P("chan"),
            P("chan"),
            P(None, "chan", None),
            P("chan"),
            P("chan"),
            P("dp", "chan"),
            P("chan"),
            P("dp", "chan"),
            P("chan"),
            P("chan"),
            P("chan"),
            P("dp", "chan"),
            P("chan"),
            P("chan", "dp"),
            P("chan"),
        ),
        out_specs=(
            P("dp", "chan"),
            P("dp", "chan"),
            P("chan"),
            P("chan"),
            P(None, "chan", None),
            P("chan"),
            P("chan"),
            P("dp", "chan"),
            P("chan"),
            P("dp", "chan"),
            P("chan"),
            P("chan"),
            P("chan"),
            P("dp", "chan"),
            P("chan"),
            P("chan", "dp"),
            P("chan"),
        ),
        check_vma=False,
    )
```

```python
import math

import jax
import jax.numpy as jnp
import ml_dtypes
import numpy as np
from jax import lax
from jax.experimental import pallas as pl
from jax.experimental.pallas import tpu as pltpu
from jax.sharding import PartitionSpec as P

MODEL_WIDTH = 512
TOK_DEV = 1024


HIGHEST = lax.Precision.HIGHEST
EPSILON = 1e-05


def product(left, right):
    return jnp.dot(left, right, preferred_element_type=jnp.float32)


def product_nt(left, right):
    return lax.dot_general(
        left, right, (((1,), (1,)), ((), ())), preferred_element_type=jnp.float32
    )


def product_tn(left, right):
    return lax.dot_general(
        left, right, (((0,), (0,)), ((), ())), preferred_element_type=jnp.float32
    )


def gelu_slope(values):
    return (
        0.5 * (1.0 + lax.erf(values * 0.7071067811865476))
        + values * jnp.exp(-0.5 * values * values) * 0.3989422804014327
    )


def half_angles(length):
    angle = np.arange(length // 2 + 1, dtype=np.float64) * (math.pi / length)
    cosine, sine = np.cos(angle), np.sin(angle)
    cosine[-1] = 0.0
    return cosine.astype(np.float32), sine.astype(np.float32)


def inverse_tables(length):
    freq = np.arange(length // 2 + 1)
    turn = (freq[:, None] * np.arange(length)[None, :]) % length * (2.0 * math.pi / length)
    weight = np.where((freq == 0) | (freq == length // 2), 1.0, 2.0)[:, None] / length
    return (weight * np.cos(turn)).astype(np.float32), (weight * np.sin(turn)).astype(np.float32)


def high_einsum(form, left, right):
    return jnp.einsum(form, left, right, precision=HIGHEST)


def ssm_kernel(modes, log_dt):
    cos_h, sin_h = half_angles(TOK_DEV)
    index = jnp.arange(modes.shape[2], dtype=jnp.int32).astype(jnp.float32)
    lam_re = -0.5 * jnp.exp(modes[0])
    lam_im = math.pi * (index + modes[1])
    rank_re, rank_im, in_re, in_im, out_re, out_im = (modes[i] for i in range(2, 8))
    sigma = (2.0 * jnp.exp(-log_dt))[:, None]

    def points(values):
        return values.T[:, None, :]

    den_re = points(lam_re * lam_re + lam_im * lam_im) * (cos_h * cos_h)[:, None] - (
        sigma * sigma
    ).T * (sin_h * sin_h)[:, None]
    den_im = points(-2.0 * sigma * lam_re) * (sin_h * cos_h)[:, None]
    den_sq = den_re * den_re + den_im * den_im
    inv_re = den_re / den_sq
    inv_im = -den_im / den_sq
    sums = []
    for real, imag in (
        (out_re * in_re + out_im * in_im, out_re * in_im - out_im * in_re),
        (out_re * rank_re + out_im * rank_im, out_re * rank_im - out_im * rank_re),
        (rank_re * in_re + rank_im * in_im, rank_re * in_im - rank_im * in_re),
        (rank_re * rank_re + rank_im * rank_im, jnp.zeros_like(rank_re)),
    ):
        turned = points(real * lam_re + imag * lam_im)
        real = points(real)
        p_re, p_im = jnp.sum(real * inv_re, axis=0), jnp.sum(real * inv_im, axis=0)
        q_re, q_im = jnp.sum(turned * inv_re, axis=0), jnp.sum(turned * inv_im, axis=0)
        sine = sin_h[:, None] * sigma.T
        sums.append((-sine * p_im - cos_h[:, None] * q_re, sine * p_re - cos_h[:, None] * q_im))
    (cross_re, cross_im), (left_re, left_im), (right_re, right_im), (self_re, self_im) = sums
    twice = 2.0 * cos_h[:, None]
    loop_re, loop_im = 1.0 + twice * self_re, twice * self_im
    back_re, back_im = twice * right_re, twice * right_im
    loop_sq = loop_re * loop_re + loop_im * loop_im
    ratio_re = (back_re * loop_re + back_im * loop_im) / loop_sq
    ratio_im = (back_im * loop_re - back_re * loop_im) / loop_sq
    part_re = cross_re - (left_re * ratio_re - left_im * ratio_im)
    part_im = cross_im - (left_re * ratio_im + left_im * ratio_re)
    spec_re = 2.0 * (cos_h[:, None] * part_re - sin_h[:, None] * part_im)
    spec_im = 2.0 * (cos_h[:, None] * part_im + sin_h[:, None] * part_re)
    cos_tab, sin_tab = inverse_tables(TOK_DEV)
    return high_einsum("kl,kc->lc", cos_tab, spec_re) - high_einsum("kl,kc->lc", sin_tab, spec_im)


BLOCK = 128
BLOCKS = TOK_DEV // BLOCK
FIRST = 2 * BLOCKS
KEPT = FIRST // 2 + 1


def transform_tables():
    length = 2 * TOK_DEV
    turn = np.arange(KEPT)[:, None] * np.arange(BLOCK)[None, :] * (2.0 * math.pi / length)
    small = np.arange(BLOCK)[:, None] * np.arange(BLOCK)[None, :] % BLOCK * (2.0 * math.pi / BLOCK)
    spots = np.stack([np.arange(BLOCKS) + np.arange(BLOCKS) // (2 << b) * (2 << b) for b in range(3)])
    angle = spots[:, None, :] * np.arange(KEPT)[None, :, None] % FIRST * (2.0 * math.pi / FIRST)
    parts = (np.cos(turn), np.sin(turn), np.cos(small), np.sin(small), np.cos(angle), np.sin(angle))
    return [part.astype(np.float32) for part in parts]


def forward_transform(blocks, cos_a, sin_a):
    cos_t, sin_t, cos_s, sin_s, _, _ = transform_tables()
    step_re = high_einsum("ka,abc->kbc", cos_a, blocks)
    step_im = -high_einsum("ka,abc->kbc", sin_a, blocks)
    turned_re = step_re * cos_t[..., None] + step_im * sin_t[..., None]
    turned_im = step_im * cos_t[..., None] - step_re * sin_t[..., None]
    both = jnp.concatenate([turned_re, turned_im], axis=1)
    matrix = np.block([[cos_s, sin_s], [-sin_s, cos_s]])
    return high_einsum("pb,kbc->kpc", matrix, both)


def inverse_transform(spectrum, cos_a, sin_a):
    cos_t, sin_t, cos_s, sin_s, _, _ = transform_tables()
    matrix = np.block([[cos_s, -sin_s], [sin_s, cos_s]])
    both = high_einsum("bp,kpc->kbc", matrix, spectrum)
    step_re, step_im = both[:, :BLOCK], both[:, BLOCK:]
    turned_re = step_re * cos_t[..., None] - step_im * sin_t[..., None]
    turned_im = step_im * cos_t[..., None] + step_re * sin_t[..., None]
    weight = np.where(np.arange(KEPT) % (KEPT - 1) == 0, 1.0, 2.0).astype(np.float32) / (2 * TOK_DEV)
    return high_einsum("ka,kbc->abc", cos_a * weight[:, None], turned_re) - high_einsum(
        "ka,kbc->abc", sin_a * weight[:, None], turned_im
    )


def multiply(left, right):
    left_re, left_im = left[:, :BLOCK], left[:, BLOCK:]
    right_re, right_im = right[:, :BLOCK], right[:, BLOCK:]
    return jnp.concatenate(
        [left_re * right_re - left_im * right_im, left_re * right_im + left_im * right_re], axis=1
    )


def mixer(normed, kernel_taps, skip_gain, bucket, filled):
    _, _, _, _, cos_a, sin_a = transform_tables()
    cos_x, sin_x = jnp.asarray(cos_a)[bucket], jnp.asarray(sin_a)[bucket]
    item_blocks = 2 << bucket
    block_id = jnp.arange(BLOCKS, dtype=jnp.int32)[:, None, None]
    taps = jnp.where(block_id < item_blocks, kernel_taps.reshape(BLOCKS, BLOCK, -1), 0.0)
    signal = forward_transform(normed.reshape(BLOCKS, BLOCK, -1), cos_x, sin_x)
    answer = forward_transform(taps, cos_a[2], sin_a[2])
    result = inverse_transform(multiply(signal, answer), cos_x, sin_x)
    result = jnp.where(block_id < filled * item_blocks, result, 0.0)
    return result.reshape(normed.shape) + skip_gain * normed


def shards(
    tokens,
    cotangent,
    group_bucket,
    group_items,
    first_norm_gain,
    first_norm_bias,
    modes,
    log_dt,
    d_skip,
    w_a,
    b_a,
    w_b,
    b_b,
    second_norm_gain,
    second_norm_bias,
    w_up,
    b_up,
    w_down,
    b_down,
):
    input_tokens = tokens.astype(jnp.float32)
    sums_in = lax.psum(
        (jnp.sum(input_tokens, axis=1), jnp.sum(input_tokens * input_tokens, axis=1)), "chan"
    )
    input_average = sums_in[0][:, None] / MODEL_WIDTH
    input_inverse_deviation = lax.rsqrt(
        sums_in[1][:, None] / MODEL_WIDTH - input_average * input_average + EPSILON
    )
    input_standardized = (input_tokens - input_average) * input_inverse_deviation
    input_normalized = input_standardized * first_norm_gain + first_norm_bias
    level = group_bucket[0]
    filled = group_items[0]
    kernel_taps, kernel_back = jax.vjp(ssm_kernel, modes, log_dt)

    def local_mix(values, taps_now, skip_gain):
        return mixer(values, taps_now, skip_gain, level, filled)

    mixed, mix_back = jax.vjp(local_mix, input_normalized, kernel_taps, d_skip)
    acts_low = jax.nn.gelu(mixed, approximate=False).astype(jnp.bfloat16)
    wa_full, wb_full, up_full, down_full = (
        lax.all_gather(w_a.astype(jnp.bfloat16), "dp", axis=0, tiled=True),
        lax.all_gather(w_b.astype(jnp.bfloat16), "dp", axis=0, tiled=True),
        lax.all_gather(w_up.astype(jnp.bfloat16), "dp", axis=0, tiled=True),
        lax.all_gather(w_down.astype(jnp.bfloat16), "dp", axis=1, tiled=True),
    )
    acts_full = lax.all_gather(acts_low, "chan", axis=1, tiled=True)
    gate_a = product(acts_full, wa_full) + b_a
    gate_b = product(acts_full, wb_full) + b_b
    gate_sig = jax.nn.sigmoid(gate_b)
    residual_stream = input_tokens + gate_a * gate_sig
    sums_mid = lax.psum(
        (jnp.sum(residual_stream, axis=1), jnp.sum(residual_stream * residual_stream, axis=1)),
        "chan",
    )
    middle_average = sums_mid[0][:, None] / MODEL_WIDTH
    middle_inverse_deviation = lax.rsqrt(
        sums_mid[1][:, None] / MODEL_WIDTH - middle_average * middle_average + EPSILON
    )
    middle_standardized = (residual_stream - middle_average) * middle_inverse_deviation
    middle_reduced = (middle_standardized * second_norm_gain + second_norm_bias).astype(
        jnp.bfloat16
    )
    mid_full = lax.all_gather(middle_reduced, "chan", axis=1, tiled=True)
    pre_act = product(mid_full, up_full) + b_up
    hidden_low = jax.nn.gelu(pre_act, approximate=False).astype(jnp.bfloat16)
    branch = (
        lax.psum_scatter(product(hidden_low, down_full), "chan", scatter_dimension=1, tiled=True)
        + b_down
    )
    output = (residual_stream + branch).astype(jnp.bfloat16)
    grad_f = cotangent.astype(jnp.bfloat16)
    grad_b_down = jnp.sum(grad_f.astype(jnp.float32), axis=0)
    grad_f_full = lax.all_gather(grad_f, "chan", axis=1, tiled=True)
    grad_w_down = product_tn(hidden_low, grad_f_full)
    grad_pre = (product_nt(grad_f_full, down_full) * gelu_slope(pre_act)).astype(jnp.bfloat16)
    grad_b_up = jnp.sum(grad_pre.astype(jnp.float32), axis=0)
    grad_w_up = product_tn(mid_full, grad_pre)
    middle_gradient = lax.psum_scatter(
        product_nt(grad_pre, up_full), "chan", scatter_dimension=1, tiled=True
    )
    second_norm_gain_gradient = jnp.sum(middle_gradient * middle_standardized, axis=0)
    grad_ln2_bias = jnp.sum(middle_gradient, axis=0)
    middle_rescaled = middle_gradient * second_norm_gain
    middle_backward = lax.psum(
        (jnp.sum(middle_rescaled, axis=1), jnp.sum(middle_rescaled * middle_standardized, axis=1)),
        "chan",
    )
    grad_resid = cotangent + middle_inverse_deviation * (
        middle_rescaled
        - middle_backward[0][:, None] / MODEL_WIDTH
        - middle_standardized * middle_backward[1][:, None] / MODEL_WIDTH
    )
    grad_a = (grad_resid * gate_sig).astype(jnp.bfloat16)
    grad_b = (grad_resid * gate_a * gate_sig * (1.0 - gate_sig)).astype(jnp.bfloat16)
    grad_b_a = jnp.sum(grad_a.astype(jnp.float32), axis=0)
    grad_b_b = jnp.sum(grad_b.astype(jnp.float32), axis=0)
    grad_w_a = product_tn(acts_full, grad_a)
    grad_w_b = product_tn(acts_full, grad_b)
    grad_acts = lax.psum_scatter(
        product_nt(grad_a, wa_full) + product_nt(grad_b, wb_full),
        "chan",
        scatter_dimension=1,
        tiled=True,
    )
    grad_mixed = grad_acts * gelu_slope(mixed)
    normalized_gradient, grad_kernel, grad_skip = mix_back(grad_mixed)
    grad_modes, grad_log_dt = kernel_back(grad_kernel)
    first_norm_gain_gradient = jnp.sum(normalized_gradient * input_standardized, axis=0)
    grad_ln1_bias = jnp.sum(normalized_gradient, axis=0)
    input_rescaled = normalized_gradient * first_norm_gain
    input_backward = lax.psum(
        (jnp.sum(input_rescaled, axis=1), jnp.sum(input_rescaled * input_standardized, axis=1)),
        "chan",
    )
    grad_tokens = grad_resid + input_inverse_deviation * (
        input_rescaled
        - input_backward[0][:, None] / MODEL_WIDTH
        - input_standardized * input_backward[1][:, None] / MODEL_WIDTH
    )
    grad_w_a, grad_w_b, grad_w_up, grad_w_down = (
        lax.psum_scatter(grad_w_a, "dp", scatter_dimension=0, tiled=True),
        lax.psum_scatter(grad_w_b, "dp", scatter_dimension=0, tiled=True),
        lax.psum_scatter(grad_w_up, "dp", scatter_dimension=0, tiled=True),
        lax.psum_scatter(grad_w_down, "dp", scatter_dimension=1, tiled=True),
    )
    (
        first_norm_gain_gradient,
        grad_ln1_bias,
        grad_modes,
        grad_log_dt,
        grad_skip,
        grad_b_a,
        grad_b_b,
        second_norm_gain_gradient,
        grad_ln2_bias,
        grad_b_up,
        grad_b_down,
    ) = lax.psum(
        (
            first_norm_gain_gradient,
            grad_ln1_bias,
            grad_modes,
            grad_log_dt,
            grad_skip,
            grad_b_a,
            grad_b_b,
            second_norm_gain_gradient,
            grad_ln2_bias,
            grad_b_up,
            grad_b_down,
        ),
        "dp",
    )
    return (
        output,
        grad_tokens,
        first_norm_gain_gradient,
        grad_ln1_bias,
        grad_modes,
        grad_log_dt,
        grad_skip,
        grad_w_a,
        grad_b_a,
        grad_w_b,
        grad_b_b,
        second_norm_gain_gradient,
        grad_ln2_bias,
        grad_w_up,
        grad_b_up,
        grad_w_down,
        grad_b_down,
    )


LANES = 128
HALF = 64
PAIRS = 4
ROWS = 128
N_CHAN = 8
WIDE = 640
MESH = pl.DeviceIdType.MESH
F32 = jnp.float32
BF16 = jnp.bfloat16


def split_two(matrix):
    high = matrix.astype(ml_dtypes.bfloat16)
    low = (matrix - high.astype(np.float64)).astype(ml_dtypes.bfloat16)
    return np.concatenate([high, low], axis=1)


def lane_rows(values_low, values_high):
    return np.repeat(np.stack([values_low, values_high], -1), HALF, axis=-1)


def mixer_tables():
    line = np.arange(ROWS)
    small = np.outer(line, line) % ROWS * (2.0 * math.pi / ROWS)
    cos_s, sin_s = np.cos(small), np.sin(small)
    forward = np.block([[cos_s, sin_s], [-sin_s, cos_s]])
    real = np.zeros((2 * ROWS, 2 * ROWS))
    for row in range(HALF):
        weight = 1.0 if row == 0 else 2.0
        turn = 2.0 * math.pi / ROWS * row * line
        real[:ROWS, row] = weight * np.cos(turn)
        real[:ROWS, ROWS + row] = -weight * np.sin(turn)
        turn = 2.0 * math.pi / TOK_DEV * (4 + 8 * row) * line
        real[ROWS:, HALF + row] = 2.0 * np.cos(turn)
        real[ROWS:, ROWS + HALF + row] = -2.0 * np.sin(turn)
    mats = np.stack([split_two(m) for m in (forward, forward.T, real, real.T)])

    twiddle = []
    for pair in range(5):
        turn = np.stack([line * k * (math.pi / TOK_DEV) for k in (2 * pair, 2 * pair + 1)])
        twiddle += [lane_rows(np.cos(turn[0]), np.cos(turn[1])), lane_rows(np.sin(turn[0]), np.sin(turn[1]))]
    for first, second in ((1, 2), (3, 0)):
        turn = np.stack([line * k * (2.0 * math.pi / TOK_DEV) for k in (first, second)])
        twiddle += [lane_rows(np.cos(turn[0]), np.cos(turn[1])), lane_rows(np.sin(turn[0]), np.sin(turn[1]))]

    def forward_rows(coef, pairs):
        out = []
        for low, high in pairs:
            for part in range(2):
                for j in range(PAIRS):
                    out.append(lane_rows(coef(2 * j, low, part), coef(2 * j + 1, high, part)))
                for j in range(PAIRS):
                    out.append(lane_rows(coef(2 * j, high, part), coef(2 * j + 1, low, part)))
        return np.stack(out)

    def inverse_rows(coef, pairs):
        out = []
        for low, high in pairs:
            for part in range(2):
                for j in range(PAIRS):
                    out.append(lane_rows(coef(2 * j, low, part), coef(2 * j + 1, high, part)))
                for j in range(PAIRS):
                    out.append(lane_rows(coef(2 * j + 1, low, part), coef(2 * j, high, part)))
        return np.stack(out)

    levels = []
    pairs = [(2 * p, 2 * p + 1) for p in range(5)]
    for level in range(3):
        item = 2 << level

        def angle(block, k):
            return 2.0 * math.pi / 16 * ((block + block // item * item) * k % 16)

        def fwd(block, k, part):
            if k > 8:
                return np.zeros(())
            return np.cos(angle(block, k)) if part == 0 else -np.sin(angle(block, k))

        def inv(block, k, part):
            weight = (1.0 if k in (0, 8) else 2.0) / (2 * TOK_DEV)
            return weight * fwd(block, k, part)

        levels.append(np.concatenate([forward_rows(fwd, pairs), inverse_rows(inv, pairs)]))

    def taps(block, k, part):
        if k == 0:
            return np.asarray((1.0 if part == 0 else (-1.0) ** block) / TOK_DEV)
        turn = 2.0 * math.pi / 8 * (block * k % 8)
        return np.asarray((np.cos(turn) if part == 0 else -np.sin(turn)) * 2.0 / TOK_DEV)

    tap_pairs = [(1, 2), (3, 0)]
    taps_back = forward_rows(taps, tap_pairs)
    taps_rows = inverse_rows(taps, tap_pairs)
    freq_even = np.where(line < HALF, 8 * line, 4 + 8 * (line - HALF))
    half_angle = np.stack(
        [lane_rows(1 + 8 * line, 2 + 8 * line), lane_rows(3 + 8 * line, freq_even)]
    ) * (math.pi / TOK_DEV)
    wave = np.stack([np.cos(half_angle), np.sin(half_angle)])
    return (
        mats,
        np.stack(twiddle).astype(np.float32),
        np.stack(levels).astype(np.float32),
        np.concatenate([levels[2], taps_rows, taps_back]).astype(np.float32),
        wave.astype(np.float32),
    )


def low_lanes(rows):
    return lax.broadcasted_iota(jnp.int32, (rows, LANES), 1) < HALF


def turn_half(values):
    return pltpu.roll(values, HALF, 1)


def split_pair(values):
    upper, lower = values[:HALF], values[HALF:]
    mask = low_lanes(HALF)
    return jnp.where(mask, upper, turn_half(lower)), jnp.where(mask, turn_half(upper), lower)


def join_pair(first, second):
    mask = low_lanes(HALF)
    return jnp.concatenate(
        [jnp.where(mask, first, turn_half(second)), jnp.where(mask, turn_half(first), second)], axis=0
    )


def interleave(first, second):
    mask = low_lanes(first.shape[0])
    return jnp.where(mask, first, turn_half(second)), jnp.where(mask, turn_half(first), second)


def fold(values):
    return values + turn_half(values)


def reciprocal(values):
    guess = pl.reciprocal(values, approx=True)
    return guess * (2.0 - values * guess)


ERF_TERMS = (1.061405429, -1.453152027, 1.421413741, -0.284496736, 0.254829592)


def normal_parts(values):
    bell = jnp.exp(-0.5 * values * values)
    t = reciprocal(1.0 + (0.3275911 * 0.7071067811865476) * jnp.abs(values))
    tail = ERF_TERMS[0]
    for term in ERF_TERMS[1:]:
        tail = tail * t + term
    tail = 0.5 * (tail * t) * bell
    return jnp.where(values < 0.0, tail, 1.0 - tail), bell * 0.3989422804014327


def column_sum(values):
    return jnp.sum(values, axis=0, keepdims=True)


def dot_nt(left, right):
    return lax.dot_general(left, right, (((1,), (1,)), ((), ())), preferred_element_type=F32)


def dot_nn(left, right):
    return jnp.dot(left, right, preferred_element_type=F32)


def store_split(ref, row, lane, values, exact=True):
    high = values.astype(BF16)
    place = (pl.ds(row, values.shape[0]), pl.ds(lane, values.shape[1]))
    ref[(0,) + place] = high
    if exact:
        ref[(1,) + place] = (values - high.astype(F32)).astype(BF16)


def split_product(mat_ref, which, rhs_ref, lane, width, exact=True):
    high = mat_ref[which, :, 0:256]
    low = mat_ref[which, :, 256:512]
    rhs_high = rhs_ref[0, :, lane : lane + width]
    product = dot_nn(high, rhs_high) + dot_nn(low, rhs_high)
    if exact:
        product = product + dot_nn(high, rhs_ref[1, :, lane : lane + width])
    return product


CHUNK = 32


def over_chunks(body, size=CHUNK, first=0, rows=ROWS):
    def step(index, carry):
        body(pl.multiple_of(first + index * size, size))
        return carry

    lax.fori_loop(0, rows // size, step, 0)


def spread_pairs(src, coef_ref, base, twiddle_ref, twiddle_base, pairs, rhs_ref, exact=True):
    def body(row):
        rows = pl.ds(row, CHUNK)
        blocks = [src(j, rows) for j in range(PAIRS)]
        for pair in range(pairs):
            parts = []
            for part in range(2):
                at = base + (pair * 2 + part) * 8
                straight = sum(blocks[j] * coef_ref[at + j : at + j + 1, :] for j in range(PAIRS))
                crossed = sum(blocks[j] * coef_ref[at + 4 + j : at + 5 + j, :] for j in range(PAIRS))
                parts.append(straight + turn_half(crossed))
            cosine = twiddle_ref[twiddle_base + 2 * pair, rows, :]
            sine = twiddle_ref[twiddle_base + 2 * pair + 1, rows, :]
            store_split(rhs_ref, row, pair * LANES, parts[0] * cosine + parts[1] * sine, exact)
            store_split(rhs_ref, row + ROWS, pair * LANES, parts[1] * cosine - parts[0] * sine, exact)

    over_chunks(body)


def gather_pairs(values_ref, coef_ref, base, twiddle_ref, twiddle_base, pairs, store):
    def body(row):
        rows = pl.ds(row, CHUNK)
        straight, crossed = [0.0] * PAIRS, [0.0] * PAIRS
        for pair in range(pairs):
            lanes = slice(pair * LANES, (pair + 1) * LANES)
            real, imag = values_ref[rows, lanes], values_ref[pl.ds(row + ROWS, CHUNK), lanes]
            cosine = twiddle_ref[twiddle_base + 2 * pair, rows, :]
            sine = twiddle_ref[twiddle_base + 2 * pair + 1, rows, :]
            for part, value in enumerate((real * cosine - imag * sine, imag * cosine + real * sine)):
                at = base + (pair * 2 + part) * 8
                for j in range(PAIRS):
                    straight[j] = straight[j] + value * coef_ref[at + j : at + j + 1, :]
                    crossed[j] = crossed[j] + value * coef_ref[at + 4 + j : at + 5 + j, :]
        for j in range(PAIRS):
            store(j, rows, straight[j] + turn_half(crossed[j]))

    over_chunks(body)


GROUPS = ((0, 256), (256, 256), (512, 128))


def transform_into(dst_ref, mat_ref, which, rhs_ref, exact=True):
    for lane, width in GROUPS:
        dst_ref[:, lane : lane + width] = split_product(mat_ref, which, rhs_ref, lane, width, exact)


def multiply_spectra(left_ref, right_ref, rhs_ref, conjugate, exact=True):
    def body(row):
        top, bottom = pl.ds(row, CHUNK), pl.ds(row + ROWS, CHUNK)
        for pair in range(5):
            lanes = slice(pair * LANES, (pair + 1) * LANES)
            a_re, a_im = left_ref[top, lanes], left_ref[bottom, lanes]
            b_re, b_im = right_ref[top, lanes], right_ref[bottom, lanes]
            if conjugate:
                out_re, out_im = a_re * b_re + a_im * b_im, a_re * b_im - a_im * b_re
            else:
                out_re, out_im = a_re * b_re - a_im * b_im, a_re * b_im + a_im * b_re
            store_split(rhs_ref, row, pair * LANES, out_re, exact)
            store_split(rhs_ref, row + ROWS, pair * LANES, out_im, exact)

    over_chunks(body)


def pair_terms(modes_ref):
    rank_re, rank_im, in_re, in_im, out_re, out_im = (modes_ref[i] for i in range(2, 8))
    return (
        (out_re * in_re + out_im * in_im, out_re * in_im - out_im * in_re),
        (out_re * rank_re + out_im * rank_im, out_re * rank_im - out_im * rank_re),
        (rank_re * in_re + rank_im * in_im, rank_re * in_im - rank_im * in_re),
        (rank_re * rank_re + rank_im * rank_im, None),
    )


def mode_values(modes_ref):
    index = lax.broadcasted_iota(jnp.int32, modes_ref.shape[1:], 0).astype(F32)
    return -0.5 * jnp.exp(modes_ref[0]), math.pi * (index + modes_ref[1])


POINT_ROWS = 16


def resolvent(coef_ref, n, square_cos, cos_sin, scaled):
    den_re = coef_ref[8, pl.ds(n, 1), :] * square_cos - scaled
    den_im = coef_ref[9, pl.ds(n, 1), :] * cos_sin
    inverse = reciprocal(den_re * den_re + den_im * den_im)
    return den_re * inverse, -(den_im * inverse)


def complex_multiply(a_re, a_im, b_re, b_im):
    return a_re * b_re - a_im * b_im, a_re * b_im + a_im * b_re


def conj_multiply(a_re, a_im, b_re, b_im):
    return a_re * b_re + a_im * b_im, a_re * b_im - a_im * b_re


def combine(sums, sigma, cosine, sine):
    terms = []
    for p_re, p_im, q_re, q_im in (sums[4 * q : 4 * q + 4] for q in range(4)):
        swing = sigma * sine
        terms.append((-swing * p_im - cosine * q_re, swing * p_re - cosine * q_im))
    twice = 2.0 * cosine
    loop_re, loop_im = 1.0 + twice * terms[3][0], twice * terms[3][1]
    scale = reciprocal(loop_re * loop_re + loop_im * loop_im)
    inv = (loop_re * scale, -(loop_im * scale))
    ratio = complex_multiply(twice * terms[2][0], twice * terms[2][1], *inv)
    return terms, inv, ratio


QUARTER = 32


def cauchy_coefficients(modes_ref, sigma, coef_ref):
    lam_re, lam_im = mode_values(modes_ref)
    for q, (real, imag) in enumerate(pair_terms(modes_ref)):
        coef_ref[q] = real
        coef_ref[4 + q] = real * lam_re if imag is None else real * lam_re + imag * lam_im
    coef_ref[8] = lam_re * lam_re + lam_im * lam_im
    coef_ref[9] = -2.0 * sigma * lam_re


def wave_rows(wave_ref, pair, base, row):
    rows = pl.ds(pl.multiple_of(base + row, POINT_ROWS), POINT_ROWS)
    return wave_ref[0, pair, rows, :], wave_ref[1, pair, rows, :]


def cauchy_forward(index, sigma, coef_ref, wave_ref, base, sums_ref, spec_ref):
    sigma_sq = sigma * sigma
    pair, row = index // 2, index % 2 * POINT_ROWS
    rows = slice(row, row + POINT_ROWS)
    lanes = slice(pair * LANES, (pair + 1) * LANES)
    cosine, sine = wave_rows(wave_ref, pair, base, row)
    square_cos, cos_sin, scaled = cosine * cosine, cosine * sine, sigma_sq * (sine * sine)

    def add_mode(n, sums):
        sums = list(sums)
        for k in range(4):
            at = n * 4 + k
            inv_re, inv_im = resolvent(coef_ref, at, square_cos, cos_sin, scaled)
            for q in range(4):
                plain = coef_ref[q, pl.ds(at, 1), :]
                turned = coef_ref[4 + q, pl.ds(at, 1), :]
                sums[4 * q] = sums[4 * q] + plain * inv_re
                sums[4 * q + 1] = sums[4 * q + 1] + plain * inv_im
                sums[4 * q + 2] = sums[4 * q + 2] + turned * inv_re
                sums[4 * q + 3] = sums[4 * q + 3] + turned * inv_im
        return tuple(sums)

    zero = jnp.zeros((POINT_ROWS, LANES), F32)
    sums = lax.fori_loop(0, 8, add_mode, (zero,) * 16)
    for i in range(16):
        sums_ref[pair, i, rows, :] = sums[i]
    terms, _, ratio = combine(sums, sigma, cosine, sine)
    cut_re, cut_im = complex_multiply(*terms[1], *ratio)
    part_re, part_im = terms[0][0] - cut_re, terms[0][1] - cut_im
    spec_re, spec_im = complex_multiply(2.0 * cosine, 2.0 * sine, part_re, part_im)
    spec_ref[rows, lanes] = spec_re
    spec_ref[row + QUARTER : row + QUARTER + POINT_ROWS, lanes] = spec_im


PLACES = [(pair, row) for pair in range(2) for row in range(0, QUARTER, POINT_ROWS)]


def point_grads(sigma, wave_ref, base, sums_ref, spec_ref, grad_ref):
    zero = jnp.zeros((POINT_ROWS, LANES), F32)
    sigma_sum = zero
    for pair, row in PLACES:
        rows = slice(row, row + POINT_ROWS)
        lanes = slice(pair * LANES, (pair + 1) * LANES)
        cosine, sine = wave_rows(wave_ref, pair, base, row)
        sums = [sums_ref[pair, i, rows, :] for i in range(16)]
        terms, inv, ratio = combine(sums, sigma, cosine, sine)
        spec_re, spec_im = spec_ref[rows, lanes], spec_ref[row + QUARTER : row + QUARTER + POINT_ROWS, lanes]
        part = conj_multiply(2.0 * cosine, 2.0 * sine, spec_re, spec_im)
        left = conj_multiply(*ratio, *part)
        ratio_grad = conj_multiply(*terms[1], *part)
        back = conj_multiply(*inv, -ratio_grad[0], -ratio_grad[1])
        twice = 2.0 * cosine
        loop = conj_multiply(*ratio, *back)
        grads = (
            part,
            (-left[0], -left[1]),
            (twice * back[0], twice * back[1]),
            (-twice * loop[0], -twice * loop[1]),
        )
        swing = sigma * sine
        for q, (g_re, g_im) in enumerate(grads):
            grad_ref[pair, 4 * q, rows, :] = swing * g_im
            grad_ref[pair, 4 * q + 1, rows, :] = -swing * g_re
            grad_ref[pair, 4 * q + 2, rows, :] = -cosine * g_re
            grad_ref[pair, 4 * q + 3, rows, :] = -cosine * g_im
            sigma_sum = sigma_sum + sine * (g_im * sums[4 * q] - g_re * sums[4 * q + 1])
    return sigma_sum


def mode_sums(part, square_sum, sigma, coef_ref, wave_ref, base, grad_ref, back_ref):
    sigma_sq = sigma * sigma

    def mode(n, square_sum):
        plain = [coef_ref[q, pl.ds(n, 1), :] for q in range(4)]
        turned = [coef_ref[4 + q, pl.ds(n, 1), :] for q in range(4)]
        sums = [0.0] * 10
        for pair, row in PLACES:
            rows = slice(row, row + POINT_ROWS)
            cosine, sine = wave_rows(wave_ref, pair, base, row)
            square_cos, cos_sin, square_sin = cosine * cosine, cosine * sine, sine * sine
            inv_re, inv_im = resolvent(coef_ref, n, square_cos, cos_sin, sigma_sq * square_sin)
            grad_re, grad_im = 0.0, 0.0
            for q in range(4):
                p_re, p_im = grad_ref[pair, 4 * q, rows, :], grad_ref[pair, 4 * q + 1, rows, :]
                q_re, q_im = grad_ref[pair, 4 * q + 2, rows, :], grad_ref[pair, 4 * q + 3, rows, :]
                grad_re = grad_re + (plain[q] * p_re + turned[q] * q_re)
                grad_im = grad_im + (plain[q] * p_im + turned[q] * q_im)
                sums[q] = sums[q] + (p_re * inv_re + p_im * inv_im)
                sums[4 + q] = sums[4 + q] + (q_re * inv_re + q_im * inv_im)
            square_re = inv_re * inv_re - inv_im * inv_im
            square_im = 2.0 * inv_re * inv_im
            den_re, den_im = conj_multiply(square_re, square_im, grad_re, grad_im)
            sums[8] = sums[8] - den_re * square_cos
            sums[9] = sums[9] - den_im * cos_sin
            square_sum = square_sum + den_re * square_sin
        for i in range(10):
            back_ref[i, pl.ds(n, 1), :] = column_sum(sums[i])
        return square_sum

    return lax.fori_loop(part * 8, part * 8 + 8, mode, square_sum)


def mode_gradients(modes_ref, sigma, nyquist_grad, step, sigma_sum, square_sum, back_ref):
    plain_grad = [fold(back_ref[q]) for q in range(4)]
    turned_grad = [fold(back_ref[4 + q]) for q in range(4)]
    abs_grad, skew_grad = fold(back_ref[8]), fold(back_ref[9])
    lam_re, lam_im = mode_values(modes_ref)
    plain_grad[0] = plain_grad[0] + step * nyquist_grad
    rank_re, rank_im, in_re, in_im, out_re, out_im = (modes_ref[i] for i in range(2, 8))
    lam_re_grad = 2.0 * lam_re * abs_grad - 2.0 * sigma * skew_grad
    lam_im_grad = 2.0 * lam_im * abs_grad
    real_grad, imag_grad = [], []
    terms = pair_terms(modes_ref)
    for q, (real, imag) in enumerate(terms):
        lam_re_grad = lam_re_grad + turned_grad[q] * real
        if imag is not None:
            lam_im_grad = lam_im_grad + turned_grad[q] * imag
        real_grad.append(plain_grad[q] + turned_grad[q] * lam_re)
        imag_grad.append(turned_grad[q] * lam_im)
    r0, r1, r2, r3 = real_grad
    i0, i1, i2, _ = imag_grad
    grads = (
        lam_re_grad * lam_re,
        math.pi * lam_im_grad,
        r1 * out_re - i1 * out_im + r2 * in_re + i2 * in_im + 2.0 * r3 * rank_re,
        r1 * out_im + i1 * out_re + r2 * in_im - i2 * in_re + 2.0 * r3 * rank_im,
        r0 * out_re - i0 * out_im + r2 * rank_re - i2 * rank_im,
        r0 * out_im + i0 * out_re + r2 * rank_im + i2 * rank_re,
        r0 * in_re + i0 * in_im + r1 * rank_re + i1 * rank_im,
        r0 * in_im - i0 * in_re + r1 * rank_im - i1 * rank_re,
    )
    sigma_grad = (
        fold(column_sum(sigma_sum) + 2.0 * sigma * column_sum(square_sum))
        - 2.0 * column_sum(skew_grad * lam_re)
    )
    nyquist = step * column_sum(terms[0][0])
    return grads, nyquist * nyquist_grad - sigma * sigma_grad


def ring_place(chan):
    z, y = lax.div(chan, 2), lax.rem(chan, 2)
    return z + y * (7 - 2 * z)


def ring_chan(place):
    back = lax.div(place, 4)
    z = place * (1 - back) + (7 - place) * back
    return 2 * z + back


TURNS = (1, -1)


def block_kernel(
    bucket_ref, items_ref, tokens_ref, cotangent_ref, gain1_ref, bias1_ref, raw_modes_ref, log_dt_ref, skip_ref,
    wa_ref, ba_ref, wb_ref, bb_ref, gain2_ref, bias2_ref, up_ref, bup_ref, down_ref, bdown_ref,
    levels_ref, coefc_ref, mat_ref, tw_ref, wave_ref,
    out_ref, dtok_ref, gw_ref, gm_ref, gv_ref,
    tok_ref, aux_ref, coefl_ref, modes_ref,
    wab_ref, wh_ref, gab_w_ref, gh_ref,
    stage_ref, sib_ab_ref, ring_ab_ref, ring_h_ref, part_ab_ref, cross_ref, keep_ref, swap_ref, gate_total_ref,
    in_send, in_recv, head_send, head_recv, acts_send, acts_recv, back_send, back_recv, late_send, late_recv,
    sum_send, sum_recv, tail_send, dp_send, dp_low, dp_recv, spec_send, spec_recv, sgrad_send, sgrad_recv,
    hat_ref, norm_ref, slope_ref, conv_ref, rhs_ref, freq_ref, sig_ref, ans_ref, taps_ref,
    mcoef_ref, sums_ref, pgrad_ref, mback_ref, sgrad_ref, taps_freq_ref,
    gate_ref, swish_ref, res_ref, hat2_ref, acts_ref, norm2_ref, gradf_ref, branch_ref, back2_ref, half_send, half_recv,
    gab_ref, hid_ref, gpre_ref, acts_t_ref, norm2_t_ref, gradf_t_ref,
    gring_ss, gring_rs, gsib_ss, gsib_rs, gx_ss, gx_rs, gdx_ss, gdx_rs, gswap_ss, gswap_rs, core_ss, core_rs,
    rring_ss, rring_rs, rsib_ss, rsib_rs, rx_ss, rx_rs, rdx_ss, rdx_rs, rswap_ss, rswap_rs,
    a2a_ss, a2a_rs, dp_ss, dp_rs, spec_ss, spec_rs,
):
    dp, chan = lax.axis_index("dp"), lax.axis_index("chan")
    core = lax.rem(dp, 2)
    sibling = dp + 1 - 2 * core
    place = ring_place(chan)
    spots = [lax.rem(place + offset, 8) if offset else place for offset in range(8)]
    around = [ring_chan(spot) if offset else chan for offset, spot in enumerate(spots)]
    groups = [lax.rem(spot, 4) for spot in spots]
    group_lanes = [pl.multiple_of(lax.div(spot, 4) * LANES, LANES) for spot in spots]
    nexts = [around[1], around[7]]
    chan_peers = [chan] + [lax.rem(chan + r, N_CHAN) for r in range(1, N_CHAN)]
    dp_peers = [dp] + [lax.rem(dp + r, 4) for r in range(1, 4)]
    across = dp_peers[2]

    def chan_at(offset):
        return around[offset % 8]

    barrier = pltpu.get_barrier_semaphore()
    for r in range(1, N_CHAN):
        pl.semaphore_signal(barrier, inc=1, device_id={"chan": chan_peers[r]}, device_id_type=MESH)
    for r in range(1, 4):
        pl.semaphore_signal(barrier, inc=1, device_id={"dp": dp_peers[r]}, device_id_type=MESH)

    pending = []

    def remote(src, dst, send_sem, recv_sem, **device):
        return pltpu.make_async_remote_copy(
            src_ref=src, dst_ref=dst, send_sem=send_sem, recv_sem=recv_sem, device_id=device, device_id_type=MESH
        )

    def send(*args, **device):
        copy = remote(*args, **device)
        copy.start()
        pending.append(copy)

    def exchange(which, source, recv_ref):
        def copy(r):
            peer = chan_peers[r]
            return remote(
                source(peer), recv_ref.at[chan], a2a_ss.at[which, r - 1], a2a_rs.at[which, r - 1], chan=peer
            )

        def start():
            for r in range(1, N_CHAN):
                copy(r).start()

        def wait():
            for r in range(1, N_CHAN):
                copy(r).wait_recv()

        def finish():
            for r in range(1, N_CHAN):
                copy(r).wait_send()

        return start, wait, finish

    def rows_at(number, count):
        return pl.ds(pl.multiple_of(number, ROWS), count)

    def launch(copy):
        copy.start()
        pending.append(copy)

    own_row = dp * ROWS
    pair_row = (dp - core) * ROWS
    away_row = 2 * ROWS - pair_row
    gate_row, gate_away = (core * 2 + lax.div(dp, 2)) * ROWS, (core * 2 + 1 - lax.div(dp, 2)) * ROWS
    gate_pair, gate_other = core * 2 * ROWS, (1 - core) * 2 * ROWS
    half_lanes = pl.multiple_of(core * LANES, LANES)
    other_lanes = pl.multiple_of((1 - core) * LANES, LANES)

    def gate_view(ref):
        return lambda offset, row, count: ref.at[around[offset % 8], rows_at(row, count), :]

    def hidden_view(ref):
        return lambda offset, row, count: ref.at[
            :, groups[offset % 8], rows_at(row, count), pl.ds(group_lanes[offset % 8], LANES)
        ]

    class Ring:
        def __init__(self, which, view, base, count, hook=None):
            self.which, self.view, self.base, self.count, self.hook = which, view, base, count, hook

        def piece(self, turn, step, base):
            half = self.count // 2
            if step == 4:
                return self.view(4, base + turn * half, half)
            return self.view(-TURNS[turn] * step, base, self.count)

        def copy(self, turn, step, ref):
            slot = turn * 4 + step - 1
            return remote(ref, ref, gring_ss.at[self.which, slot], gring_rs.at[self.which, slot], chan=nexts[turn])

        def send(self, turn, step):
            half = self.count // 2
            if step == 4:
                ref = self.view(-TURNS[turn] * 3, self.base + turn * half, half)
            else:
                ref = self.piece(turn, step - 1, self.base)
            launch(self.copy(turn, step, ref))

        def start(self):
            for turn in range(2):
                self.send(turn, 1)

        def step(self, step):
            for turn in range(2):
                self.copy(turn, step, self.piece(turn, step, self.base)).wait_recv()
                if step < 4:
                    self.send(turn, step + 1)
                if self.hook:
                    self.hook(turn, step)

    def slot_of(turn, step):
        return turn * 4 + step - 1 if step else 8

    def gate_sib(base):
        ref = wab_ref.at[:, rows_at(base, 256), :]
        return remote(ref, ref, gsib_ss, gsib_rs, dp=sibling)

    def gate_spread():
        launch(gate_sib(gate_pair))

    def hidden_cross(turn, step, base):
        ref, slot = hidden_ring.piece(turn, step, base), slot_of(turn, step)
        return remote(ref, ref, gdx_ss.at[slot], gdx_rs.at[slot], dp=across)

    gate_ring = Ring(0, gate_view(wab_ref), gate_pair, 256)
    hidden_ring = Ring(
        1, hidden_view(wh_ref), pair_row, 256, lambda turn, step: launch(hidden_cross(turn, step, pair_row))
    )

    def gate_over(row):
        ref = gate_ring.view(0, row, ROWS)
        return remote(ref, ref, gx_ss, gx_rs, dp=across)

    def swap_copy(row):
        return remote(stage_ref, hidden_ring.view(0, row, ROWS), gswap_ss, gswap_rs, dp=sibling)

    def gather_prepare():
        gates = jnp.concatenate([wa_ref[...], wb_ref[...]], axis=0).T.astype(BF16)
        wab_ref[chan, rows_at(gate_row, ROWS), :] = gates
        for which, values in enumerate((up_ref[...], down_ref[...].T)):
            first, second = values[:, :LANES], values[:, LANES:]
            kept = jnp.where(core == 0, first, second)
            wh_ref[which, groups[0], rows_at(own_row, ROWS), pl.ds(group_lanes[0], LANES)] = kept.astype(BF16)
            stage_ref[which] = jnp.where(core == 0, second, first).astype(BF16)

    def gather_start():
        launch(swap_copy(own_row))
        launch(gate_over(gate_row))

    def hidden_first():
        swap_copy(sibling * ROWS).wait_recv()
        hidden_ring.start()
        launch(hidden_cross(0, 0, pair_row))

    def gate_first():
        gate_over(gate_away).wait_recv()
        gate_ring.start()

    ring_steps = [(0, 0)] + [(turn, step) for step in range(1, 5) for turn in range(2)]

    def gates_arrived():
        gate_sib(gate_other).wait_recv()

    def hidden_arrived(*steps):
        for turn, step in ring_steps:
            if step in steps:
                hidden_cross(turn, step, away_row).wait_recv()

    def beside(ref, j):
        start = 2 * j * ROWS
        return jnp.concatenate(
            [ref[:, start : start + ROWS].astype(F32), ref[:, start + ROWS : start + 2 * ROWS].astype(F32)], axis=0
        ).T

    for j in range(PAIRS):
        packed = beside(tokens_ref, j)
        tok_ref[j * ROWS : (j + 1) * ROWS, :] = packed.astype(BF16)
        for first, values in ((0, packed), (HALF, beside(cotangent_ref, j))):
            low, high = split_pair(values)
            in_send[2 * j, first : first + HALF, :] = low.astype(BF16)
            in_send[2 * j + 1, first : first + HALF, :] = high.astype(BF16)
    in_recv[chan] = in_send[chan]

    lane_id = lax.broadcasted_iota(jnp.int32, (8, LANES), 1)
    row_id = lax.broadcasted_iota(jnp.int32, (8, LANES), 0)
    halves = jnp.where((lane_id >= HALF) == (row_id == 1), 1.0, 0.0) * jnp.where(row_id < 2, 1.0, 0.0)
    halves = halves.astype(BF16)

    def token_sums(parts):
        total = 0.0
        for part in parts:
            total = total + dot_nt(halves, part)
        return [total[h : h + 1, j * ROWS : (j + 1) * ROWS] for h in range(2) for j in range(PAIRS)]

    def split(values):
        high = values.astype(BF16)
        return high, (values - high.astype(F32)).astype(BF16)

    tokens = tok_ref[...]
    wide_tokens = tokens.astype(F32)
    for i, sums in enumerate(token_sums([tokens]) + token_sums(split(wide_tokens * wide_tokens))):
        head_send[i : i + 1, :] = sums

    def row(*refs):
        return jnp.concatenate([ref[...].reshape(1, HALF) for ref in refs], axis=1)

    bup = bup_ref[...].reshape(1, 2 * LANES)
    head_send[16:17, :] = row(ba_ref, bb_ref)
    head_send[17:18, :] = row(gain2_ref, bias2_ref)
    head_send[18:19, :] = row(bdown_ref, bdown_ref)
    head_send[19:20, :] = bup[:, :LANES]
    head_send[20:21, :] = bup[:, LANES:]
    head_send[21:24, :] = jnp.zeros((3, LANES), F32)
    head_recv[chan] = head_send[...]
    head = exchange(0, lambda peer: head_send, head_recv)
    inputs = exchange(1, lambda peer: in_send.at[peer], in_recv)
    gather_prepare()
    pl.semaphore_wait(barrier, N_CHAN - 1 + 3)
    head[0]()
    gather_start()
    hidden_first()

    level, filled = bucket_ref[0], items_ref[0]
    coefl_ref[...] = levels_ref[level]
    item_blocks = jnp.where(level == 0, 2, jnp.where(level == 1, 4, 8))
    block_id = 2 * (row_id % PAIRS) + jnp.where(lane_id >= HALF, 1, 0)
    bound = jnp.where(row_id < PAIRS, filled * item_blocks, item_blocks)
    aux_ref[...] = jnp.where(block_id < bound, 1.0, 0.0)
    for i in range(8):
        modes_ref[i] = jnp.concatenate([raw_modes_ref[i], raw_modes_ref[i]], axis=1)
    log_dt = row(log_dt_ref, log_dt_ref)
    sigma, step_size = 2.0 * jnp.exp(-log_dt), jnp.exp(log_dt)
    gate_first()

    base = pl.multiple_of(dp * QUARTER, QUARTER)

    def spec_copy(which, r):
        peer = dp_peers[r]
        src, dst = ((spec_send, spec_recv), (sgrad_send.at[peer], sgrad_recv))[which]
        return remote(src, dst.at[dp], spec_ss.at[which, r - 1], spec_rs.at[which, r - 1], dp=peer)

    cauchy_coefficients(modes_ref, sigma, mcoef_ref)
    cauchy_forward(0, sigma, mcoef_ref, wave_ref, base, sums_ref, spec_send)
    inputs[0]()
    cauchy_forward(1, sigma, mcoef_ref, wave_ref, base, sums_ref, spec_send)
    cauchy_forward(2, sigma, mcoef_ref, wave_ref, base, sums_ref, spec_send)
    cauchy_forward(3, sigma, mcoef_ref, wave_ref, base, sums_ref, spec_send)
    spec_recv[dp] = spec_send[...]
    for r in range(1, 4):
        spec_copy(0, r).start()
    gate_ring.step(1)
    hidden_ring.step(1)

    head[1]()
    sums = head_recv[0, 0:16, :]
    for c in range(1, N_CHAN):
        sums = sums + head_recv[c, 0:16, :]
    mean = sums[0:8] * (1.0 / MODEL_WIDTH)
    rstd = lax.rsqrt(sums[8:16] * (1.0 / MODEL_WIDTH) - mean * mean + EPSILON)

    def columns(rows):
        tall = rows.T
        return [jnp.where(low_lanes(ROWS), tall[:, j : j + 1], tall[:, 4 + j : 5 + j]) for j in range(PAIRS)]

    gain1, bias1, skip = row(gain1_ref, gain1_ref), row(bias1_ref, bias1_ref), row(skip_ref, skip_ref)
    mean_cols, rstd_cols = columns(mean), columns(rstd)
    for j in range(PAIRS):
        hat = (tok_ref[j * ROWS : (j + 1) * ROWS, :].astype(F32) - mean_cols[j]) * rstd_cols[j]
        hat_ref[j] = hat
        norm_ref[j] = hat * gain1 + bias1

    spread_pairs(lambda j, rows: norm_ref[j, rows, :], coefl_ref, 0, tw_ref, 0, 5, rhs_ref, False)
    transform_into(sig_ref, mat_ref, 0, rhs_ref, False)

    for r in range(1, 4):
        spec_copy(0, r).wait_recv()
    for source in range(4):
        store_split(rhs_ref, source * QUARTER, 0, spec_recv[source, :QUARTER, :])
        store_split(rhs_ref, ROWS + source * QUARTER, 0, spec_recv[source, QUARTER:, :])
    gate_ring.step(2)
    freq_ref[:, 0:256] = split_product(mat_ref, 1, rhs_ref, 0, 256)
    hidden_ring.step(2)
    even = split_product(mat_ref, 2, rhs_ref, LANES, LANES)
    freq_ref[:, LANES:256] = jnp.where(low_lanes(256), freq_ref[:, LANES:256], even)
    sign = 1.0 - 2.0 * (lax.broadcasted_iota(jnp.int32, (CHUNK, LANES), 0) % 2).astype(F32)
    nyquist = step_size * column_sum(mcoef_ref[0]) * (1.0 / TOK_DEV)

    def store_taps(j, rows, values):
        taps_ref[j, rows, :] = (values + sign * nyquist) * aux_ref[4 + j : 5 + j, :]

    gather_pairs(freq_ref, coefc_ref, 160, tw_ref, 10, 2, store_taps)
    spread_pairs(lambda j, rows: taps_ref[j, rows, :], coefc_ref, 0, tw_ref, 0, 5, rhs_ref, False)
    transform_into(ans_ref, mat_ref, 0, rhs_ref, False)
    multiply_spectra(sig_ref, ans_ref, rhs_ref, False, False)
    transform_into(freq_ref, mat_ref, 1, rhs_ref, False)
    gate_ring.step(3)
    hidden_ring.step(3)

    def store_conv(j, rows, values):
        conv_ref[j, rows, :] = values
    gather_pairs(freq_ref, coefl_ref, 80, tw_ref, 0, 5, store_conv)
    for j in range(PAIRS):
        mixed = conv_ref[j] * aux_ref[j : j + 1, :] + skip * norm_ref[j]
        cumulative, density = normal_parts(mixed)
        slope_ref[j] = cumulative + mixed * density
        low, high = split_pair(mixed * cumulative)
        acts_send[2 * j] = low.astype(BF16)
        acts_send[2 * j + 1] = high.astype(BF16)
    acts_recv[chan] = acts_send[chan]
    acts = exchange(2, lambda peer: acts_send.at[peer], acts_recv)
    acts[0]()

    def joined(ref, pair, first):
        return join_pair(
            ref[2 * pair, first : first + HALF, :].astype(F32), ref[2 * pair + 1, first : first + HALF, :].astype(F32)
        )

    def lanes_of(pair):
        return slice(pair * LANES, (pair + 1) * LANES)

    def gate_lanes(pair):
        return lanes_of(pair % 2 * 2 + pair // 2)

    def core_copy(which, src, dst):
        return remote(src, dst, core_ss.at[which], core_rs.at[which], dp=sibling)

    def other_core(which, ref):
        return core_copy(which, ref.at[core], ref.at[core])

    def vector(row, first, second):
        return interleave(head_recv[first, 16 + row : 17 + row, :], head_recv[second, 16 + row : 17 + row, :])

    def both_cores(ref):
        return ref[...].reshape(2 * ROWS, MODEL_WIDTH)

    def hidden_group(offset):
        group = groups[offset]
        low, high = 2 * group, 7 - 2 * group
        bias = jnp.concatenate(
            [jnp.where(core == 0, head_recv[c, 19:20, :], head_recv[c, 20:21, :]) for c in (low, high)], axis=1
        )
        pre = dot_nn(both_cores(norm2_ref), wh_ref[0, group]) + bias
        cumulative, density = normal_parts(pre)
        hidden = (pre * cumulative).astype(BF16)
        hid_ref[group] = hidden
        grad = dot_nn(both_cores(gradf_ref), wh_ref[1, group]) * (cumulative + pre * density)
        grad = grad.astype(BF16)
        gpre_ref[group] = grad
        sums = column_sum(grad.astype(F32))
        tail_send[low, pl.ds(3 + core, 1), :] = sums[:, 0:LANES]
        tail_send[high, pl.ds(3 + core, 1), :] = sums[:, LANES : 2 * LANES]
        branch_ref[...] += dot_nt(hidden, wh_ref[1, group]).reshape(2, ROWS, MODEL_WIDTH)
        back2_ref[...] += dot_nt(grad, wh_ref[0, group]).reshape(2, ROWS, MODEL_WIDTH)

    def offset_of(turn, step):
        return TURNS[turn] * (5 - step)

    def far(offset):
        return 4 if offset == -4 else offset

    class RingBack:
        def __init__(self, which, view, base, count, ring_ref, extra):
            self.which, self.view, self.base, self.count = which, view, base, count
            self.ring_ref, self.extra = ring_ref, extra

        def copy(self, turn, step):
            slot = turn * 4 + step - 1
            half = self.count // 2
            if step == 1:
                dst = self.ring_ref.at[slot]
                lead = (slice(None),) * (len(dst.shape) - 2)
                src, dst = self.view(4, self.base + turn * half, half), dst.at[lead + (pl.ds(0, half), slice(None))]
            else:
                src, dst = self.view(offset_of(turn, step), self.base, self.count), self.ring_ref.at[slot]
            return remote(src, dst, rring_ss.at[self.which, slot], rring_rs.at[self.which, slot], chan=nexts[turn])

        def whole(self, offset):
            return self.view(offset, self.base, self.count)[...].astype(F32) + self.extra(offset)

        def step(self, step):
            half = self.count // 2
            if step == 1:
                self.view(4, self.base, self.count)[...] = self.whole(4).astype(BF16)
                for turn in range(2):
                    launch(self.copy(turn, 1))
                return
            for turn in range(2):
                offset, slot = offset_of(turn, step), turn * 4 + step - 2
                total = self.whole(offset)
                self.copy(turn, step - 1).wait_recv()
                if step == 2:
                    parts = [total[..., :half, :], total[..., half:, :]]
                    parts[turn] = parts[turn] + self.ring_ref[slot][..., :half, :].astype(F32)
                    total = jnp.concatenate(parts, axis=-2)
                else:
                    total = total + self.ring_ref[slot].astype(F32)
                self.view(offset, self.base, self.count)[...] = total.astype(BF16)
                launch(self.copy(turn, step))

        def total(self):
            total = self.whole(0)
            for turn in range(2):
                self.copy(turn, 4).wait_recv()
                total = total + self.ring_ref[turn * 4 + 3].astype(F32)
            return total

    waited = set()

    def wait_once(name, copy):
        if name not in waited:
            waited.add(name)
            copy().wait_recv()

    def gate_share():
        ref = gab_w_ref.at[:, rows_at(gate_other, 256), :]
        return remote(ref, sib_ab_ref, rsib_ss, rsib_rs, dp=sibling)

    def gate_extra(offset):
        wait_once("gates", gate_share)
        return sib_ab_ref[around[offset % 8]].astype(F32)

    def cross_copy(pair):
        src = gh_ref.at[:, groups[pair], rows_at(away_row, 256), :]
        return remote(src, cross_ref.at[pair], rdx_ss.at[pair], rdx_rs.at[pair], dp=across)

    def hidden_extra(offset):
        pair = offset % 4
        wait_once(pair, lambda: cross_copy(pair))
        return cross_ref[pair, :, :, pl.ds(group_lanes[offset % 8], LANES)].astype(F32)

    gate_g = RingBack(0, gate_view(gab_w_ref), gate_pair, 256, ring_ab_ref, gate_extra)

    hidden_g = RingBack(1, hidden_view(gh_ref), pair_row, 256, ring_h_ref, hidden_extra)

    def hidden_grads(offset):
        group = groups[offset]
        gh_ref[1, group] = dot_nn(gradf_t_ref[...], hid_ref[group]).astype(BF16)
        gh_ref[0, group] = dot_nn(norm2_t_ref[...], gpre_ref[group]).astype(BF16)
        launch(cross_copy(offset))

    def part_copy():
        return remote(part_ab_ref.at[0], part_ab_ref.at[1], rx_ss, rx_rs, dp=across)

    def last_swap():
        return remote(keep_ref.at[:, rows_at((1 - core) * ROWS, ROWS), :], swap_ref, rswap_ss, rswap_rs, dp=sibling)

    def gate_last():
        gate_total_ref[...] = gate_g.total()
        part_ab_ref[0] = gate_total_ref[rows_at((1 - lax.div(dp, 2)) * ROWS, ROWS), :].astype(BF16)
        launch(part_copy())

    def gate_finish():
        part_copy().wait_recv()
        gw_ref[:, 0:128] = gate_total_ref[rows_at(lax.div(dp, 2) * ROWS, ROWS), :] + part_ab_ref[1].astype(F32)

    def hidden_last():
        keep_ref[...] = hidden_g.total()
        launch(last_swap())
        for which in range(2):
            gw_ref[:, pl.ds(pl.multiple_of(128 + 256 * which + half_lanes, LANES), LANES)] = keep_ref[
                which, rows_at(core * ROWS, ROWS), :
            ]

    def hidden_finish():
        last_swap().wait_recv()
        for which in range(2):
            gw_ref[:, pl.ds(pl.multiple_of(128 + 256 * which + other_lanes, LANES), LANES)] = swap_ref[which]

    late = exchange(4, lambda peer: late_send.at[peer], late_recv)


    def gate_grads(*offsets):
        for offset in offsets:
            c = chan_at(offset)
            gab_w_ref[c] = dot_nn(acts_t_ref[...], gab_ref[c]).astype(BF16)
        if 0 in offsets:
            launch(gate_share())

    def late_messages():
        core_copy(3, half_send.at[1], half_recv.at[1]).wait_recv()
        for p in range(PAIRS):
            out = res_ref[p] + (branch_ref[core, :, lanes_of(p)] + half_recv[1, :, lanes_of(p)].astype(F32)) + interleave(head_recv[2 * p, 18:19, :], head_recv[2 * p + 1, 18:19, :])[0]
            low, high = split_pair(out)
            late_send[2 * p, :HALF, :] = low.astype(BF16)
            late_send[2 * p + 1, :HALF, :] = high.astype(BF16)
        for c in range(N_CHAN):
            late_send[c, ROWS:, :] = jnp.concatenate([tail_send[c], jnp.zeros((8, LANES), F32)], axis=0).astype(BF16)
        late_recv[chan] = late_send[chan]
        late[0]()

    back = exchange(3, lambda peer: back_send.at[peer], back_recv)

    inputs[1]()
    for p in range(PAIRS):
        gradf_ref[core, :, lanes_of(p)] = joined(in_recv, p, HALF).astype(BF16)
    gate_ring.step(4)
    gate_spread()
    gates_arrived()
    launch(other_core(0, gradf_ref))
    acts[1]()
    for p in range(PAIRS):
        acts_ref[:, gate_lanes(p)] = joined(acts_recv, p, 0).astype(BF16)

    total = 0.0
    for p in range(PAIRS):
        first = dot_nn(acts_ref[...], wab_ref[2 * p]) + head_recv[2 * p, 16:17, :]
        second = dot_nn(acts_ref[...], wab_ref[2 * p + 1]) + head_recv[2 * p + 1, 16:17, :]
        gate, raw = interleave(first, second)
        swish = lax.logistic(raw)
        gate_ref[p], swish_ref[p] = gate, swish
        resid = joined(in_recv, p, 0) + gate * swish
        res_ref[p] = resid
        total = total + resid
    mean2 = jnp.sum(total, axis=1, keepdims=True) * (1.0 / MODEL_WIDTH)
    total = 0.0
    for p in range(PAIRS):
        centred = res_ref[p] - mean2
        total = total + centred * centred
    rstd2 = lax.rsqrt(jnp.sum(total, axis=1, keepdims=True) * (1.0 / MODEL_WIDTH) + EPSILON)
    gain2 = []
    for p in range(PAIRS):
        gain, bias = vector(1, 2 * p, 2 * p + 1)
        gain2.append(gain)
        hat = (res_ref[p] - mean2) * rstd2
        hat2_ref[p] = hat
        norm2_ref[core, :, lanes_of(p)] = (hat * gain + bias).astype(BF16)
    launch(other_core(1, norm2_ref))
    branch_ref[...] = jnp.zeros_like(branch_ref)
    back2_ref[...] = jnp.zeros_like(back2_ref)
    for c in range(N_CHAN):
        tail_send[c, 3:8, :] = jnp.zeros((5, LANES), F32)
    hidden_arrived(2)
    hidden_ring.step(4)
    other_core(0, gradf_ref).wait_recv()
    gradf_t_ref[...] = both_cores(gradf_ref).astype(F32).T.astype(BF16)
    other_core(1, norm2_ref).wait_recv()
    hidden_arrived(1, 3)
    hidden_group(3)
    norm2_t_ref[...] = both_cores(norm2_ref).astype(F32).T.astype(BF16)
    hidden_group(1)
    hidden_grads(3)
    hidden_group(2)
    hidden_arrived(0, 4)
    hidden_group(0)
    half_send[0] = back2_ref[1 - core].astype(BF16)
    launch(core_copy(2, half_send.at[0], half_recv.at[0]))
    hidden_grads(0)
    half_send[1] = branch_ref[1 - core].astype(BF16)
    launch(core_copy(3, half_send.at[1], half_recv.at[1]))
    acts_t_ref[...] = acts_ref[...].astype(F32).T.astype(BF16)
    core_copy(2, half_send.at[0], half_recv.at[0]).wait_recv()
    back2 = back2_ref[core] + half_recv[0].astype(F32)
    back2_ref[core] = back2

    mean_q, mean_qx = 0.0, 0.0
    for p in range(PAIRS):
        grad, hat = back2_ref[core, :, lanes_of(p)], hat2_ref[p]
        q = grad * gain2[p]
        mean_q = mean_q + q
        mean_qx = mean_qx + q * hat
        gain_grad, bias_grad = interleave(column_sum(grad * hat), column_sum(grad))
        tail_send[2 * p, 1:2, :] = gain_grad
        first, second = interleave(turn_half(column_sum(grad * hat)), turn_half(column_sum(grad)))
        tail_send[2 * p + 1, 1:2, :] = first
    mean_q = jnp.sum(mean_q, axis=1, keepdims=True) * (1.0 / MODEL_WIDTH)
    mean_qx = jnp.sum(mean_qx, axis=1, keepdims=True) * (1.0 / MODEL_WIDTH)
    for p in range(PAIRS):
        hat = hat2_ref[p]
        extra = rstd2 * (back2_ref[core, :, lanes_of(p)] * gain2[p] - mean_q - hat * mean_qx)
        grad_f = joined(in_recv, p, HALF)
        grad_resid = grad_f + extra
        gate, swish = gate_ref[p], swish_ref[p]
        grad_a = (grad_resid * swish).astype(BF16).astype(F32)
        grad_b = (grad_resid * gate * swish * (1.0 - swish)).astype(BF16).astype(F32)
        first, second = interleave(grad_a, grad_b)
        gab_ref[2 * p] = first.astype(BF16)
        gab_ref[2 * p + 1] = second.astype(BF16)
        tail_send[2 * p, 0:1, :] = column_sum(first)
        tail_send[2 * p + 1, 0:1, :] = column_sum(second)
        low, high = interleave(column_sum(grad_f), column_sum(grad_f))
        tail_send[2 * p, 2:3, :] = low
        tail_send[2 * p + 1, 2:3, :] = high
        low, high = split_pair(extra)
        late_send[2 * p, HALF:ROWS, :] = low.astype(BF16)
        late_send[2 * p + 1, HALF:ROWS, :] = high.astype(BF16)
    grad_acts = 0.0
    for c in range(N_CHAN):
        grad_acts = grad_acts + dot_nt(gab_ref[c], wab_ref[c])
    for p in range(PAIRS):
        low, high = split_pair(grad_acts[:, gate_lanes(p)])
        back_send[2 * p] = low.astype(BF16)
        back_send[2 * p + 1] = high.astype(BF16)
    back_recv[chan] = back_send[chan]
    back[0]()
    gate_grads(4, 3, -3)
    hidden_grads(1)
    late_messages()

    back[1]()
    skip_grad = 0.0
    for j in range(PAIRS):
        grad = joined(back_recv, j, 0) * slope_ref[j]
        slope_ref[j] = grad
        conv_ref[j] = grad * aux_ref[j : j + 1, :]
        skip_grad = skip_grad + column_sum(grad * norm_ref[j])
    gate_grads(2, -2, 1, -1, 0)
    spread_pairs(lambda j, rows: conv_ref[j, rows, :], coefl_ref, 0, tw_ref, 0, 5, rhs_ref, False)
    gate_g.step(1)
    hidden_g.step(1)
    hidden_grads(2)
    transform_into(freq_ref, mat_ref, 0, rhs_ref, False)
    gate_g.step(2)
    hidden_g.step(2)
    multiply_spectra(sig_ref, freq_ref, rhs_ref, True)
    transform_into(sig_ref, mat_ref, 1, rhs_ref)

    def store_kernel_grad(j, rows, values):
        taps_ref[j, rows, :] = values * aux_ref[4 + j : 5 + j, :]

    gather_pairs(sig_ref, coefc_ref, 80, tw_ref, 0, 5, store_kernel_grad)
    nyquist_grad = 0.0
    for j in range(PAIRS):
        whole_sign = 1.0 - 2.0 * (lax.broadcasted_iota(jnp.int32, (ROWS, LANES), 0) % 2).astype(F32)
        nyquist_grad = nyquist_grad + column_sum(taps_ref[j] * whole_sign)
    nyquist_grad = fold(nyquist_grad) * (1.0 / TOK_DEV)
    spread_pairs(lambda j, rows: taps_ref[j, rows, :], coefc_ref, 192, tw_ref, 10, 2, rhs_ref)
    gate_g.step(3)
    taps_freq_ref[...] = split_product(mat_ref, 0, rhs_ref, 0, 256)
    even = split_product(mat_ref, 3, rhs_ref, LANES, LANES)
    taps_freq_ref[:, LANES:256] = jnp.where(low_lanes(256), taps_freq_ref[:, LANES:256], even)
    for source in range(4):
        rows = slice(source * QUARTER, (source + 1) * QUARTER)
        sgrad_send[source, :QUARTER, :] = taps_freq_ref[rows, :]
        sgrad_send[source, QUARTER:, :] = taps_freq_ref[ROWS + source * QUARTER : ROWS + (source + 1) * QUARTER, :]
    sgrad_recv[dp] = sgrad_send[dp]
    for r in range(1, 4):
        spec_copy(1, r).start()

    multiply_spectra(ans_ref, freq_ref, rhs_ref, True, False)
    transform_into(freq_ref, mat_ref, 1, rhs_ref, False)
    hidden_g.step(3)
    gather_pairs(freq_ref, coefl_ref, 80, tw_ref, 0, 5, store_conv)
    gain_grad, bias_grad = 0.0, 0.0
    scaled, crossed = [], []
    for j in range(PAIRS):
        grad = conv_ref[j] + skip * slope_ref[j]
        conv_ref[j] = grad
        gain_grad = gain_grad + column_sum(grad * hat_ref[j])
        bias_grad = bias_grad + column_sum(grad)
    late[1]()
    conv = conv_ref[...].reshape(PAIRS * ROWS, LANES) * gain1
    for i, sums in enumerate(
        token_sums(split(conv)) + token_sums(split(conv * hat_ref[...].reshape(PAIRS * ROWS, LANES)))
    ):
        sum_send[i : i + 1, :] = sums
    sum_recv[chan] = sum_send[...]
    sums_back = exchange(6, lambda peer: sum_send, sum_recv)

    for r in range(1, 4):
        spec_copy(1, r).wait_recv()
    gate_g.step(4)
    sgrad_ref[...] = sgrad_recv[0] + sgrad_recv[1] + sgrad_recv[2] + sgrad_recv[3]

    sigma_sum = point_grads(sigma, wave_ref, base, sums_ref, sgrad_ref, pgrad_ref)
    hidden_g.step(4)
    square_sum = mode_sums(0, jnp.zeros_like(sigma_sum), sigma, mcoef_ref, wave_ref, base, pgrad_ref, mback_ref)
    square_sum = mode_sums(1, square_sum, sigma, mcoef_ref, wave_ref, base, pgrad_ref, mback_ref)
    square_sum = mode_sums(2, square_sum, sigma, mcoef_ref, wave_ref, base, pgrad_ref, mback_ref)
    sums_back[0]()
    gate_last()
    square_sum = mode_sums(3, square_sum, sigma, mcoef_ref, wave_ref, base, pgrad_ref, mback_ref)
    mode_grads, dt_grad = mode_gradients(modes_ref, sigma, nyquist_grad, step_size, sigma_sum, square_sum, mback_ref)
    mask = low_lanes(32)
    for i in range(4):
        dp_send[i * 32 : (i + 1) * 32, :] = jnp.where(mask, mode_grads[i], mode_grads[i + 4])
    first = low_lanes(1)
    dp_send[128:129, :] = jnp.where(first, dt_grad, fold(skip_grad))
    dp_send[129:130, :] = jnp.where(first, fold(gain_grad), fold(bias_grad))
    dp_send[130:136, :] = jnp.zeros((6, LANES), F32)
    tail_sum = late_recv[0, ROWS:, :].astype(F32)
    for c in range(1, N_CHAN):
        tail_sum = tail_sum + late_recv[c, ROWS:, :].astype(F32)
    dp_send[136:144, :] = tail_sum[:8]
    dp_low[...] = dp_send[...].astype(BF16)

    def dp_copy(r):
        return remote(dp_low, dp_recv.at[r - 1], dp_ss.at[r - 1], dp_rs.at[r - 1], dp=dp_peers[r])

    for r in range(1, 4):
        dp_copy(r).start()
    hidden_last()

    sums_back[1]()
    gate_finish()
    sums = sum_recv[0]
    for c in range(1, N_CHAN):
        sums = sums + sum_recv[c]
    sums = sums * (1.0 / MODEL_WIDTH)
    rstd_cols, q_cols, qx_cols = columns(rstd), columns(sums[0:8]), columns(sums[8:16])
    for j in range(PAIRS):
        rows = slice(j * ROWS, (j + 1) * ROWS)
        out_ref[rows, :] = joined(late_recv, j, 0).astype(BF16)
        dtok_ref[rows, :] = joined(late_recv, j, HALF) + rstd_cols[j] * (
            conv_ref[j] * gain1 - q_cols[j] - hat_ref[j] * qx_cols[j]
        )
    for r in range(1, 4):
        dp_copy(r).wait_recv()
    total = dp_send[...] + (dp_recv[0].astype(F32) + dp_recv[1].astype(F32) + dp_recv[2].astype(F32))
    gm_ref[...] = total[0:128]
    hidden_finish()
    gv_ref[...] = total[128:144]
    for copy in pending:
        copy.wait_send()
    for group in (head, inputs, acts, back, late, sums_back):
        group[2]()
    for r in range(1, 4):
        dp_copy(r).wait_send()
        spec_copy(0, r).wait_send()
        spec_copy(1, r).wait_send()
def unpack_kernel(
    out_ref, dtok_ref, gw_ref, gm_ref, gv_ref, cotangent_ref,
    output_ref, tokens_ref, gain1_ref, bias1_ref, modes_ref, dt_ref, skip_ref, wa_ref, ba_ref, wb_ref, bb_ref,
    gain2_ref, bias2_ref, up_ref, bup_ref, down_ref, bdown_ref,
):
    for j in range(PAIRS):
        out = out_ref[j * ROWS : (j + 1) * ROWS, :].astype(F32).T.astype(BF16)
        grad = dtok_ref[j * ROWS : (j + 1) * ROWS, :].T
        for h in range(2):
            lanes, rows = slice((2 * j + h) * ROWS, (2 * j + h + 1) * ROWS), slice(h * HALF, (h + 1) * HALF)
            output_ref[:, lanes] = out[rows]
            tokens_ref[:, lanes] = cotangent_ref[:, lanes] + grad[rows]
    for i in range(8):
        modes_ref[i] = gm_ref[i % 4 * 32 : i % 4 * 32 + 32, i // 4 * HALF : (i // 4 + 1) * HALF]
    gates = gw_ref[:, :LANES].T
    wa_ref[...] = gates[:HALF]
    wb_ref[...] = gates[HALF:]
    up_ref[...] = gw_ref[:, 128:384]
    down_ref[...] = gw_ref[:, 384:640].T
    for at, low, high in (
        (0, dt_ref, skip_ref), (1, gain1_ref, bias1_ref), (8, ba_ref, bb_ref), (9, gain2_ref, bias2_ref),
    ):
        low[...] = gv_ref[at, :HALF]
        high[...] = gv_ref[at, HALF:]
    bdown_ref[...] = gv_ref[10, :HALF]
    bup_ref[:LANES] = gv_ref[11, :]
    bup_ref[LANES:] = gv_ref[12, :]


def block_program():
    mats, twiddle, levels, constant, wave = mixer_tables()

    def run(tokens, cotangent, bucket, items, gain1, bias1, modes, log_dt, skip, w_a, b_a, w_b, b_b, gain2, bias2, w_up, b_up, w_down, b_down):
        vmem = pl.BlockSpec(memory_space=pltpu.VMEM)
        smem = pl.BlockSpec(memory_space=pltpu.SMEM)
        dma = pltpu.SemaphoreType.DMA

        def buf(*shape):
            return pltpu.VMEM(shape, F32)

        def low(*shape):
            return pltpu.VMEM(shape, BF16)

        def full(*shape):
            return jax.ShapeDtypeStruct(shape, F32)

        big, wide = (PAIRS, ROWS, LANES), (256, WIDE)
        packed = pl.pallas_call(
            block_kernel,
            out_shape=(
                jax.ShapeDtypeStruct((512, LANES), BF16), full(512, LANES), full(ROWS, WIDE), full(ROWS, LANES),
                full(16, LANES),
            ),
            in_specs=[smem] * 2 + [vmem] * 22,
            out_specs=(vmem,) * 5,
            scratch_shapes=[
                low(512, LANES), buf(8, LANES), buf(160, LANES), buf(8, 32, LANES),
                low(N_CHAN, 512, 128), low(2, 4, 512, 256), low(N_CHAN, 512, 128), low(2, 4, 512, 256),
                low(2, ROWS, LANES), low(N_CHAN, 256, LANES), low(8, 256, LANES), low(8, 2, 256, LANES), low(2, ROWS, LANES),
                low(4, 2, 256, 256), buf(2, 256, LANES), buf(2, ROWS, LANES), buf(256, LANES),
                low(N_CHAN, ROWS, LANES), low(N_CHAN, ROWS, LANES), buf(24, LANES), buf(N_CHAN, 24, LANES),
                low(N_CHAN, HALF, LANES), low(N_CHAN, HALF, LANES), low(N_CHAN, HALF, LANES), low(N_CHAN, HALF, LANES),
                low(N_CHAN, 144, LANES), low(N_CHAN, 144, LANES),
                buf(16, LANES), buf(N_CHAN, 16, LANES), buf(N_CHAN, 8, LANES),
                buf(144, LANES), low(144, LANES), low(3, 144, LANES), buf(64, 256), buf(4, 64, 256), buf(4, 64, 256), buf(4, 64, 256),
                buf(*big), buf(*big), buf(*big), buf(*big), low(2, *wide), buf(*wide), buf(*wide), buf(*wide), buf(*big),
                buf(10, 32, LANES), buf(2, 16, QUARTER, LANES), buf(2, 16, QUARTER, LANES), buf(10, 32, LANES),
                buf(64, 256), buf(256, 256),
                buf(*big), buf(*big), buf(*big), buf(*big), low(ROWS, 512), low(2, ROWS, 512), low(2, ROWS, 512),
                buf(2, ROWS, 512), buf(2, ROWS, 512), low(2, ROWS, 512), low(2, ROWS, 512),
                low(N_CHAN, ROWS, LANES), low(4, 256, 256), low(4, 256, 256), low(512, ROWS), low(512, 256), low(512, 256),
                dma((2, 8)), dma((2, 8)), dma, dma, dma, dma, dma((9,)), dma((9,)), dma, dma, dma((4,)), dma((4,)),
                dma((2, 8)), dma((2, 8)), dma, dma, dma, dma, dma((4,)), dma((4,)), dma, dma,
                dma((7, 7)), dma((7, 7)), dma((3,)), dma((3,)), dma((2, 3)), dma((2, 3)),
            ],
            compiler_params=pltpu.CompilerParams(
                collective_id=0, has_side_effects=True, vmem_limit_bytes=60 * 1024 * 1024
            ),
            name="block",
        )(
            bucket, items, tokens.T, cotangent.T, gain1, bias1, jnp.swapaxes(modes, 1, 2), log_dt, skip,
            w_a.T, b_a, w_b.T, b_b, gain2, bias2,
            w_up, b_up, w_down, b_down, levels, constant, mats, twiddle, wave,
        )
        small = full(HALF)
        results = pl.pallas_call(
            unpack_kernel,
            out_shape=(
                jax.ShapeDtypeStruct((HALF, TOK_DEV), BF16), full(HALF, TOK_DEV), small, small, full(8, 32, HALF),
                small, small, full(HALF, ROWS), small, full(HALF, ROWS), small, small, small, full(ROWS, 256),
                full(256), full(256, ROWS), small,
            ),
            in_specs=[vmem] * 6,
            out_specs=(vmem,) * 17,
            name="unpack",
        )(*packed, cotangent.T)
        turned = {0, 1, 4, 7, 9}
        return tuple(jnp.swapaxes(r, -1, -2) if i in turned else r for i, r in enumerate(results))

    return run


def solution(mesh):
    small = mesh.shape["chan"] == N_CHAN and mesh.shape["dp"] == 4
    return jax.shard_map(
        block_program() if small else shards,
        mesh=mesh,
        in_specs=(
            P("dp", "chan"),
            P("dp", "chan"),
            P("dp"),
            P("dp"),
            P("chan"),
            P("chan"),
            P(None, "chan", None),
            P("chan"),
            P("chan"),
            P("dp", "chan"),
            P("chan"),
            P("dp", "chan"),
            P("chan"),
            P("chan"),
            P("chan"),
            P("dp", "chan"),
            P("chan"),
            P("chan", "dp"),
            P("chan"),
        ),
        out_specs=(
            P("dp", "chan"),
            P("dp", "chan"),
            P("chan"),
            P("chan"),
            P(None, "chan", None),
            P("chan"),
            P("chan"),
            P("dp", "chan"),
            P("chan"),
            P("dp", "chan"),
            P("chan"),
            P("chan"),
            P("chan"),
            P("dp", "chan"),
            P("chan"),
            P("chan", "dp"),
            P("chan"),
        ),
        check_vma=False,
    )
```

```python
import math

import jax
import jax.numpy as jnp
import ml_dtypes
import numpy as np
from jax import lax
from jax.experimental import pallas as pl
from jax.experimental.pallas import tpu as pltpu
from jax.sharding import PartitionSpec as P

MODEL_WIDTH = 512
TOK_DEV = 1024


HIGHEST = lax.Precision.HIGHEST
EPSILON = 1e-05


def product(left, right):
    return jnp.dot(left, right, preferred_element_type=jnp.float32)


def product_nt(left, right):
    return lax.dot_general(
        left, right, (((1,), (1,)), ((), ())), preferred_element_type=jnp.float32
    )


def product_tn(left, right):
    return lax.dot_general(
        left, right, (((0,), (0,)), ((), ())), preferred_element_type=jnp.float32
    )


def gelu_slope(values):
    return (
        0.5 * (1.0 + lax.erf(values * 0.7071067811865476))
        + values * jnp.exp(-0.5 * values * values) * 0.3989422804014327
    )


def half_angles(length):
    angle = np.arange(length // 2 + 1, dtype=np.float64) * (math.pi / length)
    cosine, sine = np.cos(angle), np.sin(angle)
    cosine[-1] = 0.0
    return cosine.astype(np.float32), sine.astype(np.float32)


def inverse_tables(length):
    freq = np.arange(length // 2 + 1)
    turn = (freq[:, None] * np.arange(length)[None, :]) % length * (2.0 * math.pi / length)
    weight = np.where((freq == 0) | (freq == length // 2), 1.0, 2.0)[:, None] / length
    return (weight * np.cos(turn)).astype(np.float32), (weight * np.sin(turn)).astype(np.float32)


def high_einsum(form, left, right):
    return jnp.einsum(form, left, right, precision=HIGHEST)


def ssm_kernel(modes, log_dt):
    cos_h, sin_h = half_angles(TOK_DEV)
    index = jnp.arange(modes.shape[2], dtype=jnp.int32).astype(jnp.float32)
    lam_re = -0.5 * jnp.exp(modes[0])
    lam_im = math.pi * (index + modes[1])
    rank_re, rank_im, in_re, in_im, out_re, out_im = (modes[i] for i in range(2, 8))
    sigma = (2.0 * jnp.exp(-log_dt))[:, None]

    def points(values):
        return values.T[:, None, :]

    den_re = points(lam_re * lam_re + lam_im * lam_im) * (cos_h * cos_h)[:, None] - (
        sigma * sigma
    ).T * (sin_h * sin_h)[:, None]
    den_im = points(-2.0 * sigma * lam_re) * (sin_h * cos_h)[:, None]
    den_sq = den_re * den_re + den_im * den_im
    inv_re = den_re / den_sq
    inv_im = -den_im / den_sq
    sums = []
    for real, imag in (
        (out_re * in_re + out_im * in_im, out_re * in_im - out_im * in_re),
        (out_re * rank_re + out_im * rank_im, out_re * rank_im - out_im * rank_re),
        (rank_re * in_re + rank_im * in_im, rank_re * in_im - rank_im * in_re),
        (rank_re * rank_re + rank_im * rank_im, jnp.zeros_like(rank_re)),
    ):
        turned = points(real * lam_re + imag * lam_im)
        real = points(real)
        p_re, p_im = jnp.sum(real * inv_re, axis=0), jnp.sum(real * inv_im, axis=0)
        q_re, q_im = jnp.sum(turned * inv_re, axis=0), jnp.sum(turned * inv_im, axis=0)
        sine = sin_h[:, None] * sigma.T
        sums.append((-sine * p_im - cos_h[:, None] * q_re, sine * p_re - cos_h[:, None] * q_im))
    (cross_re, cross_im), (left_re, left_im), (right_re, right_im), (self_re, self_im) = sums
    twice = 2.0 * cos_h[:, None]
    loop_re, loop_im = 1.0 + twice * self_re, twice * self_im
    back_re, back_im = twice * right_re, twice * right_im
    loop_sq = loop_re * loop_re + loop_im * loop_im
    ratio_re = (back_re * loop_re + back_im * loop_im) / loop_sq
    ratio_im = (back_im * loop_re - back_re * loop_im) / loop_sq
    part_re = cross_re - (left_re * ratio_re - left_im * ratio_im)
    part_im = cross_im - (left_re * ratio_im + left_im * ratio_re)
    spec_re = 2.0 * (cos_h[:, None] * part_re - sin_h[:, None] * part_im)
    spec_im = 2.0 * (cos_h[:, None] * part_im + sin_h[:, None] * part_re)
    cos_tab, sin_tab = inverse_tables(TOK_DEV)
    return high_einsum("kl,kc->lc", cos_tab, spec_re) - high_einsum("kl,kc->lc", sin_tab, spec_im)


BLOCK = 128
BLOCKS = TOK_DEV // BLOCK
FIRST = 2 * BLOCKS
KEPT = FIRST // 2 + 1


def transform_tables():
    length = 2 * TOK_DEV
    turn = np.arange(KEPT)[:, None] * np.arange(BLOCK)[None, :] * (2.0 * math.pi / length)
    small = np.arange(BLOCK)[:, None] * np.arange(BLOCK)[None, :] % BLOCK * (2.0 * math.pi / BLOCK)
    spots = np.stack([np.arange(BLOCKS) + np.arange(BLOCKS) // (2 << b) * (2 << b) for b in range(3)])
    angle = spots[:, None, :] * np.arange(KEPT)[None, :, None] % FIRST * (2.0 * math.pi / FIRST)
    parts = (np.cos(turn), np.sin(turn), np.cos(small), np.sin(small), np.cos(angle), np.sin(angle))
    return [part.astype(np.float32) for part in parts]


def forward_transform(blocks, cos_a, sin_a):
    cos_t, sin_t, cos_s, sin_s, _, _ = transform_tables()
    step_re = high_einsum("ka,abc->kbc", cos_a, blocks)
    step_im = -high_einsum("ka,abc->kbc", sin_a, blocks)
    turned_re = step_re * cos_t[..., None] + step_im * sin_t[..., None]
    turned_im = step_im * cos_t[..., None] - step_re * sin_t[..., None]
    both = jnp.concatenate([turned_re, turned_im], axis=1)
    matrix = np.block([[cos_s, sin_s], [-sin_s, cos_s]])
    return high_einsum("pb,kbc->kpc", matrix, both)


def inverse_transform(spectrum, cos_a, sin_a):
    cos_t, sin_t, cos_s, sin_s, _, _ = transform_tables()
    matrix = np.block([[cos_s, -sin_s], [sin_s, cos_s]])
    both = high_einsum("bp,kpc->kbc", matrix, spectrum)
    step_re, step_im = both[:, :BLOCK], both[:, BLOCK:]
    turned_re = step_re * cos_t[..., None] - step_im * sin_t[..., None]
    turned_im = step_im * cos_t[..., None] + step_re * sin_t[..., None]
    weight = np.where(np.arange(KEPT) % (KEPT - 1) == 0, 1.0, 2.0).astype(np.float32) / (2 * TOK_DEV)
    return high_einsum("ka,kbc->abc", cos_a * weight[:, None], turned_re) - high_einsum(
        "ka,kbc->abc", sin_a * weight[:, None], turned_im
    )


def multiply(left, right):
    left_re, left_im = left[:, :BLOCK], left[:, BLOCK:]
    right_re, right_im = right[:, :BLOCK], right[:, BLOCK:]
    return jnp.concatenate(
        [left_re * right_re - left_im * right_im, left_re * right_im + left_im * right_re], axis=1
    )


def mixer(normed, kernel_taps, skip_gain, bucket, filled):
    _, _, _, _, cos_a, sin_a = transform_tables()
    cos_x, sin_x = jnp.asarray(cos_a)[bucket], jnp.asarray(sin_a)[bucket]
    item_blocks = 2 << bucket
    block_id = jnp.arange(BLOCKS, dtype=jnp.int32)[:, None, None]
    taps = jnp.where(block_id < item_blocks, kernel_taps.reshape(BLOCKS, BLOCK, -1), 0.0)
    signal = forward_transform(normed.reshape(BLOCKS, BLOCK, -1), cos_x, sin_x)
    answer = forward_transform(taps, cos_a[2], sin_a[2])
    result = inverse_transform(multiply(signal, answer), cos_x, sin_x)
    result = jnp.where(block_id < filled * item_blocks, result, 0.0)
    return result.reshape(normed.shape) + skip_gain * normed


def shards(
    tokens,
    cotangent,
    group_bucket,
    group_items,
    first_norm_gain,
    first_norm_bias,
    modes,
    log_dt,
    d_skip,
    w_a,
    b_a,
    w_b,
    b_b,
    second_norm_gain,
    second_norm_bias,
    w_up,
    b_up,
    w_down,
    b_down,
):
    input_tokens = tokens.astype(jnp.float32)
    sums_in = lax.psum(
        (jnp.sum(input_tokens, axis=1), jnp.sum(input_tokens * input_tokens, axis=1)), "chan"
    )
    input_average = sums_in[0][:, None] / MODEL_WIDTH
    input_inverse_deviation = lax.rsqrt(
        sums_in[1][:, None] / MODEL_WIDTH - input_average * input_average + EPSILON
    )
    input_standardized = (input_tokens - input_average) * input_inverse_deviation
    input_normalized = input_standardized * first_norm_gain + first_norm_bias
    level = group_bucket[0]
    filled = group_items[0]
    kernel_taps, kernel_back = jax.vjp(ssm_kernel, modes, log_dt)

    def local_mix(values, taps_now, skip_gain):
        return mixer(values, taps_now, skip_gain, level, filled)

    mixed, mix_back = jax.vjp(local_mix, input_normalized, kernel_taps, d_skip)
    acts_low = jax.nn.gelu(mixed, approximate=False).astype(jnp.bfloat16)
    wa_full, wb_full, up_full, down_full = (
        lax.all_gather(w_a.astype(jnp.bfloat16), "dp", axis=0, tiled=True),
        lax.all_gather(w_b.astype(jnp.bfloat16), "dp", axis=0, tiled=True),
        lax.all_gather(w_up.astype(jnp.bfloat16), "dp", axis=0, tiled=True),
        lax.all_gather(w_down.astype(jnp.bfloat16), "dp", axis=1, tiled=True),
    )
    acts_full = lax.all_gather(acts_low, "chan", axis=1, tiled=True)
    gate_a = product(acts_full, wa_full) + b_a
    gate_b = product(acts_full, wb_full) + b_b
    gate_sig = jax.nn.sigmoid(gate_b)
    residual_stream = input_tokens + gate_a * gate_sig
    sums_mid = lax.psum(
        (jnp.sum(residual_stream, axis=1), jnp.sum(residual_stream * residual_stream, axis=1)),
        "chan",
    )
    middle_average = sums_mid[0][:, None] / MODEL_WIDTH
    middle_inverse_deviation = lax.rsqrt(
        sums_mid[1][:, None] / MODEL_WIDTH - middle_average * middle_average + EPSILON
    )
    middle_standardized = (residual_stream - middle_average) * middle_inverse_deviation
    middle_reduced = (middle_standardized * second_norm_gain + second_norm_bias).astype(
        jnp.bfloat16
    )
    mid_full = lax.all_gather(middle_reduced, "chan", axis=1, tiled=True)
    pre_act = product(mid_full, up_full) + b_up
    hidden_low = jax.nn.gelu(pre_act, approximate=False).astype(jnp.bfloat16)
    branch = (
        lax.psum_scatter(product(hidden_low, down_full), "chan", scatter_dimension=1, tiled=True)
        + b_down
    )
    output = (residual_stream + branch).astype(jnp.bfloat16)
    grad_f = cotangent.astype(jnp.bfloat16)
    grad_b_down = jnp.sum(grad_f.astype(jnp.float32), axis=0)
    grad_f_full = lax.all_gather(grad_f, "chan", axis=1, tiled=True)
    grad_w_down = product_tn(hidden_low, grad_f_full)
    grad_pre = (product_nt(grad_f_full, down_full) * gelu_slope(pre_act)).astype(jnp.bfloat16)
    grad_b_up = jnp.sum(grad_pre.astype(jnp.float32), axis=0)
    grad_w_up = product_tn(mid_full, grad_pre)
    middle_gradient = lax.psum_scatter(
        product_nt(grad_pre, up_full), "chan", scatter_dimension=1, tiled=True
    )
    second_norm_gain_gradient = jnp.sum(middle_gradient * middle_standardized, axis=0)
    grad_ln2_bias = jnp.sum(middle_gradient, axis=0)
    middle_rescaled = middle_gradient * second_norm_gain
    middle_backward = lax.psum(
        (jnp.sum(middle_rescaled, axis=1), jnp.sum(middle_rescaled * middle_standardized, axis=1)),
        "chan",
    )
    grad_resid = cotangent + middle_inverse_deviation * (
        middle_rescaled
        - middle_backward[0][:, None] / MODEL_WIDTH
        - middle_standardized * middle_backward[1][:, None] / MODEL_WIDTH
    )
    grad_a = (grad_resid * gate_sig).astype(jnp.bfloat16)
    grad_b = (grad_resid * gate_a * gate_sig * (1.0 - gate_sig)).astype(jnp.bfloat16)
    grad_b_a = jnp.sum(grad_a.astype(jnp.float32), axis=0)
    grad_b_b = jnp.sum(grad_b.astype(jnp.float32), axis=0)
    grad_w_a = product_tn(acts_full, grad_a)
    grad_w_b = product_tn(acts_full, grad_b)
    grad_acts = lax.psum_scatter(
        product_nt(grad_a, wa_full) + product_nt(grad_b, wb_full),
        "chan",
        scatter_dimension=1,
        tiled=True,
    )
    grad_mixed = grad_acts * gelu_slope(mixed)
    normalized_gradient, grad_kernel, grad_skip = mix_back(grad_mixed)
    grad_modes, grad_log_dt = kernel_back(grad_kernel)
    first_norm_gain_gradient = jnp.sum(normalized_gradient * input_standardized, axis=0)
    grad_ln1_bias = jnp.sum(normalized_gradient, axis=0)
    input_rescaled = normalized_gradient * first_norm_gain
    input_backward = lax.psum(
        (jnp.sum(input_rescaled, axis=1), jnp.sum(input_rescaled * input_standardized, axis=1)),
        "chan",
    )
    grad_tokens = grad_resid + input_inverse_deviation * (
        input_rescaled
        - input_backward[0][:, None] / MODEL_WIDTH
        - input_standardized * input_backward[1][:, None] / MODEL_WIDTH
    )
    grad_w_a, grad_w_b, grad_w_up, grad_w_down = (
        lax.psum_scatter(grad_w_a, "dp", scatter_dimension=0, tiled=True),
        lax.psum_scatter(grad_w_b, "dp", scatter_dimension=0, tiled=True),
        lax.psum_scatter(grad_w_up, "dp", scatter_dimension=0, tiled=True),
        lax.psum_scatter(grad_w_down, "dp", scatter_dimension=1, tiled=True),
    )
    (
        first_norm_gain_gradient,
        grad_ln1_bias,
        grad_modes,
        grad_log_dt,
        grad_skip,
        grad_b_a,
        grad_b_b,
        second_norm_gain_gradient,
        grad_ln2_bias,
        grad_b_up,
        grad_b_down,
    ) = lax.psum(
        (
            first_norm_gain_gradient,
            grad_ln1_bias,
            grad_modes,
            grad_log_dt,
            grad_skip,
            grad_b_a,
            grad_b_b,
            second_norm_gain_gradient,
            grad_ln2_bias,
            grad_b_up,
            grad_b_down,
        ),
        "dp",
    )
    return (
        output,
        grad_tokens,
        first_norm_gain_gradient,
        grad_ln1_bias,
        grad_modes,
        grad_log_dt,
        grad_skip,
        grad_w_a,
        grad_b_a,
        grad_w_b,
        grad_b_b,
        second_norm_gain_gradient,
        grad_ln2_bias,
        grad_w_up,
        grad_b_up,
        grad_w_down,
        grad_b_down,
    )


LANES = 128
HALF = 64
PAIRS = 4
ROWS = 128
N_CHAN = 8
WIDE = 640
MESH = pl.DeviceIdType.MESH
F32 = jnp.float32
BF16 = jnp.bfloat16


def split_two(matrix):
    high = matrix.astype(ml_dtypes.bfloat16)
    low = (matrix - high.astype(np.float64)).astype(ml_dtypes.bfloat16)
    return np.concatenate([high, low], axis=1)


def lane_rows(values_low, values_high):
    return np.repeat(np.stack([values_low, values_high], -1), HALF, axis=-1)


def mixer_tables():
    line = np.arange(ROWS)
    small = np.outer(line, line) % ROWS * (2.0 * math.pi / ROWS)
    cos_s, sin_s = np.cos(small), np.sin(small)
    forward = np.block([[cos_s, sin_s], [-sin_s, cos_s]])
    real = np.zeros((2 * ROWS, 2 * ROWS))
    for row in range(HALF):
        weight = 1.0 if row == 0 else 2.0
        turn = 2.0 * math.pi / ROWS * row * line
        real[:ROWS, row] = weight * np.cos(turn)
        real[:ROWS, ROWS + row] = -weight * np.sin(turn)
        turn = 2.0 * math.pi / TOK_DEV * (4 + 8 * row) * line
        real[ROWS:, HALF + row] = 2.0 * np.cos(turn)
        real[ROWS:, ROWS + HALF + row] = -2.0 * np.sin(turn)
    mats = np.stack([split_two(m) for m in (forward, forward.T, real, real.T)])

    twiddle = []
    for pair in range(5):
        turn = np.stack([line * k * (math.pi / TOK_DEV) for k in (2 * pair, 2 * pair + 1)])
        twiddle += [lane_rows(np.cos(turn[0]), np.cos(turn[1])), lane_rows(np.sin(turn[0]), np.sin(turn[1]))]
    for first, second in ((1, 2), (3, 0)):
        turn = np.stack([line * k * (2.0 * math.pi / TOK_DEV) for k in (first, second)])
        twiddle += [lane_rows(np.cos(turn[0]), np.cos(turn[1])), lane_rows(np.sin(turn[0]), np.sin(turn[1]))]

    def forward_rows(coef, pairs):
        out = []
        for low, high in pairs:
            for part in range(2):
                for j in range(PAIRS):
                    out.append(lane_rows(coef(2 * j, low, part), coef(2 * j + 1, high, part)))
                for j in range(PAIRS):
                    out.append(lane_rows(coef(2 * j, high, part), coef(2 * j + 1, low, part)))
        return np.stack(out)

    def inverse_rows(coef, pairs):
        out = []
        for low, high in pairs:
            for part in range(2):
                for j in range(PAIRS):
                    out.append(lane_rows(coef(2 * j, low, part), coef(2 * j + 1, high, part)))
                for j in range(PAIRS):
                    out.append(lane_rows(coef(2 * j + 1, low, part), coef(2 * j, high, part)))
        return np.stack(out)

    levels = []
    pairs = [(2 * p, 2 * p + 1) for p in range(5)]
    for level in range(3):
        item = 2 << level

        def angle(block, k):
            return 2.0 * math.pi / 16 * ((block + block // item * item) * k % 16)

        def fwd(block, k, part):
            if k > 8:
                return np.zeros(())
            return np.cos(angle(block, k)) if part == 0 else -np.sin(angle(block, k))

        def inv(block, k, part):
            weight = (1.0 if k in (0, 8) else 2.0) / (2 * TOK_DEV)
            return weight * fwd(block, k, part)

        levels.append(np.concatenate([forward_rows(fwd, pairs), inverse_rows(inv, pairs)]))

    def taps(block, k, part):
        if k == 0:
            return np.asarray((1.0 if part == 0 else (-1.0) ** block) / TOK_DEV)
        turn = 2.0 * math.pi / 8 * (block * k % 8)
        return np.asarray((np.cos(turn) if part == 0 else -np.sin(turn)) * 2.0 / TOK_DEV)

    tap_pairs = [(1, 2), (3, 0)]
    taps_back = forward_rows(taps, tap_pairs)
    taps_rows = inverse_rows(taps, tap_pairs)
    freq_even = np.where(line < HALF, 8 * line, 4 + 8 * (line - HALF))
    half_angle = np.stack(
        [lane_rows(1 + 8 * line, 2 + 8 * line), lane_rows(3 + 8 * line, freq_even)]
    ) * (math.pi / TOK_DEV)
    wave = np.stack([np.cos(half_angle), np.sin(half_angle)])
    return (
        mats,
        np.stack(twiddle).astype(np.float32),
        np.stack(levels).astype(np.float32),
        np.concatenate([levels[2], taps_rows, taps_back]).astype(np.float32),
        wave.astype(np.float32),
    )


def low_lanes(rows):
    return lax.broadcasted_iota(jnp.int32, (rows, LANES), 1) < HALF


def turn_half(values):
    return pltpu.roll(values, HALF, 1)


def split_pair(values):
    upper, lower = values[:HALF], values[HALF:]
    mask = low_lanes(HALF)
    return jnp.where(mask, upper, turn_half(lower)), jnp.where(mask, turn_half(upper), lower)


def join_pair(first, second):
    mask = low_lanes(HALF)
    return jnp.concatenate(
        [jnp.where(mask, first, turn_half(second)), jnp.where(mask, turn_half(first), second)], axis=0
    )


def interleave(first, second):
    mask = low_lanes(first.shape[0])
    return jnp.where(mask, first, turn_half(second)), jnp.where(mask, turn_half(first), second)


def fold(values):
    return values + turn_half(values)


def reciprocal(values):
    guess = pl.reciprocal(values, approx=True)
    return guess * (2.0 - values * guess)


ERF_TERMS = (1.061405429, -1.453152027, 1.421413741, -0.284496736, 0.254829592)


def normal_parts(values):
    bell = jnp.exp(-0.5 * values * values)
    t = reciprocal(1.0 + (0.3275911 * 0.7071067811865476) * jnp.abs(values))
    tail = ERF_TERMS[0]
    for term in ERF_TERMS[1:]:
        tail = tail * t + term
    tail = 0.5 * (tail * t) * bell
    return jnp.where(values < 0.0, tail, 1.0 - tail), bell * 0.3989422804014327


def column_sum(values):
    return jnp.sum(values, axis=0, keepdims=True)


def dot_nt(left, right):
    return lax.dot_general(left, right, (((1,), (1,)), ((), ())), preferred_element_type=F32)


def dot_nn(left, right):
    return jnp.dot(left, right, preferred_element_type=F32)


def store_split(ref, row, lane, values, exact=True):
    high = values.astype(BF16)
    place = (pl.ds(row, values.shape[0]), pl.ds(lane, values.shape[1]))
    ref[(0,) + place] = high
    if exact:
        ref[(1,) + place] = (values - high.astype(F32)).astype(BF16)


def split_product(mat_ref, which, rhs_ref, lane, width, exact=True):
    high = mat_ref[which, :, 0:256]
    low = mat_ref[which, :, 256:512]
    rhs_high = rhs_ref[0, :, lane : lane + width]
    product = dot_nn(high, rhs_high) + dot_nn(low, rhs_high)
    if exact:
        product = product + dot_nn(high, rhs_ref[1, :, lane : lane + width])
    return product


CHUNK = 32


def over_chunks(body, size=CHUNK, first=0, rows=ROWS):
    def step(index, carry):
        body(pl.multiple_of(first + index * size, size))
        return carry

    lax.fori_loop(0, rows // size, step, 0)


def spread_pairs(src, coef_ref, base, twiddle_ref, twiddle_base, pairs, rhs_ref, exact=True):
    def body(row):
        rows = pl.ds(row, CHUNK)
        blocks = [src(j, rows) for j in range(PAIRS)]
        for pair in range(pairs):
            parts = []
            for part in range(2):
                at = base + (pair * 2 + part) * 8
                straight = sum(blocks[j] * coef_ref[at + j : at + j + 1, :] for j in range(PAIRS))
                crossed = sum(blocks[j] * coef_ref[at + 4 + j : at + 5 + j, :] for j in range(PAIRS))
                parts.append(straight + turn_half(crossed))
            cosine = twiddle_ref[twiddle_base + 2 * pair, rows, :]
            sine = twiddle_ref[twiddle_base + 2 * pair + 1, rows, :]
            store_split(rhs_ref, row, pair * LANES, parts[0] * cosine + parts[1] * sine, exact)
            store_split(rhs_ref, row + ROWS, pair * LANES, parts[1] * cosine - parts[0] * sine, exact)

    over_chunks(body)


def gather_pairs(values_ref, coef_ref, base, twiddle_ref, twiddle_base, pairs, store):
    def body(row):
        rows = pl.ds(row, CHUNK)
        straight, crossed = [0.0] * PAIRS, [0.0] * PAIRS
        for pair in range(pairs):
            lanes = slice(pair * LANES, (pair + 1) * LANES)
            real, imag = values_ref[rows, lanes], values_ref[pl.ds(row + ROWS, CHUNK), lanes]
            cosine = twiddle_ref[twiddle_base + 2 * pair, rows, :]
            sine = twiddle_ref[twiddle_base + 2 * pair + 1, rows, :]
            for part, value in enumerate((real * cosine - imag * sine, imag * cosine + real * sine)):
                at = base + (pair * 2 + part) * 8
                for j in range(PAIRS):
                    straight[j] = straight[j] + value * coef_ref[at + j : at + j + 1, :]
                    crossed[j] = crossed[j] + value * coef_ref[at + 4 + j : at + 5 + j, :]
        for j in range(PAIRS):
            store(j, rows, straight[j] + turn_half(crossed[j]))

    over_chunks(body)


GROUPS = ((0, 256), (256, 256), (512, 128))


def transform_into(dst_ref, mat_ref, which, rhs_ref, exact=True):
    for lane, width in GROUPS:
        dst_ref[:, lane : lane + width] = split_product(mat_ref, which, rhs_ref, lane, width, exact)


def multiply_spectra(left_ref, right_ref, rhs_ref, conjugate, exact=True):
    def body(row):
        top, bottom = pl.ds(row, CHUNK), pl.ds(row + ROWS, CHUNK)
        for pair in range(5):
            lanes = slice(pair * LANES, (pair + 1) * LANES)
            a_re, a_im = left_ref[top, lanes], left_ref[bottom, lanes]
            b_re, b_im = right_ref[top, lanes], right_ref[bottom, lanes]
            if conjugate:
                out_re, out_im = a_re * b_re + a_im * b_im, a_re * b_im - a_im * b_re
            else:
                out_re, out_im = a_re * b_re - a_im * b_im, a_re * b_im + a_im * b_re
            store_split(rhs_ref, row, pair * LANES, out_re, exact)
            store_split(rhs_ref, row + ROWS, pair * LANES, out_im, exact)

    over_chunks(body)


def pair_terms(modes_ref):
    rank_re, rank_im, in_re, in_im, out_re, out_im = (modes_ref[i] for i in range(2, 8))
    return (
        (out_re * in_re + out_im * in_im, out_re * in_im - out_im * in_re),
        (out_re * rank_re + out_im * rank_im, out_re * rank_im - out_im * rank_re),
        (rank_re * in_re + rank_im * in_im, rank_re * in_im - rank_im * in_re),
        (rank_re * rank_re + rank_im * rank_im, None),
    )


def mode_values(modes_ref):
    index = lax.broadcasted_iota(jnp.int32, modes_ref.shape[1:], 0).astype(F32)
    return -0.5 * jnp.exp(modes_ref[0]), math.pi * (index + modes_ref[1])


POINT_ROWS = 16


def resolvent(coef_ref, n, square_cos, cos_sin, scaled):
    den_re = coef_ref[8, pl.ds(n, 1), :] * square_cos - scaled
    den_im = coef_ref[9, pl.ds(n, 1), :] * cos_sin
    inverse = reciprocal(den_re * den_re + den_im * den_im)
    return den_re * inverse, -(den_im * inverse)


def complex_multiply(a_re, a_im, b_re, b_im):
    return a_re * b_re - a_im * b_im, a_re * b_im + a_im * b_re


def conj_multiply(a_re, a_im, b_re, b_im):
    return a_re * b_re + a_im * b_im, a_re * b_im - a_im * b_re


def combine(sums, sigma, cosine, sine):
    terms = []
    for p_re, p_im, q_re, q_im in (sums[4 * q : 4 * q + 4] for q in range(4)):
        swing = sigma * sine
        terms.append((-swing * p_im - cosine * q_re, swing * p_re - cosine * q_im))
    twice = 2.0 * cosine
    loop_re, loop_im = 1.0 + twice * terms[3][0], twice * terms[3][1]
    scale = reciprocal(loop_re * loop_re + loop_im * loop_im)
    inv = (loop_re * scale, -(loop_im * scale))
    ratio = complex_multiply(twice * terms[2][0], twice * terms[2][1], *inv)
    return terms, inv, ratio


QUARTER = 32


def cauchy_coefficients(modes_ref, sigma, coef_ref):
    lam_re, lam_im = mode_values(modes_ref)
    for q, (real, imag) in enumerate(pair_terms(modes_ref)):
        coef_ref[q] = real
        coef_ref[4 + q] = real * lam_re if imag is None else real * lam_re + imag * lam_im
    coef_ref[8] = lam_re * lam_re + lam_im * lam_im
    coef_ref[9] = -2.0 * sigma * lam_re


def wave_rows(wave_ref, pair, base, row):
    rows = pl.ds(pl.multiple_of(base + row, POINT_ROWS), POINT_ROWS)
    return wave_ref[0, pair, rows, :], wave_ref[1, pair, rows, :]


def cauchy_forward(index, sigma, coef_ref, wave_ref, base, sums_ref, spec_ref):
    sigma_sq = sigma * sigma
    pair, row = index // 2, index % 2 * POINT_ROWS
    rows = slice(row, row + POINT_ROWS)
    lanes = slice(pair * LANES, (pair + 1) * LANES)
    cosine, sine = wave_rows(wave_ref, pair, base, row)
    square_cos, cos_sin, scaled = cosine * cosine, cosine * sine, sigma_sq * (sine * sine)

    def add_mode(n, sums):
        sums = list(sums)
        for k in range(4):
            at = n * 4 + k
            inv_re, inv_im = resolvent(coef_ref, at, square_cos, cos_sin, scaled)
            for q in range(4):
                plain = coef_ref[q, pl.ds(at, 1), :]
                turned = coef_ref[4 + q, pl.ds(at, 1), :]
                sums[4 * q] = sums[4 * q] + plain * inv_re
                sums[4 * q + 1] = sums[4 * q + 1] + plain * inv_im
                sums[4 * q + 2] = sums[4 * q + 2] + turned * inv_re
                sums[4 * q + 3] = sums[4 * q + 3] + turned * inv_im
        return tuple(sums)

    zero = jnp.zeros((POINT_ROWS, LANES), F32)
    sums = lax.fori_loop(0, 8, add_mode, (zero,) * 16)
    for i in range(16):
        sums_ref[pair, i, rows, :] = sums[i]
    terms, _, ratio = combine(sums, sigma, cosine, sine)
    cut_re, cut_im = complex_multiply(*terms[1], *ratio)
    part_re, part_im = terms[0][0] - cut_re, terms[0][1] - cut_im
    spec_re, spec_im = complex_multiply(2.0 * cosine, 2.0 * sine, part_re, part_im)
    spec_ref[rows, lanes] = spec_re
    spec_ref[row + QUARTER : row + QUARTER + POINT_ROWS, lanes] = spec_im


PLACES = [(pair, row) for pair in range(2) for row in range(0, QUARTER, POINT_ROWS)]


def point_grads(sigma, wave_ref, base, sums_ref, spec_ref, grad_ref):
    zero = jnp.zeros((POINT_ROWS, LANES), F32)
    sigma_sum = zero
    for pair, row in PLACES:
        rows = slice(row, row + POINT_ROWS)
        lanes = slice(pair * LANES, (pair + 1) * LANES)
        cosine, sine = wave_rows(wave_ref, pair, base, row)
        sums = [sums_ref[pair, i, rows, :] for i in range(16)]
        terms, inv, ratio = combine(sums, sigma, cosine, sine)
        spec_re, spec_im = spec_ref[rows, lanes], spec_ref[row + QUARTER : row + QUARTER + POINT_ROWS, lanes]
        part = conj_multiply(2.0 * cosine, 2.0 * sine, spec_re, spec_im)
        left = conj_multiply(*ratio, *part)
        ratio_grad = conj_multiply(*terms[1], *part)
        back = conj_multiply(*inv, -ratio_grad[0], -ratio_grad[1])
        twice = 2.0 * cosine
        loop = conj_multiply(*ratio, *back)
        grads = (
            part,
            (-left[0], -left[1]),
            (twice * back[0], twice * back[1]),
            (-twice * loop[0], -twice * loop[1]),
        )
        swing = sigma * sine
        for q, (g_re, g_im) in enumerate(grads):
            grad_ref[pair, 4 * q, rows, :] = swing * g_im
            grad_ref[pair, 4 * q + 1, rows, :] = -swing * g_re
            grad_ref[pair, 4 * q + 2, rows, :] = -cosine * g_re
            grad_ref[pair, 4 * q + 3, rows, :] = -cosine * g_im
            sigma_sum = sigma_sum + sine * (g_im * sums[4 * q] - g_re * sums[4 * q + 1])
    return sigma_sum


def mode_sums(part, square_sum, sigma, coef_ref, wave_ref, base, grad_ref, back_ref):
    sigma_sq = sigma * sigma

    def mode(n, square_sum):
        plain = [coef_ref[q, pl.ds(n, 1), :] for q in range(4)]
        turned = [coef_ref[4 + q, pl.ds(n, 1), :] for q in range(4)]
        sums = [0.0] * 10
        for pair, row in PLACES:
            rows = slice(row, row + POINT_ROWS)
            cosine, sine = wave_rows(wave_ref, pair, base, row)
            square_cos, cos_sin, square_sin = cosine * cosine, cosine * sine, sine * sine
            inv_re, inv_im = resolvent(coef_ref, n, square_cos, cos_sin, sigma_sq * square_sin)
            grad_re, grad_im = 0.0, 0.0
            for q in range(4):
                p_re, p_im = grad_ref[pair, 4 * q, rows, :], grad_ref[pair, 4 * q + 1, rows, :]
                q_re, q_im = grad_ref[pair, 4 * q + 2, rows, :], grad_ref[pair, 4 * q + 3, rows, :]
                grad_re = grad_re + (plain[q] * p_re + turned[q] * q_re)
                grad_im = grad_im + (plain[q] * p_im + turned[q] * q_im)
                sums[q] = sums[q] + (p_re * inv_re + p_im * inv_im)
                sums[4 + q] = sums[4 + q] + (q_re * inv_re + q_im * inv_im)
            square_re = inv_re * inv_re - inv_im * inv_im
            square_im = 2.0 * inv_re * inv_im
            den_re, den_im = conj_multiply(square_re, square_im, grad_re, grad_im)
            sums[8] = sums[8] - den_re * square_cos
            sums[9] = sums[9] - den_im * cos_sin
            square_sum = square_sum + den_re * square_sin
        for i in range(10):
            back_ref[i, pl.ds(n, 1), :] = column_sum(sums[i])
        return square_sum

    return lax.fori_loop(part * 8, part * 8 + 8, mode, square_sum)


def mode_gradients(modes_ref, sigma, nyquist_grad, step, sigma_sum, square_sum, back_ref):
    plain_grad = [fold(back_ref[q]) for q in range(4)]
    turned_grad = [fold(back_ref[4 + q]) for q in range(4)]
    abs_grad, skew_grad = fold(back_ref[8]), fold(back_ref[9])
    lam_re, lam_im = mode_values(modes_ref)
    plain_grad[0] = plain_grad[0] + step * nyquist_grad
    rank_re, rank_im, in_re, in_im, out_re, out_im = (modes_ref[i] for i in range(2, 8))
    lam_re_grad = 2.0 * lam_re * abs_grad - 2.0 * sigma * skew_grad
    lam_im_grad = 2.0 * lam_im * abs_grad
    real_grad, imag_grad = [], []
    terms = pair_terms(modes_ref)
    for q, (real, imag) in enumerate(terms):
        lam_re_grad = lam_re_grad + turned_grad[q] * real
        if imag is not None:
            lam_im_grad = lam_im_grad + turned_grad[q] * imag
        real_grad.append(plain_grad[q] + turned_grad[q] * lam_re)
        imag_grad.append(turned_grad[q] * lam_im)
    r0, r1, r2, r3 = real_grad
    i0, i1, i2, _ = imag_grad
    grads = (
        lam_re_grad * lam_re,
        math.pi * lam_im_grad,
        r1 * out_re - i1 * out_im + r2 * in_re + i2 * in_im + 2.0 * r3 * rank_re,
        r1 * out_im + i1 * out_re + r2 * in_im - i2 * in_re + 2.0 * r3 * rank_im,
        r0 * out_re - i0 * out_im + r2 * rank_re - i2 * rank_im,
        r0 * out_im + i0 * out_re + r2 * rank_im + i2 * rank_re,
        r0 * in_re + i0 * in_im + r1 * rank_re + i1 * rank_im,
        r0 * in_im - i0 * in_re + r1 * rank_im - i1 * rank_re,
    )
    sigma_grad = (
        fold(column_sum(sigma_sum) + 2.0 * sigma * column_sum(square_sum))
        - 2.0 * column_sum(skew_grad * lam_re)
    )
    nyquist = step * column_sum(terms[0][0])
    return grads, nyquist * nyquist_grad - sigma * sigma_grad


def ring_place(chan):
    z, y = lax.div(chan, 2), lax.rem(chan, 2)
    return z + y * (7 - 2 * z)


def ring_chan(place):
    back = lax.div(place, 4)
    z = place * (1 - back) + (7 - place) * back
    return 2 * z + back


TURNS = (1, -1)


def block_kernel(
    bucket_ref, items_ref, tokens_ref, cotangent_ref, gain1_ref, bias1_ref, raw_modes_ref, log_dt_ref, skip_ref,
    wa_ref, ba_ref, wb_ref, bb_ref, gain2_ref, bias2_ref, up_ref, bup_ref, down_ref, bdown_ref,
    levels_ref, coefc_ref, mat_ref, tw_ref, wave_ref,
    out_ref, dtok_ref, gw_ref, gm_ref, gv_ref,
    tok_ref, aux_ref, coefl_ref, modes_ref,
    wab_ref, wh_ref, gab_w_ref, gh_ref,
    stage_ref, sib_ab_ref, ring_ab_ref, ring_h_ref, part_ab_ref, cross_ref, keep_ref, swap_ref, gate_total_ref,
    in_send, in_recv, head_send, head_recv, acts_send, acts_recv, back_send, back_recv, late_send, late_recv,
    sum_send, sum_recv, tail_send, dp_send, dp_low, dp_recv, spec_send, spec_recv, sgrad_send, sgrad_recv,
    hat_ref, norm_ref, slope_ref, conv_ref, rhs_ref, freq_ref, sig_ref, ans_ref, taps_ref,
    mcoef_ref, sums_ref, pgrad_ref, mback_ref, sgrad_ref, taps_freq_ref,
    gate_ref, swish_ref, res_ref, hat2_ref, acts_ref, norm2_ref, gradf_ref, branch_ref, back2_ref, half_send, half_recv,
    gab_ref, hid_ref, gpre_ref, acts_t_ref, norm2_t_ref, gradf_t_ref,
    gring_ss, gring_rs, gsib_ss, gsib_rs, gx_ss, gx_rs, gdx_ss, gdx_rs, gswap_ss, gswap_rs, core_ss, core_rs,
    rring_ss, rring_rs, rsib_ss, rsib_rs, rx_ss, rx_rs, rdx_ss, rdx_rs, rswap_ss, rswap_rs,
    a2a_ss, a2a_rs, dp_ss, dp_rs, spec_ss, spec_rs,
):
    dp, chan = lax.axis_index("dp"), lax.axis_index("chan")
    core = lax.rem(dp, 2)
    sibling = dp + 1 - 2 * core
    place = ring_place(chan)
    spots = [lax.rem(place + offset, 8) if offset else place for offset in range(8)]
    around = [ring_chan(spot) if offset else chan for offset, spot in enumerate(spots)]
    groups = [lax.rem(spot, 4) for spot in spots]
    group_lanes = [pl.multiple_of(lax.div(spot, 4) * LANES, LANES) for spot in spots]
    nexts = [around[1], around[7]]
    chan_peers = [chan] + [lax.rem(chan + r, N_CHAN) for r in range(1, N_CHAN)]
    dp_peers = [dp] + [lax.rem(dp + r, 4) for r in range(1, 4)]
    across = dp_peers[2]

    def chan_at(offset):
        return around[offset % 8]

    barrier = pltpu.get_barrier_semaphore()
    for r in range(1, N_CHAN):
        pl.semaphore_signal(barrier, inc=1, device_id={"chan": chan_peers[r]}, device_id_type=MESH)
    for r in range(1, 4):
        pl.semaphore_signal(barrier, inc=1, device_id={"dp": dp_peers[r]}, device_id_type=MESH)

    pending = []

    def remote(src, dst, send_sem, recv_sem, **device):
        return pltpu.make_async_remote_copy(
            src_ref=src, dst_ref=dst, send_sem=send_sem, recv_sem=recv_sem, device_id=device, device_id_type=MESH
        )

    def send(*args, **device):
        copy = remote(*args, **device)
        copy.start()
        pending.append(copy)

    def exchange(which, source, recv_ref):
        def copy(r):
            peer = chan_peers[r]
            return remote(
                source(peer), recv_ref.at[chan], a2a_ss.at[which, r - 1], a2a_rs.at[which, r - 1], chan=peer
            )

        def start():
            for r in range(1, N_CHAN):
                copy(r).start()

        def wait():
            for r in range(1, N_CHAN):
                copy(r).wait_recv()

        def finish():
            for r in range(1, N_CHAN):
                copy(r).wait_send()

        return start, wait, finish

    def rows_at(number, count):
        return pl.ds(pl.multiple_of(number, ROWS), count)

    def launch(copy):
        copy.start()
        pending.append(copy)

    own_row = dp * ROWS
    pair_row = (dp - core) * ROWS
    away_row = 2 * ROWS - pair_row
    gate_row, gate_away = (core * 2 + lax.div(dp, 2)) * ROWS, (core * 2 + 1 - lax.div(dp, 2)) * ROWS
    gate_pair, gate_other = core * 2 * ROWS, (1 - core) * 2 * ROWS
    half_lanes = pl.multiple_of(core * LANES, LANES)
    other_lanes = pl.multiple_of((1 - core) * LANES, LANES)

    def gate_view(ref):
        return lambda offset, row, count: ref.at[around[offset % 8], rows_at(row, count), :]

    def hidden_view(ref):
        return lambda offset, row, count: ref.at[
            :, groups[offset % 8], rows_at(row, count), pl.ds(group_lanes[offset % 8], LANES)
        ]

    class Ring:
        def __init__(self, which, view, base, count, hook=None):
            self.which, self.view, self.base, self.count, self.hook = which, view, base, count, hook

        def piece(self, turn, step, base):
            half = self.count // 2
            if step == 4:
                return self.view(4, base + turn * half, half)
            return self.view(-TURNS[turn] * step, base, self.count)

        def copy(self, turn, step, ref):
            slot = turn * 4 + step - 1
            return remote(ref, ref, gring_ss.at[self.which, slot], gring_rs.at[self.which, slot], chan=nexts[turn])

        def send(self, turn, step):
            half = self.count // 2
            if step == 4:
                ref = self.view(-TURNS[turn] * 3, self.base + turn * half, half)
            else:
                ref = self.piece(turn, step - 1, self.base)
            launch(self.copy(turn, step, ref))

        def start(self):
            for turn in range(2):
                self.send(turn, 1)

        def step(self, step):
            for turn in range(2):
                self.copy(turn, step, self.piece(turn, step, self.base)).wait_recv()
                if step < 4:
                    self.send(turn, step + 1)
                if self.hook:
                    self.hook(turn, step)

    def slot_of(turn, step):
        return turn * 4 + step - 1 if step else 8

    def gate_sib(base):
        ref = wab_ref.at[:, rows_at(base, 256), :]
        return remote(ref, ref, gsib_ss, gsib_rs, dp=sibling)

    def gate_spread():
        launch(gate_sib(gate_pair))

    def hidden_cross(which, turn, step, base):
        ref, slot = hidden_rings[which].piece(turn, step, base), slot_of(turn, step)
        return remote(ref, ref, gdx_ss.at[which, slot], gdx_rs.at[which, slot], dp=across)

    gate_ring = Ring(0, gate_view(wab_ref), gate_pair, 256)
    def hidden_part(which):
        def view(offset, row, count):
            lanes = pl.ds(group_lanes[offset % 8], LANES)
            return wh_ref.at[which, groups[offset % 8], rows_at(row, count), lanes]

        return Ring(
            1 + which, view, pair_row, 256, lambda turn, step: launch(hidden_cross(which, turn, step, pair_row))
        )

    hidden_rings = up_ring, down_ring = hidden_part(0), hidden_part(1)

    def gate_over(row):
        ref = gate_ring.view(0, row, ROWS)
        return remote(ref, ref, gx_ss, gx_rs, dp=across)

    def swap_copy(row):
        return remote(stage_ref, hidden_view(wh_ref)(0, row, ROWS), gswap_ss, gswap_rs, dp=sibling)

    def gather_prepare():
        gates = jnp.concatenate([wa_ref[...], wb_ref[...]], axis=0).T.astype(BF16)
        wab_ref[chan, rows_at(gate_row, ROWS), :] = gates
        for which, values in enumerate((up_ref[...], down_ref[...].T)):
            first, second = values[:, :LANES], values[:, LANES:]
            kept = jnp.where(core == 0, first, second)
            wh_ref[which, groups[0], rows_at(own_row, ROWS), pl.ds(group_lanes[0], LANES)] = kept.astype(BF16)
            stage_ref[which] = jnp.where(core == 0, second, first).astype(BF16)

    def gather_start():
        launch(swap_copy(own_row))
        launch(gate_over(gate_row))

    def hidden_first():
        swap_copy(sibling * ROWS).wait_recv()
        for which in range(2):
            hidden_rings[which].start()
            launch(hidden_cross(which, 0, 0, pair_row))

    def gate_first():
        gate_over(gate_away).wait_recv()
        gate_ring.start()

    ring_steps = [(0, 0)] + [(turn, step) for step in range(1, 5) for turn in range(2)]

    def gates_arrived():
        gate_sib(gate_other).wait_recv()

    def hidden_arrived(*steps):
        for turn, step in ring_steps:
            if step in steps:
                for which in range(2):
                    hidden_cross(which, turn, step, away_row).wait_recv()

    def beside(ref, j):
        start = 2 * j * ROWS
        return jnp.concatenate(
            [ref[:, start : start + ROWS].astype(F32), ref[:, start + ROWS : start + 2 * ROWS].astype(F32)], axis=0
        ).T

    for j in range(PAIRS):
        packed = beside(tokens_ref, j)
        tok_ref[j * ROWS : (j + 1) * ROWS, :] = packed.astype(BF16)
        for first, values in ((0, packed), (HALF, beside(cotangent_ref, j))):
            low, high = split_pair(values)
            in_send[2 * j, first : first + HALF, :] = low.astype(BF16)
            in_send[2 * j + 1, first : first + HALF, :] = high.astype(BF16)
    in_recv[chan] = in_send[chan]

    lane_id = lax.broadcasted_iota(jnp.int32, (8, LANES), 1)
    row_id = lax.broadcasted_iota(jnp.int32, (8, LANES), 0)
    halves = jnp.where((lane_id >= HALF) == (row_id == 1), 1.0, 0.0) * jnp.where(row_id < 2, 1.0, 0.0)
    halves = halves.astype(BF16)

    def token_sums(parts):
        total = 0.0
        for part in parts:
            total = total + dot_nt(halves, part)
        return [total[h : h + 1, j * ROWS : (j + 1) * ROWS] for h in range(2) for j in range(PAIRS)]

    def split(values):
        high = values.astype(BF16)
        return high, (values - high.astype(F32)).astype(BF16)

    tokens = tok_ref[...]
    wide_tokens = tokens.astype(F32)
    for i, sums in enumerate(token_sums([tokens]) + token_sums(split(wide_tokens * wide_tokens))):
        head_send[i : i + 1, :] = sums

    def row(*refs):
        return jnp.concatenate([ref[...].reshape(1, HALF) for ref in refs], axis=1)

    bup = bup_ref[...].reshape(1, 2 * LANES)
    head_send[16:17, :] = row(ba_ref, bb_ref)
    head_send[17:18, :] = row(gain2_ref, bias2_ref)
    head_send[18:19, :] = row(bdown_ref, bdown_ref)
    head_send[19:20, :] = bup[:, :LANES]
    head_send[20:21, :] = bup[:, LANES:]
    head_send[21:24, :] = jnp.zeros((3, LANES), F32)
    head_recv[chan] = head_send[...]
    head = exchange(0, lambda peer: head_send, head_recv)
    inputs = exchange(1, lambda peer: in_send.at[peer], in_recv)
    gather_prepare()
    pl.semaphore_wait(barrier, N_CHAN - 1 + 3)
    gather_start()
    head[0]()
    hidden_first()

    level, filled = bucket_ref[0], items_ref[0]
    coefl_ref[...] = levels_ref[level]
    item_blocks = jnp.where(level == 0, 2, jnp.where(level == 1, 4, 8))
    block_id = 2 * (row_id % PAIRS) + jnp.where(lane_id >= HALF, 1, 0)
    bound = jnp.where(row_id < PAIRS, filled * item_blocks, item_blocks)
    aux_ref[...] = jnp.where(block_id < bound, 1.0, 0.0)
    for i in range(8):
        modes_ref[i] = jnp.concatenate([raw_modes_ref[i], raw_modes_ref[i]], axis=1)
    inputs[0]()
    gate_first()
    log_dt = row(log_dt_ref, log_dt_ref)
    sigma, step_size = 2.0 * jnp.exp(-log_dt), jnp.exp(log_dt)

    base = pl.multiple_of(dp * QUARTER, QUARTER)

    def spec_copy(which, r):
        peer = dp_peers[r]
        src, dst = ((spec_send, spec_recv), (sgrad_send.at[peer], sgrad_recv))[which]
        return remote(src, dst.at[dp], spec_ss.at[which, r - 1], spec_rs.at[which, r - 1], dp=peer)

    cauchy_coefficients(modes_ref, sigma, mcoef_ref)
    cauchy_forward(0, sigma, mcoef_ref, wave_ref, base, sums_ref, spec_send)
    cauchy_forward(1, sigma, mcoef_ref, wave_ref, base, sums_ref, spec_send)
    cauchy_forward(2, sigma, mcoef_ref, wave_ref, base, sums_ref, spec_send)
    cauchy_forward(3, sigma, mcoef_ref, wave_ref, base, sums_ref, spec_send)
    spec_recv[dp] = spec_send[...]
    for r in range(1, 4):
        spec_copy(0, r).start()
    up_ring.step(1)
    gate_ring.step(1)
    down_ring.step(1)

    head[1]()
    sums = head_recv[0, 0:16, :]
    for c in range(1, N_CHAN):
        sums = sums + head_recv[c, 0:16, :]
    mean = sums[0:8] * (1.0 / MODEL_WIDTH)
    rstd = lax.rsqrt(sums[8:16] * (1.0 / MODEL_WIDTH) - mean * mean + EPSILON)

    def columns(rows):
        tall = rows.T
        return [jnp.where(low_lanes(ROWS), tall[:, j : j + 1], tall[:, 4 + j : 5 + j]) for j in range(PAIRS)]

    gain1, bias1, skip = row(gain1_ref, gain1_ref), row(bias1_ref, bias1_ref), row(skip_ref, skip_ref)
    mean_cols, rstd_cols = columns(mean), columns(rstd)
    for j in range(PAIRS):
        hat = (tok_ref[j * ROWS : (j + 1) * ROWS, :].astype(F32) - mean_cols[j]) * rstd_cols[j]
        hat_ref[j] = hat
        norm_ref[j] = hat * gain1 + bias1

    spread_pairs(lambda j, rows: norm_ref[j, rows, :], coefl_ref, 0, tw_ref, 0, 5, rhs_ref, False)
    transform_into(sig_ref, mat_ref, 0, rhs_ref, False)

    for r in range(1, 4):
        spec_copy(0, r).wait_recv()
    for source in range(4):
        store_split(rhs_ref, source * QUARTER, 0, spec_recv[source, :QUARTER, :])
        store_split(rhs_ref, ROWS + source * QUARTER, 0, spec_recv[source, QUARTER:, :])
    up_ring.step(2)
    gate_ring.step(2)
    freq_ref[:, 0:256] = split_product(mat_ref, 1, rhs_ref, 0, 256)
    even = split_product(mat_ref, 2, rhs_ref, LANES, LANES)
    freq_ref[:, LANES:256] = jnp.where(low_lanes(256), freq_ref[:, LANES:256], even)
    sign = 1.0 - 2.0 * (lax.broadcasted_iota(jnp.int32, (CHUNK, LANES), 0) % 2).astype(F32)
    nyquist = step_size * column_sum(mcoef_ref[0]) * (1.0 / TOK_DEV)
    down_ring.step(2)

    def store_taps(j, rows, values):
        taps_ref[j, rows, :] = (values + sign * nyquist) * aux_ref[4 + j : 5 + j, :]

    gather_pairs(freq_ref, coefc_ref, 160, tw_ref, 10, 2, store_taps)
    spread_pairs(lambda j, rows: taps_ref[j, rows, :], coefc_ref, 0, tw_ref, 0, 5, rhs_ref, False)
    transform_into(ans_ref, mat_ref, 0, rhs_ref, False)
    multiply_spectra(sig_ref, ans_ref, rhs_ref, False, False)
    transform_into(freq_ref, mat_ref, 1, rhs_ref, False)
    gate_ring.step(3)
    up_ring.step(3)

    def store_conv(j, rows, values):
        conv_ref[j, rows, :] = values
    gather_pairs(freq_ref, coefl_ref, 80, tw_ref, 0, 5, store_conv)
    for j in range(PAIRS):
        mixed = conv_ref[j] * aux_ref[j : j + 1, :] + skip * norm_ref[j]
        cumulative, density = normal_parts(mixed)
        slope_ref[j] = cumulative + mixed * density
        low, high = split_pair(mixed * cumulative)
        acts_send[2 * j] = low.astype(BF16)
        acts_send[2 * j + 1] = high.astype(BF16)
    acts_recv[chan] = acts_send[chan]
    acts = exchange(2, lambda peer: acts_send.at[peer], acts_recv)
    acts[0]()

    def joined(ref, pair, first):
        return join_pair(
            ref[2 * pair, first : first + HALF, :].astype(F32), ref[2 * pair + 1, first : first + HALF, :].astype(F32)
        )

    def lanes_of(pair):
        return slice(pair * LANES, (pair + 1) * LANES)

    def gate_lanes(pair):
        return lanes_of(pair % 2 * 2 + pair // 2)

    def core_copy(which, src, dst):
        return remote(src, dst, core_ss.at[which], core_rs.at[which], dp=sibling)

    def other_core(which, ref):
        return core_copy(which, ref.at[core], ref.at[core])

    def vector(row, first, second):
        return interleave(head_recv[first, 16 + row : 17 + row, :], head_recv[second, 16 + row : 17 + row, :])

    def both_cores(ref):
        return ref[...].reshape(2 * ROWS, MODEL_WIDTH)

    def hidden_group(offset):
        group = groups[offset]
        low, high = 2 * group, 7 - 2 * group
        bias = jnp.concatenate(
            [jnp.where(core == 0, head_recv[c, 19:20, :], head_recv[c, 20:21, :]) for c in (low, high)], axis=1
        )
        pre = dot_nn(both_cores(norm2_ref), wh_ref[0, group]) + bias
        cumulative, density = normal_parts(pre)
        hidden = (pre * cumulative).astype(BF16)
        hid_ref[group] = hidden
        grad = dot_nn(both_cores(gradf_ref), wh_ref[1, group]) * (cumulative + pre * density)
        grad = grad.astype(BF16)
        gpre_ref[group] = grad
        sums = column_sum(grad.astype(F32))
        tail_send[low, pl.ds(3 + core, 1), :] = sums[:, 0:LANES]
        tail_send[high, pl.ds(3 + core, 1), :] = sums[:, LANES : 2 * LANES]
        branch_ref[...] += dot_nt(hidden, wh_ref[1, group]).reshape(2, ROWS, MODEL_WIDTH)
        back2_ref[...] += dot_nt(grad, wh_ref[0, group]).reshape(2, ROWS, MODEL_WIDTH)

    def offset_of(turn, step):
        return TURNS[turn] * (5 - step)

    def far(offset):
        return 4 if offset == -4 else offset

    class RingBack:
        def __init__(self, which, view, base, count, ring_ref, extra):
            self.which, self.view, self.base, self.count = which, view, base, count
            self.ring_ref, self.extra = ring_ref, extra

        def copy(self, turn, step):
            slot = turn * 4 + step - 1
            half = self.count // 2
            if step == 1:
                dst = self.ring_ref.at[slot]
                lead = (slice(None),) * (len(dst.shape) - 2)
                src, dst = self.view(4, self.base + turn * half, half), dst.at[lead + (pl.ds(0, half), slice(None))]
            else:
                src, dst = self.view(offset_of(turn, step), self.base, self.count), self.ring_ref.at[slot]
            return remote(src, dst, rring_ss.at[self.which, slot], rring_rs.at[self.which, slot], chan=nexts[turn])

        def whole(self, offset):
            return self.view(offset, self.base, self.count)[...].astype(F32) + self.extra(offset)

        def step(self, step):
            half = self.count // 2
            if step == 1:
                self.view(4, self.base, self.count)[...] = self.whole(4).astype(BF16)
                for turn in range(2):
                    launch(self.copy(turn, 1))
                return
            for turn in range(2):
                offset, slot = offset_of(turn, step), turn * 4 + step - 2
                total = self.whole(offset)
                self.copy(turn, step - 1).wait_recv()
                if step == 2:
                    parts = [total[..., :half, :], total[..., half:, :]]
                    parts[turn] = parts[turn] + self.ring_ref[slot][..., :half, :].astype(F32)
                    total = jnp.concatenate(parts, axis=-2)
                else:
                    total = total + self.ring_ref[slot].astype(F32)
                self.view(offset, self.base, self.count)[...] = total.astype(BF16)
                launch(self.copy(turn, step))

        def total(self):
            total = self.whole(0)
            for turn in range(2):
                self.copy(turn, 4).wait_recv()
                total = total + self.ring_ref[turn * 4 + 3].astype(F32)
            return total

    waited = set()

    def wait_once(name, copy):
        if name not in waited:
            waited.add(name)
            copy().wait_recv()

    def gate_share():
        ref = gab_w_ref.at[:, rows_at(gate_other, 256), :]
        return remote(ref, sib_ab_ref, rsib_ss, rsib_rs, dp=sibling)

    def gate_extra(offset):
        wait_once("gates", gate_share)
        return sib_ab_ref[around[offset % 8]].astype(F32)

    def cross_copy(pair):
        src = gh_ref.at[:, groups[pair], rows_at(away_row, 256), :]
        return remote(src, cross_ref.at[pair], rdx_ss.at[pair], rdx_rs.at[pair], dp=across)

    def hidden_extra(offset):
        pair = offset % 4
        wait_once(pair, lambda: cross_copy(pair))
        return cross_ref[pair, :, :, pl.ds(group_lanes[offset % 8], LANES)].astype(F32)

    gate_g = RingBack(0, gate_view(gab_w_ref), gate_pair, 256, ring_ab_ref, gate_extra)

    hidden_g = RingBack(1, hidden_view(gh_ref), pair_row, 256, ring_h_ref, hidden_extra)

    def hidden_grads(offset):
        group = groups[offset]
        gh_ref[1, group] = dot_nn(gradf_t_ref[...], hid_ref[group]).astype(BF16)
        gh_ref[0, group] = dot_nn(norm2_t_ref[...], gpre_ref[group]).astype(BF16)
        launch(cross_copy(offset))

    def part_copy():
        return remote(part_ab_ref.at[0], part_ab_ref.at[1], rx_ss, rx_rs, dp=across)

    def last_swap():
        return remote(keep_ref.at[:, rows_at((1 - core) * ROWS, ROWS), :], swap_ref, rswap_ss, rswap_rs, dp=sibling)

    def gate_last():
        gate_total_ref[...] = gate_g.total()
        part_ab_ref[0] = gate_total_ref[rows_at((1 - lax.div(dp, 2)) * ROWS, ROWS), :].astype(BF16)
        launch(part_copy())

    def gate_finish():
        part_copy().wait_recv()
        gw_ref[:, 0:128] = gate_total_ref[rows_at(lax.div(dp, 2) * ROWS, ROWS), :] + part_ab_ref[1].astype(F32)

    def hidden_last():
        keep_ref[...] = hidden_g.total()
        launch(last_swap())
        for which in range(2):
            gw_ref[:, pl.ds(pl.multiple_of(128 + 256 * which + half_lanes, LANES), LANES)] = keep_ref[
                which, rows_at(core * ROWS, ROWS), :
            ]

    def hidden_finish():
        last_swap().wait_recv()
        for which in range(2):
            gw_ref[:, pl.ds(pl.multiple_of(128 + 256 * which + other_lanes, LANES), LANES)] = swap_ref[which]

    late = exchange(4, lambda peer: late_send.at[peer], late_recv)


    def gate_grads(*offsets):
        for offset in offsets:
            c = chan_at(offset)
            gab_w_ref[c] = dot_nn(acts_t_ref[...], gab_ref[c]).astype(BF16)
        if 0 in offsets:
            launch(gate_share())

    def late_messages():
        core_copy(3, half_send.at[1], half_recv.at[1]).wait_recv()
        for p in range(PAIRS):
            out = res_ref[p] + (branch_ref[core, :, lanes_of(p)] + half_recv[1, :, lanes_of(p)].astype(F32)) + interleave(head_recv[2 * p, 18:19, :], head_recv[2 * p + 1, 18:19, :])[0]
            low, high = split_pair(out)
            late_send[2 * p, :HALF, :] = low.astype(BF16)
            late_send[2 * p + 1, :HALF, :] = high.astype(BF16)
        for c in range(N_CHAN):
            late_send[c, ROWS:, :] = jnp.concatenate([tail_send[c], jnp.zeros((8, LANES), F32)], axis=0).astype(BF16)
        late_recv[chan] = late_send[chan]
        late[0]()

    back = exchange(3, lambda peer: back_send.at[peer], back_recv)

    inputs[1]()
    for p in range(PAIRS):
        gradf_ref[core, :, lanes_of(p)] = joined(in_recv, p, HALF).astype(BF16)
    launch(other_core(0, gradf_ref))
    gate_ring.step(4)
    gate_spread()
    down_ring.step(3)
    gates_arrived()
    acts[1]()
    for p in range(PAIRS):
        acts_ref[:, gate_lanes(p)] = joined(acts_recv, p, 0).astype(BF16)

    total = 0.0
    for p in range(PAIRS):
        first = dot_nn(acts_ref[...], wab_ref[2 * p]) + head_recv[2 * p, 16:17, :]
        second = dot_nn(acts_ref[...], wab_ref[2 * p + 1]) + head_recv[2 * p + 1, 16:17, :]
        gate, raw = interleave(first, second)
        swish = lax.logistic(raw)
        gate_ref[p], swish_ref[p] = gate, swish
        resid = joined(in_recv, p, 0) + gate * swish
        res_ref[p] = resid
        total = total + resid
    mean2 = jnp.sum(total, axis=1, keepdims=True) * (1.0 / MODEL_WIDTH)
    total = 0.0
    for p in range(PAIRS):
        centred = res_ref[p] - mean2
        total = total + centred * centred
    rstd2 = lax.rsqrt(jnp.sum(total, axis=1, keepdims=True) * (1.0 / MODEL_WIDTH) + EPSILON)
    gain2 = []
    for p in range(PAIRS):
        gain, bias = vector(1, 2 * p, 2 * p + 1)
        gain2.append(gain)
        hat = (res_ref[p] - mean2) * rstd2
        hat2_ref[p] = hat
        norm2_ref[core, :, lanes_of(p)] = (hat * gain + bias).astype(BF16)
    launch(other_core(1, norm2_ref))
    branch_ref[...] = jnp.zeros_like(branch_ref)
    acts_t_ref[...] = acts_ref[...].astype(F32).T.astype(BF16)
    back2_ref[...] = jnp.zeros_like(back2_ref)
    for c in range(N_CHAN):
        tail_send[c, 3:8, :] = jnp.zeros((5, LANES), F32)
    hidden_arrived(2)
    down_ring.step(4)
    other_core(0, gradf_ref).wait_recv()
    up_ring.step(4)
    gradf_t_ref[...] = both_cores(gradf_ref).astype(F32).T.astype(BF16)
    hidden_arrived(1, 3)
    other_core(1, norm2_ref).wait_recv()
    norm2_t_ref[...] = both_cores(norm2_ref).astype(F32).T.astype(BF16)
    hidden_group(3)
    hidden_group(1)
    hidden_grads(3)
    hidden_arrived(0, 4)
    hidden_group(0)
    hidden_group(2)
    half_send[0] = back2_ref[1 - core].astype(BF16)
    launch(core_copy(2, half_send.at[0], half_recv.at[0]))
    hidden_grads(0)
    half_send[1] = branch_ref[1 - core].astype(BF16)
    launch(core_copy(3, half_send.at[1], half_recv.at[1]))
    core_copy(2, half_send.at[0], half_recv.at[0]).wait_recv()
    back2 = back2_ref[core] + half_recv[0].astype(F32)
    back2_ref[core] = back2

    mean_q, mean_qx = 0.0, 0.0
    for p in range(PAIRS):
        grad, hat = back2_ref[core, :, lanes_of(p)], hat2_ref[p]
        q = grad * gain2[p]
        mean_q = mean_q + q
        mean_qx = mean_qx + q * hat
        gain_grad, bias_grad = interleave(column_sum(grad * hat), column_sum(grad))
        tail_send[2 * p, 1:2, :] = gain_grad
        first, second = interleave(turn_half(column_sum(grad * hat)), turn_half(column_sum(grad)))
        tail_send[2 * p + 1, 1:2, :] = first
    mean_q = jnp.sum(mean_q, axis=1, keepdims=True) * (1.0 / MODEL_WIDTH)
    mean_qx = jnp.sum(mean_qx, axis=1, keepdims=True) * (1.0 / MODEL_WIDTH)
    for p in range(PAIRS):
        hat = hat2_ref[p]
        extra = rstd2 * (back2_ref[core, :, lanes_of(p)] * gain2[p] - mean_q - hat * mean_qx)
        grad_f = joined(in_recv, p, HALF)
        grad_resid = grad_f + extra
        gate, swish = gate_ref[p], swish_ref[p]
        grad_a = (grad_resid * swish).astype(BF16).astype(F32)
        grad_b = (grad_resid * gate * swish * (1.0 - swish)).astype(BF16).astype(F32)
        first, second = interleave(grad_a, grad_b)
        gab_ref[2 * p] = first.astype(BF16)
        gab_ref[2 * p + 1] = second.astype(BF16)
        tail_send[2 * p, 0:1, :] = column_sum(first)
        tail_send[2 * p + 1, 0:1, :] = column_sum(second)
        low, high = interleave(column_sum(grad_f), column_sum(grad_f))
        tail_send[2 * p, 2:3, :] = low
        tail_send[2 * p + 1, 2:3, :] = high
        low, high = split_pair(extra)
        late_send[2 * p, HALF:ROWS, :] = low.astype(BF16)
        late_send[2 * p + 1, HALF:ROWS, :] = high.astype(BF16)
    grad_acts = 0.0
    for c in range(N_CHAN):
        grad_acts = grad_acts + dot_nt(gab_ref[c], wab_ref[c])
    for p in range(PAIRS):
        low, high = split_pair(grad_acts[:, gate_lanes(p)])
        back_send[2 * p] = low.astype(BF16)
        back_send[2 * p + 1] = high.astype(BF16)
    back_recv[chan] = back_send[chan]
    back[0]()
    hidden_grads(1)
    gate_grads(4, 3, -3)
    late_messages()
    gate_grads(2, -2, 1, -1, 0)

    back[1]()
    skip_grad = 0.0
    for j in range(PAIRS):
        grad = joined(back_recv, j, 0) * slope_ref[j]
        slope_ref[j] = grad
        conv_ref[j] = grad * aux_ref[j : j + 1, :]
        skip_grad = skip_grad + column_sum(grad * norm_ref[j])
    hidden_g.step(1)
    gate_g.step(1)
    hidden_grads(2)
    spread_pairs(lambda j, rows: conv_ref[j, rows, :], coefl_ref, 0, tw_ref, 0, 5, rhs_ref, False)
    transform_into(freq_ref, mat_ref, 0, rhs_ref, False)
    multiply_spectra(sig_ref, freq_ref, rhs_ref, True)
    gate_g.step(2)
    hidden_g.step(2)
    transform_into(sig_ref, mat_ref, 1, rhs_ref)

    def store_kernel_grad(j, rows, values):
        taps_ref[j, rows, :] = values * aux_ref[4 + j : 5 + j, :]

    gather_pairs(sig_ref, coefc_ref, 80, tw_ref, 0, 5, store_kernel_grad)
    nyquist_grad = 0.0
    for j in range(PAIRS):
        whole_sign = 1.0 - 2.0 * (lax.broadcasted_iota(jnp.int32, (ROWS, LANES), 0) % 2).astype(F32)
        nyquist_grad = nyquist_grad + column_sum(taps_ref[j] * whole_sign)
    nyquist_grad = fold(nyquist_grad) * (1.0 / TOK_DEV)
    spread_pairs(lambda j, rows: taps_ref[j, rows, :], coefc_ref, 192, tw_ref, 10, 2, rhs_ref)
    taps_freq_ref[...] = split_product(mat_ref, 0, rhs_ref, 0, 256)
    even = split_product(mat_ref, 3, rhs_ref, LANES, LANES)
    taps_freq_ref[:, LANES:256] = jnp.where(low_lanes(256), taps_freq_ref[:, LANES:256], even)
    for source in range(4):
        rows = slice(source * QUARTER, (source + 1) * QUARTER)
        sgrad_send[source, :QUARTER, :] = taps_freq_ref[rows, :]
        sgrad_send[source, QUARTER:, :] = taps_freq_ref[ROWS + source * QUARTER : ROWS + (source + 1) * QUARTER, :]
    sgrad_recv[dp] = sgrad_send[dp]
    for r in range(1, 4):
        spec_copy(1, r).start()
    gate_g.step(3)
    hidden_g.step(3)

    multiply_spectra(ans_ref, freq_ref, rhs_ref, True, False)
    transform_into(freq_ref, mat_ref, 1, rhs_ref, False)
    late[1]()
    gather_pairs(freq_ref, coefl_ref, 80, tw_ref, 0, 5, store_conv)
    gain_grad, bias_grad = 0.0, 0.0
    scaled, crossed = [], []
    for j in range(PAIRS):
        grad = conv_ref[j] + skip * slope_ref[j]
        conv_ref[j] = grad
        gain_grad = gain_grad + column_sum(grad * hat_ref[j])
        bias_grad = bias_grad + column_sum(grad)
    conv = conv_ref[...].reshape(PAIRS * ROWS, LANES) * gain1
    for i, sums in enumerate(
        token_sums(split(conv)) + token_sums(split(conv * hat_ref[...].reshape(PAIRS * ROWS, LANES)))
    ):
        sum_send[i : i + 1, :] = sums
    gate_g.step(4)
    sum_recv[chan] = sum_send[...]
    sums_back = exchange(6, lambda peer: sum_send, sum_recv)

    for r in range(1, 4):
        spec_copy(1, r).wait_recv()
    sgrad_ref[...] = sgrad_recv[0] + sgrad_recv[1] + sgrad_recv[2] + sgrad_recv[3]

    sigma_sum = point_grads(sigma, wave_ref, base, sums_ref, sgrad_ref, pgrad_ref)
    square_sum = mode_sums(0, jnp.zeros_like(sigma_sum), sigma, mcoef_ref, wave_ref, base, pgrad_ref, mback_ref)
    sums_back[0]()
    hidden_g.step(4)
    square_sum = mode_sums(1, square_sum, sigma, mcoef_ref, wave_ref, base, pgrad_ref, mback_ref)
    gate_last()
    square_sum = mode_sums(2, square_sum, sigma, mcoef_ref, wave_ref, base, pgrad_ref, mback_ref)
    square_sum = mode_sums(3, square_sum, sigma, mcoef_ref, wave_ref, base, pgrad_ref, mback_ref)
    mode_grads, dt_grad = mode_gradients(modes_ref, sigma, nyquist_grad, step_size, sigma_sum, square_sum, mback_ref)
    mask = low_lanes(32)
    for i in range(4):
        dp_send[i * 32 : (i + 1) * 32, :] = jnp.where(mask, mode_grads[i], mode_grads[i + 4])
    first = low_lanes(1)
    dp_send[128:129, :] = jnp.where(first, dt_grad, fold(skip_grad))
    dp_send[129:130, :] = jnp.where(first, fold(gain_grad), fold(bias_grad))
    dp_send[130:136, :] = jnp.zeros((6, LANES), F32)
    tail_sum = late_recv[0, ROWS:, :].astype(F32)
    for c in range(1, N_CHAN):
        tail_sum = tail_sum + late_recv[c, ROWS:, :].astype(F32)
    dp_send[136:144, :] = tail_sum[:8]
    dp_low[...] = dp_send[...].astype(BF16)

    def dp_copy(r):
        return remote(dp_low, dp_recv.at[r - 1], dp_ss.at[r - 1], dp_rs.at[r - 1], dp=dp_peers[r])

    for r in range(1, 4):
        dp_copy(r).start()
    gate_finish()

    sums_back[1]()
    sums = sum_recv[0]
    for c in range(1, N_CHAN):
        sums = sums + sum_recv[c]
    hidden_last()
    sums = sums * (1.0 / MODEL_WIDTH)
    rstd_cols, q_cols, qx_cols = columns(rstd), columns(sums[0:8]), columns(sums[8:16])
    for j in range(PAIRS):
        rows = slice(j * ROWS, (j + 1) * ROWS)
        out_ref[rows, :] = joined(late_recv, j, 0).astype(BF16)
        dtok_ref[rows, :] = joined(late_recv, j, HALF) + rstd_cols[j] * (
            conv_ref[j] * gain1 - q_cols[j] - hat_ref[j] * qx_cols[j]
        )
    for r in range(1, 4):
        dp_copy(r).wait_recv()
    total = dp_send[...] + (dp_recv[0].astype(F32) + dp_recv[1].astype(F32) + dp_recv[2].astype(F32))
    hidden_finish()
    gm_ref[...] = total[0:128]
    gv_ref[...] = total[128:144]
    for copy in pending:
        copy.wait_send()
    for group in (head, inputs, acts, back, late, sums_back):
        group[2]()
    for r in range(1, 4):
        dp_copy(r).wait_send()
        spec_copy(0, r).wait_send()
        spec_copy(1, r).wait_send()
def unpack_kernel(
    out_ref, dtok_ref, gw_ref, gm_ref, gv_ref, cotangent_ref,
    output_ref, tokens_ref, gain1_ref, bias1_ref, modes_ref, dt_ref, skip_ref, wa_ref, ba_ref, wb_ref, bb_ref,
    gain2_ref, bias2_ref, up_ref, bup_ref, down_ref, bdown_ref,
):
    for j in range(PAIRS):
        out = out_ref[j * ROWS : (j + 1) * ROWS, :].astype(F32).T.astype(BF16)
        grad = dtok_ref[j * ROWS : (j + 1) * ROWS, :].T
        for h in range(2):
            lanes, rows = slice((2 * j + h) * ROWS, (2 * j + h + 1) * ROWS), slice(h * HALF, (h + 1) * HALF)
            output_ref[:, lanes] = out[rows]
            tokens_ref[:, lanes] = cotangent_ref[:, lanes] + grad[rows]
    for i in range(8):
        modes_ref[i] = gm_ref[i % 4 * 32 : i % 4 * 32 + 32, i // 4 * HALF : (i // 4 + 1) * HALF]
    gates = gw_ref[:, :LANES].T
    wa_ref[...] = gates[:HALF]
    wb_ref[...] = gates[HALF:]
    up_ref[...] = gw_ref[:, 128:384]
    down_ref[...] = gw_ref[:, 384:640].T
    for at, low, high in (
        (0, dt_ref, skip_ref), (1, gain1_ref, bias1_ref), (8, ba_ref, bb_ref), (9, gain2_ref, bias2_ref),
    ):
        low[...] = gv_ref[at, :HALF]
        high[...] = gv_ref[at, HALF:]
    bdown_ref[...] = gv_ref[10, :HALF]
    bup_ref[:LANES] = gv_ref[11, :]
    bup_ref[LANES:] = gv_ref[12, :]


def block_program():
    mats, twiddle, levels, constant, wave = mixer_tables()

    def run(tokens, cotangent, bucket, items, gain1, bias1, modes, log_dt, skip, w_a, b_a, w_b, b_b, gain2, bias2, w_up, b_up, w_down, b_down):
        vmem = pl.BlockSpec(memory_space=pltpu.VMEM)
        smem = pl.BlockSpec(memory_space=pltpu.SMEM)
        dma = pltpu.SemaphoreType.DMA

        def buf(*shape):
            return pltpu.VMEM(shape, F32)

        def low(*shape):
            return pltpu.VMEM(shape, BF16)

        def full(*shape):
            return jax.ShapeDtypeStruct(shape, F32)

        big, wide = (PAIRS, ROWS, LANES), (256, WIDE)
        packed = pl.pallas_call(
            block_kernel,
            out_shape=(
                jax.ShapeDtypeStruct((512, LANES), BF16), full(512, LANES), full(ROWS, WIDE), full(ROWS, LANES),
                full(16, LANES),
            ),
            in_specs=[smem] * 2 + [vmem] * 22,
            out_specs=(vmem,) * 5,
            scratch_shapes=[
                low(512, LANES), buf(8, LANES), buf(160, LANES), buf(8, 32, LANES),
                low(N_CHAN, 512, 128), low(2, 4, 512, 256), low(N_CHAN, 512, 128), low(2, 4, 512, 256),
                low(2, ROWS, LANES), low(N_CHAN, 256, LANES), low(8, 256, LANES), low(8, 2, 256, LANES), low(2, ROWS, LANES),
                low(4, 2, 256, 256), buf(2, 256, LANES), buf(2, ROWS, LANES), buf(256, LANES),
                low(N_CHAN, ROWS, LANES), low(N_CHAN, ROWS, LANES), buf(24, LANES), buf(N_CHAN, 24, LANES),
                low(N_CHAN, HALF, LANES), low(N_CHAN, HALF, LANES), low(N_CHAN, HALF, LANES), low(N_CHAN, HALF, LANES),
                low(N_CHAN, 144, LANES), low(N_CHAN, 144, LANES),
                buf(16, LANES), buf(N_CHAN, 16, LANES), buf(N_CHAN, 8, LANES),
                buf(144, LANES), low(144, LANES), low(3, 144, LANES), buf(64, 256), buf(4, 64, 256), buf(4, 64, 256), buf(4, 64, 256),
                buf(*big), buf(*big), buf(*big), buf(*big), low(2, *wide), buf(*wide), buf(*wide), buf(*wide), buf(*big),
                buf(10, 32, LANES), buf(2, 16, QUARTER, LANES), buf(2, 16, QUARTER, LANES), buf(10, 32, LANES),
                buf(64, 256), buf(256, 256),
                buf(*big), buf(*big), buf(*big), buf(*big), low(ROWS, 512), low(2, ROWS, 512), low(2, ROWS, 512),
                buf(2, ROWS, 512), buf(2, ROWS, 512), low(2, ROWS, 512), low(2, ROWS, 512),
                low(N_CHAN, ROWS, LANES), low(4, 256, 256), low(4, 256, 256), low(512, ROWS), low(512, 256), low(512, 256),
                dma((3, 8)), dma((3, 8)), dma, dma, dma, dma, dma((2, 9)), dma((2, 9)), dma, dma, dma((4,)), dma((4,)),
                dma((2, 8)), dma((2, 8)), dma, dma, dma, dma, dma((4,)), dma((4,)), dma, dma,
                dma((7, 7)), dma((7, 7)), dma((3,)), dma((3,)), dma((2, 3)), dma((2, 3)),
            ],
            compiler_params=pltpu.CompilerParams(
                collective_id=0, has_side_effects=True, vmem_limit_bytes=28 * 1024 * 1024
            ),
            name="block",
        )(
            bucket, items, tokens.T, cotangent.T, gain1, bias1, jnp.swapaxes(modes, 1, 2), log_dt, skip,
            w_a.T, b_a, w_b.T, b_b, gain2, bias2,
            w_up, b_up, w_down, b_down, levels, constant, mats, twiddle, wave,
        )
        small = full(HALF)
        results = pl.pallas_call(
            unpack_kernel,
            out_shape=(
                jax.ShapeDtypeStruct((HALF, TOK_DEV), BF16), full(HALF, TOK_DEV), small, small, full(8, 32, HALF),
                small, small, full(HALF, ROWS), small, full(HALF, ROWS), small, small, small, full(ROWS, 256),
                full(256), full(256, ROWS), small,
            ),
            in_specs=[vmem] * 6,
            out_specs=(vmem,) * 17,
            name="unpack",
        )(*packed, cotangent.T)
        turned = {0, 1, 4, 7, 9}
        return tuple(jnp.swapaxes(r, -1, -2) if i in turned else r for i, r in enumerate(results))

    return run


def solution(mesh):
    small = mesh.shape["chan"] == N_CHAN and mesh.shape["dp"] == 4
    return jax.shard_map(
        block_program() if small else shards,
        mesh=mesh,
        in_specs=(
            P("dp", "chan"),
            P("dp", "chan"),
            P("dp"),
            P("dp"),
            P("chan"),
            P("chan"),
            P(None, "chan", None),
            P("chan"),
            P("chan"),
            P("dp", "chan"),
            P("chan"),
            P("dp", "chan"),
            P("chan"),
            P("chan"),
            P("chan"),
            P("dp", "chan"),
            P("chan"),
            P("chan", "dp"),
            P("chan"),
        ),
        out_specs=(
            P("dp", "chan"),
            P("dp", "chan"),
            P("chan"),
            P("chan"),
            P(None, "chan", None),
            P("chan"),
            P("chan"),
            P("dp", "chan"),
            P("chan"),
            P("dp", "chan"),
            P("chan"),
            P("chan"),
            P("chan"),
            P("dp", "chan"),
            P("chan"),
            P("chan", "dp"),
            P("chan"),
        ),
        check_vma=False,
    )
```

```python
import math

import jax
import jax.numpy as jnp
import ml_dtypes
import numpy as np
from jax import lax
from jax.experimental import pallas as pl
from jax.experimental.pallas import tpu as pltpu
from jax.sharding import PartitionSpec as P

MODEL_WIDTH = 512
TOK_DEV = 1024


HIGHEST = lax.Precision.HIGHEST
EPSILON = 1e-05


def product(left, right):
    return jnp.dot(left, right, preferred_element_type=jnp.float32)


def product_nt(left, right):
    return lax.dot_general(
        left, right, (((1,), (1,)), ((), ())), preferred_element_type=jnp.float32
    )


def product_tn(left, right):
    return lax.dot_general(
        left, right, (((0,), (0,)), ((), ())), preferred_element_type=jnp.float32
    )


def gelu_slope(values):
    return (
        0.5 * (1.0 + lax.erf(values * 0.7071067811865476))
        + values * jnp.exp(-0.5 * values * values) * 0.3989422804014327
    )


def half_angles(length):
    angle = np.arange(length // 2 + 1, dtype=np.float64) * (math.pi / length)
    cosine, sine = np.cos(angle), np.sin(angle)
    cosine[-1] = 0.0
    return cosine.astype(np.float32), sine.astype(np.float32)


def inverse_tables(length):
    freq = np.arange(length // 2 + 1)
    turn = (freq[:, None] * np.arange(length)[None, :]) % length * (2.0 * math.pi / length)
    weight = np.where((freq == 0) | (freq == length // 2), 1.0, 2.0)[:, None] / length
    return (weight * np.cos(turn)).astype(np.float32), (weight * np.sin(turn)).astype(np.float32)


def high_einsum(form, left, right):
    return jnp.einsum(form, left, right, precision=HIGHEST)


def ssm_kernel(modes, log_dt):
    cos_h, sin_h = half_angles(TOK_DEV)
    index = jnp.arange(modes.shape[2], dtype=jnp.int32).astype(jnp.float32)
    lam_re = -0.5 * jnp.exp(modes[0])
    lam_im = math.pi * (index + modes[1])
    rank_re, rank_im, in_re, in_im, out_re, out_im = (modes[i] for i in range(2, 8))
    sigma = (2.0 * jnp.exp(-log_dt))[:, None]

    def points(values):
        return values.T[:, None, :]

    den_re = points(lam_re * lam_re + lam_im * lam_im) * (cos_h * cos_h)[:, None] - (
        sigma * sigma
    ).T * (sin_h * sin_h)[:, None]
    den_im = points(-2.0 * sigma * lam_re) * (sin_h * cos_h)[:, None]
    den_sq = den_re * den_re + den_im * den_im
    inv_re = den_re / den_sq
    inv_im = -den_im / den_sq
    sums = []
    for real, imag in (
        (out_re * in_re + out_im * in_im, out_re * in_im - out_im * in_re),
        (out_re * rank_re + out_im * rank_im, out_re * rank_im - out_im * rank_re),
        (rank_re * in_re + rank_im * in_im, rank_re * in_im - rank_im * in_re),
        (rank_re * rank_re + rank_im * rank_im, jnp.zeros_like(rank_re)),
    ):
        turned = points(real * lam_re + imag * lam_im)
        real = points(real)
        p_re, p_im = jnp.sum(real * inv_re, axis=0), jnp.sum(real * inv_im, axis=0)
        q_re, q_im = jnp.sum(turned * inv_re, axis=0), jnp.sum(turned * inv_im, axis=0)
        sine = sin_h[:, None] * sigma.T
        sums.append((-sine * p_im - cos_h[:, None] * q_re, sine * p_re - cos_h[:, None] * q_im))
    (cross_re, cross_im), (left_re, left_im), (right_re, right_im), (self_re, self_im) = sums
    twice = 2.0 * cos_h[:, None]
    loop_re, loop_im = 1.0 + twice * self_re, twice * self_im
    back_re, back_im = twice * right_re, twice * right_im
    loop_sq = loop_re * loop_re + loop_im * loop_im
    ratio_re = (back_re * loop_re + back_im * loop_im) / loop_sq
    ratio_im = (back_im * loop_re - back_re * loop_im) / loop_sq
    part_re = cross_re - (left_re * ratio_re - left_im * ratio_im)
    part_im = cross_im - (left_re * ratio_im + left_im * ratio_re)
    spec_re = 2.0 * (cos_h[:, None] * part_re - sin_h[:, None] * part_im)
    spec_im = 2.0 * (cos_h[:, None] * part_im + sin_h[:, None] * part_re)
    cos_tab, sin_tab = inverse_tables(TOK_DEV)
    return high_einsum("kl,kc->lc", cos_tab, spec_re) - high_einsum("kl,kc->lc", sin_tab, spec_im)


BLOCK = 128
BLOCKS = TOK_DEV // BLOCK
FIRST = 2 * BLOCKS
KEPT = FIRST // 2 + 1


def transform_tables():
    length = 2 * TOK_DEV
    turn = np.arange(KEPT)[:, None] * np.arange(BLOCK)[None, :] * (2.0 * math.pi / length)
    small = np.arange(BLOCK)[:, None] * np.arange(BLOCK)[None, :] % BLOCK * (2.0 * math.pi / BLOCK)
    spots = np.stack([np.arange(BLOCKS) + np.arange(BLOCKS) // (2 << b) * (2 << b) for b in range(3)])
    angle = spots[:, None, :] * np.arange(KEPT)[None, :, None] % FIRST * (2.0 * math.pi / FIRST)
    parts = (np.cos(turn), np.sin(turn), np.cos(small), np.sin(small), np.cos(angle), np.sin(angle))
    return [part.astype(np.float32) for part in parts]


def forward_transform(blocks, cos_a, sin_a):
    cos_t, sin_t, cos_s, sin_s, _, _ = transform_tables()
    step_re = high_einsum("ka,abc->kbc", cos_a, blocks)
    step_im = -high_einsum("ka,abc->kbc", sin_a, blocks)
    turned_re = step_re * cos_t[..., None] + step_im * sin_t[..., None]
    turned_im = step_im * cos_t[..., None] - step_re * sin_t[..., None]
    both = jnp.concatenate([turned_re, turned_im], axis=1)
    matrix = np.block([[cos_s, sin_s], [-sin_s, cos_s]])
    return high_einsum("pb,kbc->kpc", matrix, both)


def inverse_transform(spectrum, cos_a, sin_a):
    cos_t, sin_t, cos_s, sin_s, _, _ = transform_tables()
    matrix = np.block([[cos_s, -sin_s], [sin_s, cos_s]])
    both = high_einsum("bp,kpc->kbc", matrix, spectrum)
    step_re, step_im = both[:, :BLOCK], both[:, BLOCK:]
    turned_re = step_re * cos_t[..., None] - step_im * sin_t[..., None]
    turned_im = step_im * cos_t[..., None] + step_re * sin_t[..., None]
    weight = np.where(np.arange(KEPT) % (KEPT - 1) == 0, 1.0, 2.0).astype(np.float32) / (2 * TOK_DEV)
    return high_einsum("ka,kbc->abc", cos_a * weight[:, None], turned_re) - high_einsum(
        "ka,kbc->abc", sin_a * weight[:, None], turned_im
    )


def multiply(left, right):
    left_re, left_im = left[:, :BLOCK], left[:, BLOCK:]
    right_re, right_im = right[:, :BLOCK], right[:, BLOCK:]
    return jnp.concatenate(
        [left_re * right_re - left_im * right_im, left_re * right_im + left_im * right_re], axis=1
    )


def mixer(normed, kernel_taps, skip_gain, bucket, filled):
    _, _, _, _, cos_a, sin_a = transform_tables()
    cos_x, sin_x = jnp.asarray(cos_a)[bucket], jnp.asarray(sin_a)[bucket]
    item_blocks = 2 << bucket
    block_id = jnp.arange(BLOCKS, dtype=jnp.int32)[:, None, None]
    taps = jnp.where(block_id < item_blocks, kernel_taps.reshape(BLOCKS, BLOCK, -1), 0.0)
    signal = forward_transform(normed.reshape(BLOCKS, BLOCK, -1), cos_x, sin_x)
    answer = forward_transform(taps, cos_a[2], sin_a[2])
    result = inverse_transform(multiply(signal, answer), cos_x, sin_x)
    result = jnp.where(block_id < filled * item_blocks, result, 0.0)
    return result.reshape(normed.shape) + skip_gain * normed


def shards(
    tokens,
    cotangent,
    group_bucket,
    group_items,
    first_norm_gain,
    first_norm_bias,
    modes,
    log_dt,
    d_skip,
    w_a,
    b_a,
    w_b,
    b_b,
    second_norm_gain,
    second_norm_bias,
    w_up,
    b_up,
    w_down,
    b_down,
):
    input_tokens = tokens.astype(jnp.float32)
    sums_in = lax.psum(
        (jnp.sum(input_tokens, axis=1), jnp.sum(input_tokens * input_tokens, axis=1)), "chan"
    )
    input_average = sums_in[0][:, None] / MODEL_WIDTH
    input_inverse_deviation = lax.rsqrt(
        sums_in[1][:, None] / MODEL_WIDTH - input_average * input_average + EPSILON
    )
    input_standardized = (input_tokens - input_average) * input_inverse_deviation
    input_normalized = input_standardized * first_norm_gain + first_norm_bias
    level = group_bucket[0]
    filled = group_items[0]
    kernel_taps, kernel_back = jax.vjp(ssm_kernel, modes, log_dt)

    def local_mix(values, taps_now, skip_gain):
        return mixer(values, taps_now, skip_gain, level, filled)

    mixed, mix_back = jax.vjp(local_mix, input_normalized, kernel_taps, d_skip)
    acts_low = jax.nn.gelu(mixed, approximate=False).astype(jnp.bfloat16)
    wa_full, wb_full, up_full, down_full = (
        lax.all_gather(w_a.astype(jnp.bfloat16), "dp", axis=0, tiled=True),
        lax.all_gather(w_b.astype(jnp.bfloat16), "dp", axis=0, tiled=True),
        lax.all_gather(w_up.astype(jnp.bfloat16), "dp", axis=0, tiled=True),
        lax.all_gather(w_down.astype(jnp.bfloat16), "dp", axis=1, tiled=True),
    )
    acts_full = lax.all_gather(acts_low, "chan", axis=1, tiled=True)
    gate_a = product(acts_full, wa_full) + b_a
    gate_b = product(acts_full, wb_full) + b_b
    gate_sig = jax.nn.sigmoid(gate_b)
    residual_stream = input_tokens + gate_a * gate_sig
    sums_mid = lax.psum(
        (jnp.sum(residual_stream, axis=1), jnp.sum(residual_stream * residual_stream, axis=1)),
        "chan",
    )
    middle_average = sums_mid[0][:, None] / MODEL_WIDTH
    middle_inverse_deviation = lax.rsqrt(
        sums_mid[1][:, None] / MODEL_WIDTH - middle_average * middle_average + EPSILON
    )
    middle_standardized = (residual_stream - middle_average) * middle_inverse_deviation
    middle_reduced = (middle_standardized * second_norm_gain + second_norm_bias).astype(
        jnp.bfloat16
    )
    mid_full = lax.all_gather(middle_reduced, "chan", axis=1, tiled=True)
    pre_act = product(mid_full, up_full) + b_up
    hidden_low = jax.nn.gelu(pre_act, approximate=False).astype(jnp.bfloat16)
    branch = (
        lax.psum_scatter(product(hidden_low, down_full), "chan", scatter_dimension=1, tiled=True)
        + b_down
    )
    output = (residual_stream + branch).astype(jnp.bfloat16)
    grad_f = cotangent.astype(jnp.bfloat16)
    grad_b_down = jnp.sum(grad_f.astype(jnp.float32), axis=0)
    grad_f_full = lax.all_gather(grad_f, "chan", axis=1, tiled=True)
    grad_w_down = product_tn(hidden_low, grad_f_full)
    grad_pre = (product_nt(grad_f_full, down_full) * gelu_slope(pre_act)).astype(jnp.bfloat16)
    grad_b_up = jnp.sum(grad_pre.astype(jnp.float32), axis=0)
    grad_w_up = product_tn(mid_full, grad_pre)
    middle_gradient = lax.psum_scatter(
        product_nt(grad_pre, up_full), "chan", scatter_dimension=1, tiled=True
    )
    second_norm_gain_gradient = jnp.sum(middle_gradient * middle_standardized, axis=0)
    grad_ln2_bias = jnp.sum(middle_gradient, axis=0)
    middle_rescaled = middle_gradient * second_norm_gain
    middle_backward = lax.psum(
        (jnp.sum(middle_rescaled, axis=1), jnp.sum(middle_rescaled * middle_standardized, axis=1)),
        "chan",
    )
    grad_resid = cotangent + middle_inverse_deviation * (
        middle_rescaled
        - middle_backward[0][:, None] / MODEL_WIDTH
        - middle_standardized * middle_backward[1][:, None] / MODEL_WIDTH
    )
    grad_a = (grad_resid * gate_sig).astype(jnp.bfloat16)
    grad_b = (grad_resid * gate_a * gate_sig * (1.0 - gate_sig)).astype(jnp.bfloat16)
    grad_b_a = jnp.sum(grad_a.astype(jnp.float32), axis=0)
    grad_b_b = jnp.sum(grad_b.astype(jnp.float32), axis=0)
    grad_w_a = product_tn(acts_full, grad_a)
    grad_w_b = product_tn(acts_full, grad_b)
    grad_acts = lax.psum_scatter(
        product_nt(grad_a, wa_full) + product_nt(grad_b, wb_full),
        "chan",
        scatter_dimension=1,
        tiled=True,
    )
    grad_mixed = grad_acts * gelu_slope(mixed)
    normalized_gradient, grad_kernel, grad_skip = mix_back(grad_mixed)
    grad_modes, grad_log_dt = kernel_back(grad_kernel)
    first_norm_gain_gradient = jnp.sum(normalized_gradient * input_standardized, axis=0)
    grad_ln1_bias = jnp.sum(normalized_gradient, axis=0)
    input_rescaled = normalized_gradient * first_norm_gain
    input_backward = lax.psum(
        (jnp.sum(input_rescaled, axis=1), jnp.sum(input_rescaled * input_standardized, axis=1)),
        "chan",
    )
    grad_tokens = grad_resid + input_inverse_deviation * (
        input_rescaled
        - input_backward[0][:, None] / MODEL_WIDTH
        - input_standardized * input_backward[1][:, None] / MODEL_WIDTH
    )
    grad_w_a, grad_w_b, grad_w_up, grad_w_down = (
        lax.psum_scatter(grad_w_a, "dp", scatter_dimension=0, tiled=True),
        lax.psum_scatter(grad_w_b, "dp", scatter_dimension=0, tiled=True),
        lax.psum_scatter(grad_w_up, "dp", scatter_dimension=0, tiled=True),
        lax.psum_scatter(grad_w_down, "dp", scatter_dimension=1, tiled=True),
    )
    (
        first_norm_gain_gradient,
        grad_ln1_bias,
        grad_modes,
        grad_log_dt,
        grad_skip,
        grad_b_a,
        grad_b_b,
        second_norm_gain_gradient,
        grad_ln2_bias,
        grad_b_up,
        grad_b_down,
    ) = lax.psum(
        (
            first_norm_gain_gradient,
            grad_ln1_bias,
            grad_modes,
            grad_log_dt,
            grad_skip,
            grad_b_a,
            grad_b_b,
            second_norm_gain_gradient,
            grad_ln2_bias,
            grad_b_up,
            grad_b_down,
        ),
        "dp",
    )
    return (
        output,
        grad_tokens,
        first_norm_gain_gradient,
        grad_ln1_bias,
        grad_modes,
        grad_log_dt,
        grad_skip,
        grad_w_a,
        grad_b_a,
        grad_w_b,
        grad_b_b,
        second_norm_gain_gradient,
        grad_ln2_bias,
        grad_w_up,
        grad_b_up,
        grad_w_down,
        grad_b_down,
    )


LANES = 128
HALF = 64
PAIRS = 4
ROWS = 128
N_CHAN = 8
WIDE = 640
MESH = pl.DeviceIdType.MESH
F32 = jnp.float32
BF16 = jnp.bfloat16


def split_two(matrix):
    high = matrix.astype(ml_dtypes.bfloat16)
    low = (matrix - high.astype(np.float64)).astype(ml_dtypes.bfloat16)
    return np.concatenate([high, low], axis=1)


def lane_rows(values_low, values_high):
    return np.repeat(np.stack([values_low, values_high], -1), HALF, axis=-1)


def mixer_tables():
    line = np.arange(ROWS)
    small = np.outer(line, line) % ROWS * (2.0 * math.pi / ROWS)
    cos_s, sin_s = np.cos(small), np.sin(small)
    forward = np.block([[cos_s, sin_s], [-sin_s, cos_s]])
    real = np.zeros((2 * ROWS, 2 * ROWS))
    for row in range(HALF):
        weight = 1.0 if row == 0 else 2.0
        turn = 2.0 * math.pi / ROWS * row * line
        real[:ROWS, row] = weight * np.cos(turn)
        real[:ROWS, ROWS + row] = -weight * np.sin(turn)
        turn = 2.0 * math.pi / TOK_DEV * (4 + 8 * row) * line
        real[ROWS:, HALF + row] = 2.0 * np.cos(turn)
        real[ROWS:, ROWS + HALF + row] = -2.0 * np.sin(turn)
    mats = np.stack([split_two(m) for m in (forward, forward.T, real, real.T)])

    twiddle = []
    for pair in range(5):
        turn = np.stack([line * k * (math.pi / TOK_DEV) for k in (2 * pair, 2 * pair + 1)])
        twiddle += [lane_rows(np.cos(turn[0]), np.cos(turn[1])), lane_rows(np.sin(turn[0]), np.sin(turn[1]))]
    for first, second in ((1, 2), (3, 0)):
        turn = np.stack([line * k * (2.0 * math.pi / TOK_DEV) for k in (first, second)])
        twiddle += [lane_rows(np.cos(turn[0]), np.cos(turn[1])), lane_rows(np.sin(turn[0]), np.sin(turn[1]))]

    def forward_rows(coef, pairs):
        out = []
        for low, high in pairs:
            for part in range(2):
                for j in range(PAIRS):
                    out.append(lane_rows(coef(2 * j, low, part), coef(2 * j + 1, high, part)))
                for j in range(PAIRS):
                    out.append(lane_rows(coef(2 * j, high, part), coef(2 * j + 1, low, part)))
        return np.stack(out)

    def inverse_rows(coef, pairs):
        out = []
        for low, high in pairs:
            for part in range(2):
                for j in range(PAIRS):
                    out.append(lane_rows(coef(2 * j, low, part), coef(2 * j + 1, high, part)))
                for j in range(PAIRS):
                    out.append(lane_rows(coef(2 * j + 1, low, part), coef(2 * j, high, part)))
        return np.stack(out)

    levels = []
    pairs = [(2 * p, 2 * p + 1) for p in range(5)]
    for level in range(3):
        item = 2 << level

        def angle(block, k):
            return 2.0 * math.pi / 16 * ((block + block // item * item) * k % 16)

        def fwd(block, k, part):
            if k > 8:
                return np.zeros(())
            return np.cos(angle(block, k)) if part == 0 else -np.sin(angle(block, k))

        def inv(block, k, part):
            weight = (1.0 if k in (0, 8) else 2.0) / (2 * TOK_DEV)
            return weight * fwd(block, k, part)

        levels.append(np.concatenate([forward_rows(fwd, pairs), inverse_rows(inv, pairs)]))

    def taps(block, k, part):
        if k == 0:
            return np.asarray((1.0 if part == 0 else (-1.0) ** block) / TOK_DEV)
        turn = 2.0 * math.pi / 8 * (block * k % 8)
        return np.asarray((np.cos(turn) if part == 0 else -np.sin(turn)) * 2.0 / TOK_DEV)

    tap_pairs = [(1, 2), (3, 0)]
    taps_back = forward_rows(taps, tap_pairs)
    taps_rows = inverse_rows(taps, tap_pairs)
    freq_even = np.where(line < HALF, 8 * line, 4 + 8 * (line - HALF))
    half_angle = np.stack(
        [lane_rows(1 + 8 * line, 2 + 8 * line), lane_rows(3 + 8 * line, freq_even)]
    ) * (math.pi / TOK_DEV)
    wave = np.stack([np.cos(half_angle), np.sin(half_angle)])
    return (
        mats,
        np.stack(twiddle).astype(np.float32),
        np.stack(levels).astype(np.float32),
        np.concatenate([levels[2], taps_rows, taps_back]).astype(np.float32),
        wave.astype(np.float32),
    )


def low_lanes(rows):
    return lax.broadcasted_iota(jnp.int32, (rows, LANES), 1) < HALF


def turn_half(values):
    return pltpu.roll(values, HALF, 1)


def split_pair(values):
    upper, lower = values[:HALF], values[HALF:]
    mask = low_lanes(HALF)
    return jnp.where(mask, upper, turn_half(lower)), jnp.where(mask, turn_half(upper), lower)


def join_pair(first, second):
    mask = low_lanes(HALF)
    return jnp.concatenate(
        [jnp.where(mask, first, turn_half(second)), jnp.where(mask, turn_half(first), second)], axis=0
    )


def interleave(first, second):
    mask = low_lanes(first.shape[0])
    return jnp.where(mask, first, turn_half(second)), jnp.where(mask, turn_half(first), second)


def fold(values):
    return values + turn_half(values)


def reciprocal(values):
    guess = pl.reciprocal(values, approx=True)
    return guess * (2.0 - values * guess)


ERF_TERMS = (1.061405429, -1.453152027, 1.421413741, -0.284496736, 0.254829592)


def normal_parts(values):
    bell = jnp.exp(-0.5 * values * values)
    t = reciprocal(1.0 + (0.3275911 * 0.7071067811865476) * jnp.abs(values))
    tail = ERF_TERMS[0]
    for term in ERF_TERMS[1:]:
        tail = tail * t + term
    tail = 0.5 * (tail * t) * bell
    return jnp.where(values < 0.0, tail, 1.0 - tail), bell * 0.3989422804014327


def column_sum(values):
    return jnp.sum(values, axis=0, keepdims=True)


def dot_nt(left, right):
    return lax.dot_general(left, right, (((1,), (1,)), ((), ())), preferred_element_type=F32)


def dot_nn(left, right):
    return jnp.dot(left, right, preferred_element_type=F32)


def store_split(ref, row, lane, values, exact=True):
    high = values.astype(BF16)
    place = (pl.ds(row, values.shape[0]), pl.ds(lane, values.shape[1]))
    ref[(0,) + place] = high
    if exact:
        ref[(1,) + place] = (values - high.astype(F32)).astype(BF16)


def split_product(mat_ref, which, rhs_ref, lane, width, exact=True):
    high = mat_ref[which, :, 0:256]
    low = mat_ref[which, :, 256:512]
    rhs_high = rhs_ref[0, :, lane : lane + width]
    product = dot_nn(high, rhs_high) + dot_nn(low, rhs_high)
    if exact:
        product = product + dot_nn(high, rhs_ref[1, :, lane : lane + width])
    return product


CHUNK = 32


def over_chunks(body, size=CHUNK, first=0, rows=ROWS):
    def step(index, carry):
        body(pl.multiple_of(first + index * size, size))
        return carry

    lax.fori_loop(0, rows // size, step, 0)


def spread_pairs(src, coef_ref, base, twiddle_ref, twiddle_base, pairs, rhs_ref, exact=True):
    def body(row):
        rows = pl.ds(row, CHUNK)
        blocks = [src(j, rows) for j in range(PAIRS)]
        for pair in range(pairs):
            parts = []
            for part in range(2):
                at = base + (pair * 2 + part) * 8
                straight = sum(blocks[j] * coef_ref[at + j : at + j + 1, :] for j in range(PAIRS))
                crossed = sum(blocks[j] * coef_ref[at + 4 + j : at + 5 + j, :] for j in range(PAIRS))
                parts.append(straight + turn_half(crossed))
            cosine = twiddle_ref[twiddle_base + 2 * pair, rows, :]
            sine = twiddle_ref[twiddle_base + 2 * pair + 1, rows, :]
            store_split(rhs_ref, row, pair * LANES, parts[0] * cosine + parts[1] * sine, exact)
            store_split(rhs_ref, row + ROWS, pair * LANES, parts[1] * cosine - parts[0] * sine, exact)

    over_chunks(body)


def gather_pairs(values_ref, coef_ref, base, twiddle_ref, twiddle_base, pairs, store):
    def body(row):
        rows = pl.ds(row, CHUNK)
        straight, crossed = [0.0] * PAIRS, [0.0] * PAIRS
        for pair in range(pairs):
            lanes = slice(pair * LANES, (pair + 1) * LANES)
            real, imag = values_ref[rows, lanes], values_ref[pl.ds(row + ROWS, CHUNK), lanes]
            cosine = twiddle_ref[twiddle_base + 2 * pair, rows, :]
            sine = twiddle_ref[twiddle_base + 2 * pair + 1, rows, :]
            for part, value in enumerate((real * cosine - imag * sine, imag * cosine + real * sine)):
                at = base + (pair * 2 + part) * 8
                for j in range(PAIRS):
                    straight[j] = straight[j] + value * coef_ref[at + j : at + j + 1, :]
                    crossed[j] = crossed[j] + value * coef_ref[at + 4 + j : at + 5 + j, :]
        for j in range(PAIRS):
            store(j, rows, straight[j] + turn_half(crossed[j]))

    over_chunks(body)


GROUPS = ((0, 256), (256, 256), (512, 128))


def transform_into(dst_ref, mat_ref, which, rhs_ref, exact=True):
    for lane, width in GROUPS:
        dst_ref[:, lane : lane + width] = split_product(mat_ref, which, rhs_ref, lane, width, exact)


def multiply_spectra(left_ref, right_ref, rhs_ref, conjugate, exact=True):
    def body(row):
        top, bottom = pl.ds(row, CHUNK), pl.ds(row + ROWS, CHUNK)
        for pair in range(5):
            lanes = slice(pair * LANES, (pair + 1) * LANES)
            a_re, a_im = left_ref[top, lanes], left_ref[bottom, lanes]
            b_re, b_im = right_ref[top, lanes], right_ref[bottom, lanes]
            if conjugate:
                out_re, out_im = a_re * b_re + a_im * b_im, a_re * b_im - a_im * b_re
            else:
                out_re, out_im = a_re * b_re - a_im * b_im, a_re * b_im + a_im * b_re
            store_split(rhs_ref, row, pair * LANES, out_re, exact)
            store_split(rhs_ref, row + ROWS, pair * LANES, out_im, exact)

    over_chunks(body)


def pair_terms(modes_ref):
    rank_re, rank_im, in_re, in_im, out_re, out_im = (modes_ref[i] for i in range(2, 8))
    return (
        (out_re * in_re + out_im * in_im, out_re * in_im - out_im * in_re),
        (out_re * rank_re + out_im * rank_im, out_re * rank_im - out_im * rank_re),
        (rank_re * in_re + rank_im * in_im, rank_re * in_im - rank_im * in_re),
        (rank_re * rank_re + rank_im * rank_im, None),
    )


def mode_values(modes_ref):
    index = lax.broadcasted_iota(jnp.int32, modes_ref.shape[1:], 0).astype(F32)
    return -0.5 * jnp.exp(modes_ref[0]), math.pi * (index + modes_ref[1])


POINT_ROWS = 16


def resolvent(coef_ref, n, square_cos, cos_sin, scaled):
    den_re = coef_ref[8, pl.ds(n, 1), :] * square_cos - scaled
    den_im = coef_ref[9, pl.ds(n, 1), :] * cos_sin
    inverse = reciprocal(den_re * den_re + den_im * den_im)
    return den_re * inverse, -(den_im * inverse)


def complex_multiply(a_re, a_im, b_re, b_im):
    return a_re * b_re - a_im * b_im, a_re * b_im + a_im * b_re


def conj_multiply(a_re, a_im, b_re, b_im):
    return a_re * b_re + a_im * b_im, a_re * b_im - a_im * b_re


def combine(sums, sigma, cosine, sine):
    terms = []
    for p_re, p_im, q_re, q_im in (sums[4 * q : 4 * q + 4] for q in range(4)):
        swing = sigma * sine
        terms.append((-swing * p_im - cosine * q_re, swing * p_re - cosine * q_im))
    twice = 2.0 * cosine
    loop_re, loop_im = 1.0 + twice * terms[3][0], twice * terms[3][1]
    scale = reciprocal(loop_re * loop_re + loop_im * loop_im)
    inv = (loop_re * scale, -(loop_im * scale))
    ratio = complex_multiply(twice * terms[2][0], twice * terms[2][1], *inv)
    return terms, inv, ratio


QUARTER = 32


def cauchy_coefficients(modes_ref, sigma, coef_ref):
    lam_re, lam_im = mode_values(modes_ref)
    for q, (real, imag) in enumerate(pair_terms(modes_ref)):
        coef_ref[q] = real
        coef_ref[4 + q] = real * lam_re if imag is None else real * lam_re + imag * lam_im
    coef_ref[8] = lam_re * lam_re + lam_im * lam_im
    coef_ref[9] = -2.0 * sigma * lam_re


def wave_rows(wave_ref, pair, base, row):
    rows = pl.ds(pl.multiple_of(base + row, POINT_ROWS), POINT_ROWS)
    return wave_ref[0, pair, rows, :], wave_ref[1, pair, rows, :]


def cauchy_forward(index, sigma, coef_ref, wave_ref, base, sums_ref, spec_ref):
    sigma_sq = sigma * sigma
    pair, row = index // 2, index % 2 * POINT_ROWS
    rows = slice(row, row + POINT_ROWS)
    lanes = slice(pair * LANES, (pair + 1) * LANES)
    cosine, sine = wave_rows(wave_ref, pair, base, row)
    square_cos, cos_sin, scaled = cosine * cosine, cosine * sine, sigma_sq * (sine * sine)

    def add_mode(n, sums):
        sums = list(sums)
        for k in range(4):
            at = n * 4 + k
            inv_re, inv_im = resolvent(coef_ref, at, square_cos, cos_sin, scaled)
            for q in range(4):
                plain = coef_ref[q, pl.ds(at, 1), :]
                turned = coef_ref[4 + q, pl.ds(at, 1), :]
                sums[4 * q] = sums[4 * q] + plain * inv_re
                sums[4 * q + 1] = sums[4 * q + 1] + plain * inv_im
                sums[4 * q + 2] = sums[4 * q + 2] + turned * inv_re
                sums[4 * q + 3] = sums[4 * q + 3] + turned * inv_im
        return tuple(sums)

    zero = jnp.zeros((POINT_ROWS, LANES), F32)
    sums = lax.fori_loop(0, 8, add_mode, (zero,) * 16)
    for i in range(16):
        sums_ref[pair, i, rows, :] = sums[i]
    terms, _, ratio = combine(sums, sigma, cosine, sine)
    cut_re, cut_im = complex_multiply(*terms[1], *ratio)
    part_re, part_im = terms[0][0] - cut_re, terms[0][1] - cut_im
    spec_re, spec_im = complex_multiply(2.0 * cosine, 2.0 * sine, part_re, part_im)
    spec_ref[rows, lanes] = spec_re
    spec_ref[row + QUARTER : row + QUARTER + POINT_ROWS, lanes] = spec_im


PLACES = [(pair, row) for pair in range(2) for row in range(0, QUARTER, POINT_ROWS)]


def point_grads(sigma, wave_ref, base, sums_ref, spec_ref, grad_ref):
    zero = jnp.zeros((POINT_ROWS, LANES), F32)
    sigma_sum = zero
    for pair, row in PLACES:
        rows = slice(row, row + POINT_ROWS)
        lanes = slice(pair * LANES, (pair + 1) * LANES)
        cosine, sine = wave_rows(wave_ref, pair, base, row)
        sums = [sums_ref[pair, i, rows, :] for i in range(16)]
        terms, inv, ratio = combine(sums, sigma, cosine, sine)
        spec_re, spec_im = spec_ref[rows, lanes], spec_ref[row + QUARTER : row + QUARTER + POINT_ROWS, lanes]
        part = conj_multiply(2.0 * cosine, 2.0 * sine, spec_re, spec_im)
        left = conj_multiply(*ratio, *part)
        ratio_grad = conj_multiply(*terms[1], *part)
        back = conj_multiply(*inv, -ratio_grad[0], -ratio_grad[1])
        twice = 2.0 * cosine
        loop = conj_multiply(*ratio, *back)
        grads = (
            part,
            (-left[0], -left[1]),
            (twice * back[0], twice * back[1]),
            (-twice * loop[0], -twice * loop[1]),
        )
        swing = sigma * sine
        for q, (g_re, g_im) in enumerate(grads):
            grad_ref[pair, 4 * q, rows, :] = swing * g_im
            grad_ref[pair, 4 * q + 1, rows, :] = -swing * g_re
            grad_ref[pair, 4 * q + 2, rows, :] = -cosine * g_re
            grad_ref[pair, 4 * q + 3, rows, :] = -cosine * g_im
            sigma_sum = sigma_sum + sine * (g_im * sums[4 * q] - g_re * sums[4 * q + 1])
    return sigma_sum


def mode_sums(part, square_sum, sigma, coef_ref, wave_ref, base, grad_ref, back_ref):
    sigma_sq = sigma * sigma

    def mode(n, square_sum):
        plain = [coef_ref[q, pl.ds(n, 1), :] for q in range(4)]
        turned = [coef_ref[4 + q, pl.ds(n, 1), :] for q in range(4)]
        sums = [0.0] * 10
        for pair, row in PLACES:
            rows = slice(row, row + POINT_ROWS)
            cosine, sine = wave_rows(wave_ref, pair, base, row)
            square_cos, cos_sin, square_sin = cosine * cosine, cosine * sine, sine * sine
            inv_re, inv_im = resolvent(coef_ref, n, square_cos, cos_sin, sigma_sq * square_sin)
            grad_re, grad_im = 0.0, 0.0
            for q in range(4):
                p_re, p_im = grad_ref[pair, 4 * q, rows, :], grad_ref[pair, 4 * q + 1, rows, :]
                q_re, q_im = grad_ref[pair, 4 * q + 2, rows, :], grad_ref[pair, 4 * q + 3, rows, :]
                grad_re = grad_re + (plain[q] * p_re + turned[q] * q_re)
                grad_im = grad_im + (plain[q] * p_im + turned[q] * q_im)
                sums[q] = sums[q] + (p_re * inv_re + p_im * inv_im)
                sums[4 + q] = sums[4 + q] + (q_re * inv_re + q_im * inv_im)
            square_re = inv_re * inv_re - inv_im * inv_im
            square_im = 2.0 * inv_re * inv_im
            den_re, den_im = conj_multiply(square_re, square_im, grad_re, grad_im)
            sums[8] = sums[8] - den_re * square_cos
            sums[9] = sums[9] - den_im * cos_sin
            square_sum = square_sum + den_re * square_sin
        for i in range(10):
            back_ref[i, pl.ds(n, 1), :] = column_sum(sums[i])
        return square_sum

    return lax.fori_loop(part * 8, part * 8 + 8, mode, square_sum)


def mode_gradients(modes_ref, sigma, nyquist_grad, step, sigma_sum, square_sum, back_ref):
    plain_grad = [fold(back_ref[q]) for q in range(4)]
    turned_grad = [fold(back_ref[4 + q]) for q in range(4)]
    abs_grad, skew_grad = fold(back_ref[8]), fold(back_ref[9])
    lam_re, lam_im = mode_values(modes_ref)
    plain_grad[0] = plain_grad[0] + step * nyquist_grad
    rank_re, rank_im, in_re, in_im, out_re, out_im = (modes_ref[i] for i in range(2, 8))
    lam_re_grad = 2.0 * lam_re * abs_grad - 2.0 * sigma * skew_grad
    lam_im_grad = 2.0 * lam_im * abs_grad
    real_grad, imag_grad = [], []
    terms = pair_terms(modes_ref)
    for q, (real, imag) in enumerate(terms):
        lam_re_grad = lam_re_grad + turned_grad[q] * real
        if imag is not None:
            lam_im_grad = lam_im_grad + turned_grad[q] * imag
        real_grad.append(plain_grad[q] + turned_grad[q] * lam_re)
        imag_grad.append(turned_grad[q] * lam_im)
    r0, r1, r2, r3 = real_grad
    i0, i1, i2, _ = imag_grad
    grads = (
        lam_re_grad * lam_re,
        math.pi * lam_im_grad,
        r1 * out_re - i1 * out_im + r2 * in_re + i2 * in_im + 2.0 * r3 * rank_re,
        r1 * out_im + i1 * out_re + r2 * in_im - i2 * in_re + 2.0 * r3 * rank_im,
        r0 * out_re - i0 * out_im + r2 * rank_re - i2 * rank_im,
        r0 * out_im + i0 * out_re + r2 * rank_im + i2 * rank_re,
        r0 * in_re + i0 * in_im + r1 * rank_re + i1 * rank_im,
        r0 * in_im - i0 * in_re + r1 * rank_im - i1 * rank_re,
    )
    sigma_grad = (
        fold(column_sum(sigma_sum) + 2.0 * sigma * column_sum(square_sum))
        - 2.0 * column_sum(skew_grad * lam_re)
    )
    nyquist = step * column_sum(terms[0][0])
    return grads, nyquist * nyquist_grad - sigma * sigma_grad


def ring_place(chan):
    z, y = lax.div(chan, 2), lax.rem(chan, 2)
    return z + y * (7 - 2 * z)


def ring_chan(place):
    back = lax.div(place, 4)
    z = place * (1 - back) + (7 - place) * back
    return 2 * z + back


TURNS = (1, -1)


def block_kernel(
    loaded, bucket_ref, items_ref, tokens_ref, cotangent_ref, gain1_ref, bias1_ref, raw_modes_ref, log_dt_ref, skip_ref,
    wa_ref, ba_ref, wb_ref, bb_ref, gain2_ref, bias2_ref, up_ref, bup_ref, down_ref, bdown_ref,
    levels_ref, coefc_ref, mat_ref, tw_ref, wave_ref,
    out_ref, dtok_ref, gw_ref, gm_ref, gv_ref,
    tok_ref, aux_ref, coefl_ref, modes_ref,
    wab_ref, wh_ref, gab_w_ref, gh_ref,
    stage_ref, sib_ab_ref, ring_ab_ref, ring_h_ref, part_ab_ref, cross_ref, keep_ref, swap_ref, gate_total_ref,
    in_send, in_recv, head_send, head_recv, acts_send, acts_recv, back_send, back_recv, late_send, late_recv,
    sum_send, sum_recv, tail_send, dp_send, dp_low, dp_recv, spec_send, spec_recv, sgrad_send, sgrad_recv,
    hat_ref, norm_ref, slope_ref, conv_ref, rhs_ref, freq_ref, sig_ref, ans_ref, taps_ref,
    mcoef_ref, sums_ref, pgrad_ref, mback_ref, sgrad_ref, taps_freq_ref,
    gate_ref, swish_ref, res_ref, hat2_ref, acts_ref, norm2_ref, gradf_ref, branch_ref, back2_ref, half_send, half_recv,
    gab_ref, hid_ref, gpre_ref, acts_t_ref, norm2_t_ref, gradf_t_ref,
    gring_ss, gring_rs, gsib_ss, gsib_rs, gx_ss, gx_rs, gdx_ss, gdx_rs, gswap_ss, gswap_rs, core_ss, core_rs,
    rring_ss, rring_rs, rsib_ss, rsib_rs, rx_ss, rx_rs, rdx_ss, rdx_rs, rswap_ss, rswap_rs,
    a2a_ss, a2a_rs, dp_ss, dp_rs, spec_ss, spec_rs,
):
    dp, chan = lax.axis_index("dp"), lax.axis_index("chan")
    core = lax.rem(dp, 2)
    sibling = dp + 1 - 2 * core
    place = ring_place(chan)
    spots = [lax.rem(place + offset, 8) if offset else place for offset in range(8)]
    around = [ring_chan(spot) if offset else chan for offset, spot in enumerate(spots)]
    groups = [lax.rem(spot, 4) for spot in spots]
    group_lanes = [pl.multiple_of(lax.div(spot, 4) * LANES, LANES) for spot in spots]
    nexts = [around[1], around[7]]
    chan_peers = [chan] + [lax.rem(chan + r, N_CHAN) for r in range(1, N_CHAN)]
    dp_peers = [dp] + [lax.rem(dp + r, 4) for r in range(1, 4)]
    across = dp_peers[2]

    def chan_at(offset):
        return around[offset % 8]

    barrier = pltpu.get_barrier_semaphore()
    for r in range(1, N_CHAN):
        pl.semaphore_signal(barrier, inc=1, device_id={"chan": chan_peers[r]}, device_id_type=MESH)
    for r in range(1, 4):
        pl.semaphore_signal(barrier, inc=1, device_id={"dp": dp_peers[r]}, device_id_type=MESH)

    loaded(0, 1, 7, 8, 9, 10, 11, 12, 13, 14, 15, 16)
    pending = []

    def remote(src, dst, send_sem, recv_sem, **device):
        return pltpu.make_async_remote_copy(
            src_ref=src, dst_ref=dst, send_sem=send_sem, recv_sem=recv_sem, device_id=device, device_id_type=MESH
        )

    def send(*args, **device):
        copy = remote(*args, **device)
        copy.start()
        pending.append(copy)

    def exchange(which, source, recv_ref):
        def copy(r):
            peer = chan_peers[r]
            return remote(
                source(peer), recv_ref.at[chan], a2a_ss.at[which, r - 1], a2a_rs.at[which, r - 1], chan=peer
            )

        def start():
            for r in range(1, N_CHAN):
                copy(r).start()

        def wait():
            for r in range(1, N_CHAN):
                copy(r).wait_recv()

        def finish():
            for r in range(1, N_CHAN):
                copy(r).wait_send()

        return start, wait, finish

    def rows_at(number, count):
        return pl.ds(pl.multiple_of(number, ROWS), count)

    def launch(copy):
        copy.start()
        pending.append(copy)

    own_row = dp * ROWS
    pair_row = (dp - core) * ROWS
    away_row = 2 * ROWS - pair_row
    gate_row, gate_away = (core * 2 + lax.div(dp, 2)) * ROWS, (core * 2 + 1 - lax.div(dp, 2)) * ROWS
    gate_pair, gate_other = core * 2 * ROWS, (1 - core) * 2 * ROWS
    half_lanes = pl.multiple_of(core * LANES, LANES)
    other_lanes = pl.multiple_of((1 - core) * LANES, LANES)

    def gate_view(ref):
        return lambda offset, row, count: ref.at[around[offset % 8], rows_at(row, count), :]

    def hidden_view(ref):
        return lambda offset, row, count: ref.at[
            :, groups[offset % 8], rows_at(row, count), pl.ds(group_lanes[offset % 8], LANES)
        ]

    class Ring:
        def __init__(self, which, view, base, count, hook=None):
            self.which, self.view, self.base, self.count, self.hook = which, view, base, count, hook

        def piece(self, turn, step, base):
            half = self.count // 2
            if step == 4:
                return self.view(4, base + turn * half, half)
            return self.view(-TURNS[turn] * step, base, self.count)

        def copy(self, turn, step, ref):
            slot = turn * 4 + step - 1
            return remote(ref, ref, gring_ss.at[self.which, slot], gring_rs.at[self.which, slot], chan=nexts[turn])

        def send(self, turn, step):
            half = self.count // 2
            if step == 4:
                ref = self.view(-TURNS[turn] * 3, self.base + turn * half, half)
            else:
                ref = self.piece(turn, step - 1, self.base)
            launch(self.copy(turn, step, ref))

        def start(self):
            for turn in range(2):
                self.send(turn, 1)

        def step(self, step):
            for turn in range(2):
                self.copy(turn, step, self.piece(turn, step, self.base)).wait_recv()
                if step < 4:
                    self.send(turn, step + 1)
                if self.hook:
                    self.hook(turn, step)

    def slot_of(turn, step):
        return turn * 4 + step - 1 if step else 8

    def gate_sib(base):
        ref = wab_ref.at[:, rows_at(base, 256), :]
        return remote(ref, ref, gsib_ss, gsib_rs, dp=sibling)

    def gate_spread():
        launch(gate_sib(gate_pair))

    def hidden_cross(which, turn, step, base):
        ref, slot = hidden_rings[which].piece(turn, step, base), slot_of(turn, step)
        return remote(ref, ref, gdx_ss.at[which, slot], gdx_rs.at[which, slot], dp=across)

    gate_ring = Ring(0, gate_view(wab_ref), gate_pair, 256)
    def hidden_part(which):
        def view(offset, row, count):
            lanes = pl.ds(group_lanes[offset % 8], LANES)
            return wh_ref.at[which, groups[offset % 8], rows_at(row, count), lanes]

        return Ring(
            1 + which, view, pair_row, 256, lambda turn, step: launch(hidden_cross(which, turn, step, pair_row))
        )

    hidden_rings = up_ring, down_ring = hidden_part(0), hidden_part(1)

    def gate_over(row):
        ref = gate_ring.view(0, row, ROWS)
        return remote(ref, ref, gx_ss, gx_rs, dp=across)

    def swap_copy(row):
        return remote(stage_ref, hidden_view(wh_ref)(0, row, ROWS), gswap_ss, gswap_rs, dp=sibling)

    def gather_prepare():
        gates = jnp.concatenate([wa_ref[...], wb_ref[...]], axis=0).T.astype(BF16)
        wab_ref[chan, rows_at(gate_row, ROWS), :] = gates
        for which, values in enumerate((up_ref[...], down_ref[...].T)):
            first, second = values[:, :LANES], values[:, LANES:]
            kept = jnp.where(core == 0, first, second)
            wh_ref[which, groups[0], rows_at(own_row, ROWS), pl.ds(group_lanes[0], LANES)] = kept.astype(BF16)
            stage_ref[which] = jnp.where(core == 0, second, first).astype(BF16)

    def gather_start():
        launch(swap_copy(own_row))
        launch(gate_over(gate_row))

    def hidden_first():
        swap_copy(sibling * ROWS).wait_recv()
        for which in range(2):
            hidden_rings[which].start()
            launch(hidden_cross(which, 0, 0, pair_row))

    def gate_first():
        gate_over(gate_away).wait_recv()
        gate_ring.start()

    ring_steps = [(0, 0)] + [(turn, step) for step in range(1, 5) for turn in range(2)]

    def gates_arrived():
        gate_sib(gate_other).wait_recv()

    def hidden_arrived(*steps):
        for turn, step in ring_steps:
            if step in steps:
                for which in range(2):
                    hidden_cross(which, turn, step, away_row).wait_recv()

    def beside(ref, j):
        start = 2 * j * ROWS
        return jnp.concatenate(
            [ref[:, start : start + ROWS].astype(F32), ref[:, start + ROWS : start + 2 * ROWS].astype(F32)], axis=0
        ).T

    for j in range(PAIRS):
        packed = beside(tokens_ref, j)
        tok_ref[j * ROWS : (j + 1) * ROWS, :] = packed.astype(BF16)
        for first, values in ((0, packed), (HALF, beside(cotangent_ref, j))):
            low, high = split_pair(values)
            in_send[2 * j, first : first + HALF, :] = low.astype(BF16)
            in_send[2 * j + 1, first : first + HALF, :] = high.astype(BF16)
    in_recv[chan] = in_send[chan]

    lane_id = lax.broadcasted_iota(jnp.int32, (8, LANES), 1)
    row_id = lax.broadcasted_iota(jnp.int32, (8, LANES), 0)
    halves = jnp.where((lane_id >= HALF) == (row_id == 1), 1.0, 0.0) * jnp.where(row_id < 2, 1.0, 0.0)
    halves = halves.astype(BF16)

    def token_sums(parts):
        total = 0.0
        for part in parts:
            total = total + dot_nt(halves, part)
        return [total[h : h + 1, j * ROWS : (j + 1) * ROWS] for h in range(2) for j in range(PAIRS)]

    def split(values):
        high = values.astype(BF16)
        return high, (values - high.astype(F32)).astype(BF16)

    tokens = tok_ref[...]
    wide_tokens = tokens.astype(F32)
    for i, sums in enumerate(token_sums([tokens]) + token_sums(split(wide_tokens * wide_tokens))):
        head_send[i : i + 1, :] = sums

    def row(*refs):
        return jnp.concatenate([ref[...].reshape(1, HALF) for ref in refs], axis=1)

    bup = bup_ref[...].reshape(1, 2 * LANES)
    head_send[16:17, :] = row(ba_ref, bb_ref)
    head_send[17:18, :] = row(gain2_ref, bias2_ref)
    head_send[18:19, :] = row(bdown_ref, bdown_ref)
    head_send[19:20, :] = bup[:, :LANES]
    head_send[20:21, :] = bup[:, LANES:]
    head_send[21:24, :] = jnp.zeros((3, LANES), F32)
    head_recv[chan] = head_send[...]
    head = exchange(0, lambda peer: head_send, head_recv)
    inputs = exchange(1, lambda peer: in_send.at[peer], in_recv)
    gather_prepare()
    pl.semaphore_wait(barrier, N_CHAN - 1 + 3)
    gather_start()
    head[0]()
    hidden_first()

    loaded(4, 5, 17, 21)
    level, filled = bucket_ref[0], items_ref[0]
    coefl_ref[...] = levels_ref[level]
    item_blocks = jnp.where(level == 0, 2, jnp.where(level == 1, 4, 8))
    block_id = 2 * (row_id % PAIRS) + jnp.where(lane_id >= HALF, 1, 0)
    bound = jnp.where(row_id < PAIRS, filled * item_blocks, item_blocks)
    aux_ref[...] = jnp.where(block_id < bound, 1.0, 0.0)
    for i in range(8):
        modes_ref[i] = jnp.concatenate([raw_modes_ref[i], raw_modes_ref[i]], axis=1)
    inputs[0]()
    gate_first()
    log_dt = row(log_dt_ref, log_dt_ref)
    sigma, step_size = 2.0 * jnp.exp(-log_dt), jnp.exp(log_dt)

    base = pl.multiple_of(dp * QUARTER, QUARTER)

    def spec_copy(which, r):
        peer = dp_peers[r]
        src, dst = ((spec_send, spec_recv), (sgrad_send.at[peer], sgrad_recv))[which]
        return remote(src, dst.at[dp], spec_ss.at[which, r - 1], spec_rs.at[which, r - 1], dp=peer)

    cauchy_coefficients(modes_ref, sigma, mcoef_ref)
    cauchy_forward(0, sigma, mcoef_ref, wave_ref, base, sums_ref, spec_send)
    cauchy_forward(1, sigma, mcoef_ref, wave_ref, base, sums_ref, spec_send)
    cauchy_forward(2, sigma, mcoef_ref, wave_ref, base, sums_ref, spec_send)
    cauchy_forward(3, sigma, mcoef_ref, wave_ref, base, sums_ref, spec_send)
    spec_recv[dp] = spec_send[...]
    for r in range(1, 4):
        spec_copy(0, r).start()
    up_ring.step(1)
    gate_ring.step(1)
    down_ring.step(1)

    head[1]()
    sums = head_recv[0, 0:16, :]
    for c in range(1, N_CHAN):
        sums = sums + head_recv[c, 0:16, :]
    mean = sums[0:8] * (1.0 / MODEL_WIDTH)
    rstd = lax.rsqrt(sums[8:16] * (1.0 / MODEL_WIDTH) - mean * mean + EPSILON)

    def columns(rows):
        tall = rows.T
        return [jnp.where(low_lanes(ROWS), tall[:, j : j + 1], tall[:, 4 + j : 5 + j]) for j in range(PAIRS)]

    loaded(2, 3, 6, 18, 19, 20)
    gain1, bias1, skip = row(gain1_ref, gain1_ref), row(bias1_ref, bias1_ref), row(skip_ref, skip_ref)
    mean_cols, rstd_cols = columns(mean), columns(rstd)
    for j in range(PAIRS):
        hat = (tok_ref[j * ROWS : (j + 1) * ROWS, :].astype(F32) - mean_cols[j]) * rstd_cols[j]
        hat_ref[j] = hat
        norm_ref[j] = hat * gain1 + bias1

    spread_pairs(lambda j, rows: norm_ref[j, rows, :], coefl_ref, 0, tw_ref, 0, 5, rhs_ref, False)
    transform_into(sig_ref, mat_ref, 0, rhs_ref, False)

    for r in range(1, 4):
        spec_copy(0, r).wait_recv()
    for source in range(4):
        store_split(rhs_ref, source * QUARTER, 0, spec_recv[source, :QUARTER, :])
        store_split(rhs_ref, ROWS + source * QUARTER, 0, spec_recv[source, QUARTER:, :])
    up_ring.step(2)
    gate_ring.step(2)
    freq_ref[:, 0:256] = split_product(mat_ref, 1, rhs_ref, 0, 256)
    even = split_product(mat_ref, 2, rhs_ref, LANES, LANES)
    freq_ref[:, LANES:256] = jnp.where(low_lanes(256), freq_ref[:, LANES:256], even)
    sign = 1.0 - 2.0 * (lax.broadcasted_iota(jnp.int32, (CHUNK, LANES), 0) % 2).astype(F32)
    nyquist = step_size * column_sum(mcoef_ref[0]) * (1.0 / TOK_DEV)
    down_ring.step(2)

    def store_taps(j, rows, values):
        taps_ref[j, rows, :] = (values + sign * nyquist) * aux_ref[4 + j : 5 + j, :]

    gather_pairs(freq_ref, coefc_ref, 160, tw_ref, 10, 2, store_taps)
    spread_pairs(lambda j, rows: taps_ref[j, rows, :], coefc_ref, 0, tw_ref, 0, 5, rhs_ref, False)
    transform_into(ans_ref, mat_ref, 0, rhs_ref, False)
    multiply_spectra(sig_ref, ans_ref, rhs_ref, False, False)
    transform_into(freq_ref, mat_ref, 1, rhs_ref, False)
    gate_ring.step(3)
    up_ring.step(3)

    def store_conv(j, rows, values):
        conv_ref[j, rows, :] = values
    gather_pairs(freq_ref, coefl_ref, 80, tw_ref, 0, 5, store_conv)
    for j in range(PAIRS):
        mixed = conv_ref[j] * aux_ref[j : j + 1, :] + skip * norm_ref[j]
        cumulative, density = normal_parts(mixed)
        slope_ref[j] = cumulative + mixed * density
        low, high = split_pair(mixed * cumulative)
        acts_send[2 * j] = low.astype(BF16)
        acts_send[2 * j + 1] = high.astype(BF16)
    acts_recv[chan] = acts_send[chan]
    acts = exchange(2, lambda peer: acts_send.at[peer], acts_recv)
    acts[0]()

    def joined(ref, pair, first):
        return join_pair(
            ref[2 * pair, first : first + HALF, :].astype(F32), ref[2 * pair + 1, first : first + HALF, :].astype(F32)
        )

    def lanes_of(pair):
        return slice(pair * LANES, (pair + 1) * LANES)

    def gate_lanes(pair):
        return lanes_of(pair % 2 * 2 + pair // 2)

    def core_copy(which, src, dst):
        return remote(src, dst, core_ss.at[which], core_rs.at[which], dp=sibling)

    def other_core(which, ref):
        return core_copy(which, ref.at[core], ref.at[core])

    def vector(row, first, second):
        return interleave(head_recv[first, 16 + row : 17 + row, :], head_recv[second, 16 + row : 17 + row, :])

    def both_cores(ref):
        return ref[...].reshape(2 * ROWS, MODEL_WIDTH)

    def hidden_group(offset):
        group = groups[offset]
        low, high = 2 * group, 7 - 2 * group
        bias = jnp.concatenate(
            [jnp.where(core == 0, head_recv[c, 19:20, :], head_recv[c, 20:21, :]) for c in (low, high)], axis=1
        )
        pre = dot_nn(both_cores(norm2_ref), wh_ref[0, group]) + bias
        cumulative, density = normal_parts(pre)
        hidden = (pre * cumulative).astype(BF16)
        hid_ref[group] = hidden
        grad = dot_nn(both_cores(gradf_ref), wh_ref[1, group]) * (cumulative + pre * density)
        grad = grad.astype(BF16)
        gpre_ref[group] = grad
        sums = column_sum(grad.astype(F32))
        tail_send[low, pl.ds(3 + core, 1), :] = sums[:, 0:LANES]
        tail_send[high, pl.ds(3 + core, 1), :] = sums[:, LANES : 2 * LANES]
        branch_ref[...] += dot_nt(hidden, wh_ref[1, group]).reshape(2, ROWS, MODEL_WIDTH)
        back2_ref[...] += dot_nt(grad, wh_ref[0, group]).reshape(2, ROWS, MODEL_WIDTH)

    def offset_of(turn, step):
        return TURNS[turn] * (5 - step)

    def far(offset):
        return 4 if offset == -4 else offset

    class RingBack:
        def __init__(self, which, view, base, count, ring_ref, extra):
            self.which, self.view, self.base, self.count = which, view, base, count
            self.ring_ref, self.extra = ring_ref, extra

        def copy(self, turn, step):
            slot = turn * 4 + step - 1
            half = self.count // 2
            if step == 1:
                dst = self.ring_ref.at[slot]
                lead = (slice(None),) * (len(dst.shape) - 2)
                src, dst = self.view(4, self.base + turn * half, half), dst.at[lead + (pl.ds(0, half), slice(None))]
            else:
                src, dst = self.view(offset_of(turn, step), self.base, self.count), self.ring_ref.at[slot]
            return remote(src, dst, rring_ss.at[self.which, slot], rring_rs.at[self.which, slot], chan=nexts[turn])

        def whole(self, offset):
            return self.view(offset, self.base, self.count)[...].astype(F32) + self.extra(offset)

        def step(self, step):
            half = self.count // 2
            if step == 1:
                self.view(4, self.base, self.count)[...] = self.whole(4).astype(BF16)
                for turn in range(2):
                    launch(self.copy(turn, 1))
                return
            for turn in range(2):
                offset, slot = offset_of(turn, step), turn * 4 + step - 2
                total = self.whole(offset)
                self.copy(turn, step - 1).wait_recv()
                if step == 2:
                    parts = [total[..., :half, :], total[..., half:, :]]
                    parts[turn] = parts[turn] + self.ring_ref[slot][..., :half, :].astype(F32)
                    total = jnp.concatenate(parts, axis=-2)
                else:
                    total = total + self.ring_ref[slot].astype(F32)
                self.view(offset, self.base, self.count)[...] = total.astype(BF16)
                launch(self.copy(turn, step))

        def total(self):
            total = self.whole(0)
            for turn in range(2):
                self.copy(turn, 4).wait_recv()
                total = total + self.ring_ref[turn * 4 + 3].astype(F32)
            return total

    waited = set()

    def wait_once(name, copy):
        if name not in waited:
            waited.add(name)
            copy().wait_recv()

    def gate_share():
        ref = gab_w_ref.at[:, rows_at(gate_other, 256), :]
        return remote(ref, sib_ab_ref, rsib_ss, rsib_rs, dp=sibling)

    def gate_extra(offset):
        wait_once("gates", gate_share)
        return sib_ab_ref[around[offset % 8]].astype(F32)

    def cross_copy(pair):
        src = gh_ref.at[:, groups[pair], rows_at(away_row, 256), :]
        return remote(src, cross_ref.at[pair], rdx_ss.at[pair], rdx_rs.at[pair], dp=across)

    def hidden_extra(offset):
        pair = offset % 4
        wait_once(pair, lambda: cross_copy(pair))
        return cross_ref[pair, :, :, pl.ds(group_lanes[offset % 8], LANES)].astype(F32)

    gate_g = RingBack(0, gate_view(gab_w_ref), gate_pair, 256, ring_ab_ref, gate_extra)

    hidden_g = RingBack(1, hidden_view(gh_ref), pair_row, 256, ring_h_ref, hidden_extra)

    def hidden_grads(offset):
        group = groups[offset]
        gh_ref[1, group] = dot_nn(gradf_t_ref[...], hid_ref[group]).astype(BF16)
        gh_ref[0, group] = dot_nn(norm2_t_ref[...], gpre_ref[group]).astype(BF16)
        launch(cross_copy(offset))

    def part_copy():
        return remote(part_ab_ref.at[0], part_ab_ref.at[1], rx_ss, rx_rs, dp=across)

    def last_swap():
        return remote(keep_ref.at[:, rows_at((1 - core) * ROWS, ROWS), :], swap_ref, rswap_ss, rswap_rs, dp=sibling)

    def gate_last():
        gate_total_ref[...] = gate_g.total()
        part_ab_ref[0] = gate_total_ref[rows_at((1 - lax.div(dp, 2)) * ROWS, ROWS), :].astype(BF16)
        launch(part_copy())

    def gate_finish():
        part_copy().wait_recv()
        gw_ref[:, 0:128] = gate_total_ref[rows_at(lax.div(dp, 2) * ROWS, ROWS), :] + part_ab_ref[1].astype(F32)

    def hidden_last():
        keep_ref[...] = hidden_g.total()
        launch(last_swap())
        for which in range(2):
            gw_ref[:, pl.ds(pl.multiple_of(128 + 256 * which + half_lanes, LANES), LANES)] = keep_ref[
                which, rows_at(core * ROWS, ROWS), :
            ]

    def hidden_finish():
        last_swap().wait_recv()
        for which in range(2):
            gw_ref[:, pl.ds(pl.multiple_of(128 + 256 * which + other_lanes, LANES), LANES)] = swap_ref[which]

    late = exchange(4, lambda peer: late_send.at[peer], late_recv)


    def gate_grads(*offsets):
        for offset in offsets:
            c = chan_at(offset)
            gab_w_ref[c] = dot_nn(acts_t_ref[...], gab_ref[c]).astype(BF16)
        if 0 in offsets:
            launch(gate_share())

    def late_messages():
        core_copy(3, half_send.at[1], half_recv.at[1]).wait_recv()
        for p in range(PAIRS):
            out = res_ref[p] + (branch_ref[core, :, lanes_of(p)] + half_recv[1, :, lanes_of(p)].astype(F32)) + interleave(head_recv[2 * p, 18:19, :], head_recv[2 * p + 1, 18:19, :])[0]
            low, high = split_pair(out)
            late_send[2 * p, :HALF, :] = low.astype(BF16)
            late_send[2 * p + 1, :HALF, :] = high.astype(BF16)
        for c in range(N_CHAN):
            late_send[c, ROWS:, :] = jnp.concatenate([tail_send[c], jnp.zeros((8, LANES), F32)], axis=0).astype(BF16)
        late_recv[chan] = late_send[chan]
        late[0]()

    back = exchange(3, lambda peer: back_send.at[peer], back_recv)

    inputs[1]()
    for p in range(PAIRS):
        gradf_ref[core, :, lanes_of(p)] = joined(in_recv, p, HALF).astype(BF16)
    launch(other_core(0, gradf_ref))
    gate_ring.step(4)
    gate_spread()
    down_ring.step(3)
    gates_arrived()
    acts[1]()
    for p in range(PAIRS):
        acts_ref[:, gate_lanes(p)] = joined(acts_recv, p, 0).astype(BF16)

    total = 0.0
    for p in range(PAIRS):
        first = dot_nn(acts_ref[...], wab_ref[2 * p]) + head_recv[2 * p, 16:17, :]
        second = dot_nn(acts_ref[...], wab_ref[2 * p + 1]) + head_recv[2 * p + 1, 16:17, :]
        gate, raw = interleave(first, second)
        swish = lax.logistic(raw)
        gate_ref[p], swish_ref[p] = gate, swish
        resid = joined(in_recv, p, 0) + gate * swish
        res_ref[p] = resid
        total = total + resid
    mean2 = jnp.sum(total, axis=1, keepdims=True) * (1.0 / MODEL_WIDTH)
    total = 0.0
    for p in range(PAIRS):
        centred = res_ref[p] - mean2
        total = total + centred * centred
    rstd2 = lax.rsqrt(jnp.sum(total, axis=1, keepdims=True) * (1.0 / MODEL_WIDTH) + EPSILON)
    gain2 = []
    for p in range(PAIRS):
        gain, bias = vector(1, 2 * p, 2 * p + 1)
        gain2.append(gain)
        hat = (res_ref[p] - mean2) * rstd2
        hat2_ref[p] = hat
        norm2_ref[core, :, lanes_of(p)] = (hat * gain + bias).astype(BF16)
    launch(other_core(1, norm2_ref))
    branch_ref[...] = jnp.zeros_like(branch_ref)
    acts_t_ref[...] = acts_ref[...].astype(F32).T.astype(BF16)
    back2_ref[...] = jnp.zeros_like(back2_ref)
    for c in range(N_CHAN):
        tail_send[c, 3:8, :] = jnp.zeros((5, LANES), F32)
    hidden_arrived(2)
    down_ring.step(4)
    other_core(0, gradf_ref).wait_recv()
    up_ring.step(4)
    gradf_t_ref[...] = both_cores(gradf_ref).astype(F32).T.astype(BF16)
    hidden_arrived(1, 3)
    other_core(1, norm2_ref).wait_recv()
    norm2_t_ref[...] = both_cores(norm2_ref).astype(F32).T.astype(BF16)
    hidden_group(3)
    hidden_group(1)
    hidden_grads(3)
    hidden_arrived(0, 4)
    hidden_group(0)
    hidden_group(2)
    half_send[0] = back2_ref[1 - core].astype(BF16)
    launch(core_copy(2, half_send.at[0], half_recv.at[0]))
    hidden_grads(0)
    half_send[1] = branch_ref[1 - core].astype(BF16)
    launch(core_copy(3, half_send.at[1], half_recv.at[1]))
    core_copy(2, half_send.at[0], half_recv.at[0]).wait_recv()
    back2 = back2_ref[core] + half_recv[0].astype(F32)
    back2_ref[core] = back2

    mean_q, mean_qx = 0.0, 0.0
    for p in range(PAIRS):
        grad, hat = back2_ref[core, :, lanes_of(p)], hat2_ref[p]
        q = grad * gain2[p]
        mean_q = mean_q + q
        mean_qx = mean_qx + q * hat
        gain_grad, bias_grad = interleave(column_sum(grad * hat), column_sum(grad))
        tail_send[2 * p, 1:2, :] = gain_grad
        first, second = interleave(turn_half(column_sum(grad * hat)), turn_half(column_sum(grad)))
        tail_send[2 * p + 1, 1:2, :] = first
    mean_q = jnp.sum(mean_q, axis=1, keepdims=True) * (1.0 / MODEL_WIDTH)
    mean_qx = jnp.sum(mean_qx, axis=1, keepdims=True) * (1.0 / MODEL_WIDTH)
    for p in range(PAIRS):
        hat = hat2_ref[p]
        extra = rstd2 * (back2_ref[core, :, lanes_of(p)] * gain2[p] - mean_q - hat * mean_qx)
        grad_f = joined(in_recv, p, HALF)
        grad_resid = grad_f + extra
        gate, swish = gate_ref[p], swish_ref[p]
        grad_a = (grad_resid * swish).astype(BF16).astype(F32)
        grad_b = (grad_resid * gate * swish * (1.0 - swish)).astype(BF16).astype(F32)
        first, second = interleave(grad_a, grad_b)
        gab_ref[2 * p] = first.astype(BF16)
        gab_ref[2 * p + 1] = second.astype(BF16)
        tail_send[2 * p, 0:1, :] = column_sum(first)
        tail_send[2 * p + 1, 0:1, :] = column_sum(second)
        low, high = interleave(column_sum(grad_f), column_sum(grad_f))
        tail_send[2 * p, 2:3, :] = low
        tail_send[2 * p + 1, 2:3, :] = high
        low, high = split_pair(extra)
        late_send[2 * p, HALF:ROWS, :] = low.astype(BF16)
        late_send[2 * p + 1, HALF:ROWS, :] = high.astype(BF16)
    grad_acts = 0.0
    for c in range(N_CHAN):
        grad_acts = grad_acts + dot_nt(gab_ref[c], wab_ref[c])
    for p in range(PAIRS):
        low, high = split_pair(grad_acts[:, gate_lanes(p)])
        back_send[2 * p] = low.astype(BF16)
        back_send[2 * p + 1] = high.astype(BF16)
    back_recv[chan] = back_send[chan]
    back[0]()
    hidden_grads(1)
    gate_grads(4, 3, -3)
    late_messages()
    gate_grads(2, -2, 1, -1, 0)

    back[1]()
    skip_grad = 0.0
    for j in range(PAIRS):
        grad = joined(back_recv, j, 0) * slope_ref[j]
        slope_ref[j] = grad
        conv_ref[j] = grad * aux_ref[j : j + 1, :]
        skip_grad = skip_grad + column_sum(grad * norm_ref[j])
    hidden_g.step(1)
    gate_g.step(1)
    hidden_grads(2)
    spread_pairs(lambda j, rows: conv_ref[j, rows, :], coefl_ref, 0, tw_ref, 0, 5, rhs_ref, False)
    transform_into(freq_ref, mat_ref, 0, rhs_ref, False)
    multiply_spectra(sig_ref, freq_ref, rhs_ref, True)
    gate_g.step(2)
    hidden_g.step(2)
    transform_into(sig_ref, mat_ref, 1, rhs_ref)

    def store_kernel_grad(j, rows, values):
        taps_ref[j, rows, :] = values * aux_ref[4 + j : 5 + j, :]

    gather_pairs(sig_ref, coefc_ref, 80, tw_ref, 0, 5, store_kernel_grad)
    nyquist_grad = 0.0
    for j in range(PAIRS):
        whole_sign = 1.0 - 2.0 * (lax.broadcasted_iota(jnp.int32, (ROWS, LANES), 0) % 2).astype(F32)
        nyquist_grad = nyquist_grad + column_sum(taps_ref[j] * whole_sign)
    nyquist_grad = fold(nyquist_grad) * (1.0 / TOK_DEV)
    spread_pairs(lambda j, rows: taps_ref[j, rows, :], coefc_ref, 192, tw_ref, 10, 2, rhs_ref)
    taps_freq_ref[...] = split_product(mat_ref, 0, rhs_ref, 0, 256)
    even = split_product(mat_ref, 3, rhs_ref, LANES, LANES)
    taps_freq_ref[:, LANES:256] = jnp.where(low_lanes(256), taps_freq_ref[:, LANES:256], even)
    for source in range(4):
        rows = slice(source * QUARTER, (source + 1) * QUARTER)
        sgrad_send[source, :QUARTER, :] = taps_freq_ref[rows, :]
        sgrad_send[source, QUARTER:, :] = taps_freq_ref[ROWS + source * QUARTER : ROWS + (source + 1) * QUARTER, :]
    sgrad_recv[dp] = sgrad_send[dp]
    for r in range(1, 4):
        spec_copy(1, r).start()
    gate_g.step(3)
    hidden_g.step(3)

    multiply_spectra(ans_ref, freq_ref, rhs_ref, True, False)
    transform_into(freq_ref, mat_ref, 1, rhs_ref, False)
    late[1]()
    gather_pairs(freq_ref, coefl_ref, 80, tw_ref, 0, 5, store_conv)
    gain_grad, bias_grad = 0.0, 0.0
    scaled, crossed = [], []
    for j in range(PAIRS):
        grad = conv_ref[j] + skip * slope_ref[j]
        conv_ref[j] = grad
        gain_grad = gain_grad + column_sum(grad * hat_ref[j])
        bias_grad = bias_grad + column_sum(grad)
    conv = conv_ref[...].reshape(PAIRS * ROWS, LANES) * gain1
    for i, sums in enumerate(
        token_sums(split(conv)) + token_sums(split(conv * hat_ref[...].reshape(PAIRS * ROWS, LANES)))
    ):
        sum_send[i : i + 1, :] = sums
    gate_g.step(4)
    sum_recv[chan] = sum_send[...]
    sums_back = exchange(6, lambda peer: sum_send, sum_recv)

    for r in range(1, 4):
        spec_copy(1, r).wait_recv()
    sgrad_ref[...] = sgrad_recv[0] + sgrad_recv[1] + sgrad_recv[2] + sgrad_recv[3]

    sigma_sum = point_grads(sigma, wave_ref, base, sums_ref, sgrad_ref, pgrad_ref)
    square_sum = mode_sums(0, jnp.zeros_like(sigma_sum), sigma, mcoef_ref, wave_ref, base, pgrad_ref, mback_ref)
    sums_back[0]()
    hidden_g.step(4)
    square_sum = mode_sums(1, square_sum, sigma, mcoef_ref, wave_ref, base, pgrad_ref, mback_ref)
    gate_last()
    square_sum = mode_sums(2, square_sum, sigma, mcoef_ref, wave_ref, base, pgrad_ref, mback_ref)
    square_sum = mode_sums(3, square_sum, sigma, mcoef_ref, wave_ref, base, pgrad_ref, mback_ref)
    mode_grads, dt_grad = mode_gradients(modes_ref, sigma, nyquist_grad, step_size, sigma_sum, square_sum, mback_ref)
    mask = low_lanes(32)
    for i in range(4):
        dp_send[i * 32 : (i + 1) * 32, :] = jnp.where(mask, mode_grads[i], mode_grads[i + 4])
    first = low_lanes(1)
    dp_send[128:129, :] = jnp.where(first, dt_grad, fold(skip_grad))
    dp_send[129:130, :] = jnp.where(first, fold(gain_grad), fold(bias_grad))
    dp_send[130:136, :] = jnp.zeros((6, LANES), F32)
    tail_sum = late_recv[0, ROWS:, :].astype(F32)
    for c in range(1, N_CHAN):
        tail_sum = tail_sum + late_recv[c, ROWS:, :].astype(F32)
    dp_send[136:144, :] = tail_sum[:8]
    dp_low[...] = dp_send[...].astype(BF16)

    def dp_copy(r):
        return remote(dp_low, dp_recv.at[r - 1], dp_ss.at[r - 1], dp_rs.at[r - 1], dp=dp_peers[r])

    for r in range(1, 4):
        dp_copy(r).start()
    gate_finish()

    sums_back[1]()
    sums = sum_recv[0]
    for c in range(1, N_CHAN):
        sums = sums + sum_recv[c]
    hidden_last()
    sums = sums * (1.0 / MODEL_WIDTH)
    rstd_cols, q_cols, qx_cols = columns(rstd), columns(sums[0:8]), columns(sums[8:16])
    for j in range(PAIRS):
        rows = slice(j * ROWS, (j + 1) * ROWS)
        out_ref[rows, :] = joined(late_recv, j, 0).astype(BF16)
        dtok_ref[rows, :] = joined(late_recv, j, HALF) + rstd_cols[j] * (
            conv_ref[j] * gain1 - q_cols[j] - hat_ref[j] * qx_cols[j]
        )
    for r in range(1, 4):
        dp_copy(r).wait_recv()
    total = dp_send[...] + (dp_recv[0].astype(F32) + dp_recv[1].astype(F32) + dp_recv[2].astype(F32))
    hidden_finish()
    gm_ref[...] = total[0:128]
    gv_ref[...] = total[128:144]
    for copy in pending:
        copy.wait_send()
    for group in (head, inputs, acts, back, late, sums_back):
        group[2]()
    for r in range(1, 4):
        dp_copy(r).wait_send()
        spec_copy(0, r).wait_send()
        spec_copy(1, r).wait_send()
def block_entry(bucket_ref, items_ref, *refs):
    n_in, n_out = 22, 5
    given, results = refs[:n_in], refs[n_in : n_in + n_out]
    held = refs[n_in + n_out : 2 * n_in + n_out]
    made = refs[2 * n_in + n_out : 2 * (n_in + n_out)]
    scratch, in_sem, out_sem = refs[2 * (n_in + n_out) : -2], refs[-2], refs[-1]

    def load(number):
        return pltpu.make_async_copy(given[number], held[number], in_sem.at[number])

    def loaded(*numbers):
        for number in numbers:
            load(number).wait()

    for number in (0, 7, 9, 13, 15, 1, 8, 10, 11, 12, 14, 16, 4, 5, 21, 17, 2, 3, 6, 18, 20, 19):
        load(number).start()
    block_kernel(loaded, bucket_ref, items_ref, *held, *made, *scratch)
    copies = [pltpu.make_async_copy(made[n], results[n], out_sem.at[n]) for n in range(n_out)]
    for copy in copies:
        copy.start()
    for copy in copies:
        copy.wait()


def unpack_entry(*refs):
    n_in, n_out = 6, 17
    given, results = refs[:n_in], refs[n_in : n_in + n_out]
    held = refs[n_in + n_out : 2 * n_in + n_out]
    made, in_sem, out_sem = refs[2 * n_in + n_out : -2], refs[-2], refs[-1]
    loads = [pltpu.make_async_copy(given[n], held[n], in_sem.at[n]) for n in range(n_in)]
    stores = [pltpu.make_async_copy(made[n], results[n], out_sem.at[n]) for n in range(n_out)]
    for copy in loads:
        copy.start()
    for copy in loads:
        copy.wait()
    unpack_kernel(*held, *made)
    for copy in stores:
        copy.start()
    for copy in stores:
        copy.wait()


def unpack_kernel(
    out_ref, dtok_ref, gw_ref, gm_ref, gv_ref, cotangent_ref,
    output_ref, tokens_ref, gain1_ref, bias1_ref, modes_ref, dt_ref, skip_ref, wa_ref, ba_ref, wb_ref, bb_ref,
    gain2_ref, bias2_ref, up_ref, bup_ref, down_ref, bdown_ref,
):
    for j in range(PAIRS):
        out = out_ref[j * ROWS : (j + 1) * ROWS, :].astype(F32).T.astype(BF16)
        grad = dtok_ref[j * ROWS : (j + 1) * ROWS, :].T
        for h in range(2):
            lanes, rows = slice((2 * j + h) * ROWS, (2 * j + h + 1) * ROWS), slice(h * HALF, (h + 1) * HALF)
            output_ref[:, lanes] = out[rows]
            tokens_ref[:, lanes] = cotangent_ref[:, lanes] + grad[rows]
    for i in range(8):
        modes_ref[i] = gm_ref[i % 4 * 32 : i % 4 * 32 + 32, i // 4 * HALF : (i // 4 + 1) * HALF]
    gates = gw_ref[:, :LANES].T
    wa_ref[...] = gates[:HALF]
    wb_ref[...] = gates[HALF:]
    up_ref[...] = gw_ref[:, 128:384]
    down_ref[...] = gw_ref[:, 384:640].T
    for at, low, high in (
        (0, dt_ref, skip_ref), (1, gain1_ref, bias1_ref), (8, ba_ref, bb_ref), (9, gain2_ref, bias2_ref),
    ):
        low[...] = gv_ref[at, :HALF]
        high[...] = gv_ref[at, HALF:]
    bdown_ref[...] = gv_ref[10, :HALF]
    bup_ref[:LANES] = gv_ref[11, :]
    bup_ref[LANES:] = gv_ref[12, :]


def block_program():
    mats, twiddle, levels, constant, wave = mixer_tables()

    def run(tokens, cotangent, bucket, items, gain1, bias1, modes, log_dt, skip, w_a, b_a, w_b, b_b, gain2, bias2, w_up, b_up, w_down, b_down):
        anywhere = pl.BlockSpec(memory_space=pl.ANY)
        smem = pl.BlockSpec(memory_space=pltpu.SMEM)
        dma = pltpu.SemaphoreType.DMA

        def buf(*shape):
            return pltpu.VMEM(shape, F32)

        def low(*shape):
            return pltpu.VMEM(shape, BF16)

        def full(*shape):
            return jax.ShapeDtypeStruct(shape, F32)

        big, wide = (PAIRS, ROWS, LANES), (256, WIDE)
        def like(arrays):
            return [pltpu.VMEM(tuple(a.shape), a.dtype) for a in arrays]

        arguments = (
            tokens.T, cotangent.T, gain1, bias1, jnp.swapaxes(modes, 1, 2), log_dt, skip, w_a.T, b_a, w_b.T, b_b, gain2,
            bias2, w_up, b_up, w_down, b_down, levels, constant, mats, twiddle, wave,
        )
        middle = (
            jax.ShapeDtypeStruct((512, LANES), BF16), full(512, LANES), full(ROWS, WIDE), full(ROWS, LANES),
            full(16, LANES),
        )
        packed = pl.pallas_call(
            block_entry,
            out_shape=middle,
            in_specs=[smem] * 2 + [anywhere] * 22,
            out_specs=(anywhere,) * 5,
            scratch_shapes=like(arguments) + like(middle) + [
                low(512, LANES), buf(8, LANES), buf(160, LANES), buf(8, 32, LANES),
                low(N_CHAN, 512, 128), low(2, 4, 512, 256), low(N_CHAN, 512, 128), low(2, 4, 512, 256),
                low(2, ROWS, LANES), low(N_CHAN, 256, LANES), low(8, 256, LANES), low(8, 2, 256, LANES), low(2, ROWS, LANES),
                low(4, 2, 256, 256), buf(2, 256, LANES), buf(2, ROWS, LANES), buf(256, LANES),
                low(N_CHAN, ROWS, LANES), low(N_CHAN, ROWS, LANES), buf(24, LANES), buf(N_CHAN, 24, LANES),
                low(N_CHAN, HALF, LANES), low(N_CHAN, HALF, LANES), low(N_CHAN, HALF, LANES), low(N_CHAN, HALF, LANES),
                low(N_CHAN, 144, LANES), low(N_CHAN, 144, LANES),
                buf(16, LANES), buf(N_CHAN, 16, LANES), buf(N_CHAN, 8, LANES),
                buf(144, LANES), low(144, LANES), low(3, 144, LANES), buf(64, 256), buf(4, 64, 256), buf(4, 64, 256), buf(4, 64, 256),
                buf(*big), buf(*big), buf(*big), buf(*big), low(2, *wide), buf(*wide), buf(*wide), buf(*wide), buf(*big),
                buf(10, 32, LANES), buf(2, 16, QUARTER, LANES), buf(2, 16, QUARTER, LANES), buf(10, 32, LANES),
                buf(64, 256), buf(256, 256),
                buf(*big), buf(*big), buf(*big), buf(*big), low(ROWS, 512), low(2, ROWS, 512), low(2, ROWS, 512),
                buf(2, ROWS, 512), buf(2, ROWS, 512), low(2, ROWS, 512), low(2, ROWS, 512),
                low(N_CHAN, ROWS, LANES), low(4, 256, 256), low(4, 256, 256), low(512, ROWS), low(512, 256), low(512, 256),
                dma((3, 8)), dma((3, 8)), dma, dma, dma, dma, dma((2, 9)), dma((2, 9)), dma, dma, dma((4,)), dma((4,)),
                dma((2, 8)), dma((2, 8)), dma, dma, dma, dma, dma((4,)), dma((4,)), dma, dma,
                dma((7, 7)), dma((7, 7)), dma((3,)), dma((3,)), dma((2, 3)), dma((2, 3)), dma((22,)), dma((5,)),
            ],
            compiler_params=pltpu.CompilerParams(
                collective_id=0, has_side_effects=True, vmem_limit_bytes=60 * 1024 * 1024
            ),
            name="block",
        )(bucket, items, *arguments)
        small = full(HALF)
        final = (
                jax.ShapeDtypeStruct((HALF, TOK_DEV), BF16), full(HALF, TOK_DEV), small, small, full(8, 32, HALF),
                small, small, full(HALF, ROWS), small, full(HALF, ROWS), small, small, small, full(ROWS, 256),
                full(256), full(256, ROWS), small,
            )
        sources = (*packed, cotangent.T)
        results = pl.pallas_call(
            unpack_entry,
            out_shape=final,
            in_specs=[anywhere] * 6,
            out_specs=(anywhere,) * 17,
            scratch_shapes=like(sources) + like(final) + [dma((6,)), dma((17,))],
            name="unpack",
        )(*sources)
        turned = {0, 1, 4, 7, 9}
        return tuple(jnp.swapaxes(r, -1, -2) if i in turned else r for i, r in enumerate(results))

    return run


def solution(mesh):
    small = mesh.shape["chan"] == N_CHAN and mesh.shape["dp"] == 4
    return jax.shard_map(
        block_program() if small else shards,
        mesh=mesh,
        in_specs=(
            P("dp", "chan"),
            P("dp", "chan"),
            P("dp"),
            P("dp"),
            P("chan"),
            P("chan"),
            P(None, "chan", None),
            P("chan"),
            P("chan"),
            P("dp", "chan"),
            P("chan"),
            P("dp", "chan"),
            P("chan"),
            P("chan"),
            P("chan"),
            P("dp", "chan"),
            P("chan"),
            P("chan", "dp"),
            P("chan"),
        ),
        out_specs=(
            P("dp", "chan"),
            P("dp", "chan"),
            P("chan"),
            P("chan"),
            P(None, "chan", None),
            P("chan"),
            P("chan"),
            P("dp", "chan"),
            P("chan"),
            P("dp", "chan"),
            P("chan"),
            P("chan"),
            P("chan"),
            P("dp", "chan"),
            P("chan"),
            P("chan", "dp"),
            P("chan"),
        ),
        check_vma=False,
    )
```

```python
import math

import jax
import jax.numpy as jnp
import ml_dtypes
import numpy as np
from jax import lax
from jax.experimental import pallas as pl
from jax.experimental.pallas import tpu as pltpu
from jax.sharding import PartitionSpec as P

MODEL_WIDTH = 512
TOK_DEV = 1024


HIGHEST = lax.Precision.HIGHEST
EPSILON = 1e-05


def product(left, right):
    return jnp.dot(left, right, preferred_element_type=jnp.float32)


def product_nt(left, right):
    return lax.dot_general(
        left, right, (((1,), (1,)), ((), ())), preferred_element_type=jnp.float32
    )


def product_tn(left, right):
    return lax.dot_general(
        left, right, (((0,), (0,)), ((), ())), preferred_element_type=jnp.float32
    )


def gelu_slope(values):
    return (
        0.5 * (1.0 + lax.erf(values * 0.7071067811865476))
        + values * jnp.exp(-0.5 * values * values) * 0.3989422804014327
    )


def half_angles(length):
    angle = np.arange(length // 2 + 1, dtype=np.float64) * (math.pi / length)
    cosine, sine = np.cos(angle), np.sin(angle)
    cosine[-1] = 0.0
    return cosine.astype(np.float32), sine.astype(np.float32)


def inverse_tables(length):
    freq = np.arange(length // 2 + 1)
    turn = (freq[:, None] * np.arange(length)[None, :]) % length * (2.0 * math.pi / length)
    weight = np.where((freq == 0) | (freq == length // 2), 1.0, 2.0)[:, None] / length
    return (weight * np.cos(turn)).astype(np.float32), (weight * np.sin(turn)).astype(np.float32)


def high_einsum(form, left, right):
    return jnp.einsum(form, left, right, precision=HIGHEST)


def ssm_kernel(modes, log_dt):
    cos_h, sin_h = half_angles(TOK_DEV)
    index = jnp.arange(modes.shape[2], dtype=jnp.int32).astype(jnp.float32)
    lam_re = -0.5 * jnp.exp(modes[0])
    lam_im = math.pi * (index + modes[1])
    rank_re, rank_im, in_re, in_im, out_re, out_im = (modes[i] for i in range(2, 8))
    sigma = (2.0 * jnp.exp(-log_dt))[:, None]

    def points(values):
        return values.T[:, None, :]

    den_re = points(lam_re * lam_re + lam_im * lam_im) * (cos_h * cos_h)[:, None] - (
        sigma * sigma
    ).T * (sin_h * sin_h)[:, None]
    den_im = points(-2.0 * sigma * lam_re) * (sin_h * cos_h)[:, None]
    den_sq = den_re * den_re + den_im * den_im
    inv_re = den_re / den_sq
    inv_im = -den_im / den_sq
    sums = []
    for real, imag in (
        (out_re * in_re + out_im * in_im, out_re * in_im - out_im * in_re),
        (out_re * rank_re + out_im * rank_im, out_re * rank_im - out_im * rank_re),
        (rank_re * in_re + rank_im * in_im, rank_re * in_im - rank_im * in_re),
        (rank_re * rank_re + rank_im * rank_im, jnp.zeros_like(rank_re)),
    ):
        turned = points(real * lam_re + imag * lam_im)
        real = points(real)
        p_re, p_im = jnp.sum(real * inv_re, axis=0), jnp.sum(real * inv_im, axis=0)
        q_re, q_im = jnp.sum(turned * inv_re, axis=0), jnp.sum(turned * inv_im, axis=0)
        sine = sin_h[:, None] * sigma.T
        sums.append((-sine * p_im - cos_h[:, None] * q_re, sine * p_re - cos_h[:, None] * q_im))
    (cross_re, cross_im), (left_re, left_im), (right_re, right_im), (self_re, self_im) = sums
    twice = 2.0 * cos_h[:, None]
    loop_re, loop_im = 1.0 + twice * self_re, twice * self_im
    back_re, back_im = twice * right_re, twice * right_im
    loop_sq = loop_re * loop_re + loop_im * loop_im
    ratio_re = (back_re * loop_re + back_im * loop_im) / loop_sq
    ratio_im = (back_im * loop_re - back_re * loop_im) / loop_sq
    part_re = cross_re - (left_re * ratio_re - left_im * ratio_im)
    part_im = cross_im - (left_re * ratio_im + left_im * ratio_re)
    spec_re = 2.0 * (cos_h[:, None] * part_re - sin_h[:, None] * part_im)
    spec_im = 2.0 * (cos_h[:, None] * part_im + sin_h[:, None] * part_re)
    cos_tab, sin_tab = inverse_tables(TOK_DEV)
    return high_einsum("kl,kc->lc", cos_tab, spec_re) - high_einsum("kl,kc->lc", sin_tab, spec_im)


BLOCK = 128
BLOCKS = TOK_DEV // BLOCK
FIRST = 2 * BLOCKS
KEPT = FIRST // 2 + 1


def transform_tables():
    length = 2 * TOK_DEV
    turn = np.arange(KEPT)[:, None] * np.arange(BLOCK)[None, :] * (2.0 * math.pi / length)
    small = np.arange(BLOCK)[:, None] * np.arange(BLOCK)[None, :] % BLOCK * (2.0 * math.pi / BLOCK)
    spots = np.stack([np.arange(BLOCKS) + np.arange(BLOCKS) // (2 << b) * (2 << b) for b in range(3)])
    angle = spots[:, None, :] * np.arange(KEPT)[None, :, None] % FIRST * (2.0 * math.pi / FIRST)
    parts = (np.cos(turn), np.sin(turn), np.cos(small), np.sin(small), np.cos(angle), np.sin(angle))
    return [part.astype(np.float32) for part in parts]


def forward_transform(blocks, cos_a, sin_a):
    cos_t, sin_t, cos_s, sin_s, _, _ = transform_tables()
    step_re = high_einsum("ka,abc->kbc", cos_a, blocks)
    step_im = -high_einsum("ka,abc->kbc", sin_a, blocks)
    turned_re = step_re * cos_t[..., None] + step_im * sin_t[..., None]
    turned_im = step_im * cos_t[..., None] - step_re * sin_t[..., None]
    both = jnp.concatenate([turned_re, turned_im], axis=1)
    matrix = np.block([[cos_s, sin_s], [-sin_s, cos_s]])
    return high_einsum("pb,kbc->kpc", matrix, both)


def inverse_transform(spectrum, cos_a, sin_a):
    cos_t, sin_t, cos_s, sin_s, _, _ = transform_tables()
    matrix = np.block([[cos_s, -sin_s], [sin_s, cos_s]])
    both = high_einsum("bp,kpc->kbc", matrix, spectrum)
    step_re, step_im = both[:, :BLOCK], both[:, BLOCK:]
    turned_re = step_re * cos_t[..., None] - step_im * sin_t[..., None]
    turned_im = step_im * cos_t[..., None] + step_re * sin_t[..., None]
    weight = np.where(np.arange(KEPT) % (KEPT - 1) == 0, 1.0, 2.0).astype(np.float32) / (2 * TOK_DEV)
    return high_einsum("ka,kbc->abc", cos_a * weight[:, None], turned_re) - high_einsum(
        "ka,kbc->abc", sin_a * weight[:, None], turned_im
    )


def multiply(left, right):
    left_re, left_im = left[:, :BLOCK], left[:, BLOCK:]
    right_re, right_im = right[:, :BLOCK], right[:, BLOCK:]
    return jnp.concatenate(
        [left_re * right_re - left_im * right_im, left_re * right_im + left_im * right_re], axis=1
    )


def mixer(normed, kernel_taps, skip_gain, bucket, filled):
    _, _, _, _, cos_a, sin_a = transform_tables()
    cos_x, sin_x = jnp.asarray(cos_a)[bucket], jnp.asarray(sin_a)[bucket]
    item_blocks = 2 << bucket
    block_id = jnp.arange(BLOCKS, dtype=jnp.int32)[:, None, None]
    taps = jnp.where(block_id < item_blocks, kernel_taps.reshape(BLOCKS, BLOCK, -1), 0.0)
    signal = forward_transform(normed.reshape(BLOCKS, BLOCK, -1), cos_x, sin_x)
    answer = forward_transform(taps, cos_a[2], sin_a[2])
    result = inverse_transform(multiply(signal, answer), cos_x, sin_x)
    result = jnp.where(block_id < filled * item_blocks, result, 0.0)
    return result.reshape(normed.shape) + skip_gain * normed


def shards(
    tokens,
    cotangent,
    group_bucket,
    group_items,
    first_norm_gain,
    first_norm_bias,
    modes,
    log_dt,
    d_skip,
    w_a,
    b_a,
    w_b,
    b_b,
    second_norm_gain,
    second_norm_bias,
    w_up,
    b_up,
    w_down,
    b_down,
):
    input_tokens = tokens.astype(jnp.float32)
    sums_in = lax.psum(
        (jnp.sum(input_tokens, axis=1), jnp.sum(input_tokens * input_tokens, axis=1)), "chan"
    )
    input_average = sums_in[0][:, None] / MODEL_WIDTH
    input_inverse_deviation = lax.rsqrt(
        sums_in[1][:, None] / MODEL_WIDTH - input_average * input_average + EPSILON
    )
    input_standardized = (input_tokens - input_average) * input_inverse_deviation
    input_normalized = input_standardized * first_norm_gain + first_norm_bias
    level = group_bucket[0]
    filled = group_items[0]
    kernel_taps, kernel_back = jax.vjp(ssm_kernel, modes, log_dt)

    def local_mix(values, taps_now, skip_gain):
        return mixer(values, taps_now, skip_gain, level, filled)

    mixed, mix_back = jax.vjp(local_mix, input_normalized, kernel_taps, d_skip)
    acts_low = jax.nn.gelu(mixed, approximate=False).astype(jnp.bfloat16)
    wa_full, wb_full, up_full, down_full = (
        lax.all_gather(w_a.astype(jnp.bfloat16), "dp", axis=0, tiled=True),
        lax.all_gather(w_b.astype(jnp.bfloat16), "dp", axis=0, tiled=True),
        lax.all_gather(w_up.astype(jnp.bfloat16), "dp", axis=0, tiled=True),
        lax.all_gather(w_down.astype(jnp.bfloat16), "dp", axis=1, tiled=True),
    )
    acts_full = lax.all_gather(acts_low, "chan", axis=1, tiled=True)
    gate_a = product(acts_full, wa_full) + b_a
    gate_b = product(acts_full, wb_full) + b_b
    gate_sig = jax.nn.sigmoid(gate_b)
    residual_stream = input_tokens + gate_a * gate_sig
    sums_mid = lax.psum(
        (jnp.sum(residual_stream, axis=1), jnp.sum(residual_stream * residual_stream, axis=1)),
        "chan",
    )
    middle_average = sums_mid[0][:, None] / MODEL_WIDTH
    middle_inverse_deviation = lax.rsqrt(
        sums_mid[1][:, None] / MODEL_WIDTH - middle_average * middle_average + EPSILON
    )
    middle_standardized = (residual_stream - middle_average) * middle_inverse_deviation
    middle_reduced = (middle_standardized * second_norm_gain + second_norm_bias).astype(
        jnp.bfloat16
    )
    mid_full = lax.all_gather(middle_reduced, "chan", axis=1, tiled=True)
    pre_act = product(mid_full, up_full) + b_up
    hidden_low = jax.nn.gelu(pre_act, approximate=False).astype(jnp.bfloat16)
    branch = (
        lax.psum_scatter(product(hidden_low, down_full), "chan", scatter_dimension=1, tiled=True)
        + b_down
    )
    output = (residual_stream + branch).astype(jnp.bfloat16)
    grad_f = cotangent.astype(jnp.bfloat16)
    grad_b_down = jnp.sum(grad_f.astype(jnp.float32), axis=0)
    grad_f_full = lax.all_gather(grad_f, "chan", axis=1, tiled=True)
    grad_w_down = product_tn(hidden_low, grad_f_full)
    grad_pre = (product_nt(grad_f_full, down_full) * gelu_slope(pre_act)).astype(jnp.bfloat16)
    grad_b_up = jnp.sum(grad_pre.astype(jnp.float32), axis=0)
    grad_w_up = product_tn(mid_full, grad_pre)
    middle_gradient = lax.psum_scatter(
        product_nt(grad_pre, up_full), "chan", scatter_dimension=1, tiled=True
    )
    second_norm_gain_gradient = jnp.sum(middle_gradient * middle_standardized, axis=0)
    grad_ln2_bias = jnp.sum(middle_gradient, axis=0)
    middle_rescaled = middle_gradient * second_norm_gain
    middle_backward = lax.psum(
        (jnp.sum(middle_rescaled, axis=1), jnp.sum(middle_rescaled * middle_standardized, axis=1)),
        "chan",
    )
    grad_resid = cotangent + middle_inverse_deviation * (
        middle_rescaled
        - middle_backward[0][:, None] / MODEL_WIDTH
        - middle_standardized * middle_backward[1][:, None] / MODEL_WIDTH
    )
    grad_a = (grad_resid * gate_sig).astype(jnp.bfloat16)
    grad_b = (grad_resid * gate_a * gate_sig * (1.0 - gate_sig)).astype(jnp.bfloat16)
    grad_b_a = jnp.sum(grad_a.astype(jnp.float32), axis=0)
    grad_b_b = jnp.sum(grad_b.astype(jnp.float32), axis=0)
    grad_w_a = product_tn(acts_full, grad_a)
    grad_w_b = product_tn(acts_full, grad_b)
    grad_acts = lax.psum_scatter(
        product_nt(grad_a, wa_full) + product_nt(grad_b, wb_full),
        "chan",
        scatter_dimension=1,
        tiled=True,
    )
    grad_mixed = grad_acts * gelu_slope(mixed)
    normalized_gradient, grad_kernel, grad_skip = mix_back(grad_mixed)
    grad_modes, grad_log_dt = kernel_back(grad_kernel)
    first_norm_gain_gradient = jnp.sum(normalized_gradient * input_standardized, axis=0)
    grad_ln1_bias = jnp.sum(normalized_gradient, axis=0)
    input_rescaled = normalized_gradient * first_norm_gain
    input_backward = lax.psum(
        (jnp.sum(input_rescaled, axis=1), jnp.sum(input_rescaled * input_standardized, axis=1)),
        "chan",
    )
    grad_tokens = grad_resid + input_inverse_deviation * (
        input_rescaled
        - input_backward[0][:, None] / MODEL_WIDTH
        - input_standardized * input_backward[1][:, None] / MODEL_WIDTH
    )
    grad_w_a, grad_w_b, grad_w_up, grad_w_down = (
        lax.psum_scatter(grad_w_a, "dp", scatter_dimension=0, tiled=True),
        lax.psum_scatter(grad_w_b, "dp", scatter_dimension=0, tiled=True),
        lax.psum_scatter(grad_w_up, "dp", scatter_dimension=0, tiled=True),
        lax.psum_scatter(grad_w_down, "dp", scatter_dimension=1, tiled=True),
    )
    (
        first_norm_gain_gradient,
        grad_ln1_bias,
        grad_modes,
        grad_log_dt,
        grad_skip,
        grad_b_a,
        grad_b_b,
        second_norm_gain_gradient,
        grad_ln2_bias,
        grad_b_up,
        grad_b_down,
    ) = lax.psum(
        (
            first_norm_gain_gradient,
            grad_ln1_bias,
            grad_modes,
            grad_log_dt,
            grad_skip,
            grad_b_a,
            grad_b_b,
            second_norm_gain_gradient,
            grad_ln2_bias,
            grad_b_up,
            grad_b_down,
        ),
        "dp",
    )
    return (
        output,
        grad_tokens,
        first_norm_gain_gradient,
        grad_ln1_bias,
        grad_modes,
        grad_log_dt,
        grad_skip,
        grad_w_a,
        grad_b_a,
        grad_w_b,
        grad_b_b,
        second_norm_gain_gradient,
        grad_ln2_bias,
        grad_w_up,
        grad_b_up,
        grad_w_down,
        grad_b_down,
    )


LANES = 128
HALF = 64
PAIRS = 4
ROWS = 128
N_CHAN = 8
WIDE = 640
MESH = pl.DeviceIdType.MESH
F32 = jnp.float32
BF16 = jnp.bfloat16


def split_two(matrix):
    high = matrix.astype(ml_dtypes.bfloat16)
    low = (matrix - high.astype(np.float64)).astype(ml_dtypes.bfloat16)
    return np.concatenate([high, low], axis=1)


def lane_rows(values_low, values_high):
    return np.repeat(np.stack([values_low, values_high], -1), HALF, axis=-1)


def mixer_tables():
    line = np.arange(ROWS)
    small = np.outer(line, line) % ROWS * (2.0 * math.pi / ROWS)
    cos_s, sin_s = np.cos(small), np.sin(small)
    forward = np.block([[cos_s, sin_s], [-sin_s, cos_s]])
    real = np.zeros((2 * ROWS, 2 * ROWS))
    for row in range(HALF):
        weight = 1.0 if row == 0 else 2.0
        turn = 2.0 * math.pi / ROWS * row * line
        real[:ROWS, row] = weight * np.cos(turn)
        real[:ROWS, ROWS + row] = -weight * np.sin(turn)
        turn = 2.0 * math.pi / TOK_DEV * (4 + 8 * row) * line
        real[ROWS:, HALF + row] = 2.0 * np.cos(turn)
        real[ROWS:, ROWS + HALF + row] = -2.0 * np.sin(turn)
    mats = np.stack([split_two(m) for m in (forward, forward.T, real, real.T)])

    twiddle = []
    for pair in range(5):
        turn = np.stack([line * k * (math.pi / TOK_DEV) for k in (2 * pair, 2 * pair + 1)])
        twiddle += [lane_rows(np.cos(turn[0]), np.cos(turn[1])), lane_rows(np.sin(turn[0]), np.sin(turn[1]))]
    for first, second in ((1, 2), (3, 0)):
        turn = np.stack([line * k * (2.0 * math.pi / TOK_DEV) for k in (first, second)])
        twiddle += [lane_rows(np.cos(turn[0]), np.cos(turn[1])), lane_rows(np.sin(turn[0]), np.sin(turn[1]))]

    def forward_rows(coef, pairs):
        out = []
        for low, high in pairs:
            for part in range(2):
                for j in range(PAIRS):
                    out.append(lane_rows(coef(2 * j, low, part), coef(2 * j + 1, high, part)))
                for j in range(PAIRS):
                    out.append(lane_rows(coef(2 * j, high, part), coef(2 * j + 1, low, part)))
        return np.stack(out)

    def inverse_rows(coef, pairs):
        out = []
        for low, high in pairs:
            for part in range(2):
                for j in range(PAIRS):
                    out.append(lane_rows(coef(2 * j, low, part), coef(2 * j + 1, high, part)))
                for j in range(PAIRS):
                    out.append(lane_rows(coef(2 * j + 1, low, part), coef(2 * j, high, part)))
        return np.stack(out)

    levels = []
    pairs = [(2 * p, 2 * p + 1) for p in range(5)]
    for level in range(3):
        item = 2 << level

        def angle(block, k):
            return 2.0 * math.pi / 16 * ((block + block // item * item) * k % 16)

        def fwd(block, k, part):
            if k > 8:
                return np.zeros(())
            return np.cos(angle(block, k)) if part == 0 else -np.sin(angle(block, k))

        def inv(block, k, part):
            weight = (1.0 if k in (0, 8) else 2.0) / (2 * TOK_DEV)
            return weight * fwd(block, k, part)

        levels.append(np.concatenate([forward_rows(fwd, pairs), inverse_rows(inv, pairs)]))

    def taps(block, k, part):
        if k == 0:
            return np.asarray((1.0 if part == 0 else (-1.0) ** block) / TOK_DEV)
        turn = 2.0 * math.pi / 8 * (block * k % 8)
        return np.asarray((np.cos(turn) if part == 0 else -np.sin(turn)) * 2.0 / TOK_DEV)

    tap_pairs = [(1, 2), (3, 0)]
    taps_back = forward_rows(taps, tap_pairs)
    taps_rows = inverse_rows(taps, tap_pairs)
    freq_even = np.where(line < HALF, 8 * line, 4 + 8 * (line - HALF))
    half_angle = np.stack(
        [lane_rows(1 + 8 * line, 2 + 8 * line), lane_rows(3 + 8 * line, freq_even)]
    ) * (math.pi / TOK_DEV)
    wave = np.stack([np.cos(half_angle), np.sin(half_angle)])
    return (
        mats,
        np.stack(twiddle).astype(np.float32),
        np.stack(levels).astype(np.float32),
        np.concatenate([levels[2], taps_rows, taps_back]).astype(np.float32),
        wave.astype(np.float32),
    )


def low_lanes(rows):
    return lax.broadcasted_iota(jnp.int32, (rows, LANES), 1) < HALF


def turn_half(values):
    return pltpu.roll(values, HALF, 1)


def split_pair(values):
    upper, lower = values[:HALF], values[HALF:]
    mask = low_lanes(HALF)
    return jnp.where(mask, upper, turn_half(lower)), jnp.where(mask, turn_half(upper), lower)


def join_pair(first, second):
    mask = low_lanes(HALF)
    return jnp.concatenate(
        [jnp.where(mask, first, turn_half(second)), jnp.where(mask, turn_half(first), second)], axis=0
    )


def interleave(first, second):
    mask = low_lanes(first.shape[0])
    return jnp.where(mask, first, turn_half(second)), jnp.where(mask, turn_half(first), second)


def fold(values):
    return values + turn_half(values)


def reciprocal(values):
    guess = pl.reciprocal(values, approx=True)
    return guess * (2.0 - values * guess)


ERF_TERMS = (1.061405429, -1.453152027, 1.421413741, -0.284496736, 0.254829592)


def normal_parts(values):
    bell = jnp.exp(-0.5 * values * values)
    t = reciprocal(1.0 + (0.3275911 * 0.7071067811865476) * jnp.abs(values))
    tail = ERF_TERMS[0]
    for term in ERF_TERMS[1:]:
        tail = tail * t + term
    tail = 0.5 * (tail * t) * bell
    return jnp.where(values < 0.0, tail, 1.0 - tail), bell * 0.3989422804014327


def column_sum(values):
    return jnp.sum(values, axis=0, keepdims=True)


def dot_nt(left, right):
    return lax.dot_general(left, right, (((1,), (1,)), ((), ())), preferred_element_type=F32)


def dot_nn(left, right):
    return jnp.dot(left, right, preferred_element_type=F32)


def store_split(ref, row, lane, values, exact=True):
    high = values.astype(BF16)
    place = (pl.ds(row, values.shape[0]), pl.ds(lane, values.shape[1]))
    ref[(0,) + place] = high
    if exact:
        ref[(1,) + place] = (values - high.astype(F32)).astype(BF16)


def split_product(mat_ref, which, rhs_ref, lane, width, exact=True):
    high = mat_ref[which, :, 0:256]
    low = mat_ref[which, :, 256:512]
    rhs_high = rhs_ref[0, :, lane : lane + width]
    product = dot_nn(high, rhs_high) + dot_nn(low, rhs_high)
    if exact:
        product = product + dot_nn(high, rhs_ref[1, :, lane : lane + width])
    return product


CHUNK = 32


def over_chunks(body, size=CHUNK, first=0, rows=ROWS):
    def step(index, carry):
        body(pl.multiple_of(first + index * size, size))
        return carry

    lax.fori_loop(0, rows // size, step, 0)


def spread_pairs(src, coef_ref, base, twiddle_ref, twiddle_base, pairs, rhs_ref, exact=True):
    def body(row):
        rows = pl.ds(row, CHUNK)
        blocks = [src(j, rows) for j in range(PAIRS)]
        for pair in range(pairs):
            parts = []
            for part in range(2):
                at = base + (pair * 2 + part) * 8
                straight = sum(blocks[j] * coef_ref[at + j : at + j + 1, :] for j in range(PAIRS))
                crossed = sum(blocks[j] * coef_ref[at + 4 + j : at + 5 + j, :] for j in range(PAIRS))
                parts.append(straight + turn_half(crossed))
            cosine = twiddle_ref[twiddle_base + 2 * pair, rows, :]
            sine = twiddle_ref[twiddle_base + 2 * pair + 1, rows, :]
            store_split(rhs_ref, row, pair * LANES, parts[0] * cosine + parts[1] * sine, exact)
            store_split(rhs_ref, row + ROWS, pair * LANES, parts[1] * cosine - parts[0] * sine, exact)

    over_chunks(body)


def gather_pairs(values_ref, coef_ref, base, twiddle_ref, twiddle_base, pairs, store):
    def body(row):
        rows = pl.ds(row, CHUNK)
        straight, crossed = [0.0] * PAIRS, [0.0] * PAIRS
        for pair in range(pairs):
            lanes = slice(pair * LANES, (pair + 1) * LANES)
            real, imag = values_ref[rows, lanes], values_ref[pl.ds(row + ROWS, CHUNK), lanes]
            cosine = twiddle_ref[twiddle_base + 2 * pair, rows, :]
            sine = twiddle_ref[twiddle_base + 2 * pair + 1, rows, :]
            for part, value in enumerate((real * cosine - imag * sine, imag * cosine + real * sine)):
                at = base + (pair * 2 + part) * 8
                for j in range(PAIRS):
                    straight[j] = straight[j] + value * coef_ref[at + j : at + j + 1, :]
                    crossed[j] = crossed[j] + value * coef_ref[at + 4 + j : at + 5 + j, :]
        for j in range(PAIRS):
            store(j, rows, straight[j] + turn_half(crossed[j]))

    over_chunks(body)


GROUPS = ((0, 256), (256, 256), (512, 128))


def transform_into(dst_ref, mat_ref, which, rhs_ref, exact=True):
    for lane, width in GROUPS:
        dst_ref[:, lane : lane + width] = split_product(mat_ref, which, rhs_ref, lane, width, exact)


def multiply_spectra(left_ref, right_ref, rhs_ref, conjugate, exact=True):
    def body(row):
        top, bottom = pl.ds(row, CHUNK), pl.ds(row + ROWS, CHUNK)
        for pair in range(5):
            lanes = slice(pair * LANES, (pair + 1) * LANES)
            a_re, a_im = left_ref[top, lanes], left_ref[bottom, lanes]
            b_re, b_im = right_ref[top, lanes], right_ref[bottom, lanes]
            if conjugate:
                out_re, out_im = a_re * b_re + a_im * b_im, a_re * b_im - a_im * b_re
            else:
                out_re, out_im = a_re * b_re - a_im * b_im, a_re * b_im + a_im * b_re
            store_split(rhs_ref, row, pair * LANES, out_re, exact)
            store_split(rhs_ref, row + ROWS, pair * LANES, out_im, exact)

    over_chunks(body)


def pair_terms(modes_ref):
    rank_re, rank_im, in_re, in_im, out_re, out_im = (modes_ref[i] for i in range(2, 8))
    return (
        (out_re * in_re + out_im * in_im, out_re * in_im - out_im * in_re),
        (out_re * rank_re + out_im * rank_im, out_re * rank_im - out_im * rank_re),
        (rank_re * in_re + rank_im * in_im, rank_re * in_im - rank_im * in_re),
        (rank_re * rank_re + rank_im * rank_im, None),
    )


def mode_values(modes_ref):
    index = lax.broadcasted_iota(jnp.int32, modes_ref.shape[1:], 0).astype(F32)
    return -0.5 * jnp.exp(modes_ref[0]), math.pi * (index + modes_ref[1])


POINT_ROWS = 16


def resolvent(coef_ref, n, square_cos, cos_sin, scaled):
    den_re = coef_ref[8, pl.ds(n, 1), :] * square_cos - scaled
    den_im = coef_ref[9, pl.ds(n, 1), :] * cos_sin
    inverse = reciprocal(den_re * den_re + den_im * den_im)
    return den_re * inverse, -(den_im * inverse)


def complex_multiply(a_re, a_im, b_re, b_im):
    return a_re * b_re - a_im * b_im, a_re * b_im + a_im * b_re


def conj_multiply(a_re, a_im, b_re, b_im):
    return a_re * b_re + a_im * b_im, a_re * b_im - a_im * b_re


def combine(sums, sigma, cosine, sine):
    terms = []
    for p_re, p_im, q_re, q_im in (sums[4 * q : 4 * q + 4] for q in range(4)):
        swing = sigma * sine
        terms.append((-swing * p_im - cosine * q_re, swing * p_re - cosine * q_im))
    twice = 2.0 * cosine
    loop_re, loop_im = 1.0 + twice * terms[3][0], twice * terms[3][1]
    scale = reciprocal(loop_re * loop_re + loop_im * loop_im)
    inv = (loop_re * scale, -(loop_im * scale))
    ratio = complex_multiply(twice * terms[2][0], twice * terms[2][1], *inv)
    return terms, inv, ratio


QUARTER = 32


def cauchy_coefficients(modes_ref, sigma, coef_ref):
    lam_re, lam_im = mode_values(modes_ref)
    for q, (real, imag) in enumerate(pair_terms(modes_ref)):
        coef_ref[q] = real
        coef_ref[4 + q] = real * lam_re if imag is None else real * lam_re + imag * lam_im
    coef_ref[8] = lam_re * lam_re + lam_im * lam_im
    coef_ref[9] = -2.0 * sigma * lam_re


def wave_rows(wave_ref, pair, base, row):
    rows = pl.ds(pl.multiple_of(base + row, POINT_ROWS), POINT_ROWS)
    return wave_ref[0, pair, rows, :], wave_ref[1, pair, rows, :]


def cauchy_forward(index, sigma, coef_ref, wave_ref, base, sums_ref, spec_ref):
    sigma_sq = sigma * sigma
    pair, row = index // 2, index % 2 * POINT_ROWS
    rows = slice(row, row + POINT_ROWS)
    lanes = slice(pair * LANES, (pair + 1) * LANES)
    cosine, sine = wave_rows(wave_ref, pair, base, row)
    square_cos, cos_sin, scaled = cosine * cosine, cosine * sine, sigma_sq * (sine * sine)

    def add_mode(n, sums):
        sums = list(sums)
        for k in range(4):
            at = n * 4 + k
            inv_re, inv_im = resolvent(coef_ref, at, square_cos, cos_sin, scaled)
            for q in range(4):
                plain = coef_ref[q, pl.ds(at, 1), :]
                turned = coef_ref[4 + q, pl.ds(at, 1), :]
                sums[4 * q] = sums[4 * q] + plain * inv_re
                sums[4 * q + 1] = sums[4 * q + 1] + plain * inv_im
                sums[4 * q + 2] = sums[4 * q + 2] + turned * inv_re
                sums[4 * q + 3] = sums[4 * q + 3] + turned * inv_im
        return tuple(sums)

    zero = jnp.zeros((POINT_ROWS, LANES), F32)
    sums = lax.fori_loop(0, 8, add_mode, (zero,) * 16)
    for i in range(16):
        sums_ref[pair, i, rows, :] = sums[i]
    terms, _, ratio = combine(sums, sigma, cosine, sine)
    cut_re, cut_im = complex_multiply(*terms[1], *ratio)
    part_re, part_im = terms[0][0] - cut_re, terms[0][1] - cut_im
    spec_re, spec_im = complex_multiply(2.0 * cosine, 2.0 * sine, part_re, part_im)
    spec_ref[rows, lanes] = spec_re
    spec_ref[row + QUARTER : row + QUARTER + POINT_ROWS, lanes] = spec_im


PLACES = [(pair, row) for pair in range(2) for row in range(0, QUARTER, POINT_ROWS)]


def point_grads(sigma, wave_ref, base, sums_ref, spec_ref, grad_ref):
    zero = jnp.zeros((POINT_ROWS, LANES), F32)
    sigma_sum = zero
    for pair, row in PLACES:
        rows = slice(row, row + POINT_ROWS)
        lanes = slice(pair * LANES, (pair + 1) * LANES)
        cosine, sine = wave_rows(wave_ref, pair, base, row)
        sums = [sums_ref[pair, i, rows, :] for i in range(16)]
        terms, inv, ratio = combine(sums, sigma, cosine, sine)
        spec_re, spec_im = spec_ref[rows, lanes], spec_ref[row + QUARTER : row + QUARTER + POINT_ROWS, lanes]
        part = conj_multiply(2.0 * cosine, 2.0 * sine, spec_re, spec_im)
        left = conj_multiply(*ratio, *part)
        ratio_grad = conj_multiply(*terms[1], *part)
        back = conj_multiply(*inv, -ratio_grad[0], -ratio_grad[1])
        twice = 2.0 * cosine
        loop = conj_multiply(*ratio, *back)
        grads = (
            part,
            (-left[0], -left[1]),
            (twice * back[0], twice * back[1]),
            (-twice * loop[0], -twice * loop[1]),
        )
        swing = sigma * sine
        for q, (g_re, g_im) in enumerate(grads):
            grad_ref[pair, 4 * q, rows, :] = swing * g_im
            grad_ref[pair, 4 * q + 1, rows, :] = -swing * g_re
            grad_ref[pair, 4 * q + 2, rows, :] = -cosine * g_re
            grad_ref[pair, 4 * q + 3, rows, :] = -cosine * g_im
            sigma_sum = sigma_sum + sine * (g_im * sums[4 * q] - g_re * sums[4 * q + 1])
    return sigma_sum


def mode_sums(part, square_sum, sigma, coef_ref, wave_ref, base, grad_ref, back_ref):
    sigma_sq = sigma * sigma

    def mode(n, square_sum):
        plain = [coef_ref[q, pl.ds(n, 1), :] for q in range(4)]
        turned = [coef_ref[4 + q, pl.ds(n, 1), :] for q in range(4)]
        sums = [0.0] * 10
        for pair, row in PLACES:
            rows = slice(row, row + POINT_ROWS)
            cosine, sine = wave_rows(wave_ref, pair, base, row)
            square_cos, cos_sin, square_sin = cosine * cosine, cosine * sine, sine * sine
            inv_re, inv_im = resolvent(coef_ref, n, square_cos, cos_sin, sigma_sq * square_sin)
            grad_re, grad_im = 0.0, 0.0
            for q in range(4):
                p_re, p_im = grad_ref[pair, 4 * q, rows, :], grad_ref[pair, 4 * q + 1, rows, :]
                q_re, q_im = grad_ref[pair, 4 * q + 2, rows, :], grad_ref[pair, 4 * q + 3, rows, :]
                grad_re = grad_re + (plain[q] * p_re + turned[q] * q_re)
                grad_im = grad_im + (plain[q] * p_im + turned[q] * q_im)
                sums[q] = sums[q] + (p_re * inv_re + p_im * inv_im)
                sums[4 + q] = sums[4 + q] + (q_re * inv_re + q_im * inv_im)
            square_re = inv_re * inv_re - inv_im * inv_im
            square_im = 2.0 * inv_re * inv_im
            den_re, den_im = conj_multiply(square_re, square_im, grad_re, grad_im)
            sums[8] = sums[8] - den_re * square_cos
            sums[9] = sums[9] - den_im * cos_sin
            square_sum = square_sum + den_re * square_sin
        for i in range(10):
            back_ref[i, pl.ds(n, 1), :] = column_sum(sums[i])
        return square_sum

    return lax.fori_loop(part * 8, part * 8 + 8, mode, square_sum)


def mode_gradients(modes_ref, sigma, nyquist_grad, step, sigma_sum, square_sum, back_ref):
    plain_grad = [fold(back_ref[q]) for q in range(4)]
    turned_grad = [fold(back_ref[4 + q]) for q in range(4)]
    abs_grad, skew_grad = fold(back_ref[8]), fold(back_ref[9])
    lam_re, lam_im = mode_values(modes_ref)
    plain_grad[0] = plain_grad[0] + step * nyquist_grad
    rank_re, rank_im, in_re, in_im, out_re, out_im = (modes_ref[i] for i in range(2, 8))
    lam_re_grad = 2.0 * lam_re * abs_grad - 2.0 * sigma * skew_grad
    lam_im_grad = 2.0 * lam_im * abs_grad
    real_grad, imag_grad = [], []
    terms = pair_terms(modes_ref)
    for q, (real, imag) in enumerate(terms):
        lam_re_grad = lam_re_grad + turned_grad[q] * real
        if imag is not None:
            lam_im_grad = lam_im_grad + turned_grad[q] * imag
        real_grad.append(plain_grad[q] + turned_grad[q] * lam_re)
        imag_grad.append(turned_grad[q] * lam_im)
    r0, r1, r2, r3 = real_grad
    i0, i1, i2, _ = imag_grad
    grads = (
        lam_re_grad * lam_re,
        math.pi * lam_im_grad,
        r1 * out_re - i1 * out_im + r2 * in_re + i2 * in_im + 2.0 * r3 * rank_re,
        r1 * out_im + i1 * out_re + r2 * in_im - i2 * in_re + 2.0 * r3 * rank_im,
        r0 * out_re - i0 * out_im + r2 * rank_re - i2 * rank_im,
        r0 * out_im + i0 * out_re + r2 * rank_im + i2 * rank_re,
        r0 * in_re + i0 * in_im + r1 * rank_re + i1 * rank_im,
        r0 * in_im - i0 * in_re + r1 * rank_im - i1 * rank_re,
    )
    sigma_grad = (
        fold(column_sum(sigma_sum) + 2.0 * sigma * column_sum(square_sum))
        - 2.0 * column_sum(skew_grad * lam_re)
    )
    nyquist = step * column_sum(terms[0][0])
    return grads, nyquist * nyquist_grad - sigma * sigma_grad


def ring_place(chan):
    z, y = lax.div(chan, 2), lax.rem(chan, 2)
    return z + y * (7 - 2 * z)


def ring_chan(place):
    back = lax.div(place, 4)
    z = place * (1 - back) + (7 - place) * back
    return 2 * z + back


TURNS = (1, -1)


def block_kernel(
    bring_in, loaded, bucket_ref, items_ref, tokens_ref, cotangent_ref, gain1_ref, bias1_ref, raw_modes_ref, log_dt_ref, skip_ref,
    wa_ref, ba_ref, wb_ref, bb_ref, gain2_ref, bias2_ref, up_ref, bup_ref, down_ref, bdown_ref,
    levels_ref, coefc_ref, mat_ref, tw_ref, wave_ref,
    out_ref, dtok_ref, gw_ref, gm_ref, gv_ref,
    tok_ref, aux_ref, coefl_ref, modes_ref,
    wab_ref, wh_ref, gab_w_ref, gh_ref,
    stage_ref, sib_ab_ref, ring_ab_ref, ring_h_ref, part_ab_ref, cross_ref, keep_ref, swap_ref, gate_total_ref,
    in_send, in_recv, head_send, head_recv, acts_send, acts_recv, back_send, back_recv, late_send, late_recv,
    sum_send, sum_recv, tail_send, dp_send, dp_low, dp_recv, spec_send, spec_recv, sgrad_send, sgrad_recv,
    hat_ref, norm_ref, slope_ref, conv_ref, rhs_ref, freq_ref, sig_ref, ans_ref, taps_ref,
    mcoef_ref, sums_ref, pgrad_ref, mback_ref, sgrad_ref, taps_freq_ref,
    gate_ref, swish_ref, res_ref, hat2_ref, acts_ref, norm2_ref, gradf_ref, branch_ref, back2_ref, half_send, half_recv,
    gab_ref, hid_ref, gpre_ref, acts_t_ref, norm2_t_ref, gradf_t_ref,
    gring_ss, gring_rs, gsib_ss, gsib_rs, gx_ss, gx_rs, gdx_ss, gdx_rs, gswap_ss, gswap_rs, core_ss, core_rs,
    rring_ss, rring_rs, rsib_ss, rsib_rs, rx_ss, rx_rs, rdx_ss, rdx_rs, rswap_ss, rswap_rs,
    a2a_ss, a2a_rs, dp_ss, dp_rs, spec_ss, spec_rs,
):
    dp, chan = lax.axis_index("dp"), lax.axis_index("chan")
    core = lax.rem(dp, 2)
    sibling = dp + 1 - 2 * core
    place = ring_place(chan)
    spots = [lax.rem(place + offset, 8) if offset else place for offset in range(8)]
    around = [ring_chan(spot) if offset else chan for offset, spot in enumerate(spots)]
    groups = [lax.rem(spot, 4) for spot in spots]
    group_lanes = [pl.multiple_of(lax.div(spot, 4) * LANES, LANES) for spot in spots]
    nexts = [around[1], around[7]]
    chan_peers = [chan] + [lax.rem(chan + r, N_CHAN) for r in range(1, N_CHAN)]
    dp_peers = [dp] + [lax.rem(dp + r, 4) for r in range(1, 4)]
    across = dp_peers[2]

    def chan_at(offset):
        return around[offset % 8]

    barrier = pltpu.get_barrier_semaphore()
    for r in range(1, N_CHAN):
        pl.semaphore_signal(barrier, inc=1, device_id={"chan": chan_peers[r]}, device_id_type=MESH)
    for r in range(1, 4):
        pl.semaphore_signal(barrier, inc=1, device_id={"dp": dp_peers[r]}, device_id_type=MESH)

    bring_in()
    loaded(0, 1, 7, 8, 9, 10, 11, 12, 13, 14, 15, 16)
    pending = []

    def remote(src, dst, send_sem, recv_sem, **device):
        return pltpu.make_async_remote_copy(
            src_ref=src, dst_ref=dst, send_sem=send_sem, recv_sem=recv_sem, device_id=device, device_id_type=MESH
        )

    def send(*args, **device):
        copy = remote(*args, **device)
        copy.start()
        pending.append(copy)

    def exchange(which, source, recv_ref):
        def copy(r):
            peer = chan_peers[r]
            return remote(
                source(peer), recv_ref.at[chan], a2a_ss.at[which, r - 1], a2a_rs.at[which, r - 1], chan=peer
            )

        def start():
            for r in range(1, N_CHAN):
                copy(r).start()

        def wait():
            for r in range(1, N_CHAN):
                copy(r).wait_recv()

        def finish():
            for r in range(1, N_CHAN):
                copy(r).wait_send()

        return start, wait, finish

    def rows_at(number, count):
        return pl.ds(pl.multiple_of(number, ROWS), count)

    def launch(copy):
        copy.start()
        pending.append(copy)

    own_row = dp * ROWS
    pair_row = (dp - core) * ROWS
    away_row = 2 * ROWS - pair_row
    gate_row, gate_away = (core * 2 + lax.div(dp, 2)) * ROWS, (core * 2 + 1 - lax.div(dp, 2)) * ROWS
    gate_pair, gate_other = core * 2 * ROWS, (1 - core) * 2 * ROWS
    half_lanes = pl.multiple_of(core * LANES, LANES)
    other_lanes = pl.multiple_of((1 - core) * LANES, LANES)

    def gate_view(ref):
        return lambda offset, row, count: ref.at[around[offset % 8], rows_at(row, count), :]

    def hidden_view(ref):
        return lambda offset, row, count: ref.at[
            :, groups[offset % 8], rows_at(row, count), pl.ds(group_lanes[offset % 8], LANES)
        ]

    class Ring:
        def __init__(self, which, view, base, count, hook=None):
            self.which, self.view, self.base, self.count, self.hook = which, view, base, count, hook

        def piece(self, turn, step, base):
            half = self.count // 2
            if step == 4:
                return self.view(4, base + turn * half, half)
            return self.view(-TURNS[turn] * step, base, self.count)

        def copy(self, turn, step, ref):
            slot = turn * 4 + step - 1
            return remote(ref, ref, gring_ss.at[self.which, slot], gring_rs.at[self.which, slot], chan=nexts[turn])

        def send(self, turn, step):
            half = self.count // 2
            if step == 4:
                ref = self.view(-TURNS[turn] * 3, self.base + turn * half, half)
            else:
                ref = self.piece(turn, step - 1, self.base)
            launch(self.copy(turn, step, ref))

        def start(self):
            for turn in range(2):
                self.send(turn, 1)

        def step(self, step):
            for turn in range(2):
                self.copy(turn, step, self.piece(turn, step, self.base)).wait_recv()
                if step < 4:
                    self.send(turn, step + 1)
                if self.hook:
                    self.hook(turn, step)

    def slot_of(turn, step):
        return turn * 4 + step - 1 if step else 8

    def gate_sib(base):
        ref = wab_ref.at[:, rows_at(base, 256), :]
        return remote(ref, ref, gsib_ss, gsib_rs, dp=sibling)

    def gate_spread():
        launch(gate_sib(gate_pair))

    def hidden_cross(which, turn, step, base):
        ref, slot = hidden_rings[which].piece(turn, step, base), slot_of(turn, step)
        return remote(ref, ref, gdx_ss.at[which, slot], gdx_rs.at[which, slot], dp=across)

    gate_ring = Ring(0, gate_view(wab_ref), gate_pair, 256)
    def hidden_part(which):
        def view(offset, row, count):
            lanes = pl.ds(group_lanes[offset % 8], LANES)
            return wh_ref.at[which, groups[offset % 8], rows_at(row, count), lanes]

        return Ring(
            1 + which, view, pair_row, 256, lambda turn, step: launch(hidden_cross(which, turn, step, pair_row))
        )

    hidden_rings = up_ring, down_ring = hidden_part(0), hidden_part(1)

    def gate_over(row):
        ref = gate_ring.view(0, row, ROWS)
        return remote(ref, ref, gx_ss, gx_rs, dp=across)

    def swap_copy(row):
        return remote(stage_ref, hidden_view(wh_ref)(0, row, ROWS), gswap_ss, gswap_rs, dp=sibling)

    def gather_prepare():
        gates = jnp.concatenate([wa_ref[...], wb_ref[...]], axis=0).T.astype(BF16)
        wab_ref[chan, rows_at(gate_row, ROWS), :] = gates
        for which, values in enumerate((up_ref[...], down_ref[...].T)):
            first, second = values[:, :LANES], values[:, LANES:]
            kept = jnp.where(core == 0, first, second)
            wh_ref[which, groups[0], rows_at(own_row, ROWS), pl.ds(group_lanes[0], LANES)] = kept.astype(BF16)
            stage_ref[which] = jnp.where(core == 0, second, first).astype(BF16)

    def gather_start():
        launch(swap_copy(own_row))
        launch(gate_over(gate_row))

    def hidden_first():
        swap_copy(sibling * ROWS).wait_recv()
        for which in range(2):
            hidden_rings[which].start()
            launch(hidden_cross(which, 0, 0, pair_row))

    def gate_first():
        gate_over(gate_away).wait_recv()
        gate_ring.start()

    ring_steps = [(0, 0)] + [(turn, step) for step in range(1, 5) for turn in range(2)]

    def gates_arrived():
        gate_sib(gate_other).wait_recv()

    def hidden_arrived(*steps):
        for turn, step in ring_steps:
            if step in steps:
                for which in range(2):
                    hidden_cross(which, turn, step, away_row).wait_recv()

    def beside(ref, j):
        start = 2 * j * ROWS
        return jnp.concatenate(
            [ref[:, start : start + ROWS].astype(F32), ref[:, start + ROWS : start + 2 * ROWS].astype(F32)], axis=0
        ).T

    for j in range(PAIRS):
        packed = beside(tokens_ref, j)
        tok_ref[j * ROWS : (j + 1) * ROWS, :] = packed.astype(BF16)
        for first, values in ((0, packed), (HALF, beside(cotangent_ref, j))):
            low, high = split_pair(values)
            in_send[2 * j, first : first + HALF, :] = low.astype(BF16)
            in_send[2 * j + 1, first : first + HALF, :] = high.astype(BF16)
    in_recv[chan] = in_send[chan]

    lane_id = lax.broadcasted_iota(jnp.int32, (8, LANES), 1)
    row_id = lax.broadcasted_iota(jnp.int32, (8, LANES), 0)
    halves = jnp.where((lane_id >= HALF) == (row_id == 1), 1.0, 0.0) * jnp.where(row_id < 2, 1.0, 0.0)
    halves = halves.astype(BF16)

    def token_sums(parts):
        total = 0.0
        for part in parts:
            total = total + dot_nt(halves, part)
        return [total[h : h + 1, j * ROWS : (j + 1) * ROWS] for h in range(2) for j in range(PAIRS)]

    def split(values):
        high = values.astype(BF16)
        return high, (values - high.astype(F32)).astype(BF16)

    tokens = tok_ref[...]
    wide_tokens = tokens.astype(F32)
    for i, sums in enumerate(token_sums([tokens]) + token_sums(split(wide_tokens * wide_tokens))):
        head_send[i : i + 1, :] = sums

    def row(*refs):
        return jnp.concatenate([ref[...].reshape(1, HALF) for ref in refs], axis=1)

    bup = bup_ref[...].reshape(1, 2 * LANES)
    head_send[16:17, :] = row(ba_ref, bb_ref)
    head_send[17:18, :] = row(gain2_ref, bias2_ref)
    head_send[18:19, :] = row(bdown_ref, bdown_ref)
    head_send[19:20, :] = bup[:, :LANES]
    head_send[20:21, :] = bup[:, LANES:]
    head_send[21:24, :] = jnp.zeros((3, LANES), F32)
    head_recv[chan] = head_send[...]
    head = exchange(0, lambda peer: head_send, head_recv)
    inputs = exchange(1, lambda peer: in_send.at[peer], in_recv)
    gather_prepare()
    pl.semaphore_wait(barrier, N_CHAN - 1 + 3)
    gather_start()
    head[0]()
    hidden_first()

    loaded(4, 5, 17, 21)
    level, filled = bucket_ref[0], items_ref[0]
    coefl_ref[...] = levels_ref[level]
    item_blocks = jnp.where(level == 0, 2, jnp.where(level == 1, 4, 8))
    block_id = 2 * (row_id % PAIRS) + jnp.where(lane_id >= HALF, 1, 0)
    bound = jnp.where(row_id < PAIRS, filled * item_blocks, item_blocks)
    aux_ref[...] = jnp.where(block_id < bound, 1.0, 0.0)
    for i in range(8):
        modes_ref[i] = jnp.concatenate([raw_modes_ref[i], raw_modes_ref[i]], axis=1)
    inputs[0]()
    gate_first()
    log_dt = row(log_dt_ref, log_dt_ref)
    sigma, step_size = 2.0 * jnp.exp(-log_dt), jnp.exp(log_dt)

    base = pl.multiple_of(dp * QUARTER, QUARTER)

    def spec_copy(which, r):
        peer = dp_peers[r]
        src, dst = ((spec_send, spec_recv), (sgrad_send.at[peer], sgrad_recv))[which]
        return remote(src, dst.at[dp], spec_ss.at[which, r - 1], spec_rs.at[which, r - 1], dp=peer)

    cauchy_coefficients(modes_ref, sigma, mcoef_ref)
    cauchy_forward(0, sigma, mcoef_ref, wave_ref, base, sums_ref, spec_send)
    cauchy_forward(1, sigma, mcoef_ref, wave_ref, base, sums_ref, spec_send)
    cauchy_forward(2, sigma, mcoef_ref, wave_ref, base, sums_ref, spec_send)
    cauchy_forward(3, sigma, mcoef_ref, wave_ref, base, sums_ref, spec_send)
    spec_recv[dp] = spec_send[...]
    for r in range(1, 4):
        spec_copy(0, r).start()
    up_ring.step(1)
    gate_ring.step(1)
    down_ring.step(1)

    head[1]()
    sums = head_recv[0, 0:16, :]
    for c in range(1, N_CHAN):
        sums = sums + head_recv[c, 0:16, :]
    mean = sums[0:8] * (1.0 / MODEL_WIDTH)
    rstd = lax.rsqrt(sums[8:16] * (1.0 / MODEL_WIDTH) - mean * mean + EPSILON)

    def columns(rows):
        tall = rows.T
        return [jnp.where(low_lanes(ROWS), tall[:, j : j + 1], tall[:, 4 + j : 5 + j]) for j in range(PAIRS)]

    loaded(2, 3, 6, 18, 19, 20)
    gain1, bias1, skip = row(gain1_ref, gain1_ref), row(bias1_ref, bias1_ref), row(skip_ref, skip_ref)
    mean_cols, rstd_cols = columns(mean), columns(rstd)
    for j in range(PAIRS):
        hat = (tok_ref[j * ROWS : (j + 1) * ROWS, :].astype(F32) - mean_cols[j]) * rstd_cols[j]
        hat_ref[j] = hat
        norm_ref[j] = hat * gain1 + bias1

    spread_pairs(lambda j, rows: norm_ref[j, rows, :], coefl_ref, 0, tw_ref, 0, 5, rhs_ref, False)
    transform_into(sig_ref, mat_ref, 0, rhs_ref, False)

    for r in range(1, 4):
        spec_copy(0, r).wait_recv()
    for source in range(4):
        store_split(rhs_ref, source * QUARTER, 0, spec_recv[source, :QUARTER, :])
        store_split(rhs_ref, ROWS + source * QUARTER, 0, spec_recv[source, QUARTER:, :])
    up_ring.step(2)
    gate_ring.step(2)
    freq_ref[:, 0:256] = split_product(mat_ref, 1, rhs_ref, 0, 256)
    even = split_product(mat_ref, 2, rhs_ref, LANES, LANES)
    freq_ref[:, LANES:256] = jnp.where(low_lanes(256), freq_ref[:, LANES:256], even)
    sign = 1.0 - 2.0 * (lax.broadcasted_iota(jnp.int32, (CHUNK, LANES), 0) % 2).astype(F32)
    nyquist = step_size * column_sum(mcoef_ref[0]) * (1.0 / TOK_DEV)
    down_ring.step(2)

    def store_taps(j, rows, values):
        taps_ref[j, rows, :] = (values + sign * nyquist) * aux_ref[4 + j : 5 + j, :]

    gather_pairs(freq_ref, coefc_ref, 160, tw_ref, 10, 2, store_taps)
    spread_pairs(lambda j, rows: taps_ref[j, rows, :], coefc_ref, 0, tw_ref, 0, 5, rhs_ref, False)
    transform_into(ans_ref, mat_ref, 0, rhs_ref, False)
    multiply_spectra(sig_ref, ans_ref, rhs_ref, False, False)
    transform_into(freq_ref, mat_ref, 1, rhs_ref, False)
    gate_ring.step(3)
    up_ring.step(3)

    def store_conv(j, rows, values):
        conv_ref[j, rows, :] = values
    gather_pairs(freq_ref, coefl_ref, 80, tw_ref, 0, 5, store_conv)
    for j in range(PAIRS):
        mixed = conv_ref[j] * aux_ref[j : j + 1, :] + skip * norm_ref[j]
        cumulative, density = normal_parts(mixed)
        slope_ref[j] = cumulative + mixed * density
        low, high = split_pair(mixed * cumulative)
        acts_send[2 * j] = low.astype(BF16)
        acts_send[2 * j + 1] = high.astype(BF16)
    acts_recv[chan] = acts_send[chan]
    acts = exchange(2, lambda peer: acts_send.at[peer], acts_recv)
    acts[0]()

    def joined(ref, pair, first):
        return join_pair(
            ref[2 * pair, first : first + HALF, :].astype(F32), ref[2 * pair + 1, first : first + HALF, :].astype(F32)
        )

    def lanes_of(pair):
        return slice(pair * LANES, (pair + 1) * LANES)

    def gate_lanes(pair):
        return lanes_of(pair % 2 * 2 + pair // 2)

    def core_copy(which, src, dst):
        return remote(src, dst, core_ss.at[which], core_rs.at[which], dp=sibling)

    def other_core(which, ref):
        return core_copy(which, ref.at[core], ref.at[core])

    def vector(row, first, second):
        return interleave(head_recv[first, 16 + row : 17 + row, :], head_recv[second, 16 + row : 17 + row, :])

    def both_cores(ref):
        return ref[...].reshape(2 * ROWS, MODEL_WIDTH)

    def hidden_group(offset):
        group = groups[offset]
        low, high = 2 * group, 7 - 2 * group
        bias = jnp.concatenate(
            [jnp.where(core == 0, head_recv[c, 19:20, :], head_recv[c, 20:21, :]) for c in (low, high)], axis=1
        )
        pre = dot_nn(both_cores(norm2_ref), wh_ref[0, group]) + bias
        cumulative, density = normal_parts(pre)
        hidden = (pre * cumulative).astype(BF16)
        hid_ref[group] = hidden
        grad = dot_nn(both_cores(gradf_ref), wh_ref[1, group]) * (cumulative + pre * density)
        grad = grad.astype(BF16)
        gpre_ref[group] = grad
        sums = column_sum(grad.astype(F32))
        tail_send[low, pl.ds(3 + core, 1), :] = sums[:, 0:LANES]
        tail_send[high, pl.ds(3 + core, 1), :] = sums[:, LANES : 2 * LANES]
        branch_ref[...] += dot_nt(hidden, wh_ref[1, group]).reshape(2, ROWS, MODEL_WIDTH)
        back2_ref[...] += dot_nt(grad, wh_ref[0, group]).reshape(2, ROWS, MODEL_WIDTH)

    def offset_of(turn, step):
        return TURNS[turn] * (5 - step)

    def far(offset):
        return 4 if offset == -4 else offset

    class RingBack:
        def __init__(self, which, view, base, count, ring_ref, extra):
            self.which, self.view, self.base, self.count = which, view, base, count
            self.ring_ref, self.extra = ring_ref, extra

        def copy(self, turn, step):
            slot = turn * 4 + step - 1
            half = self.count // 2
            if step == 1:
                dst = self.ring_ref.at[slot]
                lead = (slice(None),) * (len(dst.shape) - 2)
                src, dst = self.view(4, self.base + turn * half, half), dst.at[lead + (pl.ds(0, half), slice(None))]
            else:
                src, dst = self.view(offset_of(turn, step), self.base, self.count), self.ring_ref.at[slot]
            return remote(src, dst, rring_ss.at[self.which, slot], rring_rs.at[self.which, slot], chan=nexts[turn])

        def whole(self, offset):
            return self.view(offset, self.base, self.count)[...].astype(F32) + self.extra(offset)

        def step(self, step):
            half = self.count // 2
            if step == 1:
                self.view(4, self.base, self.count)[...] = self.whole(4).astype(BF16)
                for turn in range(2):
                    launch(self.copy(turn, 1))
                return
            for turn in range(2):
                offset, slot = offset_of(turn, step), turn * 4 + step - 2
                total = self.whole(offset)
                self.copy(turn, step - 1).wait_recv()
                if step == 2:
                    parts = [total[..., :half, :], total[..., half:, :]]
                    parts[turn] = parts[turn] + self.ring_ref[slot][..., :half, :].astype(F32)
                    total = jnp.concatenate(parts, axis=-2)
                else:
                    total = total + self.ring_ref[slot].astype(F32)
                self.view(offset, self.base, self.count)[...] = total.astype(BF16)
                launch(self.copy(turn, step))

        def total(self):
            total = self.whole(0)
            for turn in range(2):
                self.copy(turn, 4).wait_recv()
                total = total + self.ring_ref[turn * 4 + 3].astype(F32)
            return total

    waited = set()

    def wait_once(name, copy):
        if name not in waited:
            waited.add(name)
            copy().wait_recv()

    def gate_share():
        ref = gab_w_ref.at[:, rows_at(gate_other, 256), :]
        return remote(ref, sib_ab_ref, rsib_ss, rsib_rs, dp=sibling)

    def gate_extra(offset):
        wait_once("gates", gate_share)
        return sib_ab_ref[around[offset % 8]].astype(F32)

    def cross_copy(pair):
        src = gh_ref.at[:, groups[pair], rows_at(away_row, 256), :]
        return remote(src, cross_ref.at[pair], rdx_ss.at[pair], rdx_rs.at[pair], dp=across)

    def hidden_extra(offset):
        pair = offset % 4
        wait_once(pair, lambda: cross_copy(pair))
        return cross_ref[pair, :, :, pl.ds(group_lanes[offset % 8], LANES)].astype(F32)

    gate_g = RingBack(0, gate_view(gab_w_ref), gate_pair, 256, ring_ab_ref, gate_extra)

    hidden_g = RingBack(1, hidden_view(gh_ref), pair_row, 256, ring_h_ref, hidden_extra)

    def hidden_grads(offset):
        group = groups[offset]
        gh_ref[1, group] = dot_nn(gradf_t_ref[...], hid_ref[group]).astype(BF16)
        gh_ref[0, group] = dot_nn(norm2_t_ref[...], gpre_ref[group]).astype(BF16)
        launch(cross_copy(offset))

    def part_copy():
        return remote(part_ab_ref.at[0], part_ab_ref.at[1], rx_ss, rx_rs, dp=across)

    def last_swap():
        return remote(keep_ref.at[:, rows_at((1 - core) * ROWS, ROWS), :], swap_ref, rswap_ss, rswap_rs, dp=sibling)

    def gate_last():
        gate_total_ref[...] = gate_g.total()
        part_ab_ref[0] = gate_total_ref[rows_at((1 - lax.div(dp, 2)) * ROWS, ROWS), :].astype(BF16)
        launch(part_copy())

    def gate_finish():
        part_copy().wait_recv()
        gw_ref[:, 0:128] = gate_total_ref[rows_at(lax.div(dp, 2) * ROWS, ROWS), :] + part_ab_ref[1].astype(F32)

    def hidden_last():
        keep_ref[...] = hidden_g.total()
        launch(last_swap())
        for which in range(2):
            gw_ref[:, pl.ds(pl.multiple_of(128 + 256 * which + half_lanes, LANES), LANES)] = keep_ref[
                which, rows_at(core * ROWS, ROWS), :
            ]

    def hidden_finish():
        last_swap().wait_recv()
        for which in range(2):
            gw_ref[:, pl.ds(pl.multiple_of(128 + 256 * which + other_lanes, LANES), LANES)] = swap_ref[which]

    late = exchange(4, lambda peer: late_send.at[peer], late_recv)


    def gate_grads(*offsets):
        for offset in offsets:
            c = chan_at(offset)
            gab_w_ref[c] = dot_nn(acts_t_ref[...], gab_ref[c]).astype(BF16)
        if 0 in offsets:
            launch(gate_share())

    def late_messages():
        core_copy(3, half_send.at[1], half_recv.at[1]).wait_recv()
        for p in range(PAIRS):
            out = res_ref[p] + (branch_ref[core, :, lanes_of(p)] + half_recv[1, :, lanes_of(p)].astype(F32)) + interleave(head_recv[2 * p, 18:19, :], head_recv[2 * p + 1, 18:19, :])[0]
            low, high = split_pair(out)
            late_send[2 * p, :HALF, :] = low.astype(BF16)
            late_send[2 * p + 1, :HALF, :] = high.astype(BF16)
        for c in range(N_CHAN):
            late_send[c, ROWS:, :] = jnp.concatenate([tail_send[c], jnp.zeros((8, LANES), F32)], axis=0).astype(BF16)
        late_recv[chan] = late_send[chan]
        late[0]()

    back = exchange(3, lambda peer: back_send.at[peer], back_recv)

    inputs[1]()
    for p in range(PAIRS):
        gradf_ref[core, :, lanes_of(p)] = joined(in_recv, p, HALF).astype(BF16)
    launch(other_core(0, gradf_ref))
    gate_ring.step(4)
    gate_spread()
    down_ring.step(3)
    gates_arrived()
    acts[1]()
    for p in range(PAIRS):
        acts_ref[:, gate_lanes(p)] = joined(acts_recv, p, 0).astype(BF16)

    total = 0.0
    for p in range(PAIRS):
        first = dot_nn(acts_ref[...], wab_ref[2 * p]) + head_recv[2 * p, 16:17, :]
        second = dot_nn(acts_ref[...], wab_ref[2 * p + 1]) + head_recv[2 * p + 1, 16:17, :]
        gate, raw = interleave(first, second)
        swish = lax.logistic(raw)
        gate_ref[p], swish_ref[p] = gate, swish
        resid = joined(in_recv, p, 0) + gate * swish
        res_ref[p] = resid
        total = total + resid
    mean2 = jnp.sum(total, axis=1, keepdims=True) * (1.0 / MODEL_WIDTH)
    total = 0.0
    for p in range(PAIRS):
        centred = res_ref[p] - mean2
        total = total + centred * centred
    rstd2 = lax.rsqrt(jnp.sum(total, axis=1, keepdims=True) * (1.0 / MODEL_WIDTH) + EPSILON)
    gain2 = []
    for p in range(PAIRS):
        gain, bias = vector(1, 2 * p, 2 * p + 1)
        gain2.append(gain)
        hat = (res_ref[p] - mean2) * rstd2
        hat2_ref[p] = hat
        norm2_ref[core, :, lanes_of(p)] = (hat * gain + bias).astype(BF16)
    launch(other_core(1, norm2_ref))
    branch_ref[...] = jnp.zeros_like(branch_ref)
    acts_t_ref[...] = acts_ref[...].astype(F32).T.astype(BF16)
    back2_ref[...] = jnp.zeros_like(back2_ref)
    for c in range(N_CHAN):
        tail_send[c, 3:8, :] = jnp.zeros((5, LANES), F32)
    hidden_arrived(2)
    down_ring.step(4)
    other_core(0, gradf_ref).wait_recv()
    up_ring.step(4)
    gradf_t_ref[...] = both_cores(gradf_ref).astype(F32).T.astype(BF16)
    hidden_arrived(1, 3)
    other_core(1, norm2_ref).wait_recv()
    norm2_t_ref[...] = both_cores(norm2_ref).astype(F32).T.astype(BF16)
    hidden_group(3)
    hidden_group(1)
    hidden_grads(3)
    hidden_arrived(0, 4)
    hidden_group(0)
    hidden_group(2)
    half_send[0] = back2_ref[1 - core].astype(BF16)
    launch(core_copy(2, half_send.at[0], half_recv.at[0]))
    hidden_grads(0)
    half_send[1] = branch_ref[1 - core].astype(BF16)
    launch(core_copy(3, half_send.at[1], half_recv.at[1]))
    core_copy(2, half_send.at[0], half_recv.at[0]).wait_recv()
    back2 = back2_ref[core] + half_recv[0].astype(F32)
    back2_ref[core] = back2

    mean_q, mean_qx = 0.0, 0.0
    for p in range(PAIRS):
        grad, hat = back2_ref[core, :, lanes_of(p)], hat2_ref[p]
        q = grad * gain2[p]
        mean_q = mean_q + q
        mean_qx = mean_qx + q * hat
        gain_grad, bias_grad = interleave(column_sum(grad * hat), column_sum(grad))
        tail_send[2 * p, 1:2, :] = gain_grad
        first, second = interleave(turn_half(column_sum(grad * hat)), turn_half(column_sum(grad)))
        tail_send[2 * p + 1, 1:2, :] = first
    mean_q = jnp.sum(mean_q, axis=1, keepdims=True) * (1.0 / MODEL_WIDTH)
    mean_qx = jnp.sum(mean_qx, axis=1, keepdims=True) * (1.0 / MODEL_WIDTH)
    for p in range(PAIRS):
        hat = hat2_ref[p]
        extra = rstd2 * (back2_ref[core, :, lanes_of(p)] * gain2[p] - mean_q - hat * mean_qx)
        grad_f = joined(in_recv, p, HALF)
        grad_resid = grad_f + extra
        gate, swish = gate_ref[p], swish_ref[p]
        grad_a = (grad_resid * swish).astype(BF16).astype(F32)
        grad_b = (grad_resid * gate * swish * (1.0 - swish)).astype(BF16).astype(F32)
        first, second = interleave(grad_a, grad_b)
        gab_ref[2 * p] = first.astype(BF16)
        gab_ref[2 * p + 1] = second.astype(BF16)
        tail_send[2 * p, 0:1, :] = column_sum(first)
        tail_send[2 * p + 1, 0:1, :] = column_sum(second)
        low, high = interleave(column_sum(grad_f), column_sum(grad_f))
        tail_send[2 * p, 2:3, :] = low
        tail_send[2 * p + 1, 2:3, :] = high
        low, high = split_pair(extra)
        late_send[2 * p, HALF:ROWS, :] = low.astype(BF16)
        late_send[2 * p + 1, HALF:ROWS, :] = high.astype(BF16)
    grad_acts = 0.0
    for c in range(N_CHAN):
        grad_acts = grad_acts + dot_nt(gab_ref[c], wab_ref[c])
    for p in range(PAIRS):
        low, high = split_pair(grad_acts[:, gate_lanes(p)])
        back_send[2 * p] = low.astype(BF16)
        back_send[2 * p + 1] = high.astype(BF16)
    back_recv[chan] = back_send[chan]
    back[0]()
    hidden_grads(1)
    gate_grads(4, 3, -3)
    late_messages()
    gate_grads(2, -2, 1, -1, 0)

    back[1]()
    skip_grad = 0.0
    for j in range(PAIRS):
        grad = joined(back_recv, j, 0) * slope_ref[j]
        slope_ref[j] = grad
        conv_ref[j] = grad * aux_ref[j : j + 1, :]
        skip_grad = skip_grad + column_sum(grad * norm_ref[j])
    hidden_g.step(1)
    gate_g.step(1)
    hidden_grads(2)
    spread_pairs(lambda j, rows: conv_ref[j, rows, :], coefl_ref, 0, tw_ref, 0, 5, rhs_ref, False)
    transform_into(freq_ref, mat_ref, 0, rhs_ref, False)
    multiply_spectra(sig_ref, freq_ref, rhs_ref, True)
    gate_g.step(2)
    hidden_g.step(2)
    transform_into(sig_ref, mat_ref, 1, rhs_ref)

    def store_kernel_grad(j, rows, values):
        taps_ref[j, rows, :] = values * aux_ref[4 + j : 5 + j, :]

    gather_pairs(sig_ref, coefc_ref, 80, tw_ref, 0, 5, store_kernel_grad)
    nyquist_grad = 0.0
    for j in range(PAIRS):
        whole_sign = 1.0 - 2.0 * (lax.broadcasted_iota(jnp.int32, (ROWS, LANES), 0) % 2).astype(F32)
        nyquist_grad = nyquist_grad + column_sum(taps_ref[j] * whole_sign)
    nyquist_grad = fold(nyquist_grad) * (1.0 / TOK_DEV)
    spread_pairs(lambda j, rows: taps_ref[j, rows, :], coefc_ref, 192, tw_ref, 10, 2, rhs_ref)
    taps_freq_ref[...] = split_product(mat_ref, 0, rhs_ref, 0, 256)
    even = split_product(mat_ref, 3, rhs_ref, LANES, LANES)
    taps_freq_ref[:, LANES:256] = jnp.where(low_lanes(256), taps_freq_ref[:, LANES:256], even)
    for source in range(4):
        rows = slice(source * QUARTER, (source + 1) * QUARTER)
        sgrad_send[source, :QUARTER, :] = taps_freq_ref[rows, :]
        sgrad_send[source, QUARTER:, :] = taps_freq_ref[ROWS + source * QUARTER : ROWS + (source + 1) * QUARTER, :]
    sgrad_recv[dp] = sgrad_send[dp]
    for r in range(1, 4):
        spec_copy(1, r).start()
    gate_g.step(3)
    hidden_g.step(3)

    multiply_spectra(ans_ref, freq_ref, rhs_ref, True, False)
    transform_into(freq_ref, mat_ref, 1, rhs_ref, False)
    late[1]()
    gather_pairs(freq_ref, coefl_ref, 80, tw_ref, 0, 5, store_conv)
    gain_grad, bias_grad = 0.0, 0.0
    scaled, crossed = [], []
    for j in range(PAIRS):
        grad = conv_ref[j] + skip * slope_ref[j]
        conv_ref[j] = grad
        gain_grad = gain_grad + column_sum(grad * hat_ref[j])
        bias_grad = bias_grad + column_sum(grad)
    conv = conv_ref[...].reshape(PAIRS * ROWS, LANES) * gain1
    for i, sums in enumerate(
        token_sums(split(conv)) + token_sums(split(conv * hat_ref[...].reshape(PAIRS * ROWS, LANES)))
    ):
        sum_send[i : i + 1, :] = sums
    gate_g.step(4)
    sum_recv[chan] = sum_send[...]
    sums_back = exchange(6, lambda peer: sum_send, sum_recv)

    for r in range(1, 4):
        spec_copy(1, r).wait_recv()
    sgrad_ref[...] = sgrad_recv[0] + sgrad_recv[1] + sgrad_recv[2] + sgrad_recv[3]

    sigma_sum = point_grads(sigma, wave_ref, base, sums_ref, sgrad_ref, pgrad_ref)
    square_sum = mode_sums(0, jnp.zeros_like(sigma_sum), sigma, mcoef_ref, wave_ref, base, pgrad_ref, mback_ref)
    sums_back[0]()
    hidden_g.step(4)
    square_sum = mode_sums(1, square_sum, sigma, mcoef_ref, wave_ref, base, pgrad_ref, mback_ref)
    gate_last()
    square_sum = mode_sums(2, square_sum, sigma, mcoef_ref, wave_ref, base, pgrad_ref, mback_ref)
    square_sum = mode_sums(3, square_sum, sigma, mcoef_ref, wave_ref, base, pgrad_ref, mback_ref)
    mode_grads, dt_grad = mode_gradients(modes_ref, sigma, nyquist_grad, step_size, sigma_sum, square_sum, mback_ref)
    mask = low_lanes(32)
    for i in range(4):
        dp_send[i * 32 : (i + 1) * 32, :] = jnp.where(mask, mode_grads[i], mode_grads[i + 4])
    first = low_lanes(1)
    dp_send[128:129, :] = jnp.where(first, dt_grad, fold(skip_grad))
    dp_send[129:130, :] = jnp.where(first, fold(gain_grad), fold(bias_grad))
    dp_send[130:136, :] = jnp.zeros((6, LANES), F32)
    tail_sum = late_recv[0, ROWS:, :].astype(F32)
    for c in range(1, N_CHAN):
        tail_sum = tail_sum + late_recv[c, ROWS:, :].astype(F32)
    dp_send[136:144, :] = tail_sum[:8]
    dp_low[...] = dp_send[...].astype(BF16)

    def dp_copy(r):
        return remote(dp_low, dp_recv.at[r - 1], dp_ss.at[r - 1], dp_rs.at[r - 1], dp=dp_peers[r])

    for r in range(1, 4):
        dp_copy(r).start()
    gate_finish()

    sums_back[1]()
    sums = sum_recv[0]
    for c in range(1, N_CHAN):
        sums = sums + sum_recv[c]
    hidden_last()
    sums = sums * (1.0 / MODEL_WIDTH)
    rstd_cols, q_cols, qx_cols = columns(rstd), columns(sums[0:8]), columns(sums[8:16])
    for j in range(PAIRS):
        rows = slice(j * ROWS, (j + 1) * ROWS)
        out_ref[rows, :] = joined(late_recv, j, 0).astype(BF16)
        dtok_ref[rows, :] = joined(late_recv, j, HALF) + rstd_cols[j] * (
            conv_ref[j] * gain1 - q_cols[j] - hat_ref[j] * qx_cols[j]
        )
    for r in range(1, 4):
        dp_copy(r).wait_recv()
    total = dp_send[...] + (dp_recv[0].astype(F32) + dp_recv[1].astype(F32) + dp_recv[2].astype(F32))
    hidden_finish()
    gm_ref[...] = total[0:128]
    gv_ref[...] = total[128:144]
    for copy in pending:
        copy.wait_send()
    for group in (head, inputs, acts, back, late, sums_back):
        group[2]()
    for r in range(1, 4):
        dp_copy(r).wait_send()
        spec_copy(0, r).wait_send()
        spec_copy(1, r).wait_send()
def block_entry(bucket_ref, items_ref, *refs):
    n_in, n_out = 22, 5
    given, results = refs[:n_in], refs[n_in : n_in + n_out]
    held = refs[n_in + n_out : 2 * n_in + n_out]
    made = refs[2 * n_in + n_out : 2 * (n_in + n_out)]
    scratch, in_sem, out_sem = refs[2 * (n_in + n_out) : -2], refs[-2], refs[-1]

    def load(number):
        return pltpu.make_async_copy(given[number], held[number], in_sem.at[number])

    def loaded(*numbers):
        for number in numbers:
            load(number).wait()

    def bring_in():
        for number in (0, 7, 9, 13, 15, 1, 8, 10, 11, 12, 14, 16, 4, 5, 21, 17, 2, 3, 6, 18, 20, 19):
            load(number).start()

    block_kernel(bring_in, loaded, bucket_ref, items_ref, *held, *made, *scratch)
    copies = [pltpu.make_async_copy(made[n], results[n], out_sem.at[n]) for n in range(n_out)]
    for copy in copies:
        copy.start()
    for copy in copies:
        copy.wait()


def unpack_entry(*refs):
    n_in, n_out = 6, 17
    given, results = refs[:n_in], refs[n_in : n_in + n_out]
    held = refs[n_in + n_out : 2 * n_in + n_out]
    made, in_sem, out_sem = refs[2 * n_in + n_out : -2], refs[-2], refs[-1]
    loads = [pltpu.make_async_copy(given[n], held[n], in_sem.at[n]) for n in range(n_in)]
    stores = [pltpu.make_async_copy(made[n], results[n], out_sem.at[n]) for n in range(n_out)]
    for copy in loads:
        copy.start()
    for copy in loads:
        copy.wait()
    unpack_kernel(*held, *made)
    for copy in stores:
        copy.start()
    for copy in stores:
        copy.wait()


def unpack_kernel(
    out_ref, dtok_ref, gw_ref, gm_ref, gv_ref, cotangent_ref,
    output_ref, tokens_ref, gain1_ref, bias1_ref, modes_ref, dt_ref, skip_ref, wa_ref, ba_ref, wb_ref, bb_ref,
    gain2_ref, bias2_ref, up_ref, bup_ref, down_ref, bdown_ref,
):
    for j in range(PAIRS):
        out = out_ref[j * ROWS : (j + 1) * ROWS, :].astype(F32).T.astype(BF16)
        grad = dtok_ref[j * ROWS : (j + 1) * ROWS, :].T
        for h in range(2):
            lanes, rows = slice((2 * j + h) * ROWS, (2 * j + h + 1) * ROWS), slice(h * HALF, (h + 1) * HALF)
            output_ref[:, lanes] = out[rows]
            tokens_ref[:, lanes] = cotangent_ref[:, lanes] + grad[rows]
    for i in range(8):
        modes_ref[i] = gm_ref[i % 4 * 32 : i % 4 * 32 + 32, i // 4 * HALF : (i // 4 + 1) * HALF]
    gates = gw_ref[:, :LANES].T
    wa_ref[...] = gates[:HALF]
    wb_ref[...] = gates[HALF:]
    up_ref[...] = gw_ref[:, 128:384]
    down_ref[...] = gw_ref[:, 384:640].T
    for at, low, high in (
        (0, dt_ref, skip_ref), (1, gain1_ref, bias1_ref), (8, ba_ref, bb_ref), (9, gain2_ref, bias2_ref),
    ):
        low[...] = gv_ref[at, :HALF]
        high[...] = gv_ref[at, HALF:]
    bdown_ref[...] = gv_ref[10, :HALF]
    bup_ref[:LANES] = gv_ref[11, :]
    bup_ref[LANES:] = gv_ref[12, :]


def block_program():
    mats, twiddle, levels, constant, wave = mixer_tables()

    def run(tokens, cotangent, bucket, items, gain1, bias1, modes, log_dt, skip, w_a, b_a, w_b, b_b, gain2, bias2, w_up, b_up, w_down, b_down):
        anywhere = pl.BlockSpec(memory_space=pl.ANY)
        smem = pl.BlockSpec(memory_space=pltpu.SMEM)
        dma = pltpu.SemaphoreType.DMA

        def buf(*shape):
            return pltpu.VMEM(shape, F32)

        def low(*shape):
            return pltpu.VMEM(shape, BF16)

        def full(*shape):
            return jax.ShapeDtypeStruct(shape, F32)

        big, wide = (PAIRS, ROWS, LANES), (256, WIDE)
        def like(arrays):
            return [pltpu.VMEM(tuple(a.shape), a.dtype) for a in arrays]

        arguments = (
            tokens.T, cotangent.T, gain1, bias1, jnp.swapaxes(modes, 1, 2), log_dt, skip, w_a.T, b_a, w_b.T, b_b, gain2,
            bias2, w_up, b_up, w_down, b_down, levels, constant, mats, twiddle, wave,
        )
        middle = (
            jax.ShapeDtypeStruct((512, LANES), BF16), full(512, LANES), full(ROWS, WIDE), full(ROWS, LANES),
            full(16, LANES),
        )
        packed = pl.pallas_call(
            block_entry,
            out_shape=middle,
            in_specs=[smem] * 2 + [anywhere] * 22,
            out_specs=(anywhere,) * 5,
            scratch_shapes=like(arguments) + like(middle) + [
                low(512, LANES), buf(8, LANES), buf(160, LANES), buf(8, 32, LANES),
                low(N_CHAN, 512, 128), low(2, 4, 512, 256), low(N_CHAN, 512, 128), low(2, 4, 512, 256),
                low(2, ROWS, LANES), low(N_CHAN, 256, LANES), low(8, 256, LANES), low(8, 2, 256, LANES), low(2, ROWS, LANES),
                low(4, 2, 256, 256), buf(2, 256, LANES), buf(2, ROWS, LANES), buf(256, LANES),
                low(N_CHAN, ROWS, LANES), low(N_CHAN, ROWS, LANES), buf(24, LANES), buf(N_CHAN, 24, LANES),
                low(N_CHAN, HALF, LANES), low(N_CHAN, HALF, LANES), low(N_CHAN, HALF, LANES), low(N_CHAN, HALF, LANES),
                low(N_CHAN, 144, LANES), low(N_CHAN, 144, LANES),
                buf(16, LANES), buf(N_CHAN, 16, LANES), buf(N_CHAN, 8, LANES),
                buf(144, LANES), low(144, LANES), low(3, 144, LANES), buf(64, 256), buf(4, 64, 256), buf(4, 64, 256), buf(4, 64, 256),
                buf(*big), buf(*big), buf(*big), buf(*big), low(2, *wide), buf(*wide), buf(*wide), buf(*wide), buf(*big),
                buf(10, 32, LANES), buf(2, 16, QUARTER, LANES), buf(2, 16, QUARTER, LANES), buf(10, 32, LANES),
                buf(64, 256), buf(256, 256),
                buf(*big), buf(*big), buf(*big), buf(*big), low(ROWS, 512), low(2, ROWS, 512), low(2, ROWS, 512),
                buf(2, ROWS, 512), buf(2, ROWS, 512), low(2, ROWS, 512), low(2, ROWS, 512),
                low(N_CHAN, ROWS, LANES), low(4, 256, 256), low(4, 256, 256), low(512, ROWS), low(512, 256), low(512, 256),
                dma((3, 8)), dma((3, 8)), dma, dma, dma, dma, dma((2, 9)), dma((2, 9)), dma, dma, dma((4,)), dma((4,)),
                dma((2, 8)), dma((2, 8)), dma, dma, dma, dma, dma((4,)), dma((4,)), dma, dma,
                dma((7, 7)), dma((7, 7)), dma((3,)), dma((3,)), dma((2, 3)), dma((2, 3)), dma((22,)), dma((5,)),
            ],
            compiler_params=pltpu.CompilerParams(
                collective_id=0, has_side_effects=True, vmem_limit_bytes=60 * 1024 * 1024
            ),
            name="block",
        )(bucket, items, *arguments)
        small = full(HALF)
        final = (
                jax.ShapeDtypeStruct((HALF, TOK_DEV), BF16), full(HALF, TOK_DEV), small, small, full(8, 32, HALF),
                small, small, full(HALF, ROWS), small, full(HALF, ROWS), small, small, small, full(ROWS, 256),
                full(256), full(256, ROWS), small,
            )
        sources = (*packed, cotangent.T)
        results = pl.pallas_call(
            unpack_entry,
            out_shape=final,
            in_specs=[anywhere] * 6,
            out_specs=(anywhere,) * 17,
            scratch_shapes=like(sources) + like(final) + [dma((6,)), dma((17,))],
            name="unpack",
        )(*sources)
        turned = {0, 1, 4, 7, 9}
        return tuple(jnp.swapaxes(r, -1, -2) if i in turned else r for i, r in enumerate(results))

    return run


def solution(mesh):
    small = mesh.shape["chan"] == N_CHAN and mesh.shape["dp"] == 4
    return jax.shard_map(
        block_program() if small else shards,
        mesh=mesh,
        in_specs=(
            P("dp", "chan"),
            P("dp", "chan"),
            P("dp"),
            P("dp"),
            P("chan"),
            P("chan"),
            P(None, "chan", None),
            P("chan"),
            P("chan"),
            P("dp", "chan"),
            P("chan"),
            P("dp", "chan"),
            P("chan"),
            P("chan"),
            P("chan"),
            P("dp", "chan"),
            P("chan"),
            P("chan", "dp"),
            P("chan"),
        ),
        out_specs=(
            P("dp", "chan"),
            P("dp", "chan"),
            P("chan"),
            P("chan"),
            P(None, "chan", None),
            P("chan"),
            P("chan"),
            P("dp", "chan"),
            P("chan"),
            P("dp", "chan"),
            P("chan"),
            P("chan"),
            P("chan"),
            P("dp", "chan"),
            P("chan"),
            P("chan", "dp"),
            P("chan"),
        ),
        check_vma=False,
    )
```
